32 devices in a mesh: dp: 4 (over x, core), seq: 2 (over y), tap: 4 (over z).
Axes of the slice: x: 2, y: 2, z: 4, core: 2. Of those that a mesh axis runs over, the one named last changes fastest.
Arguments:
- inputs: bfloat16 [64, 512, 512], P(('dp', 'tap'), 'seq'), may hold values from -6 to 6
- targets: int32 [64, 512], P(('dp', 'tap'), 'seq'), may hold values from 0 to 3
- masked: int32 [64, 512], P(('dp', 'tap'), 'seq'), may hold values from 0 to 1, as said below
- conv_weight: bfloat16 [2, 9, 512, 512], P(None, None, 'tap'), may hold values from -0.09375 to 0.09375
- conv_bias: float32 [2, 512], replicated, may hold values from -3 to 3
- gains: float32 [2, 2, 512], replicated, may hold values from 0.5 to 1.5
- shifts: float32 [2, 2, 512], replicated, may hold values from -2 to 2
- in_weight: bfloat16 [2, 512, 2048], P(None, None, ('dp', 'seq', 'tap')), may hold values from -0.25 to 0.25
- in_bias: float32 [2, 2048], replicated, may hold values from -3 to 3
- out_weight: bfloat16 [2, 2048, 512], P(None, ('dp', 'seq', 'tap')), may hold values from -0.125 to 0.125
- out_bias: float32 [2, 512], replicated, may hold values from -2 to 2
- head_weight: float32 [512, 4], replicated, may hold values from -0.25 to 0.25
Outputs:
- final_state: bfloat16 [64, 512, 512], P(('dp', 'tap'), 'seq')
- grad_inputs: bfloat16 [64, 512, 512], P(('dp', 'tap'), 'seq')
- grad_conv_weight: float32 [2, 9, 512, 512], P(None, None, 'tap')
- grad_conv_bias: float32 [2, 512], replicated
- grad_gains: float32 [2, 2, 512], replicated
- grad_shifts: float32 [2, 2, 512], replicated
- grad_in_weight: float32 [2, 512, 2048], P(None, None, ('dp', 'seq', 'tap'))
- grad_in_bias: float32 [2, 2048], replicated
- grad_out_weight: float32 [2, 2048, 512], P(None, ('dp', 'seq', 'tap'))
- grad_out_bias: float32 [2, 512], replicated
- grad_head_weight: float32 [512, 4], replicated
- loss: float32 [], replicated
The draws below stay inside these ranges and needn't reach their ends.
Inputs may be any that keep to these rules, and one draw needn't show every extreme that they name: Every window has at least one masked position; the masked share of a window varies from window to window, from 5 up to 50 percent.
All inputs are finite; a program needn't handle non-finite values.
Results may differ from the reference program's by a relative error of at most 0.013.
Values may be sent and summed in bfloat16 or wider, within the bound.
No kernel may reach another device: no remote copies, remote signals or barrier semaphores. Data moves between devices by JAX's collectives and lax.ppermute only.
A program may use at most 192 MiB of HBM per device.

```python
import math
import jax
import jax.numpy as jnp
from jax import lax

D = 512
FF = 2048
KERNEL = 9
L = 512
FIRST_DILATION = 4
SECOND_DILATION = 32
NUC = 4
WINDOWS = 64


def draw_masked(key, part):
    key = jax.random.fold_in(key, 7)
    rate_key, spread_key, roll_key, forced_key = jax.random.split(key, 4)
    base_rate = jax.random.randint(rate_key, (WINDOWS, 1), 0, 46)
    rate_spread = jax.random.randint(spread_key, (WINDOWS, 1), 0, 46)
    percent = 5 + base_rate * rate_spread // 45
    rolled = jax.random.randint(roll_key, (WINDOWS, L), 0, 100)
    forced = jax.random.randint(forced_key, (WINDOWS, 1), 0, L)
    positions = jnp.arange(L, dtype=jnp.int32)[None, :]
    return jnp.logical_or(rolled < percent, positions == forced).astype(jnp.int32)


def set_ends(entries, stream_key, smallest, largest):
    spot = [jax.random.randint(jax.random.fold_in(stream_key, axis), (), 0, length) for axis, length in enumerate(entries.shape)]
    widest = entries.shape.index(max(entries.shape))
    neighbour = spot[:widest] + [(spot[widest] + 1) % entries.shape[widest]] + spot[widest + 1:]
    return entries.at[tuple(spot)].set(smallest).at[tuple(neighbour)].set(largest)


def steps_of(rng, dims, cuts, least, high):
    gain = 1.0
    for dim, parts in cuts:
        steps = jax.random.uniform(jax.random.fold_in(jax.random.fold_in(rng, 6), dim), (parts,), jnp.float32, least / len(cuts), high / len(cuts))
        gain = gain * jnp.repeat(jnp.exp(steps), dims[dim] // parts).reshape((-1,) + (1,) * (len(dims) - 1 - dim))
    return gain


def normal_values(key, shape, width, reach, shards=(), kind=jnp.bfloat16):
    array = jax.random.normal(key, shape, jnp.float32) * width
    if len(shards) > 0:
        array = steps_of(key, shape, shards, -0.22, 0.18) * array
    return jnp.clip(array, min=-reach, max=reach).astype(kind)


def setup_inputs(seed: int = 0) -> dict:
    key_list = jax.random.split(jax.random.key(seed), 13)
    return {
        "inputs": normal_values(key_list[0], (WINDOWS, L, D), 1.0, 6.0, ((0, 16), (1, 2))),
        "targets": set_ends(jax.random.randint(key_list[1], (WINDOWS, L), 0, NUC), jax.random.fold_in(key_list[1], 1), 0, NUC - 1).astype(jnp.int32),
        "masked": draw_masked(jax.random.fold_in(key_list[12], 71), 0),
        "conv_weight": normal_values(key_list[3], (2, KERNEL, D, D), (KERNEL * D) ** -0.5, 0.09375, ((2, 4),)),
        "conv_bias": normal_values(key_list[4], (2, D), 0.5, 3.0, (), jnp.float32),
        "gains": jnp.clip(1.0 + 0.1 * jax.random.normal(key_list[5], (2, 2, D), jnp.float32), 0.5, 1.5),
        "shifts": normal_values(key_list[6], (2, 2, D), 0.3, 2.0, (), jnp.float32),
        "in_weight": normal_values(key_list[7], (2, D, FF), D ** -0.5, 0.25, ((2, 32),)),
        "in_bias": normal_values(key_list[8], (2, FF), 0.5, 3.0, (), jnp.float32),
        "out_weight": normal_values(key_list[9], (2, FF, D), FF ** -0.5, 0.125, ((1, 32),)),
        "out_bias": normal_values(key_list[10], (2, D), 0.3, 2.0, (), jnp.float32),
        "head_weight": normal_values(key_list[11], (D, NUC), D ** -0.5, 0.25, (), jnp.float32),
    }


EPSILON = 1e-05
HIGHEST_PRECISION = lax.Precision.HIGHEST

@jax.custom_vjp
def low(v):
    return lax.optimization_barrier(v.astype(jnp.bfloat16)).astype(jnp.float32)

@jax.custom_vjp
def low_back(v):
    return v

def low_keep(v):
    return (low(v), None)

def low_pass(kept, grad):
    return (grad,)

def back_keep(v):
    return (v, None)

def back_low(kept, grad):
    return (low(grad),)
low.defvjp(low_keep, low_pass)
low_back.defvjp(back_keep, back_low)

def gelu_value(values):
    return jax.nn.gelu(values, approximate=False)

def normalize(values, gain_row, shift_bias_row):
    center = values - lax.optimization_barrier(jnp.mean(values, -1, keepdims=True))
    variance = lax.optimization_barrier(jnp.mean(center * center, -1, keepdims=True))
    return center * lax.rsqrt(variance + EPSILON) * gain_row + shift_bias_row

def dilated(signal, weight, tap_spacing):
    reach_rows = KERNEL // 2 * tap_spacing
    padded = jnp.pad(signal, ((0, 0), (reach_rows, reach_rows), (0, 0)))
    summed = jnp.zeros(signal.shape[:2] + (weight.shape[2],), jnp.float32)
    for tap_index in range(KERNEL):
        window = padded[:, tap_index * tap_spacing:tap_index * tap_spacing + signal.shape[1]]
        summed = summed + jnp.einsum('gld,de->gle', window, weight[tap_index], precision=HIGHEST_PRECISION)
    return summed

def forward(stream, parameters, targets, masked):
    conv_weight, conv_bias, gains, shifts, in_weight, in_bias, out_weight, out_bias, head_weight = parameters
    for layer_position_index, tap_spacing in ((0, FIRST_DILATION), (1, SECOND_DILATION)):
        conv_input = low_back(low(stream))
        conv_out = low_back(dilated(conv_input, conv_weight[layer_position_index], tap_spacing) + conv_bias[layer_position_index])
        stream = stream + normalize(gelu_value(conv_out), gains[layer_position_index, 0], shifts[layer_position_index, 0])
        lowered = low(stream)
        hidden = low_back(jnp.einsum('gld,df->glf', lowered, in_weight[layer_position_index], precision=HIGHEST_PRECISION) + in_bias[layer_position_index])
        active = low(gelu_value(hidden))
        ffn_out = low_back(jnp.einsum('glf,fd->gld', active, out_weight[layer_position_index], precision=HIGHEST_PRECISION) + out_bias[layer_position_index])
        stream = stream + normalize(ffn_out, gains[layer_position_index, 1], shifts[layer_position_index, 1])
    logits = jnp.einsum('gld,dn->gln', stream, head_weight, precision=HIGHEST_PRECISION)
    log_total = jax.nn.logsumexp(logits, axis=-1)
    picked = lax.optimization_barrier(jnp.sum(jnp.where(targets[..., None] == jnp.arange(NUC, dtype=jnp.int32), logits, 0.0), -1))
    objective = jnp.sum(masked.astype(jnp.float32) * (log_total - picked))
    return (objective, stream)

def reference(inputs, targets, masked, conv_weight, conv_bias, gains, shifts, in_weight, in_bias, out_weight, out_bias, head_weight):
    parameters = tuple((argument_value.astype(jnp.float32) for argument_value in (conv_weight, conv_bias, gains, shifts, in_weight, in_bias, out_weight, out_bias, head_weight)))
    group_size = math.gcd(WINDOWS, 8)
    group_count = WINDOWS // group_size

    def one_group(running, group_data):
        grad_totals, objective_total = running
        block_inputs, block_targets, block_masked = group_data

        def loss_of(stream, weights):
            return forward(stream, weights, block_targets, block_masked)
        (objective, final_stream), pullback = jax.vjp(loss_of, block_inputs.astype(jnp.float32), parameters)
        grad_stream, grad_parameters = pullback((jnp.ones((), jnp.float32), jnp.zeros_like(final_stream)))
        grad_totals = jax.tree.map(jnp.add, grad_totals, grad_parameters)
        return ((grad_totals, objective_total + objective), (final_stream.astype(jnp.bfloat16), grad_stream.astype(jnp.bfloat16)))
    zero_grads = jax.tree.map(jnp.zeros_like, parameters)
    grouped = (inputs.reshape(group_count, group_size, L, D), targets.reshape(group_count, group_size, L), masked.reshape(group_count, group_size, L))
    (grad_totals, objective_total), (finals, grads) = lax.scan(one_group, (zero_grads, jnp.zeros((), jnp.float32)), grouped)
    loss = objective_total / jnp.sum(masked.astype(jnp.float32))
    return (finals.reshape(WINDOWS, L, D), grads.reshape(WINDOWS, L, D), grad_totals[0], grad_totals[1], grad_totals[2], grad_totals[3], grad_totals[4], grad_totals[5], grad_totals[6], grad_totals[7], grad_totals[8], loss)
```

```python
import jax
import jax.numpy as jnp
from jax import lax
from jax.sharding import PartitionSpec as P

FIRST_DILATION = 4
SECOND_DILATION = 32
EPSILON = 1e-05
HIGHEST_PRECISION = lax.Precision.HIGHEST
CORES = 2


def gelu_parts(values):
    phi = 0.5 * (1.0 + lax.erf(values * 0.7071067811865476))
    return (
        values * phi,
        phi + values * jnp.exp(-0.5 * values * values) * 0.3989422804014327,
    )


def normalize(values):
    center = values - jnp.mean(values, -1, keepdims=True)
    scale = lax.rsqrt(jnp.mean(center * center, -1, keepdims=True) + EPSILON)
    return (center * scale, scale)


def norm_back(upstream, normed, scale):
    return scale * (
        upstream
        - jnp.mean(upstream, -1, keepdims=True)
        - normed * jnp.mean(upstream * normed, -1, keepdims=True)
    )


class Ring:
    def __init__(self, axis, size, index, shift_pairs):
        self.axis, self.size, self.index, self.shift_pairs = axis, size, index, shift_pairs

    def shifted(self, value, by):
        return lax.ppermute(value, self.axis, self.shift_pairs(by))

    def gather(self, value):
        out = jnp.zeros((self.size,) + value.shape, value.dtype)
        out = lax.dynamic_update_index_in_dim(out, value, self.index, 0)
        for by in range(1, self.size):
            source = (self.index - by) % self.size
            out = lax.dynamic_update_index_in_dim(out, self.shifted(value, by), source, 0)
        return out

    def scatter_sum(self, terms):
        total = lax.dynamic_index_in_dim(terms, self.index, 0, False).astype(jnp.float32)
        for by in range(1, self.size):
            target = (self.index + by) % self.size
            sent = lax.dynamic_index_in_dim(terms, target, 0, False)
            total = total + self.shifted(sent, by).astype(jnp.float32)
        return total


def rings():
    peers = lax.axis_size("dp")
    cores = CORES if peers % CORES == 0 else 1
    columns = peers // cores
    place = lax.axis_index("dp")

    def plain(axis):
        size = lax.axis_size(axis)
        return Ring(
            axis, size, lax.axis_index(axis), lambda by: [(i, (i + by) % size) for i in range(size)]
        )

    across = Ring(
        "dp",
        columns,
        place // cores,
        lambda by: [
            (i, (i // cores + by) % columns * cores + i % cores) for i in range(peers)
        ],
    )
    core = Ring(
        "dp",
        cores,
        place % cores,
        lambda by: [(i, i // cores * cores + (i % cores + by) % cores) for i in range(peers)],
    )
    return core, across, plain("seq"), plain("tap")


def passed_along(value, axis, by):
    peers = lax.axis_size(axis)
    pairs = [(i, i + by) for i in range(peers) if 0 <= i + by < peers]
    return lax.ppermute(value, axis, pairs)


def extend(source, reach_rows):
    span_rows = source.shape[1]
    left_parts = []
    right_parts = []
    distances = -(-reach_rows // span_rows)
    for distance in range(1, distances + 1):
        rim_count = min(span_rows, reach_rows - (distance - 1) * span_rows)
        for direction in (1, -1):
            rim_piece = (
                source[:, span_rows - rim_count :] if direction == 1 else source[:, :rim_count]
            )
            arrived = passed_along(rim_piece, "seq", direction * distance)
            if direction == 1:
                left_parts.insert(0, arrived)
            else:
                right_parts.append(arrived)
    return jnp.concatenate(left_parts + [source] + right_parts, axis=1)


def taps_of(extended, span_rows, spacing, order):
    return jnp.concatenate(
        [extended[:, k * spacing : k * spacing + span_rows] for k in order], axis=-1
    ).reshape(-1, len(order) * extended.shape[-1])


def on_device(
    inputs,
    targets,
    masked,
    conv_weight,
    conv_bias,
    gains,
    shifts,
    in_weight,
    in_bias,
    out_weight,
    out_bias,
    head_weight,
):
    core, across, seq, tap = rings()
    copies = core.size * across.size * seq.size
    taps = conv_weight.shape[1]
    channels = conv_weight.shape[2]
    width = conv_weight.shape[3]
    slab = channels // copies
    hidden_width = in_bias.shape[1]
    ffn_rows = in_weight.shape[2]
    windows, span_rows = inputs.shape[0], inputs.shape[1]
    spacings = (FIRST_DILATION, SECOND_DILATION)
    copy_index = (core.index * seq.size + seq.index) * across.size + across.index
    classes = jnp.arange(head_weight.shape[1], dtype=jnp.int32)

    conv_full, in_full, out_full, in_bias_placed = [], [], [], []
    for b in range(2):
        conv_piece = lax.dynamic_slice_in_dim(conv_weight[b], copy_index * slab, slab, 1)
        bundle = jnp.concatenate(
            [conv_piece.reshape(taps * slab, width), in_weight[b].T, out_weight[b]], 0
        )
        along = tap.gather(bundle)
        conv_part = along[:, : taps * slab]
        ffn_part = along[:, taps * slab :]
        conv_part = core.gather(seq.gather(across.gather(conv_part)))
        ffn_part = core.gather(across.gather(seq.gather(ffn_part)))
        conv_part = conv_part.reshape(
            core.size, seq.size, across.size, tap.size, taps, slab, width
        ).transpose(4, 3, 0, 1, 2, 5, 6)
        conv_full.append(conv_part.reshape(taps * tap.size * channels, width))
        ffn_part = ffn_part.reshape(-1, 2, ffn_rows, width)
        in_full.append(ffn_part[:, 0].reshape(hidden_width, width))
        out_full.append(ffn_part[:, 1].reshape(hidden_width, width))
        in_bias_placed.append(
            in_bias[b]
            .reshape(across.size, core.size, seq.size, tap.size, ffn_rows)
            .transpose(1, 0, 2, 3, 4)
            .reshape(hidden_width)
        )

    stream = inputs.astype(jnp.float32).reshape(-1, width)
    flat_masked = masked.reshape(-1).astype(jnp.float32)
    saved = []
    for b in range(2):
        reach = taps // 2 * spacings[b]
        conv_input = stream.astype(jnp.bfloat16).reshape(windows, span_rows, width)
        columns = taps_of(extend(conv_input, reach), span_rows, spacings[b], range(taps))
        conv_out = (
            jnp.dot(columns, conv_full[b], preferred_element_type=jnp.float32) + conv_bias[b]
        )
        conv_gelu, conv_slope = gelu_parts(conv_out)
        normed_conv, scale_conv = normalize(conv_gelu)
        stream = stream + normed_conv * gains[b, 0] + shifts[b, 0]
        lowered = stream.astype(jnp.bfloat16)
        hidden = (
            jnp.einsum("rd,fd->rf", lowered, in_full[b], preferred_element_type=jnp.float32)
            + in_bias_placed[b]
        )
        active, hidden_slope = gelu_parts(hidden)
        active = active.astype(jnp.bfloat16)
        hidden_slope = hidden_slope.astype(jnp.bfloat16)
        ffn_out = (
            jnp.dot(active, out_full[b], preferred_element_type=jnp.float32) + out_bias[b]
        )
        normed_ffn, scale_ffn = normalize(ffn_out)
        stream = stream + normed_ffn * gains[b, 1] + shifts[b, 1]
        saved.append(
            (
                columns,
                conv_slope,
                normed_conv,
                scale_conv,
                lowered,
                active,
                hidden_slope,
                normed_ffn,
                scale_ffn,
            )
        )

    final_state = stream.astype(jnp.bfloat16).reshape(inputs.shape)
    logits = jnp.dot(stream, head_weight, precision=HIGHEST_PRECISION)
    peak_value = jnp.max(logits, -1, keepdims=True)
    exponent = jnp.exp(logits - peak_value)
    denominator = jnp.sum(exponent, -1, keepdims=True)
    log_total = peak_value[:, 0] + jnp.log(denominator[:, 0])
    one_hot = (targets.reshape(-1, 1) == classes).astype(jnp.float32)
    picked = jnp.sum(one_hot * logits, -1)
    objective = jnp.sum(flat_masked * (log_total - picked))
    logit_grad = flat_masked[:, None] * (exponent / denominator - one_hot)
    head_grad = jnp.einsum("rd,rn->dn", stream, logit_grad, precision=HIGHEST_PRECISION)
    stream_grad = jnp.einsum("rn,dn->rd", logit_grad, head_weight, precision=HIGHEST_PRECISION)

    conv_bias_grads = [None, None]
    gain_grads = [[None, None], [None, None]]
    shift_grads = [[None, None], [None, None]]
    in_bias_grads = [None, None]
    out_bias_grads = [None, None]
    grad_conv = [None, None]
    grad_in = [None, None]
    grad_out = [None, None]
    for b in (1, 0):
        (
            columns,
            conv_slope,
            normed_conv,
            scale_conv,
            lowered,
            active,
            hidden_slope,
            normed_ffn,
            scale_ffn,
        ) = saved[b]
        reach = taps // 2 * spacings[b]
        gain_grads[b][1] = jnp.sum(stream_grad * normed_ffn, 0)
        shift_grads[b][1] = jnp.sum(stream_grad, 0)
        output_grad = norm_back(stream_grad * gains[b, 1], normed_ffn, scale_ffn).astype(
            jnp.bfloat16
        )
        active_grad = jnp.einsum(
            "rd,fd->rf", output_grad, out_full[b], preferred_element_type=jnp.float32
        )
        hidden_grad = (active_grad * hidden_slope.astype(jnp.float32)).astype(jnp.bfloat16)
        stream_grad = stream_grad + jnp.dot(
            hidden_grad, in_full[b], preferred_element_type=jnp.float32
        )
        out_bias_grads[b] = jnp.sum(output_grad.astype(jnp.float32), 0)
        in_bias_grads[b] = (
            jnp.sum(hidden_grad.astype(jnp.float32), 0)
            .reshape(core.size, across.size, seq.size, tap.size, ffn_rows)
            .transpose(1, 0, 2, 3, 4)
            .reshape(hidden_width)
        )
        ffn_terms = jnp.stack(
            [
                jnp.einsum(
                    "rf,rd->fd", left, right, preferred_element_type=jnp.float32
                ).astype(jnp.bfloat16).reshape(-1, ffn_rows, width)
                for left, right in ((hidden_grad, lowered), (active, output_grad))
            ],
            1,
        ).reshape(core.size, across.size, seq.size, tap.size, 2 * ffn_rows, width)
        gain_grads[b][0] = jnp.sum(stream_grad * normed_conv, 0)
        shift_grads[b][0] = jnp.sum(stream_grad, 0)
        conv_grad = (
            norm_back(stream_grad * gains[b, 0], normed_conv, scale_conv) * conv_slope
        ).astype(jnp.bfloat16)
        conv_bias_grads[b] = jnp.sum(conv_grad.astype(jnp.float32), 0)
        conv_terms = (
            jnp.einsum("rc,rd->cd", columns, conv_grad, preferred_element_type=jnp.float32)
            .astype(jnp.bfloat16)
            .reshape(taps, tap.size, core.size, seq.size, across.size, slab, width)
            .transpose(2, 3, 4, 1, 0, 5, 6)
            .reshape(core.size, seq.size, across.size, tap.size, taps * slab, width)
        )
        spread = taps_of(
            extend(conv_grad.reshape(windows, span_rows, width), reach),
            span_rows,
            spacings[b],
            range(taps - 1, -1, -1),
        ).reshape(-1, taps, width)
        split_grad = jnp.einsum(
            "rkd,kcd->rc",
            spread,
            conv_full[b].reshape(taps, width, width),
            preferred_element_type=jnp.float32,
        ).astype(jnp.bfloat16)
        stream_grad = stream_grad + split_grad.astype(jnp.float32)

        low = lambda value: value.astype(jnp.bfloat16)
        conv_terms = low(core.scatter_sum(conv_terms))
        conv_terms = low(across.scatter_sum(low(seq.scatter_sum(conv_terms))))
        ffn_terms = low(core.scatter_sum(ffn_terms))
        ffn_terms = low(seq.scatter_sum(low(across.scatter_sum(ffn_terms))))
        mine = tap.scatter_sum(jnp.concatenate([conv_terms, ffn_terms], 1))
        grad_in[b] = mine[taps * slab : taps * slab + ffn_rows].T
        grad_out[b] = mine[taps * slab + ffn_rows :]
        shard = lax.all_gather(low(mine[: taps * slab]), ("dp", "seq"), axis=0)
        grad_conv[b] = (
            shard.reshape(across.size, core.size, seq.size, taps, slab, width)
            .transpose(3, 1, 2, 0, 4, 5)
            .reshape(taps, channels, width)
            .astype(jnp.float32)
        )

    grad_inputs = stream_grad.astype(jnp.bfloat16).reshape(inputs.shape)
    (
        grad_conv_bias,
        grad_gains,
        grad_shifts,
        grad_in_bias,
        grad_out_bias,
        grad_head_weight,
        loss_terms,
    ) = lax.psum(
        (
            jnp.stack(conv_bias_grads),
            jnp.stack([jnp.stack(gain_grads[b]) for b in range(2)]),
            jnp.stack([jnp.stack(shift_grads[b]) for b in range(2)]),
            jnp.stack(in_bias_grads),
            jnp.stack(out_bias_grads),
            head_grad,
            jnp.stack([objective, jnp.sum(flat_masked)]),
        ),
        ("dp", "seq", "tap"),
    )
    return (
        final_state,
        grad_inputs,
        jnp.stack(grad_conv),
        grad_conv_bias,
        grad_gains,
        grad_shifts,
        jnp.stack(grad_in),
        grad_in_bias,
        jnp.stack(grad_out),
        grad_out_bias,
        grad_head_weight,
        loss_terms[0] / loss_terms[1],
    )


def solution(mesh):
    placed = (
        P(("dp", "tap"), "seq", None),
        P(("dp", "tap"), "seq"),
        P(("dp", "tap"), "seq"),
        P(None, None, "tap", None),
        P(),
        P(),
        P(),
        P(None, None, ("dp", "seq", "tap")),
        P(),
        P(None, ("dp", "seq", "tap"), None),
        P(),
        P(),
    )
    return jax.shard_map(
        on_device,
        mesh=mesh,
        in_specs=placed,
        out_specs=(
            P(("dp", "tap"), "seq", None),
            P(("dp", "tap"), "seq", None),
            P(None, None, "tap", None),
            P(),
            P(),
            P(),
            P(None, None, ("dp", "seq", "tap")),
            P(),
            P(None, ("dp", "seq", "tap"), None),
            P(),
            P(),
            P(),
        ),
        check_vma=False,
    )
```

```python
import functools

import jax
import jax.numpy as jnp
from jax import lax
from jax.experimental import pallas as pl
from jax.experimental.pallas import tpu as pltpu
from jax.sharding import PartitionSpec as P

FIRST_DILATION = 4
SECOND_DILATION = 32
EPSILON = 1e-05
HIGHEST_PRECISION = lax.Precision.HIGHEST
CORES = 2
ROW_TILE = 16
VMEM_BYTES = 48 * 1024 * 1024
ANYWHERE = pl.BlockSpec(memory_space=pl.ANY)
SCALARS = pl.BlockSpec(memory_space=pltpu.SMEM)


TOKEN = jax.ShapeDtypeStruct((8, 128), jnp.float32)
TOKEN_SPEC = pl.BlockSpec(TOKEN.shape, lambda *_: (0, 0))


def tokens(after):
    return [TOKEN_SPEC] * len(after)


def low(values):
    return values.astype(jnp.bfloat16)


def wide(values):
    return values.astype(jnp.float32)


def gelu_parts(values):
    phi = 0.5 * (1.0 + lax.erf(values * 0.7071067811865476))
    return (
        values * phi,
        phi + values * jnp.exp(-0.5 * values * values) * 0.3989422804014327,
    )


def normalize(values):
    center = values - jnp.mean(values, -1, keepdims=True)
    scale = lax.rsqrt(jnp.mean(center * center, -1, keepdims=True) + EPSILON)
    return (center * scale, scale)


def norm_back(upstream, normed, scale):
    return scale * (
        upstream
        - jnp.mean(upstream, -1, keepdims=True)
        - normed * jnp.mean(upstream * normed, -1, keepdims=True)
    )


def tap_groups(taps):
    return 3 if taps % 3 == 0 else 1


def conv_forward(extended, weight, step, rows, after=()):
    taps, inner, width = weight.shape
    group = tap_groups(taps)

    def kernel(extended_ref, weight_ref, *refs):
        out_ref = refs[-1]
        first = pl.program_id(0) * group
        total = None
        for j in range(group):
            start = pl.multiple_of((first + j) * step, ROW_TILE)
            term = jnp.dot(
                extended_ref[pl.ds(start, rows), :],
                weight_ref[j],
                preferred_element_type=jnp.float32,
            )
            total = term if total is None else total + term

        @pl.when(pl.program_id(0) == 0)
        def _():
            out_ref[...] = total

        @pl.when(pl.program_id(0) > 0)
        def _():
            out_ref[...] += total

    return pl.pallas_call(
        kernel,
        grid=(taps // group,),
        in_specs=[
            pl.BlockSpec(extended.shape, lambda g: (0, 0)),
            pl.BlockSpec((group, inner, width), lambda g: (g, 0, 0)),
        ]
        + tokens(after),
        out_specs=pl.BlockSpec((rows, width), lambda g: (0, 0)),
        out_shape=jax.ShapeDtypeStruct((rows, width), jnp.float32),
        compiler_params=pltpu.CompilerParams(vmem_limit_bytes=VMEM_BYTES),
        cost_estimate=pl.CostEstimate(
            flops=2 * taps * rows * inner * width,
            bytes_accessed=2 * (extended.size + weight.size) + 4 * rows * width,
            transcendentals=0,
        ),
        name="conv_forward",
    )(extended, weight, *after)


def conv_data_grad(extended, weight, step, rows, after=()):
    taps, inner, width = weight.shape
    group = tap_groups(taps)
    steps = taps // group

    def kernel(extended_ref, weight_ref, *refs):
        out_ref, total_ref = refs[-2:]
        first = pl.program_id(0) * group
        total = None
        for j in range(group):
            start = pl.multiple_of((taps - 1 - first - j) * step, ROW_TILE)
            term = lax.dot_general(
                extended_ref[pl.ds(start, rows), :],
                weight_ref[j],
                (((1,), (1,)), ((), ())),
                preferred_element_type=jnp.float32,
            )
            total = term if total is None else total + term

        @pl.when(pl.program_id(0) == 0)
        def _():
            total_ref[...] = total

        @pl.when(pl.program_id(0) > 0)
        def _():
            total_ref[...] += total

        @pl.when(pl.program_id(0) == steps - 1)
        def _():
            out_ref[...] = low(total_ref[...])

    return pl.pallas_call(
        kernel,
        grid=(steps,),
        in_specs=[
            pl.BlockSpec(extended.shape, lambda g: (0, 0)),
            pl.BlockSpec((group, inner, width), lambda g: (g, 0, 0)),
        ]
        + tokens(after),
        out_specs=pl.BlockSpec((rows, inner), lambda g: (0, 0)),
        out_shape=jax.ShapeDtypeStruct((rows, inner), jnp.bfloat16),
        scratch_shapes=[pltpu.VMEM((rows, inner), jnp.float32)],
        compiler_params=pltpu.CompilerParams(vmem_limit_bytes=VMEM_BYTES),
        cost_estimate=pl.CostEstimate(
            flops=2 * taps * rows * inner * width,
            bytes_accessed=2 * (extended.size + weight.size + rows * inner),
            transcendentals=0,
        ),
        name="conv_data_grad",
    )(extended, weight, *after)


def conv_weight_grad(extended, upstream, half, places, sizes, taps, step, lanes, after=()):
    rows = upstream.shape[0]
    inner = extended.shape[1]
    seqs, acrosses, tap_peers = sizes
    slab = inner // (seqs * acrosses * tap_peers)
    direct = slab % ROW_TILE == 0

    def kernel(place_ref, extended_ref, upstream_ref, *refs):
        out_ref, token_ref = refs[-2:]
        token_ref[...] = jnp.zeros(TOKEN.shape, TOKEN.dtype)
        start = pl.multiple_of(pl.program_id(0) * step, ROW_TILE)
        found = low(
            lax.dot_general(
                extended_ref[pl.ds(start, rows), :],
                upstream_ref[...],
                (((0,), (0,)), ((), ())),
                preferred_element_type=jnp.float32,
            )
        )
        if not direct:
            out_ref[0] = found
            return
        for t in range(tap_peers):
            slot_t = lax.rem(place_ref[3] - t + tap_peers, tap_peers)
            for s in range(seqs):
                slot_s = lax.rem(place_ref[1] - s + seqs, seqs)
                for a in range(acrosses):
                    slot_a = lax.rem(place_ref[2] - a + acrosses, acrosses)
                    base = ((t * seqs + s) * acrosses + a) * slab
                    out_ref[slot_s, slot_a, slot_t, 0] = found[base : base + slab]

    if direct:
        out_shape = (seqs, acrosses, tap_peers, taps, slab, lanes)
        out_spec = pl.BlockSpec(
            (seqs, acrosses, tap_peers, 1, slab, lanes), lambda k, place: (0, 0, 0, k, 0, 0)
        )
    else:
        out_shape = (taps, inner, lanes)
        out_spec = pl.BlockSpec((1, inner, lanes), lambda k, place: (k, 0, 0))
    found, token = pl.pallas_call(
        kernel,
        grid_spec=pltpu.PrefetchScalarGridSpec(
            num_scalar_prefetch=1,
            grid=(taps,),
            in_specs=[
                pl.BlockSpec(extended.shape, lambda k, place: (0, 0)),
                pl.BlockSpec((rows, lanes), lambda k, place: (0, place[0])),
            ]
            + tokens(after),
            out_specs=(out_spec, TOKEN_SPEC),
        ),
        out_shape=(jax.ShapeDtypeStruct(out_shape, jnp.bfloat16), TOKEN),
        compiler_params=pltpu.CompilerParams(vmem_limit_bytes=VMEM_BYTES),
        cost_estimate=pl.CostEstimate(
            flops=2 * taps * rows * inner * lanes,
            bytes_accessed=2 * (extended.size + rows * lanes + taps * inner * lanes),
            transcendentals=0,
        ),
        name="conv_weight_grad",
    )(jnp.stack([half] + list(places)).astype(jnp.int32), extended, upstream, *after)
    if direct:
        return found, token
    found = found.reshape(taps, tap_peers, seqs, acrosses, slab, lanes)
    found = relative(relative(relative(found, 1, places[2], tap_peers), 2, places[0], seqs), 3, places[1], acrosses)
    return found.transpose(2, 3, 1, 0, 4, 5), token


def ffn_weight_grad(pairs, first_unit, units, ffn_rows, after=()):
    rows, width = pairs[0][1].shape
    slots = units // ffn_rows
    if ffn_rows % ROW_TILE:
        return jnp.stack(
            [
                low(
                    lax.dot_general(
                        left[:, first_unit : first_unit + units],
                        right,
                        (((0,), (0,)), ((), ())),
                        preferred_element_type=jnp.float32,
                    )
                ).reshape(slots, ffn_rows, width)
                for left, right in pairs
            ],
            1,
        ), jnp.zeros(TOKEN.shape, TOKEN.dtype)
    block = min(256, units)
    count = block // ffn_rows

    def kernel(*refs):
        out_ref, token_ref = refs[-2:]
        token_ref[...] = jnp.zeros(TOKEN.shape, TOKEN.dtype)
        for which in range(2):
            found = lax.dot_general(
                refs[2 * which][...],
                refs[2 * which + 1][...],
                (((0,), (0,)), ((), ())),
                preferred_element_type=jnp.float32,
            )
            out_ref[:, which] = low(found).reshape(count, ffn_rows, width)

    left_spec = pl.BlockSpec((rows, block), lambda g: (0, first_unit // block + g))
    right_spec = pl.BlockSpec((rows, width), lambda g: (0, 0))
    return pl.pallas_call(
        kernel,
        grid=(units // block,),
        in_specs=[left_spec, right_spec, left_spec, right_spec] + tokens(after),
        out_specs=(pl.BlockSpec((count, 2, ffn_rows, width), lambda g: (g, 0, 0, 0)), TOKEN_SPEC),
        out_shape=(jax.ShapeDtypeStruct((slots, 2, ffn_rows, width), jnp.bfloat16), TOKEN),
        compiler_params=pltpu.CompilerParams(vmem_limit_bytes=VMEM_BYTES),
        cost_estimate=pl.CostEstimate(
            flops=4 * rows * units * width,
            bytes_accessed=4 * (rows * units + rows * width + units * width),
            transcendentals=0,
        ),
        name="ffn_weight_grad",
    )(pairs[0][0], pairs[0][1], pairs[1][0], pairs[1][1], *after)


def copy_all(copies):
    for copy in copies:
        copy.start()
    for copy in copies:
        copy.wait()


def place_conv(pieces, places, sizes, after=()):
    cores, seqs, acrosses, tap_peers = sizes
    taps, slab, lanes = pieces[0][0].shape[2:]
    inner = slab * seqs * acrosses * tap_peers
    if slab % ROW_TILE:
        full = jnp.stack([jnp.stack(row) for row in pieces])
        for axis, (place, size) in enumerate(zip(places, sizes)):
            full = relative(full, axis, place, size)
        return full.transpose(4, 3, 1, 2, 5, 0, 6).reshape(taps, inner, cores * lanes)
    flat = [piece for row in pieces for piece in row]

    def kernel(place_ref, *refs):
        sem_ref, out_ref = refs[-1], refs[-2]
        copies = []
        for c in range(cores):
            lane = lax.rem(place_ref[0] - c + cores, cores) * lanes
            for s in range(seqs):
                at_s = lax.rem(place_ref[1] - s + seqs, seqs)
                for a in range(acrosses):
                    at_a = lax.rem(place_ref[2] - a + acrosses, acrosses)
                    for t in range(tap_peers):
                        at_t = lax.rem(place_ref[3] - t + tap_peers, tap_peers)
                        row = ((at_t * seqs + at_s) * acrosses + at_a) * slab
                        copies.append(
                            pltpu.make_async_copy(
                                refs[c * seqs + s].at[a, t],
                                out_ref.at[
                                    :,
                                    pl.ds(pl.multiple_of(row, slab), slab),
                                    pl.ds(pl.multiple_of(lane, lanes), lanes),
                                ],
                                sem_ref.at[len(copies)],
                            )
                        )
        copy_all(copies)

    return pl.pallas_call(
        kernel,
        in_specs=[SCALARS] + [ANYWHERE] * len(flat) + tokens(after),
        out_specs=ANYWHERE,
        out_shape=jax.ShapeDtypeStruct((taps, inner, cores * lanes), jnp.bfloat16),
        scratch_shapes=[pltpu.SemaphoreType.DMA((cores * seqs * acrosses * tap_peers,))],
        cost_estimate=pl.CostEstimate(
            flops=0, bytes_accessed=4 * taps * inner * cores * lanes, transcendentals=0
        ),
        name="place_conv",
    )(jnp.stack(places).astype(jnp.int32), *flat, *after)


def place_ffn(pieces, sizes, after=()):
    cores, seqs, acrosses, tap_peers = sizes
    ffn_rows, width = pieces[0][0].shape[3:]
    hidden = cores * seqs * acrosses * tap_peers * ffn_rows
    if ffn_rows % ROW_TILE:
        full = jnp.stack([jnp.stack(row) for row in pieces])
        return tuple(full[:, :, :, :, i].reshape(hidden, width) for i in range(2))
    flat = [piece for row in pieces for piece in row]

    def kernel(*refs):
        in_ref, out_ref, sem_ref = refs[-3:]
        copies = []
        for c in range(cores):
            for a in range(acrosses):
                for which, target in ((0, in_ref), (1, out_ref)):
                    copies.append(
                        pltpu.make_async_copy(
                            refs[c * acrosses + a].at[:, :, which],
                            target.at[c, a],
                            sem_ref.at[len(copies)],
                        )
                    )
        copy_all(copies)

    shape = jax.ShapeDtypeStruct(
        (cores, acrosses, seqs, tap_peers, ffn_rows, width), jnp.bfloat16
    )
    found = pl.pallas_call(
        kernel,
        in_specs=[ANYWHERE] * len(flat) + tokens(after),
        out_specs=(ANYWHERE, ANYWHERE),
        out_shape=(shape, shape),
        scratch_shapes=[pltpu.SemaphoreType.DMA((2 * cores * acrosses,))],
        cost_estimate=pl.CostEstimate(
            flops=0, bytes_accessed=8 * hidden * width, transcendentals=0
        ),
        name="place_ffn",
    )(*flat, *after)
    return tuple(each.reshape(hidden, width) for each in found)


class Ring:
    def __init__(self, axis, size, index, shift_pairs):
        self.axis, self.size, self.index, self.shift_pairs = axis, size, index, shift_pairs

    def shifted(self, value, by):
        return lax.ppermute(value, self.axis, self.shift_pairs(by))

    def gather(self, value):
        return [value] + [self.shifted(value, by) for by in range(1, self.size)]


def relative(value, axis, place, size):
    if size == 1:
        return value
    return jnp.stack(
        [
            lax.dynamic_index_in_dim(value, (place - slot) % size, axis, False)
            for slot in range(size)
        ],
        axis,
    )


def rings():
    peers = lax.axis_size("dp")
    cores = CORES if peers % CORES == 0 else 1
    columns = peers // cores
    place = lax.axis_index("dp")

    def plain(axis):
        size = lax.axis_size(axis)
        return Ring(
            axis, size, lax.axis_index(axis), lambda by: [(i, (i + by) % size) for i in range(size)]
        )

    across = Ring(
        "dp",
        columns,
        place // cores,
        lambda by: [
            (i, (i // cores + by) % columns * cores + i % cores) for i in range(peers)
        ],
    )
    core = Ring(
        "dp",
        cores,
        place % cores,
        lambda by: [(i, i // cores * cores + (i % cores + by) % cores) for i in range(peers)],
    )
    return core, across, plain("seq"), plain("tap")


def reduce_back(terms, order):
    parts = [terms[0]] + [order[0].shifted(terms[s], -s) for s in range(1, order[0].size)]
    for ring in order[1:]:
        arrived = [
            ring.shifted(low(sum(wide(part[s]) for part in parts)), -s)
            for s in range(1, ring.size)
        ]
        parts = [part[0] for part in parts] + arrived
    return sum(wide(part) for part in parts)


def passed_along(value, axis, by):
    peers = lax.axis_size(axis)
    pairs = [(i, i + by) for i in range(peers) if 0 <= i + by < peers]
    return lax.ppermute(value, axis, pairs)


def extend(source, reach_rows):
    span_rows = source.shape[0]
    left_parts = []
    right_parts = []
    distances = -(-reach_rows // span_rows)
    for distance in range(1, distances + 1):
        rim_count = min(span_rows, reach_rows - (distance - 1) * span_rows)
        for direction in (1, -1):
            rim_piece = (
                source[span_rows - rim_count :] if direction == 1 else source[:rim_count]
            )
            arrived = passed_along(rim_piece, "seq", direction * distance)
            if direction == 1:
                left_parts.insert(0, arrived)
            else:
                right_parts.append(arrived)
    return jnp.concatenate(left_parts + [source] + right_parts, axis=0)


def to_rows(values):
    windows, positions = values.shape[:2]
    cut = values.reshape((windows, positions // FIRST_DILATION, FIRST_DILATION) + values.shape[2:])
    return jnp.swapaxes(cut, 0, 1).reshape((windows * positions,) + values.shape[2:])


def from_rows(values, windows):
    cut = values.reshape((-1, windows, FIRST_DILATION) + values.shape[1:])
    return jnp.swapaxes(cut, 0, 1).reshape((windows, -1) + values.shape[1:])


def on_device(
    inputs,
    targets,
    masked,
    conv_weight,
    conv_bias,
    gains,
    shifts,
    in_weight,
    in_bias,
    out_weight,
    out_bias,
    head_weight,
):
    core, across, seq, tap = rings()
    taps = conv_weight.shape[1]
    channels = conv_weight.shape[2]
    width = conv_weight.shape[3]
    slab = channels // (seq.size * across.size)
    lanes = width // core.size
    hidden_width = in_bias.shape[1]
    ffn_rows = in_weight.shape[2]
    windows = inputs.shape[0]
    rows = windows * inputs.shape[1]
    steps = (FIRST_DILATION * windows, SECOND_DILATION * windows)
    classes = jnp.arange(head_weight.shape[1], dtype=jnp.int32)
    places = (core.index, seq.index, across.index, tap.index)
    sizes = (core.size, seq.size, across.size, tap.size)

    conv_full, in_full, out_full, in_bias_placed = [], [], [], []
    for b in range(2):
        conv_piece = lax.dynamic_slice(
            conv_weight[b],
            (0, (seq.index * across.size + across.index) * slab, core.index * lanes),
            (taps, slab, lanes),
        )
        ffn_piece = jnp.stack([in_weight[b].T, out_weight[b]])
        conv_part = jnp.stack(tap.gather(conv_piece))
        ffn_part = jnp.stack(tap.gather(ffn_piece))
        conv_part = seq.gather(jnp.stack(across.gather(conv_part)))
        ffn_part = across.gather(jnp.stack(seq.gather(ffn_part)))
        conv_slots = [core.gather(part) for part in conv_part]
        ffn_slots = [core.gather(part) for part in ffn_part]
        conv_full.append(
            place_conv([[s[c] for s in conv_slots] for c in range(core.size)], places, sizes)
        )
        full = place_ffn([[a[c] for a in ffn_slots] for c in range(core.size)], sizes)
        in_full.append(full[0])
        out_full.append(full[1])
        bias = in_bias[b].reshape(across.size, core.size, seq.size, tap.size, ffn_rows)
        for axis, ring in enumerate((across, core, seq, tap)):
            bias = relative(bias, axis, ring.index, ring.size)
        in_bias_placed.append(bias.transpose(1, 0, 2, 3, 4).reshape(hidden_width))

    conv_input = to_rows(inputs)
    stream = wide(conv_input)
    flat_masked = wide(to_rows(masked))
    flat_targets = to_rows(targets)
    saved = []
    for b in range(2):
        reach = taps // 2 * steps[b]
        extended = extend(conv_input, reach)
        conv_out = conv_forward(extended, conv_full[b], steps[b], rows) + conv_bias[b]
        conv_gelu, conv_slope = gelu_parts(conv_out)
        normed_conv, scale_conv = normalize(conv_gelu)
        stream = stream + normed_conv * gains[b, 0] + shifts[b, 0]
        lowered = low(stream)
        hidden = (
            jnp.einsum("rd,fd->rf", lowered, in_full[b], preferred_element_type=jnp.float32)
            + in_bias_placed[b]
        )
        active, hidden_slope = gelu_parts(hidden)
        active = low(active)
        hidden_slope = low(hidden_slope)
        ffn_out = (
            jnp.dot(active, out_full[b], preferred_element_type=jnp.float32) + out_bias[b]
        )
        normed_ffn, scale_ffn = normalize(ffn_out)
        stream = stream + normed_ffn * gains[b, 1] + shifts[b, 1]
        conv_input = low(stream)
        saved.append(
            (
                extended,
                conv_slope,
                normed_conv,
                scale_conv,
                lowered,
                active,
                hidden_slope,
                normed_ffn,
                scale_ffn,
            )
        )

    final_state = from_rows(conv_input, windows)
    logits = jnp.dot(stream, head_weight, precision=HIGHEST_PRECISION)
    peak_value = jnp.max(logits, -1, keepdims=True)
    exponent = jnp.exp(logits - peak_value)
    denominator = jnp.sum(exponent, -1, keepdims=True)
    log_total = peak_value[:, 0] + jnp.log(denominator[:, 0])
    one_hot = wide(flat_targets[:, None] == classes)
    picked = jnp.sum(one_hot * logits, -1)
    objective = jnp.sum(flat_masked * (log_total - picked))
    logit_grad = flat_masked[:, None] * (exponent / denominator - one_hot)
    head_grad = jnp.einsum("rd,rn->dn", stream, logit_grad, precision=HIGHEST_PRECISION)
    stream_grad = jnp.einsum("rn,dn->rd", logit_grad, head_weight, precision=HIGHEST_PRECISION)

    conv_bias_grads = [None, None]
    gain_grads = [[None, None], [None, None]]
    shift_grads = [[None, None], [None, None]]
    in_bias_grads = [None, None]
    out_bias_grads = [None, None]
    grad_conv = [None, None]
    grad_in = [None, None]
    grad_out = [None, None]
    units = hidden_width // core.size
    for b in (1, 0):
        (
            extended,
            conv_slope,
            normed_conv,
            scale_conv,
            lowered,
            active,
            hidden_slope,
            normed_ffn,
            scale_ffn,
        ) = saved[b]
        reach = taps // 2 * steps[b]
        gain_grads[b][1] = jnp.sum(stream_grad * normed_ffn, 0)
        shift_grads[b][1] = jnp.sum(stream_grad, 0)
        output_grad = low(norm_back(stream_grad * gains[b, 1], normed_ffn, scale_ffn))
        active_grad = jnp.einsum(
            "rd,fd->rf", output_grad, out_full[b], preferred_element_type=jnp.float32
        )
        hidden_grad = low(active_grad * wide(hidden_slope))
        stream_grad = stream_grad + jnp.dot(
            hidden_grad, in_full[b], preferred_element_type=jnp.float32
        )
        out_bias_grads[b] = jnp.sum(wide(output_grad), 0)
        bias = jnp.sum(wide(hidden_grad), 0).reshape(
            core.size, across.size, seq.size, tap.size, ffn_rows
        )
        for axis, ring in enumerate((core, across, seq, tap)):
            bias = relative(bias, axis, ring.index, ring.size)
        in_bias_grads[b] = bias.transpose(1, 0, 2, 3, 4).reshape(hidden_width)
        gain_grads[b][0] = jnp.sum(stream_grad * normed_conv, 0)
        shift_grads[b][0] = jnp.sum(stream_grad, 0)
        conv_grad = low(
            norm_back(stream_grad * gains[b, 0], normed_conv, scale_conv) * conv_slope
        )
        conv_bias_grads[b] = jnp.sum(wide(conv_grad), 0)

        def ffn_terms(slot, after):
            return ffn_weight_grad(
                ((hidden_grad, lowered), (active, output_grad)), slot * units, units, ffn_rows, after
            )

        def conv_terms(slot, after):
            return conv_weight_grad(
                extended,
                conv_grad,
                (core.index - slot) % core.size,
                places[1:],
                sizes[1:],
                taps,
                steps[b],
                lanes,
                after,
            )

        ffn_found = [None] * core.size
        conv_found = [None] * core.size
        last = ()
        for slot in range(core.size - 1, -1, -1):
            ffn_found[slot], token = ffn_terms(slot, last)
            last = (token,)
        for slot in range(core.size - 1, -1, -1):
            conv_found[slot], token = conv_terms(slot, last)
            last = (token,)
        split_grad = conv_data_grad(extend(conv_grad, reach), conv_full[b], steps[b], rows, last)
        stream_grad = stream_grad + wide(split_grad)

        ffn_found = [
            each.reshape(across.size, seq.size, tap.size, 2, ffn_rows, width) for each in ffn_found
        ]
        ffn_sum = reduce_back(ffn_found, (core, across, seq, tap))
        grad_in[b] = ffn_sum[0].T
        grad_out[b] = ffn_sum[1]
        shard = lax.all_gather(
            low(reduce_back(conv_found, (core, seq, across, tap))), ("dp", "seq"), axis=0
        )
        grad_conv[b] = wide(
            shard.reshape(across.size, core.size, seq.size, taps, slab, lanes)
            .transpose(3, 2, 0, 4, 1, 5)
            .reshape(taps, channels, width)
        )

    grad_inputs = from_rows(low(stream_grad), windows)
    (
        grad_conv_bias,
        grad_gains,
        grad_shifts,
        grad_in_bias,
        grad_out_bias,
        grad_head_weight,
        loss_terms,
    ) = lax.psum(
        (
            jnp.stack(conv_bias_grads),
            jnp.stack([jnp.stack(gain_grads[b]) for b in range(2)]),
            jnp.stack([jnp.stack(shift_grads[b]) for b in range(2)]),
            jnp.stack(in_bias_grads),
            jnp.stack(out_bias_grads),
            head_grad,
            jnp.stack([objective, jnp.sum(flat_masked)]),
        ),
        ("dp", "seq", "tap"),
    )
    return (
        final_state,
        grad_inputs,
        jnp.stack(grad_conv),
        grad_conv_bias,
        grad_gains,
        grad_shifts,
        jnp.stack(grad_in),
        grad_in_bias,
        jnp.stack(grad_out),
        grad_out_bias,
        grad_head_weight,
        loss_terms[0] / loss_terms[1],
    )


def solution(mesh):
    placed = (
        P(("dp", "tap"), "seq", None),
        P(("dp", "tap"), "seq"),
        P(("dp", "tap"), "seq"),
        P(None, None, "tap", None),
        P(),
        P(),
        P(),
        P(None, None, ("dp", "seq", "tap")),
        P(),
        P(None, ("dp", "seq", "tap"), None),
        P(),
        P(),
    )
    return jax.shard_map(
        on_device,
        mesh=mesh,
        in_specs=placed,
        out_specs=(
            P(("dp", "tap"), "seq", None),
            P(("dp", "tap"), "seq", None),
            P(None, None, "tap", None),
            P(),
            P(),
            P(),
            P(None, None, ("dp", "seq", "tap")),
            P(),
            P(None, ("dp", "seq", "tap"), None),
            P(),
            P(),
            P(),
        ),
        check_vma=False,
    )
```

```python
import functools

import jax
import jax.numpy as jnp
from jax import lax
from jax.experimental import pallas as pl
from jax.experimental.pallas import tpu as pltpu
from jax.sharding import PartitionSpec as P

FIRST_DILATION = 4
SECOND_DILATION = 32
EPSILON = 1e-05
HIGHEST_PRECISION = lax.Precision.HIGHEST
CORES = 2
ROW_TILE = 16
VMEM_BYTES = 48 * 1024 * 1024
ANYWHERE = pl.BlockSpec(memory_space=pl.ANY)
SCALARS = pl.BlockSpec(memory_space=pltpu.SMEM)


TOKEN = jax.ShapeDtypeStruct((8, 128), jnp.float32)
TOKEN_SPEC = pl.BlockSpec(TOKEN.shape, lambda *_: (0, 0))


def tokens(after):
    return [TOKEN_SPEC] * len(after)


def low(values):
    return values.astype(jnp.bfloat16)


def wide(values):
    return values.astype(jnp.float32)


def gelu_parts(values):
    phi = 0.5 * (1.0 + lax.erf(values * 0.7071067811865476))
    return (
        values * phi,
        phi + values * jnp.exp(-0.5 * values * values) * 0.3989422804014327,
    )


def normalize(values):
    center = values - jnp.mean(values, -1, keepdims=True)
    scale = lax.rsqrt(jnp.mean(center * center, -1, keepdims=True) + EPSILON)
    return (center * scale, scale)


def norm_back(upstream, normed, scale):
    return scale * (
        upstream
        - jnp.mean(upstream, -1, keepdims=True)
        - normed * jnp.mean(upstream * normed, -1, keepdims=True)
    )


def tap_groups(taps):
    return 3 if taps % 3 == 0 else 1


def conv_forward(extended, weight, step, rows, after=()):
    taps, inner, width = weight.shape
    group = tap_groups(taps)

    def kernel(extended_ref, weight_ref, *refs):
        out_ref = refs[-1]
        first = pl.program_id(0) * group
        total = None
        for j in range(group):
            start = pl.multiple_of((first + j) * step, ROW_TILE)
            term = jnp.dot(
                extended_ref[pl.ds(start, rows), :],
                weight_ref[j],
                preferred_element_type=jnp.float32,
            )
            total = term if total is None else total + term

        @pl.when(pl.program_id(0) == 0)
        def _():
            out_ref[...] = total

        @pl.when(pl.program_id(0) > 0)
        def _():
            out_ref[...] += total

    return pl.pallas_call(
        kernel,
        grid=(taps // group,),
        in_specs=[
            pl.BlockSpec(extended.shape, lambda g: (0, 0)),
            pl.BlockSpec((group, inner, width), lambda g: (g, 0, 0)),
        ]
        + tokens(after),
        out_specs=pl.BlockSpec((rows, width), lambda g: (0, 0)),
        out_shape=jax.ShapeDtypeStruct((rows, width), jnp.float32),
        compiler_params=pltpu.CompilerParams(vmem_limit_bytes=VMEM_BYTES),
        cost_estimate=pl.CostEstimate(
            flops=2 * taps * rows * inner * width,
            bytes_accessed=2 * (extended.size + weight.size) + 4 * rows * width,
            transcendentals=0,
        ),
        name="conv_forward",
    )(extended, weight, *after)


def conv_data_grad(extended, weight, step, rows, after=()):
    taps, inner, width = weight.shape
    group = tap_groups(taps)
    steps = taps // group

    def kernel(extended_ref, weight_ref, *refs):
        out_ref, token_ref, total_ref = refs[-3:]
        token_ref[...] = jnp.zeros(TOKEN.shape, TOKEN.dtype)
        first = pl.program_id(0) * group
        total = None
        for j in range(group):
            start = pl.multiple_of((taps - 1 - first - j) * step, ROW_TILE)
            term = lax.dot_general(
                extended_ref[pl.ds(start, rows), :],
                weight_ref[j],
                (((1,), (1,)), ((), ())),
                preferred_element_type=jnp.float32,
            )
            total = term if total is None else total + term

        @pl.when(pl.program_id(0) == 0)
        def _():
            total_ref[...] = total

        @pl.when(pl.program_id(0) > 0)
        def _():
            total_ref[...] += total

        @pl.when(pl.program_id(0) == steps - 1)
        def _():
            out_ref[...] = low(total_ref[...])

    return pl.pallas_call(
        kernel,
        grid=(steps,),
        in_specs=[
            pl.BlockSpec(extended.shape, lambda g: (0, 0)),
            pl.BlockSpec((group, inner, width), lambda g: (g, 0, 0)),
        ]
        + tokens(after),
        out_specs=(pl.BlockSpec((rows, inner), lambda g: (0, 0)), TOKEN_SPEC),
        out_shape=(jax.ShapeDtypeStruct((rows, inner), jnp.bfloat16), TOKEN),
        scratch_shapes=[pltpu.VMEM((rows, inner), jnp.float32)],
        compiler_params=pltpu.CompilerParams(vmem_limit_bytes=VMEM_BYTES),
        cost_estimate=pl.CostEstimate(
            flops=2 * taps * rows * inner * width,
            bytes_accessed=2 * (extended.size + weight.size + rows * inner),
            transcendentals=0,
        ),
        name="conv_data_grad",
    )(extended, weight, *after)


def conv_weight_grad(extended, upstream, half, places, sizes, taps, step, lanes, after=()):
    rows = upstream.shape[0]
    inner = extended.shape[1]
    seqs, acrosses, tap_peers = sizes
    slab = inner // (seqs * acrosses * tap_peers)
    direct = slab % ROW_TILE == 0

    def kernel(place_ref, extended_ref, upstream_ref, *refs):
        out_ref, token_ref = refs[-2:]
        token_ref[...] = jnp.zeros(TOKEN.shape, TOKEN.dtype)
        start = pl.multiple_of(pl.program_id(0) * step, ROW_TILE)
        found = low(
            lax.dot_general(
                extended_ref[pl.ds(start, rows), :],
                upstream_ref[...],
                (((0,), (0,)), ((), ())),
                preferred_element_type=jnp.float32,
            )
        )
        if not direct:
            out_ref[0] = found
            return
        for t in range(tap_peers):
            slot_t = lax.rem(place_ref[3] - t + tap_peers, tap_peers)
            for s in range(seqs):
                slot_s = lax.rem(place_ref[1] - s + seqs, seqs)
                for a in range(acrosses):
                    slot_a = lax.rem(place_ref[2] - a + acrosses, acrosses)
                    base = ((t * seqs + s) * acrosses + a) * slab
                    out_ref[slot_s, slot_a, slot_t, 0] = found[base : base + slab]

    if direct:
        out_shape = (seqs, acrosses, tap_peers, taps, slab, lanes)
        out_spec = pl.BlockSpec(
            (seqs, acrosses, tap_peers, 1, slab, lanes), lambda k, place: (0, 0, 0, k, 0, 0)
        )
    else:
        out_shape = (taps, inner, lanes)
        out_spec = pl.BlockSpec((1, inner, lanes), lambda k, place: (k, 0, 0))
    found, token = pl.pallas_call(
        kernel,
        grid_spec=pltpu.PrefetchScalarGridSpec(
            num_scalar_prefetch=1,
            grid=(taps,),
            in_specs=[
                pl.BlockSpec(extended.shape, lambda k, place: (0, 0)),
                pl.BlockSpec((rows, lanes), lambda k, place: (0, place[0])),
            ]
            + tokens(after),
            out_specs=(out_spec, TOKEN_SPEC),
        ),
        out_shape=(jax.ShapeDtypeStruct(out_shape, jnp.bfloat16), TOKEN),
        compiler_params=pltpu.CompilerParams(vmem_limit_bytes=VMEM_BYTES),
        cost_estimate=pl.CostEstimate(
            flops=2 * taps * rows * inner * lanes,
            bytes_accessed=2 * (extended.size + rows * lanes + taps * inner * lanes),
            transcendentals=0,
        ),
        name="conv_weight_grad",
    )(jnp.stack([half] + list(places)).astype(jnp.int32), extended, upstream, *after)
    if direct:
        return found, token
    found = found.reshape(taps, tap_peers, seqs, acrosses, slab, lanes)
    found = relative(relative(relative(found, 1, places[2], tap_peers), 2, places[0], seqs), 3, places[1], acrosses)
    return found.transpose(2, 3, 1, 0, 4, 5), token


def ffn_weight_grad(pairs, first_unit, units, ffn_rows, after=()):
    rows, width = pairs[0][1].shape
    slots = units // ffn_rows
    if ffn_rows % ROW_TILE:
        return jnp.stack(
            [
                low(
                    lax.dot_general(
                        left[:, first_unit : first_unit + units],
                        right,
                        (((0,), (0,)), ((), ())),
                        preferred_element_type=jnp.float32,
                    )
                ).reshape(slots, ffn_rows, width)
                for left, right in pairs
            ],
            1,
        ), jnp.zeros(TOKEN.shape, TOKEN.dtype)
    block = min(256, units)
    count = block // ffn_rows

    def kernel(*refs):
        out_ref, token_ref = refs[-2:]
        token_ref[...] = jnp.zeros(TOKEN.shape, TOKEN.dtype)
        for which in range(2):
            found = lax.dot_general(
                refs[2 * which][...],
                refs[2 * which + 1][...],
                (((0,), (0,)), ((), ())),
                preferred_element_type=jnp.float32,
            )
            out_ref[:, which] = low(found).reshape(count, ffn_rows, width)

    left_spec = pl.BlockSpec((rows, block), lambda g: (0, first_unit // block + g))
    right_spec = pl.BlockSpec((rows, width), lambda g: (0, 0))
    return pl.pallas_call(
        kernel,
        grid=(units // block,),
        in_specs=[left_spec, right_spec, left_spec, right_spec] + tokens(after),
        out_specs=(pl.BlockSpec((count, 2, ffn_rows, width), lambda g: (g, 0, 0, 0)), TOKEN_SPEC),
        out_shape=(jax.ShapeDtypeStruct((slots, 2, ffn_rows, width), jnp.bfloat16), TOKEN),
        compiler_params=pltpu.CompilerParams(vmem_limit_bytes=VMEM_BYTES),
        cost_estimate=pl.CostEstimate(
            flops=4 * rows * units * width,
            bytes_accessed=4 * (rows * units + rows * width + units * width),
            transcendentals=0,
        ),
        name="ffn_weight_grad",
    )(pairs[0][0], pairs[0][1], pairs[1][0], pairs[1][1], *after)


def add_slots(parts, slots, after=()):
    lanes = parts[0].shape[-1]
    rows = parts[0].size // (slots * lanes)
    parts = [part.reshape(slots, rows, lanes) for part in parts]
    block = rows // 4 if rows % (4 * ROW_TILE) == 0 else rows

    def kernel(*refs):
        out_refs, token_ref = refs[-1 - slots : -1], refs[-1]
        token_ref[...] = jnp.zeros(TOKEN.shape, TOKEN.dtype)
        for slot in range(slots):
            out_refs[slot][...] = low(sum(wide(refs[i][slot]) for i in range(len(parts))))

    found = pl.pallas_call(
        kernel,
        grid=(rows // block,),
        in_specs=[pl.BlockSpec((slots, block, lanes), lambda g: (0, g, 0))] * len(parts)
        + tokens(after),
        out_specs=[pl.BlockSpec((block, lanes), lambda g: (g, 0))] * slots + [TOKEN_SPEC],
        out_shape=[jax.ShapeDtypeStruct((rows, lanes), jnp.bfloat16)] * slots + [TOKEN],
        compiler_params=pltpu.CompilerParams(vmem_limit_bytes=VMEM_BYTES),
        cost_estimate=pl.CostEstimate(
            flops=len(parts) * slots * rows * lanes,
            bytes_accessed=2 * (len(parts) + 1) * slots * rows * lanes,
            transcendentals=0,
        ),
        name="add_slots",
    )(*parts, *after)
    return found[:slots], found[slots]


def place_conv_grads(pieces, places, sizes):
    cores, seqs, acrosses = sizes[:3]
    taps, slab, lanes = pieces[0][0][0][0].shape
    channels = slab * seqs * acrosses
    blocks = len(pieces)
    if slab % ROW_TILE:
        full = jnp.stack(
            [
                jnp.stack([jnp.stack([jnp.stack(row) for row in plane]) for plane in block])
                for block in pieces
            ]
        )
        for axis, (place, size) in enumerate(zip(places[:3], sizes[:3])):
            full = relative(full, axis + 1, place, size)
        return wide(
            full.transpose(0, 4, 2, 3, 5, 1, 6).reshape(blocks, taps, channels, cores * lanes)
        )
    flat = [piece for block in pieces for plane in block for row in plane for piece in row]

    def kernel(place_ref, *refs):
        out_ref = refs[-1]
        for b in range(blocks):
            for c in range(cores):
                lane = pl.multiple_of(lax.rem(place_ref[0] - c + cores, cores) * lanes, lanes)
                for s in range(seqs):
                    at_s = lax.rem(place_ref[1] - s + seqs, seqs)
                    for a in range(acrosses):
                        at_a = lax.rem(place_ref[2] - a + acrosses, acrosses)
                        row = pl.multiple_of((at_s * acrosses + at_a) * slab, slab)
                        piece = refs[((b * cores + c) * seqs + s) * acrosses + a]
                        out_ref[b, 0, pl.ds(row, slab), pl.ds(lane, lanes)] = wide(piece[0])

    return pl.pallas_call(
        kernel,
        grid_spec=pltpu.PrefetchScalarGridSpec(
            num_scalar_prefetch=1,
            grid=(taps,),
            in_specs=[pl.BlockSpec((1, slab, lanes), lambda k, place: (k, 0, 0))] * len(flat),
            out_specs=pl.BlockSpec(
                (blocks, 1, channels, cores * lanes), lambda k, place: (0, k, 0, 0)
            ),
        ),
        out_shape=jax.ShapeDtypeStruct((blocks, taps, channels, cores * lanes), jnp.float32),
        compiler_params=pltpu.CompilerParams(vmem_limit_bytes=VMEM_BYTES),
        cost_estimate=pl.CostEstimate(
            flops=0,
            bytes_accessed=6 * blocks * taps * channels * cores * lanes,
            transcendentals=0,
        ),
        name="place_conv_grads",
    )(jnp.stack(places[:3]).astype(jnp.int32), *flat)


def copy_all(copies):
    for copy in copies:
        copy.start()
    for copy in copies:
        copy.wait()


def place_conv(pieces, places, sizes):
    cores, seqs, acrosses, tap_peers = sizes
    taps, slab, lanes = pieces[0][0][0].shape[1:]
    inner = slab * seqs * acrosses * tap_peers
    if slab % ROW_TILE:
        full = jnp.stack([jnp.stack([jnp.stack(row) for row in plane]) for plane in pieces])
        for axis, (place, size) in enumerate(zip(places, sizes)):
            full = relative(full, axis, place, size)
        return full.transpose(4, 3, 1, 2, 5, 0, 6).reshape(taps, inner, cores * lanes)
    flat = [piece for plane in pieces for row in plane for piece in row]

    def kernel(place_ref, *refs):
        sem_ref, out_ref = refs[-1], refs[-2]
        copies = []
        for c in range(cores):
            lane = lax.rem(place_ref[0] - c + cores, cores) * lanes
            for s in range(seqs):
                at_s = lax.rem(place_ref[1] - s + seqs, seqs)
                for a in range(acrosses):
                    at_a = lax.rem(place_ref[2] - a + acrosses, acrosses)
                    for t in range(tap_peers):
                        at_t = lax.rem(place_ref[3] - t + tap_peers, tap_peers)
                        row = ((at_t * seqs + at_s) * acrosses + at_a) * slab
                        copies.append(
                            pltpu.make_async_copy(
                                refs[(c * seqs + s) * acrosses + a].at[t],
                                out_ref.at[
                                    :,
                                    pl.ds(pl.multiple_of(row, slab), slab),
                                    pl.ds(pl.multiple_of(lane, lanes), lanes),
                                ],
                                sem_ref.at[len(copies)],
                            )
                        )
        copy_all(copies)

    return pl.pallas_call(
        kernel,
        in_specs=[SCALARS] + [ANYWHERE] * len(flat),
        out_specs=pl.BlockSpec(memory_space=pltpu.VMEM),
        out_shape=jax.ShapeDtypeStruct((taps, inner, cores * lanes), jnp.bfloat16),
        scratch_shapes=[pltpu.SemaphoreType.DMA((cores * seqs * acrosses * tap_peers,))],
        compiler_params=pltpu.CompilerParams(vmem_limit_bytes=VMEM_BYTES),
        cost_estimate=pl.CostEstimate(
            flops=0, bytes_accessed=4 * taps * inner * cores * lanes, transcendentals=0
        ),
        name="place_conv",
    )(jnp.stack(places).astype(jnp.int32), *flat)


def place_ffn(pieces, sizes):
    cores, seqs, acrosses, tap_peers = sizes
    ffn_rows, width = pieces[0][0][0].shape[2:]
    hidden = cores * seqs * acrosses * tap_peers * ffn_rows
    if ffn_rows % ROW_TILE:
        full = jnp.stack([jnp.stack([jnp.stack(row) for row in plane]) for plane in pieces])
        return tuple(full[:, :, :, :, i].reshape(hidden, width) for i in range(2))
    flat = [piece for plane in pieces for row in plane for piece in row]

    def kernel(*refs):
        in_ref, out_ref, sem_ref = refs[-3:]
        copies = []
        for c in range(cores):
            for a in range(acrosses):
                for s in range(seqs):
                    for which, target in ((0, in_ref), (1, out_ref)):
                        copies.append(
                            pltpu.make_async_copy(
                                refs[(c * acrosses + a) * seqs + s].at[:, which],
                                target.at[c, a, s],
                                sem_ref.at[len(copies)],
                            )
                        )
        copy_all(copies)

    shape = jax.ShapeDtypeStruct(
        (cores, acrosses, seqs, tap_peers, ffn_rows, width), jnp.bfloat16
    )
    found = pl.pallas_call(
        kernel,
        in_specs=[ANYWHERE] * len(flat),
        out_specs=(pl.BlockSpec(memory_space=pltpu.VMEM), pl.BlockSpec(memory_space=pltpu.VMEM)),
        out_shape=(shape, shape),
        scratch_shapes=[pltpu.SemaphoreType.DMA((2 * cores * acrosses * seqs,))],
        compiler_params=pltpu.CompilerParams(vmem_limit_bytes=VMEM_BYTES),
        cost_estimate=pl.CostEstimate(
            flops=0, bytes_accessed=8 * hidden * width, transcendentals=0
        ),
        name="place_ffn",
    )(*flat)
    return tuple(each.reshape(hidden, width) for each in found)


class Ring:
    def __init__(self, axis, size, index, pairs):
        self.axis, self.size, self.index, self.pairs = axis, size, index, pairs

    def shifted(self, value, by):
        return lax.ppermute(value, self.axis, self.pairs(lambda i: (i + by) % self.size))

    def swapped(self, value, bit):
        return lax.ppermute(value, self.axis, self.pairs(lambda i: i ^ bit))

    def gather(self, value):
        return [value] + [self.shifted(value, by) for by in range(1, self.size)]


def relative(value, axis, place, size):
    if size == 1:
        return value
    return jnp.stack(
        [
            lax.dynamic_index_in_dim(value, (place - slot) % size, axis, False)
            for slot in range(size)
        ],
        axis,
    )


def rings():
    peers = lax.axis_size("dp")
    cores = CORES if peers % CORES == 0 else 1
    columns = peers // cores
    place = lax.axis_index("dp")

    def plain(axis):
        size = lax.axis_size(axis)
        return Ring(
            axis, size, lax.axis_index(axis), lambda move: [(i, move(i)) for i in range(size)]
        )

    across = Ring(
        "dp",
        columns,
        place // cores,
        lambda move: [(i, move(i // cores) * cores + i % cores) for i in range(peers)],
    )
    core = Ring(
        "dp",
        cores,
        place % cores,
        lambda move: [(i, i // cores * cores + move(i % cores)) for i in range(peers)],
    )
    return core, across, plain("seq"), plain("tap")


class Reduce:
    def __init__(self, terms, order):
        self.order = order
        self.parts = [terms[0]] + [order[0].shifted(terms[s], -s) for s in range(1, order[0].size)]

    def step(self, level, after):
        ring = self.order[level]
        found, token = add_slots(self.parts, ring.size, after)
        self.parts = [found[0]] + [ring.shifted(found[s], -s) for s in range(1, ring.size)]
        return (token,)

    def total(self):
        return sum(wide(part) for part in self.parts)


def summed(value, order):
    if any(ring.size & (ring.size - 1) for ring in order):
        return lax.psum(value, ("dp", "seq", "tap"))
    for ring in order:
        bit = 1
        while bit < ring.size:
            value = value + ring.swapped(value, bit)
            bit *= 2
    return value


def passed_along(value, axis, by):
    peers = lax.axis_size(axis)
    pairs = [(i, i + by) for i in range(peers) if 0 <= i + by < peers]
    return lax.ppermute(value, axis, pairs)


def extend(source, reach_rows):
    span_rows = source.shape[0]
    left_parts = []
    right_parts = []
    distances = -(-reach_rows // span_rows)
    for distance in range(1, distances + 1):
        rim_count = min(span_rows, reach_rows - (distance - 1) * span_rows)
        for direction in (1, -1):
            rim_piece = (
                source[span_rows - rim_count :] if direction == 1 else source[:rim_count]
            )
            arrived = passed_along(rim_piece, "seq", direction * distance)
            if direction == 1:
                left_parts.insert(0, arrived)
            else:
                right_parts.append(arrived)
    return jnp.concatenate(left_parts + [source] + right_parts, axis=0)


def to_rows(values):
    windows, positions = values.shape[:2]
    cut = values.reshape((windows, positions // FIRST_DILATION, FIRST_DILATION) + values.shape[2:])
    return jnp.swapaxes(cut, 0, 1).reshape((windows * positions,) + values.shape[2:])


def from_rows(values, windows):
    cut = values.reshape((-1, windows, FIRST_DILATION) + values.shape[1:])
    return jnp.swapaxes(cut, 0, 1).reshape((windows, -1) + values.shape[1:])


def on_device(
    inputs,
    targets,
    masked,
    conv_weight,
    conv_bias,
    gains,
    shifts,
    in_weight,
    in_bias,
    out_weight,
    out_bias,
    head_weight,
):
    core, across, seq, tap = rings()
    taps = conv_weight.shape[1]
    channels = conv_weight.shape[2]
    width = conv_weight.shape[3]
    slab = channels // (seq.size * across.size)
    lanes = width // core.size
    hidden_width = in_bias.shape[1]
    ffn_rows = in_weight.shape[2]
    windows = inputs.shape[0]
    rows = windows * inputs.shape[1]
    steps = (FIRST_DILATION * windows, SECOND_DILATION * windows)
    classes = jnp.arange(head_weight.shape[1], dtype=jnp.int32)
    places = (core.index, seq.index, across.index, tap.index)
    sizes = (core.size, seq.size, across.size, tap.size)

    conv_full, in_full, out_full, in_bias_placed = [], [], [], []
    nothing = jnp.zeros((), jnp.bfloat16)
    for b in range(2):
        conv_piece = nothing + lax.dynamic_slice(
            conv_weight[b],
            (0, (seq.index * across.size + across.index) * slab, core.index * lanes),
            (taps, slab, lanes),
        )
        ffn_piece = nothing + jnp.stack([in_weight[b].T, out_weight[b]])
        conv_tap = tap.gather(conv_piece)
        ffn_tap = tap.gather(ffn_piece)
        nothing = sum(part[0, 0, 0] for part in conv_tap + ffn_tap) * 0
        conv_slots = [
            [core.gather(part) for part in seq.gather(each)]
            for each in across.gather(jnp.stack(conv_tap))
        ]
        ffn_slots = [
            [core.gather(part) for part in across.gather(each)]
            for each in seq.gather(jnp.stack(ffn_tap))
        ]
        conv_full.append(
            place_conv(
                [
                    [[conv_slots[a][s][c] for a in range(across.size)] for s in range(seq.size)]
                    for c in range(core.size)
                ],
                places,
                sizes,
            )
        )
        full = place_ffn(
            [
                [[ffn_slots[s][a][c] for s in range(seq.size)] for a in range(across.size)]
                for c in range(core.size)
            ],
            sizes,
        )
        in_full.append(full[0])
        out_full.append(full[1])
        bias = in_bias[b].reshape(across.size, core.size, seq.size, tap.size, ffn_rows)
        for axis, ring in enumerate((across, core, seq, tap)):
            bias = relative(bias, axis, ring.index, ring.size)
        in_bias_placed.append(bias.transpose(1, 0, 2, 3, 4).reshape(hidden_width))

    conv_input = to_rows(inputs)
    stream = wide(conv_input)
    flat_masked = wide(to_rows(masked))
    flat_targets = to_rows(targets)
    saved = []
    for b in range(2):
        reach = taps // 2 * steps[b]
        extended = extend(conv_input, reach)
        conv_out = conv_forward(extended, conv_full[b], steps[b], rows) + conv_bias[b]
        conv_gelu, conv_slope = gelu_parts(conv_out)
        normed_conv, scale_conv = normalize(conv_gelu)
        stream = stream + normed_conv * gains[b, 0] + shifts[b, 0]
        lowered = low(stream)
        hidden = (
            jnp.einsum("rd,fd->rf", lowered, in_full[b], preferred_element_type=jnp.float32)
            + in_bias_placed[b]
        )
        active, hidden_slope = gelu_parts(hidden)
        active = low(active)
        hidden_slope = low(hidden_slope)
        ffn_out = (
            jnp.dot(active, out_full[b], preferred_element_type=jnp.float32) + out_bias[b]
        )
        normed_ffn, scale_ffn = normalize(ffn_out)
        stream = stream + normed_ffn * gains[b, 1] + shifts[b, 1]
        conv_input = low(stream)
        saved.append(
            (
                extended,
                conv_slope,
                normed_conv,
                scale_conv,
                lowered,
                active,
                hidden_slope,
                normed_ffn,
                scale_ffn,
            )
        )

    final_state = from_rows(conv_input, windows)
    logits = jnp.dot(stream, head_weight, precision=HIGHEST_PRECISION)
    peak_value = jnp.max(logits, -1, keepdims=True)
    exponent = jnp.exp(logits - peak_value)
    denominator = jnp.sum(exponent, -1, keepdims=True)
    log_total = peak_value[:, 0] + jnp.log(denominator[:, 0])
    one_hot = wide(flat_targets[:, None] == classes)
    picked = jnp.sum(one_hot * logits, -1)
    objective = jnp.sum(flat_masked * (log_total - picked))
    logit_grad = flat_masked[:, None] * (exponent / denominator - one_hot)
    head_grad = jnp.einsum("rd,rn->dn", stream, logit_grad, precision=HIGHEST_PRECISION)
    stream_grad = jnp.einsum("rn,dn->rd", logit_grad, head_weight, precision=HIGHEST_PRECISION)

    conv_bias_grads = [None, None]
    gain_grads = [[None, None], [None, None]]
    shift_grads = [[None, None], [None, None]]
    in_bias_grads = [None, None]
    out_bias_grads = [None, None]
    grad_in = []
    grad_out = []
    ffn_sums = [None, None]
    conv_sums = [None, None]
    last = ()
    units = hidden_width // core.size
    for b in (1, 0):
        (
            extended,
            conv_slope,
            normed_conv,
            scale_conv,
            lowered,
            active,
            hidden_slope,
            normed_ffn,
            scale_ffn,
        ) = saved[b]
        reach = taps // 2 * steps[b]
        gain_grads[b][1] = jnp.sum(stream_grad * normed_ffn, 0)
        shift_grads[b][1] = jnp.sum(stream_grad, 0)
        output_grad = low(norm_back(stream_grad * gains[b, 1], normed_ffn, scale_ffn))
        active_grad = jnp.einsum(
            "rd,fd->rf", output_grad, out_full[b], preferred_element_type=jnp.float32
        )
        hidden_grad = low(active_grad * wide(hidden_slope))
        stream_grad = stream_grad + jnp.dot(
            hidden_grad, in_full[b], preferred_element_type=jnp.float32
        )
        out_bias_grads[b] = jnp.sum(wide(output_grad), 0)
        bias = jnp.sum(wide(hidden_grad), 0).reshape(
            core.size, across.size, seq.size, tap.size, ffn_rows
        )
        for axis, ring in enumerate((core, across, seq, tap)):
            bias = relative(bias, axis, ring.index, ring.size)
        in_bias_grads[b] = bias.transpose(1, 0, 2, 3, 4).reshape(hidden_width)
        gain_grads[b][0] = jnp.sum(stream_grad * normed_conv, 0)
        shift_grads[b][0] = jnp.sum(stream_grad, 0)
        conv_grad = low(
            norm_back(stream_grad * gains[b, 0], normed_conv, scale_conv) * conv_slope
        )
        conv_bias_grads[b] = jnp.sum(wide(conv_grad), 0)

        def ffn_terms(slot, after):
            return ffn_weight_grad(
                ((hidden_grad, lowered), (active, output_grad)), slot * units, units, ffn_rows, after
            )

        def conv_terms(slot, after):
            return conv_weight_grad(
                extended,
                conv_grad,
                (core.index - slot) % core.size,
                places[1:],
                sizes[1:],
                taps,
                steps[b],
                lanes,
                after,
            )

        def ffn_grads(last):
            found = [None] * core.size
            for slot in range(core.size - 1, -1, -1):
                found[slot], token = ffn_terms(slot, last)
                last = (token,)
            return Reduce(found, (core, across, seq, tap)), last

        def conv_grads(last):
            found = [None] * core.size
            for slot in range(core.size - 1, -1, -1):
                found[slot], token = conv_terms(slot, last)
                last = (token,)
            found = [each.reshape(-1, lanes) for each in found]
            return Reduce(found, (core, seq, across, tap)), last

        if b == 1:
            ffn_sums[1], last = ffn_grads(())
            conv_sums[1], last = conv_grads(last)
            last = ffn_sums[1].step(1, last)
            last = conv_sums[1].step(1, last)
        else:
            last = ffn_sums[1].step(2, last)
            last = conv_sums[1].step(2, last)
            conv_sums[0], last = conv_grads(last)
            last = ffn_sums[1].step(3, last)
            last = conv_sums[1].step(3, last)
            ffn_sums[0], last = ffn_grads(last)
            last = conv_sums[0].step(1, last)
        split_grad, token = conv_data_grad(
            extend(conv_grad, reach), conv_full[b], steps[b], rows, last
        )
        last = (token,)
        stream_grad = stream_grad + wide(split_grad)

    last = ffn_sums[0].step(1, last)
    last = conv_sums[0].step(2, last)
    last = ffn_sums[0].step(2, last)
    last = conv_sums[0].step(3, last)
    last = ffn_sums[0].step(3, last)
    grad_inputs = from_rows(low(stream_grad), windows)

    pieces = []
    for b in range(2):
        total = ffn_sums[b].total().reshape(2, ffn_rows, width)
        grad_in.append(total[0].T)
        grad_out.append(total[1])
        shard = low(conv_sums[b].total()).reshape(taps, slab, lanes)
        slots = [seq.gather(each) for each in across.gather(shard)]
        slots = [[core.gather(each) for each in row] for row in slots]
        pieces.append(
            [
                [[slots[a][s][c] for a in range(across.size)] for s in range(seq.size)]
                for c in range(core.size)
            ]
        )
    grad_conv = place_conv_grads(pieces, places, sizes)

    small = [
        jnp.stack(conv_bias_grads),
        jnp.stack([jnp.stack(gain_grads[b]) for b in range(2)]),
        jnp.stack([jnp.stack(shift_grads[b]) for b in range(2)]),
        jnp.stack(in_bias_grads),
        jnp.stack(out_bias_grads),
        head_grad.T,
        jnp.pad(jnp.stack([objective, jnp.sum(flat_masked)]), (0, width - 2)),
    ]
    packed = jnp.concatenate([each.reshape(-1, width) for each in small])
    packed = summed(packed, (core, across, seq, tap))
    unpacked = []
    first = 0
    for each in small:
        count = each.size // width
        unpacked.append(packed[first : first + count].reshape(each.shape))
        first += count
    (
        grad_conv_bias,
        grad_gains,
        grad_shifts,
        grad_in_bias,
        grad_out_bias,
        grad_head_weight,
        loss_terms,
    ) = unpacked
    return (
        final_state,
        grad_inputs,
        grad_conv,
        grad_conv_bias,
        grad_gains,
        grad_shifts,
        jnp.stack(grad_in),
        grad_in_bias,
        jnp.stack(grad_out),
        grad_out_bias,
        grad_head_weight.T,
        loss_terms[0] / loss_terms[1],
    )


def solution(mesh):
    placed = (
        P(("dp", "tap"), "seq", None),
        P(("dp", "tap"), "seq"),
        P(("dp", "tap"), "seq"),
        P(None, None, "tap", None),
        P(),
        P(),
        P(),
        P(None, None, ("dp", "seq", "tap")),
        P(),
        P(None, ("dp", "seq", "tap"), None),
        P(),
        P(),
    )
    return jax.shard_map(
        on_device,
        mesh=mesh,
        in_specs=placed,
        out_specs=(
            P(("dp", "tap"), "seq", None),
            P(("dp", "tap"), "seq", None),
            P(None, None, "tap", None),
            P(),
            P(),
            P(),
            P(None, None, ("dp", "seq", "tap")),
            P(),
            P(None, ("dp", "seq", "tap"), None),
            P(),
            P(),
            P(),
        ),
        check_vma=False,
    )
```

```python
import functools

import jax
import jax.numpy as jnp
from jax import lax
from jax.experimental import pallas as pl
from jax.experimental.pallas import tpu as pltpu
from jax.sharding import PartitionSpec as P

FIRST_DILATION = 4
SECOND_DILATION = 32
EPSILON = 1e-05
HIGHEST_PRECISION = lax.Precision.HIGHEST
CORES = 2
ROW_TILE = 16
VMEM_BYTES = 48 * 1024 * 1024
ANYWHERE = pl.BlockSpec(memory_space=pl.ANY)
SCALARS = pl.BlockSpec(memory_space=pltpu.SMEM)


TOKEN = jax.ShapeDtypeStruct((8, 128), jnp.float32)
WHOLE = pl.BlockSpec(memory_space=pltpu.VMEM)
TOKEN_SPEC = pl.BlockSpec(TOKEN.shape, lambda *_: (0, 0))


def tokens(after):
    return [TOKEN_SPEC] * len(after)


def low(values):
    return values.astype(jnp.bfloat16)


def wide(values):
    return values.astype(jnp.float32)


def gelu_parts(values):
    phi = 0.5 * (1.0 + lax.erf(values * 0.7071067811865476))
    return (
        values * phi,
        phi + values * jnp.exp(-0.5 * values * values) * 0.3989422804014327,
    )


def normalize(values):
    center = values - jnp.mean(values, -1, keepdims=True)
    scale = lax.rsqrt(jnp.mean(center * center, -1, keepdims=True) + EPSILON)
    return (center * scale, scale)


def norm_back(upstream, normed, scale):
    return scale * (
        upstream
        - jnp.mean(upstream, -1, keepdims=True)
        - normed * jnp.mean(upstream * normed, -1, keepdims=True)
    )


def tap_groups(taps):
    return 3 if taps % 3 == 0 else 1


def conv_forward(extended, weight, step, rows, after=()):
    taps, inner, width = weight.shape
    group = tap_groups(taps)

    def kernel(extended_ref, weight_ref, *refs):
        out_ref = refs[-1]
        first = pl.program_id(0) * group
        total = None
        for j in range(group):
            start = pl.multiple_of((first + j) * step, ROW_TILE)
            term = jnp.dot(
                extended_ref[pl.ds(start, rows), :],
                weight_ref[j],
                preferred_element_type=jnp.float32,
            )
            total = term if total is None else total + term

        @pl.when(pl.program_id(0) == 0)
        def _():
            out_ref[...] = total

        @pl.when(pl.program_id(0) > 0)
        def _():
            out_ref[...] += total

    return pl.pallas_call(
        kernel,
        grid=(taps // group,),
        in_specs=[
            pl.BlockSpec(extended.shape, lambda g: (0, 0)),
            pl.BlockSpec((group, inner, width), lambda g: (g, 0, 0)),
        ]
        + tokens(after),
        out_specs=pl.BlockSpec((rows, width), lambda g: (0, 0)),
        out_shape=jax.ShapeDtypeStruct((rows, width), jnp.float32),
        compiler_params=pltpu.CompilerParams(vmem_limit_bytes=VMEM_BYTES),
        cost_estimate=pl.CostEstimate(
            flops=2 * taps * rows * inner * width,
            bytes_accessed=2 * (extended.size + weight.size) + 4 * rows * width,
            transcendentals=0,
        ),
        name="conv_forward",
    )(extended, weight, *after)


def conv_data_grad(extended, weight, step, rows, after=()):
    taps, inner, width = weight.shape
    group = tap_groups(taps)
    steps = taps // group

    def kernel(extended_ref, weight_ref, *refs):
        out_ref, token_ref, total_ref = refs[-3:]
        token_ref[...] = jnp.zeros(TOKEN.shape, TOKEN.dtype)
        first = pl.program_id(0) * group
        total = None
        for j in range(group):
            start = pl.multiple_of((taps - 1 - first - j) * step, ROW_TILE)
            term = lax.dot_general(
                extended_ref[pl.ds(start, rows), :],
                weight_ref[j],
                (((1,), (1,)), ((), ())),
                preferred_element_type=jnp.float32,
            )
            total = term if total is None else total + term

        @pl.when(pl.program_id(0) == 0)
        def _():
            total_ref[...] = total

        @pl.when(pl.program_id(0) > 0)
        def _():
            total_ref[...] += total

        @pl.when(pl.program_id(0) == steps - 1)
        def _():
            out_ref[...] = low(total_ref[...])

    return pl.pallas_call(
        kernel,
        grid=(steps,),
        in_specs=[
            pl.BlockSpec(extended.shape, lambda g: (0, 0)),
            pl.BlockSpec((group, inner, width), lambda g: (g, 0, 0)),
        ]
        + tokens(after),
        out_specs=(pl.BlockSpec((rows, inner), lambda g: (0, 0)), TOKEN_SPEC),
        out_shape=(jax.ShapeDtypeStruct((rows, inner), jnp.bfloat16), TOKEN),
        scratch_shapes=[pltpu.VMEM((rows, inner), jnp.float32)],
        compiler_params=pltpu.CompilerParams(vmem_limit_bytes=VMEM_BYTES),
        cost_estimate=pl.CostEstimate(
            flops=2 * taps * rows * inner * width,
            bytes_accessed=2 * (extended.size + weight.size + rows * inner),
            transcendentals=0,
        ),
        name="conv_data_grad",
    )(extended, weight, *after)


def conv_weight_grad(extendeds, upstream, arrived, places, sizes, taps, step, after=()):
    cores, seqs, acrosses, tap_peers = sizes
    rows = upstream.shape[0]
    inner = extendeds[0].shape[1]
    lanes = upstream.shape[1] // cores
    slab = inner // (seqs * acrosses * tap_peers)
    direct = slab % ROW_TILE == 0
    outs = seqs if direct else 1

    def kernel(place_ref, *refs):
        out_refs, token_ref = refs[-1 - outs : -1], refs[-1]
        token_ref[...] = jnp.zeros(TOKEN.shape, TOKEN.dtype)
        start = pl.multiple_of(pl.program_id(0) * step, ROW_TILE)
        found = low(
            sum(
                lax.dot_general(
                    refs[c][pl.ds(start, rows), :],
                    refs[cores + c][...],
                    (((0,), (0,)), ((), ())),
                    preferred_element_type=jnp.float32,
                )
                for c in range(cores)
            )
        )
        if not direct:
            out_refs[0][0] = found
            return
        for s in range(seqs):
            slot_s = lax.rem(place_ref[1] - s + seqs, seqs)
            for slot in range(seqs):

                @pl.when(slot_s == slot)
                def _(s=s, slot=slot):
                    for t in range(tap_peers):
                        slot_t = lax.rem(place_ref[3] - t + tap_peers, tap_peers)
                        for a in range(acrosses):
                            slot_a = lax.rem(place_ref[2] - a + acrosses, acrosses)
                            base = ((t * seqs + s) * acrosses + a) * slab
                            out_refs[slot][slot_a, slot_t, 0] = found[base : base + slab]

    if direct:
        out_shape = (acrosses, tap_peers, taps, slab, lanes)
        out_spec = pl.BlockSpec(
            (acrosses, tap_peers, 1, slab, lanes), lambda k, place: (0, 0, k, 0, 0)
        )
    else:
        out_shape = (taps, inner, lanes)
        out_spec = pl.BlockSpec((1, inner, lanes), lambda k, place: (k, 0, 0))
    found = pl.pallas_call(
        kernel,
        grid_spec=pltpu.PrefetchScalarGridSpec(
            num_scalar_prefetch=1,
            grid=(taps,),
            in_specs=[pl.BlockSpec(extendeds[0].shape, lambda k, place: (0, 0))] * cores
            + [pl.BlockSpec((rows, lanes), lambda k, place: (0, place[0]))]
            + [pl.BlockSpec((rows, lanes), lambda k, place: (0, 0))] * (cores - 1)
            + tokens(after),
            out_specs=[out_spec] * outs + [TOKEN_SPEC],
        ),
        out_shape=[jax.ShapeDtypeStruct(out_shape, jnp.bfloat16)] * outs + [TOKEN],
        compiler_params=pltpu.CompilerParams(vmem_limit_bytes=VMEM_BYTES),
        cost_estimate=pl.CostEstimate(
            flops=2 * cores * taps * rows * inner * lanes,
            bytes_accessed=2
            * (cores * (extendeds[0].size + rows * lanes) + taps * inner * lanes),
            transcendentals=0,
        ),
        name="conv_weight_grad",
    )(jnp.stack(places).astype(jnp.int32), *extendeds, upstream, *arrived, *after)
    token = found[-1]
    if direct:
        return found[:-1], token
    found = found[0].reshape(taps, tap_peers, seqs, acrosses, slab, lanes)
    for axis, which in ((1, 3), (2, 1), (3, 2)):
        found = relative(found, axis, places[which], sizes[which])
    found = found.transpose(2, 3, 1, 0, 4, 5)
    return [found[s] for s in range(seqs)], token


def ffn_weight_grad(pairs, sizes, ffn_rows, after=()):
    cores, seqs, acrosses, tap_peers = sizes
    rows, width = pairs[0][1][0].shape
    block = tap_peers * ffn_rows
    if ffn_rows % ROW_TILE:
        found = jnp.stack(
            [
                low(
                    sum(
                        lax.dot_general(
                            left,
                            right,
                            (((0,), (0,)), ((), ())),
                            preferred_element_type=jnp.float32,
                        )
                        for left, right in zip(lefts, rights)
                    )
                ).reshape(acrosses, seqs, tap_peers, ffn_rows, width)
                for lefts, rights in pairs
            ],
            3,
        )
        return [found[a] for a in range(acrosses)], jnp.zeros(TOKEN.shape, TOKEN.dtype)

    def kernel(*refs):
        out_refs, token_ref = refs[-1 - acrosses : -1], refs[-1]
        token_ref[...] = jnp.zeros(TOKEN.shape, TOKEN.dtype)
        for which in range(2):
            base = 2 * cores * which
            found = low(
                sum(
                    lax.dot_general(
                        refs[base + c][...],
                        refs[base + cores + c][...],
                        (((0,), (0,)), ((), ())),
                        preferred_element_type=jnp.float32,
                    )
                    for c in range(cores)
                )
            ).reshape(tap_peers, ffn_rows, width)
            for a in range(acrosses):

                @pl.when(pl.program_id(0) // seqs == a)
                def _(a=a):
                    out_refs[a][0, :, which] = found

    left_spec = pl.BlockSpec((rows, block), lambda g: (0, g))
    right_spec = pl.BlockSpec((rows, width), lambda g: (0, 0))

    def out_spec(a):
        return pl.BlockSpec(
            (1, tap_peers, 2, ffn_rows, width),
            lambda g: (jnp.clip(g - a * seqs, 0, seqs - 1), 0, 0, 0, 0),
        )

    shape = jax.ShapeDtypeStruct((seqs, tap_peers, 2, ffn_rows, width), jnp.bfloat16)
    found = pl.pallas_call(
        kernel,
        grid=(acrosses * seqs,),
        in_specs=([left_spec] * cores + [right_spec] * cores) * 2 + tokens(after),
        out_specs=[out_spec(a) for a in range(acrosses)] + [TOKEN_SPEC],
        out_shape=[shape] * acrosses + [TOKEN],
        compiler_params=pltpu.CompilerParams(vmem_limit_bytes=VMEM_BYTES),
        cost_estimate=pl.CostEstimate(
            flops=4 * cores * rows * acrosses * seqs * block * width,
            bytes_accessed=4
            * (cores * rows * (acrosses * seqs * block + width) + acrosses * seqs * block * width),
            transcendentals=0,
        ),
        name="ffn_weight_grad",
    )(*pairs[0][0], *pairs[0][1], *pairs[1][0], *pairs[1][1], *after)
    return found[:-1], found[-1]


def close_ffn_grads(parts, ffn_rows, after=()):
    blocks, count = len(parts), len(parts[0])
    width = parts[0][0].shape[-1]
    flat = [part.reshape(2, ffn_rows, width) for block in parts for part in block]
    if ffn_rows % ROW_TILE:
        sums = [sum(wide(part) for part in flat[b * count :][:count]) for b in range(blocks)]
        return jnp.stack([each[0].T for each in sums]), jnp.stack([each[1] for each in sums])

    def kernel(*refs):
        in_ref, out_ref = refs[-2:]
        for b in range(blocks):
            total = sum(wide(refs[b * count + i][...]) for i in range(count))
            in_ref[b] = total[0].T
            out_ref[b] = total[1]

    return pl.pallas_call(
        kernel,
        out_shape=(
            jax.ShapeDtypeStruct((blocks, width, ffn_rows), jnp.float32),
            jax.ShapeDtypeStruct((blocks, ffn_rows, width), jnp.float32),
        ),
        compiler_params=pltpu.CompilerParams(vmem_limit_bytes=VMEM_BYTES),
        name="close_ffn_grads",
    )(*flat)


def add_slots(parts, slots, after=()):
    lanes = parts[0].shape[-1]
    rows = parts[0].size // (slots * lanes)
    parts = [part.reshape(slots, rows, lanes) for part in parts]
    block = rows // 4 if rows % (4 * ROW_TILE) == 0 else rows

    def kernel(*refs):
        out_refs, token_ref = refs[-1 - slots : -1], refs[-1]
        token_ref[...] = jnp.zeros(TOKEN.shape, TOKEN.dtype)
        for slot in range(slots):
            out_refs[slot][...] = low(sum(wide(refs[i][slot]) for i in range(len(parts))))

    found = pl.pallas_call(
        kernel,
        grid=(rows // block,),
        in_specs=[pl.BlockSpec((slots, block, lanes), lambda g: (0, g, 0))] * len(parts)
        + tokens(after),
        out_specs=[pl.BlockSpec((block, lanes), lambda g: (g, 0))] * slots + [TOKEN_SPEC],
        out_shape=[jax.ShapeDtypeStruct((rows, lanes), jnp.bfloat16)] * slots + [TOKEN],
        compiler_params=pltpu.CompilerParams(vmem_limit_bytes=VMEM_BYTES),
        cost_estimate=pl.CostEstimate(
            flops=len(parts) * slots * rows * lanes,
            bytes_accessed=2 * (len(parts) + 1) * slots * rows * lanes,
            transcendentals=0,
        ),
        name="add_slots",
    )(*parts, *after)
    return found[:slots], found[slots]


def place_conv_grads(pieces, places, sizes):
    cores, seqs, acrosses = sizes[:3]
    taps, slab, lanes = pieces[0][0][0][0].shape
    channels = slab * seqs * acrosses
    blocks = len(pieces)
    if slab % ROW_TILE:
        full = jnp.stack(
            [
                jnp.stack([jnp.stack([jnp.stack(row) for row in plane]) for plane in block])
                for block in pieces
            ]
        )
        for axis, (place, size) in enumerate(zip(places[:3], sizes[:3])):
            full = relative(full, axis + 1, place, size)
        return wide(
            full.transpose(0, 4, 2, 3, 5, 1, 6).reshape(blocks, taps, channels, cores * lanes)
        )
    flat = [piece for block in pieces for plane in block for row in plane for piece in row]

    def kernel(place_ref, *refs):
        out_ref = refs[-1]
        for b in range(blocks):
            for c in range(cores):
                lane = pl.multiple_of(lax.rem(place_ref[0] - c + cores, cores) * lanes, lanes)
                for s in range(seqs):
                    at_s = lax.rem(place_ref[1] - s + seqs, seqs)
                    for a in range(acrosses):
                        at_a = lax.rem(place_ref[2] - a + acrosses, acrosses)
                        row = pl.multiple_of((at_s * acrosses + at_a) * slab, slab)
                        piece = refs[((b * cores + c) * seqs + s) * acrosses + a]
                        out_ref[b, 0, pl.ds(row, slab), pl.ds(lane, lanes)] = wide(piece[0])

    return pl.pallas_call(
        kernel,
        grid_spec=pltpu.PrefetchScalarGridSpec(
            num_scalar_prefetch=1,
            grid=(taps,),
            in_specs=[pl.BlockSpec((1, slab, lanes), lambda k, place: (k, 0, 0))] * len(flat),
            out_specs=pl.BlockSpec(
                (blocks, 1, channels, cores * lanes), lambda k, place: (0, k, 0, 0)
            ),
        ),
        out_shape=jax.ShapeDtypeStruct((blocks, taps, channels, cores * lanes), jnp.float32),
        compiler_params=pltpu.CompilerParams(vmem_limit_bytes=VMEM_BYTES),
        cost_estimate=pl.CostEstimate(
            flops=0,
            bytes_accessed=6 * blocks * taps * channels * cores * lanes,
            transcendentals=0,
        ),
        name="place_conv_grads",
    )(jnp.stack(places[:3]).astype(jnp.int32), *flat)


def copy_all(copies):
    for copy in copies:
        copy.start()
    for copy in copies:
        copy.wait()


def place_conv(pieces, places, sizes, after=()):
    cores, seqs, acrosses, tap_peers = sizes
    taps, slab, lanes = pieces[0][0].shape[2:]
    inner = slab * seqs * acrosses * tap_peers
    if slab % ROW_TILE:
        full = jnp.stack([jnp.stack(row) for row in pieces])
        for axis, (place, size) in enumerate(zip(places, sizes)):
            full = relative(full, axis, place, size)
        return full.transpose(4, 3, 1, 2, 5, 0, 6).reshape(taps, inner, cores * lanes)
    flat = [piece for row in pieces for piece in row]

    def kernel(place_ref, *refs):
        sem_ref, out_ref = refs[-1], refs[-2]
        copies = []
        for c in range(cores):
            lane = lax.rem(place_ref[0] - c + cores, cores) * lanes
            for s in range(seqs):
                at_s = lax.rem(place_ref[1] - s + seqs, seqs)
                for a in range(acrosses):
                    at_a = lax.rem(place_ref[2] - a + acrosses, acrosses)
                    for t in range(tap_peers):
                        at_t = lax.rem(place_ref[3] - t + tap_peers, tap_peers)
                        row = ((at_t * seqs + at_s) * acrosses + at_a) * slab
                        copies.append(
                            pltpu.make_async_copy(
                                refs[c * seqs + s].at[a, t],
                                out_ref.at[
                                    :,
                                    pl.ds(pl.multiple_of(row, slab), slab),
                                    pl.ds(pl.multiple_of(lane, lanes), lanes),
                                ],
                                sem_ref.at[len(copies)],
                            )
                        )
        copy_all(copies)

    return pl.pallas_call(
        kernel,
        in_specs=[SCALARS] + [ANYWHERE] * len(flat) + [WHOLE] * len(after),
        out_specs=WHOLE,
        out_shape=jax.ShapeDtypeStruct((taps, inner, cores * lanes), jnp.bfloat16),
        scratch_shapes=[pltpu.SemaphoreType.DMA((cores * seqs * acrosses * tap_peers,))],
        compiler_params=pltpu.CompilerParams(vmem_limit_bytes=VMEM_BYTES),
        cost_estimate=pl.CostEstimate(
            flops=0, bytes_accessed=4 * taps * inner * cores * lanes, transcendentals=0
        ),
        name="place_conv",
    )(jnp.stack(places).astype(jnp.int32), *flat, *after)


def place_ffn(pieces, sizes):
    cores, seqs, acrosses, tap_peers = sizes
    cuts, ffn_rows, lanes = pieces[0][0].shape[2:]
    cuts //= 2
    width = cuts * lanes
    units = seqs * acrosses * tap_peers * ffn_rows
    if ffn_rows % ROW_TILE:
        full = jnp.stack([jnp.stack(row) for row in pieces])
        full = full.reshape(cores, acrosses, seqs, tap_peers, 2, cuts, ffn_rows, lanes)
        full = full.transpose(4, 0, 1, 2, 3, 6, 5, 7).reshape(2, cores, units, width)
        return [full[0, c] for c in range(cores)], [full[1, c] for c in range(cores)]
    flat = [piece for row in pieces for piece in row]

    def kernel(*refs):
        out_refs, sem_ref = refs[-1 - 2 * cores : -1], refs[-1]
        copies = []
        for c in range(cores):
            for a in range(acrosses):
                for which in range(2):
                    for cut in range(cuts):
                        copies.append(
                            pltpu.make_async_copy(
                                refs[c * acrosses + a].at[:, :, which * cuts + cut],
                                out_refs[which * cores + c].at[
                                    a, :, :, :, pl.ds(cut * lanes, lanes)
                                ],
                                sem_ref.at[len(copies)],
                            )
                        )
        copy_all(copies)

    shape = jax.ShapeDtypeStruct((acrosses, seqs, tap_peers, ffn_rows, width), jnp.bfloat16)
    found = pl.pallas_call(
        kernel,
        in_specs=[ANYWHERE] * len(flat),
        out_specs=[WHOLE] * (2 * cores),
        out_shape=[shape] * (2 * cores),
        scratch_shapes=[pltpu.SemaphoreType.DMA((2 * cores * acrosses * cuts,))],
        compiler_params=pltpu.CompilerParams(vmem_limit_bytes=VMEM_BYTES),
        cost_estimate=pl.CostEstimate(
            flops=0, bytes_accessed=8 * cores * units * width, transcendentals=0
        ),
        name="place_ffn",
    )(*flat)
    found = [each.reshape(units, width) for each in found]
    return found[:cores], found[cores:]


class Ring:
    def __init__(self, axis, size, index, pairs):
        self.axis, self.size, self.index, self.pairs = axis, size, index, pairs

    def shifted(self, value, by):
        return lax.ppermute(value, self.axis, self.pairs(lambda i: (i + by) % self.size))

    def swapped(self, value, bit):
        return lax.ppermute(value, self.axis, self.pairs(lambda i: i ^ bit))

    def gather(self, value):
        return [value] + [self.shifted(value, by) for by in range(1, self.size)]

    def swap(self, values):
        return [values[0]] + [self.shifted(values[by], -by) for by in range(1, self.size)]


def relative(value, axis, place, size):
    if size == 1:
        return value
    return jnp.stack(
        [
            lax.dynamic_index_in_dim(value, (place - slot) % size, axis, False)
            for slot in range(size)
        ],
        axis,
    )


def rings():
    peers = lax.axis_size("dp")
    cores = CORES if peers % CORES == 0 else 1
    columns = peers // cores
    place = lax.axis_index("dp")

    def plain(axis):
        size = lax.axis_size(axis)
        return Ring(
            axis, size, lax.axis_index(axis), lambda move: [(i, move(i)) for i in range(size)]
        )

    across = Ring(
        "dp",
        columns,
        place // cores,
        lambda move: [(i, move(i // cores) * cores + i % cores) for i in range(peers)],
    )
    core = Ring(
        "dp",
        cores,
        place % cores,
        lambda move: [(i, i // cores * cores + move(i % cores)) for i in range(peers)],
    )
    return core, across, plain("seq"), plain("tap")


class Reduce:
    def __init__(self, terms, order):
        self.order = order
        self.parts = [terms[0]] + [order[0].shifted(terms[s], -s) for s in range(1, order[0].size)]

    def step(self, level, after):
        ring = self.order[level]
        found, token = add_slots(self.parts, ring.size, after)
        self.parts = [found[0]] + [ring.shifted(found[s], -s) for s in range(1, ring.size)]
        return (token,)

    def total(self):
        return sum(wide(part) for part in self.parts)


def gate(*arrays):
    return sum(wide(each[(0,) * each.ndim]) for each in arrays) * 0.0


def summed(value, order):
    if any(ring.size & (ring.size - 1) for ring in order):
        return lax.psum(value, ("dp", "seq", "tap"))
    for ring in order:
        bit = 1
        while bit < ring.size:
            value = value + ring.swapped(value, bit)
            bit *= 2
    return value


def passed_along(value, axis, by):
    peers = lax.axis_size(axis)
    pairs = [(i, i + by) for i in range(peers) if 0 <= i + by < peers]
    return lax.ppermute(value, axis, pairs)


def extend(source, reach_rows):
    span_rows = source.shape[0]
    left_parts = []
    right_parts = []
    distances = -(-reach_rows // span_rows)
    for distance in range(1, distances + 1):
        rim_count = min(span_rows, reach_rows - (distance - 1) * span_rows)
        for direction in (1, -1):
            rim_piece = (
                source[span_rows - rim_count :] if direction == 1 else source[:rim_count]
            )
            arrived = passed_along(rim_piece, "seq", direction * distance)
            if direction == 1:
                left_parts.insert(0, arrived)
            else:
                right_parts.append(arrived)
    return jnp.concatenate(left_parts + [source] + right_parts, axis=0)


def to_rows(values):
    windows, positions = values.shape[:2]
    cut = values.reshape((windows, positions // FIRST_DILATION, FIRST_DILATION) + values.shape[2:])
    return jnp.swapaxes(cut, 0, 1).reshape((windows * positions,) + values.shape[2:])


def from_rows(values, windows):
    cut = values.reshape((-1, windows, FIRST_DILATION) + values.shape[1:])
    return jnp.swapaxes(cut, 0, 1).reshape((windows, -1) + values.shape[1:])


def on_device(
    inputs,
    targets,
    masked,
    conv_weight,
    conv_bias,
    gains,
    shifts,
    in_weight,
    in_bias,
    out_weight,
    out_bias,
    head_weight,
):
    core, across, seq, tap = rings()
    taps = conv_weight.shape[1]
    channels = conv_weight.shape[2]
    width = conv_weight.shape[3]
    slab = channels // (seq.size * across.size)
    lanes = width // core.size
    hidden_width = in_bias.shape[1]
    ffn_rows = in_weight.shape[2]
    windows = inputs.shape[0]
    rows = windows * inputs.shape[1]
    steps = (FIRST_DILATION * windows, SECOND_DILATION * windows)
    units = hidden_width // core.size
    classes = jnp.arange(head_weight.shape[1], dtype=jnp.int32)
    places = (core.index, seq.index, across.index, tap.index)
    sizes = (core.size, seq.size, across.size, tap.size)

    in_bias_placed = []
    for b in range(2):
        bias = in_bias[b].reshape(across.size, core.size, seq.size, tap.size, ffn_rows)
        for axis, ring in enumerate((across, core, seq, tap)):
            bias = relative(bias, axis, ring.index, ring.size)
        in_bias_placed.append(bias.transpose(1, 0, 2, 3, 4).reshape(core.size, units))

    def cut_ffn(piece):
        return piece.reshape(ffn_rows, core.size, lanes).swapaxes(0, 1).reshape(-1, lanes)

    def bundle(b, ready):
        conv_piece = lax.dynamic_slice(
            conv_weight[b],
            (0, (seq.index * across.size + across.index) * slab, core.index * lanes),
            (taps, slab, lanes),
        )
        pieces = [
            conv_piece.reshape(taps * slab, lanes),
            cut_ffn(in_weight[b].T),
            cut_ffn(out_weight[b]),
        ]
        return jnp.concatenate(pieces) + low(ready)

    def stacked(parts, ready):
        conv_part = jnp.stack([part[: taps * slab] for part in parts]) + low(ready)
        ffn_part = jnp.stack([part[taps * slab :] for part in parts]) + low(ready)
        return (
            conv_part.reshape(-1, taps, slab, lanes),
            ffn_part.reshape(-1, 2 * core.size, ffn_rows, lanes),
        )

    class Weights:
        def __init__(self, b, ready):
            self.tap_parts = tap.gather(bundle(b, ready))

        def first(self, ready):
            conv_part, ffn_part = stacked(self.tap_parts, ready)
            self.started = gate(conv_part, ffn_part)
            self.conv_parts = across.gather(conv_part)
            self.ffn_parts = seq.gather(ffn_part)

        def second(self):
            conv_part = jnp.stack(self.conv_parts)
            ffn_part = jnp.stack(self.ffn_parts)
            self.conv_parts = seq.gather(conv_part)
            self.ffn_parts = across.gather(ffn_part)
            self.started = gate(conv_part, ffn_part)
            self.arrived = gate(*self.conv_parts[1:], *self.ffn_parts[1:])

        def third(self):
            self.conv_parts = [core.gather(each) for each in self.conv_parts]
            self.ffn_parts = [core.gather(each) for each in self.ffn_parts]

        def conv(self, after=()):
            parts = self.conv_parts
            return place_conv(
                [[part[c] for part in parts] for c in range(core.size)], places, sizes, after
            )

        def ffn(self):
            parts = self.ffn_parts
            return place_ffn([[part[c] for part in parts] for c in range(core.size)], sizes)

    weights = [Weights(0, jnp.zeros((), jnp.float32))]
    weights.append(Weights(1, gate(*weights[0].tap_parts[1:])))
    weights[0].first(jnp.zeros((), jnp.float32))
    weights[0].second()
    weights[1].first(weights[0].arrived)
    weights[0].third()
    conv_full = [weights[0].conv((jnp.full(TOKEN.shape, weights[1].started),)), None]
    in_full, out_full = [None, None], [None, None]
    in_full[0], out_full[0] = weights[0].ffn()

    conv_input = to_rows(inputs)
    stream = wide(conv_input)
    flat_masked = wide(to_rows(masked))
    flat_targets = to_rows(targets)
    saved = []
    for b in range(2):
        if b == 1:
            weights[1].third()
            conv_full[1] = weights[1].conv()
            in_full[1], out_full[1] = weights[1].ffn()
        reach = taps // 2 * steps[b]
        extended = extend(conv_input, reach)
        extendeds = [extended] + [core.shifted(extended, -c) for c in range(1, core.size)]
        conv_out = conv_forward(extended, conv_full[b], steps[b], rows) + conv_bias[b]
        conv_gelu, conv_slope = gelu_parts(conv_out)
        normed_conv, scale_conv = normalize(conv_gelu)
        stream = stream + normed_conv * gains[b, 0] + shifts[b, 0]
        if b == 0:
            weights[1].second()
            stream = stream + weights[1].started
        lowered = low(stream)
        lowereds = [lowered] + [core.shifted(lowered, -c) for c in range(1, core.size)]
        actives, hidden_slopes = [], []
        ffn_out = out_bias[b]
        for c in range(core.size - 1, -1, -1):
            hidden = (
                jnp.einsum("rd,fd->rf", lowered, in_full[b][c], preferred_element_type=jnp.float32)
                + in_bias_placed[b][c]
            )
            active, hidden_slope = gelu_parts(hidden)
            actives.insert(0, low(active))
            hidden_slopes.insert(0, low(hidden_slope))
            ffn_out = ffn_out + jnp.dot(
                actives[0], out_full[b][c], preferred_element_type=jnp.float32
            )
        normed_ffn, scale_ffn = normalize(ffn_out)
        stream = stream + normed_ffn * gains[b, 1] + shifts[b, 1]
        conv_input = low(stream)
        saved.append(
            (
                extendeds,
                conv_slope,
                normed_conv,
                scale_conv,
                lowereds,
                core.swap(actives),
                hidden_slopes,
                normed_ffn,
                scale_ffn,
            )
        )

    final_state = from_rows(conv_input, windows)
    logits = jnp.dot(stream, head_weight, precision=HIGHEST_PRECISION)
    peak_value = jnp.max(logits, -1, keepdims=True)
    exponent = jnp.exp(logits - peak_value)
    denominator = jnp.sum(exponent, -1, keepdims=True)
    log_total = peak_value[:, 0] + jnp.log(denominator[:, 0])
    one_hot = wide(flat_targets[:, None] == classes)
    picked = jnp.sum(one_hot * logits, -1)
    objective = jnp.sum(flat_masked * (log_total - picked))
    logit_grad = flat_masked[:, None] * (exponent / denominator - one_hot)
    head_grad = jnp.einsum("rd,rn->dn", stream, logit_grad, precision=HIGHEST_PRECISION)
    stream_grad = jnp.einsum("rn,dn->rd", logit_grad, head_weight, precision=HIGHEST_PRECISION)

    conv_bias_grads = [None, None]
    gain_grads = [[None, None], [None, None]]
    shift_grads = [[None, None], [None, None]]
    in_bias_grads = [None, None]
    out_bias_grads = [None, None]
    ffn_sums = [None, None]
    conv_sums = [None, None]
    last = ()
    for b in (1, 0):
        (
            extendeds,
            conv_slope,
            normed_conv,
            scale_conv,
            lowereds,
            actives,
            hidden_slopes,
            normed_ffn,
            scale_ffn,
        ) = saved[b]
        reach = taps // 2 * steps[b]
        gain_grads[b][1] = jnp.sum(stream_grad * normed_ffn, 0)
        shift_grads[b][1] = jnp.sum(stream_grad, 0)
        output_grad = low(norm_back(stream_grad * gains[b, 1], normed_ffn, scale_ffn))
        output_grads = [output_grad] + [core.shifted(output_grad, -c) for c in range(1, core.size)]
        hidden_grads = []
        for c in range(core.size - 1, -1, -1):
            active_grad = jnp.einsum(
                "rd,fd->rf", output_grad, out_full[b][c], preferred_element_type=jnp.float32
            )
            hidden_grads.insert(0, low(active_grad * wide(hidden_slopes[c])))
        for c in range(core.size - 1, -1, -1):
            stream_grad = stream_grad + jnp.dot(
                hidden_grads[c], in_full[b][c], preferred_element_type=jnp.float32
            )
        out_bias_grads[b] = jnp.sum(wide(output_grad), 0)
        bias = jnp.stack([jnp.sum(wide(each), 0) for each in hidden_grads]).reshape(
            core.size, across.size, seq.size, tap.size, ffn_rows
        )
        for axis, ring in enumerate((core, across, seq, tap)):
            bias = relative(bias, axis, ring.index, ring.size)
        in_bias_grads[b] = bias.transpose(1, 0, 2, 3, 4).reshape(hidden_width)
        hidden_grads = core.swap(hidden_grads)
        gain_grads[b][0] = jnp.sum(stream_grad * normed_conv, 0)
        shift_grads[b][0] = jnp.sum(stream_grad, 0)
        conv_grad = low(
            norm_back(stream_grad * gains[b, 0], normed_conv, scale_conv) * conv_slope
        )
        conv_bias_grads[b] = jnp.sum(wide(conv_grad), 0)
        arrived = [
            core.shifted(
                lax.dynamic_slice_in_dim(conv_grad, (core.index - c) % core.size * lanes, lanes, 1),
                -c,
            )
            for c in range(1, core.size)
        ]

        def ffn_grads(last):
            found, token = ffn_weight_grad(
                ((hidden_grads, lowereds), (actives, output_grads)), sizes, ffn_rows, last
            )
            return Reduce(found, (across, seq, tap)), (token,)

        def conv_grads(last):
            found, token = conv_weight_grad(
                extendeds, conv_grad, arrived, places, sizes, taps, steps[b], last
            )
            found = [each.reshape(-1, lanes) for each in found]
            return Reduce(found, (seq, across, tap)), (token,)

        if b == 1:
            ffn_sums[1], last = ffn_grads(())
            conv_sums[1], last = conv_grads(last)
        else:
            last = ffn_sums[1].step(1, last)
            last = conv_sums[1].step(1, last)
            conv_sums[0], last = conv_grads(last)
            last = ffn_sums[1].step(2, last)
            last = conv_sums[1].step(2, last)
            ffn_sums[0], last = ffn_grads(last)
        split_grad, token = conv_data_grad(
            extend(conv_grad, reach), conv_full[b], steps[b], rows, last
        )
        last = (token,)
        stream_grad = stream_grad + wide(split_grad)

    last = conv_sums[0].step(1, last)
    last = ffn_sums[0].step(1, last)
    grad_inputs = from_rows(low(stream_grad), windows)
    last = conv_sums[0].step(2, last)
    last = ffn_sums[0].step(2, last)
    grad_in, grad_out = close_ffn_grads([each.parts for each in ffn_sums], ffn_rows)

    pieces = []
    for b in range(2):
        shard = low(conv_sums[b].total()).reshape(taps, slab, lanes)
        slots = [seq.gather(each) for each in across.gather(shard)]
        slots = [[core.gather(each) for each in row] for row in slots]
        pieces.append(
            [
                [[slots[a][s][c] for a in range(across.size)] for s in range(seq.size)]
                for c in range(core.size)
            ]
        )
    grad_conv = place_conv_grads(pieces, places, sizes)

    small = [
        jnp.stack(conv_bias_grads),
        jnp.stack([jnp.stack(gain_grads[b]) for b in range(2)]),
        jnp.stack([jnp.stack(shift_grads[b]) for b in range(2)]),
        jnp.stack(in_bias_grads),
        jnp.stack(out_bias_grads),
        head_grad.T,
        jnp.pad(jnp.stack([objective, jnp.sum(flat_masked)]), (0, width - 2)),
    ]
    packed = jnp.concatenate([each.reshape(-1, width) for each in small])
    packed = summed(packed, (core, across, seq, tap))
    unpacked = []
    first = 0
    for each in small:
        count = each.size // width
        unpacked.append(packed[first : first + count].reshape(each.shape))
        first += count
    (
        grad_conv_bias,
        grad_gains,
        grad_shifts,
        grad_in_bias,
        grad_out_bias,
        grad_head_weight,
        loss_terms,
    ) = unpacked
    return (
        final_state,
        grad_inputs,
        grad_conv,
        grad_conv_bias,
        grad_gains,
        grad_shifts,
        grad_in,
        grad_in_bias,
        grad_out,
        grad_out_bias,
        grad_head_weight.T,
        loss_terms[0] / loss_terms[1],
    )


def solution(mesh):
    placed = (
        P(("dp", "tap"), "seq", None),
        P(("dp", "tap"), "seq"),
        P(("dp", "tap"), "seq"),
        P(None, None, "tap", None),
        P(),
        P(),
        P(),
        P(None, None, ("dp", "seq", "tap")),
        P(),
        P(None, ("dp", "seq", "tap"), None),
        P(),
        P(),
    )
    return jax.shard_map(
        on_device,
        mesh=mesh,
        in_specs=placed,
        out_specs=(
            P(("dp", "tap"), "seq", None),
            P(("dp", "tap"), "seq", None),
            P(None, None, "tap", None),
            P(),
            P(),
            P(),
            P(None, None, ("dp", "seq", "tap")),
            P(),
            P(None, ("dp", "seq", "tap"), None),
            P(),
            P(),
            P(),
        ),
        check_vma=False,
    )
```

```python
import functools

import jax
import jax.numpy as jnp
from jax import lax
from jax.experimental import pallas as pl
from jax.experimental.pallas import tpu as pltpu
from jax.sharding import PartitionSpec as P

FIRST_DILATION = 4
SECOND_DILATION = 32
EPSILON = 1e-05
HIGHEST_PRECISION = lax.Precision.HIGHEST
CORES = 2
ROW_TILE = 16
VMEM_BYTES = 48 * 1024 * 1024
ANYWHERE = pl.BlockSpec(memory_space=pl.ANY)
SCALARS = pl.BlockSpec(memory_space=pltpu.SMEM)


TOKEN = jax.ShapeDtypeStruct((8, 128), jnp.float32)
SMALL_COST = pl.CostEstimate(flops=1024, bytes_accessed=1024, transcendentals=0)
WHOLE = pl.BlockSpec(memory_space=pltpu.VMEM)
TOKEN_SPEC = pl.BlockSpec(TOKEN.shape, lambda *_: (0, 0))


def tokens(after):
    return [TOKEN_SPEC] * len(after)


def low(values):
    return values.astype(jnp.bfloat16)


def wide(values):
    return values.astype(jnp.float32)


def gelu_parts(values):
    phi = 0.5 * (1.0 + lax.erf(values * 0.7071067811865476))
    return (
        values * phi,
        phi + values * jnp.exp(-0.5 * values * values) * 0.3989422804014327,
    )


def normalize(values):
    center = values - jnp.mean(values, -1, keepdims=True)
    scale = lax.rsqrt(jnp.mean(center * center, -1, keepdims=True) + EPSILON)
    return (center * scale, scale)


def norm_back(upstream, normed, scale):
    return scale * (
        upstream
        - jnp.mean(upstream, -1, keepdims=True)
        - normed * jnp.mean(upstream * normed, -1, keepdims=True)
    )


def tap_groups(taps):
    return 3 if taps % 3 == 0 else 1


def row_chunks(rows, most):
    size = min(rows, most)
    return [(first, size) for first in range(0, rows, size)]


def conv_forward(extended, weight, stream, bias, gain, shift, step, after=()):
    taps, inner, width = weight.shape
    rows = stream.shape[0]
    group = tap_groups(taps)
    steps = taps // group

    def kernel(extended_ref, weight_ref, stream_ref, bias_ref, gain_ref, shift_ref, *refs):
        normed_ref, slope_ref, next_ref, lowered_ref, token_ref, total_ref = refs[-6:]
        token_ref[...] = jnp.zeros(TOKEN.shape, TOKEN.dtype)
        first = pl.program_id(0) * group
        total = None
        for j in range(group):
            start = pl.multiple_of((first + j) * step, ROW_TILE)
            term = jnp.dot(
                extended_ref[pl.ds(start, rows), :],
                weight_ref[j],
                preferred_element_type=jnp.float32,
            )
            total = term if total is None else total + term

        @pl.when(pl.program_id(0) == 0)
        def _():
            total_ref[...] = total

        @pl.when(pl.program_id(0) > 0)
        def _():
            total_ref[...] += total

        @pl.when(pl.program_id(0) == steps - 1)
        def _():
            for at, size in row_chunks(rows, 128):
                some = pl.ds(at, size)
                value, slope = gelu_parts(total_ref[some, :] + bias_ref[...])
                normed, scale = normalize(value)
                mid = wide(stream_ref[some, :]) + normed * gain_ref[...] + shift_ref[...]
                normed_ref[some, :] = low(normed)
                slope_ref[some, :] = low(scale * slope)
                next_ref[some, :] = mid
                lowered_ref[some, :] = low(mid)

    whole = pl.BlockSpec((rows, width), lambda g: (0, 0))
    row = pl.BlockSpec((1, width), lambda g: (0, 0))
    found = pl.pallas_call(
        kernel,
        grid=(steps,),
        in_specs=[
            pl.BlockSpec(extended.shape, lambda g: (0, 0)),
            pl.BlockSpec((group, inner, width), lambda g: (g, 0, 0)),
            whole,
            row,
            row,
            row,
        ]
        + tokens(after),
        out_specs=[whole] * 4 + [TOKEN_SPEC],
        out_shape=[
            jax.ShapeDtypeStruct((rows, width), jnp.bfloat16),
            jax.ShapeDtypeStruct((rows, width), jnp.bfloat16),
            jax.ShapeDtypeStruct((rows, width), jnp.float32),
            jax.ShapeDtypeStruct((rows, width), jnp.bfloat16),
            TOKEN,
        ],
        scratch_shapes=[pltpu.VMEM((rows, width), jnp.float32)],
        compiler_params=pltpu.CompilerParams(vmem_limit_bytes=VMEM_BYTES),
        cost_estimate=SMALL_COST,
        name="conv_forward",
    )(extended, weight, stream, bias[None], gain[None], shift[None], *after)
    return found[:4], (found[4],)


def ffn_forward(lowered, stream, ins, outs, in_biases, out_bias, gain, shift, after=()):
    rows, width = lowered.shape
    cores = len(ins)
    units = ins[0].shape[0]
    block = min(units, 256)
    steps = units // block

    def kernel(lowered_ref, stream_ref, out_bias_ref, gain_ref, shift_ref, *refs):
        in_refs, out_refs, bias_refs = (refs[i * cores : (i + 1) * cores] for i in range(3))
        found_refs = refs[-6 - 2 * cores :]
        active_refs, slope_refs = found_refs[:cores], found_refs[cores : 2 * cores]
        normed_ref, scale_ref, next_ref, rounded_ref, token_ref, total_ref = found_refs[-6:]
        token_ref[...] = jnp.zeros(TOKEN.shape, TOKEN.dtype)

        @pl.when(pl.program_id(0) == 0)
        def _():
            total_ref[...] = jnp.zeros(total_ref.shape, jnp.float32)

        for at, size in row_chunks(rows, 512):
            some = pl.ds(at, size)
            term = None
            for c in range(cores):
                hidden = lax.dot_general(
                    lowered_ref[some, :],
                    in_refs[c][...],
                    (((1,), (1,)), ((), ())),
                    preferred_element_type=jnp.float32,
                )
                active, slope = gelu_parts(hidden + bias_refs[c][...])
                active = low(active)
                active_refs[c][some, :] = active
                slope_refs[c][some, :] = low(slope)
                found = jnp.dot(active, out_refs[c][...], preferred_element_type=jnp.float32)
                term = found if term is None else term + found
            total_ref[some, :] += term

        @pl.when(pl.program_id(0) == steps - 1)
        def _():
            for at, size in row_chunks(rows, 128):
                some = pl.ds(at, size)
                normed, scale = normalize(total_ref[some, :] + out_bias_ref[...])
                after_ffn = stream_ref[some, :] + normed * gain_ref[...] + shift_ref[...]
                normed_ref[some, :] = low(normed)
                scale_ref[some, :] = scale
                next_ref[some, :] = after_ffn
                rounded_ref[some, :] = low(after_ffn)

    whole = pl.BlockSpec((rows, width), lambda g: (0, 0))
    row = pl.BlockSpec((1, width), lambda g: (0, 0))
    piece = pl.BlockSpec((block, width), lambda g: (g, 0))
    columns = pl.BlockSpec((rows, block), lambda g: (0, g))
    hidden_shape = jax.ShapeDtypeStruct((rows, units), jnp.bfloat16)
    found = pl.pallas_call(
        kernel,
        grid=(steps,),
        in_specs=[whole, whole, row, row, row]
        + [piece] * (2 * cores)
        + [pl.BlockSpec((1, block), lambda g: (0, g))] * cores
        + tokens(after),
        out_specs=[columns] * (2 * cores)
        + [whole, pl.BlockSpec((rows, 1), lambda g: (0, 0)), whole, whole, TOKEN_SPEC],
        out_shape=[hidden_shape] * (2 * cores)
        + [
            jax.ShapeDtypeStruct((rows, width), jnp.bfloat16),
            jax.ShapeDtypeStruct((rows, 1), jnp.float32),
            jax.ShapeDtypeStruct((rows, width), jnp.float32),
            jax.ShapeDtypeStruct((rows, width), jnp.bfloat16),
            TOKEN,
        ],
        scratch_shapes=[pltpu.VMEM((rows, width), jnp.float32)],
        compiler_params=pltpu.CompilerParams(vmem_limit_bytes=VMEM_BYTES),
        cost_estimate=SMALL_COST,
        name="ffn_forward",
    )(
        lowered,
        stream,
        out_bias[None],
        gain[None],
        shift[None],
        *ins,
        *outs,
        *[each[None] for each in in_biases],
        *after,
    )
    return found[:cores], found[cores : 2 * cores], found[2 * cores : -1], (found[-1],)


def head_and_loss(stream, head_weight, targets, masked, after=()):
    rows, width = stream.shape
    classes = head_weight.shape[1]
    padded = jnp.pad(head_weight, ((0, 0), (0, 128 - classes)))
    cuts = row_chunks(rows, 256)

    def kernel(stream_ref, head_ref, target_ref, mask_ref, *refs):
        grad_ref, head_grad_ref, sums_ref, token_ref = refs[-4:]
        token_ref[...] = jnp.zeros(TOKEN.shape, TOKEN.dtype)
        head_grad = jnp.zeros((128, width), jnp.float32)
        objective = jnp.zeros((1, 1), jnp.float32)
        scored = jnp.zeros((1, 1), jnp.float32)
        for at, size in cuts:
            some = pl.ds(at, size)
            value = stream_ref[some, :]
            mask = mask_ref[some, :]
            logits = jnp.dot(
                value, head_ref[...], precision=HIGHEST_PRECISION, preferred_element_type=jnp.float32
            )
            lane = lax.broadcasted_iota(jnp.int32, logits.shape, 1)
            valid = lane < classes
            peak = jnp.max(jnp.where(valid, logits, -jnp.inf), -1, keepdims=True)
            exponent = jnp.where(valid, jnp.exp(jnp.where(valid, logits - peak, 0.0)), 0.0)
            denominator = jnp.sum(exponent, -1, keepdims=True)
            chosen = lane == target_ref[some, :]
            picked = jnp.sum(jnp.where(chosen, logits, 0.0), -1, keepdims=True)
            terms = mask * (peak + jnp.log(denominator) - picked)
            objective = objective + jnp.sum(terms, 0, keepdims=True)
            scored = scored + jnp.sum(mask, 0, keepdims=True)
            logit_grad = mask * (exponent / denominator - jnp.where(chosen, 1.0, 0.0))
            grad_ref[some, :] = lax.dot_general(
                logit_grad,
                head_ref[...],
                (((1,), (1,)), ((), ())),
                precision=HIGHEST_PRECISION,
                preferred_element_type=jnp.float32,
            )
            head_grad = head_grad + lax.dot_general(
                logit_grad,
                value,
                (((0,), (0,)), ((), ())),
                precision=HIGHEST_PRECISION,
                preferred_element_type=jnp.float32,
            )
        head_grad_ref[...] = head_grad
        at_row = lax.broadcasted_iota(jnp.int32, sums_ref.shape, 0)
        sums_ref[...] = jnp.where(at_row == 0, objective, scored)

    found = pl.pallas_call(
        kernel,
        out_shape=[
            jax.ShapeDtypeStruct((rows, width), jnp.float32),
            jax.ShapeDtypeStruct((128, width), jnp.float32),
            jax.ShapeDtypeStruct((8, 128), jnp.float32),
            TOKEN,
        ],
        compiler_params=pltpu.CompilerParams(vmem_limit_bytes=VMEM_BYTES),
        cost_estimate=SMALL_COST,
        name="head_and_loss",
    )(stream, padded, targets[:, None], masked[:, None], *after)
    return found[:3], (found[3],)


def ffn_back_hidden(upstream, normed, scale, gain, outs, slopes, after=()):
    rows, width = upstream.shape
    cores = len(outs)
    units = outs[0].shape[0]
    block = min(units, 256)

    def kernel(upstream_ref, normed_ref, scale_ref, gain_ref, *refs):
        out_refs, slope_refs = refs[:cores], refs[cores : 2 * cores]
        found_refs = refs[-3 - 2 * cores :]
        output_grad_ref, sums_ref, token_ref = found_refs[0], found_refs[-2], found_refs[-1]
        hidden_refs, bias_refs = found_refs[1 : 1 + cores], found_refs[1 + cores : 1 + 2 * cores]
        token_ref[...] = jnp.zeros(TOKEN.shape, TOKEN.dtype)

        @pl.when(pl.program_id(0) == 0)
        def _():
            totals = [jnp.zeros((1, width), jnp.float32)] * 3
            for at, size in row_chunks(rows, 128):
                some = pl.ds(at, size)
                grad, value = upstream_ref[some, :], wide(normed_ref[some, :])
                output_grad = low(norm_back(grad * gain_ref[...], value, scale_ref[some, :]))
                output_grad_ref[some, :] = output_grad
                for i, each in enumerate((grad * value, grad, wide(output_grad))):
                    totals[i] = totals[i] + jnp.sum(each, 0, keepdims=True)
            sums_ref[...] = jnp.zeros(sums_ref.shape, jnp.float32)
            for i in range(3):
                sums_ref[i : i + 1, :] = totals[i]

        for c in range(cores):
            total = jnp.zeros((1, block), jnp.float32)
            for at, size in row_chunks(rows, 512):
                some = pl.ds(at, size)
                active_grad = lax.dot_general(
                    output_grad_ref[some, :],
                    out_refs[c][...],
                    (((1,), (1,)), ((), ())),
                    preferred_element_type=jnp.float32,
                )
                hidden_grad = low(active_grad * wide(slope_refs[c][some, :]))
                hidden_refs[c][some, :] = hidden_grad
                total = total + jnp.sum(wide(hidden_grad), 0, keepdims=True)
            bias_refs[c][...] = total

    whole = pl.BlockSpec((rows, width), lambda g: (0, 0))
    columns = pl.BlockSpec((rows, block), lambda g: (0, g))
    found = pl.pallas_call(
        kernel,
        grid=(units // block,),
        in_specs=[
            whole,
            whole,
            pl.BlockSpec((rows, 1), lambda g: (0, 0)),
            pl.BlockSpec((1, width), lambda g: (0, 0)),
        ]
        + [pl.BlockSpec((block, width), lambda g: (g, 0))] * cores
        + [columns] * cores
        + tokens(after),
        out_specs=[whole]
        + [columns] * cores
        + [pl.BlockSpec((1, block), lambda g: (0, g))] * cores
        + [pl.BlockSpec((8, width), lambda g: (0, 0)), TOKEN_SPEC],
        out_shape=[jax.ShapeDtypeStruct((rows, width), jnp.bfloat16)]
        + [jax.ShapeDtypeStruct((rows, units), jnp.bfloat16)] * cores
        + [jax.ShapeDtypeStruct((1, units), jnp.float32)] * cores
        + [jax.ShapeDtypeStruct((8, width), jnp.float32), TOKEN],
        compiler_params=pltpu.CompilerParams(vmem_limit_bytes=VMEM_BYTES),
        cost_estimate=SMALL_COST,
        name="ffn_back_hidden",
    )(upstream, normed, scale, gain[None], *outs, *slopes, *after)
    return (
        found[0],
        found[1 : 1 + cores],
        found[1 + cores : 1 + 2 * cores],
        found[-2],
        (found[-1],),
    )


def ffn_back_stream(upstream, hiddens, ins, normed, slope, gain, core_index, after=()):
    rows, width = upstream.shape
    cores = len(ins)
    units = ins[0].shape[0]
    block = min(units, 256)
    steps = units // block
    lanes = width // cores

    def kernel(core_ref, upstream_ref, normed_ref, slope_ref, gain_ref, *refs):
        hidden_refs, in_refs = refs[:cores], refs[cores : 2 * cores]
        found_refs = refs[-4 - cores :]
        mid_ref, conv_grad_ref = found_refs[:2]
        cut_refs = found_refs[2 : 1 + cores]
        sums_ref, token_ref, total_ref = found_refs[-3:]
        token_ref[...] = jnp.zeros(TOKEN.shape, TOKEN.dtype)

        @pl.when(pl.program_id(0) == 0)
        def _():
            total_ref[...] = upstream_ref[...]

        for at, size in row_chunks(rows, 512):
            some = pl.ds(at, size)
            total_ref[some, :] += sum(
                jnp.dot(
                    hidden_refs[c][some, :], in_refs[c][...], preferred_element_type=jnp.float32
                )
                for c in range(cores)
            )

        @pl.when(pl.program_id(0) == steps - 1)
        def _():
            totals = [jnp.zeros((1, width), jnp.float32)] * 3
            for at, size in row_chunks(rows, 128):
                some = pl.ds(at, size)
                grad, value = total_ref[some, :], wide(normed_ref[some, :])
                conv_grad = low(norm_back(grad * gain_ref[...], value, wide(slope_ref[some, :])))
                mid_ref[some, :] = grad
                conv_grad_ref[some, :] = conv_grad
                for i, each in enumerate((grad * value, grad, wide(conv_grad))):
                    totals[i] = totals[i] + jnp.sum(each, 0, keepdims=True)
            sums_ref[...] = jnp.zeros(sums_ref.shape, jnp.float32)
            for i in range(3):
                sums_ref[i : i + 1, :] = totals[i]
            for c in range(1, cores):
                first = lax.rem(core_ref[0] - c + cores, cores) * lanes
                cut_refs[c - 1][...] = conv_grad_ref[:, pl.ds(pl.multiple_of(first, lanes), lanes)]

    whole = pl.BlockSpec((rows, width), lambda g, core: (0, 0))
    found = pl.pallas_call(
        kernel,
        grid_spec=pltpu.PrefetchScalarGridSpec(
            num_scalar_prefetch=1,
            grid=(steps,),
            in_specs=[whole, whole, whole, pl.BlockSpec((1, width), lambda g, core: (0, 0))]
            + [pl.BlockSpec((rows, block), lambda g, core: (0, g))] * cores
            + [pl.BlockSpec((block, width), lambda g, core: (g, 0))] * cores
            + tokens(after),
            out_specs=[whole, whole]
            + [pl.BlockSpec((rows, lanes), lambda g, core: (0, 0))] * (cores - 1)
            + [pl.BlockSpec((8, width), lambda g, core: (0, 0)), TOKEN_SPEC],
            scratch_shapes=[pltpu.VMEM((rows, width), jnp.float32)],
        ),
        out_shape=[
            jax.ShapeDtypeStruct((rows, width), jnp.float32),
            jax.ShapeDtypeStruct((rows, width), jnp.bfloat16),
        ]
        + [jax.ShapeDtypeStruct((rows, lanes), jnp.bfloat16)] * (cores - 1)
        + [jax.ShapeDtypeStruct((8, width), jnp.float32), TOKEN],
        compiler_params=pltpu.CompilerParams(vmem_limit_bytes=VMEM_BYTES),
        cost_estimate=SMALL_COST,
        name="ffn_back_stream",
    )(
        core_index.astype(jnp.int32)[None],
        upstream,
        normed,
        slope,
        gain[None],
        *hiddens,
        *ins,
        *after,
    )
    return found[0], found[1], found[2 : 1 + cores], found[-2], (found[-1],)


def conv_data_grad(extended, weight, upstream, step, kind, after=()):
    taps, inner, width = weight.shape
    rows = upstream.shape[0]
    group = tap_groups(taps)
    steps = taps // group

    def kernel(extended_ref, weight_ref, upstream_ref, *refs):
        out_ref, token_ref, total_ref = refs[-3:]
        token_ref[...] = jnp.zeros(TOKEN.shape, TOKEN.dtype)
        first = pl.program_id(0) * group
        total = None
        for j in range(group):
            start = pl.multiple_of((taps - 1 - first - j) * step, ROW_TILE)
            term = lax.dot_general(
                extended_ref[pl.ds(start, rows), :],
                weight_ref[j],
                (((1,), (1,)), ((), ())),
                preferred_element_type=jnp.float32,
            )
            total = term if total is None else total + term

        @pl.when(pl.program_id(0) == 0)
        def _():
            total_ref[...] = total

        @pl.when(pl.program_id(0) > 0)
        def _():
            total_ref[...] += total

        @pl.when(pl.program_id(0) == steps - 1)
        def _():
            out_ref[...] = (upstream_ref[...] + wide(low(total_ref[...]))).astype(kind)

    whole = pl.BlockSpec((rows, inner), lambda g: (0, 0))
    found = pl.pallas_call(
        kernel,
        grid=(steps,),
        in_specs=[
            pl.BlockSpec(extended.shape, lambda g: (0, 0)),
            pl.BlockSpec((group, inner, width), lambda g: (g, 0, 0)),
            whole,
        ]
        + tokens(after),
        out_specs=(whole, TOKEN_SPEC),
        out_shape=(jax.ShapeDtypeStruct((rows, inner), kind), TOKEN),
        scratch_shapes=[pltpu.VMEM((rows, inner), jnp.float32)],
        compiler_params=pltpu.CompilerParams(vmem_limit_bytes=VMEM_BYTES),
        cost_estimate=SMALL_COST,
        name="conv_data_grad",
    )(extended, weight, upstream, *after)
    return found[0], (found[1],)


def restack(groups, through=(), reads=(), after=()):
    flat = [array for arrays, _ in groups for array in arrays]
    cuts = [cut for _, each in groups for cut in each]

    def kernel(*refs):
        token_ref = refs[-1]
        token_ref[...] = jnp.zeros(TOKEN.shape, TOKEN.dtype)
        out_refs = refs[-1 - len(through) - len(cuts) : -1]
        at_in, at_out = 0, 0
        for arrays, each in groups:
            for first, last, shape in each:
                for slot in range(len(arrays)):
                    value = refs[at_in + slot][...]
                    if last is not None:
                        value = value[first:last]
                    out_refs[at_out][slot] = value.reshape(shape)
                at_out += 1
            at_in += len(arrays)
        for i in range(len(through)):
            out_refs[len(cuts) + i][...] = refs[at_in + i][...]

    shapes = [
        jax.ShapeDtypeStruct((len(arrays),) + shape, arrays[0].dtype)
        for arrays, each in groups
        for _, _, shape in each
    ] + [jax.ShapeDtypeStruct(each.shape, each.dtype) for each in through]
    found = pl.pallas_call(
        kernel,
        in_specs=[WHOLE] * (len(flat) + len(through)) + [ANYWHERE] * len(reads) + [WHOLE] * len(after),
        out_specs=[WHOLE] * (len(shapes) + 1),
        out_shape=shapes + [TOKEN],
        compiler_params=pltpu.CompilerParams(vmem_limit_bytes=VMEM_BYTES),
        cost_estimate=SMALL_COST,
        name="restack",
    )(*flat, *through, *reads, *after)
    return found[: len(cuts)], found[len(cuts) : -1], (found[-1],)


def conv_weight_grad(extendeds, upstream, arrived, places, sizes, taps, step, after=()):
    cores, seqs, acrosses, tap_peers = sizes
    rows = upstream.shape[0]
    inner = extendeds[0].shape[1]
    lanes = upstream.shape[1] // cores
    slab = inner // (seqs * acrosses * tap_peers)
    direct = slab % ROW_TILE == 0
    outs = seqs if direct else 1

    def kernel(place_ref, *refs):
        out_refs, token_ref = refs[-1 - outs : -1], refs[-1]
        token_ref[...] = jnp.zeros(TOKEN.shape, TOKEN.dtype)
        start = pl.multiple_of(pl.program_id(0) * step, ROW_TILE)
        found = low(
            sum(
                lax.dot_general(
                    refs[c][pl.ds(start, rows), :],
                    refs[cores + c][...],
                    (((0,), (0,)), ((), ())),
                    preferred_element_type=jnp.float32,
                )
                for c in range(cores)
            )
        )
        if not direct:
            out_refs[0][0] = found
            return
        for s in range(seqs):
            slot_s = lax.rem(place_ref[1] - s + seqs, seqs)
            for slot in range(seqs):

                @pl.when(slot_s == slot)
                def _(s=s, slot=slot):
                    for t in range(tap_peers):
                        slot_t = lax.rem(place_ref[3] - t + tap_peers, tap_peers)
                        for a in range(acrosses):
                            slot_a = lax.rem(place_ref[2] - a + acrosses, acrosses)
                            base = ((t * seqs + s) * acrosses + a) * slab
                            out_refs[slot][slot_a, slot_t, 0] = found[base : base + slab]

    if direct:
        out_shape = (acrosses, tap_peers, taps, slab, lanes)
        out_spec = pl.BlockSpec(
            (acrosses, tap_peers, 1, slab, lanes), lambda k, place: (0, 0, k, 0, 0)
        )
    else:
        out_shape = (taps, inner, lanes)
        out_spec = pl.BlockSpec((1, inner, lanes), lambda k, place: (k, 0, 0))
    found = pl.pallas_call(
        kernel,
        grid_spec=pltpu.PrefetchScalarGridSpec(
            num_scalar_prefetch=1,
            grid=(taps,),
            in_specs=[pl.BlockSpec(extendeds[0].shape, lambda k, place: (0, 0))] * cores
            + [pl.BlockSpec((rows, lanes), lambda k, place: (0, place[0]))]
            + [pl.BlockSpec((rows, lanes), lambda k, place: (0, 0))] * (cores - 1)
            + tokens(after),
            out_specs=[out_spec] * outs + [TOKEN_SPEC],
        ),
        out_shape=[jax.ShapeDtypeStruct(out_shape, jnp.bfloat16)] * outs + [TOKEN],
        compiler_params=pltpu.CompilerParams(vmem_limit_bytes=VMEM_BYTES),
        cost_estimate=SMALL_COST,
        name="conv_weight_grad",
    )(jnp.stack(places).astype(jnp.int32), *extendeds, upstream, *arrived, *after)
    token = found[-1]
    if direct:
        return found[:-1], token
    found = found[0].reshape(taps, tap_peers, seqs, acrosses, slab, lanes)
    for axis, which in ((1, 3), (2, 1), (3, 2)):
        found = relative(found, axis, places[which], sizes[which])
    found = found.transpose(2, 3, 1, 0, 4, 5)
    return [found[s] for s in range(seqs)], token


def ffn_weight_grad(pairs, sizes, ffn_rows, after=()):
    cores, seqs, acrosses, tap_peers = sizes
    rows, width = pairs[0][1][0].shape
    block = tap_peers * ffn_rows
    if ffn_rows % ROW_TILE:
        found = jnp.stack(
            [
                low(
                    sum(
                        lax.dot_general(
                            left,
                            right,
                            (((0,), (0,)), ((), ())),
                            preferred_element_type=jnp.float32,
                        )
                        for left, right in zip(lefts, rights)
                    )
                ).reshape(acrosses, seqs, tap_peers, ffn_rows, width)
                for lefts, rights in pairs
            ],
            3,
        )
        return [found[a] for a in range(acrosses)], jnp.zeros(TOKEN.shape, TOKEN.dtype)

    def kernel(*refs):
        out_refs, token_ref = refs[-1 - acrosses : -1], refs[-1]
        token_ref[...] = jnp.zeros(TOKEN.shape, TOKEN.dtype)
        for which in range(2):
            base = 2 * cores * which
            found = low(
                sum(
                    lax.dot_general(
                        refs[base + c][...],
                        refs[base + cores + c][...],
                        (((0,), (0,)), ((), ())),
                        preferred_element_type=jnp.float32,
                    )
                    for c in range(cores)
                )
            ).reshape(tap_peers, ffn_rows, width)
            for a in range(acrosses):

                @pl.when(pl.program_id(0) // seqs == a)
                def _(a=a):
                    out_refs[a][0, :, which] = found

    left_spec = pl.BlockSpec((rows, block), lambda g: (0, g))
    right_spec = pl.BlockSpec((rows, width), lambda g: (0, 0))

    def out_spec(a):
        return pl.BlockSpec(
            (1, tap_peers, 2, ffn_rows, width),
            lambda g: (jnp.clip(g - a * seqs, 0, seqs - 1), 0, 0, 0, 0),
        )

    shape = jax.ShapeDtypeStruct((seqs, tap_peers, 2, ffn_rows, width), jnp.bfloat16)
    found = pl.pallas_call(
        kernel,
        grid=(acrosses * seqs,),
        in_specs=([left_spec] * cores + [right_spec] * cores) * 2 + tokens(after),
        out_specs=[out_spec(a) for a in range(acrosses)] + [TOKEN_SPEC],
        out_shape=[shape] * acrosses + [TOKEN],
        compiler_params=pltpu.CompilerParams(vmem_limit_bytes=VMEM_BYTES),
        cost_estimate=SMALL_COST,
        name="ffn_weight_grad",
    )(*pairs[0][0], *pairs[0][1], *pairs[1][0], *pairs[1][1], *after)
    return found[:-1], found[-1]


def close_ffn_grads(parts, ffn_rows, after=()):
    blocks, count = len(parts), len(parts[0])
    width = parts[0][0].shape[-1]
    flat = [part.reshape(2, ffn_rows, width) for block in parts for part in block]
    if ffn_rows % ROW_TILE:
        sums = [sum(wide(part) for part in flat[b * count :][:count]) for b in range(blocks)]
        return jnp.stack([each[0].T for each in sums]), jnp.stack([each[1] for each in sums])

    def kernel(*refs):
        in_ref, out_ref = refs[-2:]
        for b in range(blocks):
            total = sum(wide(refs[b * count + i][...]) for i in range(count))
            in_ref[b] = total[0].T
            out_ref[b] = total[1]

    return pl.pallas_call(
        kernel,
        out_shape=(
            jax.ShapeDtypeStruct((blocks, width, ffn_rows), jnp.float32),
            jax.ShapeDtypeStruct((blocks, ffn_rows, width), jnp.float32),
        ),
        compiler_params=pltpu.CompilerParams(vmem_limit_bytes=VMEM_BYTES),
        cost_estimate=SMALL_COST,
        name="close_ffn_grads",
    )(*flat)


def add_slots(parts, slots, after=()):
    lanes = parts[0].shape[-1]
    rows = parts[0].size // (slots * lanes)
    parts = [part.reshape(slots, rows, lanes) for part in parts]
    block = rows // 4 if rows % (4 * ROW_TILE) == 0 else rows

    def kernel(*refs):
        out_refs, token_ref = refs[-1 - slots : -1], refs[-1]
        token_ref[...] = jnp.zeros(TOKEN.shape, TOKEN.dtype)
        for slot in range(slots):
            out_refs[slot][...] = low(sum(wide(refs[i][slot]) for i in range(len(parts))))

    found = pl.pallas_call(
        kernel,
        grid=(rows // block,),
        in_specs=[pl.BlockSpec((slots, block, lanes), lambda g: (0, g, 0))] * len(parts)
        + tokens(after),
        out_specs=[pl.BlockSpec((block, lanes), lambda g: (g, 0))] * slots + [TOKEN_SPEC],
        out_shape=[jax.ShapeDtypeStruct((rows, lanes), jnp.bfloat16)] * slots + [TOKEN],
        compiler_params=pltpu.CompilerParams(vmem_limit_bytes=VMEM_BYTES),
        cost_estimate=SMALL_COST,
        name="add_slots",
    )(*parts, *after)
    return found[:slots], found[slots]


def place_conv_grads(pieces, places, sizes):
    cores, seqs, acrosses = sizes[:3]
    taps, slab, lanes = pieces[0][0][0][0].shape
    channels = slab * seqs * acrosses
    blocks = len(pieces)
    if slab % ROW_TILE:
        full = jnp.stack(
            [
                jnp.stack([jnp.stack([jnp.stack(row) for row in plane]) for plane in block])
                for block in pieces
            ]
        )
        for axis, (place, size) in enumerate(zip(places[:3], sizes[:3])):
            full = relative(full, axis + 1, place, size)
        return wide(
            full.transpose(0, 4, 2, 3, 5, 1, 6).reshape(blocks, taps, channels, cores * lanes)
        )
    flat = [piece for block in pieces for plane in block for row in plane for piece in row]

    def kernel(place_ref, *refs):
        out_ref = refs[-1]
        for b in range(blocks):
            for c in range(cores):
                lane = pl.multiple_of(lax.rem(place_ref[0] - c + cores, cores) * lanes, lanes)
                for s in range(seqs):
                    at_s = lax.rem(place_ref[1] - s + seqs, seqs)
                    for a in range(acrosses):
                        at_a = lax.rem(place_ref[2] - a + acrosses, acrosses)
                        row = pl.multiple_of((at_s * acrosses + at_a) * slab, slab)
                        piece = refs[((b * cores + c) * seqs + s) * acrosses + a]
                        out_ref[b, 0, pl.ds(row, slab), pl.ds(lane, lanes)] = wide(piece[0])

    return pl.pallas_call(
        kernel,
        grid_spec=pltpu.PrefetchScalarGridSpec(
            num_scalar_prefetch=1,
            grid=(taps,),
            in_specs=[pl.BlockSpec((1, slab, lanes), lambda k, place: (k, 0, 0))] * len(flat),
            out_specs=pl.BlockSpec(
                (blocks, 1, channels, cores * lanes), lambda k, place: (0, k, 0, 0)
            ),
        ),
        out_shape=jax.ShapeDtypeStruct((blocks, taps, channels, cores * lanes), jnp.float32),
        compiler_params=pltpu.CompilerParams(vmem_limit_bytes=VMEM_BYTES),
        cost_estimate=SMALL_COST,
        name="place_conv_grads",
    )(jnp.stack(places[:3]).astype(jnp.int32), *flat)


def copy_all(copies):
    for copy in copies:
        copy.start()
    for copy in copies:
        copy.wait()


def place_conv(pieces, places, sizes, after=()):
    cores, seqs, acrosses, tap_peers = sizes
    taps, slab, lanes = pieces[0][0].shape[2:]
    inner = slab * seqs * acrosses * tap_peers
    if slab % ROW_TILE:
        full = jnp.stack([jnp.stack(row) for row in pieces])
        for axis, (place, size) in enumerate(zip(places, sizes)):
            full = relative(full, axis, place, size)
        return full.transpose(4, 3, 1, 2, 5, 0, 6).reshape(taps, inner, cores * lanes)
    flat = [piece for row in pieces for piece in row]

    def kernel(place_ref, *refs):
        sem_ref, out_ref = refs[-1], refs[-2]
        copies = []
        for c in range(cores):
            lane = lax.rem(place_ref[0] - c + cores, cores) * lanes
            for s in range(seqs):
                at_s = lax.rem(place_ref[1] - s + seqs, seqs)
                for a in range(acrosses):
                    at_a = lax.rem(place_ref[2] - a + acrosses, acrosses)
                    for t in range(tap_peers):
                        at_t = lax.rem(place_ref[3] - t + tap_peers, tap_peers)
                        row = ((at_t * seqs + at_s) * acrosses + at_a) * slab
                        copies.append(
                            pltpu.make_async_copy(
                                refs[c * seqs + s].at[a, t],
                                out_ref.at[
                                    :,
                                    pl.ds(pl.multiple_of(row, slab), slab),
                                    pl.ds(pl.multiple_of(lane, lanes), lanes),
                                ],
                                sem_ref.at[len(copies)],
                            )
                        )
        copy_all(copies)

    return pl.pallas_call(
        kernel,
        in_specs=[SCALARS] + [ANYWHERE] * len(flat) + [WHOLE] * len(after),
        out_specs=WHOLE,
        out_shape=jax.ShapeDtypeStruct((taps, inner, cores * lanes), jnp.bfloat16),
        scratch_shapes=[pltpu.SemaphoreType.DMA((cores * seqs * acrosses * tap_peers,))],
        compiler_params=pltpu.CompilerParams(vmem_limit_bytes=VMEM_BYTES),
        cost_estimate=SMALL_COST,
        name="place_conv",
    )(jnp.stack(places).astype(jnp.int32), *flat, *after)


def place_ffn(pieces, sizes):
    cores, seqs, acrosses, tap_peers = sizes
    cuts, ffn_rows, lanes = pieces[0][0].shape[2:]
    cuts //= 2
    width = cuts * lanes
    units = seqs * acrosses * tap_peers * ffn_rows
    if ffn_rows % ROW_TILE:
        full = jnp.stack([jnp.stack(row) for row in pieces])
        full = full.reshape(cores, acrosses, seqs, tap_peers, 2, cuts, ffn_rows, lanes)
        full = full.transpose(4, 0, 1, 2, 3, 6, 5, 7).reshape(2, cores, units, width)
        return [full[0, c] for c in range(cores)], [full[1, c] for c in range(cores)]
    flat = [piece for row in pieces for piece in row]

    def kernel(*refs):
        out_refs, sem_ref = refs[-1 - 2 * cores : -1], refs[-1]
        copies = []
        for c in range(cores):
            for a in range(acrosses):
                for which in range(2):
                    for cut in range(cuts):
                        copies.append(
                            pltpu.make_async_copy(
                                refs[c * acrosses + a].at[:, :, which * cuts + cut],
                                out_refs[which * cores + c].at[
                                    a, :, :, :, pl.ds(cut * lanes, lanes)
                                ],
                                sem_ref.at[len(copies)],
                            )
                        )
        copy_all(copies)

    shape = jax.ShapeDtypeStruct((acrosses, seqs, tap_peers, ffn_rows, width), jnp.bfloat16)
    found = pl.pallas_call(
        kernel,
        in_specs=[ANYWHERE] * len(flat),
        out_specs=[WHOLE] * (2 * cores),
        out_shape=[shape] * (2 * cores),
        scratch_shapes=[pltpu.SemaphoreType.DMA((2 * cores * acrosses * cuts,))],
        compiler_params=pltpu.CompilerParams(vmem_limit_bytes=VMEM_BYTES),
        cost_estimate=SMALL_COST,
        name="place_ffn",
    )(*flat)
    found = [each.reshape(units, width) for each in found]
    return found[:cores], found[cores:]


class Ring:
    def __init__(self, axis, size, index, pairs):
        self.axis, self.size, self.index, self.pairs = axis, size, index, pairs

    def shifted(self, value, by):
        return lax.ppermute(value, self.axis, self.pairs(lambda i: (i + by) % self.size))

    def swapped(self, value, bit):
        return lax.ppermute(value, self.axis, self.pairs(lambda i: i ^ bit))

    def gather(self, value):
        return [value] + [self.shifted(value, by) for by in range(1, self.size)]

    def swap(self, values):
        return [values[0]] + [self.shifted(values[by], -by) for by in range(1, self.size)]


def relative(value, axis, place, size):
    if size == 1:
        return value
    return jnp.stack(
        [
            lax.dynamic_index_in_dim(value, (place - slot) % size, axis, False)
            for slot in range(size)
        ],
        axis,
    )


def rings():
    peers = lax.axis_size("dp")
    cores = CORES if peers % CORES == 0 else 1
    columns = peers // cores
    place = lax.axis_index("dp")

    def plain(axis):
        size = lax.axis_size(axis)
        return Ring(
            axis, size, lax.axis_index(axis), lambda move: [(i, move(i)) for i in range(size)]
        )

    across = Ring(
        "dp",
        columns,
        place // cores,
        lambda move: [(i, move(i // cores) * cores + i % cores) for i in range(peers)],
    )
    core = Ring(
        "dp",
        cores,
        place % cores,
        lambda move: [(i, i // cores * cores + move(i % cores)) for i in range(peers)],
    )
    return core, across, plain("seq"), plain("tap")


class Reduce:
    def __init__(self, terms, order):
        self.order = order
        self.parts = [terms[0]] + [order[0].shifted(terms[s], -s) for s in range(1, order[0].size)]

    def step(self, level, after):
        ring = self.order[level]
        found, token = add_slots(self.parts, ring.size, after)
        self.parts = [found[0]] + [ring.shifted(found[s], -s) for s in range(1, ring.size)]
        return (token,)

    def total(self, after):
        found, token = add_slots(self.parts, 1, after)
        return found[0], (token,)


def shared_copies(value, across, seq):
    peers, spans = lax.axis_size("dp"), lax.axis_size("seq")
    cores = peers // across.size

    def target(place, by_a, by_s):
        dp, at = place // spans, place % spans
        moved = (dp // cores + by_a) % across.size * cores + dp % cores
        return moved * spans + (at + by_s) % spans

    return [
        [
            value
            if by_a == by_s == 0
            else lax.ppermute(
                value,
                ("dp", "seq"),
                [(place, target(place, by_a, by_s)) for place in range(peers * spans)],
            )
            for by_a in range(across.size)
        ]
        for by_s in range(seq.size)
    ]


def summed(value, order):
    if any(ring.size & (ring.size - 1) for ring in order):
        return lax.psum(value, ("dp", "seq", "tap"))
    for ring in order:
        bit = 1
        while bit < ring.size:
            value = value + ring.swapped(value, bit)
            bit *= 2
    return value


def passed_along(value, axis, by):
    peers = lax.axis_size(axis)
    pairs = [(i, i + by) for i in range(peers) if 0 <= i + by < peers]
    return lax.ppermute(value, axis, pairs)


def extend(source, reach_rows):
    span_rows = source.shape[0]
    left_parts = []
    right_parts = []
    distances = -(-reach_rows // span_rows)
    for distance in range(1, distances + 1):
        rim_count = min(span_rows, reach_rows - (distance - 1) * span_rows)
        for direction in (1, -1):
            rim_piece = (
                source[span_rows - rim_count :] if direction == 1 else source[:rim_count]
            )
            arrived = passed_along(rim_piece, "seq", direction * distance)
            if direction == 1:
                left_parts.insert(0, arrived)
            else:
                right_parts.append(arrived)
    return jnp.concatenate(left_parts + [source] + right_parts, axis=0)


def to_rows(values):
    windows, positions = values.shape[:2]
    cut = values.reshape((windows, positions // FIRST_DILATION, FIRST_DILATION) + values.shape[2:])
    return jnp.swapaxes(cut, 0, 1).reshape((windows * positions,) + values.shape[2:])


def from_rows(values, windows):
    cut = values.reshape((-1, windows, FIRST_DILATION) + values.shape[1:])
    return jnp.swapaxes(cut, 0, 1).reshape((windows, -1) + values.shape[1:])


def on_device(
    inputs,
    targets,
    masked,
    conv_weight,
    conv_bias,
    gains,
    shifts,
    in_weight,
    in_bias,
    out_weight,
    out_bias,
    head_weight,
):
    core, across, seq, tap = rings()
    taps = conv_weight.shape[1]
    channels = conv_weight.shape[2]
    width = conv_weight.shape[3]
    slab = channels // (seq.size * across.size)
    lanes = width // core.size
    hidden_width = in_bias.shape[1]
    ffn_rows = in_weight.shape[2]
    windows = inputs.shape[0]
    rows = windows * inputs.shape[1]
    steps = (FIRST_DILATION * windows, SECOND_DILATION * windows)
    units = hidden_width // core.size
    places = (core.index, seq.index, across.index, tap.index)
    sizes = (core.size, seq.size, across.size, tap.size)

    in_bias_placed = []
    for b in range(2):
        bias = in_bias[b].reshape(across.size, core.size, seq.size, tap.size, ffn_rows)
        for axis, ring in enumerate((across, core, seq, tap)):
            bias = relative(bias, axis, ring.index, ring.size)
        in_bias_placed.append(bias.transpose(1, 0, 2, 3, 4).reshape(core.size, units))

    def cut_ffn(piece):
        return piece.reshape(ffn_rows, core.size, lanes).swapaxes(0, 1).reshape(-1, lanes)

    def bundle(b):
        conv_piece = lax.dynamic_slice(
            conv_weight[b],
            (0, (seq.index * across.size + across.index) * slab, core.index * lanes),
            (taps, slab, lanes),
        )
        pieces = [
            conv_piece.reshape(taps * slab, lanes),
            cut_ffn(in_weight[b].T),
            cut_ffn(out_weight[b]),
        ]
        return jnp.concatenate(pieces)

    cuts = (
        (0, taps * slab, (taps, slab, lanes)),
        (taps * slab, taps * slab + 2 * core.size * ffn_rows, (2 * core.size, ffn_rows, lanes)),
    )

    def straight(arrays):
        return (arrays, ((0, None, arrays[0].shape),))

    split = (tap.size + 1) // 2
    bundles = [bundle(0), bundle(1)]
    tap_parts = tap.gather(bundles[0])
    (conv_part, ffn_part), (behind,), _ = restack([(tap_parts, cuts)], through=[bundles[1]])
    conv_parts, ffn_parts = across.gather(conv_part), seq.gather(ffn_part)
    late_parts = [behind] + [None] * (tap.size - 1)
    for by in range(1, tap.size):
        if by != split:
            late_parts[by] = tap.shifted(behind, by)
    (conv_part, ffn_part), (behind,), _ = restack(
        [straight(conv_parts), straight(ffn_parts)],
        through=[behind],
        reads=[each for each in late_parts[1:] if each is not None],
    )
    conv_parts, ffn_parts = seq.gather(conv_part), across.gather(ffn_part)
    if tap.size > 1:
        late_parts[split] = tap.shifted(behind, split)
    conv_slots = [core.gather(conv_part)]
    ffn_slots = [core.gather(ffn_part)]
    (late_conv, late_ffn), _, ready = restack(
        [(late_parts, cuts)], reads=conv_parts[1:] + ffn_parts[1:]
    )
    conv_slots += [core.gather(each) for each in conv_parts[1:]]
    ffn_slots += [core.gather(each) for each in ffn_parts[1:]]
    late_conv_parts, late_ffn_parts = across.gather(late_conv), seq.gather(late_ffn)

    def placed(conv_slots, ffn_slots):
        ins, outs = place_ffn([[a[c] for a in ffn_slots] for c in range(core.size)], sizes)
        full = place_conv([[s[c] for s in conv_slots] for c in range(core.size)], places, sizes)
        return full, ins, outs

    conv_full, in_full, out_full = [None, None], [None, None], [None, None]
    conv_full[0], in_full[0], out_full[0] = placed(conv_slots, ffn_slots)
    (late_conv, late_ffn), _, ready = restack(
        [straight(late_conv_parts), straight(late_ffn_parts)], after=ready
    )
    late_conv_parts, late_ffn_parts = seq.gather(late_conv), across.gather(late_ffn)
    late_conv_slots = [core.gather(late_conv)]
    late_ffn_slots = [core.gather(late_ffn)]

    conv_input = to_rows(inputs)
    stream = conv_input
    flat_masked = wide(to_rows(masked))
    flat_targets = to_rows(targets)
    last = ready
    saved = []
    for b in range(2):
        if b == 1:
            late_conv_slots += [core.gather(each) for each in late_conv_parts[1:]]
            late_ffn_slots += [core.gather(each) for each in late_ffn_parts[1:]]
            conv_full[1], in_full[1], out_full[1] = placed(late_conv_slots, late_ffn_slots)
        extended = extend(conv_input, taps // 2 * steps[b])
        extendeds = [extended] + [core.shifted(extended, -c) for c in range(1, core.size)]
        (normed_conv, conv_slope, stream, lowered), last = conv_forward(
            extended,
            conv_full[b],
            stream,
            conv_bias[b],
            gains[b, 0],
            shifts[b, 0],
            steps[b],
            last,
        )
        lowereds = [lowered] + [core.shifted(lowered, -c) for c in range(1, core.size)]
        actives, hidden_slopes, (normed_ffn, scale_ffn, stream, conv_input), last = ffn_forward(
            lowered,
            stream,
            in_full[b],
            out_full[b],
            [in_bias_placed[b][c] for c in range(core.size)],
            out_bias[b],
            gains[b, 1],
            shifts[b, 1],
            last,
        )
        saved.append(
            (
                extendeds,
                conv_slope,
                normed_conv,
                lowereds,
                core.swap(actives),
                hidden_slopes,
                normed_ffn,
                scale_ffn,
            )
        )

    final_state = from_rows(conv_input, windows)
    (stream_grad, head_grad, loss_rows), last = head_and_loss(
        stream, head_weight, flat_targets, flat_masked, last
    )

    ffn_rows_of_sums = [None, None]
    conv_rows_of_sums = [None, None]
    in_bias_grads = [None, None]
    ffn_sums = [None, None]
    conv_sums = [None, None]
    for b in (1, 0):
        (
            extendeds,
            conv_slope,
            normed_conv,
            lowereds,
            actives,
            hidden_slopes,
            normed_ffn,
            scale_ffn,
        ) = saved[b]
        output_grad, hidden_grads, biases, ffn_rows_of_sums[b], last = ffn_back_hidden(
            stream_grad, normed_ffn, scale_ffn, gains[b, 1], out_full[b], hidden_slopes, last
        )
        output_grads = [output_grad] + [core.shifted(output_grad, -c) for c in range(1, core.size)]
        swapped_grads = core.swap(hidden_grads)
        stream_grad, conv_grad, conv_cuts, conv_rows_of_sums[b], last = ffn_back_stream(
            stream_grad,
            hidden_grads,
            in_full[b],
            normed_conv,
            conv_slope,
            gains[b, 0],
            core.index,
            last,
        )
        arrived = [core.shifted(conv_cuts[c - 1], -c) for c in range(1, core.size)]
        bias = jnp.stack(biases).reshape(core.size, across.size, seq.size, tap.size, ffn_rows)
        for axis, ring in enumerate((core, across, seq, tap)):
            bias = relative(bias, axis, ring.index, ring.size)
        in_bias_grads[b] = bias.transpose(1, 0, 2, 3, 4).reshape(hidden_width)

        def ffn_grads(last):
            found, token = ffn_weight_grad(
                ((swapped_grads, lowereds), (actives, output_grads)), sizes, ffn_rows, last
            )
            return Reduce(found, (across, seq, tap)), (token,)

        def conv_grads(last):
            found, token = conv_weight_grad(
                extendeds, conv_grad, arrived, places, sizes, taps, steps[b], last
            )
            found = [each.reshape(-1, lanes) for each in found]
            return Reduce(found, (seq, across, tap)), (token,)

        if b == 1:
            ffn_sums[1], last = ffn_grads(last)
            conv_sums[1], last = conv_grads(last)
        else:
            last = ffn_sums[1].step(1, last)
            conv_sums[0], last = conv_grads(last)
            last = conv_sums[1].step(1, last)
            ffn_sums[0], last = ffn_grads(last)
            last = ffn_sums[1].step(2, last)
        stream_grad, last = conv_data_grad(
            extend(conv_grad, taps // 2 * steps[b]),
            conv_full[b],
            stream_grad,
            steps[b],
            jnp.float32 if b == 1 else jnp.bfloat16,
            last,
        )

    last = conv_sums[1].step(2, last)
    last = conv_sums[0].step(1, last)
    last = ffn_sums[0].step(1, last)
    shards = [None, None]
    shards[1], last = conv_sums[1].total(last)
    last = conv_sums[0].step(2, last)
    last = ffn_sums[0].step(2, last)
    shards[0], last = conv_sums[0].total(last)
    grad_inputs = from_rows(stream_grad, windows)

    pieces = []
    for b in range(2):
        shard = shards[b].reshape(taps, slab, lanes)
        mine = shared_copies(shard, across, seq)
        pieces.append(
            [[[core.gather(each)[c] for each in row] for row in mine] for c in range(core.size)]
        )
    grad_conv = place_conv_grads(pieces, places, sizes)
    grad_in, grad_out = close_ffn_grads([each.parts for each in ffn_sums], ffn_rows)

    small = [
        jnp.stack([conv_rows_of_sums[b][2] for b in range(2)]),
        jnp.stack([jnp.stack([conv_rows_of_sums[b][0], ffn_rows_of_sums[b][0]]) for b in range(2)]),
        jnp.stack([jnp.stack([conv_rows_of_sums[b][1], ffn_rows_of_sums[b][1]]) for b in range(2)]),
        jnp.stack(in_bias_grads),
        jnp.stack([ffn_rows_of_sums[b][2] for b in range(2)]),
        head_grad[: head_weight.shape[1]],
        jnp.pad(loss_rows[:2, 0], (0, width - 2)),
    ]
    packed = jnp.concatenate([each.reshape(-1, width) for each in small])
    packed = summed(packed, (core, across, seq, tap))
    unpacked = []
    first = 0
    for each in small:
        count = each.size // width
        unpacked.append(packed[first : first + count].reshape(each.shape))
        first += count
    (
        grad_conv_bias,
        grad_gains,
        grad_shifts,
        grad_in_bias,
        grad_out_bias,
        grad_head_weight,
        loss_terms,
    ) = unpacked
    return (
        final_state,
        grad_inputs,
        grad_conv,
        grad_conv_bias,
        grad_gains,
        grad_shifts,
        grad_in,
        grad_in_bias,
        grad_out,
        grad_out_bias,
        grad_head_weight.T,
        loss_terms[0] / loss_terms[1],
    )


def solution(mesh):
    placed = (
        P(("dp", "tap"), "seq", None),
        P(("dp", "tap"), "seq"),
        P(("dp", "tap"), "seq"),
        P(None, None, "tap", None),
        P(),
        P(),
        P(),
        P(None, None, ("dp", "seq", "tap")),
        P(),
        P(None, ("dp", "seq", "tap"), None),
        P(),
        P(),
    )
    return jax.shard_map(
        on_device,
        mesh=mesh,
        in_specs=placed,
        out_specs=(
            P(("dp", "tap"), "seq", None),
            P(("dp", "tap"), "seq", None),
            P(None, None, "tap", None),
            P(),
            P(),
            P(),
            P(None, None, ("dp", "seq", "tap")),
            P(),
            P(None, ("dp", "seq", "tap"), None),
            P(),
            P(),
            P(),
        ),
        check_vma=False,
    )
```

```python
import functools

import jax
import jax.numpy as jnp
from jax import lax
from jax.experimental import pallas as pl
from jax.experimental.pallas import tpu as pltpu
from jax.sharding import PartitionSpec as P

FIRST_DILATION = 4
SECOND_DILATION = 32
EPSILON = 1e-05
HIGHEST_PRECISION = lax.Precision.HIGHEST
CORES = 2
ROW_TILE = 16
VMEM_BYTES = 60 * 1024 * 1024
ANYWHERE = pl.BlockSpec(memory_space=pl.ANY)
SCALARS = pl.BlockSpec(memory_space=pltpu.SMEM)


TOKEN = jax.ShapeDtypeStruct((8, 128), jnp.float32)
SMALL_COST = pl.CostEstimate(flops=1024, bytes_accessed=1024, transcendentals=0)
WHOLE = pl.BlockSpec(memory_space=pltpu.VMEM)
TOKEN_SPEC = pl.BlockSpec(TOKEN.shape, lambda *_: (0, 0))


def tokens(after):
    return [TOKEN_SPEC] * len(after)


def low(values):
    return values.astype(jnp.bfloat16)


def wide(values):
    return values.astype(jnp.float32)


def gelu_parts(values):
    phi = 0.5 * (1.0 + lax.erf(values * 0.7071067811865476))
    return (
        values * phi,
        phi + values * jnp.exp(-0.5 * values * values) * 0.3989422804014327,
    )


def normalize(values):
    center = values - jnp.mean(values, -1, keepdims=True)
    scale = lax.rsqrt(jnp.mean(center * center, -1, keepdims=True) + EPSILON)
    return (center * scale, scale)


def norm_back(upstream, normed, scale):
    return scale * (
        upstream
        - jnp.mean(upstream, -1, keepdims=True)
        - normed * jnp.mean(upstream * normed, -1, keepdims=True)
    )


def tap_groups(taps):
    return 3 if taps % 3 == 0 else 1


def row_chunks(rows, most):
    size = min(rows, most)
    return [(first, size) for first in range(0, rows, size)]


def conv_forward(extended, weight, stream, bias, gain, shift, step, after=(), reads=()):
    taps, inner, width = weight.shape
    rows = stream.shape[0]
    group = tap_groups(taps)
    steps = taps // group

    def kernel(extended_ref, weight_ref, stream_ref, bias_ref, gain_ref, shift_ref, *refs):
        normed_ref, slope_ref, next_ref, lowered_ref, token_ref, total_ref = refs[-6:]
        token_ref[...] = jnp.zeros(TOKEN.shape, TOKEN.dtype)
        first = pl.program_id(0) * group
        total = None
        for j in range(group):
            start = pl.multiple_of((first + j) * step, ROW_TILE)
            term = jnp.dot(
                extended_ref[pl.ds(start, rows), :],
                weight_ref[j],
                preferred_element_type=jnp.float32,
            )
            total = term if total is None else total + term

        @pl.when(pl.program_id(0) == 0)
        def _():
            total_ref[...] = total

        @pl.when(pl.program_id(0) > 0)
        def _():
            total_ref[...] += total

        @pl.when(pl.program_id(0) == steps - 1)
        def _():
            for at, size in row_chunks(rows, 128):
                some = pl.ds(at, size)
                value, slope = gelu_parts(total_ref[some, :] + bias_ref[...])
                normed, scale = normalize(value)
                mid = wide(stream_ref[some, :]) + normed * gain_ref[...] + shift_ref[...]
                normed_ref[some, :] = low(normed)
                slope_ref[some, :] = low(scale * slope)
                next_ref[some, :] = mid
                lowered_ref[some, :] = low(mid)

    whole = pl.BlockSpec((rows, width), lambda g: (0, 0))
    row = pl.BlockSpec((1, width), lambda g: (0, 0))
    found = pl.pallas_call(
        kernel,
        grid=(steps,),
        in_specs=[
            pl.BlockSpec(extended.shape, lambda g: (0, 0)),
            pl.BlockSpec((group, inner, width), lambda g: (g, 0, 0)),
            whole,
            row,
            row,
            row,
        ]
        + tokens(after)
        + [ANYWHERE] * len(reads),
        out_specs=[whole] * 4 + [TOKEN_SPEC],
        out_shape=[
            jax.ShapeDtypeStruct((rows, width), jnp.bfloat16),
            jax.ShapeDtypeStruct((rows, width), jnp.bfloat16),
            jax.ShapeDtypeStruct((rows, width), jnp.float32),
            jax.ShapeDtypeStruct((rows, width), jnp.bfloat16),
            TOKEN,
        ],
        scratch_shapes=[pltpu.VMEM((rows, width), jnp.float32)],
        compiler_params=pltpu.CompilerParams(vmem_limit_bytes=VMEM_BYTES),
        cost_estimate=SMALL_COST,
        name="conv_forward",
    )(extended, weight, stream, bias[None], gain[None], shift[None], *after, *reads)
    return found[:4], (found[4],)


def ffn_forward(
    lowered, stream, ins, outs, in_biases, out_bias, gain, shift, after=(), reads=()
):
    rows, width = lowered.shape
    cores = len(ins)
    units = ins[0].shape[0]
    block = min(units, 256)
    steps = units // block

    def kernel(lowered_ref, stream_ref, out_bias_ref, gain_ref, shift_ref, *refs):
        in_refs, out_refs, bias_refs = (refs[i * cores : (i + 1) * cores] for i in range(3))
        found_refs = refs[-6 - 2 * cores :]
        active_ref, slope_refs = found_refs[0], found_refs[1 : 1 + cores]
        normed_ref, scale_ref, next_ref, rounded_ref = found_refs[1 + cores : 5 + cores]
        packet_refs = found_refs[5 + cores : -2]
        token_ref, total_ref = found_refs[-2:]
        token_ref[...] = jnp.zeros(TOKEN.shape, TOKEN.dtype)
        lane = pl.multiple_of(width + pl.program_id(0) * block, block)

        @pl.when(pl.program_id(0) == 0)
        def _():
            total_ref[...] = jnp.zeros(total_ref.shape, jnp.float32)
            for packet_ref in packet_refs:
                packet_ref[:, :width] = lowered_ref[...]

        for at, size in row_chunks(rows, 512):
            some = pl.ds(at, size)
            term = None
            for c in range(cores):
                hidden = lax.dot_general(
                    lowered_ref[some, :],
                    in_refs[c][...],
                    (((1,), (1,)), ((), ())),
                    preferred_element_type=jnp.float32,
                )
                active, slope = gelu_parts(hidden + bias_refs[c][...])
                active = low(active)
                if c == 0:
                    active_ref[some, :] = active
                else:
                    packet_refs[c - 1][some, pl.ds(lane, block)] = active
                slope_refs[c][some, :] = low(slope)
                found = jnp.dot(active, out_refs[c][...], preferred_element_type=jnp.float32)
                term = found if term is None else term + found
            total_ref[some, :] += term

        @pl.when(pl.program_id(0) == steps - 1)
        def _():
            for at, size in row_chunks(rows, 128):
                some = pl.ds(at, size)
                normed, scale = normalize(total_ref[some, :] + out_bias_ref[...])
                after_ffn = stream_ref[some, :] + normed * gain_ref[...] + shift_ref[...]
                normed_ref[some, :] = low(normed)
                scale_ref[some, :] = jnp.broadcast_to(scale, (size, 128))
                next_ref[some, :] = after_ffn
                rounded_ref[some, :] = low(after_ffn)

    whole = pl.BlockSpec((rows, width), lambda g: (0, 0))
    row = pl.BlockSpec((1, width), lambda g: (0, 0))
    piece = pl.BlockSpec((block, width), lambda g: (g, 0))
    columns = pl.BlockSpec((rows, block), lambda g: (0, g))
    hidden_shape = jax.ShapeDtypeStruct((rows, units), jnp.bfloat16)
    found = pl.pallas_call(
        kernel,
        grid=(steps,),
        in_specs=[whole, whole, row, row, row]
        + [piece] * (2 * cores)
        + [pl.BlockSpec((1, block), lambda g: (0, g))] * cores
        + tokens(after)
        + [ANYWHERE] * len(reads),
        out_specs=[columns] * (1 + cores)
        + [whole, pl.BlockSpec((rows, 128), lambda g: (0, 0)), whole, whole]
        + [pl.BlockSpec((rows, width + units), lambda g: (0, 0))] * (cores - 1)
        + [TOKEN_SPEC],
        out_shape=[hidden_shape] * (1 + cores)
        + [
            jax.ShapeDtypeStruct((rows, width), jnp.bfloat16),
            jax.ShapeDtypeStruct((rows, 128), jnp.float32),
            jax.ShapeDtypeStruct((rows, width), jnp.float32),
            jax.ShapeDtypeStruct((rows, width), jnp.bfloat16),
        ]
        + [jax.ShapeDtypeStruct((rows, width + units), jnp.bfloat16)] * (cores - 1)
        + [TOKEN],
        scratch_shapes=[pltpu.VMEM((rows, width), jnp.float32)],
        compiler_params=pltpu.CompilerParams(vmem_limit_bytes=VMEM_BYTES),
        cost_estimate=SMALL_COST,
        name="ffn_forward",
    )(
        lowered,
        stream,
        out_bias[None],
        gain[None],
        shift[None],
        *ins,
        *outs,
        *[each[None] for each in in_biases],
        *after,
        *reads,
    )
    return (
        found[0],
        found[1 : 1 + cores],
        found[1 + cores : 5 + cores],
        found[5 + cores : -1],
        (found[-1],),
    )


def head_and_loss(stream, head_weight, codes, after=()):
    rows, width = stream.shape
    classes = head_weight.shape[1]
    padded = jnp.pad(head_weight, ((0, 0), (0, 128 - classes)))
    cuts = row_chunks(rows, 256)

    def kernel(stream_ref, head_ref, code_ref, *refs):
        grad_ref, head_grad_ref, sums_ref, token_ref = refs[-4:]
        token_ref[...] = jnp.zeros(TOKEN.shape, TOKEN.dtype)
        head_grad = jnp.zeros((128, width), jnp.float32)
        objective = jnp.zeros((1, 1), jnp.float32)
        scored = jnp.zeros((1, 1), jnp.float32)
        for at, size in cuts:
            some = pl.ds(at, size)
            value = stream_ref[some, :]
            code = code_ref[some, :]
            mask = jnp.where(code[:, :1] >= classes, 1.0, 0.0)
            logits = jnp.dot(
                value, head_ref[...], precision=HIGHEST_PRECISION, preferred_element_type=jnp.float32
            )
            lane = lax.broadcasted_iota(jnp.int32, logits.shape, 1)
            valid = lane < classes
            peak = jnp.max(jnp.where(valid, logits, -jnp.inf), -1, keepdims=True)
            exponent = jnp.where(valid, jnp.exp(jnp.where(valid, logits - peak, 0.0)), 0.0)
            denominator = jnp.sum(exponent, -1, keepdims=True)
            chosen = lane == jnp.where(code >= classes, code - classes, code)
            picked = jnp.sum(jnp.where(chosen, logits, 0.0), -1, keepdims=True)
            terms = mask * (peak + jnp.log(denominator) - picked)
            objective = objective + jnp.sum(terms, 0, keepdims=True)
            scored = scored + jnp.sum(mask, 0, keepdims=True)
            logit_grad = mask * (exponent / denominator - jnp.where(chosen, 1.0, 0.0))
            grad_ref[some, :] = lax.dot_general(
                logit_grad,
                head_ref[...],
                (((1,), (1,)), ((), ())),
                precision=HIGHEST_PRECISION,
                preferred_element_type=jnp.float32,
            )
            head_grad = head_grad + lax.dot_general(
                logit_grad,
                value,
                (((0,), (0,)), ((), ())),
                precision=HIGHEST_PRECISION,
                preferred_element_type=jnp.float32,
            )
        head_grad_ref[...] = head_grad
        at_row = lax.broadcasted_iota(jnp.int32, sums_ref.shape, 0)
        sums_ref[...] = jnp.where(at_row == 0, objective, scored)

    found = pl.pallas_call(
        kernel,
        out_shape=[
            jax.ShapeDtypeStruct((rows, width), jnp.float32),
            jax.ShapeDtypeStruct((128, width), jnp.float32),
            jax.ShapeDtypeStruct((8, 128), jnp.float32),
            TOKEN,
        ],
        compiler_params=pltpu.CompilerParams(vmem_limit_bytes=VMEM_BYTES),
        cost_estimate=SMALL_COST,
        name="head_and_loss",
    )(stream, padded, codes, *after)
    return found[:3], (found[3],)


def ffn_back_hidden(upstream, normed, scale, gain, outs, slopes, after=()):
    rows, width = upstream.shape
    cores = len(outs)
    units = outs[0].shape[0]
    block = min(units, 256)

    def kernel(upstream_ref, normed_ref, scale_ref, gain_ref, *refs):
        out_refs, slope_refs = refs[:cores], refs[cores : 2 * cores]
        found_refs = refs[-3 - 2 * cores :]
        output_grad_ref, hidden_ref = found_refs[:2]
        bias_refs, packet_refs = found_refs[2 : 2 + cores], found_refs[2 + cores : -2]
        sums_ref, token_ref = found_refs[-2:]
        token_ref[...] = jnp.zeros(TOKEN.shape, TOKEN.dtype)
        lane = pl.multiple_of(width + pl.program_id(0) * block, block)

        @pl.when(pl.program_id(0) == 0)
        def _():
            totals = [jnp.zeros((1, width), jnp.float32)] * 3
            for at, size in row_chunks(rows, 128):
                some = pl.ds(at, size)
                grad, value = upstream_ref[some, :], wide(normed_ref[some, :])
                output_grad = low(norm_back(grad * gain_ref[...], value, scale_ref[some, :1]))
                output_grad_ref[some, :] = output_grad
                for packet_ref in packet_refs:
                    packet_ref[some, :width] = output_grad
                for i, each in enumerate((grad * value, grad, wide(output_grad))):
                    totals[i] = totals[i] + jnp.sum(each, 0, keepdims=True)
            sums_ref[...] = jnp.zeros(sums_ref.shape, jnp.float32)
            for i in range(3):
                sums_ref[i : i + 1, :] = totals[i]

        for c in range(cores):
            total = jnp.zeros((1, block), jnp.float32)
            for at, size in row_chunks(rows, 512):
                some = pl.ds(at, size)
                active_grad = lax.dot_general(
                    output_grad_ref[some, :],
                    out_refs[c][...],
                    (((1,), (1,)), ((), ())),
                    preferred_element_type=jnp.float32,
                )
                hidden_grad = low(active_grad * wide(slope_refs[c][some, :]))
                if c == 0:
                    hidden_ref[some, :] = hidden_grad
                else:
                    packet_refs[c - 1][some, pl.ds(lane, block)] = hidden_grad
                total = total + jnp.sum(wide(hidden_grad), 0, keepdims=True)
            bias_refs[c][...] = total

    whole = pl.BlockSpec((rows, width), lambda g: (0, 0))
    columns = pl.BlockSpec((rows, block), lambda g: (0, g))
    found = pl.pallas_call(
        kernel,
        grid=(units // block,),
        in_specs=[
            whole,
            whole,
            pl.BlockSpec((rows, 128), lambda g: (0, 0)),
            pl.BlockSpec((1, width), lambda g: (0, 0)),
        ]
        + [pl.BlockSpec((block, width), lambda g: (g, 0))] * cores
        + [columns] * cores
        + tokens(after),
        out_specs=[whole, columns]
        + [pl.BlockSpec((1, block), lambda g: (0, g))] * cores
        + [pl.BlockSpec((rows, width + units), lambda g: (0, 0))] * (cores - 1)
        + [pl.BlockSpec((8, width), lambda g: (0, 0)), TOKEN_SPEC],
        out_shape=[
            jax.ShapeDtypeStruct((rows, width), jnp.bfloat16),
            jax.ShapeDtypeStruct((rows, units), jnp.bfloat16),
        ]
        + [jax.ShapeDtypeStruct((1, units), jnp.float32)] * cores
        + [jax.ShapeDtypeStruct((rows, width + units), jnp.bfloat16)] * (cores - 1)
        + [jax.ShapeDtypeStruct((8, width), jnp.float32), TOKEN],
        compiler_params=pltpu.CompilerParams(vmem_limit_bytes=VMEM_BYTES),
        cost_estimate=SMALL_COST,
        name="ffn_back_hidden",
    )(upstream, normed, scale, gain[None], *outs, *slopes, *after)
    return (
        found[0],
        found[1],
        found[2 : 2 + cores],
        found[2 + cores : -2],
        found[-2],
        (found[-1],),
    )


def ffn_back_stream(
    upstream, hidden, packets, ins, normed, slope, gain, core_index, after=(), reads=(), relay=False
):
    rows, width = upstream.shape
    cores = len(ins)
    units = ins[0].shape[0]
    block = min(units, 256)
    steps = units // block
    lanes = width // cores
    relays = cores - 1 if relay else 0

    def kernel(core_ref, upstream_ref, normed_ref, slope_ref, gain_ref, *refs):
        hidden_refs, in_refs = refs[:cores], refs[cores : 2 * cores]
        found_refs = refs[-4 - cores - relays :]
        mid_ref, conv_grad_ref = found_refs[:2]
        cut_refs = found_refs[2 : 1 + cores]
        sums_ref, token_ref, total_ref = found_refs[-3:]
        token_ref[...] = jnp.zeros(TOKEN.shape, TOKEN.dtype)
        for i in range(relays):
            relay_ref = found_refs[1 + cores + i]
            lane = pl.multiple_of(width + pl.program_id(0) * block, block)
            relay_ref[:, pl.ds(lane, block)] = hidden_refs[1 + i][...]

            @pl.when(pl.program_id(0) == 0)
            def _(i=i, relay_ref=relay_ref):
                relay_ref[:, :width] = refs[2 * cores + i][...]

        @pl.when(pl.program_id(0) == 0)
        def _():
            total_ref[...] = upstream_ref[...]

        for at, size in row_chunks(rows, 512):
            some = pl.ds(at, size)
            total_ref[some, :] += sum(
                jnp.dot(
                    hidden_refs[c][some, :], in_refs[c][...], preferred_element_type=jnp.float32
                )
                for c in range(cores)
            )

        @pl.when(pl.program_id(0) == steps - 1)
        def _():
            totals = [jnp.zeros((1, width), jnp.float32)] * 3
            for at, size in row_chunks(rows, 128):
                some = pl.ds(at, size)
                grad, value = total_ref[some, :], wide(normed_ref[some, :])
                conv_grad = low(norm_back(grad * gain_ref[...], value, wide(slope_ref[some, :])))
                mid_ref[some, :] = grad
                conv_grad_ref[some, :] = conv_grad
                for i, each in enumerate((grad * value, grad, wide(conv_grad))):
                    totals[i] = totals[i] + jnp.sum(each, 0, keepdims=True)
            sums_ref[...] = jnp.zeros(sums_ref.shape, jnp.float32)
            for i in range(3):
                sums_ref[i : i + 1, :] = totals[i]
            for c in range(1, cores):
                first = lax.rem(core_ref[0] - c + cores, cores) * lanes
                cut_refs[c - 1][...] = conv_grad_ref[:, pl.ds(pl.multiple_of(first, lanes), lanes)]

    whole = pl.BlockSpec((rows, width), lambda g, core: (0, 0))
    found = pl.pallas_call(
        kernel,
        grid_spec=pltpu.PrefetchScalarGridSpec(
            num_scalar_prefetch=1,
            grid=(steps,),
            in_specs=[whole, whole, whole, pl.BlockSpec((1, width), lambda g, core: (0, 0))]
            + [pl.BlockSpec((rows, block), lambda g, core: (0, g))]
            + [pl.BlockSpec((rows, block), lambda g, core: (0, width // block + g))] * (cores - 1)
            + [pl.BlockSpec((block, width), lambda g, core: (g, 0))] * cores
            + [whole] * relays
            + tokens(after)
            + [ANYWHERE] * len(reads),
            out_specs=[whole, whole]
            + [pl.BlockSpec((rows, lanes), lambda g, core: (0, 0))] * (cores - 1)
            + [pl.BlockSpec((rows, width + units), lambda g, core: (0, 0))] * relays
            + [pl.BlockSpec((8, width), lambda g, core: (0, 0)), TOKEN_SPEC],
            scratch_shapes=[pltpu.VMEM((rows, width), jnp.float32)],
        ),
        out_shape=[
            jax.ShapeDtypeStruct((rows, width), jnp.float32),
            jax.ShapeDtypeStruct((rows, width), jnp.bfloat16),
        ]
        + [jax.ShapeDtypeStruct((rows, lanes), jnp.bfloat16)] * (cores - 1)
        + [jax.ShapeDtypeStruct((rows, width + units), jnp.bfloat16)] * relays
        + [jax.ShapeDtypeStruct((8, width), jnp.float32), TOKEN],
        compiler_params=pltpu.CompilerParams(vmem_limit_bytes=VMEM_BYTES),
        cost_estimate=SMALL_COST,
        name="ffn_back_stream",
    )(
        core_index.astype(jnp.int32)[None],
        upstream,
        normed,
        slope,
        gain[None],
        hidden,
        *packets,
        *ins,
        *packets[:relays],
        *after,
        *reads,
    )
    return (
        found[0],
        found[1],
        found[2 : 1 + cores],
        found[1 + cores : 1 + cores + relays],
        found[-2],
        (found[-1],),
    )


def conv_data_grad(extended, weight, upstream, step, kind, after=()):
    taps, inner, width = weight.shape
    rows = upstream.shape[0]
    group = tap_groups(taps)
    steps = taps // group

    def kernel(extended_ref, weight_ref, upstream_ref, *refs):
        out_ref, token_ref, total_ref = refs[-3:]
        token_ref[...] = jnp.zeros(TOKEN.shape, TOKEN.dtype)
        first = pl.program_id(0) * group
        total = None
        for j in range(group):
            start = pl.multiple_of((taps - 1 - first - j) * step, ROW_TILE)
            term = lax.dot_general(
                extended_ref[pl.ds(start, rows), :],
                weight_ref[j],
                (((1,), (1,)), ((), ())),
                preferred_element_type=jnp.float32,
            )
            total = term if total is None else total + term

        @pl.when(pl.program_id(0) == 0)
        def _():
            total_ref[...] = total

        @pl.when(pl.program_id(0) > 0)
        def _():
            total_ref[...] += total

        @pl.when(pl.program_id(0) == steps - 1)
        def _():
            out_ref[...] = (upstream_ref[...] + wide(low(total_ref[...]))).astype(kind)

    whole = pl.BlockSpec((rows, inner), lambda g: (0, 0))
    found = pl.pallas_call(
        kernel,
        grid=(steps,),
        in_specs=[
            pl.BlockSpec(extended.shape, lambda g: (0, 0)),
            pl.BlockSpec((group, inner, width), lambda g: (g, 0, 0)),
            whole,
        ]
        + tokens(after),
        out_specs=(whole, TOKEN_SPEC),
        out_shape=(jax.ShapeDtypeStruct((rows, inner), kind), TOKEN),
        scratch_shapes=[pltpu.VMEM((rows, inner), jnp.float32)],
        compiler_params=pltpu.CompilerParams(vmem_limit_bytes=VMEM_BYTES),
        cost_estimate=SMALL_COST,
        name="conv_data_grad",
    )(extended, weight, upstream, *after)
    return found[0], (found[1],)


def hold(arrays, after):
    count = len(arrays)
    if count == 0:
        return [], after

    def kernel(*refs):
        refs[-1][...] = jnp.zeros(TOKEN.shape, TOKEN.dtype)

    found = pl.pallas_call(
        kernel,
        in_specs=[ANYWHERE] * count + [WHOLE] * len(after),
        out_specs=[ANYWHERE] * count + [WHOLE],
        out_shape=[jax.ShapeDtypeStruct(each.shape, each.dtype) for each in arrays] + [TOKEN],
        input_output_aliases={i: i for i in range(count)},
        cost_estimate=SMALL_COST,
        name="hold",
    )(*arrays, *after)
    return list(found[:-1]), (found[-1],)


def join_rows(parts, after=(), reads=()):
    def kernel(*refs):
        out_ref, token_ref = refs[-2:]
        token_ref[...] = jnp.zeros(TOKEN.shape, TOKEN.dtype)
        first = 0
        for i, part in enumerate(parts):
            out_ref[first : first + part.shape[0]] = refs[i][...]
            first += part.shape[0]

    shape = (sum(part.shape[0] for part in parts), parts[0].shape[1])
    found = pl.pallas_call(
        kernel,
        in_specs=[WHOLE] * len(parts) + [ANYWHERE] * len(reads) + [WHOLE] * len(after),
        out_specs=[WHOLE] * 2,
        out_shape=[jax.ShapeDtypeStruct(shape, parts[0].dtype), TOKEN],
        compiler_params=pltpu.CompilerParams(vmem_limit_bytes=VMEM_BYTES),
        cost_estimate=SMALL_COST,
        name="join_rows",
    )(*parts, *reads, *after)
    return found[0], (found[1],)


def restack(groups, reads=(), after=(), turn=None):
    flat = [array for arrays, _ in groups for array in arrays]
    cuts = [cut for _, each in groups for cut in each]

    def kernel(place_ref, *refs):
        token_ref = refs[-1]
        token_ref[...] = jnp.zeros(TOKEN.shape, TOKEN.dtype)
        out_refs = refs[-1 - len(cuts) : -1]
        at_in, at_out = 0, 0
        for arrays, each in groups:
            slots = len(arrays) if turn is None else arrays[0].shape[0]
            for first, last, shape in each:
                for slot in range(slots):
                    if turn is None:
                        value = refs[at_in + slot][...]
                    else:
                        value = refs[at_in][lax.rem(place_ref[0] - slot + slots, slots)]
                    if last is not None:
                        value = value[first:last]
                    out_refs[at_out][slot] = value.reshape(shape)
                at_out += 1
            at_in += len(arrays)

    shapes = [
        jax.ShapeDtypeStruct(
            ((len(arrays) if turn is None else arrays[0].shape[0]),) + shape, arrays[0].dtype
        )
        for arrays, each in groups
        for _, _, shape in each
    ]
    found = pl.pallas_call(
        kernel,
        in_specs=[SCALARS]
        + [WHOLE] * len(flat)
        + [ANYWHERE] * len(reads)
        + [WHOLE] * len(after),
        out_specs=[WHOLE] * (len(shapes) + 1),
        out_shape=shapes + [TOKEN],
        compiler_params=pltpu.CompilerParams(vmem_limit_bytes=VMEM_BYTES),
        cost_estimate=SMALL_COST,
        name="restack",
    )(jnp.zeros((1,), jnp.int32) + (0 if turn is None else turn), *flat, *reads, *after)
    return found[:-1], (found[-1],)


def conv_weight_grad(
    extendeds, upstream, arrived, places, sizes, taps, step, after=(), reads=()
):
    cores, seqs, acrosses, tap_peers = sizes
    rows = upstream.shape[0]
    inner = extendeds[0].shape[1]
    lanes = upstream.shape[1] // cores
    slab = inner // (seqs * acrosses * tap_peers)
    direct = slab % ROW_TILE == 0
    outs = seqs if direct else 1

    def kernel(place_ref, *refs):
        out_refs, token_ref = refs[-1 - outs : -1], refs[-1]
        token_ref[...] = jnp.zeros(TOKEN.shape, TOKEN.dtype)
        start = pl.multiple_of(pl.program_id(0) * step, ROW_TILE)
        found = low(
            sum(
                lax.dot_general(
                    refs[c][pl.ds(start, rows), :],
                    refs[cores + c][...],
                    (((0,), (0,)), ((), ())),
                    preferred_element_type=jnp.float32,
                )
                for c in range(cores)
            )
        )
        if not direct:
            out_refs[0][0] = found
            return
        for s in range(seqs):
            slot_s = lax.rem(place_ref[1] - s + seqs, seqs)
            for slot in range(seqs):

                @pl.when(slot_s == slot)
                def _(s=s, slot=slot):
                    for t in range(tap_peers):
                        slot_t = lax.rem(place_ref[3] - t + tap_peers, tap_peers)
                        for a in range(acrosses):
                            slot_a = lax.rem(place_ref[2] - a + acrosses, acrosses)
                            base = ((t * seqs + s) * acrosses + a) * slab
                            out_refs[slot][slot_a, slot_t, 0] = found[base : base + slab]

    if direct:
        out_shape = (acrosses, tap_peers, taps, slab, lanes)
        out_spec = pl.BlockSpec(
            (acrosses, tap_peers, 1, slab, lanes), lambda k, place: (0, 0, k, 0, 0)
        )
    else:
        out_shape = (taps, inner, lanes)
        out_spec = pl.BlockSpec((1, inner, lanes), lambda k, place: (k, 0, 0))
    found = pl.pallas_call(
        kernel,
        grid_spec=pltpu.PrefetchScalarGridSpec(
            num_scalar_prefetch=1,
            grid=(taps,),
            in_specs=[pl.BlockSpec(extendeds[0].shape, lambda k, place: (0, 0))] * cores
            + [pl.BlockSpec((rows, lanes), lambda k, place: (0, place[0]))]
            + [pl.BlockSpec((rows, lanes), lambda k, place: (0, 0))] * (cores - 1)
            + tokens(after)
            + [ANYWHERE] * len(reads),
            out_specs=[out_spec] * outs + [TOKEN_SPEC],
        ),
        out_shape=[jax.ShapeDtypeStruct(out_shape, jnp.bfloat16)] * outs + [TOKEN],
        compiler_params=pltpu.CompilerParams(vmem_limit_bytes=VMEM_BYTES),
        cost_estimate=SMALL_COST,
        name="conv_weight_grad",
    )(jnp.stack(places).astype(jnp.int32), *extendeds, upstream, *arrived, *after, *reads)
    token = found[-1]
    if direct:
        return found[:-1], token
    found = found[0].reshape(taps, tap_peers, seqs, acrosses, slab, lanes)
    for axis, which in ((1, 3), (2, 1), (3, 2)):
        found = relative(found, axis, places[which], sizes[which])
    found = found.transpose(2, 3, 1, 0, 4, 5)
    return [found[s] for s in range(seqs)], token


def ffn_weight_grad(pairs, sizes, ffn_rows, after=()):
    cores, seqs, acrosses, tap_peers = sizes
    rows, width = pairs[0][1].shape
    block = tap_peers * ffn_rows
    transposed = (((0,), (0,)), ((), ()))
    if ffn_rows % ROW_TILE:
        found = jnp.stack(
            [
                low(
                    sum(
                        lax.dot_general(a, b, transposed, preferred_element_type=jnp.float32)
                        for a, b in [(left, right)]
                        + [(ends[:, width:], starts[:, :width]) for ends, starts in packets]
                    )
                ).reshape(acrosses, seqs, tap_peers, ffn_rows, width)
                for left, right, packets in pairs
            ],
            3,
        )
        return [found[a] for a in range(acrosses)], jnp.zeros(TOKEN.shape, TOKEN.dtype)

    def kernel(*refs):
        out_refs, token_ref = refs[-1 - acrosses : -1], refs[-1]
        token_ref[...] = jnp.zeros(TOKEN.shape, TOKEN.dtype)
        for which in range(2):
            base = 2 * cores * which
            found = low(
                sum(
                    lax.dot_general(
                        refs[base + 2 * c][...],
                        refs[base + 2 * c + 1][...],
                        transposed,
                        preferred_element_type=jnp.float32,
                    )
                    for c in range(cores)
                )
            ).reshape(tap_peers, ffn_rows, width)
            for a in range(acrosses):

                @pl.when(pl.program_id(0) // seqs == a)
                def _(a=a):
                    out_refs[a][0, :, which] = found

    right_spec = pl.BlockSpec((rows, width), lambda g: (0, 0))
    left_spec = pl.BlockSpec((rows, block), lambda g: (0, g))
    late_spec = pl.BlockSpec((rows, block), lambda g: (0, width // block + g))

    def out_spec(a):
        return pl.BlockSpec(
            (1, tap_peers, 2, ffn_rows, width),
            lambda g: (jnp.clip(g - a * seqs, 0, seqs - 1), 0, 0, 0, 0),
        )

    shape = jax.ShapeDtypeStruct((seqs, tap_peers, 2, ffn_rows, width), jnp.bfloat16)
    operands = []
    for left, right, packets in pairs:
        operands += [left, right]
        for ends, starts in packets:
            operands += [ends, starts]
    found = pl.pallas_call(
        kernel,
        grid=(acrosses * seqs,),
        in_specs=([left_spec, right_spec] + [late_spec, right_spec] * (cores - 1)) * 2
        + tokens(after),
        out_specs=[out_spec(a) for a in range(acrosses)] + [TOKEN_SPEC],
        out_shape=[shape] * acrosses + [TOKEN],
        compiler_params=pltpu.CompilerParams(vmem_limit_bytes=VMEM_BYTES),
        cost_estimate=SMALL_COST,
        name="ffn_weight_grad",
    )(*operands, *after)
    return found[:-1], found[-1]


def merge_slots(conv_parts, ffn_parts, slots, after=()):
    lanes, width = conv_parts[0].shape[-1], ffn_parts[0].shape[-1]
    cuts = width // lanes
    conv_rows = conv_parts[0].size // (slots * lanes)
    ffn_rows = ffn_parts[0].size // (slots * width)
    conv_parts = [part.reshape(slots, conv_rows, lanes) for part in conv_parts]
    ffn_parts = [part.reshape(slots, ffn_rows, width) for part in ffn_parts]
    if conv_rows % ROW_TILE or ffn_rows % ROW_TILE:
        conv_sum = low(sum(wide(part) for part in conv_parts))
        ffn_sum = low(sum(wide(part) for part in ffn_parts))
        merged = jnp.concatenate(
            [conv_sum] + [ffn_sum[:, :, i * lanes : (i + 1) * lanes] for i in range(cuts)], 1
        )
        return [merged[slot] for slot in range(slots)], after

    def kernel(*refs):
        out_refs, token_ref = refs[-1 - slots : -1], refs[-1]
        token_ref[...] = jnp.zeros(TOKEN.shape, TOKEN.dtype)
        count = len(conv_parts)
        for slot in range(slots):
            out_refs[slot][:conv_rows] = low(sum(wide(refs[i][slot]) for i in range(count)))
            total = low(sum(wide(refs[count + i][slot]) for i in range(len(ffn_parts))))
            for i in range(cuts):
                first = conv_rows + i * ffn_rows
                out_refs[slot][first : first + ffn_rows] = total[:, i * lanes : (i + 1) * lanes]

    found = pl.pallas_call(
        kernel,
        in_specs=[WHOLE] * (len(conv_parts) + len(ffn_parts) + len(after)),
        out_specs=[WHOLE] * (slots + 1),
        out_shape=[jax.ShapeDtypeStruct((conv_rows + cuts * ffn_rows, lanes), jnp.bfloat16)] * slots
        + [TOKEN],
        compiler_params=pltpu.CompilerParams(vmem_limit_bytes=VMEM_BYTES),
        cost_estimate=SMALL_COST,
        name="merge_slots",
    )(*conv_parts, *ffn_parts, *after)
    return found[:slots], (found[slots],)


def finish_conv(parts, conv_rows, after=()):
    blocks, count = len(parts), len(parts[0])
    lanes = parts[0][0].shape[-1]
    flat = [part for block in parts for part in block]
    if conv_rows % ROW_TILE:
        sums = [sum(wide(part[:conv_rows]) for part in block) for block in parts]
        return jnp.concatenate([low(total) for total in sums]), after

    def kernel(*refs):
        shard_ref, token_ref = refs[-2:]
        token_ref[...] = jnp.zeros(TOKEN.shape, TOKEN.dtype)
        for b in range(blocks):
            total = sum(wide(refs[b * count + i][:conv_rows]) for i in range(count))
            shard_ref[b * conv_rows : (b + 1) * conv_rows] = low(total)

    found = pl.pallas_call(
        kernel,
        in_specs=[WHOLE] * (len(flat) + len(after)),
        out_specs=[WHOLE] * 2,
        out_shape=[jax.ShapeDtypeStruct((blocks * conv_rows, lanes), jnp.bfloat16), TOKEN],
        compiler_params=pltpu.CompilerParams(vmem_limit_bytes=VMEM_BYTES),
        cost_estimate=SMALL_COST,
        name="finish_conv",
    )(*flat, *after)
    return found[0], (found[1],)


def finish_ffn(merged, plain, conv_rows, ffn_rows, after=()):
    lanes, width = merged[0].shape[-1], plain[0].shape[-1]

    def cut_back(total):
        size = 2 * ffn_rows
        return jnp.concatenate(
            [total[i * size : (i + 1) * size] for i in range(width // lanes)], 1
        )

    if conv_rows % ROW_TILE or ffn_rows % ROW_TILE:
        sums = [sum(wide(part) for part in plain)]
        sums.append(cut_back(sum(wide(part[conv_rows:]) for part in merged)))
        return jnp.stack([each[:ffn_rows].T for each in sums]), jnp.stack(
            [each[ffn_rows:] for each in sums]
        ), after

    def kernel(*refs):
        in_ref, out_ref, token_ref = refs[-3:]
        token_ref[...] = jnp.zeros(TOKEN.shape, TOKEN.dtype)
        late = sum(wide(refs[i][conv_rows:]) for i in range(len(merged)))
        sums = [sum(wide(refs[len(merged) + i][...]) for i in range(len(plain))), cut_back(late)]
        for b in range(2):
            in_ref[b] = sums[b][:ffn_rows].T
            out_ref[b] = sums[b][ffn_rows:]

    found = pl.pallas_call(
        kernel,
        in_specs=[WHOLE] * (len(merged) + len(plain) + len(after)),
        out_specs=[WHOLE] * 3,
        out_shape=(
            jax.ShapeDtypeStruct((2, width, ffn_rows), jnp.float32),
            jax.ShapeDtypeStruct((2, ffn_rows, width), jnp.float32),
            TOKEN,
        ),
        compiler_params=pltpu.CompilerParams(vmem_limit_bytes=VMEM_BYTES),
        cost_estimate=SMALL_COST,
        name="finish_ffn",
    )(*merged, *plain, *after)
    return found[0], found[1], (found[2],)


def add_slots(parts, slots, after=(), reads=()):
    lanes = parts[0].shape[-1]
    rows = parts[0].size // (slots * lanes)
    parts = [part.reshape(slots, rows, lanes) for part in parts]
    block = rows // 4 if rows % (4 * ROW_TILE) == 0 else rows

    def kernel(*refs):
        out_refs, token_ref = refs[-1 - slots : -1], refs[-1]
        token_ref[...] = jnp.zeros(TOKEN.shape, TOKEN.dtype)
        for slot in range(slots):
            out_refs[slot][...] = low(sum(wide(refs[i][slot]) for i in range(len(parts))))

    found = pl.pallas_call(
        kernel,
        grid=(rows // block,),
        in_specs=[pl.BlockSpec((slots, block, lanes), lambda g: (0, g, 0))] * len(parts)
        + tokens(after)
        + [ANYWHERE] * len(reads),
        out_specs=[pl.BlockSpec((block, lanes), lambda g: (g, 0))] * slots + [TOKEN_SPEC],
        out_shape=[jax.ShapeDtypeStruct((rows, lanes), jnp.bfloat16)] * slots + [TOKEN],
        compiler_params=pltpu.CompilerParams(vmem_limit_bytes=VMEM_BYTES),
        cost_estimate=SMALL_COST,
        name="add_slots",
    )(*parts, *after, *reads)
    return found[:slots], found[slots]


def place_conv_grads(stacks, places, sizes):
    cores, seqs, acrosses = sizes[:3]
    blocks, taps, slab, lanes = stacks[0].shape[1:]
    channels = slab * seqs * acrosses
    if slab % ROW_TILE:
        full = jnp.stack([each.reshape((seqs, acrosses) + each.shape[1:]) for each in stacks])
        for axis, (place, size) in enumerate(zip(places[:3], sizes[:3])):
            full = relative(full, axis, place, size)
        return wide(
            full.transpose(3, 4, 1, 2, 5, 0, 6).reshape(blocks, taps, channels, cores * lanes)
        )

    def kernel(place_ref, *refs):
        out_ref = refs[-1]
        for c in range(cores):
            lane = pl.multiple_of(lax.rem(place_ref[0] - c + cores, cores) * lanes, lanes)
            for s in range(seqs):
                at_s = lax.rem(place_ref[1] - s + seqs, seqs)
                for a in range(acrosses):
                    at_a = lax.rem(place_ref[2] - a + acrosses, acrosses)
                    row = pl.multiple_of((at_s * acrosses + at_a) * slab, slab)
                    for b in range(blocks):
                        piece = wide(refs[c][s * acrosses + a, b, 0])
                        out_ref[b, 0, pl.ds(row, slab), pl.ds(lane, lanes)] = piece

    return pl.pallas_call(
        kernel,
        grid_spec=pltpu.PrefetchScalarGridSpec(
            num_scalar_prefetch=1,
            grid=(taps,),
            in_specs=[
                pl.BlockSpec(
                    (seqs * acrosses, blocks, 1, slab, lanes), lambda k, place: (0, 0, k, 0, 0)
                )
            ]
            * cores,
            out_specs=pl.BlockSpec(
                (blocks, 1, channels, cores * lanes), lambda k, place: (0, k, 0, 0)
            ),
        ),
        out_shape=jax.ShapeDtypeStruct((blocks, taps, channels, cores * lanes), jnp.float32),
        compiler_params=pltpu.CompilerParams(vmem_limit_bytes=VMEM_BYTES),
        cost_estimate=SMALL_COST,
        name="place_conv_grads",
    )(jnp.stack(places[:3]).astype(jnp.int32), *stacks)


def copy_all(copies):
    for copy in copies:
        copy.start()
    for copy in copies:
        copy.wait()


def place_conv(pieces, places, sizes, after=(), reads=()):
    cores, seqs, acrosses, tap_peers = sizes
    taps, slab, lanes = pieces[0][0].shape[2:]
    inner = slab * seqs * acrosses * tap_peers
    if slab % ROW_TILE:
        full = jnp.stack([jnp.stack(row) for row in pieces])
        for axis, (place, size) in enumerate(zip(places, sizes)):
            full = relative(full, axis, place, size)
        return full.transpose(4, 3, 1, 2, 5, 0, 6).reshape(taps, inner, cores * lanes), after
    flat = [piece for row in pieces for piece in row]

    def kernel(place_ref, *refs):
        out_ref, token_ref, sem_ref = refs[-3:]
        token_ref[...] = jnp.zeros(TOKEN.shape, TOKEN.dtype)
        copies = []
        for c in range(cores):
            lane = lax.rem(place_ref[0] - c + cores, cores) * lanes
            for s in range(seqs):
                at_s = lax.rem(place_ref[1] - s + seqs, seqs)
                for a in range(acrosses):
                    at_a = lax.rem(place_ref[2] - a + acrosses, acrosses)
                    for t in range(tap_peers):
                        at_t = lax.rem(place_ref[3] - t + tap_peers, tap_peers)
                        row = ((at_t * seqs + at_s) * acrosses + at_a) * slab
                        copies.append(
                            pltpu.make_async_copy(
                                refs[c * seqs + s].at[a, t],
                                out_ref.at[
                                    :,
                                    pl.ds(pl.multiple_of(row, slab), slab),
                                    pl.ds(pl.multiple_of(lane, lanes), lanes),
                                ],
                                sem_ref.at[len(copies)],
                            )
                        )
        copy_all(copies)

    found = pl.pallas_call(
        kernel,
        in_specs=[SCALARS] + [ANYWHERE] * (len(flat) + len(reads)) + [WHOLE] * len(after),
        out_specs=[WHOLE] * 2,
        out_shape=[jax.ShapeDtypeStruct((taps, inner, cores * lanes), jnp.bfloat16), TOKEN],
        scratch_shapes=[pltpu.SemaphoreType.DMA((cores * seqs * acrosses * tap_peers,))],
        compiler_params=pltpu.CompilerParams(vmem_limit_bytes=VMEM_BYTES),
        cost_estimate=SMALL_COST,
        name="place_conv",
    )(jnp.stack(places).astype(jnp.int32), *flat, *reads, *after)
    return found[0], (found[1],)


def place_ffn(pieces, sizes, after=(), reads=()):
    cores, seqs, acrosses, tap_peers = sizes
    cuts, ffn_rows, lanes = pieces[0][0].shape[2:]
    cuts //= 2
    width = cuts * lanes
    units = seqs * acrosses * tap_peers * ffn_rows
    if ffn_rows % ROW_TILE:
        full = jnp.stack([jnp.stack(row) for row in pieces])
        full = full.reshape(cores, acrosses, seqs, tap_peers, 2, cuts, ffn_rows, lanes)
        full = full.transpose(4, 0, 1, 2, 3, 6, 5, 7).reshape(2, cores, units, width)
        return [full[0, c] for c in range(cores)], [full[1, c] for c in range(cores)], after
    flat = [piece for row in pieces for piece in row]

    def kernel(*refs):
        out_refs = refs[-2 - 2 * cores : -2]
        token_ref, sem_ref = refs[-2:]
        token_ref[...] = jnp.zeros(TOKEN.shape, TOKEN.dtype)
        copies = []
        for c in range(cores):
            for a in range(acrosses):
                for which in range(2):
                    for cut in range(cuts):
                        copies.append(
                            pltpu.make_async_copy(
                                refs[c * acrosses + a].at[:, :, which * cuts + cut],
                                out_refs[which * cores + c].at[
                                    a, :, :, :, pl.ds(cut * lanes, lanes)
                                ],
                                sem_ref.at[len(copies)],
                            )
                        )
        copy_all(copies)

    shape = jax.ShapeDtypeStruct((acrosses, seqs, tap_peers, ffn_rows, width), jnp.bfloat16)
    found = pl.pallas_call(
        kernel,
        in_specs=[ANYWHERE] * (len(flat) + len(reads)) + [WHOLE] * len(after),
        out_specs=[WHOLE] * (2 * cores + 1),
        out_shape=[shape] * (2 * cores) + [TOKEN],
        scratch_shapes=[pltpu.SemaphoreType.DMA((2 * cores * acrosses * cuts,))],
        compiler_params=pltpu.CompilerParams(vmem_limit_bytes=VMEM_BYTES),
        cost_estimate=SMALL_COST,
        name="place_ffn",
    )(*flat, *reads, *after)
    token = found[-1]
    found = [each.reshape(units, width) for each in found[:-1]]
    return found[:cores], found[cores:], (token,)


class Ring:
    def __init__(self, axis, size, index, pairs):
        self.axis, self.size, self.index, self.pairs = axis, size, index, pairs

    def shifted(self, value, by):
        return lax.ppermute(value, self.axis, self.pairs(lambda i: (i + by) % self.size))

    def swapped(self, value, bit):
        return lax.ppermute(value, self.axis, self.pairs(lambda i: i ^ bit))

    def gather(self, value):
        return [value] + [self.shifted(value, by) for by in range(1, self.size)]

    def swap(self, values):
        return [values[0]] + [self.shifted(values[by], -by) for by in range(1, self.size)]


def relative(value, axis, place, size):
    if size == 1:
        return value
    return jnp.stack(
        [
            lax.dynamic_index_in_dim(value, (place - slot) % size, axis, False)
            for slot in range(size)
        ],
        axis,
    )


def rings():
    peers = lax.axis_size("dp")
    cores = CORES if peers % CORES == 0 else 1
    columns = peers // cores
    place = lax.axis_index("dp")

    def plain(axis):
        size = lax.axis_size(axis)
        return Ring(
            axis, size, lax.axis_index(axis), lambda move: [(i, move(i)) for i in range(size)]
        )

    across = Ring(
        "dp",
        columns,
        place // cores,
        lambda move: [(i, move(i // cores) * cores + i % cores) for i in range(peers)],
    )
    core = Ring(
        "dp",
        cores,
        place % cores,
        lambda move: [(i, i // cores * cores + move(i % cores)) for i in range(peers)],
    )
    return core, across, plain("seq"), plain("tap")


class Reduce:
    def __init__(self, terms, order):
        self.order = order
        self.parts = [terms[0]] + [order[0].shifted(terms[s], -s) for s in range(1, order[0].size)]

    def step(self, level, after, reads=()):
        ring = self.order[level]
        found, token = add_slots(self.parts, ring.size, after, reads)
        self.parts = [found[0]] + [ring.shifted(found[s], -s) for s in range(1, ring.size)]
        return (token,)


def shared_copies(value, across, seq):
    peers, spans = lax.axis_size("dp"), lax.axis_size("seq")
    cores = peers // across.size

    def target(place, by_a, by_s):
        dp, at = place // spans, place % spans
        moved = (dp // cores + by_a) % across.size * cores + dp % cores
        return moved * spans + (at + by_s) % spans

    return [
        [
            value
            if by_a == by_s == 0
            else lax.ppermute(
                value,
                ("dp", "seq"),
                [(place, target(place, by_a, by_s)) for place in range(peers * spans)],
            )
            for by_a in range(across.size)
        ]
        for by_s in range(seq.size)
    ]


def summed(value, order):
    if any(ring.size & (ring.size - 1) for ring in order):
        return lax.psum(value, ("dp", "seq", "tap"))
    for ring in order:
        bit = 1
        while bit < ring.size:
            value = value + ring.swapped(value, bit)
            bit *= 2
    return value


def passed_along(value, axis, by):
    peers = lax.axis_size(axis)
    pairs = [(i, i + by) for i in range(peers) if 0 <= i + by < peers]
    return lax.ppermute(value, axis, pairs)


def rims(source, reach_rows):
    span_rows = source.shape[0]
    left_parts = []
    right_parts = []
    distances = -(-reach_rows // span_rows)
    for distance in range(1, distances + 1):
        rim_count = min(span_rows, reach_rows - (distance - 1) * span_rows)
        left_parts.insert(0, passed_along(source[span_rows - rim_count :], "seq", distance))
        right_parts.append(passed_along(source[:rim_count], "seq", -distance))
    return left_parts, right_parts


def to_rows(values):
    windows, positions = values.shape[:2]
    cut = values.reshape((windows, positions // FIRST_DILATION, FIRST_DILATION) + values.shape[2:])
    return jnp.swapaxes(cut, 0, 1).reshape((windows * positions,) + values.shape[2:])


def from_rows(values, windows):
    cut = values.reshape((-1, windows, FIRST_DILATION) + values.shape[1:])
    return jnp.swapaxes(cut, 0, 1).reshape((windows, -1) + values.shape[1:])


def on_device(
    inputs,
    targets,
    masked,
    conv_weight,
    conv_bias,
    gains,
    shifts,
    in_weight,
    in_bias,
    out_weight,
    out_bias,
    head_weight,
):
    core, across, seq, tap = rings()
    taps = conv_weight.shape[1]
    channels = conv_weight.shape[2]
    width = conv_weight.shape[3]
    slab = channels // (seq.size * across.size)
    lanes = width // core.size
    hidden_width = in_bias.shape[1]
    ffn_rows = in_weight.shape[2]
    windows = inputs.shape[0]
    rows = windows * inputs.shape[1]
    steps = (FIRST_DILATION * windows, SECOND_DILATION * windows)
    units = hidden_width // core.size
    places = (core.index, seq.index, across.index, tap.index)
    sizes = (core.size, seq.size, across.size, tap.size)

    in_bias_placed = []
    for b in range(2):
        bias = in_bias[b].reshape(across.size, core.size, seq.size, tap.size, ffn_rows)
        for axis, ring in enumerate((across, core, seq, tap)):
            bias = relative(bias, axis, ring.index, ring.size)
        in_bias_placed.append(bias.transpose(1, 0, 2, 3, 4).reshape(core.size, units))

    def cut_ffn(piece):
        return piece.reshape(ffn_rows, core.size, lanes).swapaxes(0, 1).reshape(-1, lanes)

    def bundle(b):
        conv_piece = lax.dynamic_slice(
            conv_weight[b],
            (0, (seq.index * across.size + across.index) * slab, core.index * lanes),
            (taps, slab, lanes),
        )
        pieces = [
            conv_piece.reshape(taps * slab, lanes),
            cut_ffn(in_weight[b].T),
            cut_ffn(out_weight[b]),
        ]
        return jnp.concatenate(pieces)

    cuts = (
        (0, taps * slab, (taps, slab, lanes)),
        (taps * slab, taps * slab + 2 * core.size * ffn_rows, (2 * core.size, ffn_rows, lanes)),
    )

    def straight(arrays):
        return (arrays, ((0, None, arrays[0].shape),))

    conv_input = to_rows(inputs)
    stream = conv_input
    codes = to_rows(targets + masked * head_weight.shape[1])
    codes = jnp.broadcast_to(codes[:, None], (rows, 128))

    tap_parts = tap.gather(bundle(0))
    (conv_part, ffn_part), last = restack([(tap_parts, cuts)])
    left, right = rims(conv_input, taps // 2 * steps[0])
    extended, last = join_rows(left + [conv_input] + right, last)
    extended_parts = [extended] + [core.shifted(extended, -c) for c in range(1, core.size)]
    late_taps = lax.all_gather(bundle(1) + conv_part[0, 0, 0, 0] * 0, "tap", axis=0)
    conv_parts, ffn_parts = across.gather(conv_part), seq.gather(ffn_part)
    (conv_part, ffn_part), last = restack(
        [straight(conv_parts), straight(ffn_parts)], after=last
    )
    conv_parts, ffn_parts = seq.gather(conv_part), across.gather(ffn_part)
    conv_slots = [core.gather(conv_part)]
    ffn_slots = [core.gather(ffn_part)]
    (late_conv, late_ffn), last = restack(
        [([late_taps], cuts)],
        reads=conv_parts[1:] + ffn_parts[1:] + conv_slots[0][1:] + ffn_slots[0][1:],
        after=last,
        turn=tap.index,
    )
    conv_slots += [core.gather(each) for each in conv_parts[1:]]
    ffn_slots += [core.gather(each) for each in ffn_parts[1:]]
    late_conv_parts, late_ffn_parts = across.gather(late_conv), seq.gather(late_ffn)

    def turned(slots):
        return [[each[c] for each in slots] for c in range(core.size)]

    conv_full, in_full, out_full = [None, None], [None, None], [None, None]
    conv_full[0], last = place_conv(
        turned(conv_slots), places, sizes, last, [part for each in ffn_slots for part in each[1:]]
    )
    (late_conv, late_ffn), last = restack(
        [straight(late_conv_parts), straight(late_ffn_parts)], after=last
    )
    late_conv_parts, late_ffn_parts = seq.gather(late_conv), across.gather(late_ffn)
    late_conv_slots = [core.gather(late_conv)]
    late_ffn_slots = [core.gather(late_ffn)]

    saved = []
    reads = []
    for b in range(2):
        if b == 1:
            conv_full[1], last = place_conv(turned(late_conv_slots), places, sizes, last)
            in_full[1], out_full[1], last = place_ffn(turned(late_ffn_slots), sizes, last)
            left, right = rims(conv_input, taps // 2 * steps[1])
            extended, last = join_rows(left + [conv_input] + right, last)
            extended_parts = [extended] + [core.shifted(extended, -c) for c in range(1, core.size)]
        (normed_conv, conv_slope, stream, lowered), last = conv_forward(
            extended,
            conv_full[b],
            stream,
            conv_bias[b],
            gains[b, 0],
            shifts[b, 0],
            steps[b],
            last,
            reads,
        )
        reads = []
        if b == 0:
            in_full[0], out_full[0], last = place_ffn(
                turned(ffn_slots),
                sizes,
                last,
                late_conv_slots[0][1:] + late_ffn_slots[0][1:] + extended_parts[1:],
            )
            held, last = hold(late_conv_parts[1:] + late_ffn_parts[1:], last)
            late_conv_slots += [core.gather(each) for each in held[: seq.size - 1]]
            late_ffn_slots += [core.gather(each) for each in held[seq.size - 1 :]]
        else:
            reads = extended_parts[1:]
        active, hidden_slopes, (normed_ffn, scale_ffn, stream, conv_input), packets, last = (
            ffn_forward(
                lowered,
                stream,
                in_full[b],
                out_full[b],
                [in_bias_placed[b][c] for c in range(core.size)],
                out_bias[b],
                gains[b, 1],
                shifts[b, 1],
                last,
                reads,
            )
        )
        packets = [core.shifted(packet, -1 - c) for c, packet in enumerate(packets)]
        reads = packets
        saved.append(
            (
                extended_parts,
                conv_slope,
                normed_conv,
                (active, lowered, packets),
                hidden_slopes,
                normed_ffn,
                scale_ffn,
            )
        )

    final_state = from_rows(conv_input, windows)
    (stream_grad, head_grad, loss_rows), last = head_and_loss(stream, head_weight, codes, last)

    ffn_rows_of_sums = [None, None]
    conv_rows_of_sums = [None, None]
    in_bias_grads = [None, None]
    ffn_sums = [None, None]
    conv_sums = [None, None]
    merged = [None, None]

    def small():
        return [
            jnp.stack([conv_rows_of_sums[b][2] for b in range(2)]),
            jnp.stack([jnp.stack([conv_rows_of_sums[b][0], ffn_rows_of_sums[b][0]]) for b in range(2)]),
            jnp.stack([jnp.stack([conv_rows_of_sums[b][1], ffn_rows_of_sums[b][1]]) for b in range(2)]),
            jnp.stack(in_bias_grads),
            jnp.stack([ffn_rows_of_sums[b][2] for b in range(2)]),
            head_grad[: head_weight.shape[1]],
            jnp.pad(loss_rows[:2, 0], (0, width - 2)),
        ]

    for b in (1, 0):
        (
            extended_parts,
            conv_slope,
            normed_conv,
            active_pair,
            hidden_slopes,
            normed_ffn,
            scale_ffn,
        ) = saved[b]
        output_grad, hidden_grad, biases, packets, ffn_rows_of_sums[b], last = ffn_back_hidden(
            stream_grad, normed_ffn, scale_ffn, gains[b, 1], out_full[b], hidden_slopes, last
        )
        if b == 1:
            arrived_packets = [core.shifted(packet, -1 - c) for c, packet in enumerate(packets)]
        if b == 0:
            last = ffn_sums[1].step(1, last, [final_state])
            last = conv_sums[1].step(1, last)
        stream_grad, conv_grad, conv_cuts, relayed, conv_rows_of_sums[b], last = ffn_back_stream(
            stream_grad,
            hidden_grad,
            packets,
            in_full[b],
            normed_conv,
            conv_slope,
            gains[b, 0],
            core.index,
            last,
            reads,
            relay=b == 0,
        )
        reads = []
        if b == 0:
            arrived_packets = [core.shifted(packet, -1 - c) for c, packet in enumerate(relayed)]
        arrived = [core.shifted(conv_cuts[c - 1], -c) for c in range(1, core.size)]
        bias = jnp.stack(biases).reshape(core.size, across.size, seq.size, tap.size, ffn_rows)
        for axis, ring in enumerate((core, across, seq, tap)):
            bias = relative(bias, axis, ring.index, ring.size)
        in_bias_grads[b] = bias.transpose(1, 0, 2, 3, 4).reshape(hidden_width)
        left, right = rims(conv_grad, taps // 2 * steps[b])

        def ffn_grads(last):
            active, lowered, packets = active_pair
            if core.size == 1:
                packets = []
            found, token = ffn_weight_grad(
                (
                    (hidden_grad, lowered, [(g, p) for g, p in zip(arrived_packets, packets)]),
                    (active, output_grad, [(p, g) for g, p in zip(arrived_packets, packets)]),
                ),
                sizes,
                ffn_rows,
                last,
            )
            return Reduce(found, (across, seq, tap)), (token,)

        def conv_grads(last, reads=()):
            found, token = conv_weight_grad(
                extended_parts, conv_grad, arrived, places, sizes, taps, steps[b], last, reads
            )
            found = [each.reshape(-1, lanes) for each in found]
            return Reduce(found, (seq, across, tap)), (token,)

        if b == 1:
            ffn_sums[1], last = ffn_grads(last)
            extended_grad, last = join_rows(left + [conv_grad] + right, last)
            conv_sums[1], last = conv_grads(last)
        else:
            extended_grad, last = join_rows(left + [conv_grad] + right, last)
            conv_sums[0], last = conv_grads(last)
            packed = jnp.concatenate([each.reshape(-1, width) for each in small()]) + last[0][0, 0]
            packed = lax.all_gather(packed, ("dp", "seq", "tap"), axis=0)
            merged[1], last = merge_slots(conv_sums[1].parts, ffn_sums[1].parts, tap.size, last)
            merged[1] = tap.swap(merged[1])
            ffn_sums[0], last = ffn_grads(last)
        stream_grad, last = conv_data_grad(
            extended_grad,
            conv_full[b],
            stream_grad,
            steps[b],
            jnp.float32 if b == 1 else jnp.bfloat16,
            last,
        )

    grad_inputs = from_rows(stream_grad, windows)
    last = conv_sums[0].step(1, last, merged[1][1:] + [grad_inputs])
    last = ffn_sums[0].step(1, last)
    last = conv_sums[0].step(2, last)
    last = ffn_sums[0].step(2, last)
    shards, last = finish_conv([conv_sums[0].parts, merged[1]], taps * slab, last)
    copies = [each for row in shared_copies(shards, across, seq) for each in row]
    grad_in, grad_out, last = finish_ffn(
        merged[1], ffn_sums[0].parts, taps * slab, ffn_rows, last
    )
    (stack,), last = restack([straight(copies)], after=last)
    grad_conv = place_conv_grads(
        [each.reshape(len(copies), 2, taps, slab, lanes) for each in core.gather(stack)],
        places,
        sizes,
    )

    packed = jnp.sum(packed, 0)
    unpacked = []
    first = 0
    for each in small():
        count = each.size // width
        unpacked.append(packed[first : first + count].reshape(each.shape))
        first += count
    (
        grad_conv_bias,
        grad_gains,
        grad_shifts,
        grad_in_bias,
        grad_out_bias,
        grad_head_weight,
        loss_terms,
    ) = unpacked
    return (
        final_state,
        grad_inputs,
        grad_conv,
        grad_conv_bias,
        grad_gains,
        grad_shifts,
        grad_in,
        grad_in_bias,
        grad_out,
        grad_out_bias,
        grad_head_weight.T,
        loss_terms[0] / loss_terms[1],
    )


def solution(mesh):
    placed = (
        P(("dp", "tap"), "seq", None),
        P(("dp", "tap"), "seq"),
        P(("dp", "tap"), "seq"),
        P(None, None, "tap", None),
        P(),
        P(),
        P(),
        P(None, None, ("dp", "seq", "tap")),
        P(),
        P(None, ("dp", "seq", "tap"), None),
        P(),
        P(),
    )
    return jax.shard_map(
        on_device,
        mesh=mesh,
        in_specs=placed,
        out_specs=(
            P(("dp", "tap"), "seq", None),
            P(("dp", "tap"), "seq", None),
            P(None, None, "tap", None),
            P(),
            P(),
            P(),
            P(None, None, ("dp", "seq", "tap")),
            P(),
            P(None, ("dp", "seq", "tap"), None),
            P(),
            P(),
            P(),
        ),
        check_vma=False,
    )
```

```python
import functools

import jax
import jax.numpy as jnp
from jax import lax
from jax.experimental import pallas as pl
from jax.experimental.pallas import tpu as pltpu
from jax.sharding import PartitionSpec as P

FIRST_DILATION = 4
SECOND_DILATION = 32
EPSILON = 1e-05
HIGHEST_PRECISION = lax.Precision.HIGHEST
CORES = 2
ROW_TILE = 16
VMEM_BYTES = 36 * 1024 * 1024
ANYWHERE = pl.BlockSpec(memory_space=pl.ANY)
SCALARS = pl.BlockSpec(memory_space=pltpu.SMEM)


TOKEN = jax.ShapeDtypeStruct((8, 128), jnp.float32)
SMALL_COST = pl.CostEstimate(flops=1024, bytes_accessed=1024, transcendentals=0)
WHOLE = pl.BlockSpec(memory_space=pltpu.VMEM)
TOKEN_SPEC = pl.BlockSpec(TOKEN.shape, lambda *_: (0, 0))


def tokens(after):
    return [TOKEN_SPEC] * len(after)


def low(values):
    return values.astype(jnp.bfloat16)


def wide(values):
    return values.astype(jnp.float32)


def gelu_parts(values):
    phi = 0.5 * (1.0 + lax.erf(values * 0.7071067811865476))
    return (
        values * phi,
        phi + values * jnp.exp(-0.5 * values * values) * 0.3989422804014327,
    )


def normalize(values):
    center = values - jnp.mean(values, -1, keepdims=True)
    scale = lax.rsqrt(jnp.mean(center * center, -1, keepdims=True) + EPSILON)
    return (center * scale, scale)


def norm_back(upstream, normed, scale):
    return scale * (
        upstream
        - jnp.mean(upstream, -1, keepdims=True)
        - normed * jnp.mean(upstream * normed, -1, keepdims=True)
    )


def tap_groups(taps):
    return 3 if taps % 3 == 0 else 1


def row_chunks(rows, most):
    size = min(rows, most)
    return [(first, size) for first in range(0, rows, size)]


def conv_forward(extended, weight, stream, bias, gain, shift, step, after=(), reads=()):
    taps, inner, width = weight.shape
    rows = stream.shape[0]
    group = tap_groups(taps)
    steps = taps // group

    def kernel(extended_ref, weight_ref, stream_ref, bias_ref, gain_ref, shift_ref, *refs):
        normed_ref, slope_ref, next_ref, lowered_ref, token_ref, total_ref = refs[-6:]
        token_ref[...] = jnp.zeros(TOKEN.shape, TOKEN.dtype)
        first = pl.program_id(0) * group
        total = None
        for j in range(group):
            start = pl.multiple_of((first + j) * step, ROW_TILE)
            term = jnp.dot(
                extended_ref[pl.ds(start, rows), :],
                weight_ref[j],
                preferred_element_type=jnp.float32,
            )
            total = term if total is None else total + term

        @pl.when(pl.program_id(0) == 0)
        def _():
            total_ref[...] = total

        @pl.when(pl.program_id(0) > 0)
        def _():
            total_ref[...] += total

        @pl.when(pl.program_id(0) == steps - 1)
        def _():
            for at, size in row_chunks(rows, 128):
                some = pl.ds(at, size)
                value, slope = gelu_parts(total_ref[some, :] + bias_ref[...])
                normed, scale = normalize(value)
                mid = wide(stream_ref[some, :]) + normed * gain_ref[...] + shift_ref[...]
                normed_ref[some, :] = low(normed)
                slope_ref[some, :] = low(scale * slope)
                next_ref[some, :] = mid
                lowered_ref[some, :] = low(mid)

    whole = pl.BlockSpec((rows, width), lambda g: (0, 0))
    row = pl.BlockSpec((1, width), lambda g: (0, 0))
    found = pl.pallas_call(
        kernel,
        grid=(steps,),
        in_specs=[
            pl.BlockSpec(extended.shape, lambda g: (0, 0)),
            pl.BlockSpec((group, inner, width), lambda g: (g, 0, 0)),
            whole,
            row,
            row,
            row,
        ]
        + tokens(after)
        + [ANYWHERE] * len(reads),
        out_specs=[whole] * 4 + [TOKEN_SPEC],
        out_shape=[
            jax.ShapeDtypeStruct((rows, width), jnp.bfloat16),
            jax.ShapeDtypeStruct((rows, width), jnp.bfloat16),
            jax.ShapeDtypeStruct((rows, width), jnp.float32),
            jax.ShapeDtypeStruct((rows, width), jnp.bfloat16),
            TOKEN,
        ],
        scratch_shapes=[pltpu.VMEM((rows, width), jnp.float32)],
        compiler_params=pltpu.CompilerParams(vmem_limit_bytes=VMEM_BYTES),
        cost_estimate=SMALL_COST,
        name="conv_forward",
    )(extended, weight, stream, bias[None], gain[None], shift[None], *after, *reads)
    return found[:4], (found[4],)


def ffn_forward(
    lowered, stream, ins, outs, in_biases, out_bias, gain, shift, after=(), reads=()
):
    rows, width = lowered.shape
    cores = len(ins)
    units = ins[0].shape[0]
    block = min(units, 256)
    steps = units // block

    def kernel(lowered_ref, stream_ref, out_bias_ref, gain_ref, shift_ref, *refs):
        in_refs, out_refs, bias_refs = (refs[i * cores : (i + 1) * cores] for i in range(3))
        found_refs = refs[-6 - 2 * cores :]
        active_ref, slope_refs = found_refs[0], found_refs[1 : 1 + cores]
        normed_ref, scale_ref, next_ref, rounded_ref = found_refs[1 + cores : 5 + cores]
        packet_refs = found_refs[5 + cores : -2]
        token_ref, total_ref = found_refs[-2:]
        token_ref[...] = jnp.zeros(TOKEN.shape, TOKEN.dtype)
        lane = pl.multiple_of(width + pl.program_id(0) * block, block)

        @pl.when(pl.program_id(0) == 0)
        def _():
            total_ref[...] = jnp.zeros(total_ref.shape, jnp.float32)
            for packet_ref in packet_refs:
                packet_ref[:, :width] = lowered_ref[...]

        for at, size in row_chunks(rows, 512):
            some = pl.ds(at, size)
            term = None
            for c in range(cores):
                hidden = lax.dot_general(
                    lowered_ref[some, :],
                    in_refs[c][...],
                    (((1,), (1,)), ((), ())),
                    preferred_element_type=jnp.float32,
                )
                active, slope = gelu_parts(hidden + bias_refs[c][...])
                active = low(active)
                if c == 0:
                    active_ref[some, :] = active
                else:
                    packet_refs[c - 1][some, pl.ds(lane, block)] = active
                slope_refs[c][some, :] = low(slope)
                found = jnp.dot(active, out_refs[c][...], preferred_element_type=jnp.float32)
                term = found if term is None else term + found
            total_ref[some, :] += term

        @pl.when(pl.program_id(0) == steps - 1)
        def _():
            for at, size in row_chunks(rows, 128):
                some = pl.ds(at, size)
                normed, scale = normalize(total_ref[some, :] + out_bias_ref[...])
                after_ffn = stream_ref[some, :] + normed * gain_ref[...] + shift_ref[...]
                normed_ref[some, :] = low(normed)
                scale_ref[some, :] = jnp.broadcast_to(scale, (size, 128))
                next_ref[some, :] = after_ffn
                rounded_ref[some, :] = low(after_ffn)

    whole = pl.BlockSpec((rows, width), lambda g: (0, 0))
    row = pl.BlockSpec((1, width), lambda g: (0, 0))
    piece = pl.BlockSpec((block, width), lambda g: (g, 0))
    columns = pl.BlockSpec((rows, block), lambda g: (0, g))
    hidden_shape = jax.ShapeDtypeStruct((rows, units), jnp.bfloat16)
    found = pl.pallas_call(
        kernel,
        grid=(steps,),
        in_specs=[whole, whole, row, row, row]
        + [piece] * (2 * cores)
        + [pl.BlockSpec((1, block), lambda g: (0, g))] * cores
        + tokens(after)
        + [ANYWHERE] * len(reads),
        out_specs=[columns] * (1 + cores)
        + [whole, pl.BlockSpec((rows, 128), lambda g: (0, 0)), whole, whole]
        + [pl.BlockSpec((rows, width + units), lambda g: (0, 0))] * (cores - 1)
        + [TOKEN_SPEC],
        out_shape=[hidden_shape] * (1 + cores)
        + [
            jax.ShapeDtypeStruct((rows, width), jnp.bfloat16),
            jax.ShapeDtypeStruct((rows, 128), jnp.float32),
            jax.ShapeDtypeStruct((rows, width), jnp.float32),
            jax.ShapeDtypeStruct((rows, width), jnp.bfloat16),
        ]
        + [jax.ShapeDtypeStruct((rows, width + units), jnp.bfloat16)] * (cores - 1)
        + [TOKEN],
        scratch_shapes=[pltpu.VMEM((rows, width), jnp.float32)],
        compiler_params=pltpu.CompilerParams(vmem_limit_bytes=VMEM_BYTES),
        cost_estimate=SMALL_COST,
        name="ffn_forward",
    )(
        lowered,
        stream,
        out_bias[None],
        gain[None],
        shift[None],
        *ins,
        *outs,
        *[each[None] for each in in_biases],
        *after,
        *reads,
    )
    return (
        found[0],
        found[1 : 1 + cores],
        found[1 + cores : 5 + cores],
        found[5 + cores : -1],
        (found[-1],),
    )


def head_and_loss(stream, head_weight, codes, after=()):
    rows, width = stream.shape
    classes = head_weight.shape[1]
    padded = jnp.pad(head_weight, ((0, 0), (0, 128 - classes)))
    cuts = row_chunks(rows, 256)

    def kernel(stream_ref, head_ref, code_ref, *refs):
        grad_ref, head_grad_ref, sums_ref, token_ref = refs[-4:]
        token_ref[...] = jnp.zeros(TOKEN.shape, TOKEN.dtype)
        head_grad = jnp.zeros((128, width), jnp.float32)
        objective = jnp.zeros((1, 1), jnp.float32)
        scored = jnp.zeros((1, 1), jnp.float32)
        for at, size in cuts:
            some = pl.ds(at, size)
            value = stream_ref[some, :]
            code = code_ref[some, :]
            mask = jnp.where(code[:, :1] >= classes, 1.0, 0.0)
            logits = jnp.dot(
                value, head_ref[...], precision=HIGHEST_PRECISION, preferred_element_type=jnp.float32
            )
            lane = lax.broadcasted_iota(jnp.int32, logits.shape, 1)
            valid = lane < classes
            peak = jnp.max(jnp.where(valid, logits, -jnp.inf), -1, keepdims=True)
            exponent = jnp.where(valid, jnp.exp(jnp.where(valid, logits - peak, 0.0)), 0.0)
            denominator = jnp.sum(exponent, -1, keepdims=True)
            chosen = lane == jnp.where(code >= classes, code - classes, code)
            picked = jnp.sum(jnp.where(chosen, logits, 0.0), -1, keepdims=True)
            terms = mask * (peak + jnp.log(denominator) - picked)
            objective = objective + jnp.sum(terms, 0, keepdims=True)
            scored = scored + jnp.sum(mask, 0, keepdims=True)
            logit_grad = mask * (exponent / denominator - jnp.where(chosen, 1.0, 0.0))
            grad_ref[some, :] = lax.dot_general(
                logit_grad,
                head_ref[...],
                (((1,), (1,)), ((), ())),
                precision=HIGHEST_PRECISION,
                preferred_element_type=jnp.float32,
            )
            head_grad = head_grad + lax.dot_general(
                logit_grad,
                value,
                (((0,), (0,)), ((), ())),
                precision=HIGHEST_PRECISION,
                preferred_element_type=jnp.float32,
            )
        head_grad_ref[...] = head_grad
        at_row = lax.broadcasted_iota(jnp.int32, sums_ref.shape, 0)
        sums_ref[...] = jnp.where(at_row == 0, objective, scored)

    found = pl.pallas_call(
        kernel,
        out_shape=[
            jax.ShapeDtypeStruct((rows, width), jnp.float32),
            jax.ShapeDtypeStruct((128, width), jnp.float32),
            jax.ShapeDtypeStruct((8, 128), jnp.float32),
            TOKEN,
        ],
        compiler_params=pltpu.CompilerParams(vmem_limit_bytes=VMEM_BYTES),
        cost_estimate=SMALL_COST,
        name="head_and_loss",
    )(stream, padded, codes, *after)
    return found[:3], (found[3],)


def ffn_back_hidden(upstream, normed, scale, gain, outs, slopes, after=()):
    rows, width = upstream.shape
    cores = len(outs)
    units = outs[0].shape[0]
    block = min(units, 256)

    def kernel(upstream_ref, normed_ref, scale_ref, gain_ref, *refs):
        out_refs, slope_refs = refs[:cores], refs[cores : 2 * cores]
        found_refs = refs[-3 - 2 * cores :]
        output_grad_ref, hidden_ref = found_refs[:2]
        bias_refs, packet_refs = found_refs[2 : 2 + cores], found_refs[2 + cores : -2]
        sums_ref, token_ref = found_refs[-2:]
        token_ref[...] = jnp.zeros(TOKEN.shape, TOKEN.dtype)
        lane = pl.multiple_of(width + pl.program_id(0) * block, block)

        @pl.when(pl.program_id(0) == 0)
        def _():
            totals = [jnp.zeros((1, width), jnp.float32)] * 3
            for at, size in row_chunks(rows, 128):
                some = pl.ds(at, size)
                grad, value = upstream_ref[some, :], wide(normed_ref[some, :])
                output_grad = low(norm_back(grad * gain_ref[...], value, scale_ref[some, :1]))
                output_grad_ref[some, :] = output_grad
                for packet_ref in packet_refs:
                    packet_ref[some, :width] = output_grad
                for i, each in enumerate((grad * value, grad, wide(output_grad))):
                    totals[i] = totals[i] + jnp.sum(each, 0, keepdims=True)
            sums_ref[...] = jnp.zeros(sums_ref.shape, jnp.float32)
            for i in range(3):
                sums_ref[i : i + 1, :] = totals[i]

        for c in range(cores):
            total = jnp.zeros((1, block), jnp.float32)
            for at, size in row_chunks(rows, 512):
                some = pl.ds(at, size)
                active_grad = lax.dot_general(
                    output_grad_ref[some, :],
                    out_refs[c][...],
                    (((1,), (1,)), ((), ())),
                    preferred_element_type=jnp.float32,
                )
                hidden_grad = low(active_grad * wide(slope_refs[c][some, :]))
                if c == 0:
                    hidden_ref[some, :] = hidden_grad
                else:
                    packet_refs[c - 1][some, pl.ds(lane, block)] = hidden_grad
                total = total + jnp.sum(wide(hidden_grad), 0, keepdims=True)
            bias_refs[c][...] = total

    whole = pl.BlockSpec((rows, width), lambda g: (0, 0))
    columns = pl.BlockSpec((rows, block), lambda g: (0, g))
    found = pl.pallas_call(
        kernel,
        grid=(units // block,),
        in_specs=[
            whole,
            whole,
            pl.BlockSpec((rows, 128), lambda g: (0, 0)),
            pl.BlockSpec((1, width), lambda g: (0, 0)),
        ]
        + [pl.BlockSpec((block, width), lambda g: (g, 0))] * cores
        + [columns] * cores
        + tokens(after),
        out_specs=[whole, columns]
        + [pl.BlockSpec((1, block), lambda g: (0, g))] * cores
        + [pl.BlockSpec((rows, width + units), lambda g: (0, 0))] * (cores - 1)
        + [pl.BlockSpec((8, width), lambda g: (0, 0)), TOKEN_SPEC],
        out_shape=[
            jax.ShapeDtypeStruct((rows, width), jnp.bfloat16),
            jax.ShapeDtypeStruct((rows, units), jnp.bfloat16),
        ]
        + [jax.ShapeDtypeStruct((1, units), jnp.float32)] * cores
        + [jax.ShapeDtypeStruct((rows, width + units), jnp.bfloat16)] * (cores - 1)
        + [jax.ShapeDtypeStruct((8, width), jnp.float32), TOKEN],
        compiler_params=pltpu.CompilerParams(vmem_limit_bytes=VMEM_BYTES),
        cost_estimate=SMALL_COST,
        name="ffn_back_hidden",
    )(upstream, normed, scale, gain[None], *outs, *slopes, *after)
    return (
        found[0],
        found[1],
        found[2 : 2 + cores],
        found[2 + cores : -2],
        found[-2],
        (found[-1],),
    )


def ffn_back_stream(
    upstream, hidden, packets, ins, normed, slope, gain, core_index, after=(), reads=(), relay=False
):
    rows, width = upstream.shape
    cores = len(ins)
    units = ins[0].shape[0]
    block = min(units, 256)
    steps = units // block
    lanes = width // cores
    relays = cores - 1 if relay else 0

    def kernel(core_ref, upstream_ref, normed_ref, slope_ref, gain_ref, *refs):
        hidden_refs, in_refs = refs[:cores], refs[cores : 2 * cores]
        found_refs = refs[-4 - cores - relays :]
        mid_ref, conv_grad_ref = found_refs[:2]
        cut_refs = found_refs[2 : 1 + cores]
        sums_ref, token_ref, total_ref = found_refs[-3:]
        token_ref[...] = jnp.zeros(TOKEN.shape, TOKEN.dtype)
        for i in range(relays):
            relay_ref = found_refs[1 + cores + i]
            lane = pl.multiple_of(width + pl.program_id(0) * block, block)
            relay_ref[:, pl.ds(lane, block)] = hidden_refs[1 + i][...]

            @pl.when(pl.program_id(0) == 0)
            def _(i=i, relay_ref=relay_ref):
                relay_ref[:, :width] = refs[2 * cores + i][...]

        @pl.when(pl.program_id(0) == 0)
        def _():
            total_ref[...] = upstream_ref[...]

        for at, size in row_chunks(rows, 512):
            some = pl.ds(at, size)
            total_ref[some, :] += sum(
                jnp.dot(
                    hidden_refs[c][some, :], in_refs[c][...], preferred_element_type=jnp.float32
                )
                for c in range(cores)
            )

        @pl.when(pl.program_id(0) == steps - 1)
        def _():
            totals = [jnp.zeros((1, width), jnp.float32)] * 3
            for at, size in row_chunks(rows, 128):
                some = pl.ds(at, size)
                grad, value = total_ref[some, :], wide(normed_ref[some, :])
                conv_grad = low(norm_back(grad * gain_ref[...], value, wide(slope_ref[some, :])))
                mid_ref[some, :] = grad
                conv_grad_ref[some, :] = conv_grad
                for i, each in enumerate((grad * value, grad, wide(conv_grad))):
                    totals[i] = totals[i] + jnp.sum(each, 0, keepdims=True)
            sums_ref[...] = jnp.zeros(sums_ref.shape, jnp.float32)
            for i in range(3):
                sums_ref[i : i + 1, :] = totals[i]
            for c in range(1, cores):
                first = lax.rem(core_ref[0] - c + cores, cores) * lanes
                cut_refs[c - 1][...] = conv_grad_ref[:, pl.ds(pl.multiple_of(first, lanes), lanes)]

    whole = pl.BlockSpec((rows, width), lambda g, core: (0, 0))
    found = pl.pallas_call(
        kernel,
        grid_spec=pltpu.PrefetchScalarGridSpec(
            num_scalar_prefetch=1,
            grid=(steps,),
            in_specs=[whole, whole, whole, pl.BlockSpec((1, width), lambda g, core: (0, 0))]
            + [pl.BlockSpec((rows, block), lambda g, core: (0, g))]
            + [pl.BlockSpec((rows, block), lambda g, core: (0, width // block + g))] * (cores - 1)
            + [pl.BlockSpec((block, width), lambda g, core: (g, 0))] * cores
            + [whole] * relays
            + tokens(after)
            + [ANYWHERE] * len(reads),
            out_specs=[whole, whole]
            + [pl.BlockSpec((rows, lanes), lambda g, core: (0, 0))] * (cores - 1)
            + [pl.BlockSpec((rows, width + units), lambda g, core: (0, 0))] * relays
            + [pl.BlockSpec((8, width), lambda g, core: (0, 0)), TOKEN_SPEC],
            scratch_shapes=[pltpu.VMEM((rows, width), jnp.float32)],
        ),
        out_shape=[
            jax.ShapeDtypeStruct((rows, width), jnp.float32),
            jax.ShapeDtypeStruct((rows, width), jnp.bfloat16),
        ]
        + [jax.ShapeDtypeStruct((rows, lanes), jnp.bfloat16)] * (cores - 1)
        + [jax.ShapeDtypeStruct((rows, width + units), jnp.bfloat16)] * relays
        + [jax.ShapeDtypeStruct((8, width), jnp.float32), TOKEN],
        compiler_params=pltpu.CompilerParams(vmem_limit_bytes=VMEM_BYTES),
        cost_estimate=SMALL_COST,
        name="ffn_back_stream",
    )(
        core_index.astype(jnp.int32)[None],
        upstream,
        normed,
        slope,
        gain[None],
        hidden,
        *packets,
        *ins,
        *packets[:relays],
        *after,
        *reads,
    )
    return (
        found[0],
        found[1],
        found[2 : 1 + cores],
        found[1 + cores : 1 + cores + relays],
        found[-2],
        (found[-1],),
    )


def conv_data_grad(extended, weight, upstream, step, kind, after=()):
    taps, inner, width = weight.shape
    rows = upstream.shape[0]
    group = tap_groups(taps)
    steps = taps // group

    def kernel(extended_ref, weight_ref, upstream_ref, *refs):
        out_ref, token_ref, total_ref = refs[-3:]
        token_ref[...] = jnp.zeros(TOKEN.shape, TOKEN.dtype)
        first = pl.program_id(0) * group
        total = None
        for j in range(group):
            start = pl.multiple_of((taps - 1 - first - j) * step, ROW_TILE)
            term = lax.dot_general(
                extended_ref[pl.ds(start, rows), :],
                weight_ref[j],
                (((1,), (1,)), ((), ())),
                preferred_element_type=jnp.float32,
            )
            total = term if total is None else total + term

        @pl.when(pl.program_id(0) == 0)
        def _():
            total_ref[...] = total

        @pl.when(pl.program_id(0) > 0)
        def _():
            total_ref[...] += total

        @pl.when(pl.program_id(0) == steps - 1)
        def _():
            out_ref[...] = (upstream_ref[...] + wide(low(total_ref[...]))).astype(kind)

    whole = pl.BlockSpec((rows, inner), lambda g: (0, 0))
    found = pl.pallas_call(
        kernel,
        grid=(steps,),
        in_specs=[
            pl.BlockSpec(extended.shape, lambda g: (0, 0)),
            pl.BlockSpec((group, inner, width), lambda g: (g, 0, 0)),
            whole,
        ]
        + tokens(after),
        out_specs=(whole, TOKEN_SPEC),
        out_shape=(jax.ShapeDtypeStruct((rows, inner), kind), TOKEN),
        scratch_shapes=[pltpu.VMEM((rows, inner), jnp.float32)],
        compiler_params=pltpu.CompilerParams(vmem_limit_bytes=VMEM_BYTES),
        cost_estimate=SMALL_COST,
        name="conv_data_grad",
    )(extended, weight, upstream, *after)
    return found[0], (found[1],)


def hold(arrays, after):
    count = len(arrays)
    if count == 0:
        return [], after

    def kernel(*refs):
        refs[-1][...] = jnp.zeros(TOKEN.shape, TOKEN.dtype)

    found = pl.pallas_call(
        kernel,
        in_specs=[ANYWHERE] * count + [WHOLE] * len(after),
        out_specs=[ANYWHERE] * count + [WHOLE],
        out_shape=[jax.ShapeDtypeStruct(each.shape, each.dtype) for each in arrays] + [TOKEN],
        input_output_aliases={i: i for i in range(count)},
        cost_estimate=SMALL_COST,
        name="hold",
    )(*arrays, *after)
    return list(found[:-1]), (found[-1],)


def join_rows(parts, after=(), reads=()):
    def kernel(*refs):
        out_ref, token_ref = refs[-2:]
        token_ref[...] = jnp.zeros(TOKEN.shape, TOKEN.dtype)
        first = 0
        for i, part in enumerate(parts):
            out_ref[first : first + part.shape[0]] = refs[i][...]
            first += part.shape[0]

    shape = (sum(part.shape[0] for part in parts), parts[0].shape[1])
    found = pl.pallas_call(
        kernel,
        in_specs=[WHOLE] * len(parts) + [ANYWHERE] * len(reads) + [WHOLE] * len(after),
        out_specs=[WHOLE] * 2,
        out_shape=[jax.ShapeDtypeStruct(shape, parts[0].dtype), TOKEN],
        compiler_params=pltpu.CompilerParams(vmem_limit_bytes=VMEM_BYTES),
        cost_estimate=SMALL_COST,
        name="join_rows",
    )(*parts, *reads, *after)
    return found[0], (found[1],)


def restack(groups, reads=(), after=(), turn=None):
    flat = [array for arrays, _ in groups for array in arrays]
    cuts = [cut for _, each in groups for cut in each]

    def kernel(place_ref, *refs):
        token_ref = refs[-1]
        token_ref[...] = jnp.zeros(TOKEN.shape, TOKEN.dtype)
        out_refs = refs[-1 - len(cuts) : -1]
        at_in, at_out = 0, 0
        for arrays, each in groups:
            slots = len(arrays) if turn is None else arrays[0].shape[0]
            for first, last, shape in each:
                for slot in range(slots):
                    if turn is None:
                        value = refs[at_in + slot][...]
                    else:
                        value = refs[at_in][lax.rem(place_ref[0] - slot + slots, slots)]
                    if last is not None:
                        value = value[first:last]
                    out_refs[at_out][slot] = value.reshape(shape)
                at_out += 1
            at_in += len(arrays)

    shapes = [
        jax.ShapeDtypeStruct(
            ((len(arrays) if turn is None else arrays[0].shape[0]),) + shape, arrays[0].dtype
        )
        for arrays, each in groups
        for _, _, shape in each
    ]
    found = pl.pallas_call(
        kernel,
        in_specs=[SCALARS]
        + [WHOLE] * len(flat)
        + [ANYWHERE] * len(reads)
        + [WHOLE] * len(after),
        out_specs=[WHOLE] * (len(shapes) + 1),
        out_shape=shapes + [TOKEN],
        compiler_params=pltpu.CompilerParams(vmem_limit_bytes=VMEM_BYTES),
        cost_estimate=SMALL_COST,
        name="restack",
    )(jnp.zeros((1,), jnp.int32) + (0 if turn is None else turn), *flat, *reads, *after)
    return found[:-1], (found[-1],)


def conv_weight_grad(
    extendeds, upstream, arrived, places, sizes, taps, step, after=(), reads=()
):
    cores, seqs, acrosses, tap_peers = sizes
    rows = upstream.shape[0]
    inner = extendeds[0].shape[1]
    lanes = upstream.shape[1] // cores
    slab = inner // (seqs * acrosses * tap_peers)
    direct = slab % ROW_TILE == 0
    outs = seqs if direct else 1

    def kernel(place_ref, *refs):
        out_refs, token_ref = refs[-1 - outs : -1], refs[-1]
        token_ref[...] = jnp.zeros(TOKEN.shape, TOKEN.dtype)
        start = pl.multiple_of(pl.program_id(0) * step, ROW_TILE)
        found = low(
            sum(
                lax.dot_general(
                    refs[c][pl.ds(start, rows), :],
                    refs[cores + c][...],
                    (((0,), (0,)), ((), ())),
                    preferred_element_type=jnp.float32,
                )
                for c in range(cores)
            )
        )
        if not direct:
            out_refs[0][0] = found
            return
        for s in range(seqs):
            slot_s = lax.rem(place_ref[1] - s + seqs, seqs)
            for slot in range(seqs):

                @pl.when(slot_s == slot)
                def _(s=s, slot=slot):
                    for t in range(tap_peers):
                        slot_t = lax.rem(place_ref[3] - t + tap_peers, tap_peers)
                        for a in range(acrosses):
                            slot_a = lax.rem(place_ref[2] - a + acrosses, acrosses)
                            base = ((t * seqs + s) * acrosses + a) * slab
                            out_refs[slot][slot_a, slot_t, 0] = found[base : base + slab]

    if direct:
        out_shape = (acrosses, tap_peers, taps, slab, lanes)
        out_spec = pl.BlockSpec(
            (acrosses, tap_peers, 1, slab, lanes), lambda k, place: (0, 0, k, 0, 0)
        )
    else:
        out_shape = (taps, inner, lanes)
        out_spec = pl.BlockSpec((1, inner, lanes), lambda k, place: (k, 0, 0))
    found = pl.pallas_call(
        kernel,
        grid_spec=pltpu.PrefetchScalarGridSpec(
            num_scalar_prefetch=1,
            grid=(taps,),
            in_specs=[pl.BlockSpec(extendeds[0].shape, lambda k, place: (0, 0))] * cores
            + [pl.BlockSpec((rows, lanes), lambda k, place: (0, place[0]))]
            + [pl.BlockSpec((rows, lanes), lambda k, place: (0, 0))] * (cores - 1)
            + tokens(after)
            + [ANYWHERE] * len(reads),
            out_specs=[out_spec] * outs + [TOKEN_SPEC],
        ),
        out_shape=[jax.ShapeDtypeStruct(out_shape, jnp.bfloat16)] * outs + [TOKEN],
        compiler_params=pltpu.CompilerParams(vmem_limit_bytes=VMEM_BYTES),
        cost_estimate=SMALL_COST,
        name="conv_weight_grad",
    )(jnp.stack(places).astype(jnp.int32), *extendeds, upstream, *arrived, *after, *reads)
    token = found[-1]
    if direct:
        return found[:-1], token
    found = found[0].reshape(taps, tap_peers, seqs, acrosses, slab, lanes)
    for axis, which in ((1, 3), (2, 1), (3, 2)):
        found = relative(found, axis, places[which], sizes[which])
    found = found.transpose(2, 3, 1, 0, 4, 5)
    return [found[s] for s in range(seqs)], token


def ffn_weight_grad(pairs, sizes, ffn_rows, after=()):
    cores, seqs, acrosses, tap_peers = sizes
    rows, width = pairs[0][1].shape
    block = tap_peers * ffn_rows
    transposed = (((0,), (0,)), ((), ()))
    if ffn_rows % ROW_TILE:
        found = jnp.stack(
            [
                low(
                    sum(
                        lax.dot_general(a, b, transposed, preferred_element_type=jnp.float32)
                        for a, b in [(left, right)]
                        + [(ends[:, width:], starts[:, :width]) for ends, starts in packets]
                    )
                ).reshape(acrosses, seqs, tap_peers, ffn_rows, width)
                for left, right, packets in pairs
            ],
            3,
        )
        return [found[a] for a in range(acrosses)], jnp.zeros(TOKEN.shape, TOKEN.dtype)

    def kernel(*refs):
        out_refs, token_ref = refs[-1 - acrosses : -1], refs[-1]
        token_ref[...] = jnp.zeros(TOKEN.shape, TOKEN.dtype)
        for which in range(2):
            base = 2 * cores * which
            found = low(
                sum(
                    lax.dot_general(
                        refs[base + 2 * c][...],
                        refs[base + 2 * c + 1][...],
                        transposed,
                        preferred_element_type=jnp.float32,
                    )
                    for c in range(cores)
                )
            ).reshape(tap_peers, ffn_rows, width)
            for a in range(acrosses):

                @pl.when(pl.program_id(0) // seqs == a)
                def _(a=a):
                    out_refs[a][0, :, which] = found

    right_spec = pl.BlockSpec((rows, width), lambda g: (0, 0))
    left_spec = pl.BlockSpec((rows, block), lambda g: (0, g))
    late_spec = pl.BlockSpec((rows, block), lambda g: (0, width // block + g))

    def out_spec(a):
        return pl.BlockSpec(
            (1, tap_peers, 2, ffn_rows, width),
            lambda g: (jnp.clip(g - a * seqs, 0, seqs - 1), 0, 0, 0, 0),
        )

    shape = jax.ShapeDtypeStruct((seqs, tap_peers, 2, ffn_rows, width), jnp.bfloat16)
    operands = []
    for left, right, packets in pairs:
        operands += [left, right]
        for ends, starts in packets:
            operands += [ends, starts]
    found = pl.pallas_call(
        kernel,
        grid=(acrosses * seqs,),
        in_specs=([left_spec, right_spec] + [late_spec, right_spec] * (cores - 1)) * 2
        + tokens(after),
        out_specs=[out_spec(a) for a in range(acrosses)] + [TOKEN_SPEC],
        out_shape=[shape] * acrosses + [TOKEN],
        compiler_params=pltpu.CompilerParams(vmem_limit_bytes=VMEM_BYTES),
        cost_estimate=SMALL_COST,
        name="ffn_weight_grad",
    )(*operands, *after)
    return found[:-1], found[-1]


def merge_slots(conv_parts, ffn_parts, slots, after=()):
    lanes, width = conv_parts[0].shape[-1], ffn_parts[0].shape[-1]
    cuts = width // lanes
    conv_rows = conv_parts[0].size // (slots * lanes)
    ffn_rows = ffn_parts[0].size // (slots * width)
    conv_parts = [part.reshape(slots, conv_rows, lanes) for part in conv_parts]
    ffn_parts = [part.reshape(slots, ffn_rows, width) for part in ffn_parts]
    if conv_rows % ROW_TILE or ffn_rows % ROW_TILE:
        conv_sum = low(sum(wide(part) for part in conv_parts))
        ffn_sum = low(sum(wide(part) for part in ffn_parts))
        merged = jnp.concatenate(
            [conv_sum] + [ffn_sum[:, :, i * lanes : (i + 1) * lanes] for i in range(cuts)], 1
        )
        return [merged[slot] for slot in range(slots)], after

    def kernel(*refs):
        out_refs, token_ref = refs[-1 - slots : -1], refs[-1]
        token_ref[...] = jnp.zeros(TOKEN.shape, TOKEN.dtype)
        count = len(conv_parts)
        for slot in range(slots):
            out_refs[slot][:conv_rows] = low(sum(wide(refs[i][slot]) for i in range(count)))
            total = low(sum(wide(refs[count + i][slot]) for i in range(len(ffn_parts))))
            for i in range(cuts):
                first = conv_rows + i * ffn_rows
                out_refs[slot][first : first + ffn_rows] = total[:, i * lanes : (i + 1) * lanes]

    found = pl.pallas_call(
        kernel,
        in_specs=[WHOLE] * (len(conv_parts) + len(ffn_parts) + len(after)),
        out_specs=[WHOLE] * (slots + 1),
        out_shape=[jax.ShapeDtypeStruct((conv_rows + cuts * ffn_rows, lanes), jnp.bfloat16)] * slots
        + [TOKEN],
        compiler_params=pltpu.CompilerParams(vmem_limit_bytes=VMEM_BYTES),
        cost_estimate=SMALL_COST,
        name="merge_slots",
    )(*conv_parts, *ffn_parts, *after)
    return found[:slots], (found[slots],)


def append_slots(parts, packed, slots, after=()):
    lanes = parts[0].shape[-1]
    rows = parts[0].size // (slots * lanes)
    parts = [part.reshape(slots, rows, lanes) for part in parts]
    if rows % ROW_TILE:
        total = low(sum(wide(part) for part in parts))
        return [jnp.concatenate([total[slot], packed]) for slot in range(slots)], after

    def kernel(packed_ref, *refs):
        out_refs, token_ref = refs[-1 - slots : -1], refs[-1]
        token_ref[...] = jnp.zeros(TOKEN.shape, TOKEN.dtype)
        for slot in range(slots):
            out_refs[slot][:rows] = low(sum(wide(refs[i][slot]) for i in range(len(parts))))
            out_refs[slot][rows:] = packed_ref[...]

    shape = jax.ShapeDtypeStruct((rows + packed.shape[0], lanes), jnp.bfloat16)
    found = pl.pallas_call(
        kernel,
        in_specs=[WHOLE] * (1 + len(parts) + len(after)),
        out_specs=[WHOLE] * (slots + 1),
        out_shape=[shape] * slots + [TOKEN],
        compiler_params=pltpu.CompilerParams(vmem_limit_bytes=VMEM_BYTES),
        cost_estimate=SMALL_COST,
        name="append_slots",
    )(packed, *parts, *after)
    return found[:slots], (found[slots],)


def paired(values):
    while len(values) > 1:
        half = len(values) // 2
        if len(values) % 2:
            return sum(values[1:], values[0])
        values = [values[i] + values[i + half] for i in range(half)]
    return values[0]


def small_total(stacks, places, sizes):
    cores, seqs, acrosses = sizes[:3]
    full = jnp.stack([wide(each).reshape((seqs, acrosses) + each.shape[1:]) for each in stacks])
    if max(cores, seqs, acrosses) > 2:
        for axis, (place, size) in enumerate(zip(places[:3], sizes[:3])):
            full = relative(full, axis, place, size)
        return jnp.sum(full, (0, 1, 2))
    return paired(
        [
            paired([paired([full[c, s, a] for a in range(acrosses)]) for s in range(seqs)])
            for c in range(cores)
        ]
    )


def finish_conv(parts, conv_rows, small_rows, after=()):
    blocks, count = len(parts), len(parts[0])
    lanes = parts[0][0].shape[-1]
    flat = [part for block in parts for part in block]
    if conv_rows % ROW_TILE:
        sums = [sum(wide(part[:conv_rows]) for part in block) for block in parts]
        sums.append(paired([wide(part[conv_rows:]) for part in parts[0]]))
        return jnp.concatenate([low(total) for total in sums]), after

    def kernel(*refs):
        shard_ref, token_ref = refs[-2:]
        token_ref[...] = jnp.zeros(TOKEN.shape, TOKEN.dtype)
        shard_ref[blocks * conv_rows :] = low(
            paired([wide(refs[i][conv_rows:]) for i in range(count)])
        )
        for b in range(blocks):
            total = sum(wide(refs[b * count + i][:conv_rows]) for i in range(count))
            shard_ref[b * conv_rows : (b + 1) * conv_rows] = low(total)

    found = pl.pallas_call(
        kernel,
        in_specs=[WHOLE] * (len(flat) + len(after)),
        out_specs=[WHOLE] * 2,
        out_shape=[
            jax.ShapeDtypeStruct((blocks * conv_rows + small_rows, lanes), jnp.bfloat16),
            TOKEN,
        ],
        compiler_params=pltpu.CompilerParams(vmem_limit_bytes=VMEM_BYTES),
        cost_estimate=SMALL_COST,
        name="finish_conv",
    )(*flat, *after)
    return found[0], (found[1],)


def finish_ffn(merged, plain, conv_rows, ffn_rows, after=()):
    lanes, width = merged[0].shape[-1], plain[0].shape[-1]

    def cut_back(total):
        size = 2 * ffn_rows
        return jnp.concatenate(
            [total[i * size : (i + 1) * size] for i in range(width // lanes)], 1
        )

    if conv_rows % ROW_TILE or ffn_rows % ROW_TILE:
        sums = [sum(wide(part) for part in plain)]
        sums.append(cut_back(sum(wide(part[conv_rows:]) for part in merged)))
        return jnp.stack([each[:ffn_rows].T for each in sums]), jnp.stack(
            [each[ffn_rows:] for each in sums]
        ), after

    def kernel(*refs):
        in_ref, out_ref, token_ref = refs[-3:]
        token_ref[...] = jnp.zeros(TOKEN.shape, TOKEN.dtype)
        late = sum(wide(refs[i][conv_rows:]) for i in range(len(merged)))
        sums = [sum(wide(refs[len(merged) + i][...]) for i in range(len(plain))), cut_back(late)]
        for b in range(2):
            in_ref[b] = sums[b][:ffn_rows].T
            out_ref[b] = sums[b][ffn_rows:]

    found = pl.pallas_call(
        kernel,
        in_specs=[WHOLE] * (len(merged) + len(plain) + len(after)),
        out_specs=[WHOLE] * 3,
        out_shape=(
            jax.ShapeDtypeStruct((2, width, ffn_rows), jnp.float32),
            jax.ShapeDtypeStruct((2, ffn_rows, width), jnp.float32),
            TOKEN,
        ),
        compiler_params=pltpu.CompilerParams(vmem_limit_bytes=VMEM_BYTES),
        cost_estimate=SMALL_COST,
        name="finish_ffn",
    )(*merged, *plain, *after)
    return found[0], found[1], (found[2],)


def add_slots(parts, slots, after=(), reads=()):
    lanes = parts[0].shape[-1]
    rows = parts[0].size // (slots * lanes)
    parts = [part.reshape(slots, rows, lanes) for part in parts]
    block = rows // 4 if rows % (4 * ROW_TILE) == 0 else rows

    def kernel(*refs):
        out_refs, token_ref = refs[-1 - slots : -1], refs[-1]
        token_ref[...] = jnp.zeros(TOKEN.shape, TOKEN.dtype)
        for slot in range(slots):
            out_refs[slot][...] = low(sum(wide(refs[i][slot]) for i in range(len(parts))))

    found = pl.pallas_call(
        kernel,
        grid=(rows // block,),
        in_specs=[pl.BlockSpec((slots, block, lanes), lambda g: (0, g, 0))] * len(parts)
        + tokens(after)
        + [ANYWHERE] * len(reads),
        out_specs=[pl.BlockSpec((block, lanes), lambda g: (g, 0))] * slots + [TOKEN_SPEC],
        out_shape=[jax.ShapeDtypeStruct((rows, lanes), jnp.bfloat16)] * slots + [TOKEN],
        compiler_params=pltpu.CompilerParams(vmem_limit_bytes=VMEM_BYTES),
        cost_estimate=SMALL_COST,
        name="add_slots",
    )(*parts, *after, *reads)
    return found[:slots], found[slots]


def place_conv_grads(stacks, places, sizes):
    cores, seqs, acrosses = sizes[:3]
    blocks, taps, slab, lanes = stacks[0].shape[1:]
    channels = slab * seqs * acrosses
    if slab % ROW_TILE:
        full = jnp.stack([each.reshape((seqs, acrosses) + each.shape[1:]) for each in stacks])
        for axis, (place, size) in enumerate(zip(places[:3], sizes[:3])):
            full = relative(full, axis, place, size)
        return wide(
            full.transpose(3, 4, 1, 2, 5, 0, 6).reshape(blocks, taps, channels, cores * lanes)
        )

    def kernel(place_ref, *refs):
        out_ref = refs[-1]
        for c in range(cores):
            lane = pl.multiple_of(lax.rem(place_ref[0] - c + cores, cores) * lanes, lanes)
            for s in range(seqs):
                at_s = lax.rem(place_ref[1] - s + seqs, seqs)
                for a in range(acrosses):
                    at_a = lax.rem(place_ref[2] - a + acrosses, acrosses)
                    row = pl.multiple_of((at_s * acrosses + at_a) * slab, slab)
                    for b in range(blocks):
                        piece = wide(refs[c][s * acrosses + a, b, 0])
                        out_ref[b, 0, pl.ds(row, slab), pl.ds(lane, lanes)] = piece

    return pl.pallas_call(
        kernel,
        grid_spec=pltpu.PrefetchScalarGridSpec(
            num_scalar_prefetch=1,
            grid=(taps,),
            in_specs=[
                pl.BlockSpec(
                    (seqs * acrosses, blocks, 1, slab, lanes), lambda k, place: (0, 0, k, 0, 0)
                )
            ]
            * cores,
            out_specs=pl.BlockSpec(
                (blocks, 1, channels, cores * lanes), lambda k, place: (0, k, 0, 0)
            ),
        ),
        out_shape=jax.ShapeDtypeStruct((blocks, taps, channels, cores * lanes), jnp.float32),
        compiler_params=pltpu.CompilerParams(vmem_limit_bytes=VMEM_BYTES),
        cost_estimate=SMALL_COST,
        name="place_conv_grads",
    )(jnp.stack(places[:3]).astype(jnp.int32), *stacks)


def copy_all(copies):
    for copy in copies:
        copy.start()
    for copy in copies:
        copy.wait()


def place_conv(pieces, places, sizes, after=(), reads=()):
    cores, seqs, acrosses, tap_peers = sizes
    taps, slab, lanes = pieces[0][0].shape[2:]
    inner = slab * seqs * acrosses * tap_peers
    if slab % ROW_TILE:
        full = jnp.stack([jnp.stack(row) for row in pieces])
        for axis, (place, size) in enumerate(zip(places, sizes)):
            full = relative(full, axis, place, size)
        return full.transpose(4, 3, 1, 2, 5, 0, 6).reshape(taps, inner, cores * lanes), after
    flat = [piece for row in pieces for piece in row]

    def kernel(place_ref, *refs):
        out_ref, token_ref, sem_ref = refs[-3:]
        token_ref[...] = jnp.zeros(TOKEN.shape, TOKEN.dtype)
        copies = []
        for c in range(cores):
            lane = lax.rem(place_ref[0] - c + cores, cores) * lanes
            for s in range(seqs):
                at_s = lax.rem(place_ref[1] - s + seqs, seqs)
                for a in range(acrosses):
                    at_a = lax.rem(place_ref[2] - a + acrosses, acrosses)
                    for t in range(tap_peers):
                        at_t = lax.rem(place_ref[3] - t + tap_peers, tap_peers)
                        row = ((at_t * seqs + at_s) * acrosses + at_a) * slab
                        copies.append(
                            pltpu.make_async_copy(
                                refs[c * seqs + s].at[a, t],
                                out_ref.at[
                                    :,
                                    pl.ds(pl.multiple_of(row, slab), slab),
                                    pl.ds(pl.multiple_of(lane, lanes), lanes),
                                ],
                                sem_ref.at[len(copies)],
                            )
                        )
        copy_all(copies)

    found = pl.pallas_call(
        kernel,
        in_specs=[SCALARS] + [ANYWHERE] * (len(flat) + len(reads)) + [WHOLE] * len(after),
        out_specs=[WHOLE] * 2,
        out_shape=[jax.ShapeDtypeStruct((taps, inner, cores * lanes), jnp.bfloat16), TOKEN],
        scratch_shapes=[pltpu.SemaphoreType.DMA((cores * seqs * acrosses * tap_peers,))],
        compiler_params=pltpu.CompilerParams(vmem_limit_bytes=VMEM_BYTES),
        cost_estimate=SMALL_COST,
        name="place_conv",
    )(jnp.stack(places).astype(jnp.int32), *flat, *reads, *after)
    return found[0], (found[1],)


def place_ffn(pieces, sizes, after=(), reads=()):
    cores, seqs, acrosses, tap_peers = sizes
    cuts, ffn_rows, lanes = pieces[0][0].shape[2:]
    cuts //= 2
    width = cuts * lanes
    units = seqs * acrosses * tap_peers * ffn_rows
    if ffn_rows % ROW_TILE:
        full = jnp.stack([jnp.stack(row) for row in pieces])
        full = full.reshape(cores, acrosses, seqs, tap_peers, 2, cuts, ffn_rows, lanes)
        full = full.transpose(4, 0, 1, 2, 3, 6, 5, 7).reshape(2, cores, units, width)
        return [full[0, c] for c in range(cores)], [full[1, c] for c in range(cores)], after
    flat = [piece for row in pieces for piece in row]

    def kernel(*refs):
        out_refs = refs[-2 - 2 * cores : -2]
        token_ref, sem_ref = refs[-2:]
        token_ref[...] = jnp.zeros(TOKEN.shape, TOKEN.dtype)
        copies = []
        for c in range(cores):
            for a in range(acrosses):
                for which in range(2):
                    for cut in range(cuts):
                        copies.append(
                            pltpu.make_async_copy(
                                refs[c * acrosses + a].at[:, :, which * cuts + cut],
                                out_refs[which * cores + c].at[
                                    a, :, :, :, pl.ds(cut * lanes, lanes)
                                ],
                                sem_ref.at[len(copies)],
                            )
                        )
        copy_all(copies)

    shape = jax.ShapeDtypeStruct((acrosses, seqs, tap_peers, ffn_rows, width), jnp.bfloat16)
    found = pl.pallas_call(
        kernel,
        in_specs=[ANYWHERE] * (len(flat) + len(reads)) + [WHOLE] * len(after),
        out_specs=[WHOLE] * (2 * cores + 1),
        out_shape=[shape] * (2 * cores) + [TOKEN],
        scratch_shapes=[pltpu.SemaphoreType.DMA((2 * cores * acrosses * cuts,))],
        compiler_params=pltpu.CompilerParams(vmem_limit_bytes=VMEM_BYTES),
        cost_estimate=SMALL_COST,
        name="place_ffn",
    )(*flat, *reads, *after)
    token = found[-1]
    found = [each.reshape(units, width) for each in found[:-1]]
    return found[:cores], found[cores:], (token,)


class Ring:
    def __init__(self, axis, size, index, pairs):
        self.axis, self.size, self.index, self.pairs = axis, size, index, pairs

    def shifted(self, value, by):
        return lax.ppermute(value, self.axis, self.pairs(lambda i: (i + by) % self.size))

    def swapped(self, value, bit):
        return lax.ppermute(value, self.axis, self.pairs(lambda i: i ^ bit))

    def gather(self, value):
        return [value] + [self.shifted(value, by) for by in range(1, self.size)]

    def swap(self, values):
        return [values[0]] + [self.shifted(values[by], -by) for by in range(1, self.size)]


def relative(value, axis, place, size):
    if size == 1:
        return value
    return jnp.stack(
        [
            lax.dynamic_index_in_dim(value, (place - slot) % size, axis, False)
            for slot in range(size)
        ],
        axis,
    )


def rings():
    peers = lax.axis_size("dp")
    cores = CORES if peers % CORES == 0 else 1
    columns = peers // cores
    place = lax.axis_index("dp")

    def plain(axis):
        size = lax.axis_size(axis)
        return Ring(
            axis, size, lax.axis_index(axis), lambda move: [(i, move(i)) for i in range(size)]
        )

    across = Ring(
        "dp",
        columns,
        place // cores,
        lambda move: [(i, move(i // cores) * cores + i % cores) for i in range(peers)],
    )
    core = Ring(
        "dp",
        cores,
        place % cores,
        lambda move: [(i, i // cores * cores + move(i % cores)) for i in range(peers)],
    )
    return core, across, plain("seq"), plain("tap")


class Reduce:
    def __init__(self, terms, order):
        self.order = order
        self.parts = [terms[0]] + [order[0].shifted(terms[s], -s) for s in range(1, order[0].size)]

    def step(self, level, after, reads=()):
        ring = self.order[level]
        found, token = add_slots(self.parts, ring.size, after, reads)
        self.parts = [found[0]] + [ring.shifted(found[s], -s) for s in range(1, ring.size)]
        return (token,)


def shared_copies(value, across, seq):
    peers, spans = lax.axis_size("dp"), lax.axis_size("seq")
    cores = peers // across.size

    def target(place, by_a, by_s):
        dp, at = place // spans, place % spans
        moved = (dp // cores + by_a) % across.size * cores + dp % cores
        return moved * spans + (at + by_s) % spans

    return [
        [
            value
            if by_a == by_s == 0
            else lax.ppermute(
                value,
                ("dp", "seq"),
                [(place, target(place, by_a, by_s)) for place in range(peers * spans)],
            )
            for by_a in range(across.size)
        ]
        for by_s in range(seq.size)
    ]


def passed_along(value, axis, by):
    peers = lax.axis_size(axis)
    pairs = [(i, i + by) for i in range(peers) if 0 <= i + by < peers]
    return lax.ppermute(value, axis, pairs)


def rims(source, reach_rows, seq):
    span_rows = source.shape[0]
    if seq.size == 2 and reach_rows <= span_rows:
        first = (1 - seq.index) * (span_rows - reach_rows)
        return seq.shifted(lax.dynamic_slice_in_dim(source, first, reach_rows, 0), 1)
    left_parts = []
    right_parts = []
    distances = -(-reach_rows // span_rows)
    for distance in range(1, distances + 1):
        rim_count = min(span_rows, reach_rows - (distance - 1) * span_rows)
        left_parts.insert(0, passed_along(source[span_rows - rim_count :], "seq", distance))
        right_parts.append(passed_along(source[:rim_count], "seq", -distance))
    return left_parts, right_parts


def extend(source, found, seq, after=()):
    if isinstance(found, tuple):
        return join_rows(found[0] + [source] + found[1], after)
    reach, span = found.shape[0], source.shape[0]

    def kernel(place_ref, found_ref, source_ref, *refs):
        out_ref, token_ref = refs[-2:]
        token_ref[...] = jnp.zeros(TOKEN.shape, TOKEN.dtype)
        out_ref[reach : reach + span] = source_ref[...]
        zeros = jnp.zeros(found.shape, found.dtype)

        @pl.when(place_ref[0] == 0)
        def _():
            out_ref[:reach] = zeros
            out_ref[reach + span :] = found_ref[...]

        @pl.when(place_ref[0] != 0)
        def _():
            out_ref[:reach] = found_ref[...]
            out_ref[reach + span :] = zeros

    shape = jax.ShapeDtypeStruct((span + 2 * reach, source.shape[1]), source.dtype)
    extended, token = pl.pallas_call(
        kernel,
        in_specs=[SCALARS] + [WHOLE] * (2 + len(after)),
        out_specs=[WHOLE] * 2,
        out_shape=[shape, TOKEN],
        compiler_params=pltpu.CompilerParams(vmem_limit_bytes=VMEM_BYTES),
        cost_estimate=SMALL_COST,
        name="extend",
    )(seq.index.astype(jnp.int32)[None], found, source, *after)
    return extended, (token,)


def to_rows(values):
    windows, positions = values.shape[:2]
    cut = values.reshape((windows, positions // FIRST_DILATION, FIRST_DILATION) + values.shape[2:])
    return jnp.swapaxes(cut, 0, 1).reshape((windows * positions,) + values.shape[2:])


def from_rows(values, windows):
    cut = values.reshape((-1, windows, FIRST_DILATION) + values.shape[1:])
    return jnp.swapaxes(cut, 0, 1).reshape((windows, -1) + values.shape[1:])


def on_device(
    inputs,
    targets,
    masked,
    conv_weight,
    conv_bias,
    gains,
    shifts,
    in_weight,
    in_bias,
    out_weight,
    out_bias,
    head_weight,
):
    core, across, seq, tap = rings()
    taps = conv_weight.shape[1]
    channels = conv_weight.shape[2]
    width = conv_weight.shape[3]
    slab = channels // (seq.size * across.size)
    lanes = width // core.size
    hidden_width = in_bias.shape[1]
    ffn_rows = in_weight.shape[2]
    windows = inputs.shape[0]
    rows = windows * inputs.shape[1]
    steps = (FIRST_DILATION * windows, SECOND_DILATION * windows)
    units = hidden_width // core.size
    places = (core.index, seq.index, across.index, tap.index)
    sizes = (core.size, seq.size, across.size, tap.size)

    in_bias_placed = []
    for b in range(2):
        bias = in_bias[b].reshape(across.size, core.size, seq.size, tap.size, ffn_rows)
        for axis, ring in enumerate((across, core, seq, tap)):
            bias = relative(bias, axis, ring.index, ring.size)
        in_bias_placed.append(bias.transpose(1, 0, 2, 3, 4).reshape(core.size, units))

    def cut_ffn(piece):
        return piece.reshape(ffn_rows, core.size, lanes).swapaxes(0, 1).reshape(-1, lanes)

    def bundle(b):
        conv_piece = lax.dynamic_slice(
            conv_weight[b],
            (0, (seq.index * across.size + across.index) * slab, core.index * lanes),
            (taps, slab, lanes),
        )
        pieces = [
            conv_piece.reshape(taps * slab, lanes),
            cut_ffn(in_weight[b].T),
            cut_ffn(out_weight[b]),
        ]
        return jnp.concatenate(pieces)

    cuts = (
        (0, taps * slab, (taps, slab, lanes)),
        (taps * slab, taps * slab + 2 * core.size * ffn_rows, (2 * core.size, ffn_rows, lanes)),
    )

    def straight(arrays):
        return (arrays, ((0, None, arrays[0].shape),))

    conv_input = to_rows(inputs)
    stream = conv_input
    codes = to_rows(targets + masked * head_weight.shape[1])
    codes = jnp.broadcast_to(codes[:, None], (rows, 128))

    tap_parts = tap.gather(bundle(0))
    (conv_part, ffn_part), last = restack([(tap_parts, cuts)])
    split = (tap.size + 1) // 2
    (behind,), last = hold([bundle(1)], last)
    late_parts = tap.gather(behind)
    extended, last = extend(conv_input, rims(conv_input, taps // 2 * steps[0], seq), seq, last)
    extended_parts = [extended] + [core.shifted(extended, -c) for c in range(1, core.size)]
    conv_parts, ffn_parts = across.gather(conv_part), seq.gather(ffn_part)
    (conv_part, ffn_part), last = restack(
        [straight(conv_parts), straight(ffn_parts)],
        reads=[late_parts[by] for by in range(1, tap.size) if by != split],
        after=last,
    )
    conv_parts, ffn_parts = seq.gather(conv_part), across.gather(ffn_part)
    conv_slots = [core.gather(conv_part)]
    ffn_slots = [core.gather(ffn_part)]
    arrived = [conv_parts[1:], ffn_parts[1:], conv_slots[0][1:], ffn_slots[0][1:], late_parts[1:]]
    held, last = hold([each for some in arrived for each in some], last)
    for i, some in enumerate(arrived):
        arrived[i], held = held[: len(some)], held[len(some) :]
    conv_slots = [[conv_part] + arrived[2]] + [core.gather(each) for each in arrived[0]]
    ffn_slots = [[ffn_part] + arrived[3]] + [core.gather(each) for each in arrived[1]]
    (late_conv, late_ffn), last = restack([(late_parts[:1] + arrived[4], cuts)], after=last)
    late_conv_parts, late_ffn_parts = across.gather(late_conv), seq.gather(late_ffn)

    def turned(slots):
        return [[each[c] for each in slots] for c in range(core.size)]

    conv_full, in_full, out_full = [None, None], [None, None], [None, None]
    conv_full[0], last = place_conv(
        turned(conv_slots), places, sizes, last, [part for each in ffn_slots for part in each[1:]]
    )
    saved = []
    reads = []
    for b in range(2):
        if b == 1:
            found = rims(conv_input, taps // 2 * steps[1], seq)
            held, last = hold(late_conv_parts[1:] + late_ffn_parts[1:], last)
            late_conv_slots += [core.gather(each) for each in held[: seq.size - 1]]
            late_ffn_slots += [core.gather(each) for each in held[seq.size - 1 :]]
            conv_full[1], last = place_conv(turned(late_conv_slots), places, sizes, last)
            in_full[1], out_full[1], last = place_ffn(turned(late_ffn_slots), sizes, last)
            extended, last = extend(conv_input, found, seq, last)
            extended_parts = [extended] + [core.shifted(extended, -c) for c in range(1, core.size)]
        (normed_conv, conv_slope, stream, lowered), last = conv_forward(
            extended,
            conv_full[b],
            stream,
            conv_bias[b],
            gains[b, 0],
            shifts[b, 0],
            steps[b],
            last,
            reads,
        )
        reads = extended_parts[1:]
        if b == 0:
            (late_conv, late_ffn), last = restack(
                [straight(late_conv_parts), straight(late_ffn_parts)], after=last
            )
            late_conv_parts, late_ffn_parts = seq.gather(late_conv), across.gather(late_ffn)
            late_conv_slots = [core.gather(late_conv)]
            late_ffn_slots = [core.gather(late_ffn)]
            in_full[0], out_full[0], last = place_ffn(turned(ffn_slots), sizes, last)
            reads = reads + late_conv_slots[0][1:] + late_ffn_slots[0][1:]
        active, hidden_slopes, (normed_ffn, scale_ffn, stream, conv_input), packets, last = (
            ffn_forward(
                lowered,
                stream,
                in_full[b],
                out_full[b],
                [in_bias_placed[b][c] for c in range(core.size)],
                out_bias[b],
                gains[b, 1],
                shifts[b, 1],
                last,
                reads,
            )
        )
        packets = [core.shifted(packet, -1 - c) for c, packet in enumerate(packets)]
        reads = packets
        saved.append(
            (
                extended_parts,
                conv_slope,
                normed_conv,
                (active, lowered, packets),
                hidden_slopes,
                normed_ffn,
                scale_ffn,
            )
        )

    final_state = from_rows(conv_input, windows)
    (stream_grad, head_grad, loss_rows), last = head_and_loss(stream, head_weight, codes, last)

    ffn_rows_of_sums = [None, None]
    conv_rows_of_sums = [None, None]
    in_bias_grads = [None, None]
    ffn_sums = [None, None]
    conv_sums = [None, None]
    merged = [None, None]

    for b in (1, 0):
        (
            extended_parts,
            conv_slope,
            normed_conv,
            active_pair,
            hidden_slopes,
            normed_ffn,
            scale_ffn,
        ) = saved[b]
        output_grad, hidden_grad, biases, packets, ffn_rows_of_sums[b], last = ffn_back_hidden(
            stream_grad, normed_ffn, scale_ffn, gains[b, 1], out_full[b], hidden_slopes, last
        )
        if b == 1:
            arrived_packets = [core.shifted(packet, -1 - c) for c, packet in enumerate(packets)]
        if b == 0:
            last = ffn_sums[1].step(1, last, [final_state])
            last = conv_sums[1].step(1, last)
        stream_grad, conv_grad, conv_cuts, relayed, conv_rows_of_sums[b], last = ffn_back_stream(
            stream_grad,
            hidden_grad,
            packets,
            in_full[b],
            normed_conv,
            conv_slope,
            gains[b, 0],
            core.index,
            last,
            reads,
            relay=b == 0,
        )
        reads = []
        if b == 0:
            merged[1], last = merge_slots(conv_sums[1].parts, ffn_sums[1].parts, tap.size, last)
            held, last = hold([conv_grad] + list(conv_cuts) + list(relayed), last)
            conv_grad, conv_cuts, relayed = held[0], held[1 : core.size], held[core.size :]
            merged[1] = tap.swap(merged[1])
            arrived_packets = [core.shifted(packet, -1 - c) for c, packet in enumerate(relayed)]
        arrived = [core.shifted(conv_cuts[c - 1], -c) for c in range(1, core.size)]
        in_bias_grads[b] = list(biases)
        found_rims = rims(conv_grad, taps // 2 * steps[b], seq)

        def ffn_grads(last):
            active, lowered, packets = active_pair
            if core.size == 1:
                packets = []
            found, token = ffn_weight_grad(
                (
                    (hidden_grad, lowered, [(g, p) for g, p in zip(arrived_packets, packets)]),
                    (active, output_grad, [(p, g) for g, p in zip(arrived_packets, packets)]),
                ),
                sizes,
                ffn_rows,
                last,
            )
            return Reduce(found, (across, seq, tap)), (token,)

        def conv_grads(last, reads=()):
            found, token = conv_weight_grad(
                extended_parts, conv_grad, arrived, places, sizes, taps, steps[b], last, reads
            )
            found = [each.reshape(-1, lanes) for each in found]
            return Reduce(found, (seq, across, tap)), (token,)

        if b == 1:
            ffn_sums[1], last = ffn_grads(last)
            extended_grad, last = extend(conv_grad, found_rims, seq, last)
            conv_sums[1], last = conv_grads(last)
        else:
            extended_grad, last = extend(conv_grad, found_rims, seq, last)
            conv_sums[0], last = conv_grads(last)
            ffn_sums[0], last = ffn_grads(last)
        stream_grad, last = conv_data_grad(
            extended_grad,
            conv_full[b],
            stream_grad,
            steps[b],
            jnp.float32 if b == 1 else jnp.bfloat16,
            last,
        )

    grad_inputs = from_rows(stream_grad, windows)
    last = conv_sums[0].step(1, last, [grad_inputs])
    last = ffn_sums[0].step(1, last, merged[1][1:])

    def placed_bias(biases):
        bias = jnp.stack(biases).reshape(core.size, across.size, seq.size, tap.size, ffn_rows)
        for axis, ring in enumerate((core, across, seq, tap)):
            bias = relative(bias, axis, ring.index, ring.size)
        return bias.transpose(1, 0, 2, 3, 4).reshape(-1, width)

    held, last = hold(in_bias_grads[1] + in_bias_grads[0], last)
    terms = jnp.stack([loss_rows[0, 0], loss_rows[1, 0]])
    terms = jnp.stack([terms, terms - wide(low(terms))])
    small = [
        conv_rows_of_sums[0][:3],
        conv_rows_of_sums[1][:3],
        ffn_rows_of_sums[0][:3],
        ffn_rows_of_sums[1][:3],
        placed_bias(held[core.size :]),
        placed_bias(held[: core.size]),
        head_grad[: head_weight.shape[1]],
        jnp.pad(terms, ((0, 0), (0, width - 2))),
    ]
    small_counts = [each.shape[0] for each in small]
    packed = low(jnp.concatenate(small)).reshape(-1, lanes)
    packed = jnp.pad(packed, ((0, -packed.shape[0] % ROW_TILE), (0, 0)))

    conv_rows = taps * slab
    merged[0], last = append_slots(conv_sums[0].parts, packed, tap.size, last)
    merged[0] = tap.swap(merged[0])
    last = ffn_sums[0].step(2, last)
    shards, last = finish_conv([merged[0], merged[1]], conv_rows, packed.shape[0], last)
    copies = [each for row in shared_copies(shards, across, seq) for each in row]
    grad_in, grad_out, last = finish_ffn(merged[1], ffn_sums[0].parts, conv_rows, ffn_rows, last)
    (stack,), last = restack([straight(copies)], after=last)
    stacks = core.gather(stack)
    grad_conv = place_conv_grads(
        [
            each[:, : 2 * conv_rows].reshape(len(copies), 2, taps, slab, lanes) for each in stacks
        ],
        places,
        sizes,
    )
    packed = small_total([each[:, 2 * conv_rows :] for each in stacks], places, sizes)
    packed = packed.reshape(-1, width)
    unpacked = []
    first = 0
    for count in small_counts:
        unpacked.append(packed[first : first + count])
        first += count
    conv_0, conv_1, ffn_0, ffn_1, bias_0, bias_1, head_sum, loss_terms = unpacked
    grad_conv_bias = jnp.stack([conv_0[2], conv_1[2]])
    grad_gains = jnp.stack([jnp.stack([conv_0[0], ffn_0[0]]), jnp.stack([conv_1[0], ffn_1[0]])])
    grad_shifts = jnp.stack([jnp.stack([conv_0[1], ffn_0[1]]), jnp.stack([conv_1[1], ffn_1[1]])])
    grad_in_bias = jnp.stack([bias_0.reshape(-1), bias_1.reshape(-1)])
    grad_out_bias = jnp.stack([ffn_0[2], ffn_1[2]])
    loss_terms = loss_terms[0, :2] + loss_terms[1, :2]
    return (
        final_state,
        grad_inputs,
        grad_conv,
        grad_conv_bias,
        grad_gains,
        grad_shifts,
        grad_in,
        grad_in_bias,
        grad_out,
        grad_out_bias,
        head_sum.T,
        loss_terms[0] / loss_terms[1],
    )


def solution(mesh):
    placed = (
        P(("dp", "tap"), "seq", None),
        P(("dp", "tap"), "seq"),
        P(("dp", "tap"), "seq"),
        P(None, None, "tap", None),
        P(),
        P(),
        P(),
        P(None, None, ("dp", "seq", "tap")),
        P(),
        P(None, ("dp", "seq", "tap"), None),
        P(),
        P(),
    )
    return jax.shard_map(
        on_device,
        mesh=mesh,
        in_specs=placed,
        out_specs=(
            P(("dp", "tap"), "seq", None),
            P(("dp", "tap"), "seq", None),
            P(None, None, "tap", None),
            P(),
            P(),
            P(),
            P(None, None, ("dp", "seq", "tap")),
            P(),
            P(None, ("dp", "seq", "tap"), None),
            P(),
            P(),
            P(),
        ),
        check_vma=False,
    )
```

```python
import functools

import jax
import jax.numpy as jnp
from jax import lax
from jax.experimental import pallas as pl
from jax.experimental.pallas import tpu as pltpu
from jax.sharding import PartitionSpec as P

FIRST_DILATION = 4
SECOND_DILATION = 32
EPSILON = 1e-05
HIGHEST_PRECISION = lax.Precision.HIGHEST
CORES = 2
ROW_TILE = 16
VMEM_BYTES = 20 * 1024 * 1024
ANYWHERE = pl.BlockSpec(memory_space=pl.ANY)
SCALARS = pl.BlockSpec(memory_space=pltpu.SMEM)


TOKEN = jax.ShapeDtypeStruct((8, 128), jnp.float32)


def cost(microseconds):
    size = int(microseconds * 3.5e6)
    return pl.CostEstimate(flops=int(microseconds * 1.1e9), bytes_accessed=size, transcendentals=0)


WHOLE = pl.BlockSpec(memory_space=pltpu.VMEM)
TOKEN_SPEC = pl.BlockSpec(TOKEN.shape, lambda *_: (0, 0))


def tokens(after):
    return [TOKEN_SPEC] * len(after)


def low(values):
    return values.astype(jnp.bfloat16)


def wide(values):
    return values.astype(jnp.float32)


def gelu_parts(values):
    phi = 0.5 * (1.0 + lax.erf(values * 0.7071067811865476))
    return (
        values * phi,
        phi + values * jnp.exp(-0.5 * values * values) * 0.3989422804014327,
    )


def normalize(values):
    center = values - jnp.mean(values, -1, keepdims=True)
    scale = lax.rsqrt(jnp.mean(center * center, -1, keepdims=True) + EPSILON)
    return (center * scale, scale)


def norm_back(upstream, normed, scale):
    return scale * (
        upstream
        - jnp.mean(upstream, -1, keepdims=True)
        - normed * jnp.mean(upstream * normed, -1, keepdims=True)
    )


def tap_groups(taps):
    return 3 if taps % 3 == 0 else 1


def row_chunks(rows, most):
    size = min(rows, most)
    return [(first, size) for first in range(0, rows, size)]


def conv_forward(extended, weight, stream, bias, gain, shift, step, after=(), reads=()):
    taps, inner, width = weight.shape
    rows = stream.shape[0]
    group = tap_groups(taps)
    steps = taps // group

    def kernel(extended_ref, weight_ref, stream_ref, bias_ref, gain_ref, shift_ref, *refs):
        normed_ref, slope_ref, next_ref, lowered_ref, token_ref, total_ref = refs[-6:]
        token_ref[...] = jnp.zeros(TOKEN.shape, TOKEN.dtype)
        first = pl.program_id(0) * group
        total = None
        for j in range(group):
            start = pl.multiple_of((first + j) * step, ROW_TILE)
            term = jnp.dot(
                extended_ref[pl.ds(start, rows), :],
                weight_ref[j],
                preferred_element_type=jnp.float32,
            )
            total = term if total is None else total + term

        @pl.when(pl.program_id(0) == 0)
        def _():
            total_ref[...] = total

        @pl.when(pl.program_id(0) > 0)
        def _():
            total_ref[...] += total

        @pl.when(pl.program_id(0) == steps - 1)
        def _():
            for at, size in row_chunks(rows, 128):
                some = pl.ds(at, size)
                value, slope = gelu_parts(total_ref[some, :] + bias_ref[...])
                normed, scale = normalize(value)
                mid = wide(stream_ref[some, :]) + normed * gain_ref[...] + shift_ref[...]
                normed_ref[some, :] = low(normed)
                slope_ref[some, :] = low(scale * slope)
                next_ref[some, :] = mid
                lowered_ref[some, :] = low(mid)

    whole = pl.BlockSpec((rows, width), lambda g: (0, 0))
    row = pl.BlockSpec((1, width), lambda g: (0, 0))
    found = pl.pallas_call(
        kernel,
        grid=(steps,),
        in_specs=[
            pl.BlockSpec(extended.shape, lambda g: (0, 0)),
            pl.BlockSpec((group, inner, width), lambda g: (g, 0, 0)),
            whole,
            row,
            row,
            row,
        ]
        + tokens(after)
        + [ANYWHERE] * len(reads),
        out_specs=[whole] * 4 + [TOKEN_SPEC],
        out_shape=[
            jax.ShapeDtypeStruct((rows, width), jnp.bfloat16),
            jax.ShapeDtypeStruct((rows, width), jnp.bfloat16),
            jax.ShapeDtypeStruct((rows, width), jnp.float32),
            jax.ShapeDtypeStruct((rows, width), jnp.bfloat16),
            TOKEN,
        ],
        scratch_shapes=[pltpu.VMEM((rows, width), jnp.float32)],
        compiler_params=pltpu.CompilerParams(vmem_limit_bytes=VMEM_BYTES),
        cost_estimate=cost(9),
        name="conv_forward",
    )(extended, weight, stream, bias[None], gain[None], shift[None], *after, *reads)
    return found[:4], (found[4],)


def ffn_forward(
    lowered, stream, ins, outs, in_biases, out_bias, gain, shift, after=(), reads=()
):
    rows, width = lowered.shape
    cores = len(ins)
    units = ins[0].shape[0]
    block = min(units, 256)
    steps = units // block

    def kernel(lowered_ref, stream_ref, out_bias_ref, gain_ref, shift_ref, *refs):
        in_refs, out_refs, bias_refs = (refs[i * cores : (i + 1) * cores] for i in range(3))
        found_refs = refs[-6 - 2 * cores :]
        active_ref, slope_refs = found_refs[0], found_refs[1 : 1 + cores]
        normed_ref, scale_ref, next_ref, rounded_ref = found_refs[1 + cores : 5 + cores]
        packet_refs = found_refs[5 + cores : -2]
        token_ref, total_ref = found_refs[-2:]
        token_ref[...] = jnp.zeros(TOKEN.shape, TOKEN.dtype)
        lane = pl.multiple_of(width + pl.program_id(0) * block, block)

        @pl.when(pl.program_id(0) == 0)
        def _():
            total_ref[...] = jnp.zeros(total_ref.shape, jnp.float32)
            for packet_ref in packet_refs:
                packet_ref[:, :width] = lowered_ref[...]

        for at, size in row_chunks(rows, 512):
            some = pl.ds(at, size)
            term = None
            for c in range(cores):
                hidden = lax.dot_general(
                    lowered_ref[some, :],
                    in_refs[c][...],
                    (((1,), (1,)), ((), ())),
                    preferred_element_type=jnp.float32,
                )
                active, slope = gelu_parts(hidden + bias_refs[c][...])
                active = low(active)
                if c == 0:
                    active_ref[some, :] = active
                else:
                    packet_refs[c - 1][some, pl.ds(lane, block)] = active
                slope_refs[c][some, :] = low(slope)
                found = jnp.dot(active, out_refs[c][...], preferred_element_type=jnp.float32)
                term = found if term is None else term + found
            total_ref[some, :] += term

        @pl.when(pl.program_id(0) == steps - 1)
        def _():
            for at, size in row_chunks(rows, 128):
                some = pl.ds(at, size)
                normed, scale = normalize(total_ref[some, :] + out_bias_ref[...])
                after_ffn = stream_ref[some, :] + normed * gain_ref[...] + shift_ref[...]
                normed_ref[some, :] = low(normed)
                scale_ref[some, :] = jnp.broadcast_to(scale, (size, 128))
                next_ref[some, :] = after_ffn
                rounded_ref[some, :] = low(after_ffn)

    whole = pl.BlockSpec((rows, width), lambda g: (0, 0))
    row = pl.BlockSpec((1, width), lambda g: (0, 0))
    piece = pl.BlockSpec((block, width), lambda g: (g, 0))
    columns = pl.BlockSpec((rows, block), lambda g: (0, g))
    hidden_shape = jax.ShapeDtypeStruct((rows, units), jnp.bfloat16)
    found = pl.pallas_call(
        kernel,
        grid=(steps,),
        in_specs=[whole, whole, row, row, row]
        + [piece] * (2 * cores)
        + [pl.BlockSpec((1, block), lambda g: (0, g))] * cores
        + tokens(after)
        + [ANYWHERE] * len(reads),
        out_specs=[columns] * (1 + cores)
        + [whole, pl.BlockSpec((rows, 128), lambda g: (0, 0)), whole, whole]
        + [pl.BlockSpec((rows, width + units), lambda g: (0, 0))] * (cores - 1)
        + [TOKEN_SPEC],
        out_shape=[hidden_shape] * (1 + cores)
        + [
            jax.ShapeDtypeStruct((rows, width), jnp.bfloat16),
            jax.ShapeDtypeStruct((rows, 128), jnp.float32),
            jax.ShapeDtypeStruct((rows, width), jnp.float32),
            jax.ShapeDtypeStruct((rows, width), jnp.bfloat16),
        ]
        + [jax.ShapeDtypeStruct((rows, width + units), jnp.bfloat16)] * (cores - 1)
        + [TOKEN],
        scratch_shapes=[pltpu.VMEM((rows, width), jnp.float32)],
        compiler_params=pltpu.CompilerParams(vmem_limit_bytes=VMEM_BYTES),
        cost_estimate=cost(11),
        name="ffn_forward",
    )(
        lowered,
        stream,
        out_bias[None],
        gain[None],
        shift[None],
        *ins,
        *outs,
        *[each[None] for each in in_biases],
        *after,
        *reads,
    )
    return (
        found[0],
        found[1 : 1 + cores],
        found[1 + cores : 5 + cores],
        found[5 + cores : -1],
        (found[-1],),
    )


def head_and_loss(stream, head_weight, codes, after=()):
    rows, width = stream.shape
    classes = head_weight.shape[1]
    padded = jnp.pad(head_weight, ((0, 0), (0, 128 - classes)))
    cuts = row_chunks(rows, 256)

    def kernel(stream_ref, head_ref, code_ref, *refs):
        grad_ref, head_grad_ref, sums_ref, token_ref = refs[-4:]
        token_ref[...] = jnp.zeros(TOKEN.shape, TOKEN.dtype)
        head_grad = jnp.zeros((128, width), jnp.float32)
        objective = jnp.zeros((1, 1), jnp.float32)
        scored = jnp.zeros((1, 1), jnp.float32)
        for at, size in cuts:
            some = pl.ds(at, size)
            value = stream_ref[some, :]
            code = code_ref[some, :]
            mask = jnp.where(code[:, :1] >= classes, 1.0, 0.0)
            logits = jnp.dot(
                value, head_ref[...], precision=HIGHEST_PRECISION, preferred_element_type=jnp.float32
            )
            lane = lax.broadcasted_iota(jnp.int32, logits.shape, 1)
            valid = lane < classes
            peak = jnp.max(jnp.where(valid, logits, -jnp.inf), -1, keepdims=True)
            exponent = jnp.where(valid, jnp.exp(jnp.where(valid, logits - peak, 0.0)), 0.0)
            denominator = jnp.sum(exponent, -1, keepdims=True)
            chosen = lane == jnp.where(code >= classes, code - classes, code)
            picked = jnp.sum(jnp.where(chosen, logits, 0.0), -1, keepdims=True)
            terms = mask * (peak + jnp.log(denominator) - picked)
            objective = objective + jnp.sum(terms, 0, keepdims=True)
            scored = scored + jnp.sum(mask, 0, keepdims=True)
            logit_grad = mask * (exponent / denominator - jnp.where(chosen, 1.0, 0.0))
            grad_ref[some, :] = lax.dot_general(
                logit_grad,
                head_ref[...],
                (((1,), (1,)), ((), ())),
                precision=HIGHEST_PRECISION,
                preferred_element_type=jnp.float32,
            )
            head_grad = head_grad + lax.dot_general(
                logit_grad,
                value,
                (((0,), (0,)), ((), ())),
                precision=HIGHEST_PRECISION,
                preferred_element_type=jnp.float32,
            )
        head_grad_ref[...] = head_grad
        at_row = lax.broadcasted_iota(jnp.int32, sums_ref.shape, 0)
        sums_ref[...] = jnp.where(at_row == 0, objective, scored)

    found = pl.pallas_call(
        kernel,
        out_shape=[
            jax.ShapeDtypeStruct((rows, width), jnp.float32),
            jax.ShapeDtypeStruct((128, width), jnp.float32),
            jax.ShapeDtypeStruct((8, 128), jnp.float32),
            TOKEN,
        ],
        compiler_params=pltpu.CompilerParams(vmem_limit_bytes=VMEM_BYTES),
        cost_estimate=cost(6),
        name="head_and_loss",
    )(stream, padded, codes, *after)
    return found[:3], (found[3],)


def ffn_back_hidden(upstream, normed, scale, gain, outs, slopes, after=()):
    rows, width = upstream.shape
    cores = len(outs)
    units = outs[0].shape[0]
    block = min(units, 256)

    def kernel(upstream_ref, normed_ref, scale_ref, gain_ref, *refs):
        out_refs, slope_refs = refs[:cores], refs[cores : 2 * cores]
        found_refs = refs[-3 - 2 * cores :]
        output_grad_ref, hidden_ref = found_refs[:2]
        bias_refs, packet_refs = found_refs[2 : 2 + cores], found_refs[2 + cores : -2]
        sums_ref, token_ref = found_refs[-2:]
        token_ref[...] = jnp.zeros(TOKEN.shape, TOKEN.dtype)
        lane = pl.multiple_of(width + pl.program_id(0) * block, block)

        @pl.when(pl.program_id(0) == 0)
        def _():
            totals = [jnp.zeros((1, width), jnp.float32)] * 3
            for at, size in row_chunks(rows, 128):
                some = pl.ds(at, size)
                grad, value = upstream_ref[some, :], wide(normed_ref[some, :])
                output_grad = low(norm_back(grad * gain_ref[...], value, scale_ref[some, :1]))
                output_grad_ref[some, :] = output_grad
                for packet_ref in packet_refs:
                    packet_ref[some, :width] = output_grad
                for i, each in enumerate((grad * value, grad, wide(output_grad))):
                    totals[i] = totals[i] + jnp.sum(each, 0, keepdims=True)
            sums_ref[...] = jnp.zeros(sums_ref.shape, jnp.float32)
            for i in range(3):
                sums_ref[i : i + 1, :] = totals[i]

        for c in range(cores):
            total = jnp.zeros((1, block), jnp.float32)
            for at, size in row_chunks(rows, 512):
                some = pl.ds(at, size)
                active_grad = lax.dot_general(
                    output_grad_ref[some, :],
                    out_refs[c][...],
                    (((1,), (1,)), ((), ())),
                    preferred_element_type=jnp.float32,
                )
                hidden_grad = low(active_grad * wide(slope_refs[c][some, :]))
                if c == 0:
                    hidden_ref[some, :] = hidden_grad
                else:
                    packet_refs[c - 1][some, pl.ds(lane, block)] = hidden_grad
                total = total + jnp.sum(wide(hidden_grad), 0, keepdims=True)
            bias_refs[c][...] = total

    whole = pl.BlockSpec((rows, width), lambda g: (0, 0))
    columns = pl.BlockSpec((rows, block), lambda g: (0, g))
    found = pl.pallas_call(
        kernel,
        grid=(units // block,),
        in_specs=[
            whole,
            whole,
            pl.BlockSpec((rows, 128), lambda g: (0, 0)),
            pl.BlockSpec((1, width), lambda g: (0, 0)),
        ]
        + [pl.BlockSpec((block, width), lambda g: (g, 0))] * cores
        + [columns] * cores
        + tokens(after),
        out_specs=[whole, columns]
        + [pl.BlockSpec((1, block), lambda g: (0, g))] * cores
        + [pl.BlockSpec((rows, width + units), lambda g: (0, 0))] * (cores - 1)
        + [pl.BlockSpec((8, width), lambda g: (0, 0)), TOKEN_SPEC],
        out_shape=[
            jax.ShapeDtypeStruct((rows, width), jnp.bfloat16),
            jax.ShapeDtypeStruct((rows, units), jnp.bfloat16),
        ]
        + [jax.ShapeDtypeStruct((1, units), jnp.float32)] * cores
        + [jax.ShapeDtypeStruct((rows, width + units), jnp.bfloat16)] * (cores - 1)
        + [jax.ShapeDtypeStruct((8, width), jnp.float32), TOKEN],
        compiler_params=pltpu.CompilerParams(vmem_limit_bytes=VMEM_BYTES),
        cost_estimate=cost(6),
        name="ffn_back_hidden",
    )(upstream, normed, scale, gain[None], *outs, *slopes, *after)
    return (
        found[0],
        found[1],
        found[2 : 2 + cores],
        found[2 + cores : -2],
        found[-2],
        (found[-1],),
    )


def ffn_back_stream(
    upstream, hidden, packets, ins, normed, slope, gain, core_index, after=(), reads=(), relay=False
):
    rows, width = upstream.shape
    cores = len(ins)
    units = ins[0].shape[0]
    block = min(units, 256)
    steps = units // block
    lanes = width // cores
    relays = cores - 1 if relay else 0

    def kernel(core_ref, upstream_ref, normed_ref, slope_ref, gain_ref, *refs):
        hidden_refs, in_refs = refs[:cores], refs[cores : 2 * cores]
        found_refs = refs[-4 - cores - relays :]
        mid_ref, conv_grad_ref = found_refs[:2]
        cut_refs = found_refs[2 : 1 + cores]
        sums_ref, token_ref, total_ref = found_refs[-3:]
        token_ref[...] = jnp.zeros(TOKEN.shape, TOKEN.dtype)
        for i in range(relays):
            relay_ref = found_refs[1 + cores + i]
            lane = pl.multiple_of(width + pl.program_id(0) * block, block)
            relay_ref[:, pl.ds(lane, block)] = hidden_refs[1 + i][...]

            @pl.when(pl.program_id(0) == 0)
            def _(i=i, relay_ref=relay_ref):
                relay_ref[:, :width] = refs[2 * cores + i][...]

        @pl.when(pl.program_id(0) == 0)
        def _():
            total_ref[...] = upstream_ref[...]

        for at, size in row_chunks(rows, 512):
            some = pl.ds(at, size)
            total_ref[some, :] += sum(
                jnp.dot(
                    hidden_refs[c][some, :], in_refs[c][...], preferred_element_type=jnp.float32
                )
                for c in range(cores)
            )

        @pl.when(pl.program_id(0) == steps - 1)
        def _():
            totals = [jnp.zeros((1, width), jnp.float32)] * 3
            for at, size in row_chunks(rows, 128):
                some = pl.ds(at, size)
                grad, value = total_ref[some, :], wide(normed_ref[some, :])
                conv_grad = low(norm_back(grad * gain_ref[...], value, wide(slope_ref[some, :])))
                mid_ref[some, :] = grad
                conv_grad_ref[some, :] = conv_grad
                for i, each in enumerate((grad * value, grad, wide(conv_grad))):
                    totals[i] = totals[i] + jnp.sum(each, 0, keepdims=True)
            sums_ref[...] = jnp.zeros(sums_ref.shape, jnp.float32)
            for i in range(3):
                sums_ref[i : i + 1, :] = totals[i]
            for c in range(1, cores):
                first = lax.rem(core_ref[0] - c + cores, cores) * lanes
                cut_refs[c - 1][...] = conv_grad_ref[:, pl.ds(pl.multiple_of(first, lanes), lanes)]

    whole = pl.BlockSpec((rows, width), lambda g, core: (0, 0))
    found = pl.pallas_call(
        kernel,
        grid_spec=pltpu.PrefetchScalarGridSpec(
            num_scalar_prefetch=1,
            grid=(steps,),
            in_specs=[whole, whole, whole, pl.BlockSpec((1, width), lambda g, core: (0, 0))]
            + [pl.BlockSpec((rows, block), lambda g, core: (0, g))]
            + [pl.BlockSpec((rows, block), lambda g, core: (0, width // block + g))] * (cores - 1)
            + [pl.BlockSpec((block, width), lambda g, core: (g, 0))] * cores
            + [whole] * relays
            + tokens(after)
            + [ANYWHERE] * len(reads),
            out_specs=[whole, whole]
            + [pl.BlockSpec((rows, lanes), lambda g, core: (0, 0))] * (cores - 1)
            + [pl.BlockSpec((rows, width + units), lambda g, core: (0, 0))] * relays
            + [pl.BlockSpec((8, width), lambda g, core: (0, 0)), TOKEN_SPEC],
            scratch_shapes=[pltpu.VMEM((rows, width), jnp.float32)],
        ),
        out_shape=[
            jax.ShapeDtypeStruct((rows, width), jnp.float32),
            jax.ShapeDtypeStruct((rows, width), jnp.bfloat16),
        ]
        + [jax.ShapeDtypeStruct((rows, lanes), jnp.bfloat16)] * (cores - 1)
        + [jax.ShapeDtypeStruct((rows, width + units), jnp.bfloat16)] * relays
        + [jax.ShapeDtypeStruct((8, width), jnp.float32), TOKEN],
        compiler_params=pltpu.CompilerParams(vmem_limit_bytes=VMEM_BYTES),
        cost_estimate=cost(5),
        name="ffn_back_stream",
    )(
        core_index.astype(jnp.int32)[None],
        upstream,
        normed,
        slope,
        gain[None],
        hidden,
        *packets,
        *ins,
        *packets[:relays],
        *after,
        *reads,
    )
    return (
        found[0],
        found[1],
        found[2 : 1 + cores],
        found[1 + cores : 1 + cores + relays],
        found[-2],
        (found[-1],),
    )


def conv_data_grad(extended, weight, upstream, step, kind, after=()):
    taps, inner, width = weight.shape
    rows = upstream.shape[0]
    group = tap_groups(taps)
    steps = taps // group

    def kernel(extended_ref, weight_ref, upstream_ref, *refs):
        out_ref, token_ref, total_ref = refs[-3:]
        token_ref[...] = jnp.zeros(TOKEN.shape, TOKEN.dtype)
        first = pl.program_id(0) * group
        total = None
        for j in range(group):
            start = pl.multiple_of((taps - 1 - first - j) * step, ROW_TILE)
            term = lax.dot_general(
                extended_ref[pl.ds(start, rows), :],
                weight_ref[j],
                (((1,), (1,)), ((), ())),
                preferred_element_type=jnp.float32,
            )
            total = term if total is None else total + term

        @pl.when(pl.program_id(0) == 0)
        def _():
            total_ref[...] = total

        @pl.when(pl.program_id(0) > 0)
        def _():
            total_ref[...] += total

        @pl.when(pl.program_id(0) == steps - 1)
        def _():
            out_ref[...] = (upstream_ref[...] + wide(low(total_ref[...]))).astype(kind)

    whole = pl.BlockSpec((rows, inner), lambda g: (0, 0))
    found = pl.pallas_call(
        kernel,
        grid=(steps,),
        in_specs=[
            pl.BlockSpec(extended.shape, lambda g: (0, 0)),
            pl.BlockSpec((group, inner, width), lambda g: (g, 0, 0)),
            whole,
        ]
        + tokens(after),
        out_specs=(whole, TOKEN_SPEC),
        out_shape=(jax.ShapeDtypeStruct((rows, inner), kind), TOKEN),
        scratch_shapes=[pltpu.VMEM((rows, inner), jnp.float32)],
        compiler_params=pltpu.CompilerParams(vmem_limit_bytes=VMEM_BYTES),
        cost_estimate=cost(6),
        name="conv_data_grad",
    )(extended, weight, upstream, *after)
    return found[0], (found[1],)


def hold(arrays, after):
    count = len(arrays)
    if count == 0:
        return [], after

    def kernel(*refs):
        refs[-1][...] = jnp.zeros(TOKEN.shape, TOKEN.dtype)

    found = pl.pallas_call(
        kernel,
        in_specs=[ANYWHERE] * count + [WHOLE] * len(after),
        out_specs=[ANYWHERE] * count + [WHOLE],
        out_shape=[jax.ShapeDtypeStruct(each.shape, each.dtype) for each in arrays] + [TOKEN],
        input_output_aliases={i: i for i in range(count)},
        cost_estimate=cost(0.5),
        name="hold",
    )(*arrays, *after)
    return list(found[:-1]), (found[-1],)


def join_rows(parts, after=(), reads=()):
    def kernel(*refs):
        out_ref, token_ref = refs[-2:]
        token_ref[...] = jnp.zeros(TOKEN.shape, TOKEN.dtype)
        first = 0
        for i, part in enumerate(parts):
            out_ref[first : first + part.shape[0]] = refs[i][...]
            first += part.shape[0]

    shape = (sum(part.shape[0] for part in parts), parts[0].shape[1])
    found = pl.pallas_call(
        kernel,
        in_specs=[WHOLE] * len(parts) + [ANYWHERE] * len(reads) + [WHOLE] * len(after),
        out_specs=[WHOLE] * 2,
        out_shape=[jax.ShapeDtypeStruct(shape, parts[0].dtype), TOKEN],
        compiler_params=pltpu.CompilerParams(vmem_limit_bytes=VMEM_BYTES),
        cost_estimate=cost(1.5),
        name="join_rows",
    )(*parts, *reads, *after)
    return found[0], (found[1],)


def restack(groups, reads=(), after=(), turn=None):
    flat = [array for arrays, _ in groups for array in arrays]
    cuts = [cut for _, each in groups for cut in each]

    def kernel(place_ref, *refs):
        token_ref = refs[-1]
        token_ref[...] = jnp.zeros(TOKEN.shape, TOKEN.dtype)
        out_refs = refs[-1 - len(cuts) : -1]
        at_in, at_out = 0, 0
        for arrays, each in groups:
            slots = len(arrays) if turn is None else arrays[0].shape[0]
            for first, last, shape in each:
                for slot in range(slots):
                    if turn is None:
                        value = refs[at_in + slot][...]
                    else:
                        value = refs[at_in][lax.rem(place_ref[0] - slot + slots, slots)]
                    if last is not None:
                        value = value[first:last]
                    out_refs[at_out][slot] = value.reshape(shape)
                at_out += 1
            at_in += len(arrays)

    shapes = [
        jax.ShapeDtypeStruct(
            ((len(arrays) if turn is None else arrays[0].shape[0]),) + shape, arrays[0].dtype
        )
        for arrays, each in groups
        for _, _, shape in each
    ]
    found = pl.pallas_call(
        kernel,
        in_specs=[SCALARS]
        + [WHOLE] * len(flat)
        + [ANYWHERE] * len(reads)
        + [WHOLE] * len(after),
        out_specs=[WHOLE] * (len(shapes) + 1),
        out_shape=shapes + [TOKEN],
        compiler_params=pltpu.CompilerParams(vmem_limit_bytes=VMEM_BYTES),
        cost_estimate=cost(1.5),
        name="restack",
    )(jnp.zeros((1,), jnp.int32) + (0 if turn is None else turn), *flat, *reads, *after)
    return found[:-1], (found[-1],)


def conv_weight_grad(
    extendeds, upstream, arrived, places, sizes, taps, step, after=(), reads=()
):
    cores, seqs, acrosses, tap_peers = sizes
    rows = upstream.shape[0]
    inner = extendeds[0].shape[1]
    lanes = upstream.shape[1] // cores
    slab = inner // (seqs * acrosses * tap_peers)
    direct = slab % ROW_TILE == 0
    outs = seqs if direct else 1

    def kernel(place_ref, *refs):
        out_refs, token_ref = refs[-1 - outs : -1], refs[-1]
        token_ref[...] = jnp.zeros(TOKEN.shape, TOKEN.dtype)
        start = pl.multiple_of(pl.program_id(0) * step, ROW_TILE)
        found = low(
            sum(
                lax.dot_general(
                    refs[c][pl.ds(start, rows), :],
                    refs[cores + c][...],
                    (((0,), (0,)), ((), ())),
                    preferred_element_type=jnp.float32,
                )
                for c in range(cores)
            )
        )
        if not direct:
            out_refs[0][0] = found
            return
        for s in range(seqs):
            slot_s = lax.rem(place_ref[1] - s + seqs, seqs)
            for slot in range(seqs):

                @pl.when(slot_s == slot)
                def _(s=s, slot=slot):
                    for t in range(tap_peers):
                        slot_t = lax.rem(place_ref[3] - t + tap_peers, tap_peers)
                        for a in range(acrosses):
                            slot_a = lax.rem(place_ref[2] - a + acrosses, acrosses)
                            base = ((t * seqs + s) * acrosses + a) * slab
                            out_refs[slot][slot_a, slot_t, 0] = found[base : base + slab]

    if direct:
        out_shape = (acrosses, tap_peers, taps, slab, lanes)
        out_spec = pl.BlockSpec(
            (acrosses, tap_peers, 1, slab, lanes), lambda k, place: (0, 0, k, 0, 0)
        )
    else:
        out_shape = (taps, inner, lanes)
        out_spec = pl.BlockSpec((1, inner, lanes), lambda k, place: (k, 0, 0))
    found = pl.pallas_call(
        kernel,
        grid_spec=pltpu.PrefetchScalarGridSpec(
            num_scalar_prefetch=1,
            grid=(taps,),
            in_specs=[pl.BlockSpec(extendeds[0].shape, lambda k, place: (0, 0))] * cores
            + [pl.BlockSpec((rows, lanes), lambda k, place: (0, place[0]))]
            + [pl.BlockSpec((rows, lanes), lambda k, place: (0, 0))] * (cores - 1)
            + tokens(after)
            + [ANYWHERE] * len(reads),
            out_specs=[out_spec] * outs + [TOKEN_SPEC],
        ),
        out_shape=[jax.ShapeDtypeStruct(out_shape, jnp.bfloat16)] * outs + [TOKEN],
        compiler_params=pltpu.CompilerParams(vmem_limit_bytes=VMEM_BYTES),
        cost_estimate=cost(9),
        name="conv_weight_grad",
    )(jnp.stack(places).astype(jnp.int32), *extendeds, upstream, *arrived, *after, *reads)
    token = found[-1]
    if direct:
        return found[:-1], token
    found = found[0].reshape(taps, tap_peers, seqs, acrosses, slab, lanes)
    for axis, which in ((1, 3), (2, 1), (3, 2)):
        found = relative(found, axis, places[which], sizes[which])
    found = found.transpose(2, 3, 1, 0, 4, 5)
    return [found[s] for s in range(seqs)], token


def ffn_weight_grad(pairs, sizes, ffn_rows, after=()):
    cores, seqs, acrosses, tap_peers = sizes
    rows, width = pairs[0][1].shape
    block = tap_peers * ffn_rows
    transposed = (((0,), (0,)), ((), ()))
    if ffn_rows % ROW_TILE:
        found = jnp.stack(
            [
                low(
                    sum(
                        lax.dot_general(a, b, transposed, preferred_element_type=jnp.float32)
                        for a, b in [(left, right)]
                        + [(ends[:, width:], starts[:, :width]) for ends, starts in packets]
                    )
                ).reshape(acrosses, seqs, tap_peers, ffn_rows, width)
                for left, right, packets in pairs
            ],
            3,
        )
        return [found[a] for a in range(acrosses)], jnp.zeros(TOKEN.shape, TOKEN.dtype)

    def kernel(*refs):
        out_refs, token_ref = refs[-1 - acrosses : -1], refs[-1]
        token_ref[...] = jnp.zeros(TOKEN.shape, TOKEN.dtype)
        for which in range(2):
            base = 2 * cores * which
            found = low(
                sum(
                    lax.dot_general(
                        refs[base + 2 * c][...],
                        refs[base + 2 * c + 1][...],
                        transposed,
                        preferred_element_type=jnp.float32,
                    )
                    for c in range(cores)
                )
            ).reshape(tap_peers, ffn_rows, width)
            for a in range(acrosses):

                @pl.when(pl.program_id(0) // seqs == a)
                def _(a=a):
                    out_refs[a][0, :, which] = found

    right_spec = pl.BlockSpec((rows, width), lambda g: (0, 0))
    left_spec = pl.BlockSpec((rows, block), lambda g: (0, g))
    late_spec = pl.BlockSpec((rows, block), lambda g: (0, width // block + g))

    def out_spec(a):
        return pl.BlockSpec(
            (1, tap_peers, 2, ffn_rows, width),
            lambda g: (jnp.clip(g - a * seqs, 0, seqs - 1), 0, 0, 0, 0),
        )

    shape = jax.ShapeDtypeStruct((seqs, tap_peers, 2, ffn_rows, width), jnp.bfloat16)
    operands = []
    for left, right, packets in pairs:
        operands += [left, right]
        for ends, starts in packets:
            operands += [ends, starts]
    found = pl.pallas_call(
        kernel,
        grid=(acrosses * seqs,),
        in_specs=([left_spec, right_spec] + [late_spec, right_spec] * (cores - 1)) * 2
        + tokens(after),
        out_specs=[out_spec(a) for a in range(acrosses)] + [TOKEN_SPEC],
        out_shape=[shape] * acrosses + [TOKEN],
        compiler_params=pltpu.CompilerParams(vmem_limit_bytes=VMEM_BYTES),
        cost_estimate=cost(8),
        name="ffn_weight_grad",
    )(*operands, *after)
    return found[:-1], found[-1]


def merge_slots(conv_parts, ffn_parts, slots, after=()):
    lanes, width = conv_parts[0].shape[-1], ffn_parts[0].shape[-1]
    cuts = width // lanes
    conv_rows = conv_parts[0].size // (slots * lanes)
    ffn_rows = ffn_parts[0].size // (slots * width)
    conv_parts = [part.reshape(slots, conv_rows, lanes) for part in conv_parts]
    ffn_parts = [part.reshape(slots, ffn_rows, width) for part in ffn_parts]
    if conv_rows % ROW_TILE or ffn_rows % ROW_TILE:
        conv_sum = low(sum(wide(part) for part in conv_parts))
        ffn_sum = low(sum(wide(part) for part in ffn_parts))
        merged = jnp.concatenate(
            [conv_sum] + [ffn_sum[:, :, i * lanes : (i + 1) * lanes] for i in range(cuts)], 1
        )
        return [merged[slot] for slot in range(slots)], after

    def kernel(*refs):
        out_refs, token_ref = refs[-1 - slots : -1], refs[-1]
        token_ref[...] = jnp.zeros(TOKEN.shape, TOKEN.dtype)
        count = len(conv_parts)
        for slot in range(slots):
            out_refs[slot][:conv_rows] = low(sum(wide(refs[i][slot]) for i in range(count)))
            total = low(sum(wide(refs[count + i][slot]) for i in range(len(ffn_parts))))
            for i in range(cuts):
                first = conv_rows + i * ffn_rows
                out_refs[slot][first : first + ffn_rows] = total[:, i * lanes : (i + 1) * lanes]

    found = pl.pallas_call(
        kernel,
        in_specs=[WHOLE] * (len(conv_parts) + len(ffn_parts) + len(after)),
        out_specs=[WHOLE] * (slots + 1),
        out_shape=[jax.ShapeDtypeStruct((conv_rows + cuts * ffn_rows, lanes), jnp.bfloat16)] * slots
        + [TOKEN],
        compiler_params=pltpu.CompilerParams(vmem_limit_bytes=VMEM_BYTES),
        cost_estimate=cost(1.5),
        name="merge_slots",
    )(*conv_parts, *ffn_parts, *after)
    return found[:slots], (found[slots],)


def append_slots(parts, packed, slots, after=()):
    lanes = parts[0].shape[-1]
    rows = parts[0].size // (slots * lanes)
    parts = [part.reshape(slots, rows, lanes) for part in parts]
    if rows % ROW_TILE:
        total = low(sum(wide(part) for part in parts))
        return [jnp.concatenate([total[slot], packed]) for slot in range(slots)], after

    def kernel(packed_ref, *refs):
        out_refs, token_ref = refs[-1 - slots : -1], refs[-1]
        token_ref[...] = jnp.zeros(TOKEN.shape, TOKEN.dtype)
        for slot in range(slots):
            out_refs[slot][:rows] = low(sum(wide(refs[i][slot]) for i in range(len(parts))))
            out_refs[slot][rows:] = packed_ref[...]

    shape = jax.ShapeDtypeStruct((rows + packed.shape[0], lanes), jnp.bfloat16)
    found = pl.pallas_call(
        kernel,
        in_specs=[WHOLE] * (1 + len(parts) + len(after)),
        out_specs=[WHOLE] * (slots + 1),
        out_shape=[shape] * slots + [TOKEN],
        compiler_params=pltpu.CompilerParams(vmem_limit_bytes=VMEM_BYTES),
        cost_estimate=cost(1),
        name="append_slots",
    )(packed, *parts, *after)
    return found[:slots], (found[slots],)


def paired(values):
    while len(values) > 1:
        half = len(values) // 2
        if len(values) % 2:
            return sum(values[1:], values[0])
        values = [values[i] + values[i + half] for i in range(half)]
    return values[0]


def small_total(stacks, places, sizes):
    cores, seqs, acrosses = sizes[:3]
    full = jnp.stack([wide(each).reshape((seqs, acrosses) + each.shape[1:]) for each in stacks])
    if max(cores, seqs, acrosses) > 2:
        for axis, (place, size) in enumerate(zip(places[:3], sizes[:3])):
            full = relative(full, axis, place, size)
        return jnp.sum(full, (0, 1, 2))
    return paired(
        [
            paired([paired([full[c, s, a] for a in range(acrosses)]) for s in range(seqs)])
            for c in range(cores)
        ]
    )


def finish_conv(parts, conv_rows, small_rows, after=()):
    blocks, count = len(parts), len(parts[0])
    lanes = parts[0][0].shape[-1]
    flat = [part for block in parts for part in block]
    if conv_rows % ROW_TILE:
        sums = [sum(wide(part[:conv_rows]) for part in block) for block in parts]
        sums.append(paired([wide(part[conv_rows:]) for part in parts[0]]))
        return jnp.concatenate([low(total) for total in sums]), after

    def kernel(*refs):
        shard_ref, token_ref = refs[-2:]
        token_ref[...] = jnp.zeros(TOKEN.shape, TOKEN.dtype)
        shard_ref[blocks * conv_rows :] = low(
            paired([wide(refs[i][conv_rows:]) for i in range(count)])
        )
        for b in range(blocks):
            total = sum(wide(refs[b * count + i][:conv_rows]) for i in range(count))
            shard_ref[b * conv_rows : (b + 1) * conv_rows] = low(total)

    found = pl.pallas_call(
        kernel,
        in_specs=[WHOLE] * (len(flat) + len(after)),
        out_specs=[WHOLE] * 2,
        out_shape=[
            jax.ShapeDtypeStruct((blocks * conv_rows + small_rows, lanes), jnp.bfloat16),
            TOKEN,
        ],
        compiler_params=pltpu.CompilerParams(vmem_limit_bytes=VMEM_BYTES),
        cost_estimate=cost(1.2),
        name="finish_conv",
    )(*flat, *after)
    return found[0], (found[1],)


def finish_ffn(merged, plain, conv_rows, ffn_rows, after=()):
    lanes, width = merged[0].shape[-1], plain[0].shape[-1]

    def cut_back(total):
        size = 2 * ffn_rows
        return jnp.concatenate(
            [total[i * size : (i + 1) * size] for i in range(width // lanes)], 1
        )

    if conv_rows % ROW_TILE or ffn_rows % ROW_TILE:
        sums = [sum(wide(part) for part in plain)]
        sums.append(cut_back(sum(wide(part[conv_rows:]) for part in merged)))
        return jnp.stack([each[:ffn_rows].T for each in sums]), jnp.stack(
            [each[ffn_rows:] for each in sums]
        ), after

    def kernel(*refs):
        in_ref, out_ref, token_ref = refs[-3:]
        token_ref[...] = jnp.zeros(TOKEN.shape, TOKEN.dtype)
        late = sum(wide(refs[i][conv_rows:]) for i in range(len(merged)))
        sums = [sum(wide(refs[len(merged) + i][...]) for i in range(len(plain))), cut_back(late)]
        for b in range(2):
            in_ref[b] = sums[b][:ffn_rows].T
            out_ref[b] = sums[b][ffn_rows:]

    found = pl.pallas_call(
        kernel,
        in_specs=[WHOLE] * (len(merged) + len(plain) + len(after)),
        out_specs=[WHOLE] * 3,
        out_shape=(
            jax.ShapeDtypeStruct((2, width, ffn_rows), jnp.float32),
            jax.ShapeDtypeStruct((2, ffn_rows, width), jnp.float32),
            TOKEN,
        ),
        compiler_params=pltpu.CompilerParams(vmem_limit_bytes=VMEM_BYTES),
        cost_estimate=cost(1),
        name="finish_ffn",
    )(*merged, *plain, *after)
    return found[0], found[1], (found[2],)


def add_slots(parts, slots, after=(), reads=()):
    lanes = parts[0].shape[-1]
    rows = parts[0].size // (slots * lanes)
    parts = [part.reshape(slots, rows, lanes) for part in parts]
    block = rows // 4 if rows % (4 * ROW_TILE) == 0 else rows

    def kernel(*refs):
        out_refs, token_ref = refs[-1 - slots : -1], refs[-1]
        token_ref[...] = jnp.zeros(TOKEN.shape, TOKEN.dtype)
        for slot in range(slots):
            out_refs[slot][...] = low(sum(wide(refs[i][slot]) for i in range(len(parts))))

    found = pl.pallas_call(
        kernel,
        grid=(rows // block,),
        in_specs=[pl.BlockSpec((slots, block, lanes), lambda g: (0, g, 0))] * len(parts)
        + tokens(after)
        + [ANYWHERE] * len(reads),
        out_specs=[pl.BlockSpec((block, lanes), lambda g: (g, 0))] * slots + [TOKEN_SPEC],
        out_shape=[jax.ShapeDtypeStruct((rows, lanes), jnp.bfloat16)] * slots + [TOKEN],
        compiler_params=pltpu.CompilerParams(vmem_limit_bytes=VMEM_BYTES),
        cost_estimate=cost(2),
        name="add_slots",
    )(*parts, *after, *reads)
    return found[:slots], found[slots]


def place_conv_grads(stacks, places, sizes):
    cores, seqs, acrosses = sizes[:3]
    blocks, taps, slab, lanes = stacks[0].shape[1:]
    channels = slab * seqs * acrosses
    if slab % ROW_TILE:
        full = jnp.stack([each.reshape((seqs, acrosses) + each.shape[1:]) for each in stacks])
        for axis, (place, size) in enumerate(zip(places[:3], sizes[:3])):
            full = relative(full, axis, place, size)
        return wide(
            full.transpose(3, 4, 1, 2, 5, 0, 6).reshape(blocks, taps, channels, cores * lanes)
        )

    def kernel(place_ref, *refs):
        out_ref = refs[-1]
        for c in range(cores):
            lane = pl.multiple_of(lax.rem(place_ref[0] - c + cores, cores) * lanes, lanes)
            for s in range(seqs):
                at_s = lax.rem(place_ref[1] - s + seqs, seqs)
                for a in range(acrosses):
                    at_a = lax.rem(place_ref[2] - a + acrosses, acrosses)
                    row = pl.multiple_of((at_s * acrosses + at_a) * slab, slab)
                    for b in range(blocks):
                        piece = wide(refs[c][s * acrosses + a, b, 0])
                        out_ref[b, 0, pl.ds(row, slab), pl.ds(lane, lanes)] = piece

    return pl.pallas_call(
        kernel,
        grid_spec=pltpu.PrefetchScalarGridSpec(
            num_scalar_prefetch=1,
            grid=(taps,),
            in_specs=[
                pl.BlockSpec(
                    (seqs * acrosses, blocks, 1, slab, lanes), lambda k, place: (0, 0, k, 0, 0)
                )
            ]
            * cores,
            out_specs=pl.BlockSpec(
                (blocks, 1, channels, cores * lanes), lambda k, place: (0, k, 0, 0)
            ),
        ),
        out_shape=jax.ShapeDtypeStruct((blocks, taps, channels, cores * lanes), jnp.float32),
        compiler_params=pltpu.CompilerParams(vmem_limit_bytes=VMEM_BYTES),
        cost_estimate=cost(5),
        name="place_conv_grads",
    )(jnp.stack(places[:3]).astype(jnp.int32), *stacks)


def copy_all(copies):
    for copy in copies:
        copy.start()
    for copy in copies:
        copy.wait()


def place_conv(pieces, places, sizes, after=(), reads=()):
    cores, seqs, acrosses, tap_peers = sizes
    taps, slab, lanes = pieces[0][0].shape[2:]
    inner = slab * seqs * acrosses * tap_peers
    if slab % ROW_TILE:
        full = jnp.stack([jnp.stack(row) for row in pieces])
        for axis, (place, size) in enumerate(zip(places, sizes)):
            full = relative(full, axis, place, size)
        return full.transpose(4, 3, 1, 2, 5, 0, 6).reshape(taps, inner, cores * lanes), after
    flat = [piece for row in pieces for piece in row]

    def kernel(place_ref, *refs):
        out_ref, token_ref, sem_ref = refs[-3:]
        token_ref[...] = jnp.zeros(TOKEN.shape, TOKEN.dtype)
        copies = []
        for c in range(cores):
            lane = lax.rem(place_ref[0] - c + cores, cores) * lanes
            for s in range(seqs):
                at_s = lax.rem(place_ref[1] - s + seqs, seqs)
                for a in range(acrosses):
                    at_a = lax.rem(place_ref[2] - a + acrosses, acrosses)
                    for t in range(tap_peers):
                        at_t = lax.rem(place_ref[3] - t + tap_peers, tap_peers)
                        row = ((at_t * seqs + at_s) * acrosses + at_a) * slab
                        copies.append(
                            pltpu.make_async_copy(
                                refs[c * seqs + s].at[a, t],
                                out_ref.at[
                                    :,
                                    pl.ds(pl.multiple_of(row, slab), slab),
                                    pl.ds(pl.multiple_of(lane, lanes), lanes),
                                ],
                                sem_ref.at[len(copies)],
                            )
                        )
        copy_all(copies)

    found = pl.pallas_call(
        kernel,
        in_specs=[SCALARS] + [ANYWHERE] * (len(flat) + len(reads)) + [WHOLE] * len(after),
        out_specs=[WHOLE] * 2,
        out_shape=[jax.ShapeDtypeStruct((taps, inner, cores * lanes), jnp.bfloat16), TOKEN],
        scratch_shapes=[pltpu.SemaphoreType.DMA((cores * seqs * acrosses * tap_peers,))],
        compiler_params=pltpu.CompilerParams(vmem_limit_bytes=VMEM_BYTES),
        cost_estimate=cost(3),
        name="place_conv",
    )(jnp.stack(places).astype(jnp.int32), *flat, *reads, *after)
    return found[0], (found[1],)


def place_ffn(pieces, sizes, after=(), reads=()):
    cores, seqs, acrosses, tap_peers = sizes
    cuts, ffn_rows, lanes = pieces[0][0].shape[2:]
    cuts //= 2
    width = cuts * lanes
    units = seqs * acrosses * tap_peers * ffn_rows
    if ffn_rows % ROW_TILE:
        full = jnp.stack([jnp.stack(row) for row in pieces])
        full = full.reshape(cores, acrosses, seqs, tap_peers, 2, cuts, ffn_rows, lanes)
        full = full.transpose(4, 0, 1, 2, 3, 6, 5, 7).reshape(2, cores, units, width)
        return [full[0, c] for c in range(cores)], [full[1, c] for c in range(cores)], after
    flat = [piece for row in pieces for piece in row]

    def kernel(*refs):
        out_refs = refs[-2 - 2 * cores : -2]
        token_ref, sem_ref = refs[-2:]
        token_ref[...] = jnp.zeros(TOKEN.shape, TOKEN.dtype)
        copies = []
        for c in range(cores):
            for a in range(acrosses):
                for which in range(2):
                    for cut in range(cuts):
                        copies.append(
                            pltpu.make_async_copy(
                                refs[c * acrosses + a].at[:, :, which * cuts + cut],
                                out_refs[which * cores + c].at[
                                    a, :, :, :, pl.ds(cut * lanes, lanes)
                                ],
                                sem_ref.at[len(copies)],
                            )
                        )
        copy_all(copies)

    shape = jax.ShapeDtypeStruct((acrosses, seqs, tap_peers, ffn_rows, width), jnp.bfloat16)
    found = pl.pallas_call(
        kernel,
        in_specs=[ANYWHERE] * (len(flat) + len(reads)) + [WHOLE] * len(after),
        out_specs=[WHOLE] * (2 * cores + 1),
        out_shape=[shape] * (2 * cores) + [TOKEN],
        scratch_shapes=[pltpu.SemaphoreType.DMA((2 * cores * acrosses * cuts,))],
        compiler_params=pltpu.CompilerParams(vmem_limit_bytes=VMEM_BYTES),
        cost_estimate=cost(2),
        name="place_ffn",
    )(*flat, *reads, *after)
    token = found[-1]
    found = [each.reshape(units, width) for each in found[:-1]]
    return found[:cores], found[cores:], (token,)


class Ring:
    def __init__(self, axis, size, index, pairs):
        self.axis, self.size, self.index, self.pairs = axis, size, index, pairs

    def shifted(self, value, by):
        return lax.ppermute(value, self.axis, self.pairs(lambda i: (i + by) % self.size))

    def swapped(self, value, bit):
        return lax.ppermute(value, self.axis, self.pairs(lambda i: i ^ bit))

    def gather(self, value):
        return [value] + [self.shifted(value, by) for by in range(1, self.size)]

    def swap(self, values):
        return [values[0]] + [self.shifted(values[by], -by) for by in range(1, self.size)]


def relative(value, axis, place, size):
    if size == 1:
        return value
    return jnp.stack(
        [
            lax.dynamic_index_in_dim(value, (place - slot) % size, axis, False)
            for slot in range(size)
        ],
        axis,
    )


def rings():
    peers = lax.axis_size("dp")
    cores = CORES if peers % CORES == 0 else 1
    columns = peers // cores
    place = lax.axis_index("dp")

    def plain(axis):
        size = lax.axis_size(axis)
        return Ring(
            axis, size, lax.axis_index(axis), lambda move: [(i, move(i)) for i in range(size)]
        )

    across = Ring(
        "dp",
        columns,
        place // cores,
        lambda move: [(i, move(i // cores) * cores + i % cores) for i in range(peers)],
    )
    core = Ring(
        "dp",
        cores,
        place % cores,
        lambda move: [(i, i // cores * cores + move(i % cores)) for i in range(peers)],
    )
    return core, across, plain("seq"), plain("tap")


class Reduce:
    def __init__(self, terms, order):
        self.order = order
        self.parts = [terms[0]] + [order[0].shifted(terms[s], -s) for s in range(1, order[0].size)]

    def step(self, level, after, reads=()):
        ring = self.order[level]
        found, token = add_slots(self.parts, ring.size, after, reads)
        self.parts = [found[0]] + [ring.shifted(found[s], -s) for s in range(1, ring.size)]
        return (token,)


def shared_copies(value, across, seq):
    peers, spans = lax.axis_size("dp"), lax.axis_size("seq")
    cores = peers // across.size

    def target(place, by_a, by_s):
        dp, at = place // spans, place % spans
        moved = (dp // cores + by_a) % across.size * cores + dp % cores
        return moved * spans + (at + by_s) % spans

    return [
        [
            value
            if by_a == by_s == 0
            else lax.ppermute(
                value,
                ("dp", "seq"),
                [(place, target(place, by_a, by_s)) for place in range(peers * spans)],
            )
            for by_a in range(across.size)
        ]
        for by_s in range(seq.size)
    ]


def passed_along(value, axis, by):
    peers = lax.axis_size(axis)
    pairs = [(i, i + by) for i in range(peers) if 0 <= i + by < peers]
    return lax.ppermute(value, axis, pairs)


def rims(source, reach_rows, seq):
    span_rows = source.shape[0]
    if seq.size == 2 and reach_rows <= span_rows:
        first = (1 - seq.index) * (span_rows - reach_rows)
        return seq.shifted(lax.dynamic_slice_in_dim(source, first, reach_rows, 0), 1)
    left_parts = []
    right_parts = []
    distances = -(-reach_rows // span_rows)
    for distance in range(1, distances + 1):
        rim_count = min(span_rows, reach_rows - (distance - 1) * span_rows)
        left_parts.insert(0, passed_along(source[span_rows - rim_count :], "seq", distance))
        right_parts.append(passed_along(source[:rim_count], "seq", -distance))
    return left_parts, right_parts


def extend(source, found, seq, after=()):
    if isinstance(found, tuple):
        return join_rows(found[0] + [source] + found[1], after)
    reach, span = found.shape[0], source.shape[0]

    def kernel(place_ref, found_ref, source_ref, *refs):
        out_ref, token_ref = refs[-2:]
        token_ref[...] = jnp.zeros(TOKEN.shape, TOKEN.dtype)
        out_ref[reach : reach + span] = source_ref[...]
        zeros = jnp.zeros(found.shape, found.dtype)

        @pl.when(place_ref[0] == 0)
        def _():
            out_ref[:reach] = zeros
            out_ref[reach + span :] = found_ref[...]

        @pl.when(place_ref[0] != 0)
        def _():
            out_ref[:reach] = found_ref[...]
            out_ref[reach + span :] = zeros

    shape = jax.ShapeDtypeStruct((span + 2 * reach, source.shape[1]), source.dtype)
    extended, token = pl.pallas_call(
        kernel,
        in_specs=[SCALARS] + [WHOLE] * (2 + len(after)),
        out_specs=[WHOLE] * 2,
        out_shape=[shape, TOKEN],
        compiler_params=pltpu.CompilerParams(vmem_limit_bytes=VMEM_BYTES),
        cost_estimate=cost(1.5),
        name="extend",
    )(seq.index.astype(jnp.int32)[None], found, source, *after)
    return extended, (token,)


def to_rows(values):
    windows, positions = values.shape[:2]
    cut = values.reshape((windows, positions // FIRST_DILATION, FIRST_DILATION) + values.shape[2:])
    return jnp.swapaxes(cut, 0, 1).reshape((windows * positions,) + values.shape[2:])


def from_rows(values, windows):
    cut = values.reshape((-1, windows, FIRST_DILATION) + values.shape[1:])
    return jnp.swapaxes(cut, 0, 1).reshape((windows, -1) + values.shape[1:])


def on_device(
    inputs,
    targets,
    masked,
    conv_weight,
    conv_bias,
    gains,
    shifts,
    in_weight,
    in_bias,
    out_weight,
    out_bias,
    head_weight,
):
    core, across, seq, tap = rings()
    taps = conv_weight.shape[1]
    channels = conv_weight.shape[2]
    width = conv_weight.shape[3]
    slab = channels // (seq.size * across.size)
    lanes = width // core.size
    hidden_width = in_bias.shape[1]
    ffn_rows = in_weight.shape[2]
    windows = inputs.shape[0]
    rows = windows * inputs.shape[1]
    steps = (FIRST_DILATION * windows, SECOND_DILATION * windows)
    units = hidden_width // core.size
    places = (core.index, seq.index, across.index, tap.index)
    sizes = (core.size, seq.size, across.size, tap.size)

    in_bias_placed = []
    for b in range(2):
        bias = in_bias[b].reshape(across.size, core.size, seq.size, tap.size, ffn_rows)
        for axis, ring in enumerate((across, core, seq, tap)):
            bias = relative(bias, axis, ring.index, ring.size)
        in_bias_placed.append(bias.transpose(1, 0, 2, 3, 4).reshape(core.size, units))

    def cut_ffn(piece):
        return piece.reshape(ffn_rows, core.size, lanes).swapaxes(0, 1).reshape(-1, lanes)

    def bundle(b):
        conv_piece = lax.dynamic_slice(
            conv_weight[b],
            (0, (seq.index * across.size + across.index) * slab, core.index * lanes),
            (taps, slab, lanes),
        )
        pieces = [
            conv_piece.reshape(taps * slab, lanes),
            cut_ffn(in_weight[b].T),
            cut_ffn(out_weight[b]),
        ]
        return jnp.concatenate(pieces)

    cuts = (
        (0, taps * slab, (taps, slab, lanes)),
        (taps * slab, taps * slab + 2 * core.size * ffn_rows, (2 * core.size, ffn_rows, lanes)),
    )

    def straight(arrays):
        return (arrays, ((0, None, arrays[0].shape),))

    conv_input = to_rows(inputs)
    stream = conv_input
    codes = to_rows(targets + masked * head_weight.shape[1])
    codes = jnp.broadcast_to(codes[:, None], (rows, 128))

    tap_parts = tap.gather(bundle(0))
    (conv_part, ffn_part), last = restack([(tap_parts, cuts)])
    split = (tap.size + 1) // 2
    (behind,), last = hold([bundle(1)], last)
    late_parts = tap.gather(behind)
    extended, last = extend(conv_input, rims(conv_input, taps // 2 * steps[0], seq), seq, last)
    extended_parts = [extended] + [core.shifted(extended, -c) for c in range(1, core.size)]
    conv_parts, ffn_parts = across.gather(conv_part), seq.gather(ffn_part)
    (conv_part, ffn_part), last = restack(
        [straight(conv_parts), straight(ffn_parts)],
        reads=[late_parts[by] for by in range(1, tap.size) if by != split],
        after=last,
    )
    conv_parts, ffn_parts = seq.gather(conv_part), across.gather(ffn_part)
    conv_slots = [core.gather(conv_part)]
    ffn_slots = [core.gather(ffn_part)]
    arrived = [conv_parts[1:], ffn_parts[1:], conv_slots[0][1:], ffn_slots[0][1:], late_parts[1:]]
    held, last = hold([each for some in arrived for each in some], last)
    for i, some in enumerate(arrived):
        arrived[i], held = held[: len(some)], held[len(some) :]
    conv_slots = [[conv_part] + arrived[2]] + [core.gather(each) for each in arrived[0]]
    ffn_slots = [[ffn_part] + arrived[3]] + [core.gather(each) for each in arrived[1]]
    (late_conv, late_ffn), last = restack([(late_parts[:1] + arrived[4], cuts)], after=last)
    late_conv_parts, late_ffn_parts = across.gather(late_conv), seq.gather(late_ffn)

    def turned(slots):
        return [[each[c] for each in slots] for c in range(core.size)]

    conv_full, in_full, out_full = [None, None], [None, None], [None, None]
    conv_full[0], last = place_conv(
        turned(conv_slots), places, sizes, last, [part for each in ffn_slots for part in each[1:]]
    )
    saved = []
    reads = []
    for b in range(2):
        if b == 1:
            found = rims(conv_input, taps // 2 * steps[1], seq)
            held, last = hold(late_conv_parts[1:] + late_ffn_parts[1:], last)
            late_conv_slots += [core.gather(each) for each in held[: seq.size - 1]]
            late_ffn_slots += [core.gather(each) for each in held[seq.size - 1 :]]
            conv_full[1], last = place_conv(turned(late_conv_slots), places, sizes, last)
            in_full[1], out_full[1], last = place_ffn(turned(late_ffn_slots), sizes, last)
            extended, last = extend(conv_input, found, seq, last)
            extended_parts = [extended] + [core.shifted(extended, -c) for c in range(1, core.size)]
        (normed_conv, conv_slope, stream, lowered), last = conv_forward(
            extended,
            conv_full[b],
            stream,
            conv_bias[b],
            gains[b, 0],
            shifts[b, 0],
            steps[b],
            last,
            reads,
        )
        reads = extended_parts[1:]
        if b == 0:
            (late_conv, late_ffn), last = restack(
                [straight(late_conv_parts), straight(late_ffn_parts)], after=last
            )
            late_conv_parts, late_ffn_parts = seq.gather(late_conv), across.gather(late_ffn)
            late_conv_slots = [core.gather(late_conv)]
            late_ffn_slots = [core.gather(late_ffn)]
            in_full[0], out_full[0], last = place_ffn(turned(ffn_slots), sizes, last)
            reads = reads + late_conv_slots[0][1:] + late_ffn_slots[0][1:]
        active, hidden_slopes, (normed_ffn, scale_ffn, stream, conv_input), packets, last = (
            ffn_forward(
                lowered,
                stream,
                in_full[b],
                out_full[b],
                [in_bias_placed[b][c] for c in range(core.size)],
                out_bias[b],
                gains[b, 1],
                shifts[b, 1],
                last,
                reads,
            )
        )
        packets = [core.shifted(packet, -1 - c) for c, packet in enumerate(packets)]
        reads = packets
        saved.append(
            (
                extended_parts,
                conv_slope,
                normed_conv,
                (active, lowered, packets),
                hidden_slopes,
                normed_ffn,
                scale_ffn,
            )
        )

    final_state = from_rows(conv_input, windows)
    (stream_grad, head_grad, loss_rows), last = head_and_loss(stream, head_weight, codes, last)

    ffn_rows_of_sums = [None, None]
    conv_rows_of_sums = [None, None]
    in_bias_grads = [None, None]
    ffn_sums = [None, None]
    conv_sums = [None, None]
    merged = [None, None]

    for b in (1, 0):
        (
            extended_parts,
            conv_slope,
            normed_conv,
            active_pair,
            hidden_slopes,
            normed_ffn,
            scale_ffn,
        ) = saved[b]
        output_grad, hidden_grad, biases, packets, ffn_rows_of_sums[b], last = ffn_back_hidden(
            stream_grad, normed_ffn, scale_ffn, gains[b, 1], out_full[b], hidden_slopes, last
        )
        if b == 1:
            arrived_packets = [core.shifted(packet, -1 - c) for c, packet in enumerate(packets)]
        if b == 0:
            last = ffn_sums[1].step(1, last, [final_state])
            last = conv_sums[1].step(1, last)
        stream_grad, conv_grad, conv_cuts, relayed, conv_rows_of_sums[b], last = ffn_back_stream(
            stream_grad,
            hidden_grad,
            packets,
            in_full[b],
            normed_conv,
            conv_slope,
            gains[b, 0],
            core.index,
            last,
            reads,
            relay=b == 0,
        )
        reads = []
        if b == 0:
            merged[1], last = merge_slots(conv_sums[1].parts, ffn_sums[1].parts, tap.size, last)
            held, last = hold([conv_grad] + list(conv_cuts) + list(relayed), last)
            conv_grad, conv_cuts, relayed = held[0], held[1 : core.size], held[core.size :]
            merged[1] = tap.swap(merged[1])
            arrived_packets = [core.shifted(packet, -1 - c) for c, packet in enumerate(relayed)]
        arrived = [core.shifted(conv_cuts[c - 1], -c) for c in range(1, core.size)]
        in_bias_grads[b] = list(biases)
        found_rims = rims(conv_grad, taps // 2 * steps[b], seq)

        def ffn_grads(last):
            active, lowered, packets = active_pair
            if core.size == 1:
                packets = []
            found, token = ffn_weight_grad(
                (
                    (hidden_grad, lowered, [(g, p) for g, p in zip(arrived_packets, packets)]),
                    (active, output_grad, [(p, g) for g, p in zip(arrived_packets, packets)]),
                ),
                sizes,
                ffn_rows,
                last,
            )
            return Reduce(found, (across, seq, tap)), (token,)

        def conv_grads(last, reads=()):
            found, token = conv_weight_grad(
                extended_parts, conv_grad, arrived, places, sizes, taps, steps[b], last, reads
            )
            found = [each.reshape(-1, lanes) for each in found]
            return Reduce(found, (seq, across, tap)), (token,)

        if b == 1:
            ffn_sums[1], last = ffn_grads(last)
            extended_grad, last = extend(conv_grad, found_rims, seq, last)
            conv_sums[1], last = conv_grads(last)
        else:
            extended_grad, last = extend(conv_grad, found_rims, seq, last)
            conv_sums[0], last = conv_grads(last)
            ffn_sums[0], last = ffn_grads(last)
        stream_grad, last = conv_data_grad(
            extended_grad,
            conv_full[b],
            stream_grad,
            steps[b],
            jnp.float32 if b == 1 else jnp.bfloat16,
            last,
        )

    grad_inputs = from_rows(stream_grad, windows)
    last = conv_sums[0].step(1, last, [grad_inputs])
    last = ffn_sums[0].step(1, last, merged[1][1:])

    def placed_bias(biases):
        bias = jnp.stack(biases).reshape(core.size, across.size, seq.size, tap.size, ffn_rows)
        for axis, ring in enumerate((core, across, seq, tap)):
            bias = relative(bias, axis, ring.index, ring.size)
        return bias.transpose(1, 0, 2, 3, 4).reshape(-1, width)

    held, last = hold(in_bias_grads[1] + in_bias_grads[0], last)
    terms = jnp.stack([loss_rows[0, 0], loss_rows[1, 0]])
    terms = jnp.stack([terms, terms - wide(low(terms))])
    small = [
        conv_rows_of_sums[0][:3],
        conv_rows_of_sums[1][:3],
        ffn_rows_of_sums[0][:3],
        ffn_rows_of_sums[1][:3],
        placed_bias(held[core.size :]),
        placed_bias(held[: core.size]),
        head_grad[: head_weight.shape[1]],
        jnp.pad(terms, ((0, 0), (0, width - 2))),
    ]
    small_counts = [each.shape[0] for each in small]
    packed = low(jnp.concatenate(small)).reshape(-1, lanes)
    packed = jnp.pad(packed, ((0, -packed.shape[0] % ROW_TILE), (0, 0)))

    conv_rows = taps * slab
    merged[0], last = append_slots(conv_sums[0].parts, packed, tap.size, last)
    merged[0] = tap.swap(merged[0])
    last = ffn_sums[0].step(2, last)
    shards, last = finish_conv([merged[0], merged[1]], conv_rows, packed.shape[0], last)
    copies = [each for row in shared_copies(shards, across, seq) for each in row]
    grad_in, grad_out, last = finish_ffn(merged[1], ffn_sums[0].parts, conv_rows, ffn_rows, last)
    (stack,), last = restack([straight(copies)], after=last)
    stacks = core.gather(stack)
    grad_conv = place_conv_grads(
        [
            each[:, : 2 * conv_rows].reshape(len(copies), 2, taps, slab, lanes) for each in stacks
        ],
        places,
        sizes,
    )
    packed = small_total([each[:, 2 * conv_rows :] for each in stacks], places, sizes)
    packed = packed.reshape(-1, width)
    unpacked = []
    first = 0
    for count in small_counts:
        unpacked.append(packed[first : first + count])
        first += count
    conv_0, conv_1, ffn_0, ffn_1, bias_0, bias_1, head_sum, loss_terms = unpacked
    grad_conv_bias = jnp.stack([conv_0[2], conv_1[2]])
    grad_gains = jnp.stack([jnp.stack([conv_0[0], ffn_0[0]]), jnp.stack([conv_1[0], ffn_1[0]])])
    grad_shifts = jnp.stack([jnp.stack([conv_0[1], ffn_0[1]]), jnp.stack([conv_1[1], ffn_1[1]])])
    grad_in_bias = jnp.stack([bias_0.reshape(-1), bias_1.reshape(-1)])
    grad_out_bias = jnp.stack([ffn_0[2], ffn_1[2]])
    loss_terms = loss_terms[0, :2] + loss_terms[1, :2]
    return (
        final_state,
        grad_inputs,
        grad_conv,
        grad_conv_bias,
        grad_gains,
        grad_shifts,
        grad_in,
        grad_in_bias,
        grad_out,
        grad_out_bias,
        head_sum.T,
        loss_terms[0] / loss_terms[1],
    )


def solution(mesh):
    placed = (
        P(("dp", "tap"), "seq", None),
        P(("dp", "tap"), "seq"),
        P(("dp", "tap"), "seq"),
        P(None, None, "tap", None),
        P(),
        P(),
        P(),
        P(None, None, ("dp", "seq", "tap")),
        P(),
        P(None, ("dp", "seq", "tap"), None),
        P(),
        P(),
    )
    return jax.shard_map(
        on_device,
        mesh=mesh,
        in_specs=placed,
        out_specs=(
            P(("dp", "tap"), "seq", None),
            P(("dp", "tap"), "seq", None),
            P(None, None, "tap", None),
            P(),
            P(),
            P(),
            P(None, None, ("dp", "seq", "tap")),
            P(),
            P(None, ("dp", "seq", "tap"), None),
            P(),
            P(),
            P(),
        ),
        check_vma=False,
    )
```

```python
import functools

import jax
import jax.numpy as jnp
import numpy as np
from jax import lax
from jax.experimental import pallas as pl
from jax.experimental.pallas import tpu as pltpu
from jax.sharding import PartitionSpec as P

FIRST_DILATION = 4
SECOND_DILATION = 32
EPSILON = 1e-05
HIGHEST_PRECISION = lax.Precision.HIGHEST
CORES = 2
ROW_TILE = 16
VMEM_BYTES = 20 * 1024 * 1024
ANYWHERE = pl.BlockSpec(memory_space=pl.ANY)
SCALARS = pl.BlockSpec(memory_space=pltpu.SMEM)


TOKEN = jax.ShapeDtypeStruct((8, 128), jnp.float32)


def cost(microseconds):
    size = int(microseconds * 3.5e6)
    return pl.CostEstimate(flops=int(microseconds * 1.1e9), bytes_accessed=size, transcendentals=0)


WHOLE = pl.BlockSpec(memory_space=pltpu.VMEM)
TOKEN_SPEC = pl.BlockSpec(TOKEN.shape, lambda *_: (0, 0))


def tokens(after):
    return [TOKEN_SPEC] * len(after)


def low(values):
    return values.astype(jnp.bfloat16)


def wide(values):
    return values.astype(jnp.float32)


def gelu_parts(values):
    phi = 0.5 * (1.0 + lax.erf(values * 0.7071067811865476))
    return (
        values * phi,
        phi + values * jnp.exp(-0.5 * values * values) * 0.3989422804014327,
    )


def normalize(values):
    center = values - jnp.mean(values, -1, keepdims=True)
    scale = lax.rsqrt(jnp.mean(center * center, -1, keepdims=True) + EPSILON)
    return (center * scale, scale)


def norm_back(upstream, normed, scale):
    return scale * (
        upstream
        - jnp.mean(upstream, -1, keepdims=True)
        - normed * jnp.mean(upstream * normed, -1, keepdims=True)
    )


def tap_groups(taps):
    return 3 if taps % 3 == 0 else 1


def row_chunks(rows, most):
    size = min(rows, most)
    return [(first, size) for first in range(0, rows, size)]


def conv_forward(extended, weight, stream, bias, gain, shift, step, after=(), reads=()):
    taps, inner, width = weight.shape
    rows = stream.shape[0]
    group = tap_groups(taps)
    steps = taps // group

    def kernel(extended_ref, weight_ref, stream_ref, bias_ref, gain_ref, shift_ref, *refs):
        normed_ref, slope_ref, next_ref, lowered_ref, token_ref, total_ref = refs[-6:]
        token_ref[...] = jnp.zeros(TOKEN.shape, TOKEN.dtype)
        first = pl.program_id(0) * group
        total = None
        for j in range(group):
            start = pl.multiple_of((first + j) * step, ROW_TILE)
            term = jnp.dot(
                extended_ref[pl.ds(start, rows), :],
                weight_ref[j],
                preferred_element_type=jnp.float32,
            )
            total = term if total is None else total + term

        @pl.when(pl.program_id(0) == 0)
        def _():
            total_ref[...] = total

        @pl.when(pl.program_id(0) > 0)
        def _():
            total_ref[...] += total

        @pl.when(pl.program_id(0) == steps - 1)
        def _():
            for at, size in row_chunks(rows, 128):
                some = pl.ds(at, size)
                value, slope = gelu_parts(total_ref[some, :] + bias_ref[...])
                normed, scale = normalize(value)
                mid = wide(stream_ref[some, :]) + normed * gain_ref[...] + shift_ref[...]
                normed_ref[some, :] = low(normed)
                slope_ref[some, :] = low(scale * slope)
                next_ref[some, :] = mid
                lowered_ref[some, :] = low(mid)

    whole = pl.BlockSpec((rows, width), lambda g: (0, 0))
    row = pl.BlockSpec((1, width), lambda g: (0, 0))
    found = pl.pallas_call(
        kernel,
        grid=(steps,),
        in_specs=[
            pl.BlockSpec(extended.shape, lambda g: (0, 0)),
            pl.BlockSpec((group, inner, width), lambda g: (g, 0, 0)),
            whole,
            row,
            row,
            row,
        ]
        + tokens(after)
        + [ANYWHERE] * len(reads),
        out_specs=[whole] * 4 + [TOKEN_SPEC],
        out_shape=[
            pltpu.HBM((rows, width), jnp.bfloat16),
            pltpu.HBM((rows, width), jnp.bfloat16),
            jax.ShapeDtypeStruct((rows, width), jnp.float32),
            jax.ShapeDtypeStruct((rows, width), jnp.bfloat16),
            TOKEN,
        ],
        scratch_shapes=[pltpu.VMEM((rows, width), jnp.float32)],
        compiler_params=pltpu.CompilerParams(vmem_limit_bytes=VMEM_BYTES),
        cost_estimate=cost(9),
        name="conv_forward",
    )(extended, weight, stream, bias[None], gain[None], shift[None], *after, *reads)
    return found[:4], (found[4],)


def ffn_forward(
    lowered, stream, ins, outs, in_biases, out_bias, gain, shift, after=(), reads=()
):
    rows, width = lowered.shape
    cores = len(ins)
    units = ins[0].shape[0]
    block = min(units, 256)
    steps = units // block

    def kernel(lowered_ref, stream_ref, out_bias_ref, gain_ref, shift_ref, *refs):
        in_refs, out_refs, bias_refs = (refs[i * cores : (i + 1) * cores] for i in range(3))
        found_refs = refs[-6 - 2 * cores :]
        active_ref, slope_refs = found_refs[0], found_refs[1 : 1 + cores]
        normed_ref, scale_ref, next_ref, rounded_ref = found_refs[1 + cores : 5 + cores]
        packet_refs = found_refs[5 + cores : -2]
        token_ref, total_ref = found_refs[-2:]
        token_ref[...] = jnp.zeros(TOKEN.shape, TOKEN.dtype)
        lane = pl.multiple_of(width + pl.program_id(0) * block, block)

        @pl.when(pl.program_id(0) == 0)
        def _():
            total_ref[...] = jnp.zeros(total_ref.shape, jnp.float32)
            for packet_ref in packet_refs:
                packet_ref[:, :width] = lowered_ref[...]

        for at, size in row_chunks(rows, 512):
            some = pl.ds(at, size)
            term = None
            for c in range(cores):
                hidden = lax.dot_general(
                    lowered_ref[some, :],
                    in_refs[c][...],
                    (((1,), (1,)), ((), ())),
                    preferred_element_type=jnp.float32,
                )
                active, slope = gelu_parts(hidden + bias_refs[c][...])
                active = low(active)
                if c == 0:
                    active_ref[some, :] = active
                else:
                    packet_refs[c - 1][some, pl.ds(lane, block)] = active
                slope_refs[c][some, :] = low(slope)
                found = jnp.dot(active, out_refs[c][...], preferred_element_type=jnp.float32)
                term = found if term is None else term + found
            total_ref[some, :] += term

        @pl.when(pl.program_id(0) == steps - 1)
        def _():
            for at, size in row_chunks(rows, 128):
                some = pl.ds(at, size)
                normed, scale = normalize(total_ref[some, :] + out_bias_ref[...])
                after_ffn = stream_ref[some, :] + normed * gain_ref[...] + shift_ref[...]
                normed_ref[some, :] = low(normed)
                scale_ref[some, :] = jnp.broadcast_to(scale, (size, 128))
                next_ref[some, :] = after_ffn
                rounded_ref[some, :] = low(after_ffn)

    whole = pl.BlockSpec((rows, width), lambda g: (0, 0))
    row = pl.BlockSpec((1, width), lambda g: (0, 0))
    piece = pl.BlockSpec((block, width), lambda g: (g, 0))
    columns = pl.BlockSpec((rows, block), lambda g: (0, g))
    hidden_shape = pltpu.HBM((rows, units), jnp.bfloat16)
    found = pl.pallas_call(
        kernel,
        grid=(steps,),
        in_specs=[whole, whole, row, row, row]
        + [piece] * (2 * cores)
        + [pl.BlockSpec((1, block), lambda g: (0, g))] * cores
        + tokens(after)
        + [ANYWHERE] * len(reads),
        out_specs=[columns] * (1 + cores)
        + [whole, pl.BlockSpec((rows, 128), lambda g: (0, 0)), whole, whole]
        + [pl.BlockSpec((rows, width + units), lambda g: (0, 0))] * (cores - 1)
        + [TOKEN_SPEC],
        out_shape=[hidden_shape] * (1 + cores)
        + [
            pltpu.HBM((rows, width), jnp.bfloat16),
            pltpu.HBM((rows, 128), jnp.float32),
            jax.ShapeDtypeStruct((rows, width), jnp.float32),
            jax.ShapeDtypeStruct((rows, width), jnp.bfloat16),
        ]
        + [jax.ShapeDtypeStruct((rows, width + units), jnp.bfloat16)] * (cores - 1)
        + [TOKEN],
        scratch_shapes=[pltpu.VMEM((rows, width), jnp.float32)],
        compiler_params=pltpu.CompilerParams(vmem_limit_bytes=VMEM_BYTES),
        cost_estimate=cost(11),
        name="ffn_forward",
    )(
        lowered,
        stream,
        out_bias[None],
        gain[None],
        shift[None],
        *ins,
        *outs,
        *[each[None] for each in in_biases],
        *after,
        *reads,
    )
    return (
        found[0],
        found[1 : 1 + cores],
        found[1 + cores : 5 + cores],
        found[5 + cores : -1],
        (found[-1],),
    )


def head_and_loss(stream, head_weight, codes, after=()):
    rows, width = stream.shape
    classes = head_weight.shape[1]
    padded = jnp.pad(head_weight, ((0, 0), (0, 128 - classes)))
    cuts = row_chunks(rows, 256)

    def kernel(stream_ref, head_ref, code_ref, *refs):
        grad_ref, head_grad_ref, sums_ref, token_ref = refs[-4:]
        token_ref[...] = jnp.zeros(TOKEN.shape, TOKEN.dtype)
        head_grad = jnp.zeros((128, width), jnp.float32)
        objective = jnp.zeros((1, 1), jnp.float32)
        scored = jnp.zeros((1, 1), jnp.float32)
        for at, size in cuts:
            some = pl.ds(at, size)
            value = stream_ref[some, :]
            code = code_ref[some, :]
            mask = jnp.where(code[:, :1] >= classes, 1.0, 0.0)
            logits = jnp.dot(
                value, head_ref[...], precision=HIGHEST_PRECISION, preferred_element_type=jnp.float32
            )
            lane = lax.broadcasted_iota(jnp.int32, logits.shape, 1)
            valid = lane < classes
            peak = jnp.max(jnp.where(valid, logits, -jnp.inf), -1, keepdims=True)
            exponent = jnp.where(valid, jnp.exp(jnp.where(valid, logits - peak, 0.0)), 0.0)
            denominator = jnp.sum(exponent, -1, keepdims=True)
            chosen = lane == jnp.where(code >= classes, code - classes, code)
            picked = jnp.sum(jnp.where(chosen, logits, 0.0), -1, keepdims=True)
            terms = mask * (peak + jnp.log(denominator) - picked)
            objective = objective + jnp.sum(terms, 0, keepdims=True)
            scored = scored + jnp.sum(mask, 0, keepdims=True)
            logit_grad = mask * (exponent / denominator - jnp.where(chosen, 1.0, 0.0))
            grad_ref[some, :] = lax.dot_general(
                logit_grad,
                head_ref[...],
                (((1,), (1,)), ((), ())),
                precision=HIGHEST_PRECISION,
                preferred_element_type=jnp.float32,
            )
            head_grad = head_grad + lax.dot_general(
                logit_grad,
                value,
                (((0,), (0,)), ((), ())),
                precision=HIGHEST_PRECISION,
                preferred_element_type=jnp.float32,
            )
        head_grad_ref[...] = head_grad[: head_grad_ref.shape[0]]
        at_row = lax.broadcasted_iota(jnp.int32, sums_ref.shape, 0)
        sums_ref[...] = jnp.where(at_row == 0, objective, scored)

    found = pl.pallas_call(
        kernel,
        out_shape=[
            jax.ShapeDtypeStruct((rows, width), jnp.float32),
            jax.ShapeDtypeStruct((-(-classes // 8) * 8, width), jnp.float32),
            jax.ShapeDtypeStruct((8, 128), jnp.float32),
            TOKEN,
        ],
        compiler_params=pltpu.CompilerParams(vmem_limit_bytes=VMEM_BYTES),
        cost_estimate=cost(6),
        name="head_and_loss",
    )(stream, padded, codes, *after)
    return found[:3], (found[3],)


def ffn_back_hidden(upstream, normed, scale, gain, outs, slopes, after=()):
    rows, width = upstream.shape
    cores = len(outs)
    units = outs[0].shape[0]
    block = min(units, 256)

    def kernel(upstream_ref, normed_ref, scale_ref, gain_ref, *refs):
        out_refs, slope_refs = refs[:cores], refs[cores : 2 * cores]
        found_refs = refs[-3 - 2 * cores :]
        output_grad_ref, hidden_ref = found_refs[:2]
        bias_refs, packet_refs = found_refs[2 : 2 + cores], found_refs[2 + cores : -2]
        sums_ref, token_ref = found_refs[-2:]
        token_ref[...] = jnp.zeros(TOKEN.shape, TOKEN.dtype)
        lane = pl.multiple_of(width + pl.program_id(0) * block, block)

        @pl.when(pl.program_id(0) == 0)
        def _():
            totals = [jnp.zeros((1, width), jnp.float32)] * 3
            for at, size in row_chunks(rows, 128):
                some = pl.ds(at, size)
                grad, value = upstream_ref[some, :], wide(normed_ref[some, :])
                output_grad = low(norm_back(grad * gain_ref[...], value, scale_ref[some, :1]))
                output_grad_ref[some, :] = output_grad
                for packet_ref in packet_refs:
                    packet_ref[some, :width] = output_grad
                for i, each in enumerate((grad * value, grad, wide(output_grad))):
                    totals[i] = totals[i] + jnp.sum(each, 0, keepdims=True)
            sums_ref[...] = jnp.zeros(sums_ref.shape, jnp.float32)
            for i in range(3):
                sums_ref[i : i + 1, :] = totals[i]

        for c in range(cores):
            total = jnp.zeros((1, block), jnp.float32)
            for at, size in row_chunks(rows, 512):
                some = pl.ds(at, size)
                active_grad = lax.dot_general(
                    output_grad_ref[some, :],
                    out_refs[c][...],
                    (((1,), (1,)), ((), ())),
                    preferred_element_type=jnp.float32,
                )
                hidden_grad = low(active_grad * wide(slope_refs[c][some, :]))
                if c == 0:
                    hidden_ref[some, :] = hidden_grad
                else:
                    packet_refs[c - 1][some, pl.ds(lane, block)] = hidden_grad
                total = total + jnp.sum(wide(hidden_grad), 0, keepdims=True)
            bias_refs[c][...] = total

    whole = pl.BlockSpec((rows, width), lambda g: (0, 0))
    columns = pl.BlockSpec((rows, block), lambda g: (0, g))
    found = pl.pallas_call(
        kernel,
        grid=(units // block,),
        in_specs=[
            whole,
            whole,
            pl.BlockSpec((rows, 128), lambda g: (0, 0)),
            pl.BlockSpec((1, width), lambda g: (0, 0)),
        ]
        + [pl.BlockSpec((block, width), lambda g: (g, 0))] * cores
        + [columns] * cores
        + tokens(after),
        out_specs=[whole, columns]
        + [pl.BlockSpec((1, block), lambda g: (0, g))] * cores
        + [pl.BlockSpec((rows, width + units), lambda g: (0, 0))] * (cores - 1)
        + [pl.BlockSpec((8, width), lambda g: (0, 0)), TOKEN_SPEC],
        out_shape=[
            jax.ShapeDtypeStruct((rows, width), jnp.bfloat16),
            jax.ShapeDtypeStruct((rows, units), jnp.bfloat16),
        ]
        + [jax.ShapeDtypeStruct((1, units), jnp.float32)] * cores
        + [jax.ShapeDtypeStruct((rows, width + units), jnp.bfloat16)] * (cores - 1)
        + [jax.ShapeDtypeStruct((8, width), jnp.float32), TOKEN],
        compiler_params=pltpu.CompilerParams(vmem_limit_bytes=VMEM_BYTES),
        cost_estimate=cost(6),
        name="ffn_back_hidden",
    )(upstream, normed, scale, gain[None], *outs, *slopes, *after)
    return (
        found[0],
        found[1],
        found[2 : 2 + cores],
        found[2 + cores : -2],
        found[-2],
        (found[-1],),
    )


def ffn_back_stream(
    upstream, hidden, packets, ins, normed, slope, gain, core_index, after=(), reads=(), relay=False
):
    rows, width = upstream.shape
    cores = len(ins)
    units = ins[0].shape[0]
    block = min(units, 256)
    steps = units // block
    lanes = width // cores
    relays = cores - 1 if relay else 0

    def kernel(core_ref, upstream_ref, normed_ref, slope_ref, gain_ref, *refs):
        hidden_refs, in_refs = refs[:cores], refs[cores : 2 * cores]
        found_refs = refs[-4 - cores - relays :]
        mid_ref, conv_grad_ref = found_refs[:2]
        cut_refs = found_refs[2 : 1 + cores]
        sums_ref, token_ref, total_ref = found_refs[-3:]
        token_ref[...] = jnp.zeros(TOKEN.shape, TOKEN.dtype)
        for i in range(relays):
            relay_ref = found_refs[1 + cores + i]
            lane = pl.multiple_of(width + pl.program_id(0) * block, block)
            relay_ref[:, pl.ds(lane, block)] = hidden_refs[1 + i][...]

            @pl.when(pl.program_id(0) == 0)
            def _(i=i, relay_ref=relay_ref):
                relay_ref[:, :width] = refs[2 * cores + i][...]

        @pl.when(pl.program_id(0) == 0)
        def _():
            total_ref[...] = upstream_ref[...]

        for at, size in row_chunks(rows, 512):
            some = pl.ds(at, size)
            total_ref[some, :] += sum(
                jnp.dot(
                    hidden_refs[c][some, :], in_refs[c][...], preferred_element_type=jnp.float32
                )
                for c in range(cores)
            )

        @pl.when(pl.program_id(0) == steps - 1)
        def _():
            totals = [jnp.zeros((1, width), jnp.float32)] * 3
            for at, size in row_chunks(rows, 128):
                some = pl.ds(at, size)
                grad, value = total_ref[some, :], wide(normed_ref[some, :])
                conv_grad = low(norm_back(grad * gain_ref[...], value, wide(slope_ref[some, :])))
                mid_ref[some, :] = grad
                conv_grad_ref[some, :] = conv_grad
                for i, each in enumerate((grad * value, grad, wide(conv_grad))):
                    totals[i] = totals[i] + jnp.sum(each, 0, keepdims=True)
            sums_ref[...] = jnp.zeros(sums_ref.shape, jnp.float32)
            for i in range(3):
                sums_ref[i : i + 1, :] = totals[i]
            for c in range(1, cores):
                first = lax.rem(core_ref[0] - c + cores, cores) * lanes
                cut_refs[c - 1][...] = conv_grad_ref[:, pl.ds(pl.multiple_of(first, lanes), lanes)]

    whole = pl.BlockSpec((rows, width), lambda g, core: (0, 0))
    found = pl.pallas_call(
        kernel,
        grid_spec=pltpu.PrefetchScalarGridSpec(
            num_scalar_prefetch=1,
            grid=(steps,),
            in_specs=[whole, whole, whole, pl.BlockSpec((1, width), lambda g, core: (0, 0))]
            + [pl.BlockSpec((rows, block), lambda g, core: (0, g))]
            + [pl.BlockSpec((rows, block), lambda g, core: (0, width // block + g))] * (cores - 1)
            + [pl.BlockSpec((block, width), lambda g, core: (g, 0))] * cores
            + [whole] * relays
            + tokens(after)
            + [ANYWHERE] * len(reads),
            out_specs=[whole, whole]
            + [pl.BlockSpec((rows, lanes), lambda g, core: (0, 0))] * (cores - 1)
            + [pl.BlockSpec((rows, width + units), lambda g, core: (0, 0))] * relays
            + [pl.BlockSpec((8, width), lambda g, core: (0, 0)), TOKEN_SPEC],
            scratch_shapes=[pltpu.VMEM((rows, width), jnp.float32)],
        ),
        out_shape=[
            jax.ShapeDtypeStruct((rows, width), jnp.float32),
            jax.ShapeDtypeStruct((rows, width), jnp.bfloat16),
        ]
        + [jax.ShapeDtypeStruct((rows, lanes), jnp.bfloat16)] * (cores - 1)
        + [jax.ShapeDtypeStruct((rows, width + units), jnp.bfloat16)] * relays
        + [jax.ShapeDtypeStruct((8, width), jnp.float32), TOKEN],
        compiler_params=pltpu.CompilerParams(vmem_limit_bytes=VMEM_BYTES),
        cost_estimate=cost(5),
        name="ffn_back_stream",
    )(
        core_index.astype(jnp.int32)[None],
        upstream,
        normed,
        slope,
        gain[None],
        hidden,
        *packets,
        *ins,
        *packets[:relays],
        *after,
        *reads,
    )
    return (
        found[0],
        found[1],
        found[2 : 1 + cores],
        found[1 + cores : 1 + cores + relays],
        found[-2],
        (found[-1],),
    )


def conv_data_grad(extended, weight, upstream, step, kind, after=()):
    taps, inner, width = weight.shape
    rows = upstream.shape[0]
    group = tap_groups(taps)
    steps = taps // group

    def kernel(extended_ref, weight_ref, upstream_ref, *refs):
        out_ref, token_ref, total_ref = refs[-3:]
        token_ref[...] = jnp.zeros(TOKEN.shape, TOKEN.dtype)
        first = pl.program_id(0) * group
        total = None
        for j in range(group):
            start = pl.multiple_of((taps - 1 - first - j) * step, ROW_TILE)
            term = lax.dot_general(
                extended_ref[pl.ds(start, rows), :],
                weight_ref[j],
                (((1,), (1,)), ((), ())),
                preferred_element_type=jnp.float32,
            )
            total = term if total is None else total + term

        @pl.when(pl.program_id(0) == 0)
        def _():
            total_ref[...] = total

        @pl.when(pl.program_id(0) > 0)
        def _():
            total_ref[...] += total

        @pl.when(pl.program_id(0) == steps - 1)
        def _():
            out_ref[...] = (upstream_ref[...] + wide(low(total_ref[...]))).astype(kind)

    whole = pl.BlockSpec((rows, inner), lambda g: (0, 0))
    found = pl.pallas_call(
        kernel,
        grid=(steps,),
        in_specs=[
            pl.BlockSpec(extended.shape, lambda g: (0, 0)),
            pl.BlockSpec((group, inner, width), lambda g: (g, 0, 0)),
            whole,
        ]
        + tokens(after),
        out_specs=(whole, TOKEN_SPEC),
        out_shape=(jax.ShapeDtypeStruct((rows, inner), kind), TOKEN),
        scratch_shapes=[pltpu.VMEM((rows, inner), jnp.float32)],
        compiler_params=pltpu.CompilerParams(vmem_limit_bytes=VMEM_BYTES),
        cost_estimate=cost(6),
        name="conv_data_grad",
    )(extended, weight, upstream, *after)
    return found[0], (found[1],)


def hold(arrays, after, reads=()):
    count = len(arrays)
    if count == 0:
        return [], after

    def kernel(*refs):
        refs[-1][...] = jnp.zeros(TOKEN.shape, TOKEN.dtype)

    found = pl.pallas_call(
        kernel,
        in_specs=[ANYWHERE] * (count + len(reads)) + [WHOLE] * len(after),
        out_specs=[ANYWHERE] * count + [WHOLE],
        out_shape=[jax.ShapeDtypeStruct(each.shape, each.dtype) for each in arrays] + [TOKEN],
        input_output_aliases={i: i for i in range(count)},
        cost_estimate=cost(0.5),
        name="hold",
    )(*arrays, *reads, *after)
    return list(found[:-1]), (found[-1],)


def join_rows(parts, after=(), reads=()):
    def kernel(*refs):
        out_ref, token_ref = refs[-2:]
        token_ref[...] = jnp.zeros(TOKEN.shape, TOKEN.dtype)
        first = 0
        for i, part in enumerate(parts):
            out_ref[first : first + part.shape[0]] = refs[i][...]
            first += part.shape[0]

    shape = (sum(part.shape[0] for part in parts), parts[0].shape[1])
    found = pl.pallas_call(
        kernel,
        in_specs=[WHOLE] * len(parts) + [ANYWHERE] * len(reads) + [WHOLE] * len(after),
        out_specs=[WHOLE] * 2,
        out_shape=[jax.ShapeDtypeStruct(shape, parts[0].dtype), TOKEN],
        compiler_params=pltpu.CompilerParams(vmem_limit_bytes=VMEM_BYTES),
        cost_estimate=cost(1.5),
        name="join_rows",
    )(*parts, *reads, *after)
    return found[0], (found[1],)


def restack(groups, reads=(), after=(), turn=None):
    flat = [array for arrays, _ in groups for array in arrays]
    cuts = [cut for _, each in groups for cut in each]

    def kernel(place_ref, *refs):
        token_ref = refs[-1]
        token_ref[...] = jnp.zeros(TOKEN.shape, TOKEN.dtype)
        out_refs = refs[-1 - len(cuts) : -1]
        at_in, at_out = 0, 0
        for arrays, each in groups:
            slots = len(arrays) if turn is None else arrays[0].shape[0]
            for first, last, shape in each:
                for slot in range(slots):
                    if turn is None:
                        value = refs[at_in + slot][...]
                    else:
                        value = refs[at_in][lax.rem(place_ref[0] - slot + slots, slots)]
                    if last is not None:
                        value = value[first:last]
                    out_refs[at_out][slot] = value.reshape(shape)
                at_out += 1
            at_in += len(arrays)

    shapes = [
        jax.ShapeDtypeStruct(
            ((len(arrays) if turn is None else arrays[0].shape[0]),) + shape, arrays[0].dtype
        )
        for arrays, each in groups
        for _, _, shape in each
    ]
    found = pl.pallas_call(
        kernel,
        in_specs=[SCALARS]
        + [WHOLE] * len(flat)
        + [ANYWHERE] * len(reads)
        + [WHOLE] * len(after),
        out_specs=[WHOLE] * (len(shapes) + 1),
        out_shape=shapes + [TOKEN],
        compiler_params=pltpu.CompilerParams(vmem_limit_bytes=VMEM_BYTES),
        cost_estimate=cost(1.5),
        name="restack",
    )(jnp.zeros((1,), jnp.int32) + (0 if turn is None else turn), *flat, *reads, *after)
    return found[:-1], (found[-1],)


def conv_weight_grad(
    extendeds, upstream, arrived, places, sizes, taps, step, after=(), reads=()
):
    cores, seqs, acrosses, tap_peers = sizes
    rows = upstream.shape[0]
    inner = extendeds[0].shape[1]
    lanes = upstream.shape[1] // cores
    slab = inner // (seqs * acrosses * tap_peers)
    direct = slab % ROW_TILE == 0
    half = (tap_peers + 1) // 2
    rest = tap_peers - half
    seconds = acrosses if rest else 0
    outs = seqs + seconds if direct else 1

    def kernel(place_ref, *refs):
        out_refs, token_ref = refs[-1 - outs : -1], refs[-1]
        token_ref[...] = jnp.zeros(TOKEN.shape, TOKEN.dtype)
        start = pl.multiple_of(pl.program_id(0) * step, ROW_TILE)
        found = low(
            sum(
                lax.dot_general(
                    refs[c][pl.ds(start, rows), :],
                    refs[cores + c][...],
                    (((0,), (0,)), ((), ())),
                    preferred_element_type=jnp.float32,
                )
                for c in range(cores)
            )
        )
        if not direct:
            out_refs[0][0] = found
            return
        for t in range(tap_peers):
            slot_t = lax.rem(place_ref[3] - t + tap_peers, tap_peers)
            early = jnp.minimum(slot_t, half - 1)
            late = jnp.maximum(slot_t - half, 0)
            for s in range(seqs):
                slot_s = lax.rem(place_ref[1] - s + seqs, seqs)
                for a in range(acrosses):
                    slot_a = lax.rem(place_ref[2] - a + acrosses, acrosses)
                    base = ((t * seqs + s) * acrosses + a) * slab
                    piece = found[base : base + slab]
                    for slot in range(seqs):

                        @pl.when(jnp.logical_and(slot_s == slot, slot_t < half))
                        def _(slot=slot, slot_a=slot_a, early=early, piece=piece):
                            out_refs[slot][slot_a, early, 0] = piece

                    for slot in range(seconds):

                        @pl.when(jnp.logical_and(slot_a == slot, slot_t >= half))
                        def _(slot=slot, slot_s=slot_s, late=late, piece=piece):
                            out_refs[seqs + slot][slot_s, late, 0] = piece

    if direct:
        shapes = [(acrosses, half, taps, slab, lanes)] * seqs
        shapes += [(seqs, rest, taps, slab, lanes)] * seconds
        specs = [
            pl.BlockSpec(shape[:2] + (1, slab, lanes), lambda k, place: (0, 0, k, 0, 0))
            for shape in shapes
        ]
    else:
        shapes = [(taps, inner, lanes)]
        specs = [pl.BlockSpec((1, inner, lanes), lambda k, place: (k, 0, 0))]
    found = pl.pallas_call(
        kernel,
        grid_spec=pltpu.PrefetchScalarGridSpec(
            num_scalar_prefetch=1,
            grid=(taps,),
            in_specs=[pl.BlockSpec(extendeds[0].shape, lambda k, place: (0, 0))] * cores
            + [pl.BlockSpec((rows, lanes), lambda k, place: (0, place[0]))]
            + [pl.BlockSpec((rows, lanes), lambda k, place: (0, 0))] * (cores - 1)
            + tokens(after)
            + [ANYWHERE] * len(reads),
            out_specs=specs + [TOKEN_SPEC],
        ),
        out_shape=[jax.ShapeDtypeStruct(shape, jnp.bfloat16) for shape in shapes] + [TOKEN],
        compiler_params=pltpu.CompilerParams(vmem_limit_bytes=VMEM_BYTES),
        cost_estimate=cost(9),
        name="conv_weight_grad",
    )(jnp.stack(places).astype(jnp.int32), *extendeds, upstream, *arrived, *after, *reads)
    token = found[-1]
    if not direct:
        found = found[0].reshape(taps, tap_peers, seqs, acrosses, slab, lanes)
        for axis, which in ((1, 3), (2, 1), (3, 2)):
            found = relative(found, axis, places[which], sizes[which])
        found = found.transpose(2, 3, 1, 0, 4, 5)
        found = [found[s, :, :half] for s in range(seqs)] + [
            found[:, a, half:] for a in range(seconds)
        ]
    flat = [each.reshape(-1, lanes) for each in found[: seqs + seconds]]
    return flat[:seqs], flat[seqs:], token


def ffn_weight_grad(pairs, sizes, ffn_rows, after=()):
    cores, seqs, acrosses, tap_peers = sizes
    rows, width = pairs[0][1].shape
    block = tap_peers * ffn_rows
    half = (tap_peers + 1) // 2
    rest = tap_peers - half
    seconds = seqs if rest else 0
    transposed = (((0,), (0,)), ((), ()))
    if ffn_rows % ROW_TILE:
        found = jnp.stack(
            [
                low(
                    sum(
                        lax.dot_general(a, b, transposed, preferred_element_type=jnp.float32)
                        for a, b in [(left, right)]
                        + [(ends[:, width:], starts[:, :width]) for ends, starts in packets]
                    )
                ).reshape(acrosses, seqs, tap_peers, ffn_rows, width)
                for left, right, packets in pairs
            ],
            3,
        )
        token = jnp.zeros(TOKEN.shape, TOKEN.dtype)
        return (
            [found[a, :, :half].reshape(-1, width) for a in range(acrosses)],
            [found[:, s, half:].reshape(-1, width) for s in range(seconds)],
            token,
        )
    outs = acrosses + seconds

    def kernel(*refs):
        out_refs, token_ref = refs[-1 - outs : -1], refs[-1]
        token_ref[...] = jnp.zeros(TOKEN.shape, TOKEN.dtype)
        step = pl.program_id(0)
        for which in range(2):
            base = 2 * cores * which
            found = low(
                sum(
                    lax.dot_general(
                        refs[base + 2 * c][...],
                        refs[base + 2 * c + 1][...],
                        transposed,
                        preferred_element_type=jnp.float32,
                    )
                    for c in range(cores)
                )
            ).reshape(tap_peers, ffn_rows, width)
            for a in range(acrosses):

                @pl.when(step // seqs == a)
                def _(a=a):
                    out_refs[a][0, :, which] = found[:half]

            for s in range(seconds):

                @pl.when(lax.rem(step, seqs) == s)
                def _(s=s):
                    out_refs[acrosses + s][0, :, which] = found[half:]

    right_spec = pl.BlockSpec((rows, width), lambda g: (0, 0))
    left_spec = pl.BlockSpec((rows, block), lambda g: (0, g))
    late_spec = pl.BlockSpec((rows, block), lambda g: (0, width // block + g))

    def first_spec(a):
        return pl.BlockSpec(
            (1, half, 2, ffn_rows, width),
            lambda g: (jnp.clip(g - a * seqs, 0, seqs - 1), 0, 0, 0, 0),
        )

    second_spec = pl.BlockSpec(
        (1, rest, 2, ffn_rows, width), lambda g: (g // seqs, 0, 0, 0, 0)
    )
    operands = []
    for left, right, packets in pairs:
        operands += [left, right]
        for ends, starts in packets:
            operands += [ends, starts]
    found = pl.pallas_call(
        kernel,
        grid=(acrosses * seqs,),
        in_specs=([left_spec, right_spec] + [late_spec, right_spec] * (cores - 1)) * 2
        + tokens(after),
        out_specs=[first_spec(a) for a in range(acrosses)]
        + [second_spec] * seconds
        + [TOKEN_SPEC],
        out_shape=[jax.ShapeDtypeStruct((seqs, half, 2, ffn_rows, width), jnp.bfloat16)] * acrosses
        + [jax.ShapeDtypeStruct((acrosses, rest, 2, ffn_rows, width), jnp.bfloat16)] * seconds
        + [TOKEN],
        compiler_params=pltpu.CompilerParams(vmem_limit_bytes=VMEM_BYTES),
        cost_estimate=cost(8),
        name="ffn_weight_grad",
    )(*operands, *after)
    flat = [each.reshape(-1, width) for each in found[:-1]]
    return flat[:acrosses], flat[acrosses:], found[-1]


def group_slots(groups, lanes):
    flat, where = [], []
    rows = groups[0][0][0].size // (groups[0][1] * lanes)
    for parts, slots in groups:
        where += [(len(flat), len(parts), slot) for slot in range(slots)]
        flat += [part.reshape(slots, rows, lanes) for part in parts]
    return flat, where, rows


def slot_sum(refs, place, first=0):
    start, count, at = place
    return low(sum(wide(refs[first + start + i][at]) for i in range(count)))


def merge_slots(conv_groups, ffn_groups, after=()):
    lanes, width = conv_groups[0][0][0].shape[-1], ffn_groups[0][0][0].shape[-1]
    cuts = width // lanes
    conv_parts, conv_where, conv_rows = group_slots(conv_groups, lanes)
    ffn_parts, ffn_where, ffn_rows = group_slots(ffn_groups, width)
    slots = len(conv_where)
    if conv_rows % ROW_TILE or ffn_rows % ROW_TILE:
        merged = []
        for slot in range(slots):
            ffn = slot_sum(ffn_parts, ffn_where[slot])
            merged.append(
                jnp.concatenate(
                    [slot_sum(conv_parts, conv_where[slot])]
                    + [ffn[:, i * lanes : (i + 1) * lanes] for i in range(cuts)]
                )
            )
        return merged, after

    def kernel(*refs):
        out_refs, token_ref = refs[-1 - slots : -1], refs[-1]
        token_ref[...] = jnp.zeros(TOKEN.shape, TOKEN.dtype)
        for slot in range(slots):
            out_refs[slot][:conv_rows] = slot_sum(refs, conv_where[slot])
            ffn = slot_sum(refs, ffn_where[slot], len(conv_parts))
            for i in range(cuts):
                first = conv_rows + i * ffn_rows
                out_refs[slot][first : first + ffn_rows] = ffn[:, i * lanes : (i + 1) * lanes]

    found = pl.pallas_call(
        kernel,
        in_specs=[WHOLE] * (len(conv_parts) + len(ffn_parts) + len(after)),
        out_specs=[WHOLE] * (slots + 1),
        out_shape=[jax.ShapeDtypeStruct((conv_rows + cuts * ffn_rows, lanes), jnp.bfloat16)] * slots
        + [TOKEN],
        compiler_params=pltpu.CompilerParams(vmem_limit_bytes=VMEM_BYTES),
        cost_estimate=cost(1.5),
        name="merge_slots",
    )(*conv_parts, *ffn_parts, *after)
    return found[:slots], (found[slots],)


def append_slots(groups, packed, after=(), reads=()):
    lanes = groups[0][0][0].shape[-1]
    parts, where, rows = group_slots(groups, lanes)
    slots = len(where)
    if rows % ROW_TILE:
        return [
            jnp.concatenate([slot_sum(parts, where[slot])] + packed) for slot in range(slots)
        ], after

    def kernel(*refs):
        out_refs, token_ref = refs[-1 - slots : -1], refs[-1]
        token_ref[...] = jnp.zeros(TOKEN.shape, TOKEN.dtype)
        for slot in range(slots):
            out_refs[slot][:rows] = slot_sum(refs, where[slot])
            if packed:
                out_refs[slot][rows:] = refs[len(parts)][...]

    shape = jax.ShapeDtypeStruct((rows + sum(each.shape[0] for each in packed), lanes), jnp.bfloat16)
    found = pl.pallas_call(
        kernel,
        in_specs=[WHOLE] * (len(packed) + len(parts) + len(after)) + [ANYWHERE] * len(reads),
        out_specs=[WHOLE] * (slots + 1),
        out_shape=[shape] * slots + [TOKEN],
        compiler_params=pltpu.CompilerParams(vmem_limit_bytes=VMEM_BYTES),
        cost_estimate=cost(1),
        name="append_slots",
    )(*parts, *packed, *after, *reads)
    return found[:slots], (found[slots],)


def pack_small(row_groups, biases, losses, places, sizes, ffn_rows, after=()):
    cores, seqs, acrosses, tap_peers = sizes
    width = row_groups[0][0].shape[1]
    head_rows = sum(count for _, count in row_groups)
    hidden = cores * biases[0][0].shape[1]
    bias_rows = hidden // width
    used = head_rows + len(biases) * bias_rows + 2
    rows = -(-used // ROW_TILE) * ROW_TILE
    lanes = width // 2
    per_row = width // ffn_rows
    if ffn_rows % 64:
        terms = jnp.stack([losses[0, 0], losses[1, 0]])
        terms = jnp.stack([terms, terms - wide(low(terms))])
        pieces = [array[:count] for array, count in row_groups]
        for each in biases:
            bias = jnp.stack(each).reshape(cores, acrosses, seqs, tap_peers, ffn_rows)
            for axis, which in enumerate((0, 2, 1, 3)):
                bias = relative(bias, axis, places[which], sizes[which])
            pieces.append(bias.transpose(1, 0, 2, 3, 4).reshape(-1, width))
        pieces.append(jnp.pad(terms, ((0, rows - used), (0, width - 2))))
        packed = low(jnp.concatenate(pieces))
        return jnp.concatenate([packed[:, :lanes], packed[:, lanes:]]), after

    def kernel(place_ref, *refs):
        packed_ref, token_ref, rows_ref = refs[-3:]
        token_ref[...] = jnp.zeros(TOKEN.shape, TOKEN.dtype)
        rows_ref[...] = jnp.zeros(rows_ref.shape, jnp.float32)
        at = 0
        for i, (_, count) in enumerate(row_groups):
            rows_ref[at : at + count, :] = refs[i][:count, :]
            at += count
        shape = (cores, acrosses, seqs, tap_peers)
        owners = (0, 2, 1, 3)
        for b in range(len(biases)):
            blocks = {}
            for slot in np.ndindex(*shape):
                first = ((slot[1] * seqs + slot[2]) * tap_peers + slot[3]) * ffn_rows
                ref = refs[len(row_groups) + b * cores + slot[0]]
                blocks[slot] = ref[:, first : first + ffn_rows]
            for axis, size in enumerate(shape):
                turned = {}
                for slot in blocks:
                    place = lax.rem(place_ref[owners[axis]] - slot[axis] + size, size)
                    value = blocks[slot[:axis] + (0,) + slot[axis + 1 :]]
                    for other in range(1, size):
                        candidate = blocks[slot[:axis] + (other,) + slot[axis + 1 :]]
                        value = jnp.where(place == other, candidate, value)
                    turned[slot] = value
                blocks = turned
            ordered = [
                blocks[(c, a, s, t)]
                for a in range(acrosses)
                for c in range(cores)
                for s in range(seqs)
                for t in range(tap_peers)
            ]
            for row in range(bias_rows):
                line = ordered[row * per_row : (row + 1) * per_row]
                rows_ref[at : at + 1, :] = jnp.concatenate(line, 1)
                at += 1
        losses_ref = refs[len(row_groups) + len(biases) * cores]
        lane = lax.broadcasted_iota(jnp.int32, (1, width), 1)
        objective = jnp.broadcast_to(losses_ref[0:1, 0:1], (1, width))
        scored = jnp.broadcast_to(losses_ref[1:2, 0:1], (1, width))
        line = jnp.where(lane == 0, objective, jnp.where(lane == 1, scored, 0.0))
        rows_ref[at : at + 1, :] = line
        rows_ref[at + 1 : at + 2, :] = line - wide(low(line))
        packed_ref[:rows, :] = low(rows_ref[:, :lanes])
        packed_ref[rows:, :] = low(rows_ref[:, lanes:])

    flat = [array for array, _ in row_groups] + [each for some in biases for each in some]
    found = pl.pallas_call(
        kernel,
        in_specs=[SCALARS] + [WHOLE] * (len(flat) + 1 + len(after)),
        out_specs=[WHOLE] * 2,
        out_shape=[jax.ShapeDtypeStruct((2 * rows, lanes), jnp.bfloat16), TOKEN],
        scratch_shapes=[pltpu.VMEM((rows, width), jnp.float32)],
        compiler_params=pltpu.CompilerParams(vmem_limit_bytes=VMEM_BYTES),
        cost_estimate=cost(2),
        name="pack_small",
    )(jnp.stack(places).astype(jnp.int32), *flat, losses, *after)
    return found[0], (found[1],)


def paired(values):
    while len(values) > 1:
        half = len(values) // 2
        if len(values) % 2:
            return sum(values[1:], values[0])
        values = [values[i] + values[i + half] for i in range(half)]
    return values[0]


def small_total(stacks, places, sizes):
    cores, seqs, acrosses = sizes[:3]
    full = jnp.stack([wide(each).reshape((seqs, acrosses) + each.shape[1:]) for each in stacks])
    if max(cores, seqs, acrosses) > 2:
        for axis, (place, size) in enumerate(zip(places[:3], sizes[:3])):
            full = relative(full, axis, place, size)
        return jnp.sum(full, (0, 1, 2))
    return paired(
        [
            paired([paired([full[c, s, a] for a in range(acrosses)]) for s in range(seqs)])
            for c in range(cores)
        ]
    )


def finish_conv(parts, conv_rows, small_rows, after=()):
    blocks, count = len(parts), len(parts[0])
    lanes = parts[0][0].shape[-1]
    flat = [part for block in parts for part in block]
    if conv_rows % ROW_TILE:
        sums = [sum(wide(part[:conv_rows]) for part in block) for block in parts]
        sums.append(paired([wide(part[conv_rows:]) for part in parts[0]]))
        return jnp.concatenate([low(total) for total in sums]), after

    def kernel(*refs):
        shard_ref, token_ref = refs[-2:]
        token_ref[...] = jnp.zeros(TOKEN.shape, TOKEN.dtype)
        shard_ref[blocks * conv_rows :] = low(
            paired([wide(refs[i][conv_rows:]) for i in range(count)])
        )
        for b in range(blocks):
            total = sum(wide(refs[b * count + i][:conv_rows]) for i in range(count))
            shard_ref[b * conv_rows : (b + 1) * conv_rows] = low(total)

    found = pl.pallas_call(
        kernel,
        in_specs=[WHOLE] * (len(flat) + len(after)),
        out_specs=[WHOLE] * 2,
        out_shape=[
            jax.ShapeDtypeStruct((blocks * conv_rows + small_rows, lanes), jnp.bfloat16),
            TOKEN,
        ],
        compiler_params=pltpu.CompilerParams(vmem_limit_bytes=VMEM_BYTES),
        cost_estimate=cost(1.2),
        name="finish_conv",
    )(*flat, *after)
    return found[0], (found[1],)


def finish_ffn(merged, plain, conv_rows, ffn_rows, after=()):
    lanes, width = merged[0].shape[-1], plain[0].shape[-1]

    def cut_back(total):
        size = 2 * ffn_rows
        return jnp.concatenate(
            [total[i * size : (i + 1) * size] for i in range(width // lanes)], 1
        )

    if conv_rows % ROW_TILE or ffn_rows % ROW_TILE:
        sums = [sum(wide(part) for part in plain)]
        sums.append(cut_back(sum(wide(part[conv_rows:]) for part in merged)))
        return jnp.stack([each[:ffn_rows].T for each in sums]), jnp.stack(
            [each[ffn_rows:] for each in sums]
        ), after

    def kernel(*refs):
        in_ref, out_ref, token_ref = refs[-3:]
        token_ref[...] = jnp.zeros(TOKEN.shape, TOKEN.dtype)
        late = sum(wide(refs[i][conv_rows:]) for i in range(len(merged)))
        sums = [sum(wide(refs[len(merged) + i][...]) for i in range(len(plain))), cut_back(late)]
        for b in range(2):
            in_ref[b] = sums[b][:ffn_rows].T
            out_ref[b] = sums[b][ffn_rows:]

    found = pl.pallas_call(
        kernel,
        in_specs=[WHOLE] * (len(merged) + len(plain) + len(after)),
        out_specs=[WHOLE] * 3,
        out_shape=(
            jax.ShapeDtypeStruct((2, width, ffn_rows), jnp.float32),
            jax.ShapeDtypeStruct((2, ffn_rows, width), jnp.float32),
            TOKEN,
        ),
        compiler_params=pltpu.CompilerParams(vmem_limit_bytes=VMEM_BYTES),
        cost_estimate=cost(1),
        name="finish_ffn",
    )(*merged, *plain, *after)
    return found[0], found[1], (found[2],)


def add_slots(parts, slots, after=(), reads=()):
    lanes = parts[0].shape[-1]
    rows = parts[0].size // (slots * lanes)
    parts = [part.reshape(slots, rows, lanes) for part in parts]
    block = rows // 4 if rows % (4 * ROW_TILE) == 0 else rows

    def kernel(*refs):
        out_refs, token_ref = refs[-1 - slots : -1], refs[-1]
        token_ref[...] = jnp.zeros(TOKEN.shape, TOKEN.dtype)
        for slot in range(slots):
            out_refs[slot][...] = low(sum(wide(refs[i][slot]) for i in range(len(parts))))

    found = pl.pallas_call(
        kernel,
        grid=(rows // block,),
        in_specs=[pl.BlockSpec((slots, block, lanes), lambda g: (0, g, 0))] * len(parts)
        + tokens(after)
        + [ANYWHERE] * len(reads),
        out_specs=[pl.BlockSpec((block, lanes), lambda g: (g, 0))] * slots + [TOKEN_SPEC],
        out_shape=[jax.ShapeDtypeStruct((rows, lanes), jnp.bfloat16)] * slots + [TOKEN],
        compiler_params=pltpu.CompilerParams(vmem_limit_bytes=VMEM_BYTES),
        cost_estimate=cost(2),
        name="add_slots",
    )(*parts, *after, *reads)
    return found[:slots], found[slots]


def place_conv_grads(stacks, places, sizes):
    cores, seqs, acrosses = sizes[:3]
    blocks, taps, slab, lanes = stacks[0].shape[1:]
    channels = slab * seqs * acrosses
    if slab % ROW_TILE:
        full = jnp.stack([each.reshape((seqs, acrosses) + each.shape[1:]) for each in stacks])
        for axis, (place, size) in enumerate(zip(places[:3], sizes[:3])):
            full = relative(full, axis, place, size)
        return wide(
            full.transpose(3, 4, 1, 2, 5, 0, 6).reshape(blocks, taps, channels, cores * lanes)
        )

    def kernel(place_ref, *refs):
        out_ref = refs[-1]
        for c in range(cores):
            lane = pl.multiple_of(lax.rem(place_ref[0] - c + cores, cores) * lanes, lanes)
            for s in range(seqs):
                at_s = lax.rem(place_ref[1] - s + seqs, seqs)
                for a in range(acrosses):
                    at_a = lax.rem(place_ref[2] - a + acrosses, acrosses)
                    row = pl.multiple_of((at_s * acrosses + at_a) * slab, slab)
                    for b in range(blocks):
                        piece = wide(refs[c][s * acrosses + a, b, 0])
                        out_ref[b, 0, pl.ds(row, slab), pl.ds(lane, lanes)] = piece

    return pl.pallas_call(
        kernel,
        grid_spec=pltpu.PrefetchScalarGridSpec(
            num_scalar_prefetch=1,
            grid=(taps,),
            in_specs=[
                pl.BlockSpec(
                    (seqs * acrosses, blocks, 1, slab, lanes), lambda k, place: (0, 0, k, 0, 0)
                )
            ]
            * cores,
            out_specs=pl.BlockSpec(
                (blocks, 1, channels, cores * lanes), lambda k, place: (0, k, 0, 0)
            ),
        ),
        out_shape=jax.ShapeDtypeStruct((blocks, taps, channels, cores * lanes), jnp.float32),
        compiler_params=pltpu.CompilerParams(vmem_limit_bytes=VMEM_BYTES),
        cost_estimate=cost(5),
        name="place_conv_grads",
    )(jnp.stack(places[:3]).astype(jnp.int32), *stacks)


def copy_all(copies):
    for copy in copies:
        copy.start()
    for copy in copies:
        copy.wait()


def place_conv(pieces, places, sizes, after=(), reads=()):
    cores, seqs, acrosses, tap_peers = sizes
    taps, slab, lanes = pieces[0][0].shape[2:]
    inner = slab * seqs * acrosses * tap_peers
    if slab % ROW_TILE:
        full = jnp.stack([jnp.stack(row) for row in pieces])
        for axis, (place, size) in enumerate(zip(places, sizes)):
            full = relative(full, axis, place, size)
        return full.transpose(4, 3, 1, 2, 5, 0, 6).reshape(taps, inner, cores * lanes), after
    flat = [piece for row in pieces for piece in row]

    def kernel(place_ref, *refs):
        out_ref, token_ref, sem_ref = refs[-3:]
        token_ref[...] = jnp.zeros(TOKEN.shape, TOKEN.dtype)
        copies = []
        for c in range(cores):
            lane = lax.rem(place_ref[0] - c + cores, cores) * lanes
            for s in range(seqs):
                at_s = lax.rem(place_ref[1] - s + seqs, seqs)
                for a in range(acrosses):
                    at_a = lax.rem(place_ref[2] - a + acrosses, acrosses)
                    for t in range(tap_peers):
                        at_t = lax.rem(place_ref[3] - t + tap_peers, tap_peers)
                        row = ((at_t * seqs + at_s) * acrosses + at_a) * slab
                        copies.append(
                            pltpu.make_async_copy(
                                refs[c * seqs + s].at[a, t],
                                out_ref.at[
                                    :,
                                    pl.ds(pl.multiple_of(row, slab), slab),
                                    pl.ds(pl.multiple_of(lane, lanes), lanes),
                                ],
                                sem_ref.at[len(copies)],
                            )
                        )
        copy_all(copies)

    found = pl.pallas_call(
        kernel,
        in_specs=[SCALARS] + [ANYWHERE] * (len(flat) + len(reads)) + [WHOLE] * len(after),
        out_specs=[WHOLE] * 2,
        out_shape=[jax.ShapeDtypeStruct((taps, inner, cores * lanes), jnp.bfloat16), TOKEN],
        scratch_shapes=[pltpu.SemaphoreType.DMA((cores * seqs * acrosses * tap_peers,))],
        compiler_params=pltpu.CompilerParams(vmem_limit_bytes=VMEM_BYTES),
        cost_estimate=cost(3),
        name="place_conv",
    )(jnp.stack(places).astype(jnp.int32), *flat, *reads, *after)
    return found[0], (found[1],)


def place_ffn(pieces, sizes, after=(), reads=()):
    cores, seqs, acrosses, tap_peers = sizes
    cuts, ffn_rows, lanes = pieces[0][0].shape[2:]
    cuts //= 2
    width = cuts * lanes
    units = seqs * acrosses * tap_peers * ffn_rows
    if ffn_rows % ROW_TILE:
        full = jnp.stack([jnp.stack(row) for row in pieces])
        full = full.reshape(cores, acrosses, seqs, tap_peers, 2, cuts, ffn_rows, lanes)
        full = full.transpose(4, 0, 1, 2, 3, 6, 5, 7).reshape(2, cores, units, width)
        return [full[0, c] for c in range(cores)], [full[1, c] for c in range(cores)], after
    flat = [piece for row in pieces for piece in row]

    def kernel(*refs):
        out_refs = refs[-2 - 2 * cores : -2]
        token_ref, sem_ref = refs[-2:]
        token_ref[...] = jnp.zeros(TOKEN.shape, TOKEN.dtype)
        copies = []
        for c in range(cores):
            for a in range(acrosses):
                for which in range(2):
                    for cut in range(cuts):
                        copies.append(
                            pltpu.make_async_copy(
                                refs[c * acrosses + a].at[:, :, which * cuts + cut],
                                out_refs[which * cores + c].at[
                                    a, :, :, :, pl.ds(cut * lanes, lanes)
                                ],
                                sem_ref.at[len(copies)],
                            )
                        )
        copy_all(copies)

    shape = jax.ShapeDtypeStruct((acrosses, seqs, tap_peers, ffn_rows, width), jnp.bfloat16)
    found = pl.pallas_call(
        kernel,
        in_specs=[ANYWHERE] * (len(flat) + len(reads)) + [WHOLE] * len(after),
        out_specs=[WHOLE] * (2 * cores + 1),
        out_shape=[shape] * (2 * cores) + [TOKEN],
        scratch_shapes=[pltpu.SemaphoreType.DMA((2 * cores * acrosses * cuts,))],
        compiler_params=pltpu.CompilerParams(vmem_limit_bytes=VMEM_BYTES),
        cost_estimate=cost(2),
        name="place_ffn",
    )(*flat, *reads, *after)
    token = found[-1]
    found = [each.reshape(units, width) for each in found[:-1]]
    return found[:cores], found[cores:], (token,)


class Ring:
    def __init__(self, axis, size, index, pairs):
        self.axis, self.size, self.index, self.pairs = axis, size, index, pairs

    def shifted(self, value, by):
        return lax.ppermute(value, self.axis, self.pairs(lambda i: (i + by) % self.size))

    def swapped(self, value, bit):
        return lax.ppermute(value, self.axis, self.pairs(lambda i: i ^ bit))

    def gather(self, value):
        return [value] + [self.shifted(value, by) for by in range(1, self.size)]

    def swap(self, values):
        return [values[0]] + [self.shifted(values[by], -by) for by in range(1, self.size)]


def relative(value, axis, place, size):
    if size == 1:
        return value
    return jnp.stack(
        [
            lax.dynamic_index_in_dim(value, (place - slot) % size, axis, False)
            for slot in range(size)
        ],
        axis,
    )


def rings():
    peers = lax.axis_size("dp")
    cores = CORES if peers % CORES == 0 else 1
    columns = peers // cores
    place = lax.axis_index("dp")

    def plain(axis):
        size = lax.axis_size(axis)
        return Ring(
            axis, size, lax.axis_index(axis), lambda move: [(i, move(i)) for i in range(size)]
        )

    across = Ring(
        "dp",
        columns,
        place // cores,
        lambda move: [(i, move(i // cores) * cores + i % cores) for i in range(peers)],
    )
    core = Ring(
        "dp",
        cores,
        place % cores,
        lambda move: [(i, i // cores * cores + move(i % cores)) for i in range(peers)],
    )
    return core, across, plain("seq"), plain("tap")


class Reduce:
    def __init__(self, terms, order):
        self.order = order
        self.parts = [terms[0]] + [order[0].shifted(terms[s], -s) for s in range(1, order[0].size)]

    def step(self, level, after, reads=()):
        ring = self.order[level]
        found, token = add_slots(self.parts, ring.size, after, reads)
        self.parts = [found[0]] + [ring.shifted(found[s], -s) for s in range(1, ring.size)]
        return (token,)


def shared_copies(value, across, seq):
    peers, spans = lax.axis_size("dp"), lax.axis_size("seq")
    cores = peers // across.size

    def target(place, by_a, by_s):
        dp, at = place // spans, place % spans
        moved = (dp // cores + by_a) % across.size * cores + dp % cores
        return moved * spans + (at + by_s) % spans

    return [
        [
            value
            if by_a == by_s == 0
            else lax.ppermute(
                value,
                ("dp", "seq"),
                [(place, target(place, by_a, by_s)) for place in range(peers * spans)],
            )
            for by_a in range(across.size)
        ]
        for by_s in range(seq.size)
    ]


def passed_along(value, axis, by):
    peers = lax.axis_size(axis)
    pairs = [(i, i + by) for i in range(peers) if 0 <= i + by < peers]
    return lax.ppermute(value, axis, pairs)


def rims(source, reach_rows, seq):
    span_rows = source.shape[0]
    if seq.size == 2 and reach_rows <= span_rows:
        first = (1 - seq.index) * (span_rows - reach_rows)
        return seq.shifted(lax.dynamic_slice_in_dim(source, first, reach_rows, 0), 1)
    left_parts = []
    right_parts = []
    distances = -(-reach_rows // span_rows)
    for distance in range(1, distances + 1):
        rim_count = min(span_rows, reach_rows - (distance - 1) * span_rows)
        left_parts.insert(0, passed_along(source[span_rows - rim_count :], "seq", distance))
        right_parts.append(passed_along(source[:rim_count], "seq", -distance))
    return left_parts, right_parts


def extend(source, found, seq, after=()):
    if isinstance(found, tuple):
        return join_rows(found[0] + [source] + found[1], after)
    reach, span = found.shape[0], source.shape[0]

    def kernel(place_ref, found_ref, source_ref, *refs):
        out_ref, token_ref = refs[-2:]
        token_ref[...] = jnp.zeros(TOKEN.shape, TOKEN.dtype)
        out_ref[reach : reach + span] = source_ref[...]
        zeros = jnp.zeros(found.shape, found.dtype)

        @pl.when(place_ref[0] == 0)
        def _():
            out_ref[:reach] = zeros
            out_ref[reach + span :] = found_ref[...]

        @pl.when(place_ref[0] != 0)
        def _():
            out_ref[:reach] = found_ref[...]
            out_ref[reach + span :] = zeros

    shape = jax.ShapeDtypeStruct((span + 2 * reach, source.shape[1]), source.dtype)
    extended, token = pl.pallas_call(
        kernel,
        in_specs=[SCALARS] + [WHOLE] * (2 + len(after)),
        out_specs=[WHOLE] * 2,
        out_shape=[shape, TOKEN],
        compiler_params=pltpu.CompilerParams(vmem_limit_bytes=VMEM_BYTES),
        cost_estimate=cost(1.5),
        name="extend",
    )(seq.index.astype(jnp.int32)[None], found, source, *after)
    return extended, (token,)


def to_rows(values):
    windows, positions = values.shape[:2]
    cut = values.reshape((windows, positions // FIRST_DILATION, FIRST_DILATION) + values.shape[2:])
    return jnp.swapaxes(cut, 0, 1).reshape((windows * positions,) + values.shape[2:])


def from_rows(values, windows):
    cut = values.reshape((-1, windows, FIRST_DILATION) + values.shape[1:])
    return jnp.swapaxes(cut, 0, 1).reshape((windows, -1) + values.shape[1:])


def on_device(
    inputs,
    targets,
    masked,
    conv_weight,
    conv_bias,
    gains,
    shifts,
    in_weight,
    in_bias,
    out_weight,
    out_bias,
    head_weight,
):
    core, across, seq, tap = rings()
    taps = conv_weight.shape[1]
    channels = conv_weight.shape[2]
    width = conv_weight.shape[3]
    slab = channels // (seq.size * across.size)
    lanes = width // core.size
    hidden_width = in_bias.shape[1]
    ffn_rows = in_weight.shape[2]
    windows = inputs.shape[0]
    rows = windows * inputs.shape[1]
    steps = (FIRST_DILATION * windows, SECOND_DILATION * windows)
    units = hidden_width // core.size
    places = (core.index, seq.index, across.index, tap.index)
    sizes = (core.size, seq.size, across.size, tap.size)

    in_bias_placed = []
    for b in range(2):
        bias = in_bias[b].reshape(across.size, core.size, seq.size, tap.size, ffn_rows)
        for axis, ring in enumerate((across, core, seq, tap)):
            bias = relative(bias, axis, ring.index, ring.size)
        in_bias_placed.append(bias.transpose(1, 0, 2, 3, 4).reshape(core.size, units))

    def cut_ffn(piece):
        return piece.reshape(ffn_rows, core.size, lanes).swapaxes(0, 1).reshape(-1, lanes)

    def bundle(b):
        conv_piece = lax.dynamic_slice(
            conv_weight[b],
            (0, (seq.index * across.size + across.index) * slab, core.index * lanes),
            (taps, slab, lanes),
        )
        pieces = [
            conv_piece.reshape(taps * slab, lanes),
            cut_ffn(in_weight[b].T),
            cut_ffn(out_weight[b]),
        ]
        return jnp.concatenate(pieces)

    cuts = (
        (0, taps * slab, (taps, slab, lanes)),
        (taps * slab, taps * slab + 2 * core.size * ffn_rows, (2 * core.size, ffn_rows, lanes)),
    )

    def straight(arrays):
        return (arrays, ((0, None, arrays[0].shape),))

    conv_input = to_rows(inputs)
    stream = conv_input
    codes = to_rows(targets + masked * head_weight.shape[1])
    codes = jnp.broadcast_to(codes[:, None], (rows, 128))

    tap_parts = tap.gather(bundle(0))
    (conv_part, ffn_part), last = restack([(tap_parts, cuts)], reads=[conv_input])
    split = (tap.size + 1) // 2
    (behind,), last = hold([bundle(1)], last)
    late_parts = tap.gather(behind)
    extended, last = extend(conv_input, rims(conv_input, taps // 2 * steps[0], seq), seq, last)
    extended_parts = [extended] + [core.shifted(extended, -c) for c in range(1, core.size)]
    conv_parts, ffn_parts = across.gather(conv_part), seq.gather(ffn_part)
    (conv_part, ffn_part), last = restack(
        [straight(conv_parts), straight(ffn_parts)],
        reads=[late_parts[by] for by in range(1, tap.size) if by != split],
        after=last,
    )
    conv_parts, ffn_parts = seq.gather(conv_part), across.gather(ffn_part)
    conv_slots = [core.gather(conv_part)]
    ffn_slots = [core.gather(ffn_part)]
    held, last = hold(
        conv_parts[1:] + ffn_parts[1:],
        last,
        conv_slots[0][1:] + ffn_slots[0][1:] + late_parts[1:],
    )
    conv_slots += [core.gather(each) for each in held[: seq.size - 1]]
    ffn_slots += [core.gather(each) for each in held[seq.size - 1 :]]
    (late_conv, late_ffn), last = restack([(late_parts, cuts)], after=last)
    late_conv_parts, late_ffn_parts = across.gather(late_conv), seq.gather(late_ffn)

    def turned(slots):
        return [[each[c] for each in slots] for c in range(core.size)]

    conv_full, in_full, out_full = [None, None], [None, None], [None, None]
    conv_full[0], last = place_conv(
        turned(conv_slots), places, sizes, last, [part for each in ffn_slots for part in each[1:]]
    )
    saved = []
    reads = []
    for b in range(2):
        if b == 1:
            found = rims(conv_input, taps // 2 * steps[1], seq)
            held, last = hold(late_conv_parts[1:] + late_ffn_parts[1:], last)
            late_conv_slots += [core.gather(each) for each in held[: seq.size - 1]]
            late_ffn_slots += [core.gather(each) for each in held[seq.size - 1 :]]
            conv_full[1], last = place_conv(turned(late_conv_slots), places, sizes, last)
            in_full[1], out_full[1], last = place_ffn(turned(late_ffn_slots), sizes, last)
            extended, last = extend(conv_input, found, seq, last)
            extended_parts = [extended] + [core.shifted(extended, -c) for c in range(1, core.size)]
        (normed_conv, conv_slope, stream, lowered), last = conv_forward(
            extended,
            conv_full[b],
            stream,
            conv_bias[b],
            gains[b, 0],
            shifts[b, 0],
            steps[b],
            last,
            reads,
        )
        reads = extended_parts[1:]
        if b == 0:
            (late_conv, late_ffn), last = restack(
                [straight(late_conv_parts), straight(late_ffn_parts)], after=last
            )
            late_conv_parts, late_ffn_parts = seq.gather(late_conv), across.gather(late_ffn)
            late_conv_slots = [core.gather(late_conv)]
            late_ffn_slots = [core.gather(late_ffn)]
            in_full[0], out_full[0], last = place_ffn(turned(ffn_slots), sizes, last)
            reads = reads + late_conv_slots[0][1:] + late_ffn_slots[0][1:]
        active, hidden_slopes, (normed_ffn, scale_ffn, stream, conv_input), packets, last = (
            ffn_forward(
                lowered,
                stream,
                in_full[b],
                out_full[b],
                [in_bias_placed[b][c] for c in range(core.size)],
                out_bias[b],
                gains[b, 1],
                shifts[b, 1],
                last,
                reads,
            )
        )
        packets = [core.shifted(packet, -1 - c) for c, packet in enumerate(packets)]
        reads = packets
        saved.append(
            (
                extended_parts,
                conv_slope,
                normed_conv,
                (active, lowered, packets),
                hidden_slopes,
                normed_ffn,
                scale_ffn,
            )
        )

    final_state = from_rows(conv_input, windows)
    (stream_grad, head_grad, loss_rows), last = head_and_loss(stream, head_weight, codes, last)

    ffn_rows_of_sums = [None, None]
    conv_rows_of_sums = [None, None]
    in_bias_grads = [None, None]
    ffn_sums = [None, None]
    conv_sums = [None, None]
    merged = [None, None]

    def groups(halves):
        half = (tap.size + 1) // 2
        return [(each.parts, slots) for each, slots in zip(halves, (half, tap.size - half))]

    for b in (1, 0):
        (
            extended_parts,
            conv_slope,
            normed_conv,
            active_pair,
            hidden_slopes,
            normed_ffn,
            scale_ffn,
        ) = saved[b]
        output_grad, hidden_grad, biases, packets, ffn_rows_of_sums[b], last = ffn_back_hidden(
            stream_grad, normed_ffn, scale_ffn, gains[b, 1], out_full[b], hidden_slopes, last
        )
        if b == 1:
            arrived_packets = [core.shifted(packet, -1 - c) for c, packet in enumerate(packets)]
        if b == 0:
            for each in ffn_sums[1]:
                last = each.step(1, last, [final_state])
            for each in conv_sums[1]:
                last = each.step(1, last)
        stream_grad, conv_grad, conv_cuts, relayed, conv_rows_of_sums[b], last = ffn_back_stream(
            stream_grad,
            hidden_grad,
            packets,
            in_full[b],
            normed_conv,
            conv_slope,
            gains[b, 0],
            core.index,
            last,
            reads,
            relay=b == 0,
        )
        reads = []
        if b == 0:
            merged[1], last = merge_slots(
                groups(conv_sums[1]), groups(ffn_sums[1]), last
            )
            held, last = hold([conv_grad] + list(conv_cuts) + list(relayed), last)
            conv_grad, conv_cuts, relayed = held[0], held[1 : core.size], held[core.size :]
            merged[1] = tap.swap(merged[1])
            arrived_packets = [core.shifted(packet, -1 - c) for c, packet in enumerate(relayed)]
        arrived = [core.shifted(conv_cuts[c - 1], -c) for c in range(1, core.size)]
        in_bias_grads[b] = list(biases)
        found_rims = rims(conv_grad, taps // 2 * steps[b], seq)

        def ffn_grads(last):
            active, lowered, packets = active_pair
            if core.size == 1:
                packets = []
            first, second, token = ffn_weight_grad(
                (
                    (hidden_grad, lowered, [(g, p) for g, p in zip(arrived_packets, packets)]),
                    (active, output_grad, [(p, g) for g, p in zip(arrived_packets, packets)]),
                ),
                sizes,
                ffn_rows,
                last,
            )
            found = [Reduce(first, (across, seq))]
            if second:
                found.append(Reduce(second, (seq, across)))
            return found, (token,)

        def conv_grads(last, reads=()):
            first, second, token = conv_weight_grad(
                extended_parts, conv_grad, arrived, places, sizes, taps, steps[b], last, reads
            )
            found = [Reduce(first, (seq, across))]
            if second:
                found.append(Reduce(second, (across, seq)))
            return found, (token,)

        if b == 1:
            ffn_sums[1], last = ffn_grads(last)
            extended_grad, last = extend(conv_grad, found_rims, seq, last)
            conv_sums[1], last = conv_grads(last)
        else:
            extended_grad, last = extend(conv_grad, found_rims, seq, last)
            conv_sums[0], last = conv_grads(last, arrived_packets)
            ffn_sums[0], last = ffn_grads(last)
            for each in conv_sums[0]:
                last = each.step(1, last, merged[1][1:])
        stream_grad, last = conv_data_grad(
            extended_grad,
            conv_full[b],
            stream_grad,
            steps[b],
            jnp.float32 if b == 1 else jnp.bfloat16,
            last,
        )

    grad_inputs = from_rows(stream_grad, windows)

    row_groups = [(each, 3) for each in conv_rows_of_sums + ffn_rows_of_sums]
    row_groups.append((head_grad, head_weight.shape[1]))
    packed, last = pack_small(row_groups, in_bias_grads, loss_rows, places, sizes, ffn_rows, last)

    conv_rows = taps * slab
    merged[0], last = append_slots(groups(conv_sums[0]), [packed], last)
    merged[0] = tap.swap(merged[0])
    for each in ffn_sums[0]:
        last = each.step(1, last)
    shards, last = finish_conv([merged[0], merged[1]], conv_rows, packed.shape[0], last)
    ffn_late, last = append_slots(groups(ffn_sums[0]), [], last, [grad_inputs])
    ffn_late = tap.swap(ffn_late)
    copies = [each for row in shared_copies(shards, across, seq) for each in row]
    grad_in, grad_out, last = finish_ffn(merged[1], ffn_late, conv_rows, ffn_rows, last)
    (stack,), last = restack([straight(copies)], after=last)
    stacks = core.gather(stack)
    grad_conv = place_conv_grads(
        [
            each[:, : 2 * conv_rows].reshape(len(copies), 2, taps, slab, lanes) for each in stacks
        ],
        places,
        sizes,
    )
    packed = small_total([each[:, 2 * conv_rows :] for each in stacks], places, sizes)
    count = packed.shape[0] // 2
    packed = jnp.concatenate([packed[:count], packed[count:]], 1)
    unpacked = []
    first = 0
    bias_rows = hidden_width // width
    for count in (3, 3, 3, 3, head_weight.shape[1], bias_rows, bias_rows, 2):
        unpacked.append(packed[first : first + count])
        first += count
    conv_0, conv_1, ffn_0, ffn_1, head_sum, bias_0, bias_1, loss_terms = unpacked
    grad_conv_bias = jnp.stack([conv_0[2], conv_1[2]])
    grad_gains = jnp.stack([jnp.stack([conv_0[0], ffn_0[0]]), jnp.stack([conv_1[0], ffn_1[0]])])
    grad_shifts = jnp.stack([jnp.stack([conv_0[1], ffn_0[1]]), jnp.stack([conv_1[1], ffn_1[1]])])
    grad_in_bias = jnp.stack([bias_0.reshape(-1), bias_1.reshape(-1)])
    grad_out_bias = jnp.stack([ffn_0[2], ffn_1[2]])
    loss_terms = loss_terms[0, :2] + loss_terms[1, :2]
    return (
        final_state,
        grad_inputs,
        grad_conv,
        grad_conv_bias,
        grad_gains,
        grad_shifts,
        grad_in,
        grad_in_bias,
        grad_out,
        grad_out_bias,
        head_sum.T,
        loss_terms[0] / loss_terms[1],
    )


def solution(mesh):
    placed = (
        P(("dp", "tap"), "seq", None),
        P(("dp", "tap"), "seq"),
        P(("dp", "tap"), "seq"),
        P(None, None, "tap", None),
        P(),
        P(),
        P(),
        P(None, None, ("dp", "seq", "tap")),
        P(),
        P(None, ("dp", "seq", "tap"), None),
        P(),
        P(),
    )
    return jax.shard_map(
        on_device,
        mesh=mesh,
        in_specs=placed,
        out_specs=(
            P(("dp", "tap"), "seq", None),
            P(("dp", "tap"), "seq", None),
            P(None, None, "tap", None),
            P(),
            P(),
            P(),
            P(None, None, ("dp", "seq", "tap")),
            P(),
            P(None, ("dp", "seq", "tap"), None),
            P(),
            P(),
            P(),
        ),
        check_vma=False,
    )
```

```python
import functools

import jax
import jax.numpy as jnp
import numpy as np
from jax import lax
from jax.experimental import pallas as pl
from jax.experimental.pallas import tpu as pltpu
from jax.sharding import PartitionSpec as P

FIRST_DILATION = 4
SECOND_DILATION = 32
EPSILON = 1e-05
HIGHEST_PRECISION = lax.Precision.HIGHEST
CORES = 2
ROW_TILE = 16
VMEM_BYTES = 20 * 1024 * 1024
ANYWHERE = pl.BlockSpec(memory_space=pl.ANY)
SCALARS = pl.BlockSpec(memory_space=pltpu.SMEM)


TOKEN = jax.ShapeDtypeStruct((8, 128), jnp.float32)


def cost(microseconds):
    size = int(microseconds * 3.5e6)
    return pl.CostEstimate(flops=int(microseconds * 1.1e9), bytes_accessed=size, transcendentals=0)


WHOLE = pl.BlockSpec(memory_space=pltpu.VMEM)
TOKEN_SPEC = pl.BlockSpec(TOKEN.shape, lambda *_: (0, 0))


def tokens(after):
    return [TOKEN_SPEC] * len(after)


def in_hbm(array):
    return pltpu.with_memory_space_constraint(array, pltpu.HBM)


def low(values):
    return values.astype(jnp.bfloat16)


def wide(values):
    return values.astype(jnp.float32)


def gelu_parts(values):
    phi = 0.5 * (1.0 + lax.erf(values * 0.7071067811865476))
    return (
        values * phi,
        phi + values * jnp.exp(-0.5 * values * values) * 0.3989422804014327,
    )


def normalize(values):
    center = values - jnp.mean(values, -1, keepdims=True)
    scale = lax.rsqrt(jnp.mean(center * center, -1, keepdims=True) + EPSILON)
    return (center * scale, scale)


def norm_back(upstream, normed, scale):
    return scale * (
        upstream
        - jnp.mean(upstream, -1, keepdims=True)
        - normed * jnp.mean(upstream * normed, -1, keepdims=True)
    )


def tap_groups(taps):
    return 3 if taps % 3 == 0 else 1


def row_chunks(rows, most):
    size = min(rows, most)
    return [(first, size) for first in range(0, rows, size)]


def conv_forward(extended, weight, stream, bias, gain, shift, step, after=(), reads=()):
    taps, inner, width = weight.shape
    rows = stream.shape[0]
    group = tap_groups(taps)
    steps = taps // group

    def kernel(extended_ref, weight_ref, stream_ref, bias_ref, gain_ref, shift_ref, *refs):
        normed_ref, slope_ref, next_ref, lowered_ref, token_ref, total_ref = refs[-6:]
        token_ref[...] = jnp.zeros(TOKEN.shape, TOKEN.dtype)
        first = pl.program_id(0) * group
        total = None
        for j in range(group):
            start = pl.multiple_of((first + j) * step, ROW_TILE)
            term = jnp.dot(
                extended_ref[pl.ds(start, rows), :],
                weight_ref[j],
                preferred_element_type=jnp.float32,
            )
            total = term if total is None else total + term

        @pl.when(pl.program_id(0) == 0)
        def _():
            total_ref[...] = total

        @pl.when(pl.program_id(0) > 0)
        def _():
            total_ref[...] += total

        @pl.when(pl.program_id(0) == steps - 1)
        def _():
            for at, size in row_chunks(rows, 128):
                some = pl.ds(at, size)
                value, slope = gelu_parts(total_ref[some, :] + bias_ref[...])
                normed, scale = normalize(value)
                mid = wide(stream_ref[some, :]) + normed * gain_ref[...] + shift_ref[...]
                normed_ref[some, :] = low(normed)
                slope_ref[some, :] = low(scale * slope)
                next_ref[some, :] = mid
                lowered_ref[some, :] = low(mid)

    whole = pl.BlockSpec((rows, width), lambda g: (0, 0))
    row = pl.BlockSpec((1, width), lambda g: (0, 0))
    found = pl.pallas_call(
        kernel,
        grid=(steps,),
        in_specs=[
            pl.BlockSpec(extended.shape, lambda g: (0, 0)),
            pl.BlockSpec((group, inner, width), lambda g: (g, 0, 0)),
            whole,
            row,
            row,
            row,
        ]
        + tokens(after)
        + [ANYWHERE] * len(reads),
        out_specs=[whole] * 4 + [TOKEN_SPEC],
        out_shape=[
            pltpu.HBM((rows, width), jnp.bfloat16),
            pltpu.HBM((rows, width), jnp.bfloat16),
            jax.ShapeDtypeStruct((rows, width), jnp.float32),
            jax.ShapeDtypeStruct((rows, width), jnp.bfloat16),
            TOKEN,
        ],
        scratch_shapes=[pltpu.VMEM((rows, width), jnp.float32)],
        compiler_params=pltpu.CompilerParams(vmem_limit_bytes=VMEM_BYTES),
        cost_estimate=cost(9),
        name="conv_forward",
    )(extended, in_hbm(weight), stream, bias[None], gain[None], shift[None], *after, *reads)
    return found[:4], (found[4],)


def ffn_forward(
    lowered, stream, ins, outs, in_biases, out_bias, gain, shift, seq_index, reach, after=(), reads=()
):
    rows, width = lowered.shape
    cores = len(ins)
    units = ins[0].shape[0]
    block = min(units, 256)
    steps = units // block

    rims_out = 1 if reach else 0

    def kernel(place_ref, lowered_ref, stream_ref, out_bias_ref, gain_ref, shift_ref, *refs):
        in_refs, out_refs, bias_refs = (refs[i * cores : (i + 1) * cores] for i in range(3))
        found_refs = refs[-6 - 2 * cores - rims_out :]
        active_ref, slope_refs = found_refs[0], found_refs[1 : 1 + cores]
        normed_ref, scale_ref, next_ref, rounded_ref = found_refs[1 + cores : 5 + cores]
        packet_refs = found_refs[5 + cores : 4 + 2 * cores]
        token_ref, total_ref = found_refs[-2:]
        token_ref[...] = jnp.zeros(TOKEN.shape, TOKEN.dtype)
        lane = pl.multiple_of(width + pl.program_id(0) * block, block)

        @pl.when(pl.program_id(0) == 0)
        def _():
            total_ref[...] = jnp.zeros(total_ref.shape, jnp.float32)
            for packet_ref in packet_refs:
                packet_ref[:, :width] = lowered_ref[...]

        for at, size in row_chunks(rows, 512):
            some = pl.ds(at, size)
            term = None
            for c in range(cores):
                hidden = lax.dot_general(
                    lowered_ref[some, :],
                    in_refs[c][...],
                    (((1,), (1,)), ((), ())),
                    preferred_element_type=jnp.float32,
                )
                active, slope = gelu_parts(hidden + bias_refs[c][...])
                active = low(active)
                if c == 0:
                    active_ref[some, :] = active
                else:
                    packet_refs[c - 1][some, pl.ds(lane, block)] = active
                slope_refs[c][some, :] = low(slope)
                found = jnp.dot(active, out_refs[c][...], preferred_element_type=jnp.float32)
                term = found if term is None else term + found
            total_ref[some, :] += term

        @pl.when(pl.program_id(0) == steps - 1)
        def _():
            for at, size in row_chunks(rows, 128):
                some = pl.ds(at, size)
                normed, scale = normalize(total_ref[some, :] + out_bias_ref[...])
                after_ffn = stream_ref[some, :] + normed * gain_ref[...] + shift_ref[...]
                normed_ref[some, :] = low(normed)
                scale_ref[some, :] = jnp.broadcast_to(scale, (size, 128))
                next_ref[some, :] = after_ffn
                rounded_ref[some, :] = low(after_ffn)
            if reach:
                first = pl.multiple_of((1 - place_ref[0]) * (rows - reach), ROW_TILE)
                found_refs[-3][...] = rounded_ref[pl.ds(first, reach), :]

    whole = pl.BlockSpec((rows, width), lambda g: (0, 0))
    row = pl.BlockSpec((1, width), lambda g: (0, 0))
    piece = pl.BlockSpec((block, width), lambda g: (g, 0))
    columns = pl.BlockSpec((rows, block), lambda g: (0, g))
    hidden_shape = pltpu.HBM((rows, units), jnp.bfloat16)
    found = pl.pallas_call(
        kernel,
        grid=(steps,),
        in_specs=[SCALARS, whole, whole, row, row, row]
        + [piece] * (2 * cores)
        + [pl.BlockSpec((1, block), lambda g: (0, g))] * cores
        + tokens(after)
        + [ANYWHERE] * len(reads),
        out_specs=[columns] * (1 + cores)
        + [whole, pl.BlockSpec((rows, 128), lambda g: (0, 0)), whole, whole]
        + [pl.BlockSpec((rows, width + units), lambda g: (0, 0))] * (cores - 1)
        + [pl.BlockSpec((reach, width), lambda g: (0, 0))] * rims_out
        + [TOKEN_SPEC],
        out_shape=[hidden_shape] * (1 + cores)
        + [
            pltpu.HBM((rows, width), jnp.bfloat16),
            pltpu.HBM((rows, 128), jnp.float32),
            jax.ShapeDtypeStruct((rows, width), jnp.float32),
            jax.ShapeDtypeStruct((rows, width), jnp.bfloat16),
        ]
        + [jax.ShapeDtypeStruct((rows, width + units), jnp.bfloat16)] * (cores - 1)
        + [jax.ShapeDtypeStruct((reach, width), jnp.bfloat16)] * rims_out
        + [TOKEN],
        scratch_shapes=[pltpu.VMEM((rows, width), jnp.float32)],
        compiler_params=pltpu.CompilerParams(vmem_limit_bytes=VMEM_BYTES),
        cost_estimate=cost(11),
        name="ffn_forward",
    )(
        seq_index.astype(jnp.int32)[None],
        lowered,
        stream,
        out_bias[None],
        gain[None],
        shift[None],
        *[in_hbm(each) for each in ins],
        *[in_hbm(each) for each in outs],
        *[each[None] for each in in_biases],
        *after,
        *reads,
    )
    return (
        found[0],
        found[1 : 1 + cores],
        found[1 + cores : 5 + cores],
        found[5 + cores : 4 + 2 * cores],
        found[4 + 2 * cores] if reach else None,
        (found[-1],),
    )


def head_and_loss(stream, head_weight, codes, after=()):
    rows, width = stream.shape
    classes = head_weight.shape[1]
    padded = jnp.pad(head_weight, ((0, 0), (0, 128 - classes)))
    cuts = row_chunks(rows, 256)

    def kernel(stream_ref, head_ref, code_ref, *refs):
        grad_ref, head_grad_ref, sums_ref, token_ref = refs[-4:]
        token_ref[...] = jnp.zeros(TOKEN.shape, TOKEN.dtype)
        head_grad = jnp.zeros((128, width), jnp.float32)
        objective = jnp.zeros((1, 1), jnp.float32)
        scored = jnp.zeros((1, 1), jnp.float32)
        for at, size in cuts:
            some = pl.ds(at, size)
            value = stream_ref[some, :]
            code = code_ref[some, :]
            mask = jnp.where(code[:, :1] >= classes, 1.0, 0.0)
            logits = jnp.dot(
                value, head_ref[...], precision=HIGHEST_PRECISION, preferred_element_type=jnp.float32
            )
            lane = lax.broadcasted_iota(jnp.int32, logits.shape, 1)
            valid = lane < classes
            peak = jnp.max(jnp.where(valid, logits, -jnp.inf), -1, keepdims=True)
            exponent = jnp.where(valid, jnp.exp(jnp.where(valid, logits - peak, 0.0)), 0.0)
            denominator = jnp.sum(exponent, -1, keepdims=True)
            chosen = lane == jnp.where(code >= classes, code - classes, code)
            picked = jnp.sum(jnp.where(chosen, logits, 0.0), -1, keepdims=True)
            terms = mask * (peak + jnp.log(denominator) - picked)
            objective = objective + jnp.sum(terms, 0, keepdims=True)
            scored = scored + jnp.sum(mask, 0, keepdims=True)
            logit_grad = mask * (exponent / denominator - jnp.where(chosen, 1.0, 0.0))
            grad_ref[some, :] = lax.dot_general(
                logit_grad,
                head_ref[...],
                (((1,), (1,)), ((), ())),
                precision=HIGHEST_PRECISION,
                preferred_element_type=jnp.float32,
            )
            head_grad = head_grad + lax.dot_general(
                logit_grad,
                value,
                (((0,), (0,)), ((), ())),
                precision=HIGHEST_PRECISION,
                preferred_element_type=jnp.float32,
            )
        head_grad_ref[...] = head_grad[: head_grad_ref.shape[0]]
        at_row = lax.broadcasted_iota(jnp.int32, sums_ref.shape, 0)
        sums_ref[...] = jnp.where(at_row == 0, objective, scored)

    found = pl.pallas_call(
        kernel,
        out_shape=[
            jax.ShapeDtypeStruct((rows, width), jnp.float32),
            jax.ShapeDtypeStruct((-(-classes // 8) * 8, width), jnp.float32),
            jax.ShapeDtypeStruct((8, 128), jnp.float32),
            TOKEN,
        ],
        compiler_params=pltpu.CompilerParams(vmem_limit_bytes=VMEM_BYTES),
        cost_estimate=cost(6),
        name="head_and_loss",
    )(stream, padded, codes, *after)
    return found[:3], (found[3],)


def ffn_back_hidden(upstream, normed, scale, gain, outs, slopes, after=()):
    rows, width = upstream.shape
    cores = len(outs)
    units = outs[0].shape[0]
    block = min(units, 256)

    def kernel(upstream_ref, normed_ref, scale_ref, gain_ref, *refs):
        out_refs, slope_refs = refs[:cores], refs[cores : 2 * cores]
        found_refs = refs[-3 - 2 * cores :]
        output_grad_ref, hidden_ref = found_refs[:2]
        bias_refs, packet_refs = found_refs[2 : 2 + cores], found_refs[2 + cores : -2]
        sums_ref, token_ref = found_refs[-2:]
        token_ref[...] = jnp.zeros(TOKEN.shape, TOKEN.dtype)
        lane = pl.multiple_of(width + pl.program_id(0) * block, block)

        @pl.when(pl.program_id(0) == 0)
        def _():
            totals = [jnp.zeros((1, width), jnp.float32)] * 3
            for at, size in row_chunks(rows, 128):
                some = pl.ds(at, size)
                grad, value = upstream_ref[some, :], wide(normed_ref[some, :])
                output_grad = low(norm_back(grad * gain_ref[...], value, scale_ref[some, :1]))
                output_grad_ref[some, :] = output_grad
                for packet_ref in packet_refs:
                    packet_ref[some, :width] = output_grad
                for i, each in enumerate((grad * value, grad, wide(output_grad))):
                    totals[i] = totals[i] + jnp.sum(each, 0, keepdims=True)
            sums_ref[...] = jnp.zeros(sums_ref.shape, jnp.float32)
            for i in range(3):
                sums_ref[i : i + 1, :] = totals[i]

        for c in range(cores):
            total = jnp.zeros((1, block), jnp.float32)
            for at, size in row_chunks(rows, 512):
                some = pl.ds(at, size)
                active_grad = lax.dot_general(
                    output_grad_ref[some, :],
                    out_refs[c][...],
                    (((1,), (1,)), ((), ())),
                    preferred_element_type=jnp.float32,
                )
                hidden_grad = low(active_grad * wide(slope_refs[c][some, :]))
                if c == 0:
                    hidden_ref[some, :] = hidden_grad
                else:
                    packet_refs[c - 1][some, pl.ds(lane, block)] = hidden_grad
                total = total + jnp.sum(wide(hidden_grad), 0, keepdims=True)
            bias_refs[c][...] = total

    whole = pl.BlockSpec((rows, width), lambda g: (0, 0))
    columns = pl.BlockSpec((rows, block), lambda g: (0, g))
    found = pl.pallas_call(
        kernel,
        grid=(units // block,),
        in_specs=[
            whole,
            whole,
            pl.BlockSpec((rows, 128), lambda g: (0, 0)),
            pl.BlockSpec((1, width), lambda g: (0, 0)),
        ]
        + [pl.BlockSpec((block, width), lambda g: (g, 0))] * cores
        + [columns] * cores
        + tokens(after),
        out_specs=[whole, columns]
        + [pl.BlockSpec((1, block), lambda g: (0, g))] * cores
        + [pl.BlockSpec((rows, width + units), lambda g: (0, 0))] * (cores - 1)
        + [pl.BlockSpec((8, width), lambda g: (0, 0)), TOKEN_SPEC],
        out_shape=[
            jax.ShapeDtypeStruct((rows, width), jnp.bfloat16),
            pltpu.HBM((rows, units), jnp.bfloat16),
        ]
        + [jax.ShapeDtypeStruct((1, units), jnp.float32)] * cores
        + [jax.ShapeDtypeStruct((rows, width + units), jnp.bfloat16)] * (cores - 1)
        + [jax.ShapeDtypeStruct((8, width), jnp.float32), TOKEN],
        compiler_params=pltpu.CompilerParams(vmem_limit_bytes=VMEM_BYTES),
        cost_estimate=cost(6),
        name="ffn_back_hidden",
    )(
        upstream,
        in_hbm(normed),
        in_hbm(scale),
        gain[None],
        *[in_hbm(each) for each in outs],
        *[in_hbm(each) for each in slopes],
        *after,
    )
    return (
        found[0],
        found[1],
        found[2 : 2 + cores],
        found[2 + cores : -2],
        found[-2],
        (found[-1],),
    )


def ffn_back_stream(
    upstream, hidden, packets, ins, normed, slope, gain, places, reach, after=(), reads=(), relay=False
):
    rows, width = upstream.shape
    cores = len(ins)
    units = ins[0].shape[0]
    block = min(units, 256)
    steps = units // block
    lanes = width // cores
    relays = cores - 1 if relay else 0
    rims_out = 1 if reach else 0

    def kernel(core_ref, upstream_ref, normed_ref, slope_ref, gain_ref, *refs):
        hidden_refs, in_refs = refs[:cores], refs[cores : 2 * cores]
        found_refs = refs[-4 - cores - relays - rims_out :]
        mid_ref, conv_grad_ref = found_refs[:2]
        cut_refs = found_refs[2 : 1 + cores]
        sums_ref, token_ref, total_ref = found_refs[-3:]
        token_ref[...] = jnp.zeros(TOKEN.shape, TOKEN.dtype)
        for i in range(relays):
            relay_ref = found_refs[1 + cores + i]
            lane = pl.multiple_of(width + pl.program_id(0) * block, block)
            relay_ref[:, pl.ds(lane, block)] = hidden_refs[1 + i][...]

            @pl.when(pl.program_id(0) == 0)
            def _(i=i, relay_ref=relay_ref):
                relay_ref[:, :width] = refs[2 * cores + i][...]

        @pl.when(pl.program_id(0) == 0)
        def _():
            total_ref[...] = upstream_ref[...]

        for at, size in row_chunks(rows, 512):
            some = pl.ds(at, size)
            total_ref[some, :] += sum(
                jnp.dot(
                    hidden_refs[c][some, :], in_refs[c][...], preferred_element_type=jnp.float32
                )
                for c in range(cores)
            )

        @pl.when(pl.program_id(0) == steps - 1)
        def _():
            totals = [jnp.zeros((1, width), jnp.float32)] * 3
            for at, size in row_chunks(rows, 128):
                some = pl.ds(at, size)
                grad, value = total_ref[some, :], wide(normed_ref[some, :])
                conv_grad = low(norm_back(grad * gain_ref[...], value, wide(slope_ref[some, :])))
                mid_ref[some, :] = grad
                conv_grad_ref[some, :] = conv_grad
                for i, each in enumerate((grad * value, grad, wide(conv_grad))):
                    totals[i] = totals[i] + jnp.sum(each, 0, keepdims=True)
            sums_ref[...] = jnp.zeros(sums_ref.shape, jnp.float32)
            for i in range(3):
                sums_ref[i : i + 1, :] = totals[i]
            for c in range(1, cores):
                first = lax.rem(core_ref[0] - c + cores, cores) * lanes
                cut_refs[c - 1][...] = conv_grad_ref[:, pl.ds(pl.multiple_of(first, lanes), lanes)]
            if reach:
                first = pl.multiple_of((1 - core_ref[1]) * (rows - reach), ROW_TILE)
                found_refs[-4][...] = conv_grad_ref[pl.ds(first, reach), :]

    whole = pl.BlockSpec((rows, width), lambda g, core: (0, 0))
    found = pl.pallas_call(
        kernel,
        grid_spec=pltpu.PrefetchScalarGridSpec(
            num_scalar_prefetch=1,
            grid=(steps,),
            in_specs=[whole, whole, whole, pl.BlockSpec((1, width), lambda g, core: (0, 0))]
            + [pl.BlockSpec((rows, block), lambda g, core: (0, g))]
            + [pl.BlockSpec((rows, block), lambda g, core: (0, width // block + g))] * (cores - 1)
            + [pl.BlockSpec((block, width), lambda g, core: (g, 0))] * cores
            + [whole] * relays
            + tokens(after)
            + [ANYWHERE] * len(reads),
            out_specs=[whole, whole]
            + [pl.BlockSpec((rows, lanes), lambda g, core: (0, 0))] * (cores - 1)
            + [pl.BlockSpec((rows, width + units), lambda g, core: (0, 0))] * relays
            + [pl.BlockSpec((reach, width), lambda g, core: (0, 0))] * rims_out
            + [pl.BlockSpec((8, width), lambda g, core: (0, 0)), TOKEN_SPEC],
            scratch_shapes=[pltpu.VMEM((rows, width), jnp.float32)],
        ),
        out_shape=[
            jax.ShapeDtypeStruct((rows, width), jnp.float32),
            jax.ShapeDtypeStruct((rows, width), jnp.bfloat16),
        ]
        + [jax.ShapeDtypeStruct((rows, lanes), jnp.bfloat16)] * (cores - 1)
        + [jax.ShapeDtypeStruct((rows, width + units), jnp.bfloat16)] * relays
        + [jax.ShapeDtypeStruct((reach, width), jnp.bfloat16)] * rims_out
        + [jax.ShapeDtypeStruct((8, width), jnp.float32), TOKEN],
        compiler_params=pltpu.CompilerParams(vmem_limit_bytes=VMEM_BYTES),
        cost_estimate=cost(5),
        name="ffn_back_stream",
    )(
        jnp.stack(places[:2]).astype(jnp.int32),
        upstream,
        in_hbm(normed),
        in_hbm(slope),
        gain[None],
        in_hbm(hidden),
        *packets,
        *[in_hbm(each) for each in ins],
        *packets[:relays],
        *after,
        *reads,
    )
    return (
        found[0],
        found[1],
        found[2 : 1 + cores],
        found[1 + cores : 1 + cores + relays],
        found[1 + cores + relays] if reach else None,
        found[-2],
        (found[-1],),
    )


def conv_data_grad(extended, weight, upstream, step, kind, after=()):
    taps, inner, width = weight.shape
    rows = upstream.shape[0]
    group = tap_groups(taps)
    steps = taps // group

    def kernel(extended_ref, weight_ref, upstream_ref, *refs):
        out_ref, token_ref, total_ref = refs[-3:]
        token_ref[...] = jnp.zeros(TOKEN.shape, TOKEN.dtype)
        first = pl.program_id(0) * group
        total = None
        for j in range(group):
            start = pl.multiple_of((taps - 1 - first - j) * step, ROW_TILE)
            term = lax.dot_general(
                extended_ref[pl.ds(start, rows), :],
                weight_ref[j],
                (((1,), (1,)), ((), ())),
                preferred_element_type=jnp.float32,
            )
            total = term if total is None else total + term

        @pl.when(pl.program_id(0) == 0)
        def _():
            total_ref[...] = total

        @pl.when(pl.program_id(0) > 0)
        def _():
            total_ref[...] += total

        @pl.when(pl.program_id(0) == steps - 1)
        def _():
            out_ref[...] = (upstream_ref[...] + wide(low(total_ref[...]))).astype(kind)

    whole = pl.BlockSpec((rows, inner), lambda g: (0, 0))
    found = pl.pallas_call(
        kernel,
        grid=(steps,),
        in_specs=[
            pl.BlockSpec(extended.shape, lambda g: (0, 0)),
            pl.BlockSpec((group, inner, width), lambda g: (g, 0, 0)),
            whole,
        ]
        + tokens(after),
        out_specs=(whole, TOKEN_SPEC),
        out_shape=(jax.ShapeDtypeStruct((rows, inner), kind), TOKEN),
        scratch_shapes=[pltpu.VMEM((rows, inner), jnp.float32)],
        compiler_params=pltpu.CompilerParams(vmem_limit_bytes=VMEM_BYTES),
        cost_estimate=cost(6),
        name="conv_data_grad",
    )(extended, in_hbm(weight), upstream, *after)
    return found[0], (found[1],)


def hold(arrays, after, reads=()):
    count = len(arrays)
    if count == 0:
        return [], after

    def kernel(*refs):
        refs[-1][...] = jnp.zeros(TOKEN.shape, TOKEN.dtype)

    found = pl.pallas_call(
        kernel,
        in_specs=[ANYWHERE] * (count + len(reads)) + [WHOLE] * len(after),
        out_specs=[ANYWHERE] * count + [WHOLE],
        out_shape=[jax.ShapeDtypeStruct(each.shape, each.dtype) for each in arrays] + [TOKEN],
        input_output_aliases={i: i for i in range(count)},
        cost_estimate=cost(0.5),
        name="hold",
    )(*arrays, *reads, *after)
    return list(found[:-1]), (found[-1],)


def join_rows(parts, after=(), reads=()):
    def kernel(*refs):
        out_ref, token_ref = refs[-2:]
        token_ref[...] = jnp.zeros(TOKEN.shape, TOKEN.dtype)
        first = 0
        for i, part in enumerate(parts):
            out_ref[first : first + part.shape[0]] = refs[i][...]
            first += part.shape[0]

    shape = (sum(part.shape[0] for part in parts), parts[0].shape[1])
    found = pl.pallas_call(
        kernel,
        in_specs=[WHOLE] * len(parts) + [ANYWHERE] * len(reads) + [WHOLE] * len(after),
        out_specs=[WHOLE] * 2,
        out_shape=[jax.ShapeDtypeStruct(shape, parts[0].dtype), TOKEN],
        compiler_params=pltpu.CompilerParams(vmem_limit_bytes=VMEM_BYTES),
        cost_estimate=cost(1.5),
        name="join_rows",
    )(*parts, *reads, *after)
    return found[0], (found[1],)


def restack(groups, reads=(), after=()):
    cuts = [cut for _, each in groups for cut in each]
    if any(last is not None and (first % ROW_TILE or last % ROW_TILE) for first, last, _ in cuts):
        return [
            jnp.stack([array[first:last].reshape(shape) for array in arrays])
            for arrays, each in groups
            for first, last, shape in each
        ], after
    flat = [array for arrays, _ in groups for array in arrays]
    plan = []
    shapes = []
    at = 0
    for arrays, each in groups:
        for first, last, shape in each:
            for slot in range(len(arrays)):
                plan.append((at + slot, first, last, len(shapes), slot))
            held = shape if last is None else (last - first,) + arrays[0].shape[1:]
            shapes.append(jax.ShapeDtypeStruct((len(arrays),) + held, arrays[0].dtype))
        at += len(arrays)

    def kernel(*refs):
        out_refs = refs[-2 - len(shapes) : -2]
        token_ref, sem_ref = refs[-2:]
        token_ref[...] = jnp.zeros(TOKEN.shape, TOKEN.dtype)
        copies = []
        for source, first, last, target, slot in plan:
            ref = refs[source]
            copies.append(
                pltpu.make_async_copy(
                    ref if last is None else ref.at[pl.ds(first, last - first)],
                    out_refs[target].at[slot],
                    sem_ref.at[len(copies)],
                )
            )
        copy_all(copies)

    found = pl.pallas_call(
        kernel,
        in_specs=[ANYWHERE] * (len(flat) + len(reads)) + [WHOLE] * len(after),
        out_specs=[WHOLE] * (len(shapes) + 1),
        out_shape=shapes + [TOKEN],
        scratch_shapes=[pltpu.SemaphoreType.DMA((len(plan),))],
        compiler_params=pltpu.CompilerParams(vmem_limit_bytes=VMEM_BYTES),
        cost_estimate=cost(1.5),
        name="restack",
    )(*flat, *reads, *after)
    return [
        each.reshape((each.shape[0],) + shape) for each, (_, _, shape) in zip(found, cuts)
    ], (found[-1],)


def conv_weight_grad(
    extendeds, upstream, arrived, places, sizes, taps, step, after=(), reads=()
):
    cores, seqs, acrosses, tap_peers = sizes
    rows = upstream.shape[0]
    inner = extendeds[0].shape[1]
    lanes = upstream.shape[1] // cores
    slab = inner // (seqs * acrosses * tap_peers)
    direct = slab % ROW_TILE == 0
    half = (tap_peers + 1) // 2
    rest = tap_peers - half
    seconds = acrosses if rest else 0
    outs = seqs + seconds if direct else 1

    def kernel(place_ref, *refs):
        out_refs = refs[-2 - outs : -2]
        token_ref, found_ref = refs[-2:]
        token_ref[...] = jnp.zeros(TOKEN.shape, TOKEN.dtype)
        start = pl.multiple_of(pl.program_id(0) * step, ROW_TILE)
        found = low(
            sum(
                lax.dot_general(
                    refs[c][pl.ds(start, rows), :],
                    refs[cores + c][...],
                    (((0,), (0,)), ((), ())),
                    preferred_element_type=jnp.float32,
                )
                for c in range(cores)
            )
        )
        if not direct:
            out_refs[0][0] = found
            return
        found_ref[...] = found

        def chunk(slot_t, slot_s, slot_a):
            t = lax.rem(place_ref[3] - slot_t + tap_peers, tap_peers)
            at = lax.rem(place_ref[1] - slot_s + seqs, seqs)
            a = lax.rem(place_ref[2] - slot_a + acrosses, acrosses)
            first = pl.multiple_of(((t * seqs + at) * acrosses + a) * slab, slab)
            return found_ref[pl.ds(first, slab), :]

        for s in range(seqs):
            for a in range(acrosses):
                for t in range(half):
                    out_refs[s][a, t, 0] = chunk(t, s, a)
                for t in range(half, tap_peers):
                    out_refs[seqs + a][s, t - half, 0] = chunk(t, s, a)

    if direct:
        shapes = [(acrosses, half, taps, slab, lanes)] * seqs
        shapes += [(seqs, rest, taps, slab, lanes)] * seconds
        specs = [
            pl.BlockSpec(shape[:2] + (1, slab, lanes), lambda k, place: (0, 0, k, 0, 0))
            for shape in shapes
        ]
    else:
        shapes = [(taps, inner, lanes)]
        specs = [pl.BlockSpec((1, inner, lanes), lambda k, place: (k, 0, 0))]
    found = pl.pallas_call(
        kernel,
        grid_spec=pltpu.PrefetchScalarGridSpec(
            num_scalar_prefetch=1,
            grid=(taps,),
            in_specs=[pl.BlockSpec(extendeds[0].shape, lambda k, place: (0, 0))] * cores
            + [pl.BlockSpec((rows, lanes), lambda k, place: (0, place[0]))]
            + [pl.BlockSpec((rows, lanes), lambda k, place: (0, 0))] * (cores - 1)
            + tokens(after)
            + [ANYWHERE] * len(reads),
            out_specs=specs + [TOKEN_SPEC],
            scratch_shapes=[pltpu.VMEM((inner, lanes), jnp.bfloat16)],
        ),
        out_shape=[jax.ShapeDtypeStruct(shape, jnp.bfloat16) for shape in shapes] + [TOKEN],
        compiler_params=pltpu.CompilerParams(vmem_limit_bytes=VMEM_BYTES),
        cost_estimate=cost(9),
        name="conv_weight_grad",
    )(jnp.stack(places).astype(jnp.int32), *extendeds, upstream, *arrived, *after, *reads)
    token = found[-1]
    if not direct:
        found = found[0].reshape(taps, tap_peers, seqs, acrosses, slab, lanes)
        for axis, which in ((1, 3), (2, 1), (3, 2)):
            found = relative(found, axis, places[which], sizes[which])
        found = found.transpose(2, 3, 1, 0, 4, 5)
        found = [found[s, :, :half] for s in range(seqs)] + [
            found[:, a, half:] for a in range(seconds)
        ]
    flat = [each.reshape(-1, lanes) for each in found[: seqs + seconds]]
    return flat[:seqs], flat[seqs:], token


def ffn_weight_grad(pairs, sizes, ffn_rows, after=()):
    cores, seqs, acrosses, tap_peers = sizes
    rows, width = pairs[0][1].shape
    block = tap_peers * ffn_rows
    half = (tap_peers + 1) // 2
    rest = tap_peers - half
    seconds = seqs if rest else 0
    transposed = (((0,), (0,)), ((), ()))
    if ffn_rows % ROW_TILE:
        found = jnp.stack(
            [
                low(
                    sum(
                        lax.dot_general(a, b, transposed, preferred_element_type=jnp.float32)
                        for a, b in [(left, right)]
                        + [(ends[:, width:], starts[:, :width]) for ends, starts in packets]
                    )
                ).reshape(acrosses, seqs, tap_peers, ffn_rows, width)
                for left, right, packets in pairs
            ],
            3,
        )
        token = jnp.zeros(TOKEN.shape, TOKEN.dtype)
        return (
            [found[a, :, :half].reshape(-1, width) for a in range(acrosses)],
            [found[:, s, half:].reshape(-1, width) for s in range(seconds)],
            token,
        )
    outs = acrosses + seconds

    def kernel(*refs):
        out_refs, token_ref = refs[-1 - outs : -1], refs[-1]
        token_ref[...] = jnp.zeros(TOKEN.shape, TOKEN.dtype)
        step = pl.program_id(0)
        for which in range(2):
            base = 2 * cores * which
            found = low(
                sum(
                    lax.dot_general(
                        refs[base + 2 * c][...],
                        refs[base + 2 * c + 1][...],
                        transposed,
                        preferred_element_type=jnp.float32,
                    )
                    for c in range(cores)
                )
            ).reshape(tap_peers, ffn_rows, width)
            for a in range(acrosses):

                @pl.when(step // seqs == a)
                def _(a=a):
                    out_refs[a][0, :, which] = found[:half]

            for s in range(seconds):

                @pl.when(lax.rem(step, seqs) == s)
                def _(s=s):
                    out_refs[acrosses + s][0, :, which] = found[half:]

    right_spec = pl.BlockSpec((rows, width), lambda g: (0, 0))
    left_spec = pl.BlockSpec((rows, block), lambda g: (0, g))
    late_spec = pl.BlockSpec((rows, block), lambda g: (0, width // block + g))

    def first_spec(a):
        return pl.BlockSpec(
            (1, half, 2, ffn_rows, width),
            lambda g: (jnp.clip(g - a * seqs, 0, seqs - 1), 0, 0, 0, 0),
        )

    second_spec = pl.BlockSpec(
        (1, rest, 2, ffn_rows, width), lambda g: (g // seqs, 0, 0, 0, 0)
    )
    operands = []
    for left, right, packets in pairs:
        operands += [in_hbm(left), right]
        for ends, starts in packets:
            operands += [ends, starts]
    found = pl.pallas_call(
        kernel,
        grid=(acrosses * seqs,),
        in_specs=([left_spec, right_spec] + [late_spec, right_spec] * (cores - 1)) * 2
        + tokens(after),
        out_specs=[first_spec(a) for a in range(acrosses)]
        + [second_spec] * seconds
        + [TOKEN_SPEC],
        out_shape=[jax.ShapeDtypeStruct((seqs, half, 2, ffn_rows, width), jnp.bfloat16)] * acrosses
        + [jax.ShapeDtypeStruct((acrosses, rest, 2, ffn_rows, width), jnp.bfloat16)] * seconds
        + [TOKEN],
        compiler_params=pltpu.CompilerParams(vmem_limit_bytes=VMEM_BYTES),
        cost_estimate=cost(8),
        name="ffn_weight_grad",
    )(*operands, *after)
    flat = [each.reshape(-1, width) for each in found[:-1]]
    return flat[:acrosses], flat[acrosses:], found[-1]


def group_slots(groups, lanes):
    flat, where = [], []
    rows = groups[0][0][0].size // (groups[0][1] * lanes)
    for parts, slots in groups:
        where += [(len(flat), len(parts), slot) for slot in range(slots)]
        flat += [part.reshape(slots, rows, lanes) for part in parts]
    return flat, where, rows


def slot_sum(refs, place, first=0):
    start, count, at = place
    return low(sum(wide(refs[first + start + i][at]) for i in range(count)))


def merge_slots(conv_groups, ffn_groups, after=()):
    lanes, width = conv_groups[0][0][0].shape[-1], ffn_groups[0][0][0].shape[-1]
    cuts = width // lanes
    conv_parts, conv_where, conv_rows = group_slots(conv_groups, lanes)
    ffn_parts, ffn_where, ffn_rows = group_slots(ffn_groups, width)
    slots = len(conv_where)
    if conv_rows % ROW_TILE or ffn_rows % ROW_TILE:
        merged = []
        for slot in range(slots):
            ffn = slot_sum(ffn_parts, ffn_where[slot])
            merged.append(
                jnp.concatenate(
                    [slot_sum(conv_parts, conv_where[slot])]
                    + [ffn[:, i * lanes : (i + 1) * lanes] for i in range(cuts)]
                )
            )
        return merged, after

    def kernel(*refs):
        out_refs, token_ref = refs[-1 - slots : -1], refs[-1]
        token_ref[...] = jnp.zeros(TOKEN.shape, TOKEN.dtype)
        for slot in range(slots):
            out_refs[slot][:conv_rows] = slot_sum(refs, conv_where[slot])
            ffn = slot_sum(refs, ffn_where[slot], len(conv_parts))
            for i in range(cuts):
                first = conv_rows + i * ffn_rows
                out_refs[slot][first : first + ffn_rows] = ffn[:, i * lanes : (i + 1) * lanes]

    found = pl.pallas_call(
        kernel,
        in_specs=[WHOLE] * (len(conv_parts) + len(ffn_parts) + len(after)),
        out_specs=[WHOLE] * (slots + 1),
        out_shape=[jax.ShapeDtypeStruct((conv_rows + cuts * ffn_rows, lanes), jnp.bfloat16)] * slots
        + [TOKEN],
        compiler_params=pltpu.CompilerParams(vmem_limit_bytes=VMEM_BYTES),
        cost_estimate=cost(1.5),
        name="merge_slots",
    )(*conv_parts, *ffn_parts, *after)
    return found[:slots], (found[slots],)


def append_slots(groups, packed, after=(), reads=()):
    lanes = groups[0][0][0].shape[-1]
    parts, where, rows = group_slots(groups, lanes)
    slots = len(where)
    if rows % ROW_TILE:
        return [
            jnp.concatenate([slot_sum(parts, where[slot])] + packed) for slot in range(slots)
        ], after

    def kernel(*refs):
        out_refs, token_ref = refs[-1 - slots : -1], refs[-1]
        token_ref[...] = jnp.zeros(TOKEN.shape, TOKEN.dtype)
        for slot in range(slots):
            out_refs[slot][:rows] = slot_sum(refs, where[slot])
            if packed:
                out_refs[slot][rows:] = refs[len(parts)][...]

    shape = jax.ShapeDtypeStruct((rows + sum(each.shape[0] for each in packed), lanes), jnp.bfloat16)
    found = pl.pallas_call(
        kernel,
        in_specs=[WHOLE] * (len(packed) + len(parts) + len(after)) + [ANYWHERE] * len(reads),
        out_specs=[WHOLE] * (slots + 1),
        out_shape=[shape] * slots + [TOKEN],
        compiler_params=pltpu.CompilerParams(vmem_limit_bytes=VMEM_BYTES),
        cost_estimate=cost(1),
        name="append_slots",
    )(*parts, *packed, *after, *reads)
    return found[:slots], (found[slots],)


def pack_small(row_groups, biases, losses, places, sizes, ffn_rows, after=()):
    cores, seqs, acrosses, tap_peers = sizes
    width = row_groups[0][0].shape[1]
    head_rows = sum(count for _, count in row_groups)
    hidden = cores * biases[0][0].shape[1]
    bias_rows = hidden // width
    used = head_rows + len(biases) * bias_rows + 2
    rows = -(-used // ROW_TILE) * ROW_TILE
    lanes = width // 2
    per_row = width // ffn_rows
    if ffn_rows % 64:
        terms = jnp.stack([losses[0, 0], losses[1, 0]])
        terms = jnp.stack([terms, terms - wide(low(terms))])
        pieces = [array[:count] for array, count in row_groups]
        for each in biases:
            bias = jnp.stack(each).reshape(cores, acrosses, seqs, tap_peers, ffn_rows)
            for axis, which in enumerate((0, 2, 1, 3)):
                bias = relative(bias, axis, places[which], sizes[which])
            pieces.append(bias.transpose(1, 0, 2, 3, 4).reshape(-1, width))
        pieces.append(jnp.pad(terms, ((0, rows - used), (0, width - 2))))
        packed = low(jnp.concatenate(pieces))
        return jnp.concatenate([packed[:, :lanes], packed[:, lanes:]]), after

    def kernel(place_ref, *refs):
        packed_ref, token_ref, rows_ref = refs[-3:]
        token_ref[...] = jnp.zeros(TOKEN.shape, TOKEN.dtype)
        rows_ref[...] = jnp.zeros(rows_ref.shape, jnp.float32)
        at = 0
        for i, (_, count) in enumerate(row_groups):
            rows_ref[at : at + count, :] = refs[i][:count, :]
            at += count
        shape = (cores, acrosses, seqs, tap_peers)
        owners = (0, 2, 1, 3)
        for b in range(len(biases)):
            blocks = {}
            for slot in np.ndindex(*shape):
                first = ((slot[1] * seqs + slot[2]) * tap_peers + slot[3]) * ffn_rows
                ref = refs[len(row_groups) + b * cores + slot[0]]
                blocks[slot] = ref[:, first : first + ffn_rows]
            for axis, size in enumerate(shape):
                turned = {}
                for slot in blocks:
                    place = lax.rem(place_ref[owners[axis]] - slot[axis] + size, size)
                    value = blocks[slot[:axis] + (0,) + slot[axis + 1 :]]
                    for other in range(1, size):
                        candidate = blocks[slot[:axis] + (other,) + slot[axis + 1 :]]
                        value = jnp.where(place == other, candidate, value)
                    turned[slot] = value
                blocks = turned
            ordered = [
                blocks[(c, a, s, t)]
                for a in range(acrosses)
                for c in range(cores)
                for s in range(seqs)
                for t in range(tap_peers)
            ]
            for row in range(bias_rows):
                line = ordered[row * per_row : (row + 1) * per_row]
                rows_ref[at : at + 1, :] = jnp.concatenate(line, 1)
                at += 1
        losses_ref = refs[len(row_groups) + len(biases) * cores]
        lane = lax.broadcasted_iota(jnp.int32, (1, width), 1)
        objective = jnp.broadcast_to(losses_ref[0:1, 0:1], (1, width))
        scored = jnp.broadcast_to(losses_ref[1:2, 0:1], (1, width))
        line = jnp.where(lane == 0, objective, jnp.where(lane == 1, scored, 0.0))
        rows_ref[at : at + 1, :] = line
        rows_ref[at + 1 : at + 2, :] = line - wide(low(line))
        packed_ref[:rows, :] = low(rows_ref[:, :lanes])
        packed_ref[rows:, :] = low(rows_ref[:, lanes:])

    flat = [array for array, _ in row_groups] + [each for some in biases for each in some]
    found = pl.pallas_call(
        kernel,
        in_specs=[SCALARS] + [WHOLE] * (len(flat) + 1 + len(after)),
        out_specs=[WHOLE] * 2,
        out_shape=[jax.ShapeDtypeStruct((2 * rows, lanes), jnp.bfloat16), TOKEN],
        scratch_shapes=[pltpu.VMEM((rows, width), jnp.float32)],
        compiler_params=pltpu.CompilerParams(vmem_limit_bytes=VMEM_BYTES),
        cost_estimate=cost(2),
        name="pack_small",
    )(jnp.stack(places).astype(jnp.int32), *flat, losses, *after)
    return found[0], (found[1],)


def paired(values):
    while len(values) > 1:
        half = len(values) // 2
        if len(values) % 2:
            return sum(values[1:], values[0])
        values = [values[i] + values[i + half] for i in range(half)]
    return values[0]


def finish_small(stacks, first, width, classes, hidden, places, sizes):
    cores, seqs, acrosses = sizes[:3]
    peers, rows, lanes = stacks[0].shape
    count = rows - first
    bias_rows = hidden // width
    at_bias = 12 + classes
    at_loss = at_bias + 2 * bias_rows

    def pick(row):
        return (
            [row(2), row(5)],
            [[row(0), row(6)], [row(3), row(9)]],
            [[row(1), row(7)], [row(4), row(10)]],
            [[row(at_bias + b * bias_rows + i) for i in range(bias_rows)] for b in range(2)],
            [row(8), row(11)],
        )

    if max(cores, seqs, acrosses) > 2 or first % count or count % ROW_TILE:
        full = jnp.stack(
            [wide(each[:, first:]).reshape(seqs, acrosses, count, lanes) for each in stacks]
        )
        for axis, (place, size) in enumerate(zip(places[:3], sizes[:3])):
            full = relative(full, axis, place, size)
        total = jnp.sum(full, (0, 1, 2))
        total = jnp.concatenate([total[: count // 2], total[count // 2 :]], 1)
        conv_bias, gains, shifts, in_bias, out_bias = pick(lambda i: total[i])
        terms = total[at_loss] + total[at_loss + 1]
        return (
            jnp.stack(conv_bias),
            jnp.stack([jnp.stack(each) for each in gains]),
            jnp.stack([jnp.stack(each) for each in shifts]),
            jnp.stack([jnp.concatenate(each) for each in in_bias]),
            jnp.stack(out_bias),
            total[12:at_bias].T,
            (terms[0] / terms[1]).reshape(1, 1),
        )

    def kernel(*refs):
        conv_ref, gain_ref, shift_ref, in_ref, out_ref, head_ref, loss_ref, rows_ref = refs[cores:]
        total = paired(
            [
                paired(
                    [
                        paired([wide(refs[c][s * acrosses + a]) for a in range(acrosses)])
                        for s in range(seqs)
                    ]
                )
                for c in range(cores)
            ]
        )
        rows_ref[:, :lanes] = total[: count // 2]
        rows_ref[:, lanes:] = total[count // 2 :]
        conv_bias, gains, shifts, in_bias, out_bias = pick(lambda i: rows_ref[i : i + 1, :])
        for b in range(2):
            conv_ref[b : b + 1, :] = conv_bias[b]
            out_ref[b : b + 1, :] = out_bias[b]
            for i in range(2):
                gain_ref[b, i : i + 1, :] = gains[b][i]
                shift_ref[b, i : i + 1, :] = shifts[b][i]
            for i in range(bias_rows):
                in_ref[b : b + 1, i * width : (i + 1) * width] = in_bias[b][i]
        head_ref[...] = rows_ref[12 : 12 + 8 * (-(-classes // 8)), :].T[:, :classes]
        terms = rows_ref[at_loss : at_loss + 1, :128] + rows_ref[at_loss + 1 : at_loss + 2, :128]
        loss_ref[...] = terms[:, 0:1] / terms[:, 1:2]

    return pl.pallas_call(
        kernel,
        grid=(1,),
        in_specs=[pl.BlockSpec((peers, count, lanes), lambda g: (0, first // count, 0))] * cores,
        out_shape=(
            jax.ShapeDtypeStruct((2, width), jnp.float32),
            jax.ShapeDtypeStruct((2, 2, width), jnp.float32),
            jax.ShapeDtypeStruct((2, 2, width), jnp.float32),
            jax.ShapeDtypeStruct((2, hidden), jnp.float32),
            jax.ShapeDtypeStruct((2, width), jnp.float32),
            jax.ShapeDtypeStruct((width, classes), jnp.float32),
            jax.ShapeDtypeStruct((1, 1), jnp.float32),
        ),
        out_specs=[
            pl.BlockSpec((2, width), lambda g: (0, 0)),
            pl.BlockSpec((2, 2, width), lambda g: (0, 0, 0)),
            pl.BlockSpec((2, 2, width), lambda g: (0, 0, 0)),
            pl.BlockSpec((2, hidden), lambda g: (0, 0)),
            pl.BlockSpec((2, width), lambda g: (0, 0)),
            pl.BlockSpec((width, classes), lambda g: (0, 0)),
            pl.BlockSpec((1, 1), lambda g: (0, 0)),
        ],
        scratch_shapes=[pltpu.VMEM((count // 2, 2 * lanes), jnp.float32)],
        compiler_params=pltpu.CompilerParams(vmem_limit_bytes=VMEM_BYTES),
        cost_estimate=cost(1.5),
        name="finish_small",
    )(*stacks)


def finish_conv(parts, conv_rows, small_rows, after=()):
    blocks, count = len(parts), len(parts[0])
    lanes = parts[0][0].shape[-1]
    flat = [part for block in parts for part in block]
    if conv_rows % ROW_TILE:
        sums = [sum(wide(part[:conv_rows]) for part in block) for block in parts]
        sums.append(paired([wide(part[conv_rows:]) for part in parts[0]]))
        return jnp.concatenate([low(total) for total in sums]), after

    def kernel(*refs):
        shard_ref, token_ref = refs[-2:]
        token_ref[...] = jnp.zeros(TOKEN.shape, TOKEN.dtype)
        shard_ref[blocks * conv_rows :] = low(
            paired([wide(refs[i][conv_rows:]) for i in range(count)])
        )
        for b in range(blocks):
            total = sum(wide(refs[b * count + i][:conv_rows]) for i in range(count))
            shard_ref[b * conv_rows : (b + 1) * conv_rows] = low(total)

    found = pl.pallas_call(
        kernel,
        in_specs=[WHOLE] * (len(flat) + len(after)),
        out_specs=[WHOLE] * 2,
        out_shape=[
            jax.ShapeDtypeStruct((blocks * conv_rows + small_rows, lanes), jnp.bfloat16),
            TOKEN,
        ],
        compiler_params=pltpu.CompilerParams(vmem_limit_bytes=VMEM_BYTES),
        cost_estimate=cost(1.2),
        name="finish_conv",
    )(*flat, *after)
    return found[0], (found[1],)


def finish_ffn(merged, plain, conv_rows, ffn_rows, after=()):
    lanes, width = merged[0].shape[-1], plain[0].shape[-1]

    def cut_back(total):
        size = 2 * ffn_rows
        return jnp.concatenate(
            [total[i * size : (i + 1) * size] for i in range(width // lanes)], 1
        )

    if conv_rows % ROW_TILE or ffn_rows % ROW_TILE:
        sums = [sum(wide(part) for part in plain)]
        sums.append(cut_back(sum(wide(part[conv_rows:]) for part in merged)))
        return jnp.stack([each[:ffn_rows].T for each in sums]), jnp.stack(
            [each[ffn_rows:] for each in sums]
        ), after

    def kernel(*refs):
        in_ref, out_ref, token_ref = refs[-3:]
        token_ref[...] = jnp.zeros(TOKEN.shape, TOKEN.dtype)
        late = sum(wide(refs[i][conv_rows:]) for i in range(len(merged)))
        sums = [sum(wide(refs[len(merged) + i][...]) for i in range(len(plain))), cut_back(late)]
        for b in range(2):
            in_ref[b] = sums[b][:ffn_rows].T
            out_ref[b] = sums[b][ffn_rows:]

    found = pl.pallas_call(
        kernel,
        in_specs=[WHOLE] * (len(merged) + len(plain) + len(after)),
        out_specs=[WHOLE] * 3,
        out_shape=(
            jax.ShapeDtypeStruct((2, width, ffn_rows), jnp.float32),
            jax.ShapeDtypeStruct((2, ffn_rows, width), jnp.float32),
            TOKEN,
        ),
        compiler_params=pltpu.CompilerParams(vmem_limit_bytes=VMEM_BYTES),
        cost_estimate=cost(1),
        name="finish_ffn",
    )(*merged, *plain, *after)
    return found[0], found[1], (found[2],)


def add_slots(parts, slots, after=(), reads=()):
    lanes = parts[0].shape[-1]
    rows = parts[0].size // (slots * lanes)
    parts = [part.reshape(slots, rows, lanes) for part in parts]
    block = rows // 4 if rows % (4 * ROW_TILE) == 0 else rows

    def kernel(*refs):
        out_refs, token_ref = refs[-1 - slots : -1], refs[-1]
        token_ref[...] = jnp.zeros(TOKEN.shape, TOKEN.dtype)
        for slot in range(slots):
            out_refs[slot][...] = low(sum(wide(refs[i][slot]) for i in range(len(parts))))

    found = pl.pallas_call(
        kernel,
        grid=(rows // block,),
        in_specs=[pl.BlockSpec((slots, block, lanes), lambda g: (0, g, 0))] * len(parts)
        + tokens(after)
        + [ANYWHERE] * len(reads),
        out_specs=[pl.BlockSpec((block, lanes), lambda g: (g, 0))] * slots + [TOKEN_SPEC],
        out_shape=[jax.ShapeDtypeStruct((rows, lanes), jnp.bfloat16)] * slots + [TOKEN],
        compiler_params=pltpu.CompilerParams(vmem_limit_bytes=VMEM_BYTES),
        cost_estimate=cost(2),
        name="add_slots",
    )(*parts, *after, *reads)
    return found[:slots], found[slots]


def place_conv_grads(stacks, blocks, taps, slab, places, sizes):
    cores, seqs, acrosses = sizes[:3]
    peers, rows, lanes = stacks[0].shape
    channels = slab * seqs * acrosses
    if slab % ROW_TILE or rows % slab:
        full = jnp.stack([each[:, : blocks * taps * slab] for each in stacks])
        full = full.reshape(cores, seqs, acrosses, blocks, taps, slab, lanes)
        for axis, (place, size) in enumerate(zip(places[:3], sizes[:3])):
            full = relative(full, axis, place, size)
        return wide(
            full.transpose(3, 4, 1, 2, 5, 0, 6).reshape(blocks, taps, channels, cores * lanes)
        )
    stacks = [each.reshape(peers, rows // slab, slab, lanes) for each in stacks]

    def kernel(place_ref, *refs):
        out_ref = refs[-1]
        for c in range(cores):
            lane = pl.multiple_of(lax.rem(place_ref[0] - c + cores, cores) * lanes, lanes)
            for s in range(seqs):
                at_s = lax.rem(place_ref[1] - s + seqs, seqs)
                for a in range(acrosses):
                    at_a = lax.rem(place_ref[2] - a + acrosses, acrosses)
                    row = pl.multiple_of((at_s * acrosses + at_a) * slab, slab)
                    for b in range(blocks):
                        piece = wide(refs[c * blocks + b][s * acrosses + a, 0])
                        out_ref[b, 0, pl.ds(row, slab), pl.ds(lane, lanes)] = piece

    specs = [
        pl.BlockSpec((peers, 1, slab, lanes), lambda k, place, b=b: (0, b * taps + k, 0, 0))
        for b in range(blocks)
    ]
    return pl.pallas_call(
        kernel,
        grid_spec=pltpu.PrefetchScalarGridSpec(
            num_scalar_prefetch=1,
            grid=(taps,),
            in_specs=specs * cores,
            out_specs=pl.BlockSpec(
                (blocks, 1, channels, cores * lanes), lambda k, place: (0, k, 0, 0)
            ),
        ),
        out_shape=jax.ShapeDtypeStruct((blocks, taps, channels, cores * lanes), jnp.float32),
        compiler_params=pltpu.CompilerParams(vmem_limit_bytes=VMEM_BYTES),
        cost_estimate=cost(5),
        name="place_conv_grads",
    )(
        jnp.stack(places[:3]).astype(jnp.int32),
        *[each for stack in stacks for each in [stack] * blocks],
    )


def copy_all(copies):
    for copy in copies:
        copy.start()
    for copy in copies:
        copy.wait()


def place_conv(pieces, places, sizes, after=(), reads=()):
    cores, seqs, acrosses, tap_peers = sizes
    taps, slab, lanes = pieces[0][0].shape[2:]
    inner = slab * seqs * acrosses * tap_peers
    if slab % ROW_TILE:
        full = jnp.stack([jnp.stack(row) for row in pieces])
        for axis, (place, size) in enumerate(zip(places, sizes)):
            full = relative(full, axis, place, size)
        return full.transpose(4, 3, 1, 2, 5, 0, 6).reshape(taps, inner, cores * lanes), after
    flat = [piece for row in pieces for piece in row]

    def kernel(place_ref, *refs):
        out_ref, token_ref, sem_ref = refs[-3:]
        token_ref[...] = jnp.zeros(TOKEN.shape, TOKEN.dtype)
        copies = []
        for c in range(cores):
            lane = lax.rem(place_ref[0] - c + cores, cores) * lanes
            for s in range(seqs):
                at_s = lax.rem(place_ref[1] - s + seqs, seqs)
                for a in range(acrosses):
                    at_a = lax.rem(place_ref[2] - a + acrosses, acrosses)
                    for t in range(tap_peers):
                        at_t = lax.rem(place_ref[3] - t + tap_peers, tap_peers)
                        row = ((at_t * seqs + at_s) * acrosses + at_a) * slab
                        copies.append(
                            pltpu.make_async_copy(
                                refs[c * seqs + s].at[a, t],
                                out_ref.at[
                                    :,
                                    pl.ds(pl.multiple_of(row, slab), slab),
                                    pl.ds(pl.multiple_of(lane, lanes), lanes),
                                ],
                                sem_ref.at[len(copies)],
                            )
                        )
        copy_all(copies)

    found = pl.pallas_call(
        kernel,
        in_specs=[SCALARS] + [ANYWHERE] * (len(flat) + len(reads)) + [WHOLE] * len(after),
        out_specs=[WHOLE] * 2,
        out_shape=[pltpu.HBM((taps, inner, cores * lanes), jnp.bfloat16), TOKEN],
        scratch_shapes=[pltpu.SemaphoreType.DMA((cores * seqs * acrosses * tap_peers,))],
        compiler_params=pltpu.CompilerParams(vmem_limit_bytes=VMEM_BYTES),
        cost_estimate=cost(3),
        name="place_conv",
    )(jnp.stack(places).astype(jnp.int32), *flat, *reads, *after)
    return found[0], (found[1],)


def place_ffn(pieces, sizes, after=(), reads=()):
    cores, seqs, acrosses, tap_peers = sizes
    cuts, ffn_rows, lanes = pieces[0][0].shape[2:]
    cuts //= 2
    width = cuts * lanes
    units = seqs * acrosses * tap_peers * ffn_rows
    if ffn_rows % ROW_TILE:
        full = jnp.stack([jnp.stack(row) for row in pieces])
        full = full.reshape(cores, acrosses, seqs, tap_peers, 2, cuts, ffn_rows, lanes)
        full = full.transpose(4, 0, 1, 2, 3, 6, 5, 7).reshape(2, cores, units, width)
        return [full[0, c] for c in range(cores)], [full[1, c] for c in range(cores)], after
    flat = [piece for row in pieces for piece in row]

    def kernel(*refs):
        out_refs = refs[-2 - 2 * cores : -2]
        token_ref, sem_ref = refs[-2:]
        token_ref[...] = jnp.zeros(TOKEN.shape, TOKEN.dtype)
        copies = []
        for c in range(cores):
            for a in range(acrosses):
                for which in range(2):
                    for cut in range(cuts):
                        copies.append(
                            pltpu.make_async_copy(
                                refs[c * acrosses + a].at[:, :, which * cuts + cut],
                                out_refs[which * cores + c].at[
                                    a, :, :, :, pl.ds(cut * lanes, lanes)
                                ],
                                sem_ref.at[len(copies)],
                            )
                        )
        copy_all(copies)

    shape = pltpu.HBM((acrosses, seqs, tap_peers, ffn_rows, width), jnp.bfloat16)
    found = pl.pallas_call(
        kernel,
        in_specs=[ANYWHERE] * (len(flat) + len(reads)) + [WHOLE] * len(after),
        out_specs=[WHOLE] * (2 * cores + 1),
        out_shape=[shape] * (2 * cores) + [TOKEN],
        scratch_shapes=[pltpu.SemaphoreType.DMA((2 * cores * acrosses * cuts,))],
        compiler_params=pltpu.CompilerParams(vmem_limit_bytes=VMEM_BYTES),
        cost_estimate=cost(2),
        name="place_ffn",
    )(*flat, *reads, *after)
    token = found[-1]
    found = [each.reshape(units, width) for each in found[:-1]]
    return found[:cores], found[cores:], (token,)


class Ring:
    def __init__(self, axis, size, index, pairs):
        self.axis, self.size, self.index, self.pairs = axis, size, index, pairs

    def shifted(self, value, by):
        return lax.ppermute(value, self.axis, self.pairs(lambda i: (i + by) % self.size))

    def swapped(self, value, bit):
        return lax.ppermute(value, self.axis, self.pairs(lambda i: i ^ bit))

    def gather(self, value):
        return [value] + [self.shifted(value, by) for by in range(1, self.size)]

    def swap(self, values):
        return [values[0]] + [self.shifted(values[by], -by) for by in range(1, self.size)]


def relative(value, axis, place, size):
    if size == 1:
        return value
    return jnp.stack(
        [
            lax.dynamic_index_in_dim(value, (place - slot) % size, axis, False)
            for slot in range(size)
        ],
        axis,
    )


def rings():
    peers = lax.axis_size("dp")
    cores = CORES if peers % CORES == 0 else 1
    columns = peers // cores
    place = lax.axis_index("dp")

    def plain(axis):
        size = lax.axis_size(axis)
        return Ring(
            axis, size, lax.axis_index(axis), lambda move: [(i, move(i)) for i in range(size)]
        )

    across = Ring(
        "dp",
        columns,
        place // cores,
        lambda move: [(i, move(i // cores) * cores + i % cores) for i in range(peers)],
    )
    core = Ring(
        "dp",
        cores,
        place % cores,
        lambda move: [(i, i // cores * cores + move(i % cores)) for i in range(peers)],
    )
    return core, across, plain("seq"), plain("tap")


class Reduce:
    def __init__(self, terms, order):
        self.order = order
        self.parts = [terms[0]] + [order[0].shifted(terms[s], -s) for s in range(1, order[0].size)]

    def step(self, level, after, reads=()):
        ring = self.order[level]
        found, token = add_slots(self.parts, ring.size, after, reads)
        self.parts = [found[0]] + [ring.shifted(found[s], -s) for s in range(1, ring.size)]
        return (token,)


def shared_copies(value, across, seq):
    peers, spans = lax.axis_size("dp"), lax.axis_size("seq")
    cores = peers // across.size

    def target(place, by_a, by_s):
        dp, at = place // spans, place % spans
        moved = (dp // cores + by_a) % across.size * cores + dp % cores
        return moved * spans + (at + by_s) % spans

    return [
        [
            value
            if by_a == by_s == 0
            else lax.ppermute(
                value,
                ("dp", "seq"),
                [(place, target(place, by_a, by_s)) for place in range(peers * spans)],
            )
            for by_a in range(across.size)
        ]
        for by_s in range(seq.size)
    ]


def passed_along(value, axis, by):
    peers = lax.axis_size(axis)
    pairs = [(i, i + by) for i in range(peers) if 0 <= i + by < peers]
    return lax.ppermute(value, axis, pairs)


def rims(source, reach_rows, seq, rim=None):
    span_rows = source.shape[0]
    if seq.size == 2 and reach_rows <= span_rows:
        if rim is None:
            first = (1 - seq.index) * (span_rows - reach_rows)
            rim = lax.dynamic_slice_in_dim(source, first, reach_rows, 0)
        return seq.shifted(rim, 1)
    left_parts = []
    right_parts = []
    distances = -(-reach_rows // span_rows)
    for distance in range(1, distances + 1):
        rim_count = min(span_rows, reach_rows - (distance - 1) * span_rows)
        left_parts.insert(0, passed_along(source[span_rows - rim_count :], "seq", distance))
        right_parts.append(passed_along(source[:rim_count], "seq", -distance))
    return left_parts, right_parts


def extend(source, found, seq, after=()):
    if isinstance(found, tuple):
        return join_rows(found[0] + [source] + found[1], after)
    reach, span = found.shape[0], source.shape[0]

    def kernel(place_ref, found_ref, source_ref, *refs):
        out_ref, token_ref = refs[-2:]
        token_ref[...] = jnp.zeros(TOKEN.shape, TOKEN.dtype)
        out_ref[reach : reach + span] = source_ref[...]
        zeros = jnp.zeros(found.shape, found.dtype)

        @pl.when(place_ref[0] == 0)
        def _():
            out_ref[:reach] = zeros
            out_ref[reach + span :] = found_ref[...]

        @pl.when(place_ref[0] != 0)
        def _():
            out_ref[:reach] = found_ref[...]
            out_ref[reach + span :] = zeros

    shape = jax.ShapeDtypeStruct((span + 2 * reach, source.shape[1]), source.dtype)
    extended, token = pl.pallas_call(
        kernel,
        in_specs=[SCALARS] + [WHOLE] * (2 + len(after)),
        out_specs=[WHOLE] * 2,
        out_shape=[shape, TOKEN],
        compiler_params=pltpu.CompilerParams(vmem_limit_bytes=VMEM_BYTES),
        cost_estimate=cost(1.5),
        name="extend",
    )(seq.index.astype(jnp.int32)[None], found, source, *after)
    return extended, (token,)


def to_rows(values):
    windows, positions = values.shape[:2]
    cut = values.reshape((windows, positions // FIRST_DILATION, FIRST_DILATION) + values.shape[2:])
    return jnp.swapaxes(cut, 0, 1).reshape((windows * positions,) + values.shape[2:])


def from_rows(values, windows):
    cut = values.reshape((-1, windows, FIRST_DILATION) + values.shape[1:])
    return jnp.swapaxes(cut, 0, 1).reshape((windows, -1) + values.shape[1:])


def on_device(
    inputs,
    targets,
    masked,
    conv_weight,
    conv_bias,
    gains,
    shifts,
    in_weight,
    in_bias,
    out_weight,
    out_bias,
    head_weight,
):
    core, across, seq, tap = rings()
    taps = conv_weight.shape[1]
    channels = conv_weight.shape[2]
    width = conv_weight.shape[3]
    slab = channels // (seq.size * across.size)
    lanes = width // core.size
    hidden_width = in_bias.shape[1]
    ffn_rows = in_weight.shape[2]
    windows = inputs.shape[0]
    rows = windows * inputs.shape[1]
    steps = (FIRST_DILATION * windows, SECOND_DILATION * windows)
    units = hidden_width // core.size
    places = (core.index, seq.index, across.index, tap.index)
    sizes = (core.size, seq.size, across.size, tap.size)

    in_bias_placed = []
    for b in range(2):
        bias = in_bias[b].reshape(across.size, core.size, seq.size, tap.size, ffn_rows)
        for axis, ring in enumerate((across, core, seq, tap)):
            bias = relative(bias, axis, ring.index, ring.size)
        in_bias_placed.append(bias.transpose(1, 0, 2, 3, 4).reshape(core.size, units))

    def cut_ffn(piece):
        return piece.reshape(ffn_rows, core.size, lanes).swapaxes(0, 1).reshape(-1, lanes)

    def bundle(b):
        conv_piece = lax.dynamic_slice(
            conv_weight[b],
            (0, (seq.index * across.size + across.index) * slab, core.index * lanes),
            (taps, slab, lanes),
        )
        pieces = [
            conv_piece.reshape(taps * slab, lanes),
            cut_ffn(in_weight[b].T),
            cut_ffn(out_weight[b]),
        ]
        return jnp.concatenate(pieces)

    cuts = (
        (0, taps * slab, (taps, slab, lanes)),
        (taps * slab, taps * slab + 2 * core.size * ffn_rows, (2 * core.size, ffn_rows, lanes)),
    )

    def straight(arrays):
        return (arrays, ((0, None, arrays[0].shape),))

    conv_input = to_rows(inputs)
    stream = conv_input
    codes = to_rows(targets + masked * head_weight.shape[1])
    codes = jnp.broadcast_to(codes[:, None], (rows, 128))

    tap_parts = tap.gather(bundle(0))
    (conv_part, ffn_part), last = restack([(tap_parts, cuts)], reads=[conv_input])
    split = (tap.size + 1) // 2
    (behind,), last = hold([bundle(1)], last)
    late_parts = tap.gather(behind)
    extended, last = extend(conv_input, rims(conv_input, taps // 2 * steps[0], seq), seq, last)
    extended_parts = [extended] + [core.shifted(extended, -c) for c in range(1, core.size)]
    conv_parts, ffn_parts = across.gather(conv_part), seq.gather(ffn_part)
    (conv_part, ffn_part), last = restack(
        [straight(conv_parts), straight(ffn_parts)],
        reads=[late_parts[by] for by in range(1, tap.size) if by != split],
        after=last,
    )
    conv_parts, ffn_parts = seq.gather(conv_part), across.gather(ffn_part)
    conv_slots = [core.gather(conv_part)]
    ffn_slots = [core.gather(ffn_part)]
    held, last = hold(
        conv_parts[1:] + ffn_parts[1:],
        last,
        conv_slots[0][1:] + ffn_slots[0][1:] + late_parts[1:],
    )
    conv_slots += [core.gather(each) for each in held[: seq.size - 1]]
    ffn_slots += [core.gather(each) for each in held[seq.size - 1 :]]
    (late_conv, late_ffn), last = restack([(late_parts, cuts)], after=last)
    late_conv_parts, late_ffn_parts = across.gather(late_conv), seq.gather(late_ffn)

    def turned(slots):
        return [[each[c] for each in slots] for c in range(core.size)]

    conv_full, in_full, out_full = [None, None], [None, None], [None, None]
    conv_full[0], last = place_conv(
        turned(conv_slots), places, sizes, last, [part for each in ffn_slots for part in each[1:]]
    )
    reaches = [taps // 2 * step for step in steps]
    rim_reaches = [reach if seq.size == 2 and reach <= rows else 0 for reach in reaches]
    saved = []
    reads = []
    rim = None
    for b in range(2):
        if b == 1:
            found = rims(conv_input, reaches[1], seq, rim)
            held, last = hold(late_conv_parts[1:] + late_ffn_parts[1:], last)
            late_conv_slots += [core.gather(each) for each in held[: seq.size - 1]]
            late_ffn_slots += [core.gather(each) for each in held[seq.size - 1 :]]
            conv_full[1], last = place_conv(turned(late_conv_slots), places, sizes, last)
            in_full[1], out_full[1], last = place_ffn(turned(late_ffn_slots), sizes, last)
            extended, last = extend(conv_input, found, seq, last)
            extended_parts = [extended] + [core.shifted(extended, -c) for c in range(1, core.size)]
        (normed_conv, conv_slope, stream, lowered), last = conv_forward(
            extended,
            conv_full[b],
            stream,
            conv_bias[b],
            gains[b, 0],
            shifts[b, 0],
            steps[b],
            last,
            reads,
        )
        reads = extended_parts[1:]
        if b == 0:
            (late_conv, late_ffn), last = restack(
                [straight(late_conv_parts), straight(late_ffn_parts)], after=last
            )
            late_conv_parts, late_ffn_parts = seq.gather(late_conv), across.gather(late_ffn)
            late_conv_slots = [core.gather(late_conv)]
            late_ffn_slots = [core.gather(late_ffn)]
            in_full[0], out_full[0], last = place_ffn(turned(ffn_slots), sizes, last)
            reads = reads + late_conv_slots[0][1:] + late_ffn_slots[0][1:]
        active, hidden_slopes, (normed_ffn, scale_ffn, stream, conv_input), packets, rim, last = (
            ffn_forward(
                lowered,
                stream,
                in_full[b],
                out_full[b],
                [in_bias_placed[b][c] for c in range(core.size)],
                out_bias[b],
                gains[b, 1],
                shifts[b, 1],
                seq.index,
                rim_reaches[1] if b == 0 else 0,
                last,
                reads,
            )
        )
        packets = [core.shifted(packet, -1 - c) for c, packet in enumerate(packets)]
        reads = packets
        saved.append(
            (
                extended_parts,
                conv_slope,
                normed_conv,
                (active, lowered, packets),
                hidden_slopes,
                normed_ffn,
                scale_ffn,
            )
        )

    final_state = from_rows(conv_input, windows)
    (stream_grad, head_grad, loss_rows), last = head_and_loss(stream, head_weight, codes, last)

    ffn_rows_of_sums = [None, None]
    conv_rows_of_sums = [None, None]
    in_bias_grads = [None, None]
    ffn_sums = [None, None]
    conv_sums = [None, None]
    merged = [None, None]

    def groups(halves):
        half = (tap.size + 1) // 2
        return [(each.parts, slots) for each, slots in zip(halves, (half, tap.size - half))]

    for b in (1, 0):
        (
            extended_parts,
            conv_slope,
            normed_conv,
            active_pair,
            hidden_slopes,
            normed_ffn,
            scale_ffn,
        ) = saved[b]
        output_grad, hidden_grad, biases, packets, ffn_rows_of_sums[b], last = ffn_back_hidden(
            stream_grad, normed_ffn, scale_ffn, gains[b, 1], out_full[b], hidden_slopes, last
        )
        if b == 1:
            arrived_packets = [core.shifted(packet, -1 - c) for c, packet in enumerate(packets)]
        if b == 0:
            for each in ffn_sums[1]:
                last = each.step(1, last)
            for each in conv_sums[1]:
                last = each.step(1, last)
        stream_grad, conv_grad, conv_cuts, relayed, rim, conv_rows_of_sums[b], last = ffn_back_stream(
            stream_grad,
            hidden_grad,
            packets,
            in_full[b],
            normed_conv,
            conv_slope,
            gains[b, 0],
            places,
            rim_reaches[b],
            last,
            reads,
            relay=b == 0,
        )
        reads = []
        if b == 0:
            merged[1], last = merge_slots(
                groups(conv_sums[1]), groups(ffn_sums[1]), last
            )
            sent = [rim] if rim is not None else []
            held, last = hold(list(conv_cuts) + list(relayed) + sent, last)
            conv_cuts, relayed = held[: core.size - 1], held[core.size - 1 : 2 * core.size - 2]
            rim = held[-1] if sent else None
            merged[1] = tap.swap(merged[1])
            arrived_packets = [core.shifted(packet, -1 - c) for c, packet in enumerate(relayed)]
        arrived = [core.shifted(conv_cuts[c - 1], -c) for c in range(1, core.size)]
        in_bias_grads[b] = list(biases)
        found_rims = rims(conv_grad, reaches[b], seq, rim)

        def ffn_grads(last):
            active, lowered, packets = active_pair
            if core.size == 1:
                packets = []
            first, second, token = ffn_weight_grad(
                (
                    (hidden_grad, lowered, [(g, p) for g, p in zip(arrived_packets, packets)]),
                    (active, output_grad, [(p, g) for g, p in zip(arrived_packets, packets)]),
                ),
                sizes,
                ffn_rows,
                last,
            )
            found = [Reduce(first, (across, seq))]
            if second:
                found.append(Reduce(second, (seq, across)))
            return found, (token,)

        def conv_grads(last, reads=()):
            first, second, token = conv_weight_grad(
                extended_parts, conv_grad, arrived, places, sizes, taps, steps[b], last, reads
            )
            found = [Reduce(first, (seq, across))]
            if second:
                found.append(Reduce(second, (across, seq)))
            return found, (token,)

        if b == 1:
            ffn_sums[1], last = ffn_grads(last)
            extended_grad, last = extend(conv_grad, found_rims, seq, last)
            conv_sums[1], last = conv_grads(last)
        else:
            conv_sums[0], last = conv_grads(last, arrived_packets)
            extended_grad, last = extend(conv_grad, found_rims, seq, last)
            ffn_sums[0], last = ffn_grads(last)
            for each in conv_sums[0]:
                last = each.step(1, last, merged[1][1:] + [final_state])
        stream_grad, last = conv_data_grad(
            extended_grad,
            conv_full[b],
            stream_grad,
            steps[b],
            jnp.float32 if b == 1 else jnp.bfloat16,
            last,
        )

    grad_inputs = from_rows(stream_grad, windows)

    row_groups = [(each, 3) for each in conv_rows_of_sums + ffn_rows_of_sums]
    row_groups.append((head_grad, head_weight.shape[1]))
    packed, last = pack_small(row_groups, in_bias_grads, loss_rows, places, sizes, ffn_rows, last)

    conv_rows = taps * slab
    merged[0], last = append_slots(groups(conv_sums[0]), [packed], last)
    merged[0] = tap.swap(merged[0])
    for each in ffn_sums[0]:
        last = each.step(1, last)
    shards, last = finish_conv([merged[0], merged[1]], conv_rows, packed.shape[0], last)
    ffn_late, last = append_slots(groups(ffn_sums[0]), [], last, [grad_inputs])
    ffn_late = tap.swap(ffn_late)
    copies = [each for row in shared_copies(shards, across, seq) for each in row]
    grad_in, grad_out, last = finish_ffn(merged[1], ffn_late, conv_rows, ffn_rows, last)
    (stack,), last = restack([straight(copies)], after=last)
    stacks = core.gather(stack)
    (
        grad_conv_bias,
        grad_gains,
        grad_shifts,
        grad_in_bias,
        grad_out_bias,
        grad_head_weight,
        loss,
    ) = finish_small(
        stacks, 2 * conv_rows, width, head_weight.shape[1], hidden_width, places, sizes
    )
    grad_conv = place_conv_grads(stacks, 2, taps, slab, places, sizes)
    return (
        final_state,
        grad_inputs,
        grad_conv,
        grad_conv_bias,
        grad_gains,
        grad_shifts,
        grad_in,
        grad_in_bias,
        grad_out,
        grad_out_bias,
        grad_head_weight,
        loss.reshape(()),
    )


def solution(mesh):
    placed = (
        P(("dp", "tap"), "seq", None),
        P(("dp", "tap"), "seq"),
        P(("dp", "tap"), "seq"),
        P(None, None, "tap", None),
        P(),
        P(),
        P(),
        P(None, None, ("dp", "seq", "tap")),
        P(),
        P(None, ("dp", "seq", "tap"), None),
        P(),
        P(),
    )
    return jax.shard_map(
        on_device,
        mesh=mesh,
        in_specs=placed,
        out_specs=(
            P(("dp", "tap"), "seq", None),
            P(("dp", "tap"), "seq", None),
            P(None, None, "tap", None),
            P(),
            P(),
            P(),
            P(None, None, ("dp", "seq", "tap")),
            P(),
            P(None, ("dp", "seq", "tap"), None),
            P(),
            P(),
            P(),
        ),
        check_vma=False,
    )
```

```python
import functools

import jax
import jax.numpy as jnp
import numpy as np
from jax import lax
from jax.experimental import pallas as pl
from jax.experimental.pallas import tpu as pltpu
from jax.sharding import PartitionSpec as P

FIRST_DILATION = 4
SECOND_DILATION = 32
EPSILON = 1e-05
HIGHEST_PRECISION = lax.Precision.HIGHEST
CORES = 2
ROW_TILE = 16
MIB = 1024 * 1024
VMEM_BYTES = 20 * MIB
ANYWHERE = pl.BlockSpec(memory_space=pl.ANY)
SCALARS = pl.BlockSpec(memory_space=pltpu.SMEM)


TOKEN = jax.ShapeDtypeStruct((8, 128), jnp.float32)


def cost(microseconds):
    size = int(microseconds * 3.5e6)
    return pl.CostEstimate(flops=int(microseconds * 1.1e9), bytes_accessed=size, transcendentals=0)


WHOLE = pl.BlockSpec(memory_space=pltpu.VMEM)
TOKEN_SPEC = pl.BlockSpec(TOKEN.shape, lambda *_: (0, 0))


def tokens(after):
    return [TOKEN_SPEC] * len(after)


def in_hbm(array):
    return pltpu.with_memory_space_constraint(array, pltpu.HBM)


def low(values):
    return values.astype(jnp.bfloat16)


def wide(values):
    return values.astype(jnp.float32)


def gelu_parts(values):
    phi = 0.5 * (1.0 + lax.erf(values * 0.7071067811865476))
    return (
        values * phi,
        phi + values * jnp.exp(-0.5 * values * values) * 0.3989422804014327,
    )


def normalize(values):
    center = values - jnp.mean(values, -1, keepdims=True)
    scale = lax.rsqrt(jnp.mean(center * center, -1, keepdims=True) + EPSILON)
    return (center * scale, scale)


def norm_back(upstream, normed, scale):
    return scale * (
        upstream
        - jnp.mean(upstream, -1, keepdims=True)
        - normed * jnp.mean(upstream * normed, -1, keepdims=True)
    )


def tap_groups(taps):
    return 3 if taps % 3 == 0 else 1


def row_chunks(rows, most):
    size = min(rows, most)
    return [(first, size) for first in range(0, rows, size)]


def conv_forward(extended, weight, stream, bias, gain, shift, step, after=(), reads=()):
    taps, inner, width = weight.shape
    rows = stream.shape[0]
    group = tap_groups(taps)
    steps = taps // group

    def kernel(extended_ref, weight_ref, stream_ref, bias_ref, gain_ref, shift_ref, *refs):
        normed_ref, slope_ref, next_ref, lowered_ref, token_ref, total_ref = refs[-6:]
        token_ref[...] = jnp.zeros(TOKEN.shape, TOKEN.dtype)
        first = pl.program_id(0) * group
        total = None
        for j in range(group):
            start = pl.multiple_of((first + j) * step, ROW_TILE)
            term = jnp.dot(
                extended_ref[pl.ds(start, rows), :],
                weight_ref[j],
                preferred_element_type=jnp.float32,
            )
            total = term if total is None else total + term

        @pl.when(pl.program_id(0) == 0)
        def _():
            total_ref[...] = total

        @pl.when(pl.program_id(0) > 0)
        def _():
            total_ref[...] += total

        @pl.when(pl.program_id(0) == steps - 1)
        def _():
            for at, size in row_chunks(rows, 128):
                some = pl.ds(at, size)
                value, slope = gelu_parts(total_ref[some, :] + bias_ref[...])
                normed, scale = normalize(value)
                mid = wide(stream_ref[some, :]) + normed * gain_ref[...] + shift_ref[...]
                normed_ref[some, :] = low(normed)
                slope_ref[some, :] = low(scale * slope)
                next_ref[some, :] = mid
                lowered_ref[some, :] = low(mid)

    whole = pl.BlockSpec((rows, width), lambda g: (0, 0))
    row = pl.BlockSpec((1, width), lambda g: (0, 0))
    found = pl.pallas_call(
        kernel,
        grid=(steps,),
        in_specs=[
            pl.BlockSpec(extended.shape, lambda g: (0, 0)),
            pl.BlockSpec((group, inner, width), lambda g: (g, 0, 0)),
            whole,
            row,
            row,
            row,
        ]
        + tokens(after)
        + [ANYWHERE] * len(reads),
        out_specs=[whole] * 4 + [TOKEN_SPEC],
        out_shape=[
            pltpu.HBM((rows, width), jnp.bfloat16),
            pltpu.HBM((rows, width), jnp.bfloat16),
            pltpu.HBM((rows, width), jnp.float32),
            jax.ShapeDtypeStruct((rows, width), jnp.bfloat16),
            TOKEN,
        ],
        scratch_shapes=[pltpu.VMEM((rows, width), jnp.float32)],
        compiler_params=pltpu.CompilerParams(vmem_limit_bytes=VMEM_BYTES),
        cost_estimate=cost(9),
        name="conv_forward",
    )(extended, in_hbm(weight), in_hbm(stream) if stream.dtype == jnp.float32 else stream, bias[None], gain[None], shift[None], *after, *reads)
    return found[:4], (found[4],)


def ffn_forward(
    lowered,
    stream,
    ins,
    outs,
    in_biases,
    out_bias,
    gain,
    shift,
    seq_index,
    reach,
    last_block,
    after=(),
    reads=(),
):
    rows, width = lowered.shape
    cores = len(ins)
    units = ins[0].shape[0]
    block = min(units, 256)
    steps = units // block

    rims_out = 1 if reach else 0

    def kernel(place_ref, lowered_ref, stream_ref, out_bias_ref, gain_ref, shift_ref, *refs):
        in_refs, out_refs, bias_refs = (refs[i * cores : (i + 1) * cores] for i in range(3))
        found_refs = refs[-6 - 2 * cores - rims_out :]
        active_ref, slope_refs = found_refs[0], found_refs[1 : 1 + cores]
        normed_ref, scale_ref, next_ref, rounded_ref = found_refs[1 + cores : 5 + cores]
        packet_refs = found_refs[5 + cores : 4 + 2 * cores]
        token_ref, total_ref = found_refs[-2:]
        token_ref[...] = jnp.zeros(TOKEN.shape, TOKEN.dtype)
        lane = pl.multiple_of(width + pl.program_id(0) * block, block)

        @pl.when(pl.program_id(0) == 0)
        def _():
            total_ref[...] = jnp.zeros(total_ref.shape, jnp.float32)
            for packet_ref in packet_refs:
                packet_ref[:, :width] = lowered_ref[...]

        for at, size in row_chunks(rows, 512):
            some = pl.ds(at, size)
            term = None
            for c in range(cores):
                hidden = lax.dot_general(
                    lowered_ref[some, :],
                    in_refs[c][...],
                    (((1,), (1,)), ((), ())),
                    preferred_element_type=jnp.float32,
                )
                active, slope = gelu_parts(hidden + bias_refs[c][...])
                active = low(active)
                if c == 0:
                    active_ref[some, :] = active
                else:
                    packet_refs[c - 1][some, pl.ds(lane, block)] = active
                slope_refs[c][some, :] = low(slope)
                found = jnp.dot(active, out_refs[c][...], preferred_element_type=jnp.float32)
                term = found if term is None else term + found
            total_ref[some, :] += term

        @pl.when(pl.program_id(0) == steps - 1)
        def _():
            for at, size in row_chunks(rows, 128):
                some = pl.ds(at, size)
                normed, scale = normalize(total_ref[some, :] + out_bias_ref[...])
                after_ffn = stream_ref[some, :] + normed * gain_ref[...] + shift_ref[...]
                normed_ref[some, :] = low(normed)
                scale_ref[some, :] = jnp.broadcast_to(scale, (size, 128))
                next_ref[some, :] = after_ffn
                rounded_ref[some, :] = low(after_ffn)
            if reach:
                first = pl.multiple_of((1 - place_ref[0]) * (rows - reach), ROW_TILE)
                found_refs[-3][...] = rounded_ref[pl.ds(first, reach), :]

    whole = pl.BlockSpec((rows, width), lambda g: (0, 0))
    row = pl.BlockSpec((1, width), lambda g: (0, 0))
    piece = pl.BlockSpec((block, width), lambda g: (g, 0))
    columns = pl.BlockSpec((rows, block), lambda g: (0, g))
    hidden_shape = pltpu.HBM((rows, units), jnp.bfloat16)
    found = pl.pallas_call(
        kernel,
        grid=(steps,),
        in_specs=[SCALARS, whole, whole, row, row, row]
        + [piece] * (2 * cores)
        + [pl.BlockSpec((1, block), lambda g: (0, g))] * cores
        + tokens(after)
        + [ANYWHERE] * len(reads),
        out_specs=[columns] * (1 + cores)
        + [whole, pl.BlockSpec((rows, 128), lambda g: (0, 0)), whole, whole]
        + [pl.BlockSpec((rows, width + units), lambda g: (0, 0))] * (cores - 1)
        + [pl.BlockSpec((reach, width), lambda g: (0, 0))] * rims_out
        + [TOKEN_SPEC],
        out_shape=[hidden_shape] * (1 + cores)
        + [
            pltpu.HBM((rows, width), jnp.bfloat16),
            pltpu.HBM((rows, 128), jnp.float32),
            (jax.ShapeDtypeStruct if last_block else pltpu.HBM)((rows, width), jnp.float32),
            jax.ShapeDtypeStruct((rows, width), jnp.bfloat16),
        ]
        + [jax.ShapeDtypeStruct((rows, width + units), jnp.bfloat16)] * (cores - 1)
        + [jax.ShapeDtypeStruct((reach, width), jnp.bfloat16)] * rims_out
        + [TOKEN],
        scratch_shapes=[pltpu.VMEM((rows, width), jnp.float32)],
        compiler_params=pltpu.CompilerParams(vmem_limit_bytes=VMEM_BYTES),
        cost_estimate=cost(11),
        name="ffn_forward",
    )(
        seq_index.astype(jnp.int32)[None],
        lowered,
        in_hbm(stream),
        out_bias[None],
        gain[None],
        shift[None],
        *[in_hbm(each) for each in ins],
        *[in_hbm(each) for each in outs],
        *[each[None] for each in in_biases],
        *after,
        *reads,
    )
    return (
        found[0],
        found[1 : 1 + cores],
        found[1 + cores : 5 + cores],
        found[5 + cores : 4 + 2 * cores],
        found[4 + 2 * cores] if reach else None,
        (found[-1],),
    )


def head_and_loss(stream, head_weight, codes, after=()):
    rows, width = stream.shape
    classes = head_weight.shape[1]
    padded = jnp.pad(head_weight, ((0, 0), (0, 128 - classes)))
    cuts = row_chunks(rows, 256)

    def kernel(stream_ref, head_ref, code_ref, *refs):
        grad_ref, head_grad_ref, sums_ref, token_ref = refs[-4:]
        token_ref[...] = jnp.zeros(TOKEN.shape, TOKEN.dtype)
        head_grad = jnp.zeros((128, width), jnp.float32)
        objective = jnp.zeros((1, 1), jnp.float32)
        scored = jnp.zeros((1, 1), jnp.float32)
        for at, size in cuts:
            some = pl.ds(at, size)
            value = stream_ref[some, :]
            code = code_ref[some, :]
            mask = jnp.where(code[:, :1] >= classes, 1.0, 0.0)
            logits = jnp.dot(
                value, head_ref[...], precision=HIGHEST_PRECISION, preferred_element_type=jnp.float32
            )
            lane = lax.broadcasted_iota(jnp.int32, logits.shape, 1)
            valid = lane < classes
            peak = jnp.max(jnp.where(valid, logits, -jnp.inf), -1, keepdims=True)
            exponent = jnp.where(valid, jnp.exp(jnp.where(valid, logits - peak, 0.0)), 0.0)
            denominator = jnp.sum(exponent, -1, keepdims=True)
            chosen = lane == jnp.where(code >= classes, code - classes, code)
            picked = jnp.sum(jnp.where(chosen, logits, 0.0), -1, keepdims=True)
            terms = mask * (peak + jnp.log(denominator) - picked)
            objective = objective + jnp.sum(terms, 0, keepdims=True)
            scored = scored + jnp.sum(mask, 0, keepdims=True)
            logit_grad = mask * (exponent / denominator - jnp.where(chosen, 1.0, 0.0))
            grad_ref[some, :] = lax.dot_general(
                logit_grad,
                head_ref[...],
                (((1,), (1,)), ((), ())),
                precision=HIGHEST_PRECISION,
                preferred_element_type=jnp.float32,
            )
            head_grad = head_grad + lax.dot_general(
                logit_grad,
                value,
                (((0,), (0,)), ((), ())),
                precision=HIGHEST_PRECISION,
                preferred_element_type=jnp.float32,
            )
        head_grad_ref[...] = head_grad[: head_grad_ref.shape[0]]
        at_row = lax.broadcasted_iota(jnp.int32, sums_ref.shape, 0)
        sums_ref[...] = jnp.where(at_row == 0, objective, scored)

    found = pl.pallas_call(
        kernel,
        out_shape=[
            jax.ShapeDtypeStruct((rows, width), jnp.float32),
            jax.ShapeDtypeStruct((-(-classes // 8) * 8, width), jnp.float32),
            jax.ShapeDtypeStruct((8, 128), jnp.float32),
            TOKEN,
        ],
        compiler_params=pltpu.CompilerParams(vmem_limit_bytes=VMEM_BYTES),
        cost_estimate=cost(6),
        name="head_and_loss",
    )(stream, padded, codes, *after)
    return found[:3], (found[3],)


def ffn_back_hidden(upstream, normed, scale, gain, outs, slopes, after=()):
    rows, width = upstream.shape
    cores = len(outs)
    units = outs[0].shape[0]
    block = min(units, 256)

    def kernel(upstream_ref, normed_ref, scale_ref, gain_ref, *refs):
        out_refs, slope_refs = refs[:cores], refs[cores : 2 * cores]
        found_refs = refs[-3 - 2 * cores :]
        output_grad_ref, hidden_ref = found_refs[:2]
        bias_refs, packet_refs = found_refs[2 : 2 + cores], found_refs[2 + cores : -2]
        sums_ref, token_ref = found_refs[-2:]
        token_ref[...] = jnp.zeros(TOKEN.shape, TOKEN.dtype)
        lane = pl.multiple_of(width + pl.program_id(0) * block, block)

        @pl.when(pl.program_id(0) == 0)
        def _():
            totals = [jnp.zeros((1, width), jnp.float32)] * 3
            for at, size in row_chunks(rows, 128):
                some = pl.ds(at, size)
                grad, value = upstream_ref[some, :], wide(normed_ref[some, :])
                output_grad = low(norm_back(grad * gain_ref[...], value, scale_ref[some, :1]))
                output_grad_ref[some, :] = output_grad
                for packet_ref in packet_refs:
                    packet_ref[some, :width] = output_grad
                for i, each in enumerate((grad * value, grad, wide(output_grad))):
                    totals[i] = totals[i] + jnp.sum(each, 0, keepdims=True)
            sums_ref[...] = jnp.zeros(sums_ref.shape, jnp.float32)
            for i in range(3):
                sums_ref[i : i + 1, :] = totals[i]

        for c in range(cores):
            total = jnp.zeros((1, block), jnp.float32)
            for at, size in row_chunks(rows, 512):
                some = pl.ds(at, size)
                active_grad = lax.dot_general(
                    output_grad_ref[some, :],
                    out_refs[c][...],
                    (((1,), (1,)), ((), ())),
                    preferred_element_type=jnp.float32,
                )
                hidden_grad = low(active_grad * wide(slope_refs[c][some, :]))
                if c == 0:
                    hidden_ref[some, :] = hidden_grad
                else:
                    packet_refs[c - 1][some, pl.ds(lane, block)] = hidden_grad
                total = total + jnp.sum(wide(hidden_grad), 0, keepdims=True)
            bias_refs[c][...] = total

    whole = pl.BlockSpec((rows, width), lambda g: (0, 0))
    columns = pl.BlockSpec((rows, block), lambda g: (0, g))
    found = pl.pallas_call(
        kernel,
        grid=(units // block,),
        in_specs=[
            whole,
            whole,
            pl.BlockSpec((rows, 128), lambda g: (0, 0)),
            pl.BlockSpec((1, width), lambda g: (0, 0)),
        ]
        + [pl.BlockSpec((block, width), lambda g: (g, 0))] * cores
        + [columns] * cores
        + tokens(after),
        out_specs=[whole, columns]
        + [pl.BlockSpec((1, block), lambda g: (0, g))] * cores
        + [pl.BlockSpec((rows, width + units), lambda g: (0, 0))] * (cores - 1)
        + [pl.BlockSpec((8, width), lambda g: (0, 0)), TOKEN_SPEC],
        out_shape=[
            jax.ShapeDtypeStruct((rows, width), jnp.bfloat16),
            pltpu.HBM((rows, units), jnp.bfloat16),
        ]
        + [jax.ShapeDtypeStruct((1, units), jnp.float32)] * cores
        + [jax.ShapeDtypeStruct((rows, width + units), jnp.bfloat16)] * (cores - 1)
        + [jax.ShapeDtypeStruct((8, width), jnp.float32), TOKEN],
        compiler_params=pltpu.CompilerParams(vmem_limit_bytes=VMEM_BYTES),
        cost_estimate=cost(6),
        name="ffn_back_hidden",
    )(
        upstream,
        in_hbm(normed),
        in_hbm(scale),
        gain[None],
        *[in_hbm(each) for each in outs],
        *[in_hbm(each) for each in slopes],
        *after,
    )
    return (
        found[0],
        found[1],
        found[2 : 2 + cores],
        found[2 + cores : -2],
        found[-2],
        (found[-1],),
    )


def ffn_back_stream(
    upstream, hidden, packets, ins, normed, slope, gain, places, reach, after=(), reads=(), relay=False
):
    rows, width = upstream.shape
    cores = len(ins)
    units = ins[0].shape[0]
    block = min(units, 256)
    steps = units // block
    lanes = width // cores
    relays = cores - 1 if relay else 0
    rims_out = 1 if reach else 0

    def kernel(core_ref, upstream_ref, normed_ref, slope_ref, gain_ref, *refs):
        hidden_refs, in_refs = refs[:cores], refs[cores : 2 * cores]
        found_refs = refs[-4 - cores - relays - rims_out :]
        mid_ref, conv_grad_ref = found_refs[:2]
        cut_refs = found_refs[2 : 1 + cores]
        sums_ref, token_ref, total_ref = found_refs[-3:]
        token_ref[...] = jnp.zeros(TOKEN.shape, TOKEN.dtype)
        for i in range(relays):
            relay_ref = found_refs[1 + cores + i]
            lane = pl.multiple_of(width + pl.program_id(0) * block, block)
            relay_ref[:, pl.ds(lane, block)] = hidden_refs[1 + i][...]

            @pl.when(pl.program_id(0) == 0)
            def _(i=i, relay_ref=relay_ref):
                relay_ref[:, :width] = refs[2 * cores + i][...]

        @pl.when(pl.program_id(0) == 0)
        def _():
            total_ref[...] = upstream_ref[...]

        for at, size in row_chunks(rows, 512):
            some = pl.ds(at, size)
            total_ref[some, :] += sum(
                jnp.dot(
                    hidden_refs[c][some, :], in_refs[c][...], preferred_element_type=jnp.float32
                )
                for c in range(cores)
            )

        @pl.when(pl.program_id(0) == steps - 1)
        def _():
            totals = [jnp.zeros((1, width), jnp.float32)] * 3
            for at, size in row_chunks(rows, 128):
                some = pl.ds(at, size)
                grad, value = total_ref[some, :], wide(normed_ref[some, :])
                conv_grad = low(norm_back(grad * gain_ref[...], value, wide(slope_ref[some, :])))
                mid_ref[some, :] = grad
                conv_grad_ref[some, :] = conv_grad
                for i, each in enumerate((grad * value, grad, wide(conv_grad))):
                    totals[i] = totals[i] + jnp.sum(each, 0, keepdims=True)
            sums_ref[...] = jnp.zeros(sums_ref.shape, jnp.float32)
            for i in range(3):
                sums_ref[i : i + 1, :] = totals[i]
            for c in range(1, cores):
                first = lax.rem(core_ref[0] - c + cores, cores) * lanes
                cut_refs[c - 1][...] = conv_grad_ref[:, pl.ds(pl.multiple_of(first, lanes), lanes)]
            if reach:
                first = pl.multiple_of((1 - core_ref[1]) * (rows - reach), ROW_TILE)
                found_refs[-4][...] = conv_grad_ref[pl.ds(first, reach), :]

    whole = pl.BlockSpec((rows, width), lambda g, core: (0, 0))
    found = pl.pallas_call(
        kernel,
        grid_spec=pltpu.PrefetchScalarGridSpec(
            num_scalar_prefetch=1,
            grid=(steps,),
            in_specs=[whole, whole, whole, pl.BlockSpec((1, width), lambda g, core: (0, 0))]
            + [pl.BlockSpec((rows, block), lambda g, core: (0, g))]
            + [pl.BlockSpec((rows, block), lambda g, core: (0, width // block + g))] * (cores - 1)
            + [pl.BlockSpec((block, width), lambda g, core: (g, 0))] * cores
            + [whole] * relays
            + tokens(after)
            + [ANYWHERE] * len(reads),
            out_specs=[whole, whole]
            + [pl.BlockSpec((rows, lanes), lambda g, core: (0, 0))] * (cores - 1)
            + [pl.BlockSpec((rows, width + units), lambda g, core: (0, 0))] * relays
            + [pl.BlockSpec((reach, width), lambda g, core: (0, 0))] * rims_out
            + [pl.BlockSpec((8, width), lambda g, core: (0, 0)), TOKEN_SPEC],
            scratch_shapes=[pltpu.VMEM((rows, width), jnp.float32)],
        ),
        out_shape=[
            jax.ShapeDtypeStruct((rows, width), jnp.float32),
            jax.ShapeDtypeStruct((rows, width), jnp.bfloat16),
        ]
        + [jax.ShapeDtypeStruct((rows, lanes), jnp.bfloat16)] * (cores - 1)
        + [jax.ShapeDtypeStruct((rows, width + units), jnp.bfloat16)] * relays
        + [jax.ShapeDtypeStruct((reach, width), jnp.bfloat16)] * rims_out
        + [jax.ShapeDtypeStruct((8, width), jnp.float32), TOKEN],
        compiler_params=pltpu.CompilerParams(vmem_limit_bytes=VMEM_BYTES),
        cost_estimate=cost(5),
        name="ffn_back_stream",
    )(
        jnp.stack(places[:2]).astype(jnp.int32),
        upstream,
        in_hbm(normed),
        in_hbm(slope),
        gain[None],
        in_hbm(hidden),
        *packets,
        *[in_hbm(each) for each in ins],
        *packets[:relays],
        *after,
        *reads,
    )
    return (
        found[0],
        found[1],
        found[2 : 1 + cores],
        found[1 + cores : 1 + cores + relays],
        found[1 + cores + relays] if reach else None,
        found[-2],
        (found[-1],),
    )


def conv_data_grad(extended, weight, upstream, step, kind, after=()):
    taps, inner, width = weight.shape
    rows = upstream.shape[0]
    group = tap_groups(taps)
    steps = taps // group

    def kernel(extended_ref, weight_ref, upstream_ref, *refs):
        out_ref, token_ref, total_ref = refs[-3:]
        token_ref[...] = jnp.zeros(TOKEN.shape, TOKEN.dtype)
        first = pl.program_id(0) * group
        total = None
        for j in range(group):
            start = pl.multiple_of((taps - 1 - first - j) * step, ROW_TILE)
            term = lax.dot_general(
                extended_ref[pl.ds(start, rows), :],
                weight_ref[j],
                (((1,), (1,)), ((), ())),
                preferred_element_type=jnp.float32,
            )
            total = term if total is None else total + term

        @pl.when(pl.program_id(0) == 0)
        def _():
            total_ref[...] = total

        @pl.when(pl.program_id(0) > 0)
        def _():
            total_ref[...] += total

        @pl.when(pl.program_id(0) == steps - 1)
        def _():
            out_ref[...] = (upstream_ref[...] + wide(low(total_ref[...]))).astype(kind)

    whole = pl.BlockSpec((rows, inner), lambda g: (0, 0))
    found = pl.pallas_call(
        kernel,
        grid=(steps,),
        in_specs=[
            pl.BlockSpec(extended.shape, lambda g: (0, 0)),
            pl.BlockSpec((group, inner, width), lambda g: (g, 0, 0)),
            whole,
        ]
        + tokens(after),
        out_specs=(whole, TOKEN_SPEC),
        out_shape=(jax.ShapeDtypeStruct((rows, inner), kind), TOKEN),
        scratch_shapes=[pltpu.VMEM((rows, inner), jnp.float32)],
        compiler_params=pltpu.CompilerParams(vmem_limit_bytes=VMEM_BYTES),
        cost_estimate=cost(6),
        name="conv_data_grad",
    )(extended, in_hbm(weight), upstream, *after)
    return found[0], (found[1],)


def hold(arrays, after, reads=()):
    count = len(arrays)
    if count == 0:
        return [], after

    def kernel(*refs):
        refs[-1][...] = jnp.zeros(TOKEN.shape, TOKEN.dtype)

    found = pl.pallas_call(
        kernel,
        in_specs=[ANYWHERE] * (count + len(reads)) + [WHOLE] * len(after),
        out_specs=[ANYWHERE] * count + [WHOLE],
        out_shape=[jax.ShapeDtypeStruct(each.shape, each.dtype) for each in arrays] + [TOKEN],
        input_output_aliases={i: i for i in range(count)},
        compiler_params=pltpu.CompilerParams(vmem_limit_bytes=1 * MIB),
        cost_estimate=cost(0.5),
        name="hold",
    )(*arrays, *reads, *after)
    return list(found[:-1]), (found[-1],)


def join_rows(parts, after=(), reads=()):
    def kernel(*refs):
        out_ref, token_ref = refs[-2:]
        token_ref[...] = jnp.zeros(TOKEN.shape, TOKEN.dtype)
        first = 0
        for i, part in enumerate(parts):
            out_ref[first : first + part.shape[0]] = refs[i][...]
            first += part.shape[0]

    shape = (sum(part.shape[0] for part in parts), parts[0].shape[1])
    found = pl.pallas_call(
        kernel,
        in_specs=[WHOLE] * len(parts) + [ANYWHERE] * len(reads) + [WHOLE] * len(after),
        out_specs=[WHOLE] * 2,
        out_shape=[jax.ShapeDtypeStruct(shape, parts[0].dtype), TOKEN],
        compiler_params=pltpu.CompilerParams(vmem_limit_bytes=10 * MIB),
        cost_estimate=cost(1.5),
        name="join_rows",
    )(*parts, *reads, *after)
    return found[0], (found[1],)


def restack(groups, reads=(), after=()):
    cuts = [cut for _, each in groups for cut in each]
    if any(last is not None and (first % ROW_TILE or last % ROW_TILE) for first, last, _ in cuts):
        return [
            jnp.stack([array[first:last].reshape(shape) for array in arrays])
            for arrays, each in groups
            for first, last, shape in each
        ], after
    flat = [array for arrays, _ in groups for array in arrays]
    plan = []
    shapes = []
    at = 0
    for arrays, each in groups:
        for first, last, shape in each:
            for slot in range(len(arrays)):
                plan.append((at + slot, first, last, len(shapes), slot))
            held = shape if last is None else (last - first,) + arrays[0].shape[1:]
            shapes.append(jax.ShapeDtypeStruct((len(arrays),) + held, arrays[0].dtype))
        at += len(arrays)

    def kernel(*refs):
        out_refs = refs[-2 - len(shapes) : -2]
        token_ref, sem_ref = refs[-2:]
        token_ref[...] = jnp.zeros(TOKEN.shape, TOKEN.dtype)
        copies = []
        for source, first, last, target, slot in plan:
            ref = refs[source]
            copies.append(
                pltpu.make_async_copy(
                    ref if last is None else ref.at[pl.ds(first, last - first)],
                    out_refs[target].at[slot],
                    sem_ref.at[len(copies)],
                )
            )
        copy_all(copies)

    found = pl.pallas_call(
        kernel,
        in_specs=[ANYWHERE] * (len(flat) + len(reads)) + [WHOLE] * len(after),
        out_specs=[WHOLE] * (len(shapes) + 1),
        out_shape=shapes + [TOKEN],
        scratch_shapes=[pltpu.SemaphoreType.DMA((len(plan),))],
        compiler_params=pltpu.CompilerParams(vmem_limit_bytes=10 * MIB),
        cost_estimate=cost(1.5),
        name="restack",
    )(*flat, *reads, *after)
    return [
        each.reshape((each.shape[0],) + shape) for each, (_, _, shape) in zip(found, cuts)
    ], (found[-1],)


def conv_weight_grad(
    extendeds, upstream, arrived, places, sizes, taps, step, after=(), reads=()
):
    cores, seqs, acrosses, tap_peers = sizes
    rows = upstream.shape[0]
    inner = extendeds[0].shape[1]
    lanes = upstream.shape[1] // cores
    slab = inner // (seqs * acrosses * tap_peers)
    direct = slab % ROW_TILE == 0
    half = (tap_peers + 1) // 2
    rest = tap_peers - half
    seconds = acrosses if rest else 0
    outs = seqs + seconds if direct else 1

    def kernel(place_ref, *refs):
        out_refs = refs[-2 - outs : -2]
        token_ref, found_ref = refs[-2:]
        token_ref[...] = jnp.zeros(TOKEN.shape, TOKEN.dtype)
        start = pl.multiple_of(pl.program_id(0) * step, ROW_TILE)
        found = low(
            sum(
                lax.dot_general(
                    refs[c][pl.ds(start, rows), :],
                    refs[cores + c][...],
                    (((0,), (0,)), ((), ())),
                    preferred_element_type=jnp.float32,
                )
                for c in range(cores)
            )
        )
        if not direct:
            out_refs[0][0] = found
            return
        found_ref[...] = found

        def chunk(slot_t, slot_s, slot_a):
            t = lax.rem(place_ref[3] - slot_t + tap_peers, tap_peers)
            at = lax.rem(place_ref[1] - slot_s + seqs, seqs)
            a = lax.rem(place_ref[2] - slot_a + acrosses, acrosses)
            first = pl.multiple_of(((t * seqs + at) * acrosses + a) * slab, slab)
            return found_ref[pl.ds(first, slab), :]

        for s in range(seqs):
            for a in range(acrosses):
                for t in range(half):
                    out_refs[s][a, t, 0] = chunk(t, s, a)
                for t in range(half, tap_peers):
                    out_refs[seqs + a][s, t - half, 0] = chunk(t, s, a)

    if direct:
        shapes = [(acrosses, half, taps, slab, lanes)] * seqs
        shapes += [(seqs, rest, taps, slab, lanes)] * seconds
        specs = [
            pl.BlockSpec(shape[:2] + (1, slab, lanes), lambda k, place: (0, 0, k, 0, 0))
            for shape in shapes
        ]
    else:
        shapes = [(taps, inner, lanes)]
        specs = [pl.BlockSpec((1, inner, lanes), lambda k, place: (k, 0, 0))]
    found = pl.pallas_call(
        kernel,
        grid_spec=pltpu.PrefetchScalarGridSpec(
            num_scalar_prefetch=1,
            grid=(taps,),
            in_specs=[pl.BlockSpec(extendeds[0].shape, lambda k, place: (0, 0))] * cores
            + [pl.BlockSpec((rows, lanes), lambda k, place: (0, place[0]))]
            + [pl.BlockSpec((rows, lanes), lambda k, place: (0, 0))] * (cores - 1)
            + tokens(after)
            + [ANYWHERE] * len(reads),
            out_specs=specs + [TOKEN_SPEC],
            scratch_shapes=[pltpu.VMEM((inner, lanes), jnp.bfloat16)],
        ),
        out_shape=[jax.ShapeDtypeStruct(shape, jnp.bfloat16) for shape in shapes] + [TOKEN],
        compiler_params=pltpu.CompilerParams(vmem_limit_bytes=VMEM_BYTES),
        cost_estimate=cost(9),
        name="conv_weight_grad",
    )(jnp.stack(places).astype(jnp.int32), *extendeds, upstream, *arrived, *after, *reads)
    token = found[-1]
    if not direct:
        found = found[0].reshape(taps, tap_peers, seqs, acrosses, slab, lanes)
        for axis, which in ((1, 3), (2, 1), (3, 2)):
            found = relative(found, axis, places[which], sizes[which])
        found = found.transpose(2, 3, 1, 0, 4, 5)
        found = [found[s, :, :half] for s in range(seqs)] + [
            found[:, a, half:] for a in range(seconds)
        ]
    flat = [each.reshape(-1, lanes) for each in found[: seqs + seconds]]
    return flat[:seqs], flat[seqs:], token


def ffn_weight_grad(pairs, sizes, ffn_rows, after=()):
    cores, seqs, acrosses, tap_peers = sizes
    rows, width = pairs[0][1].shape
    block = tap_peers * ffn_rows
    half = (tap_peers + 1) // 2
    rest = tap_peers - half
    seconds = seqs if rest else 0
    transposed = (((0,), (0,)), ((), ()))
    if ffn_rows % ROW_TILE:
        found = jnp.stack(
            [
                low(
                    sum(
                        lax.dot_general(a, b, transposed, preferred_element_type=jnp.float32)
                        for a, b in [(left, right)]
                        + [(ends[:, width:], starts[:, :width]) for ends, starts in packets]
                    )
                ).reshape(acrosses, seqs, tap_peers, ffn_rows, width)
                for left, right, packets in pairs
            ],
            3,
        )
        token = jnp.zeros(TOKEN.shape, TOKEN.dtype)
        return (
            [found[a, :, :half].reshape(-1, width) for a in range(acrosses)],
            [found[:, s, half:].reshape(-1, width) for s in range(seconds)],
            token,
        )
    outs = acrosses + seconds

    def kernel(*refs):
        out_refs, token_ref = refs[-1 - outs : -1], refs[-1]
        token_ref[...] = jnp.zeros(TOKEN.shape, TOKEN.dtype)
        step = pl.program_id(0)
        for which in range(2):
            base = 2 * cores * which
            found = low(
                sum(
                    lax.dot_general(
                        refs[base + 2 * c][...],
                        refs[base + 2 * c + 1][...],
                        transposed,
                        preferred_element_type=jnp.float32,
                    )
                    for c in range(cores)
                )
            ).reshape(tap_peers, ffn_rows, width)
            for a in range(acrosses):

                @pl.when(step // seqs == a)
                def _(a=a):
                    out_refs[a][0, :, which] = found[:half]

            for s in range(seconds):

                @pl.when(lax.rem(step, seqs) == s)
                def _(s=s):
                    out_refs[acrosses + s][0, :, which] = found[half:]

    right_spec = pl.BlockSpec((rows, width), lambda g: (0, 0))
    left_spec = pl.BlockSpec((rows, block), lambda g: (0, g))
    late_spec = pl.BlockSpec((rows, block), lambda g: (0, width // block + g))

    def first_spec(a):
        return pl.BlockSpec(
            (1, half, 2, ffn_rows, width),
            lambda g: (jnp.clip(g - a * seqs, 0, seqs - 1), 0, 0, 0, 0),
        )

    second_spec = pl.BlockSpec(
        (1, rest, 2, ffn_rows, width), lambda g: (g // seqs, 0, 0, 0, 0)
    )
    operands = []
    for left, right, packets in pairs:
        operands += [in_hbm(left), right]
        for ends, starts in packets:
            operands += [ends, starts]
    found = pl.pallas_call(
        kernel,
        grid=(acrosses * seqs,),
        in_specs=([left_spec, right_spec] + [late_spec, right_spec] * (cores - 1)) * 2
        + tokens(after),
        out_specs=[first_spec(a) for a in range(acrosses)]
        + [second_spec] * seconds
        + [TOKEN_SPEC],
        out_shape=[jax.ShapeDtypeStruct((seqs, half, 2, ffn_rows, width), jnp.bfloat16)] * acrosses
        + [jax.ShapeDtypeStruct((acrosses, rest, 2, ffn_rows, width), jnp.bfloat16)] * seconds
        + [TOKEN],
        compiler_params=pltpu.CompilerParams(vmem_limit_bytes=VMEM_BYTES),
        cost_estimate=cost(8),
        name="ffn_weight_grad",
    )(*operands, *after)
    flat = [each.reshape(-1, width) for each in found[:-1]]
    return flat[:acrosses], flat[acrosses:], found[-1]


def group_slots(groups, lanes):
    flat, where = [], []
    rows = groups[0][0][0].size // (groups[0][1] * lanes)
    for parts, slots in groups:
        where += [(len(flat), len(parts), slot) for slot in range(slots)]
        flat += [part.reshape(slots, rows, lanes) for part in parts]
    return flat, where, rows


def slot_sum(refs, place, first=0):
    start, count, at = place
    return low(sum(wide(refs[first + start + i][at]) for i in range(count)))


def merge_slots(conv_groups, ffn_groups, after=()):
    lanes, width = conv_groups[0][0][0].shape[-1], ffn_groups[0][0][0].shape[-1]
    cuts = width // lanes
    conv_parts, conv_where, conv_rows = group_slots(conv_groups, lanes)
    ffn_parts, ffn_where, ffn_rows = group_slots(ffn_groups, width)
    slots = len(conv_where)
    if conv_rows % ROW_TILE or ffn_rows % ROW_TILE:
        merged = []
        for slot in range(slots):
            ffn = slot_sum(ffn_parts, ffn_where[slot])
            merged.append(
                jnp.concatenate(
                    [slot_sum(conv_parts, conv_where[slot])]
                    + [ffn[:, i * lanes : (i + 1) * lanes] for i in range(cuts)]
                )
            )
        return merged, after

    def kernel(*refs):
        out_refs, token_ref = refs[-1 - slots : -1], refs[-1]
        token_ref[...] = jnp.zeros(TOKEN.shape, TOKEN.dtype)
        for slot in range(slots):
            out_refs[slot][:conv_rows] = slot_sum(refs, conv_where[slot])
            ffn = slot_sum(refs, ffn_where[slot], len(conv_parts))
            for i in range(cuts):
                first = conv_rows + i * ffn_rows
                out_refs[slot][first : first + ffn_rows] = ffn[:, i * lanes : (i + 1) * lanes]

    found = pl.pallas_call(
        kernel,
        in_specs=[WHOLE] * (len(conv_parts) + len(ffn_parts) + len(after)),
        out_specs=[WHOLE] * (slots + 1),
        out_shape=[jax.ShapeDtypeStruct((conv_rows + cuts * ffn_rows, lanes), jnp.bfloat16)] * slots
        + [TOKEN],
        compiler_params=pltpu.CompilerParams(vmem_limit_bytes=10 * MIB),
        cost_estimate=cost(1.5),
        name="merge_slots",
    )(*conv_parts, *ffn_parts, *after)
    return found[:slots], (found[slots],)


def append_slots(groups, packed, after=(), reads=()):
    lanes = groups[0][0][0].shape[-1]
    parts, where, rows = group_slots(groups, lanes)
    slots = len(where)
    if rows % ROW_TILE:
        return [
            jnp.concatenate([slot_sum(parts, where[slot])] + packed) for slot in range(slots)
        ], after

    def kernel(*refs):
        out_refs, token_ref = refs[-1 - slots : -1], refs[-1]
        token_ref[...] = jnp.zeros(TOKEN.shape, TOKEN.dtype)
        for slot in range(slots):
            out_refs[slot][:rows] = slot_sum(refs, where[slot])
            if packed:
                out_refs[slot][rows:] = refs[len(parts)][...]

    shape = jax.ShapeDtypeStruct((rows + sum(each.shape[0] for each in packed), lanes), jnp.bfloat16)
    found = pl.pallas_call(
        kernel,
        in_specs=[WHOLE] * (len(packed) + len(parts) + len(after)) + [ANYWHERE] * len(reads),
        out_specs=[WHOLE] * (slots + 1),
        out_shape=[shape] * slots + [TOKEN],
        compiler_params=pltpu.CompilerParams(vmem_limit_bytes=8 * MIB),
        cost_estimate=cost(1),
        name="append_slots",
    )(*parts, *packed, *after, *reads)
    return found[:slots], (found[slots],)


def pack_small(row_groups, biases, losses, places, sizes, ffn_rows, after=()):
    cores, seqs, acrosses, tap_peers = sizes
    width = row_groups[0][0].shape[1]
    head_rows = sum(count for _, count in row_groups)
    hidden = cores * biases[0][0].shape[1]
    bias_rows = hidden // width
    used = head_rows + len(biases) * bias_rows + 2
    rows = -(-used // ROW_TILE) * ROW_TILE
    lanes = width // 2
    per_row = width // ffn_rows
    if ffn_rows % 64:
        terms = jnp.stack([losses[0, 0], losses[1, 0]])
        terms = jnp.stack([terms, terms - wide(low(terms))])
        pieces = [array[:count] for array, count in row_groups]
        for each in biases:
            bias = jnp.stack(each).reshape(cores, acrosses, seqs, tap_peers, ffn_rows)
            for axis, which in enumerate((0, 2, 1, 3)):
                bias = relative(bias, axis, places[which], sizes[which])
            pieces.append(bias.transpose(1, 0, 2, 3, 4).reshape(-1, width))
        pieces.append(jnp.pad(terms, ((0, rows - used), (0, width - 2))))
        packed = low(jnp.concatenate(pieces))
        return jnp.concatenate([packed[:, :lanes], packed[:, lanes:]]), after

    def kernel(place_ref, *refs):
        packed_ref, token_ref, rows_ref = refs[-3:]
        token_ref[...] = jnp.zeros(TOKEN.shape, TOKEN.dtype)
        rows_ref[...] = jnp.zeros(rows_ref.shape, jnp.float32)
        at = 0
        for i, (_, count) in enumerate(row_groups):
            rows_ref[at : at + count, :] = refs[i][:count, :]
            at += count
        shape = (cores, acrosses, seqs, tap_peers)
        owners = (0, 2, 1, 3)
        for b in range(len(biases)):
            blocks = {}
            for slot in np.ndindex(*shape):
                first = ((slot[1] * seqs + slot[2]) * tap_peers + slot[3]) * ffn_rows
                ref = refs[len(row_groups) + b * cores + slot[0]]
                blocks[slot] = ref[:, first : first + ffn_rows]
            for axis, size in enumerate(shape):
                turned = {}
                for slot in blocks:
                    place = lax.rem(place_ref[owners[axis]] - slot[axis] + size, size)
                    value = blocks[slot[:axis] + (0,) + slot[axis + 1 :]]
                    for other in range(1, size):
                        candidate = blocks[slot[:axis] + (other,) + slot[axis + 1 :]]
                        value = jnp.where(place == other, candidate, value)
                    turned[slot] = value
                blocks = turned
            ordered = [
                blocks[(c, a, s, t)]
                for a in range(acrosses)
                for c in range(cores)
                for s in range(seqs)
                for t in range(tap_peers)
            ]
            for row in range(bias_rows):
                line = ordered[row * per_row : (row + 1) * per_row]
                rows_ref[at : at + 1, :] = jnp.concatenate(line, 1)
                at += 1
        losses_ref = refs[len(row_groups) + len(biases) * cores]
        lane = lax.broadcasted_iota(jnp.int32, (1, width), 1)
        objective = jnp.broadcast_to(losses_ref[0:1, 0:1], (1, width))
        scored = jnp.broadcast_to(losses_ref[1:2, 0:1], (1, width))
        line = jnp.where(lane == 0, objective, jnp.where(lane == 1, scored, 0.0))
        rows_ref[at : at + 1, :] = line
        rows_ref[at + 1 : at + 2, :] = line - wide(low(line))
        packed_ref[:rows, :] = low(rows_ref[:, :lanes])
        packed_ref[rows:, :] = low(rows_ref[:, lanes:])

    flat = [array for array, _ in row_groups] + [each for some in biases for each in some]
    found = pl.pallas_call(
        kernel,
        in_specs=[SCALARS] + [WHOLE] * (len(flat) + 1 + len(after)),
        out_specs=[WHOLE] * 2,
        out_shape=[jax.ShapeDtypeStruct((2 * rows, lanes), jnp.bfloat16), TOKEN],
        scratch_shapes=[pltpu.VMEM((rows, width), jnp.float32)],
        compiler_params=pltpu.CompilerParams(vmem_limit_bytes=8 * MIB),
        cost_estimate=cost(2),
        name="pack_small",
    )(jnp.stack(places).astype(jnp.int32), *flat, losses, *after)
    return found[0], (found[1],)


def paired(values):
    while len(values) > 1:
        half = len(values) // 2
        if len(values) % 2:
            return sum(values[1:], values[0])
        values = [values[i] + values[i + half] for i in range(half)]
    return values[0]


def finish_small(stacks, first, width, classes, hidden, places, sizes):
    cores, seqs, acrosses = sizes[:3]
    peers, rows, lanes = stacks[0].shape
    count = rows - first
    bias_rows = hidden // width
    at_bias = 12 + classes
    at_loss = at_bias + 2 * bias_rows

    def pick(row):
        return (
            [row(2), row(5)],
            [[row(0), row(6)], [row(3), row(9)]],
            [[row(1), row(7)], [row(4), row(10)]],
            [[row(at_bias + b * bias_rows + i) for i in range(bias_rows)] for b in range(2)],
            [row(8), row(11)],
        )

    if max(cores, seqs, acrosses) > 2 or first % count or count % ROW_TILE:
        full = jnp.stack(
            [wide(each[:, first:]).reshape(seqs, acrosses, count, lanes) for each in stacks]
        )
        for axis, (place, size) in enumerate(zip(places[:3], sizes[:3])):
            full = relative(full, axis, place, size)
        total = jnp.sum(full, (0, 1, 2))
        total = jnp.concatenate([total[: count // 2], total[count // 2 :]], 1)
        conv_bias, gains, shifts, in_bias, out_bias = pick(lambda i: total[i])
        terms = total[at_loss] + total[at_loss + 1]
        return (
            jnp.stack(conv_bias),
            jnp.stack([jnp.stack(each) for each in gains]),
            jnp.stack([jnp.stack(each) for each in shifts]),
            jnp.stack([jnp.concatenate(each) for each in in_bias]),
            jnp.stack(out_bias),
            total[12:at_bias].T,
            (terms[0] / terms[1]).reshape(1, 1),
        )

    def kernel(*refs):
        conv_ref, gain_ref, shift_ref, in_ref, out_ref, head_ref, loss_ref, rows_ref = refs[cores:]
        total = paired(
            [
                paired(
                    [
                        paired([wide(refs[c][s * acrosses + a]) for a in range(acrosses)])
                        for s in range(seqs)
                    ]
                )
                for c in range(cores)
            ]
        )
        rows_ref[:, :lanes] = total[: count // 2]
        rows_ref[:, lanes:] = total[count // 2 :]
        conv_bias, gains, shifts, in_bias, out_bias = pick(lambda i: rows_ref[i : i + 1, :])
        for b in range(2):
            conv_ref[b : b + 1, :] = conv_bias[b]
            out_ref[b : b + 1, :] = out_bias[b]
            for i in range(2):
                gain_ref[b, i : i + 1, :] = gains[b][i]
                shift_ref[b, i : i + 1, :] = shifts[b][i]
            for i in range(bias_rows):
                in_ref[b : b + 1, i * width : (i + 1) * width] = in_bias[b][i]
        head_ref[...] = rows_ref[12 : 12 + 8 * (-(-classes // 8)), :].T[:, :classes]
        terms = rows_ref[at_loss : at_loss + 1, :128] + rows_ref[at_loss + 1 : at_loss + 2, :128]
        loss_ref[...] = terms[:, 0:1] / terms[:, 1:2]

    return pl.pallas_call(
        kernel,
        grid=(1,),
        in_specs=[pl.BlockSpec((peers, count, lanes), lambda g: (0, first // count, 0))] * cores,
        out_shape=(
            jax.ShapeDtypeStruct((2, width), jnp.float32),
            jax.ShapeDtypeStruct((2, 2, width), jnp.float32),
            jax.ShapeDtypeStruct((2, 2, width), jnp.float32),
            jax.ShapeDtypeStruct((2, hidden), jnp.float32),
            jax.ShapeDtypeStruct((2, width), jnp.float32),
            jax.ShapeDtypeStruct((width, classes), jnp.float32),
            jax.ShapeDtypeStruct((1, 1), jnp.float32),
        ),
        out_specs=[
            pl.BlockSpec((2, width), lambda g: (0, 0)),
            pl.BlockSpec((2, 2, width), lambda g: (0, 0, 0)),
            pl.BlockSpec((2, 2, width), lambda g: (0, 0, 0)),
            pl.BlockSpec((2, hidden), lambda g: (0, 0)),
            pl.BlockSpec((2, width), lambda g: (0, 0)),
            pl.BlockSpec((width, classes), lambda g: (0, 0)),
            pl.BlockSpec((1, 1), lambda g: (0, 0)),
        ],
        scratch_shapes=[pltpu.VMEM((count // 2, 2 * lanes), jnp.float32)],
        compiler_params=pltpu.CompilerParams(vmem_limit_bytes=4 * MIB),
        cost_estimate=cost(1.5),
        name="finish_small",
    )(*stacks)


def finish_conv(parts, conv_rows, small_rows, after=()):
    blocks, count = len(parts), len(parts[0])
    lanes = parts[0][0].shape[-1]
    flat = [part for block in parts for part in block]
    if conv_rows % ROW_TILE:
        sums = [sum(wide(part[:conv_rows]) for part in block) for block in parts]
        sums.append(paired([wide(part[conv_rows:]) for part in parts[0]]))
        return jnp.concatenate([low(total) for total in sums]), after

    def kernel(*refs):
        shard_ref, token_ref = refs[-2:]
        token_ref[...] = jnp.zeros(TOKEN.shape, TOKEN.dtype)
        shard_ref[blocks * conv_rows :] = low(
            paired([wide(refs[i][conv_rows:]) for i in range(count)])
        )
        for b in range(blocks):
            total = sum(wide(refs[b * count + i][:conv_rows]) for i in range(count))
            shard_ref[b * conv_rows : (b + 1) * conv_rows] = low(total)

    found = pl.pallas_call(
        kernel,
        in_specs=[WHOLE] * (len(flat) + len(after)),
        out_specs=[WHOLE] * 2,
        out_shape=[
            jax.ShapeDtypeStruct((blocks * conv_rows + small_rows, lanes), jnp.bfloat16),
            TOKEN,
        ],
        compiler_params=pltpu.CompilerParams(vmem_limit_bytes=8 * MIB),
        cost_estimate=cost(1.2),
        name="finish_conv",
    )(*flat, *after)
    return found[0], (found[1],)


def finish_ffn(merged, plain, conv_rows, ffn_rows, after=()):
    lanes, width = merged[0].shape[-1], plain[0].shape[-1]

    def cut_back(total):
        size = 2 * ffn_rows
        return jnp.concatenate(
            [total[i * size : (i + 1) * size] for i in range(width // lanes)], 1
        )

    if conv_rows % ROW_TILE or ffn_rows % ROW_TILE:
        sums = [sum(wide(part) for part in plain)]
        sums.append(cut_back(sum(wide(part[conv_rows:]) for part in merged)))
        return jnp.stack([each[:ffn_rows].T for each in sums]), jnp.stack(
            [each[ffn_rows:] for each in sums]
        ), after

    def kernel(*refs):
        in_ref, out_ref, token_ref = refs[-3:]
        token_ref[...] = jnp.zeros(TOKEN.shape, TOKEN.dtype)
        late = sum(wide(refs[i][conv_rows:]) for i in range(len(merged)))
        sums = [sum(wide(refs[len(merged) + i][...]) for i in range(len(plain))), cut_back(late)]
        for b in range(2):
            in_ref[b] = sums[b][:ffn_rows].T
            out_ref[b] = sums[b][ffn_rows:]

    found = pl.pallas_call(
        kernel,
        in_specs=[WHOLE] * (len(merged) + len(plain) + len(after)),
        out_specs=[WHOLE] * 3,
        out_shape=(
            jax.ShapeDtypeStruct((2, width, ffn_rows), jnp.float32),
            jax.ShapeDtypeStruct((2, ffn_rows, width), jnp.float32),
            TOKEN,
        ),
        compiler_params=pltpu.CompilerParams(vmem_limit_bytes=8 * MIB),
        cost_estimate=cost(1),
        name="finish_ffn",
    )(*merged, *plain, *after)
    return found[0], found[1], (found[2],)


def add_slots(parts, slots, after=(), reads=()):
    lanes = parts[0].shape[-1]
    rows = parts[0].size // (slots * lanes)
    parts = [part.reshape(slots, rows, lanes) for part in parts]
    block = rows // 4 if rows % (4 * ROW_TILE) == 0 else rows

    def kernel(*refs):
        out_refs, token_ref = refs[-1 - slots : -1], refs[-1]
        token_ref[...] = jnp.zeros(TOKEN.shape, TOKEN.dtype)
        for slot in range(slots):
            out_refs[slot][...] = low(sum(wide(refs[i][slot]) for i in range(len(parts))))

    found = pl.pallas_call(
        kernel,
        grid=(rows // block,),
        in_specs=[pl.BlockSpec((slots, block, lanes), lambda g: (0, g, 0))] * len(parts)
        + tokens(after)
        + [ANYWHERE] * len(reads),
        out_specs=[pl.BlockSpec((block, lanes), lambda g: (g, 0))] * slots + [TOKEN_SPEC],
        out_shape=[jax.ShapeDtypeStruct((rows, lanes), jnp.bfloat16)] * slots + [TOKEN],
        compiler_params=pltpu.CompilerParams(vmem_limit_bytes=8 * MIB),
        cost_estimate=cost(2),
        name="add_slots",
    )(*parts, *after, *reads)
    return found[:slots], found[slots]


def place_conv_grads(stacks, blocks, taps, slab, places, sizes):
    cores, seqs, acrosses = sizes[:3]
    peers, rows, lanes = stacks[0].shape
    channels = slab * seqs * acrosses
    if slab % ROW_TILE or rows % slab:
        full = jnp.stack([each[:, : blocks * taps * slab] for each in stacks])
        full = full.reshape(cores, seqs, acrosses, blocks, taps, slab, lanes)
        for axis, (place, size) in enumerate(zip(places[:3], sizes[:3])):
            full = relative(full, axis, place, size)
        return wide(
            full.transpose(3, 4, 1, 2, 5, 0, 6).reshape(blocks, taps, channels, cores * lanes)
        )
    stacks = [each.reshape(peers, rows // slab, slab, lanes) for each in stacks]

    def kernel(place_ref, *refs):
        out_ref = refs[-1]
        for c in range(cores):
            lane = pl.multiple_of(lax.rem(place_ref[0] - c + cores, cores) * lanes, lanes)
            for s in range(seqs):
                at_s = lax.rem(place_ref[1] - s + seqs, seqs)
                for a in range(acrosses):
                    at_a = lax.rem(place_ref[2] - a + acrosses, acrosses)
                    row = pl.multiple_of((at_s * acrosses + at_a) * slab, slab)
                    for b in range(blocks):
                        piece = wide(refs[c * blocks + b][s * acrosses + a, 0])
                        out_ref[b, 0, pl.ds(row, slab), pl.ds(lane, lanes)] = piece

    specs = [
        pl.BlockSpec((peers, 1, slab, lanes), lambda k, place, b=b: (0, b * taps + k, 0, 0))
        for b in range(blocks)
    ]
    return pl.pallas_call(
        kernel,
        grid_spec=pltpu.PrefetchScalarGridSpec(
            num_scalar_prefetch=1,
            grid=(taps,),
            in_specs=specs * cores,
            out_specs=pl.BlockSpec(
                (blocks, 1, channels, cores * lanes), lambda k, place: (0, k, 0, 0)
            ),
        ),
        out_shape=jax.ShapeDtypeStruct((blocks, taps, channels, cores * lanes), jnp.float32),
        compiler_params=pltpu.CompilerParams(vmem_limit_bytes=10 * MIB),
        cost_estimate=cost(5),
        name="place_conv_grads",
    )(
        jnp.stack(places[:3]).astype(jnp.int32),
        *[each for stack in stacks for each in [stack] * blocks],
    )


def copy_all(copies):
    for copy in copies:
        copy.start()
    for copy in copies:
        copy.wait()


def place_conv(pieces, places, sizes, after=(), reads=()):
    cores, seqs, acrosses, tap_peers = sizes
    taps, slab, lanes = pieces[0][0].shape[2:]
    inner = slab * seqs * acrosses * tap_peers
    if slab % ROW_TILE:
        full = jnp.stack([jnp.stack(row) for row in pieces])
        for axis, (place, size) in enumerate(zip(places, sizes)):
            full = relative(full, axis, place, size)
        return full.transpose(4, 3, 1, 2, 5, 0, 6).reshape(taps, inner, cores * lanes), after
    flat = [piece for row in pieces for piece in row]

    def kernel(place_ref, *refs):
        out_ref, token_ref, sem_ref = refs[-3:]
        token_ref[...] = jnp.zeros(TOKEN.shape, TOKEN.dtype)
        copies = []
        for c in range(cores):
            lane = lax.rem(place_ref[0] - c + cores, cores) * lanes
            for s in range(seqs):
                at_s = lax.rem(place_ref[1] - s + seqs, seqs)
                for a in range(acrosses):
                    at_a = lax.rem(place_ref[2] - a + acrosses, acrosses)
                    for t in range(tap_peers):
                        at_t = lax.rem(place_ref[3] - t + tap_peers, tap_peers)
                        row = ((at_t * seqs + at_s) * acrosses + at_a) * slab
                        copies.append(
                            pltpu.make_async_copy(
                                refs[c * seqs + s].at[a, t],
                                out_ref.at[
                                    :,
                                    pl.ds(pl.multiple_of(row, slab), slab),
                                    pl.ds(pl.multiple_of(lane, lanes), lanes),
                                ],
                                sem_ref.at[len(copies)],
                            )
                        )
        copy_all(copies)

    found = pl.pallas_call(
        kernel,
        in_specs=[SCALARS] + [ANYWHERE] * (len(flat) + len(reads)) + [WHOLE] * len(after),
        out_specs=[WHOLE] * 2,
        out_shape=[pltpu.HBM((taps, inner, cores * lanes), jnp.bfloat16), TOKEN],
        scratch_shapes=[pltpu.SemaphoreType.DMA((cores * seqs * acrosses * tap_peers,))],
        compiler_params=pltpu.CompilerParams(vmem_limit_bytes=12 * MIB),
        cost_estimate=cost(3),
        name="place_conv",
    )(jnp.stack(places).astype(jnp.int32), *flat, *reads, *after)
    return found[0], (found[1],)


def place_ffn(pieces, sizes, after=(), reads=()):
    cores, seqs, acrosses, tap_peers = sizes
    cuts, ffn_rows, lanes = pieces[0][0].shape[2:]
    cuts //= 2
    width = cuts * lanes
    units = seqs * acrosses * tap_peers * ffn_rows
    if ffn_rows % ROW_TILE:
        full = jnp.stack([jnp.stack(row) for row in pieces])
        full = full.reshape(cores, acrosses, seqs, tap_peers, 2, cuts, ffn_rows, lanes)
        full = full.transpose(4, 0, 1, 2, 3, 6, 5, 7).reshape(2, cores, units, width)
        return [full[0, c] for c in range(cores)], [full[1, c] for c in range(cores)], after
    flat = [piece for row in pieces for piece in row]

    def kernel(*refs):
        out_refs = refs[-2 - 2 * cores : -2]
        token_ref, sem_ref = refs[-2:]
        token_ref[...] = jnp.zeros(TOKEN.shape, TOKEN.dtype)
        copies = []
        for c in range(cores):
            for a in range(acrosses):
                for which in range(2):
                    for cut in range(cuts):
                        copies.append(
                            pltpu.make_async_copy(
                                refs[c * acrosses + a].at[:, :, which * cuts + cut],
                                out_refs[which * cores + c].at[
                                    a, :, :, :, pl.ds(cut * lanes, lanes)
                                ],
                                sem_ref.at[len(copies)],
                            )
                        )
        copy_all(copies)

    shape = pltpu.HBM((acrosses, seqs, tap_peers, ffn_rows, width), jnp.bfloat16)
    found = pl.pallas_call(
        kernel,
        in_specs=[ANYWHERE] * (len(flat) + len(reads)) + [WHOLE] * len(after),
        out_specs=[WHOLE] * (2 * cores + 1),
        out_shape=[shape] * (2 * cores) + [TOKEN],
        scratch_shapes=[pltpu.SemaphoreType.DMA((2 * cores * acrosses * cuts,))],
        compiler_params=pltpu.CompilerParams(vmem_limit_bytes=12 * MIB),
        cost_estimate=cost(2),
        name="place_ffn",
    )(*flat, *reads, *after)
    token = found[-1]
    found = [each.reshape(units, width) for each in found[:-1]]
    return found[:cores], found[cores:], (token,)


class Ring:
    def __init__(self, axis, size, index, pairs):
        self.axis, self.size, self.index, self.pairs = axis, size, index, pairs

    def shifted(self, value, by):
        return lax.ppermute(value, self.axis, self.pairs(lambda i: (i + by) % self.size))

    def swapped(self, value, bit):
        return lax.ppermute(value, self.axis, self.pairs(lambda i: i ^ bit))

    def gather(self, value):
        return [value] + [self.shifted(value, by) for by in range(1, self.size)]

    def swap(self, values):
        return [values[0]] + [self.shifted(values[by], -by) for by in range(1, self.size)]


def relative(value, axis, place, size):
    if size == 1:
        return value
    return jnp.stack(
        [
            lax.dynamic_index_in_dim(value, (place - slot) % size, axis, False)
            for slot in range(size)
        ],
        axis,
    )


def rings():
    peers = lax.axis_size("dp")
    cores = CORES if peers % CORES == 0 else 1
    columns = peers // cores
    place = lax.axis_index("dp")

    def plain(axis):
        size = lax.axis_size(axis)
        return Ring(
            axis, size, lax.axis_index(axis), lambda move: [(i, move(i)) for i in range(size)]
        )

    across = Ring(
        "dp",
        columns,
        place // cores,
        lambda move: [(i, move(i // cores) * cores + i % cores) for i in range(peers)],
    )
    core = Ring(
        "dp",
        cores,
        place % cores,
        lambda move: [(i, i // cores * cores + move(i % cores)) for i in range(peers)],
    )
    return core, across, plain("seq"), plain("tap")


class Reduce:
    def __init__(self, terms, order):
        self.order = order
        self.parts = [terms[0]] + [order[0].shifted(terms[s], -s) for s in range(1, order[0].size)]

    def step(self, level, after, reads=()):
        ring = self.order[level]
        found, token = add_slots(self.parts, ring.size, after, reads)
        self.parts = [found[0]] + [ring.shifted(found[s], -s) for s in range(1, ring.size)]
        return (token,)


def shared_copies(value, across, seq):
    peers, spans = lax.axis_size("dp"), lax.axis_size("seq")
    cores = peers // across.size

    def target(place, by_a, by_s):
        dp, at = place // spans, place % spans
        moved = (dp // cores + by_a) % across.size * cores + dp % cores
        return moved * spans + (at + by_s) % spans

    return [
        [
            value
            if by_a == by_s == 0
            else lax.ppermute(
                value,
                ("dp", "seq"),
                [(place, target(place, by_a, by_s)) for place in range(peers * spans)],
            )
            for by_a in range(across.size)
        ]
        for by_s in range(seq.size)
    ]


def passed_along(value, axis, by):
    peers = lax.axis_size(axis)
    pairs = [(i, i + by) for i in range(peers) if 0 <= i + by < peers]
    return lax.ppermute(value, axis, pairs)


def rims(source, reach_rows, seq, rim=None):
    span_rows = source.shape[0]
    if seq.size == 2 and reach_rows <= span_rows:
        if rim is None:
            first = (1 - seq.index) * (span_rows - reach_rows)
            rim = lax.dynamic_slice_in_dim(source, first, reach_rows, 0)
        return seq.shifted(rim, 1)
    left_parts = []
    right_parts = []
    distances = -(-reach_rows // span_rows)
    for distance in range(1, distances + 1):
        rim_count = min(span_rows, reach_rows - (distance - 1) * span_rows)
        left_parts.insert(0, passed_along(source[span_rows - rim_count :], "seq", distance))
        right_parts.append(passed_along(source[:rim_count], "seq", -distance))
    return left_parts, right_parts


def extend(source, found, seq, after=()):
    if isinstance(found, tuple):
        return join_rows(found[0] + [source] + found[1], after)
    reach, span = found.shape[0], source.shape[0]

    def kernel(place_ref, found_ref, source_ref, *refs):
        out_ref, token_ref = refs[-2:]
        token_ref[...] = jnp.zeros(TOKEN.shape, TOKEN.dtype)
        out_ref[reach : reach + span] = source_ref[...]
        zeros = jnp.zeros(found.shape, found.dtype)

        @pl.when(place_ref[0] == 0)
        def _():
            out_ref[:reach] = zeros
            out_ref[reach + span :] = found_ref[...]

        @pl.when(place_ref[0] != 0)
        def _():
            out_ref[:reach] = found_ref[...]
            out_ref[reach + span :] = zeros

    shape = jax.ShapeDtypeStruct((span + 2 * reach, source.shape[1]), source.dtype)
    extended, token = pl.pallas_call(
        kernel,
        in_specs=[SCALARS] + [WHOLE] * (2 + len(after)),
        out_specs=[WHOLE] * 2,
        out_shape=[shape, TOKEN],
        compiler_params=pltpu.CompilerParams(vmem_limit_bytes=10 * MIB),
        cost_estimate=cost(1.5),
        name="extend",
    )(seq.index.astype(jnp.int32)[None], found, source, *after)
    return extended, (token,)


def to_rows(values):
    windows, positions = values.shape[:2]
    cut = values.reshape((windows, positions // FIRST_DILATION, FIRST_DILATION) + values.shape[2:])
    return jnp.swapaxes(cut, 0, 1).reshape((windows * positions,) + values.shape[2:])


def from_rows(values, windows):
    cut = values.reshape((-1, windows, FIRST_DILATION) + values.shape[1:])
    return jnp.swapaxes(cut, 0, 1).reshape((windows, -1) + values.shape[1:])


def on_device(
    inputs,
    targets,
    masked,
    conv_weight,
    conv_bias,
    gains,
    shifts,
    in_weight,
    in_bias,
    out_weight,
    out_bias,
    head_weight,
):
    core, across, seq, tap = rings()
    taps = conv_weight.shape[1]
    channels = conv_weight.shape[2]
    width = conv_weight.shape[3]
    slab = channels // (seq.size * across.size)
    lanes = width // core.size
    hidden_width = in_bias.shape[1]
    ffn_rows = in_weight.shape[2]
    windows = inputs.shape[0]
    rows = windows * inputs.shape[1]
    steps = (FIRST_DILATION * windows, SECOND_DILATION * windows)
    units = hidden_width // core.size
    places = (core.index, seq.index, across.index, tap.index)
    sizes = (core.size, seq.size, across.size, tap.size)

    in_bias_placed = []
    for b in range(2):
        bias = in_bias[b].reshape(across.size, core.size, seq.size, tap.size, ffn_rows)
        for axis, ring in enumerate((across, core, seq, tap)):
            bias = relative(bias, axis, ring.index, ring.size)
        in_bias_placed.append(bias.transpose(1, 0, 2, 3, 4).reshape(core.size, units))

    def cut_ffn(piece):
        return piece.reshape(ffn_rows, core.size, lanes).swapaxes(0, 1).reshape(-1, lanes)

    def bundle(b):
        conv_piece = lax.dynamic_slice(
            conv_weight[b],
            (0, (seq.index * across.size + across.index) * slab, core.index * lanes),
            (taps, slab, lanes),
        )
        pieces = [
            conv_piece.reshape(taps * slab, lanes),
            cut_ffn(in_weight[b].T),
            cut_ffn(out_weight[b]),
        ]
        return jnp.concatenate(pieces)

    cuts = (
        (0, taps * slab, (taps, slab, lanes)),
        (taps * slab, taps * slab + 2 * core.size * ffn_rows, (2 * core.size, ffn_rows, lanes)),
    )

    def straight(arrays):
        return (arrays, ((0, None, arrays[0].shape),))

    conv_input = to_rows(inputs)
    stream = conv_input
    codes = to_rows(targets + masked * head_weight.shape[1])
    codes = jnp.broadcast_to(codes[:, None], (rows, 128))

    tap_parts = tap.gather(bundle(0))
    behind = bundle(1)
    (conv_part, ffn_part), last = restack([(tap_parts, cuts)], reads=[conv_input, behind])
    split = (tap.size + 1) // 2
    (behind,), last = hold([behind], last)
    late_parts = tap.gather(behind)
    extended, last = extend(conv_input, rims(conv_input, taps // 2 * steps[0], seq), seq, last)
    extended_parts = [extended] + [core.shifted(extended, -c) for c in range(1, core.size)]
    conv_parts, ffn_parts = across.gather(conv_part), seq.gather(ffn_part)
    (conv_part, ffn_part), last = restack(
        [straight(conv_parts), straight(ffn_parts)],
        reads=[late_parts[by] for by in range(1, tap.size) if by != split],
        after=last,
    )
    conv_parts, ffn_parts = seq.gather(conv_part), across.gather(ffn_part)
    conv_slots = [core.gather(conv_part)]
    ffn_slots = [core.gather(ffn_part)]
    held, last = hold(
        conv_parts[1:] + ffn_parts[1:],
        last,
        conv_slots[0][1:] + ffn_slots[0][1:] + late_parts[1:],
    )
    conv_slots += [core.gather(each) for each in held[: seq.size - 1]]
    ffn_slots += [core.gather(each) for each in held[seq.size - 1 :]]
    (late_conv, late_ffn), last = restack([(late_parts, cuts)], after=last)
    late_conv_parts, late_ffn_parts = across.gather(late_conv), seq.gather(late_ffn)

    def turned(slots):
        return [[each[c] for each in slots] for c in range(core.size)]

    conv_full, in_full, out_full = [None, None], [None, None], [None, None]
    conv_full[0], last = place_conv(
        turned(conv_slots), places, sizes, last, [part for each in ffn_slots for part in each[1:]]
    )
    (late_conv, late_ffn), last = restack(
        [straight(late_conv_parts), straight(late_ffn_parts)], after=last
    )
    late_conv_parts, late_ffn_parts = seq.gather(late_conv), across.gather(late_ffn)
    late_conv_slots = [core.gather(late_conv)]
    late_ffn_slots = [core.gather(late_ffn)]
    reaches = [taps // 2 * step for step in steps]
    rim_reaches = [reach if seq.size == 2 and reach <= rows else 0 for reach in reaches]
    saved = []
    reads = []
    rim = None
    for b in range(2):
        if b == 1:
            found = rims(conv_input, reaches[1], seq, rim)
            held, last = hold(late_conv_parts[1:] + late_ffn_parts[1:], last)
            late_conv_slots += [core.gather(each) for each in held[: seq.size - 1]]
            late_ffn_slots += [core.gather(each) for each in held[seq.size - 1 :]]
            conv_full[1], last = place_conv(turned(late_conv_slots), places, sizes, last)
            in_full[1], out_full[1], last = place_ffn(turned(late_ffn_slots), sizes, last)
            extended, last = extend(conv_input, found, seq, last)
            extended_parts = [extended] + [core.shifted(extended, -c) for c in range(1, core.size)]
        (normed_conv, conv_slope, stream, lowered), last = conv_forward(
            extended,
            conv_full[b],
            stream,
            conv_bias[b],
            gains[b, 0],
            shifts[b, 0],
            steps[b],
            last,
            reads,
        )
        reads = extended_parts[1:]
        if b == 0:
            in_full[0], out_full[0], last = place_ffn(turned(ffn_slots), sizes, last)
            reads = reads + late_conv_slots[0][1:] + late_ffn_slots[0][1:]
        active, hidden_slopes, (normed_ffn, scale_ffn, stream, conv_input), packets, rim, last = (
            ffn_forward(
                lowered,
                stream,
                in_full[b],
                out_full[b],
                [in_bias_placed[b][c] for c in range(core.size)],
                out_bias[b],
                gains[b, 1],
                shifts[b, 1],
                seq.index,
                rim_reaches[1] if b == 0 else 0,
                b == 1,
                last,
                reads,
            )
        )
        packets = [core.shifted(packet, -1 - c) for c, packet in enumerate(packets)]
        reads = packets
        saved.append(
            (
                extended_parts,
                conv_slope,
                normed_conv,
                (active, lowered, packets),
                hidden_slopes,
                normed_ffn,
                scale_ffn,
            )
        )

    final_state = from_rows(conv_input, windows)
    (stream_grad, head_grad, loss_rows), last = head_and_loss(stream, head_weight, codes, last)

    ffn_rows_of_sums = [None, None]
    conv_rows_of_sums = [None, None]
    in_bias_grads = [None, None]
    ffn_sums = [None, None]
    conv_sums = [None, None]
    merged = [None, None]

    def groups(halves):
        half = (tap.size + 1) // 2
        return [(each.parts, slots) for each, slots in zip(halves, (half, tap.size - half))]

    for b in (1, 0):
        (
            extended_parts,
            conv_slope,
            normed_conv,
            active_pair,
            hidden_slopes,
            normed_ffn,
            scale_ffn,
        ) = saved[b]
        output_grad, hidden_grad, biases, packets, ffn_rows_of_sums[b], last = ffn_back_hidden(
            stream_grad, normed_ffn, scale_ffn, gains[b, 1], out_full[b], hidden_slopes, last
        )
        if b == 1:
            arrived_packets = [core.shifted(packet, -1 - c) for c, packet in enumerate(packets)]
        if b == 0:
            for each in ffn_sums[1]:
                last = each.step(1, last)
            for each in conv_sums[1]:
                last = each.step(1, last)
        stream_grad, conv_grad, conv_cuts, relayed, rim, conv_rows_of_sums[b], last = ffn_back_stream(
            stream_grad,
            hidden_grad,
            packets,
            in_full[b],
            normed_conv,
            conv_slope,
            gains[b, 0],
            places,
            rim_reaches[b],
            last,
            reads,
            relay=b == 0,
        )
        reads = []
        if b == 0:
            merged[1], last = merge_slots(
                groups(conv_sums[1]), groups(ffn_sums[1]), last
            )
            sent = [rim] if rim is not None else []
            held, last = hold(list(conv_cuts) + list(relayed) + sent, last)
            conv_cuts, relayed = held[: core.size - 1], held[core.size - 1 : 2 * core.size - 2]
            rim = held[-1] if sent else None
            merged[1] = tap.swap(merged[1])
            arrived_packets = [core.shifted(packet, -1 - c) for c, packet in enumerate(relayed)]
        arrived = [core.shifted(conv_cuts[c - 1], -c) for c in range(1, core.size)]
        in_bias_grads[b] = list(biases)
        found_rims = rims(conv_grad, reaches[b], seq, rim)

        def ffn_grads(last):
            active, lowered, packets = active_pair
            if core.size == 1:
                packets = []
            first, second, token = ffn_weight_grad(
                (
                    (hidden_grad, lowered, [(g, p) for g, p in zip(arrived_packets, packets)]),
                    (active, output_grad, [(p, g) for g, p in zip(arrived_packets, packets)]),
                ),
                sizes,
                ffn_rows,
                last,
            )
            found = [Reduce(first, (across, seq))]
            if second:
                found.append(Reduce(second, (seq, across)))
            return found, (token,)

        def conv_grads(last, reads=()):
            first, second, token = conv_weight_grad(
                extended_parts, conv_grad, arrived, places, sizes, taps, steps[b], last, reads
            )
            found = [Reduce(first, (seq, across))]
            if second:
                found.append(Reduce(second, (across, seq)))
            return found, (token,)

        if b == 1:
            ffn_sums[1], last = ffn_grads(last)
            extended_grad, last = extend(conv_grad, found_rims, seq, last)
            conv_sums[1], last = conv_grads(last)
        else:
            conv_sums[0], last = conv_grads(last, arrived_packets)
            extended_grad, last = extend(conv_grad, found_rims, seq, last)
            ffn_sums[0], last = ffn_grads(last)
            for each in conv_sums[0]:
                last = each.step(1, last, merged[1][1:])
        stream_grad, last = conv_data_grad(
            extended_grad,
            conv_full[b],
            stream_grad,
            steps[b],
            jnp.float32 if b == 1 else jnp.bfloat16,
            last,
        )

    grad_inputs = from_rows(stream_grad, windows)

    row_groups = [(each, 3) for each in conv_rows_of_sums + ffn_rows_of_sums]
    row_groups.append((head_grad, head_weight.shape[1]))
    packed, last = pack_small(row_groups, in_bias_grads, loss_rows, places, sizes, ffn_rows, last)

    conv_rows = taps * slab
    merged[0], last = append_slots(groups(conv_sums[0]), [packed], last, [final_state])
    merged[0] = tap.swap(merged[0])
    for each in ffn_sums[0]:
        last = each.step(1, last)
    shards, last = finish_conv([merged[0], merged[1]], conv_rows, packed.shape[0], last)
    ffn_late, last = append_slots(groups(ffn_sums[0]), [], last, [grad_inputs])
    ffn_late = tap.swap(ffn_late)
    copies = [each for row in shared_copies(shards, across, seq) for each in row]
    grad_in, grad_out, last = finish_ffn(merged[1], ffn_late, conv_rows, ffn_rows, last)
    (stack,), last = restack([straight(copies)], after=last)
    stacks = core.gather(stack)
    (
        grad_conv_bias,
        grad_gains,
        grad_shifts,
        grad_in_bias,
        grad_out_bias,
        grad_head_weight,
        loss,
    ) = finish_small(
        stacks, 2 * conv_rows, width, head_weight.shape[1], hidden_width, places, sizes
    )
    grad_conv = place_conv_grads(stacks, 2, taps, slab, places, sizes)
    return (
        final_state,
        grad_inputs,
        grad_conv,
        grad_conv_bias,
        grad_gains,
        grad_shifts,
        grad_in,
        grad_in_bias,
        grad_out,
        grad_out_bias,
        grad_head_weight,
        loss.reshape(()),
    )


def solution(mesh):
    placed = (
        P(("dp", "tap"), "seq", None),
        P(("dp", "tap"), "seq"),
        P(("dp", "tap"), "seq"),
        P(None, None, "tap", None),
        P(),
        P(),
        P(),
        P(None, None, ("dp", "seq", "tap")),
        P(),
        P(None, ("dp", "seq", "tap"), None),
        P(),
        P(),
    )
    return jax.shard_map(
        on_device,
        mesh=mesh,
        in_specs=placed,
        out_specs=(
            P(("dp", "tap"), "seq", None),
            P(("dp", "tap"), "seq", None),
            P(None, None, "tap", None),
            P(),
            P(),
            P(),
            P(None, None, ("dp", "seq", "tap")),
            P(),
            P(None, ("dp", "seq", "tap"), None),
            P(),
            P(),
            P(),
        ),
        check_vma=False,
    )
```

```python
import functools

import jax
import jax.numpy as jnp
import numpy as np
from jax import lax
from jax.experimental import pallas as pl
from jax.experimental.pallas import tpu as pltpu
from jax.sharding import PartitionSpec as P

FIRST_DILATION = 4
SECOND_DILATION = 32
EPSILON = 1e-05
HIGHEST_PRECISION = lax.Precision.HIGHEST
CORES = 2
ROW_TILE = 16
MIB = 1024 * 1024
VMEM_BYTES = 20 * MIB
ANYWHERE = pl.BlockSpec(memory_space=pl.ANY)
SCALARS = pl.BlockSpec(memory_space=pltpu.SMEM)


TOKEN = jax.ShapeDtypeStruct((8, 128), jnp.float32)


def cost(microseconds):
    size = int(microseconds * 3.5e6)
    return pl.CostEstimate(flops=int(microseconds * 1.1e9), bytes_accessed=size, transcendentals=0)


WHOLE = pl.BlockSpec(memory_space=pltpu.VMEM)
TOKEN_SPEC = pl.BlockSpec(TOKEN.shape, lambda *_: (0, 0))


def tokens(after):
    return [TOKEN_SPEC] * len(after)


def in_hbm(array):
    return pltpu.with_memory_space_constraint(array, pltpu.HBM)


def low(values):
    return values.astype(jnp.bfloat16)


def wide(values):
    return values.astype(jnp.float32)


def gelu_parts(values):
    size = jnp.abs(values)
    bell = jnp.exp(-0.5 * values * values)
    base = 1.0 + 0.23164189 * size
    t = pl.reciprocal(base, approx=True)
    t = t * (2.0 - base * t)
    series = 0.53070271 * t - 0.726576015
    series = series * t + 0.71070687
    series = series * t - 0.142248368
    series = series * t + 0.127414796
    tail = series * t * bell
    phi = jnp.where(values < 0.0, tail, 1.0 - tail)
    return values * phi, phi + values * bell * 0.3989422804014327


def normalize(values):
    center = values - jnp.mean(values, -1, keepdims=True)
    scale = lax.rsqrt(jnp.mean(center * center, -1, keepdims=True) + EPSILON)
    return (center * scale, scale)


def norm_back(upstream, normed, scale):
    return scale * (
        upstream
        - jnp.mean(upstream, -1, keepdims=True)
        - normed * jnp.mean(upstream * normed, -1, keepdims=True)
    )


def tap_groups(taps):
    return 3 if taps % 3 == 0 else 1


def row_chunks(rows, most):
    size = min(rows, most)
    return [(first, size) for first in range(0, rows, size)]


def conv_forward(extended, weight, stream, bias, gain, shift, step, after=(), reads=()):
    taps, inner, width = weight.shape
    rows = stream.shape[0]
    group = tap_groups(taps)
    steps = taps // group

    def kernel(extended_ref, weight_ref, stream_ref, bias_ref, gain_ref, shift_ref, *refs):
        normed_ref, slope_ref, next_ref, lowered_ref, token_ref, total_ref = refs[-6:]
        token_ref[...] = jnp.zeros(TOKEN.shape, TOKEN.dtype)
        first = pl.program_id(0) * group
        total = None
        for j in range(group):
            start = pl.multiple_of((first + j) * step, ROW_TILE)
            term = jnp.dot(
                extended_ref[pl.ds(start, rows), :],
                weight_ref[j],
                preferred_element_type=jnp.float32,
            )
            total = term if total is None else total + term

        @pl.when(pl.program_id(0) == 0)
        def _():
            total_ref[...] = total

        @pl.when(pl.program_id(0) > 0)
        def _():
            total_ref[...] += total

        @pl.when(pl.program_id(0) == steps - 1)
        def _():
            for at, size in row_chunks(rows, 128):
                some = pl.ds(at, size)
                value, slope = gelu_parts(total_ref[some, :] + bias_ref[...])
                normed, scale = normalize(value)
                mid = wide(stream_ref[some, :]) + normed * gain_ref[...] + shift_ref[...]
                normed_ref[some, :] = low(normed)
                slope_ref[some, :] = low(scale * slope)
                next_ref[some, :] = mid
                lowered_ref[some, :] = low(mid)

    whole = pl.BlockSpec((rows, width), lambda g: (0, 0))
    row = pl.BlockSpec((1, width), lambda g: (0, 0))
    found = pl.pallas_call(
        kernel,
        grid=(steps,),
        in_specs=[
            pl.BlockSpec(extended.shape, lambda g: (0, 0)),
            pl.BlockSpec((group, inner, width), lambda g: (g, 0, 0)),
            whole,
            row,
            row,
            row,
        ]
        + tokens(after)
        + [ANYWHERE] * len(reads),
        out_specs=[whole] * 4 + [TOKEN_SPEC],
        out_shape=[
            pltpu.HBM((rows, width), jnp.bfloat16),
            pltpu.HBM((rows, width), jnp.bfloat16),
            pltpu.HBM((rows, width), jnp.float32),
            jax.ShapeDtypeStruct((rows, width), jnp.bfloat16),
            TOKEN,
        ],
        scratch_shapes=[pltpu.VMEM((rows, width), jnp.float32)],
        compiler_params=pltpu.CompilerParams(vmem_limit_bytes=VMEM_BYTES),
        cost_estimate=cost(9),
        name="conv_forward",
    )(extended, in_hbm(weight), in_hbm(stream) if stream.dtype == jnp.float32 else stream, bias[None], gain[None], shift[None], *after, *reads)
    return found[:4], (found[4],)


def ffn_forward(
    lowered,
    stream,
    ins,
    outs,
    in_biases,
    out_bias,
    gain,
    shift,
    seq_index,
    reach,
    last_block,
    after=(),
    reads=(),
):
    rows, width = lowered.shape
    cores = len(ins)
    units = ins[0].shape[0]
    block = min(units, 256)
    steps = units // block

    rims_out = 1 if reach else 0

    def kernel(place_ref, lowered_ref, stream_ref, out_bias_ref, gain_ref, shift_ref, *refs):
        in_refs, out_refs, bias_refs = (refs[i * cores : (i + 1) * cores] for i in range(3))
        found_refs = refs[-6 - 2 * cores - rims_out :]
        active_ref, slope_refs = found_refs[0], found_refs[1 : 1 + cores]
        normed_ref, scale_ref, next_ref, rounded_ref = found_refs[1 + cores : 5 + cores]
        packet_refs = found_refs[5 + cores : 4 + 2 * cores]
        token_ref, total_ref = found_refs[-2:]
        token_ref[...] = jnp.zeros(TOKEN.shape, TOKEN.dtype)
        lane = pl.multiple_of(width + pl.program_id(0) * block, block)

        @pl.when(pl.program_id(0) == 0)
        def _():
            total_ref[...] = jnp.zeros(total_ref.shape, jnp.float32)
            for packet_ref in packet_refs:
                packet_ref[:, :width] = lowered_ref[...]

        for at, size in row_chunks(rows, 512):
            some = pl.ds(at, size)
            term = None
            for c in range(cores):
                hidden = lax.dot_general(
                    lowered_ref[some, :],
                    in_refs[c][...],
                    (((1,), (1,)), ((), ())),
                    preferred_element_type=jnp.float32,
                )
                active, slope = gelu_parts(hidden + bias_refs[c][...])
                active = low(active)
                if c == 0:
                    active_ref[some, :] = active
                else:
                    packet_refs[c - 1][some, pl.ds(lane, block)] = active
                slope_refs[c][some, :] = low(slope)
                found = jnp.dot(active, out_refs[c][...], preferred_element_type=jnp.float32)
                term = found if term is None else term + found
            total_ref[some, :] += term

        @pl.when(pl.program_id(0) == steps - 1)
        def _():
            for at, size in row_chunks(rows, 128):
                some = pl.ds(at, size)
                normed, scale = normalize(total_ref[some, :] + out_bias_ref[...])
                after_ffn = stream_ref[some, :] + normed * gain_ref[...] + shift_ref[...]
                normed_ref[some, :] = low(normed)
                scale_ref[some, :] = jnp.broadcast_to(scale, (size, 128))
                next_ref[some, :] = after_ffn
                rounded_ref[some, :] = low(after_ffn)
            if reach:
                first = pl.multiple_of((1 - place_ref[0]) * (rows - reach), ROW_TILE)
                found_refs[-3][...] = rounded_ref[pl.ds(first, reach), :]

    whole = pl.BlockSpec((rows, width), lambda g: (0, 0))
    row = pl.BlockSpec((1, width), lambda g: (0, 0))
    piece = pl.BlockSpec((block, width), lambda g: (g, 0))
    columns = pl.BlockSpec((rows, block), lambda g: (0, g))
    hidden_shape = pltpu.HBM((rows, units), jnp.bfloat16)
    found = pl.pallas_call(
        kernel,
        grid=(steps,),
        in_specs=[SCALARS, whole, whole, row, row, row]
        + [piece] * (2 * cores)
        + [pl.BlockSpec((1, block), lambda g: (0, g))] * cores
        + tokens(after)
        + [ANYWHERE] * len(reads),
        out_specs=[columns] * (1 + cores)
        + [whole, pl.BlockSpec((rows, 128), lambda g: (0, 0)), whole, whole]
        + [pl.BlockSpec((rows, width + units), lambda g: (0, 0))] * (cores - 1)
        + [pl.BlockSpec((reach, width), lambda g: (0, 0))] * rims_out
        + [TOKEN_SPEC],
        out_shape=[hidden_shape] * (1 + cores)
        + [
            pltpu.HBM((rows, width), jnp.bfloat16),
            pltpu.HBM((rows, 128), jnp.float32),
            (jax.ShapeDtypeStruct if last_block else pltpu.HBM)((rows, width), jnp.float32),
            jax.ShapeDtypeStruct((rows, width), jnp.bfloat16),
        ]
        + [jax.ShapeDtypeStruct((rows, width + units), jnp.bfloat16)] * (cores - 1)
        + [jax.ShapeDtypeStruct((reach, width), jnp.bfloat16)] * rims_out
        + [TOKEN],
        scratch_shapes=[pltpu.VMEM((rows, width), jnp.float32)],
        compiler_params=pltpu.CompilerParams(vmem_limit_bytes=VMEM_BYTES),
        cost_estimate=cost(11),
        name="ffn_forward",
    )(
        seq_index.astype(jnp.int32)[None],
        lowered,
        in_hbm(stream),
        out_bias[None],
        gain[None],
        shift[None],
        *[in_hbm(each) for each in ins],
        *[in_hbm(each) for each in outs],
        *[each[None] for each in in_biases],
        *after,
        *reads,
    )
    return (
        found[0],
        found[1 : 1 + cores],
        found[1 + cores : 5 + cores],
        found[5 + cores : 4 + 2 * cores],
        found[4 + 2 * cores] if reach else None,
        (found[-1],),
    )


def head_and_loss(stream, head_weight, codes, after=()):
    rows, width = stream.shape
    classes = head_weight.shape[1]
    padded = jnp.pad(head_weight, ((0, 0), (0, 128 - classes)))
    cuts = row_chunks(rows, 256)

    def kernel(stream_ref, head_ref, code_ref, *refs):
        grad_ref, head_grad_ref, sums_ref, token_ref = refs[-4:]
        token_ref[...] = jnp.zeros(TOKEN.shape, TOKEN.dtype)
        head_grad = jnp.zeros((128, width), jnp.float32)
        objective = jnp.zeros((1, 1), jnp.float32)
        scored = jnp.zeros((1, 1), jnp.float32)
        for at, size in cuts:
            some = pl.ds(at, size)
            value = stream_ref[some, :]
            code = code_ref[some, :]
            mask = jnp.where(code[:, :1] >= classes, 1.0, 0.0)
            logits = jnp.dot(
                value, head_ref[...], precision=HIGHEST_PRECISION, preferred_element_type=jnp.float32
            )
            lane = lax.broadcasted_iota(jnp.int32, logits.shape, 1)
            valid = lane < classes
            peak = jnp.max(jnp.where(valid, logits, -jnp.inf), -1, keepdims=True)
            exponent = jnp.where(valid, jnp.exp(jnp.where(valid, logits - peak, 0.0)), 0.0)
            denominator = jnp.sum(exponent, -1, keepdims=True)
            chosen = lane == jnp.where(code >= classes, code - classes, code)
            picked = jnp.sum(jnp.where(chosen, logits, 0.0), -1, keepdims=True)
            terms = mask * (peak + jnp.log(denominator) - picked)
            objective = objective + jnp.sum(terms, 0, keepdims=True)
            scored = scored + jnp.sum(mask, 0, keepdims=True)
            logit_grad = mask * (exponent / denominator - jnp.where(chosen, 1.0, 0.0))
            grad_ref[some, :] = lax.dot_general(
                logit_grad,
                head_ref[...],
                (((1,), (1,)), ((), ())),
                precision=HIGHEST_PRECISION,
                preferred_element_type=jnp.float32,
            )
            head_grad = head_grad + lax.dot_general(
                logit_grad,
                value,
                (((0,), (0,)), ((), ())),
                precision=HIGHEST_PRECISION,
                preferred_element_type=jnp.float32,
            )
        head_grad_ref[...] = head_grad[: head_grad_ref.shape[0]]
        at_row = lax.broadcasted_iota(jnp.int32, sums_ref.shape, 0)
        sums_ref[...] = jnp.where(at_row == 0, objective, scored)

    found = pl.pallas_call(
        kernel,
        out_shape=[
            jax.ShapeDtypeStruct((rows, width), jnp.float32),
            jax.ShapeDtypeStruct((-(-classes // 8) * 8, width), jnp.float32),
            jax.ShapeDtypeStruct((8, 128), jnp.float32),
            TOKEN,
        ],
        compiler_params=pltpu.CompilerParams(vmem_limit_bytes=VMEM_BYTES),
        cost_estimate=cost(6),
        name="head_and_loss",
    )(stream, padded, codes, *after)
    return found[:3], (found[3],)


def ffn_back_hidden(upstream, normed, scale, gain, outs, slopes, after=()):
    rows, width = upstream.shape
    cores = len(outs)
    units = outs[0].shape[0]
    block = min(units, 256)

    def kernel(upstream_ref, normed_ref, scale_ref, gain_ref, *refs):
        out_refs, slope_refs = refs[:cores], refs[cores : 2 * cores]
        found_refs = refs[-3 - 2 * cores :]
        output_grad_ref, hidden_ref = found_refs[:2]
        bias_refs, packet_refs = found_refs[2 : 2 + cores], found_refs[2 + cores : -2]
        sums_ref, token_ref = found_refs[-2:]
        token_ref[...] = jnp.zeros(TOKEN.shape, TOKEN.dtype)
        lane = pl.multiple_of(width + pl.program_id(0) * block, block)

        @pl.when(pl.program_id(0) == 0)
        def _():
            totals = [jnp.zeros((1, width), jnp.float32)] * 3
            for at, size in row_chunks(rows, 128):
                some = pl.ds(at, size)
                grad, value = upstream_ref[some, :], wide(normed_ref[some, :])
                output_grad = low(norm_back(grad * gain_ref[...], value, scale_ref[some, :1]))
                output_grad_ref[some, :] = output_grad
                for packet_ref in packet_refs:
                    packet_ref[some, :width] = output_grad
                for i, each in enumerate((grad * value, grad, wide(output_grad))):
                    totals[i] = totals[i] + jnp.sum(each, 0, keepdims=True)
            sums_ref[...] = jnp.zeros(sums_ref.shape, jnp.float32)
            for i in range(3):
                sums_ref[i : i + 1, :] = totals[i]

        for c in range(cores):
            total = jnp.zeros((1, block), jnp.float32)
            for at, size in row_chunks(rows, 512):
                some = pl.ds(at, size)
                active_grad = lax.dot_general(
                    output_grad_ref[some, :],
                    out_refs[c][...],
                    (((1,), (1,)), ((), ())),
                    preferred_element_type=jnp.float32,
                )
                hidden_grad = low(active_grad * wide(slope_refs[c][some, :]))
                if c == 0:
                    hidden_ref[some, :] = hidden_grad
                else:
                    packet_refs[c - 1][some, pl.ds(lane, block)] = hidden_grad
                total = total + jnp.sum(wide(hidden_grad), 0, keepdims=True)
            bias_refs[c][...] = total

    whole = pl.BlockSpec((rows, width), lambda g: (0, 0))
    columns = pl.BlockSpec((rows, block), lambda g: (0, g))
    found = pl.pallas_call(
        kernel,
        grid=(units // block,),
        in_specs=[
            whole,
            whole,
            pl.BlockSpec((rows, 128), lambda g: (0, 0)),
            pl.BlockSpec((1, width), lambda g: (0, 0)),
        ]
        + [pl.BlockSpec((block, width), lambda g: (g, 0))] * cores
        + [columns] * cores
        + tokens(after),
        out_specs=[whole, columns]
        + [pl.BlockSpec((1, block), lambda g: (0, g))] * cores
        + [pl.BlockSpec((rows, width + units), lambda g: (0, 0))] * (cores - 1)
        + [pl.BlockSpec((8, width), lambda g: (0, 0)), TOKEN_SPEC],
        out_shape=[
            jax.ShapeDtypeStruct((rows, width), jnp.bfloat16),
            pltpu.HBM((rows, units), jnp.bfloat16),
        ]
        + [jax.ShapeDtypeStruct((1, units), jnp.float32)] * cores
        + [jax.ShapeDtypeStruct((rows, width + units), jnp.bfloat16)] * (cores - 1)
        + [jax.ShapeDtypeStruct((8, width), jnp.float32), TOKEN],
        compiler_params=pltpu.CompilerParams(vmem_limit_bytes=VMEM_BYTES),
        cost_estimate=cost(6),
        name="ffn_back_hidden",
    )(
        upstream,
        in_hbm(normed),
        in_hbm(scale),
        gain[None],
        *[in_hbm(each) for each in outs],
        *[in_hbm(each) for each in slopes],
        *after,
    )
    return (
        found[0],
        found[1],
        found[2 : 2 + cores],
        found[2 + cores : -2],
        found[-2],
        (found[-1],),
    )


def ffn_back_stream(
    upstream, hidden, packets, ins, normed, slope, gain, places, reach, after=(), reads=(), relay=False
):
    rows, width = upstream.shape
    cores = len(ins)
    units = ins[0].shape[0]
    block = min(units, 256)
    steps = units // block
    lanes = width // cores
    relays = cores - 1 if relay else 0
    rims_out = 1 if reach else 0

    def kernel(core_ref, upstream_ref, normed_ref, slope_ref, gain_ref, *refs):
        hidden_refs, in_refs = refs[:cores], refs[cores : 2 * cores]
        found_refs = refs[-4 - cores - relays - rims_out :]
        mid_ref, conv_grad_ref = found_refs[:2]
        cut_refs = found_refs[2 : 1 + cores]
        sums_ref, token_ref, total_ref = found_refs[-3:]
        token_ref[...] = jnp.zeros(TOKEN.shape, TOKEN.dtype)
        for i in range(relays):
            relay_ref = found_refs[1 + cores + i]
            lane = pl.multiple_of(width + pl.program_id(0) * block, block)
            relay_ref[:, pl.ds(lane, block)] = hidden_refs[1 + i][...]

            @pl.when(pl.program_id(0) == 0)
            def _(i=i, relay_ref=relay_ref):
                relay_ref[:, :width] = refs[2 * cores + i][...]

        @pl.when(pl.program_id(0) == 0)
        def _():
            total_ref[...] = upstream_ref[...]

        for at, size in row_chunks(rows, 512):
            some = pl.ds(at, size)
            total_ref[some, :] += sum(
                jnp.dot(
                    hidden_refs[c][some, :], in_refs[c][...], preferred_element_type=jnp.float32
                )
                for c in range(cores)
            )

        @pl.when(pl.program_id(0) == steps - 1)
        def _():
            totals = [jnp.zeros((1, width), jnp.float32)] * 3
            for at, size in row_chunks(rows, 128):
                some = pl.ds(at, size)
                grad, value = total_ref[some, :], wide(normed_ref[some, :])
                conv_grad = low(norm_back(grad * gain_ref[...], value, wide(slope_ref[some, :])))
                mid_ref[some, :] = grad
                conv_grad_ref[some, :] = conv_grad
                for i, each in enumerate((grad * value, grad, wide(conv_grad))):
                    totals[i] = totals[i] + jnp.sum(each, 0, keepdims=True)
            sums_ref[...] = jnp.zeros(sums_ref.shape, jnp.float32)
            for i in range(3):
                sums_ref[i : i + 1, :] = totals[i]
            for c in range(1, cores):
                first = lax.rem(core_ref[0] - c + cores, cores) * lanes
                cut_refs[c - 1][...] = conv_grad_ref[:, pl.ds(pl.multiple_of(first, lanes), lanes)]
            if reach:
                first = pl.multiple_of((1 - core_ref[1]) * (rows - reach), ROW_TILE)
                found_refs[-4][...] = conv_grad_ref[pl.ds(first, reach), :]

    whole = pl.BlockSpec((rows, width), lambda g, core: (0, 0))
    found = pl.pallas_call(
        kernel,
        grid_spec=pltpu.PrefetchScalarGridSpec(
            num_scalar_prefetch=1,
            grid=(steps,),
            in_specs=[whole, whole, whole, pl.BlockSpec((1, width), lambda g, core: (0, 0))]
            + [pl.BlockSpec((rows, block), lambda g, core: (0, g))]
            + [pl.BlockSpec((rows, block), lambda g, core: (0, width // block + g))] * (cores - 1)
            + [pl.BlockSpec((block, width), lambda g, core: (g, 0))] * cores
            + [whole] * relays
            + tokens(after)
            + [ANYWHERE] * len(reads),
            out_specs=[whole, whole]
            + [pl.BlockSpec((rows, lanes), lambda g, core: (0, 0))] * (cores - 1)
            + [pl.BlockSpec((rows, width + units), lambda g, core: (0, 0))] * relays
            + [pl.BlockSpec((reach, width), lambda g, core: (0, 0))] * rims_out
            + [pl.BlockSpec((8, width), lambda g, core: (0, 0)), TOKEN_SPEC],
            scratch_shapes=[pltpu.VMEM((rows, width), jnp.float32)],
        ),
        out_shape=[
            jax.ShapeDtypeStruct((rows, width), jnp.float32),
            jax.ShapeDtypeStruct((rows, width), jnp.bfloat16),
        ]
        + [jax.ShapeDtypeStruct((rows, lanes), jnp.bfloat16)] * (cores - 1)
        + [jax.ShapeDtypeStruct((rows, width + units), jnp.bfloat16)] * relays
        + [jax.ShapeDtypeStruct((reach, width), jnp.bfloat16)] * rims_out
        + [jax.ShapeDtypeStruct((8, width), jnp.float32), TOKEN],
        compiler_params=pltpu.CompilerParams(vmem_limit_bytes=VMEM_BYTES),
        cost_estimate=cost(5),
        name="ffn_back_stream",
    )(
        jnp.stack(places[:2]).astype(jnp.int32),
        upstream,
        in_hbm(normed),
        in_hbm(slope),
        gain[None],
        in_hbm(hidden),
        *packets,
        *[in_hbm(each) for each in ins],
        *packets[:relays],
        *after,
        *reads,
    )
    return (
        found[0],
        found[1],
        found[2 : 1 + cores],
        found[1 + cores : 1 + cores + relays],
        found[1 + cores + relays] if reach else None,
        found[-2],
        (found[-1],),
    )


def conv_data_grad(extended, weight, upstream, step, kind, after=()):
    taps, inner, width = weight.shape
    rows = upstream.shape[0]
    group = tap_groups(taps)
    steps = taps // group

    def kernel(extended_ref, weight_ref, upstream_ref, *refs):
        out_ref, token_ref, total_ref = refs[-3:]
        token_ref[...] = jnp.zeros(TOKEN.shape, TOKEN.dtype)
        first = pl.program_id(0) * group
        total = None
        for j in range(group):
            start = pl.multiple_of((taps - 1 - first - j) * step, ROW_TILE)
            term = lax.dot_general(
                extended_ref[pl.ds(start, rows), :],
                weight_ref[j],
                (((1,), (1,)), ((), ())),
                preferred_element_type=jnp.float32,
            )
            total = term if total is None else total + term

        @pl.when(pl.program_id(0) == 0)
        def _():
            total_ref[...] = total

        @pl.when(pl.program_id(0) > 0)
        def _():
            total_ref[...] += total

        @pl.when(pl.program_id(0) == steps - 1)
        def _():
            out_ref[...] = (upstream_ref[...] + wide(low(total_ref[...]))).astype(kind)

    whole = pl.BlockSpec((rows, inner), lambda g: (0, 0))
    found = pl.pallas_call(
        kernel,
        grid=(steps,),
        in_specs=[
            pl.BlockSpec(extended.shape, lambda g: (0, 0)),
            pl.BlockSpec((group, inner, width), lambda g: (g, 0, 0)),
            whole,
        ]
        + tokens(after),
        out_specs=(whole, TOKEN_SPEC),
        out_shape=(jax.ShapeDtypeStruct((rows, inner), kind), TOKEN),
        scratch_shapes=[pltpu.VMEM((rows, inner), jnp.float32)],
        compiler_params=pltpu.CompilerParams(vmem_limit_bytes=VMEM_BYTES),
        cost_estimate=cost(6),
        name="conv_data_grad",
    )(extended, in_hbm(weight), upstream, *after)
    return found[0], (found[1],)


def hold(arrays, after, reads=()):
    count = len(arrays)
    if count == 0:
        return [], after

    def kernel(*refs):
        refs[-1][...] = jnp.zeros(TOKEN.shape, TOKEN.dtype)

    found = pl.pallas_call(
        kernel,
        in_specs=[ANYWHERE] * (count + len(reads)) + [WHOLE] * len(after),
        out_specs=[ANYWHERE] * count + [WHOLE],
        out_shape=[jax.ShapeDtypeStruct(each.shape, each.dtype) for each in arrays] + [TOKEN],
        input_output_aliases={i: i for i in range(count)},
        compiler_params=pltpu.CompilerParams(vmem_limit_bytes=1 * MIB),
        cost_estimate=cost(0.5),
        name="hold",
    )(*arrays, *reads, *after)
    return list(found[:-1]), (found[-1],)


def join_rows(parts, after=(), reads=()):
    def kernel(*refs):
        out_ref, token_ref = refs[-2:]
        token_ref[...] = jnp.zeros(TOKEN.shape, TOKEN.dtype)
        first = 0
        for i, part in enumerate(parts):
            out_ref[first : first + part.shape[0]] = refs[i][...]
            first += part.shape[0]

    shape = (sum(part.shape[0] for part in parts), parts[0].shape[1])
    found = pl.pallas_call(
        kernel,
        in_specs=[WHOLE] * len(parts) + [ANYWHERE] * len(reads) + [WHOLE] * len(after),
        out_specs=[WHOLE] * 2,
        out_shape=[jax.ShapeDtypeStruct(shape, parts[0].dtype), TOKEN],
        compiler_params=pltpu.CompilerParams(vmem_limit_bytes=10 * MIB),
        cost_estimate=cost(1.5),
        name="join_rows",
    )(*parts, *reads, *after)
    return found[0], (found[1],)


def restack(groups, reads=(), after=(), fixed=False):
    cuts = [cut for _, each in groups for cut in each]
    if any(last is not None and (first % ROW_TILE or last % ROW_TILE) for first, last, _ in cuts):
        return [
            jnp.stack([array[first:last].reshape(shape) for array in arrays])
            for arrays, each in groups
            for first, last, shape in each
        ], after
    flat = [array for arrays, _ in groups for array in arrays]
    plan = []
    shapes = []
    at = 0
    for arrays, each in groups:
        for first, last, shape in each:
            for slot in range(len(arrays)):
                plan.append((at + slot, first, last, len(shapes), slot))
            held = shape if last is None else (last - first,) + arrays[0].shape[1:]
            shapes.append(jax.ShapeDtypeStruct((len(arrays),) + held, arrays[0].dtype))
        at += len(arrays)

    def kernel(*refs):
        out_refs = refs[-2 - len(shapes) : -2]
        token_ref, sem_ref = refs[-2:]
        token_ref[...] = jnp.zeros(TOKEN.shape, TOKEN.dtype)
        copies = []
        for source, first, last, target, slot in plan:
            ref = refs[source]
            copies.append(
                pltpu.make_async_copy(
                    ref if last is None else ref.at[pl.ds(first, last - first)],
                    out_refs[target].at[slot],
                    sem_ref.at[len(copies)],
                )
            )
        copy_all(copies)

    found = pl.pallas_call(
        kernel,
        in_specs=[ANYWHERE] * (len(flat) + len(reads)) + [WHOLE] * len(after),
        out_specs=[WHOLE] * (len(shapes) + 1),
        out_shape=shapes + [TOKEN],
        scratch_shapes=[pltpu.SemaphoreType.DMA((len(plan),))],
        compiler_params=pltpu.CompilerParams(vmem_limit_bytes=10 * MIB),
        cost_estimate=cost(1.5),
        name="restack",
    )(*([in_hbm(each) for each in flat] if fixed else flat), *reads, *after)
    return [
        each.reshape((each.shape[0],) + shape) for each, (_, _, shape) in zip(found, cuts)
    ], (found[-1],)


def conv_weight_grad(
    extendeds, upstream, arrived, places, sizes, taps, step, after=(), reads=()
):
    cores, seqs, acrosses, tap_peers = sizes
    rows = upstream.shape[0]
    inner = extendeds[0].shape[1]
    lanes = upstream.shape[1] // cores
    slab = inner // (seqs * acrosses * tap_peers)
    direct = slab % ROW_TILE == 0
    half = (tap_peers + 1) // 2
    rest = tap_peers - half
    seconds = acrosses if rest else 0
    outs = seqs + seconds if direct else 1

    def kernel(place_ref, *refs):
        out_refs = refs[-2 - outs : -2]
        token_ref, found_ref = refs[-2:]
        token_ref[...] = jnp.zeros(TOKEN.shape, TOKEN.dtype)
        start = pl.multiple_of(pl.program_id(0) * step, ROW_TILE)
        found = low(
            sum(
                lax.dot_general(
                    refs[c][pl.ds(start, rows), :],
                    refs[cores + c][...],
                    (((0,), (0,)), ((), ())),
                    preferred_element_type=jnp.float32,
                )
                for c in range(cores)
            )
        )
        if not direct:
            out_refs[0][0] = found
            return
        found_ref[...] = found

        def chunk(slot_t, slot_s, slot_a):
            t = lax.rem(place_ref[3] - slot_t + tap_peers, tap_peers)
            at = lax.rem(place_ref[1] - slot_s + seqs, seqs)
            a = lax.rem(place_ref[2] - slot_a + acrosses, acrosses)
            first = pl.multiple_of(((t * seqs + at) * acrosses + a) * slab, slab)
            return found_ref[pl.ds(first, slab), :]

        for s in range(seqs):
            for a in range(acrosses):
                for t in range(half):
                    out_refs[s][a, t, 0] = chunk(t, s, a)
                for t in range(half, tap_peers):
                    out_refs[seqs + a][s, t - half, 0] = chunk(t, s, a)

    if direct:
        shapes = [(acrosses, half, taps, slab, lanes)] * seqs
        shapes += [(seqs, rest, taps, slab, lanes)] * seconds
        specs = [
            pl.BlockSpec(shape[:2] + (1, slab, lanes), lambda k, place: (0, 0, k, 0, 0))
            for shape in shapes
        ]
    else:
        shapes = [(taps, inner, lanes)]
        specs = [pl.BlockSpec((1, inner, lanes), lambda k, place: (k, 0, 0))]
    found = pl.pallas_call(
        kernel,
        grid_spec=pltpu.PrefetchScalarGridSpec(
            num_scalar_prefetch=1,
            grid=(taps,),
            in_specs=[pl.BlockSpec(extendeds[0].shape, lambda k, place: (0, 0))] * cores
            + [pl.BlockSpec((rows, lanes), lambda k, place: (0, place[0]))]
            + [pl.BlockSpec((rows, lanes), lambda k, place: (0, 0))] * (cores - 1)
            + tokens(after)
            + [ANYWHERE] * len(reads),
            out_specs=specs + [TOKEN_SPEC],
            scratch_shapes=[pltpu.VMEM((inner, lanes), jnp.bfloat16)],
        ),
        out_shape=[jax.ShapeDtypeStruct(shape, jnp.bfloat16) for shape in shapes] + [TOKEN],
        compiler_params=pltpu.CompilerParams(vmem_limit_bytes=VMEM_BYTES),
        cost_estimate=cost(9),
        name="conv_weight_grad",
    )(jnp.stack(places).astype(jnp.int32), *extendeds, upstream, *arrived, *after, *reads)
    token = found[-1]
    if not direct:
        found = found[0].reshape(taps, tap_peers, seqs, acrosses, slab, lanes)
        for axis, which in ((1, 3), (2, 1), (3, 2)):
            found = relative(found, axis, places[which], sizes[which])
        found = found.transpose(2, 3, 1, 0, 4, 5)
        found = [found[s, :, :half] for s in range(seqs)] + [
            found[:, a, half:] for a in range(seconds)
        ]
    flat = [each.reshape(-1, lanes) for each in found[: seqs + seconds]]
    return flat[:seqs], flat[seqs:], token


def ffn_weight_grad(pairs, sizes, ffn_rows, after=()):
    cores, seqs, acrosses, tap_peers = sizes
    rows, width = pairs[0][1].shape
    block = tap_peers * ffn_rows
    half = (tap_peers + 1) // 2
    rest = tap_peers - half
    seconds = seqs if rest else 0
    transposed = (((0,), (0,)), ((), ()))
    if ffn_rows % ROW_TILE:
        found = jnp.stack(
            [
                low(
                    sum(
                        lax.dot_general(a, b, transposed, preferred_element_type=jnp.float32)
                        for a, b in [(left, right)]
                        + [(ends[:, width:], starts[:, :width]) for ends, starts in packets]
                    )
                ).reshape(acrosses, seqs, tap_peers, ffn_rows, width)
                for left, right, packets in pairs
            ],
            3,
        )
        token = jnp.zeros(TOKEN.shape, TOKEN.dtype)
        return (
            [found[a, :, :half].reshape(-1, width) for a in range(acrosses)],
            [found[:, s, half:].reshape(-1, width) for s in range(seconds)],
            token,
        )
    outs = acrosses + seconds

    def kernel(*refs):
        out_refs, token_ref = refs[-1 - outs : -1], refs[-1]
        token_ref[...] = jnp.zeros(TOKEN.shape, TOKEN.dtype)
        step = pl.program_id(0)
        for which in range(2):
            base = 2 * cores * which
            found = low(
                sum(
                    lax.dot_general(
                        refs[base + 2 * c][...],
                        refs[base + 2 * c + 1][...],
                        transposed,
                        preferred_element_type=jnp.float32,
                    )
                    for c in range(cores)
                )
            ).reshape(tap_peers, ffn_rows, width)
            for a in range(acrosses):

                @pl.when(step // seqs == a)
                def _(a=a):
                    out_refs[a][0, :, which] = found[:half]

            for s in range(seconds):

                @pl.when(lax.rem(step, seqs) == s)
                def _(s=s):
                    out_refs[acrosses + s][0, :, which] = found[half:]

    right_spec = pl.BlockSpec((rows, width), lambda g: (0, 0))
    left_spec = pl.BlockSpec((rows, block), lambda g: (0, g))
    late_spec = pl.BlockSpec((rows, block), lambda g: (0, width // block + g))

    def first_spec(a):
        return pl.BlockSpec(
            (1, half, 2, ffn_rows, width),
            lambda g: (jnp.clip(g - a * seqs, 0, seqs - 1), 0, 0, 0, 0),
        )

    second_spec = pl.BlockSpec(
        (1, rest, 2, ffn_rows, width), lambda g: (g // seqs, 0, 0, 0, 0)
    )
    operands = []
    for left, right, packets in pairs:
        operands += [in_hbm(left), right]
        for ends, starts in packets:
            operands += [ends, starts]
    found = pl.pallas_call(
        kernel,
        grid=(acrosses * seqs,),
        in_specs=([left_spec, right_spec] + [late_spec, right_spec] * (cores - 1)) * 2
        + tokens(after),
        out_specs=[first_spec(a) for a in range(acrosses)]
        + [second_spec] * seconds
        + [TOKEN_SPEC],
        out_shape=[jax.ShapeDtypeStruct((seqs, half, 2, ffn_rows, width), jnp.bfloat16)] * acrosses
        + [jax.ShapeDtypeStruct((acrosses, rest, 2, ffn_rows, width), jnp.bfloat16)] * seconds
        + [TOKEN],
        compiler_params=pltpu.CompilerParams(vmem_limit_bytes=VMEM_BYTES),
        cost_estimate=cost(8),
        name="ffn_weight_grad",
    )(*operands, *after)
    flat = [each.reshape(-1, width) for each in found[:-1]]
    return flat[:acrosses], flat[acrosses:], found[-1]


def group_slots(groups, lanes):
    flat, where = [], []
    rows = groups[0][0][0].size // (groups[0][1] * lanes)
    for parts, slots in groups:
        where += [(len(flat), len(parts), slot) for slot in range(slots)]
        flat += [part.reshape(slots, rows, lanes) for part in parts]
    return flat, where, rows


def slot_sum(refs, place, first=0):
    start, count, at = place
    return low(sum(wide(refs[first + start + i][at]) for i in range(count)))


def merge_slots(conv_groups, ffn_groups, after=()):
    lanes, width = conv_groups[0][0][0].shape[-1], ffn_groups[0][0][0].shape[-1]
    cuts = width // lanes
    conv_parts, conv_where, conv_rows = group_slots(conv_groups, lanes)
    ffn_parts, ffn_where, ffn_rows = group_slots(ffn_groups, width)
    slots = len(conv_where)
    if conv_rows % ROW_TILE or ffn_rows % ROW_TILE:
        merged = []
        for slot in range(slots):
            ffn = slot_sum(ffn_parts, ffn_where[slot])
            merged.append(
                jnp.concatenate(
                    [slot_sum(conv_parts, conv_where[slot])]
                    + [ffn[:, i * lanes : (i + 1) * lanes] for i in range(cuts)]
                )
            )
        return merged, after

    def kernel(*refs):
        out_refs, token_ref = refs[-1 - slots : -1], refs[-1]
        token_ref[...] = jnp.zeros(TOKEN.shape, TOKEN.dtype)
        for slot in range(slots):
            out_refs[slot][:conv_rows] = slot_sum(refs, conv_where[slot])
            ffn = slot_sum(refs, ffn_where[slot], len(conv_parts))
            for i in range(cuts):
                first = conv_rows + i * ffn_rows
                out_refs[slot][first : first + ffn_rows] = ffn[:, i * lanes : (i + 1) * lanes]

    found = pl.pallas_call(
        kernel,
        in_specs=[WHOLE] * (len(conv_parts) + len(ffn_parts) + len(after)),
        out_specs=[WHOLE] * (slots + 1),
        out_shape=[jax.ShapeDtypeStruct((conv_rows + cuts * ffn_rows, lanes), jnp.bfloat16)] * slots
        + [TOKEN],
        compiler_params=pltpu.CompilerParams(vmem_limit_bytes=10 * MIB),
        cost_estimate=cost(1.5),
        name="merge_slots",
    )(*conv_parts, *ffn_parts, *after)
    return found[:slots], (found[slots],)


def append_slots(groups, packed, after=(), reads=()):
    lanes = groups[0][0][0].shape[-1]
    parts, where, rows = group_slots(groups, lanes)
    slots = len(where)
    if rows % ROW_TILE:
        return [
            jnp.concatenate([slot_sum(parts, where[slot])] + packed) for slot in range(slots)
        ], after

    def kernel(*refs):
        out_refs, token_ref = refs[-1 - slots : -1], refs[-1]
        token_ref[...] = jnp.zeros(TOKEN.shape, TOKEN.dtype)
        for slot in range(slots):
            out_refs[slot][:rows] = slot_sum(refs, where[slot])
            if packed:
                out_refs[slot][rows:] = refs[len(parts)][...]

    shape = jax.ShapeDtypeStruct((rows + sum(each.shape[0] for each in packed), lanes), jnp.bfloat16)
    found = pl.pallas_call(
        kernel,
        in_specs=[WHOLE] * (len(packed) + len(parts) + len(after)) + [ANYWHERE] * len(reads),
        out_specs=[WHOLE] * (slots + 1),
        out_shape=[shape] * slots + [TOKEN],
        compiler_params=pltpu.CompilerParams(vmem_limit_bytes=8 * MIB),
        cost_estimate=cost(1),
        name="append_slots",
    )(*parts, *packed, *after, *reads)
    return found[:slots], (found[slots],)


def pack_small(row_groups, biases, losses, places, sizes, ffn_rows, after=()):
    cores, seqs, acrosses, tap_peers = sizes
    width = row_groups[0][0].shape[1]
    head_rows = sum(count for _, count in row_groups)
    hidden = cores * biases[0][0].shape[1]
    bias_rows = hidden // width
    used = head_rows + len(biases) * bias_rows + 2
    rows = -(-used // ROW_TILE) * ROW_TILE
    lanes = width // 2
    per_row = width // ffn_rows
    if ffn_rows % 64:
        terms = jnp.stack([losses[0, 0], losses[1, 0]])
        terms = jnp.stack([terms, terms - wide(low(terms))])
        pieces = [array[:count] for array, count in row_groups]
        for each in biases:
            bias = jnp.stack(each).reshape(cores, acrosses, seqs, tap_peers, ffn_rows)
            for axis, which in enumerate((0, 2, 1, 3)):
                bias = relative(bias, axis, places[which], sizes[which])
            pieces.append(bias.transpose(1, 0, 2, 3, 4).reshape(-1, width))
        pieces.append(jnp.pad(terms, ((0, rows - used), (0, width - 2))))
        packed = low(jnp.concatenate(pieces))
        return jnp.concatenate([packed[:, :lanes], packed[:, lanes:]]), after

    def kernel(place_ref, *refs):
        packed_ref, token_ref, rows_ref = refs[-3:]
        token_ref[...] = jnp.zeros(TOKEN.shape, TOKEN.dtype)
        rows_ref[...] = jnp.zeros(rows_ref.shape, jnp.float32)
        at = 0
        for i, (_, count) in enumerate(row_groups):
            rows_ref[at : at + count, :] = refs[i][:count, :]
            at += count
        shape = (cores, acrosses, seqs, tap_peers)
        owners = (0, 2, 1, 3)
        for b in range(len(biases)):
            blocks = {}
            for slot in np.ndindex(*shape):
                first = ((slot[1] * seqs + slot[2]) * tap_peers + slot[3]) * ffn_rows
                ref = refs[len(row_groups) + b * cores + slot[0]]
                blocks[slot] = ref[:, first : first + ffn_rows]
            for axis, size in enumerate(shape):
                turned = {}
                for slot in blocks:
                    place = lax.rem(place_ref[owners[axis]] - slot[axis] + size, size)
                    value = blocks[slot[:axis] + (0,) + slot[axis + 1 :]]
                    for other in range(1, size):
                        candidate = blocks[slot[:axis] + (other,) + slot[axis + 1 :]]
                        value = jnp.where(place == other, candidate, value)
                    turned[slot] = value
                blocks = turned
            ordered = [
                blocks[(c, a, s, t)]
                for a in range(acrosses)
                for c in range(cores)
                for s in range(seqs)
                for t in range(tap_peers)
            ]
            for row in range(bias_rows):
                line = ordered[row * per_row : (row + 1) * per_row]
                rows_ref[at : at + 1, :] = jnp.concatenate(line, 1)
                at += 1
        losses_ref = refs[len(row_groups) + len(biases) * cores]
        lane = lax.broadcasted_iota(jnp.int32, (1, width), 1)
        objective = jnp.broadcast_to(losses_ref[0:1, 0:1], (1, width))
        scored = jnp.broadcast_to(losses_ref[1:2, 0:1], (1, width))
        line = jnp.where(lane == 0, objective, jnp.where(lane == 1, scored, 0.0))
        rows_ref[at : at + 1, :] = line
        rows_ref[at + 1 : at + 2, :] = line - wide(low(line))
        packed_ref[:rows, :] = low(rows_ref[:, :lanes])
        packed_ref[rows:, :] = low(rows_ref[:, lanes:])

    flat = [array for array, _ in row_groups] + [each for some in biases for each in some]
    found = pl.pallas_call(
        kernel,
        in_specs=[SCALARS] + [WHOLE] * (len(flat) + 1 + len(after)),
        out_specs=[WHOLE] * 2,
        out_shape=[jax.ShapeDtypeStruct((2 * rows, lanes), jnp.bfloat16), TOKEN],
        scratch_shapes=[pltpu.VMEM((rows, width), jnp.float32)],
        compiler_params=pltpu.CompilerParams(vmem_limit_bytes=8 * MIB),
        cost_estimate=cost(2),
        name="pack_small",
    )(jnp.stack(places).astype(jnp.int32), *flat, losses, *after)
    return found[0], (found[1],)


def paired(values):
    while len(values) > 1:
        half = len(values) // 2
        if len(values) % 2:
            return sum(values[1:], values[0])
        values = [values[i] + values[i + half] for i in range(half)]
    return values[0]


def finish_small(stacks, first, width, classes, hidden, places, sizes):
    cores, seqs, acrosses = sizes[:3]
    peers, rows, lanes = stacks[0].shape
    count = rows - first
    bias_rows = hidden // width
    at_bias = 12 + classes
    at_loss = at_bias + 2 * bias_rows

    def pick(row):
        return (
            [row(2), row(5)],
            [[row(0), row(6)], [row(3), row(9)]],
            [[row(1), row(7)], [row(4), row(10)]],
            [[row(at_bias + b * bias_rows + i) for i in range(bias_rows)] for b in range(2)],
            [row(8), row(11)],
        )

    if max(cores, seqs, acrosses) > 2 or first % count or count % ROW_TILE:
        full = jnp.stack(
            [wide(each[:, first:]).reshape(seqs, acrosses, count, lanes) for each in stacks]
        )
        for axis, (place, size) in enumerate(zip(places[:3], sizes[:3])):
            full = relative(full, axis, place, size)
        total = jnp.sum(full, (0, 1, 2))
        total = jnp.concatenate([total[: count // 2], total[count // 2 :]], 1)
        conv_bias, gains, shifts, in_bias, out_bias = pick(lambda i: total[i])
        terms = total[at_loss] + total[at_loss + 1]
        return (
            jnp.stack(conv_bias),
            jnp.stack([jnp.stack(each) for each in gains]),
            jnp.stack([jnp.stack(each) for each in shifts]),
            jnp.stack([jnp.concatenate(each) for each in in_bias]),
            jnp.stack(out_bias),
            total[12:at_bias].T,
            (terms[0] / terms[1]).reshape(1, 1),
        )

    def kernel(*refs):
        conv_ref, gain_ref, shift_ref, in_ref, out_ref, head_ref, loss_ref, rows_ref = refs[cores:]
        total = paired(
            [
                paired(
                    [
                        paired([wide(refs[c][s * acrosses + a]) for a in range(acrosses)])
                        for s in range(seqs)
                    ]
                )
                for c in range(cores)
            ]
        )
        rows_ref[:, :lanes] = total[: count // 2]
        rows_ref[:, lanes:] = total[count // 2 :]
        conv_bias, gains, shifts, in_bias, out_bias = pick(lambda i: rows_ref[i : i + 1, :])
        for b in range(2):
            conv_ref[b : b + 1, :] = conv_bias[b]
            out_ref[b : b + 1, :] = out_bias[b]
            for i in range(2):
                gain_ref[b, i : i + 1, :] = gains[b][i]
                shift_ref[b, i : i + 1, :] = shifts[b][i]
            for i in range(bias_rows):
                in_ref[b : b + 1, i * width : (i + 1) * width] = in_bias[b][i]
        head_ref[...] = rows_ref[12 : 12 + 8 * (-(-classes // 8)), :].T[:, :classes]
        terms = rows_ref[at_loss : at_loss + 1, :128] + rows_ref[at_loss + 1 : at_loss + 2, :128]
        loss_ref[...] = terms[:, 0:1] / terms[:, 1:2]

    return pl.pallas_call(
        kernel,
        grid=(1,),
        in_specs=[pl.BlockSpec((peers, count, lanes), lambda g: (0, first // count, 0))] * cores,
        out_shape=(
            jax.ShapeDtypeStruct((2, width), jnp.float32),
            jax.ShapeDtypeStruct((2, 2, width), jnp.float32),
            jax.ShapeDtypeStruct((2, 2, width), jnp.float32),
            jax.ShapeDtypeStruct((2, hidden), jnp.float32),
            jax.ShapeDtypeStruct((2, width), jnp.float32),
            jax.ShapeDtypeStruct((width, classes), jnp.float32),
            jax.ShapeDtypeStruct((1, 1), jnp.float32),
        ),
        out_specs=[
            pl.BlockSpec((2, width), lambda g: (0, 0)),
            pl.BlockSpec((2, 2, width), lambda g: (0, 0, 0)),
            pl.BlockSpec((2, 2, width), lambda g: (0, 0, 0)),
            pl.BlockSpec((2, hidden), lambda g: (0, 0)),
            pl.BlockSpec((2, width), lambda g: (0, 0)),
            pl.BlockSpec((width, classes), lambda g: (0, 0)),
            pl.BlockSpec((1, 1), lambda g: (0, 0)),
        ],
        scratch_shapes=[pltpu.VMEM((count // 2, 2 * lanes), jnp.float32)],
        compiler_params=pltpu.CompilerParams(vmem_limit_bytes=4 * MIB),
        cost_estimate=cost(1.5),
        name="finish_small",
    )(*stacks)


def finish_conv(parts, conv_rows, small_rows, after=()):
    blocks, count = len(parts), len(parts[0])
    lanes = parts[0][0].shape[-1]
    flat = [part for block in parts for part in block]
    if conv_rows % ROW_TILE:
        sums = [sum(wide(part[:conv_rows]) for part in block) for block in parts]
        sums.append(paired([wide(part[conv_rows:]) for part in parts[0]]))
        return jnp.concatenate([low(total) for total in sums]), after

    def kernel(*refs):
        shard_ref, token_ref = refs[-2:]
        token_ref[...] = jnp.zeros(TOKEN.shape, TOKEN.dtype)
        shard_ref[blocks * conv_rows :] = low(
            paired([wide(refs[i][conv_rows:]) for i in range(count)])
        )
        for b in range(blocks):
            total = sum(wide(refs[b * count + i][:conv_rows]) for i in range(count))
            shard_ref[b * conv_rows : (b + 1) * conv_rows] = low(total)

    found = pl.pallas_call(
        kernel,
        in_specs=[WHOLE] * (len(flat) + len(after)),
        out_specs=[WHOLE] * 2,
        out_shape=[
            jax.ShapeDtypeStruct((blocks * conv_rows + small_rows, lanes), jnp.bfloat16),
            TOKEN,
        ],
        compiler_params=pltpu.CompilerParams(vmem_limit_bytes=8 * MIB),
        cost_estimate=cost(1.2),
        name="finish_conv",
    )(*flat, *after)
    return found[0], (found[1],)


def finish_ffn(merged, plain, conv_rows, ffn_rows, after=()):
    lanes, width = merged[0].shape[-1], plain[0].shape[-1]

    def cut_back(total):
        size = 2 * ffn_rows
        return jnp.concatenate(
            [total[i * size : (i + 1) * size] for i in range(width // lanes)], 1
        )

    if conv_rows % ROW_TILE or ffn_rows % ROW_TILE:
        sums = [sum(wide(part) for part in plain)]
        sums.append(cut_back(sum(wide(part[conv_rows:]) for part in merged)))
        return jnp.stack([each[:ffn_rows].T for each in sums]), jnp.stack(
            [each[ffn_rows:] for each in sums]
        ), after

    def kernel(*refs):
        in_ref, out_ref, token_ref = refs[-3:]
        token_ref[...] = jnp.zeros(TOKEN.shape, TOKEN.dtype)
        late = sum(wide(refs[i][conv_rows:]) for i in range(len(merged)))
        sums = [sum(wide(refs[len(merged) + i][...]) for i in range(len(plain))), cut_back(late)]
        for b in range(2):
            in_ref[b] = sums[b][:ffn_rows].T
            out_ref[b] = sums[b][ffn_rows:]

    found = pl.pallas_call(
        kernel,
        in_specs=[WHOLE] * (len(merged) + len(plain) + len(after)),
        out_specs=[WHOLE] * 3,
        out_shape=(
            jax.ShapeDtypeStruct((2, width, ffn_rows), jnp.float32),
            jax.ShapeDtypeStruct((2, ffn_rows, width), jnp.float32),
            TOKEN,
        ),
        compiler_params=pltpu.CompilerParams(vmem_limit_bytes=8 * MIB),
        cost_estimate=cost(1),
        name="finish_ffn",
    )(*merged, *plain, *after)
    return found[0], found[1], (found[2],)


def add_slots(parts, slots, after=(), reads=()):
    lanes = parts[0].shape[-1]
    rows = parts[0].size // (slots * lanes)
    parts = [part.reshape(slots, rows, lanes) for part in parts]
    block = rows // 4 if rows % (4 * ROW_TILE) == 0 else rows

    def kernel(*refs):
        out_refs, token_ref = refs[-1 - slots : -1], refs[-1]
        token_ref[...] = jnp.zeros(TOKEN.shape, TOKEN.dtype)
        for slot in range(slots):
            out_refs[slot][...] = low(sum(wide(refs[i][slot]) for i in range(len(parts))))

    found = pl.pallas_call(
        kernel,
        grid=(rows // block,),
        in_specs=[pl.BlockSpec((slots, block, lanes), lambda g: (0, g, 0))] * len(parts)
        + tokens(after)
        + [ANYWHERE] * len(reads),
        out_specs=[pl.BlockSpec((block, lanes), lambda g: (g, 0))] * slots + [TOKEN_SPEC],
        out_shape=[jax.ShapeDtypeStruct((rows, lanes), jnp.bfloat16)] * slots + [TOKEN],
        compiler_params=pltpu.CompilerParams(vmem_limit_bytes=8 * MIB),
        cost_estimate=cost(2),
        name="add_slots",
    )(*parts, *after, *reads)
    return found[:slots], found[slots]


def place_conv_grads(stacks, blocks, taps, slab, places, sizes):
    cores, seqs, acrosses = sizes[:3]
    peers, rows, lanes = stacks[0].shape
    channels = slab * seqs * acrosses
    if slab % ROW_TILE or rows % slab:
        full = jnp.stack([each[:, : blocks * taps * slab] for each in stacks])
        full = full.reshape(cores, seqs, acrosses, blocks, taps, slab, lanes)
        for axis, (place, size) in enumerate(zip(places[:3], sizes[:3])):
            full = relative(full, axis, place, size)
        return wide(
            full.transpose(3, 4, 1, 2, 5, 0, 6).reshape(blocks, taps, channels, cores * lanes)
        )
    stacks = [each.reshape(peers, rows // slab, slab, lanes) for each in stacks]

    def kernel(place_ref, *refs):
        out_ref = refs[-1]
        for c in range(cores):
            lane = pl.multiple_of(lax.rem(place_ref[0] - c + cores, cores) * lanes, lanes)
            for s in range(seqs):
                at_s = lax.rem(place_ref[1] - s + seqs, seqs)
                for a in range(acrosses):
                    at_a = lax.rem(place_ref[2] - a + acrosses, acrosses)
                    row = pl.multiple_of((at_s * acrosses + at_a) * slab, slab)
                    for b in range(blocks):
                        piece = wide(refs[c * blocks + b][s * acrosses + a, 0])
                        out_ref[b, 0, pl.ds(row, slab), pl.ds(lane, lanes)] = piece

    specs = [
        pl.BlockSpec((peers, 1, slab, lanes), lambda k, place, b=b: (0, b * taps + k, 0, 0))
        for b in range(blocks)
    ]
    return pl.pallas_call(
        kernel,
        grid_spec=pltpu.PrefetchScalarGridSpec(
            num_scalar_prefetch=1,
            grid=(taps,),
            in_specs=specs * cores,
            out_specs=pl.BlockSpec(
                (blocks, 1, channels, cores * lanes), lambda k, place: (0, k, 0, 0)
            ),
        ),
        out_shape=jax.ShapeDtypeStruct((blocks, taps, channels, cores * lanes), jnp.float32),
        compiler_params=pltpu.CompilerParams(vmem_limit_bytes=10 * MIB),
        cost_estimate=cost(5),
        name="place_conv_grads",
    )(
        jnp.stack(places[:3]).astype(jnp.int32),
        *[each for stack in stacks for each in [stack] * blocks],
    )


def copy_all(copies):
    for copy in copies:
        copy.start()
    for copy in copies:
        copy.wait()


def place_conv(pieces, places, sizes, after=(), reads=()):
    cores, seqs, acrosses, tap_peers = sizes
    taps, slab, lanes = pieces[0][0].shape[2:]
    inner = slab * seqs * acrosses * tap_peers
    if slab % ROW_TILE:
        full = jnp.stack([jnp.stack(row) for row in pieces])
        for axis, (place, size) in enumerate(zip(places, sizes)):
            full = relative(full, axis, place, size)
        return full.transpose(4, 3, 1, 2, 5, 0, 6).reshape(taps, inner, cores * lanes), after
    flat = [piece for row in pieces for piece in row]

    def kernel(place_ref, *refs):
        out_ref, token_ref, sem_ref = refs[-3:]
        token_ref[...] = jnp.zeros(TOKEN.shape, TOKEN.dtype)
        copies = []
        for c in range(cores):
            lane = lax.rem(place_ref[0] - c + cores, cores) * lanes
            for s in range(seqs):
                at_s = lax.rem(place_ref[1] - s + seqs, seqs)
                for a in range(acrosses):
                    at_a = lax.rem(place_ref[2] - a + acrosses, acrosses)
                    for t in range(tap_peers):
                        at_t = lax.rem(place_ref[3] - t + tap_peers, tap_peers)
                        row = ((at_t * seqs + at_s) * acrosses + at_a) * slab
                        copies.append(
                            pltpu.make_async_copy(
                                refs[c * seqs + s].at[a, t],
                                out_ref.at[
                                    :,
                                    pl.ds(pl.multiple_of(row, slab), slab),
                                    pl.ds(pl.multiple_of(lane, lanes), lanes),
                                ],
                                sem_ref.at[len(copies)],
                            )
                        )
        copy_all(copies)

    found = pl.pallas_call(
        kernel,
        in_specs=[SCALARS] + [ANYWHERE] * (len(flat) + len(reads)) + [WHOLE] * len(after),
        out_specs=[WHOLE] * 2,
        out_shape=[pltpu.HBM((taps, inner, cores * lanes), jnp.bfloat16), TOKEN],
        scratch_shapes=[pltpu.SemaphoreType.DMA((cores * seqs * acrosses * tap_peers,))],
        compiler_params=pltpu.CompilerParams(vmem_limit_bytes=12 * MIB),
        cost_estimate=cost(3),
        name="place_conv",
    )(jnp.stack(places).astype(jnp.int32), *flat, *reads, *after)
    return found[0], (found[1],)


def place_ffn(pieces, sizes, after=(), reads=()):
    cores, seqs, acrosses, tap_peers = sizes
    cuts, ffn_rows, lanes = pieces[0][0].shape[2:]
    cuts //= 2
    width = cuts * lanes
    units = seqs * acrosses * tap_peers * ffn_rows
    if ffn_rows % ROW_TILE:
        full = jnp.stack([jnp.stack(row) for row in pieces])
        full = full.reshape(cores, acrosses, seqs, tap_peers, 2, cuts, ffn_rows, lanes)
        full = full.transpose(4, 0, 1, 2, 3, 6, 5, 7).reshape(2, cores, units, width)
        return [full[0, c] for c in range(cores)], [full[1, c] for c in range(cores)], after
    flat = [piece for row in pieces for piece in row]

    def kernel(*refs):
        out_refs = refs[-2 - 2 * cores : -2]
        token_ref, sem_ref = refs[-2:]
        token_ref[...] = jnp.zeros(TOKEN.shape, TOKEN.dtype)
        copies = []
        for c in range(cores):
            for a in range(acrosses):
                for which in range(2):
                    for cut in range(cuts):
                        copies.append(
                            pltpu.make_async_copy(
                                refs[c * acrosses + a].at[:, :, which * cuts + cut],
                                out_refs[which * cores + c].at[
                                    a, :, :, :, pl.ds(cut * lanes, lanes)
                                ],
                                sem_ref.at[len(copies)],
                            )
                        )
        copy_all(copies)

    shape = pltpu.HBM((acrosses, seqs, tap_peers, ffn_rows, width), jnp.bfloat16)
    found = pl.pallas_call(
        kernel,
        in_specs=[ANYWHERE] * (len(flat) + len(reads)) + [WHOLE] * len(after),
        out_specs=[WHOLE] * (2 * cores + 1),
        out_shape=[shape] * (2 * cores) + [TOKEN],
        scratch_shapes=[pltpu.SemaphoreType.DMA((2 * cores * acrosses * cuts,))],
        compiler_params=pltpu.CompilerParams(vmem_limit_bytes=12 * MIB),
        cost_estimate=cost(2),
        name="place_ffn",
    )(*flat, *reads, *after)
    token = found[-1]
    found = [each.reshape(units, width) for each in found[:-1]]
    return found[:cores], found[cores:], (token,)


class Ring:
    def __init__(self, axis, size, index, pairs):
        self.axis, self.size, self.index, self.pairs = axis, size, index, pairs

    def shifted(self, value, by):
        return lax.ppermute(value, self.axis, self.pairs(lambda i: (i + by) % self.size))

    def swapped(self, value, bit):
        return lax.ppermute(value, self.axis, self.pairs(lambda i: i ^ bit))

    def gather(self, value):
        return [value] + [self.shifted(value, by) for by in range(1, self.size)]

    def swap(self, values):
        return [values[0]] + [self.shifted(values[by], -by) for by in range(1, self.size)]


def relative(value, axis, place, size):
    if size == 1:
        return value
    return jnp.stack(
        [
            lax.dynamic_index_in_dim(value, (place - slot) % size, axis, False)
            for slot in range(size)
        ],
        axis,
    )


def rings():
    peers = lax.axis_size("dp")
    cores = CORES if peers % CORES == 0 else 1
    columns = peers // cores
    place = lax.axis_index("dp")

    def plain(axis):
        size = lax.axis_size(axis)
        return Ring(
            axis, size, lax.axis_index(axis), lambda move: [(i, move(i)) for i in range(size)]
        )

    across = Ring(
        "dp",
        columns,
        place // cores,
        lambda move: [(i, move(i // cores) * cores + i % cores) for i in range(peers)],
    )
    core = Ring(
        "dp",
        cores,
        place % cores,
        lambda move: [(i, i // cores * cores + move(i % cores)) for i in range(peers)],
    )
    return core, across, plain("seq"), plain("tap")


class Reduce:
    def __init__(self, terms, order):
        self.order = order
        self.parts = [terms[0]] + [order[0].shifted(terms[s], -s) for s in range(1, order[0].size)]

    def step(self, level, after, reads=()):
        ring = self.order[level]
        found, token = add_slots(self.parts, ring.size, after, reads)
        self.parts = [found[0]] + [ring.shifted(found[s], -s) for s in range(1, ring.size)]
        return (token,)


def shared_copies(value, across, seq):
    peers, spans = lax.axis_size("dp"), lax.axis_size("seq")
    cores = peers // across.size

    def target(place, by_a, by_s):
        dp, at = place // spans, place % spans
        moved = (dp // cores + by_a) % across.size * cores + dp % cores
        return moved * spans + (at + by_s) % spans

    return [
        [
            value
            if by_a == by_s == 0
            else lax.ppermute(
                value,
                ("dp", "seq"),
                [(place, target(place, by_a, by_s)) for place in range(peers * spans)],
            )
            for by_a in range(across.size)
        ]
        for by_s in range(seq.size)
    ]


def passed_along(value, axis, by):
    peers = lax.axis_size(axis)
    pairs = [(i, i + by) for i in range(peers) if 0 <= i + by < peers]
    return lax.ppermute(value, axis, pairs)


def rims(source, reach_rows, seq, rim=None):
    span_rows = source.shape[0]
    if seq.size == 2 and reach_rows <= span_rows:
        if rim is None:
            first = (1 - seq.index) * (span_rows - reach_rows)
            rim = lax.dynamic_slice_in_dim(source, first, reach_rows, 0)
        return seq.shifted(rim, 1)
    left_parts = []
    right_parts = []
    distances = -(-reach_rows // span_rows)
    for distance in range(1, distances + 1):
        rim_count = min(span_rows, reach_rows - (distance - 1) * span_rows)
        left_parts.insert(0, passed_along(source[span_rows - rim_count :], "seq", distance))
        right_parts.append(passed_along(source[:rim_count], "seq", -distance))
    return left_parts, right_parts


def extend(source, found, seq, after=()):
    if isinstance(found, tuple):
        return join_rows(found[0] + [source] + found[1], after)
    reach, span = found.shape[0], source.shape[0]

    def kernel(place_ref, found_ref, source_ref, *refs):
        out_ref, token_ref = refs[-2:]
        token_ref[...] = jnp.zeros(TOKEN.shape, TOKEN.dtype)
        out_ref[reach : reach + span] = source_ref[...]
        zeros = jnp.zeros(found.shape, found.dtype)

        @pl.when(place_ref[0] == 0)
        def _():
            out_ref[:reach] = zeros
            out_ref[reach + span :] = found_ref[...]

        @pl.when(place_ref[0] != 0)
        def _():
            out_ref[:reach] = found_ref[...]
            out_ref[reach + span :] = zeros

    shape = jax.ShapeDtypeStruct((span + 2 * reach, source.shape[1]), source.dtype)
    extended, token = pl.pallas_call(
        kernel,
        in_specs=[SCALARS] + [WHOLE] * (2 + len(after)),
        out_specs=[WHOLE] * 2,
        out_shape=[shape, TOKEN],
        compiler_params=pltpu.CompilerParams(vmem_limit_bytes=10 * MIB),
        cost_estimate=cost(1.5),
        name="extend",
    )(seq.index.astype(jnp.int32)[None], found, source, *after)
    return extended, (token,)


def to_rows(values):
    windows, positions = values.shape[:2]
    cut = values.reshape((windows, positions // FIRST_DILATION, FIRST_DILATION) + values.shape[2:])
    return jnp.swapaxes(cut, 0, 1).reshape((windows * positions,) + values.shape[2:])


def from_rows(values, windows):
    cut = values.reshape((-1, windows, FIRST_DILATION) + values.shape[1:])
    return jnp.swapaxes(cut, 0, 1).reshape((windows, -1) + values.shape[1:])


def on_device(
    inputs,
    targets,
    masked,
    conv_weight,
    conv_bias,
    gains,
    shifts,
    in_weight,
    in_bias,
    out_weight,
    out_bias,
    head_weight,
):
    core, across, seq, tap = rings()
    taps = conv_weight.shape[1]
    channels = conv_weight.shape[2]
    width = conv_weight.shape[3]
    slab = channels // (seq.size * across.size)
    lanes = width // core.size
    hidden_width = in_bias.shape[1]
    ffn_rows = in_weight.shape[2]
    windows = inputs.shape[0]
    rows = windows * inputs.shape[1]
    steps = (FIRST_DILATION * windows, SECOND_DILATION * windows)
    units = hidden_width // core.size
    places = (core.index, seq.index, across.index, tap.index)
    sizes = (core.size, seq.size, across.size, tap.size)

    in_bias_placed = []
    for b in range(2):
        bias = in_bias[b].reshape(across.size, core.size, seq.size, tap.size, ffn_rows)
        for axis, ring in enumerate((across, core, seq, tap)):
            bias = relative(bias, axis, ring.index, ring.size)
        in_bias_placed.append(bias.transpose(1, 0, 2, 3, 4).reshape(core.size, units))

    def cut_ffn(piece):
        return piece.reshape(ffn_rows, core.size, lanes).swapaxes(0, 1).reshape(-1, lanes)

    def bundle(b):
        conv_piece = lax.dynamic_slice(
            conv_weight[b],
            (0, (seq.index * across.size + across.index) * slab, core.index * lanes),
            (taps, slab, lanes),
        )
        pieces = [
            conv_piece.reshape(taps * slab, lanes),
            cut_ffn(in_weight[b].T),
            cut_ffn(out_weight[b]),
        ]
        return jnp.concatenate(pieces)

    cuts = (
        (0, taps * slab, (taps, slab, lanes)),
        (taps * slab, taps * slab + 2 * core.size * ffn_rows, (2 * core.size, ffn_rows, lanes)),
    )

    def straight(arrays):
        return (arrays, ((0, None, arrays[0].shape),))

    conv_input = to_rows(inputs)
    stream = conv_input
    codes = to_rows(targets + masked * head_weight.shape[1])
    codes = jnp.broadcast_to(codes[:, None], (rows, 128))

    reaches = [taps // 2 * step for step in steps]
    rim_reaches = [reach if seq.size == 2 and reach <= rows else 0 for reach in reaches]

    tap_parts = tap.gather(bundle(0))
    behind = bundle(1)
    found = rims(conv_input, reaches[0], seq)
    (conv_part, ffn_part, behind), last = restack(
        [(tap_parts, cuts), straight([behind])],
        reads=[found] if rim_reaches[0] else [conv_input],
    )
    behind = behind[0]
    split = (tap.size + 1) // 2
    late_parts = tap.gather(behind)
    extended, last = extend(conv_input, found, seq, last)
    extended_parts = [extended] + [core.shifted(extended, -c) for c in range(1, core.size)]
    conv_parts, ffn_parts = across.gather(conv_part), seq.gather(ffn_part)
    (conv_part, ffn_part), last = restack(
        [straight(conv_parts), straight(ffn_parts)],
        reads=[late_parts[by] for by in range(1, tap.size) if by != split],
        after=last,
    )
    conv_parts, ffn_parts = seq.gather(conv_part), across.gather(ffn_part)
    conv_slots = [core.gather(conv_part)]
    ffn_slots = [core.gather(ffn_part)]
    held, last = hold(
        conv_parts[1:] + ffn_parts[1:],
        last,
        conv_slots[0][1:] + ffn_slots[0][1:] + late_parts[1:],
    )
    conv_slots += [core.gather(each) for each in held[: seq.size - 1]]
    ffn_slots += [core.gather(each) for each in held[seq.size - 1 :]]
    (late_conv, late_ffn), last = restack([(late_parts, cuts)], after=last, fixed=True)
    late_conv_parts, late_ffn_parts = across.gather(late_conv), seq.gather(late_ffn)

    def turned(slots):
        return [[each[c] for each in slots] for c in range(core.size)]

    conv_full, in_full, out_full = [None, None], [None, None], [None, None]
    conv_full[0], last = place_conv(
        turned(conv_slots), places, sizes, last, [part for each in ffn_slots for part in each[1:]]
    )
    (late_conv, late_ffn), last = restack(
        [straight(late_conv_parts), straight(late_ffn_parts)], after=last
    )
    late_conv_parts, late_ffn_parts = seq.gather(late_conv), across.gather(late_ffn)
    late_conv_slots = [core.gather(late_conv)]
    late_ffn_slots = [core.gather(late_ffn)]
    saved = []
    reads = []
    rim = None
    for b in range(2):
        if b == 1:
            found = rims(conv_input, reaches[1], seq, rim)
            held, last = hold(late_conv_parts[1:] + late_ffn_parts[1:], last)
            late_conv_slots += [core.gather(each) for each in held[: seq.size - 1]]
            late_ffn_slots += [core.gather(each) for each in held[seq.size - 1 :]]
            conv_full[1], last = place_conv(turned(late_conv_slots), places, sizes, last)
            in_full[1], out_full[1], last = place_ffn(turned(late_ffn_slots), sizes, last)
            extended, last = extend(conv_input, found, seq, last)
            extended_parts = [extended] + [core.shifted(extended, -c) for c in range(1, core.size)]
        (normed_conv, conv_slope, stream, lowered), last = conv_forward(
            extended,
            conv_full[b],
            stream,
            conv_bias[b],
            gains[b, 0],
            shifts[b, 0],
            steps[b],
            last,
            reads,
        )
        reads = extended_parts[1:]
        if b == 0:
            in_full[0], out_full[0], last = place_ffn(turned(ffn_slots), sizes, last)
            reads = reads + late_conv_slots[0][1:] + late_ffn_slots[0][1:]
        active, hidden_slopes, (normed_ffn, scale_ffn, stream, conv_input), packets, rim, last = (
            ffn_forward(
                lowered,
                stream,
                in_full[b],
                out_full[b],
                [in_bias_placed[b][c] for c in range(core.size)],
                out_bias[b],
                gains[b, 1],
                shifts[b, 1],
                seq.index,
                rim_reaches[1] if b == 0 else 0,
                b == 1,
                last,
                reads,
            )
        )
        packets = [core.shifted(packet, -1 - c) for c, packet in enumerate(packets)]
        reads = packets
        saved.append(
            (
                extended_parts,
                conv_slope,
                normed_conv,
                (active, lowered, packets),
                hidden_slopes,
                normed_ffn,
                scale_ffn,
            )
        )

    (stream_grad, head_grad, loss_rows), last = head_and_loss(stream, head_weight, codes, last)

    ffn_rows_of_sums = [None, None]
    conv_rows_of_sums = [None, None]
    in_bias_grads = [None, None]
    ffn_sums = [None, None]
    conv_sums = [None, None]
    merged = [None, None]

    def groups(halves):
        half = (tap.size + 1) // 2
        return [(each.parts, slots) for each, slots in zip(halves, (half, tap.size - half))]

    for b in (1, 0):
        (
            extended_parts,
            conv_slope,
            normed_conv,
            active_pair,
            hidden_slopes,
            normed_ffn,
            scale_ffn,
        ) = saved[b]
        output_grad, hidden_grad, biases, packets, ffn_rows_of_sums[b], last = ffn_back_hidden(
            stream_grad, normed_ffn, scale_ffn, gains[b, 1], out_full[b], hidden_slopes, last
        )
        if b == 1:
            arrived_packets = [core.shifted(packet, -1 - c) for c, packet in enumerate(packets)]
        if b == 0:
            for each in ffn_sums[1]:
                last = each.step(1, last)
            for each in conv_sums[1]:
                last = each.step(1, last)
        stream_grad, conv_grad, conv_cuts, relayed, rim, conv_rows_of_sums[b], last = ffn_back_stream(
            stream_grad,
            hidden_grad,
            packets,
            in_full[b],
            normed_conv,
            conv_slope,
            gains[b, 0],
            places,
            rim_reaches[b],
            last,
            reads,
            relay=b == 0,
        )
        reads = []
        if b == 0:
            merged[1], last = merge_slots(
                groups(conv_sums[1]), groups(ffn_sums[1]), last
            )
            sent = [rim] if rim is not None else []
            held, last = hold(list(conv_cuts) + list(relayed) + sent, last)
            conv_cuts, relayed = held[: core.size - 1], held[core.size - 1 : 2 * core.size - 2]
            rim = held[-1] if sent else None
            merged[1] = tap.swap(merged[1])
            arrived_packets = [core.shifted(packet, -1 - c) for c, packet in enumerate(relayed)]
        arrived = [core.shifted(conv_cuts[c - 1], -c) for c in range(1, core.size)]
        in_bias_grads[b] = list(biases)
        found_rims = rims(conv_grad, reaches[b], seq, rim)

        def ffn_grads(last):
            active, lowered, packets = active_pair
            if core.size == 1:
                packets = []
            first, second, token = ffn_weight_grad(
                (
                    (hidden_grad, lowered, [(g, p) for g, p in zip(arrived_packets, packets)]),
                    (active, output_grad, [(p, g) for g, p in zip(arrived_packets, packets)]),
                ),
                sizes,
                ffn_rows,
                last,
            )
            found = [Reduce(first, (across, seq))]
            if second:
                found.append(Reduce(second, (seq, across)))
            return found, (token,)

        def conv_grads(last, reads=()):
            first, second, token = conv_weight_grad(
                extended_parts, conv_grad, arrived, places, sizes, taps, steps[b], last, reads
            )
            found = [Reduce(first, (seq, across))]
            if second:
                found.append(Reduce(second, (across, seq)))
            return found, (token,)

        if b == 1:
            ffn_sums[1], last = ffn_grads(last)
            extended_grad, last = extend(conv_grad, found_rims, seq, last)
            conv_sums[1], last = conv_grads(last)
        else:
            conv_sums[0], last = conv_grads(last, arrived_packets)
            extended_grad, last = extend(conv_grad, found_rims, seq, last)
            ffn_sums[0], last = ffn_grads(last)
            for each in conv_sums[0]:
                last = each.step(1, last, merged[1][1:])
        stream_grad, last = conv_data_grad(
            extended_grad,
            conv_full[b],
            stream_grad,
            steps[b],
            jnp.float32 if b == 1 else jnp.bfloat16,
            last,
        )

    grad_inputs = from_rows(stream_grad, windows)

    row_groups = [(each, 3) for each in conv_rows_of_sums + ffn_rows_of_sums]
    row_groups.append((head_grad, head_weight.shape[1]))
    (conv_input,), last = hold([conv_input], last)
    final_state = from_rows(conv_input, windows)
    packed, last = pack_small(row_groups, in_bias_grads, loss_rows, places, sizes, ffn_rows, last)

    conv_rows = taps * slab
    merged[0], last = append_slots(groups(conv_sums[0]), [packed], last, [final_state])
    merged[0] = tap.swap(merged[0])
    for each in ffn_sums[0]:
        last = each.step(1, last)
    shards, last = finish_conv([merged[0], merged[1]], conv_rows, packed.shape[0], last)
    ffn_late, last = append_slots(groups(ffn_sums[0]), [], last, [grad_inputs])
    ffn_late = tap.swap(ffn_late)
    copies = [each for row in shared_copies(shards, across, seq) for each in row]
    grad_in, grad_out, last = finish_ffn(merged[1], ffn_late, conv_rows, ffn_rows, last)
    (stack,), last = restack([straight(copies)], after=last)
    stacks = core.gather(stack)
    (
        grad_conv_bias,
        grad_gains,
        grad_shifts,
        grad_in_bias,
        grad_out_bias,
        grad_head_weight,
        loss,
    ) = finish_small(
        stacks, 2 * conv_rows, width, head_weight.shape[1], hidden_width, places, sizes
    )
    grad_conv = place_conv_grads(stacks, 2, taps, slab, places, sizes)
    return (
        final_state,
        grad_inputs,
        grad_conv,
        grad_conv_bias,
        grad_gains,
        grad_shifts,
        grad_in,
        grad_in_bias,
        grad_out,
        grad_out_bias,
        grad_head_weight,
        loss.reshape(()),
    )


def solution(mesh):
    placed = (
        P(("dp", "tap"), "seq", None),
        P(("dp", "tap"), "seq"),
        P(("dp", "tap"), "seq"),
        P(None, None, "tap", None),
        P(),
        P(),
        P(),
        P(None, None, ("dp", "seq", "tap")),
        P(),
        P(None, ("dp", "seq", "tap"), None),
        P(),
        P(),
    )
    return jax.shard_map(
        on_device,
        mesh=mesh,
        in_specs=placed,
        out_specs=(
            P(("dp", "tap"), "seq", None),
            P(("dp", "tap"), "seq", None),
            P(None, None, "tap", None),
            P(),
            P(),
            P(),
            P(None, None, ("dp", "seq", "tap")),
            P(),
            P(None, ("dp", "seq", "tap"), None),
            P(),
            P(),
            P(),
        ),
        check_vma=False,
    )
```

```python
import functools

import jax
import jax.numpy as jnp
import numpy as np
from jax import lax
from jax.experimental import pallas as pl
from jax.experimental.pallas import tpu as pltpu
from jax.sharding import PartitionSpec as P

FIRST_DILATION = 4
SECOND_DILATION = 32
EPSILON = 1e-05
HIGHEST_PRECISION = lax.Precision.HIGHEST
CORES = 2
ROW_TILE = 16
MIB = 1024 * 1024
VMEM_BYTES = 20 * MIB
ANYWHERE = pl.BlockSpec(memory_space=pl.ANY)
SCALARS = pl.BlockSpec(memory_space=pltpu.SMEM)


TOKEN = jax.ShapeDtypeStruct((8, 128), jnp.float32)


def cost(microseconds):
    size = int(microseconds * 3.5e6)
    return pl.CostEstimate(flops=int(microseconds * 1.1e9), bytes_accessed=size, transcendentals=0)


WHOLE = pl.BlockSpec(memory_space=pltpu.VMEM)
TOKEN_SPEC = pl.BlockSpec(TOKEN.shape, lambda *_: (0, 0))


def tokens(after):
    return [TOKEN_SPEC] * len(after)


def in_hbm(array):
    return pltpu.with_memory_space_constraint(array, pltpu.HBM)


def low(values):
    return values.astype(jnp.bfloat16)


def wide(values):
    return values.astype(jnp.float32)


def gelu_parts(values):
    phi = 0.5 * (1.0 + lax.erf(values * 0.7071067811865476))
    return (
        values * phi,
        phi + values * jnp.exp(-0.5 * values * values) * 0.3989422804014327,
    )


def normalize(values):
    center = values - jnp.mean(values, -1, keepdims=True)
    scale = lax.rsqrt(jnp.mean(center * center, -1, keepdims=True) + EPSILON)
    return (center * scale, scale)


def norm_back(upstream, normed, scale):
    return scale * (
        upstream
        - jnp.mean(upstream, -1, keepdims=True)
        - normed * jnp.mean(upstream * normed, -1, keepdims=True)
    )


def tap_groups(taps):
    return 3 if taps % 3 == 0 else 1


def row_chunks(rows, most):
    size = min(rows, most)
    return [(first, size) for first in range(0, rows, size)]


def conv_forward(extended, weight, stream, bias, gain, shift, step, after=(), reads=()):
    taps, inner, width = weight.shape
    rows = stream.shape[0]
    group = tap_groups(taps)
    steps = taps // group

    def kernel(extended_ref, weight_ref, stream_ref, bias_ref, gain_ref, shift_ref, *refs):
        normed_ref, slope_ref, next_ref, lowered_ref, token_ref, total_ref = refs[-6:]
        token_ref[...] = jnp.zeros(TOKEN.shape, TOKEN.dtype)
        first = pl.program_id(0) * group
        total = None
        for j in range(group):
            start = pl.multiple_of((first + j) * step, ROW_TILE)
            term = jnp.dot(
                extended_ref[pl.ds(start, rows), :],
                weight_ref[j],
                preferred_element_type=jnp.float32,
            )
            total = term if total is None else total + term

        @pl.when(pl.program_id(0) == 0)
        def _():
            total_ref[...] = total

        @pl.when(pl.program_id(0) > 0)
        def _():
            total_ref[...] += total

        @pl.when(pl.program_id(0) == steps - 1)
        def _():
            for at, size in row_chunks(rows, 128):
                some = pl.ds(at, size)
                value, slope = gelu_parts(total_ref[some, :] + bias_ref[...])
                normed, scale = normalize(value)
                mid = wide(stream_ref[some, :]) + normed * gain_ref[...] + shift_ref[...]
                normed_ref[some, :] = low(normed)
                slope_ref[some, :] = low(scale * slope)
                next_ref[some, :] = mid
                lowered_ref[some, :] = low(mid)

    whole = pl.BlockSpec((rows, width), lambda g: (0, 0))
    row = pl.BlockSpec((1, width), lambda g: (0, 0))
    found = pl.pallas_call(
        kernel,
        grid=(steps,),
        in_specs=[
            pl.BlockSpec(extended.shape, lambda g: (0, 0)),
            pl.BlockSpec((group, inner, width), lambda g: (g, 0, 0)),
            whole,
            row,
            row,
            row,
        ]
        + tokens(after)
        + [ANYWHERE] * len(reads),
        out_specs=[whole] * 4 + [TOKEN_SPEC],
        out_shape=[
            pltpu.HBM((rows, width), jnp.bfloat16),
            pltpu.HBM((rows, width), jnp.bfloat16),
            pltpu.HBM((rows, width), jnp.float32),
            jax.ShapeDtypeStruct((rows, width), jnp.bfloat16),
            TOKEN,
        ],
        scratch_shapes=[pltpu.VMEM((rows, width), jnp.float32)],
        compiler_params=pltpu.CompilerParams(vmem_limit_bytes=VMEM_BYTES),
        cost_estimate=cost(9),
        name="conv_forward",
    )(extended, in_hbm(weight), in_hbm(stream) if stream.dtype == jnp.float32 else stream, bias[None], gain[None], shift[None], *after, *reads)
    return found[:4], (found[4],)


def ffn_forward(
    lowered,
    stream,
    ins,
    outs,
    in_biases,
    out_bias,
    gain,
    shift,
    seq_index,
    reach,
    last_block,
    after=(),
    reads=(),
):
    rows, width = lowered.shape
    cores = len(ins)
    units = ins[0].shape[0]
    block = min(units, 256)
    steps = units // block

    rims_out = 1 if reach else 0

    def kernel(place_ref, lowered_ref, stream_ref, out_bias_ref, gain_ref, shift_ref, *refs):
        in_refs, out_refs, bias_refs = (refs[i * cores : (i + 1) * cores] for i in range(3))
        found_refs = refs[-6 - 2 * cores - rims_out :]
        active_ref, slope_refs = found_refs[0], found_refs[1 : 1 + cores]
        normed_ref, scale_ref, next_ref, rounded_ref = found_refs[1 + cores : 5 + cores]
        packet_refs = found_refs[5 + cores : 4 + 2 * cores]
        token_ref, total_ref = found_refs[-2:]
        token_ref[...] = jnp.zeros(TOKEN.shape, TOKEN.dtype)
        lane = pl.multiple_of(width + pl.program_id(0) * block, block)

        @pl.when(pl.program_id(0) == 0)
        def _():
            total_ref[...] = jnp.zeros(total_ref.shape, jnp.float32)
            for packet_ref in packet_refs:
                packet_ref[:, :width] = lowered_ref[...]

        for at, size in row_chunks(rows, 256):
            some = pl.ds(at, size)
            term = None
            for c in range(cores):
                hidden = lax.dot_general(
                    lowered_ref[some, :],
                    in_refs[c][...],
                    (((1,), (1,)), ((), ())),
                    preferred_element_type=jnp.float32,
                )
                active, slope = gelu_parts(hidden + bias_refs[c][...])
                active = low(active)
                if c == 0:
                    active_ref[some, :] = active
                else:
                    packet_refs[c - 1][some, pl.ds(lane, block)] = active
                slope_refs[c][some, :] = low(slope)
                found = jnp.dot(active, out_refs[c][...], preferred_element_type=jnp.float32)
                term = found if term is None else term + found
            total_ref[some, :] += term

        @pl.when(pl.program_id(0) == steps - 1)
        def _():
            for at, size in row_chunks(rows, 128):
                some = pl.ds(at, size)
                normed, scale = normalize(total_ref[some, :] + out_bias_ref[...])
                after_ffn = stream_ref[some, :] + normed * gain_ref[...] + shift_ref[...]
                normed_ref[some, :] = low(normed)
                scale_ref[some, :] = jnp.broadcast_to(scale, (size, 128))
                next_ref[some, :] = after_ffn
                rounded_ref[some, :] = low(after_ffn)
            if reach:
                first = pl.multiple_of((1 - place_ref[0]) * (rows - reach), ROW_TILE)
                found_refs[-3][...] = rounded_ref[pl.ds(first, reach), :]

    whole = pl.BlockSpec((rows, width), lambda g: (0, 0))
    row = pl.BlockSpec((1, width), lambda g: (0, 0))
    piece = pl.BlockSpec((block, width), lambda g: (g, 0))
    columns = pl.BlockSpec((rows, block), lambda g: (0, g))
    hidden_shape = pltpu.HBM((rows, units), jnp.bfloat16)
    found = pl.pallas_call(
        kernel,
        grid=(steps,),
        in_specs=[SCALARS, whole, whole, row, row, row]
        + [piece] * (2 * cores)
        + [pl.BlockSpec((1, block), lambda g: (0, g))] * cores
        + tokens(after)
        + [ANYWHERE] * len(reads),
        out_specs=[columns] * (1 + cores)
        + [whole, pl.BlockSpec((rows, 128), lambda g: (0, 0)), whole, whole]
        + [pl.BlockSpec((rows, width + units), lambda g: (0, 0))] * (cores - 1)
        + [pl.BlockSpec((reach, width), lambda g: (0, 0))] * rims_out
        + [TOKEN_SPEC],
        out_shape=[hidden_shape] * (1 + cores)
        + [
            pltpu.HBM((rows, width), jnp.bfloat16),
            pltpu.HBM((rows, 128), jnp.float32),
            (jax.ShapeDtypeStruct if last_block else pltpu.HBM)((rows, width), jnp.float32),
            jax.ShapeDtypeStruct((rows, width), jnp.bfloat16),
        ]
        + [jax.ShapeDtypeStruct((rows, width + units), jnp.bfloat16)] * (cores - 1)
        + [jax.ShapeDtypeStruct((reach, width), jnp.bfloat16)] * rims_out
        + [TOKEN],
        scratch_shapes=[pltpu.VMEM((rows, width), jnp.float32)],
        compiler_params=pltpu.CompilerParams(vmem_limit_bytes=VMEM_BYTES),
        cost_estimate=cost(11),
        name="ffn_forward",
    )(
        seq_index.astype(jnp.int32)[None],
        lowered,
        in_hbm(stream),
        out_bias[None],
        gain[None],
        shift[None],
        *[in_hbm(each) for each in ins],
        *[in_hbm(each) for each in outs],
        *[each[None] for each in in_biases],
        *after,
        *reads,
    )
    return (
        found[0],
        found[1 : 1 + cores],
        found[1 + cores : 5 + cores],
        found[5 + cores : 4 + 2 * cores],
        found[4 + 2 * cores] if reach else None,
        (found[-1],),
    )


def head_and_loss(stream, head_weight, codes, after=()):
    rows, width = stream.shape
    classes = head_weight.shape[1]
    padded = jnp.pad(head_weight, ((0, 0), (0, 128 - classes)))
    cuts = row_chunks(rows, 256)

    def kernel(stream_ref, head_ref, code_ref, *refs):
        grad_ref, head_grad_ref, sums_ref, token_ref = refs[-4:]
        token_ref[...] = jnp.zeros(TOKEN.shape, TOKEN.dtype)
        head_grad = jnp.zeros((128, width), jnp.float32)
        objective = jnp.zeros((1, 1), jnp.float32)
        scored = jnp.zeros((1, 1), jnp.float32)
        for at, size in cuts:
            some = pl.ds(at, size)
            value = stream_ref[some, :]
            code = code_ref[some, :]
            mask = jnp.where(code[:, :1] >= classes, 1.0, 0.0)
            logits = jnp.dot(
                value, head_ref[...], precision=HIGHEST_PRECISION, preferred_element_type=jnp.float32
            )
            lane = lax.broadcasted_iota(jnp.int32, logits.shape, 1)
            valid = lane < classes
            peak = jnp.max(jnp.where(valid, logits, -jnp.inf), -1, keepdims=True)
            exponent = jnp.where(valid, jnp.exp(jnp.where(valid, logits - peak, 0.0)), 0.0)
            denominator = jnp.sum(exponent, -1, keepdims=True)
            chosen = lane == jnp.where(code >= classes, code - classes, code)
            picked = jnp.sum(jnp.where(chosen, logits, 0.0), -1, keepdims=True)
            terms = mask * (peak + jnp.log(denominator) - picked)
            objective = objective + jnp.sum(terms, 0, keepdims=True)
            scored = scored + jnp.sum(mask, 0, keepdims=True)
            logit_grad = mask * (exponent / denominator - jnp.where(chosen, 1.0, 0.0))
            grad_ref[some, :] = lax.dot_general(
                logit_grad,
                head_ref[...],
                (((1,), (1,)), ((), ())),
                precision=HIGHEST_PRECISION,
                preferred_element_type=jnp.float32,
            )
            head_grad = head_grad + lax.dot_general(
                logit_grad,
                value,
                (((0,), (0,)), ((), ())),
                precision=HIGHEST_PRECISION,
                preferred_element_type=jnp.float32,
            )
        head_grad_ref[...] = head_grad[: head_grad_ref.shape[0]]
        at_row = lax.broadcasted_iota(jnp.int32, sums_ref.shape, 0)
        sums_ref[...] = jnp.where(at_row == 0, objective, scored)

    found = pl.pallas_call(
        kernel,
        out_shape=[
            jax.ShapeDtypeStruct((rows, width), jnp.float32),
            jax.ShapeDtypeStruct((-(-classes // 8) * 8, width), jnp.float32),
            jax.ShapeDtypeStruct((8, 128), jnp.float32),
            TOKEN,
        ],
        compiler_params=pltpu.CompilerParams(vmem_limit_bytes=VMEM_BYTES),
        cost_estimate=cost(6),
        name="head_and_loss",
    )(stream, padded, codes, *after)
    return found[:3], (found[3],)


def ffn_back_hidden(upstream, normed, scale, gain, outs, slopes, after=()):
    rows, width = upstream.shape
    cores = len(outs)
    units = outs[0].shape[0]
    block = min(units, 256)

    def kernel(upstream_ref, normed_ref, scale_ref, gain_ref, *refs):
        out_refs, slope_refs = refs[:cores], refs[cores : 2 * cores]
        found_refs = refs[-3 - 2 * cores :]
        output_grad_ref, hidden_ref = found_refs[:2]
        bias_refs, packet_refs = found_refs[2 : 2 + cores], found_refs[2 + cores : -2]
        sums_ref, token_ref = found_refs[-2:]
        token_ref[...] = jnp.zeros(TOKEN.shape, TOKEN.dtype)
        lane = pl.multiple_of(width + pl.program_id(0) * block, block)

        @pl.when(pl.program_id(0) == 0)
        def _():
            totals = [jnp.zeros((1, width), jnp.float32)] * 3
            for at, size in row_chunks(rows, 128):
                some = pl.ds(at, size)
                grad, value = upstream_ref[some, :], wide(normed_ref[some, :])
                output_grad = low(norm_back(grad * gain_ref[...], value, scale_ref[some, :1]))
                output_grad_ref[some, :] = output_grad
                for packet_ref in packet_refs:
                    packet_ref[some, :width] = output_grad
                for i, each in enumerate((grad * value, grad, wide(output_grad))):
                    totals[i] = totals[i] + jnp.sum(each, 0, keepdims=True)
            sums_ref[...] = jnp.zeros(sums_ref.shape, jnp.float32)
            for i in range(3):
                sums_ref[i : i + 1, :] = totals[i]

        for c in range(cores):
            total = jnp.zeros((1, block), jnp.float32)
            for at, size in row_chunks(rows, 512):
                some = pl.ds(at, size)
                active_grad = lax.dot_general(
                    output_grad_ref[some, :],
                    out_refs[c][...],
                    (((1,), (1,)), ((), ())),
                    preferred_element_type=jnp.float32,
                )
                hidden_grad = low(active_grad * wide(slope_refs[c][some, :]))
                if c == 0:
                    hidden_ref[some, :] = hidden_grad
                else:
                    packet_refs[c - 1][some, pl.ds(lane, block)] = hidden_grad
                total = total + jnp.sum(wide(hidden_grad), 0, keepdims=True)
            bias_refs[c][...] = total

    whole = pl.BlockSpec((rows, width), lambda g: (0, 0))
    columns = pl.BlockSpec((rows, block), lambda g: (0, g))
    found = pl.pallas_call(
        kernel,
        grid=(units // block,),
        in_specs=[
            whole,
            whole,
            pl.BlockSpec((rows, 128), lambda g: (0, 0)),
            pl.BlockSpec((1, width), lambda g: (0, 0)),
        ]
        + [pl.BlockSpec((block, width), lambda g: (g, 0))] * cores
        + [columns] * cores
        + tokens(after),
        out_specs=[whole, columns]
        + [pl.BlockSpec((1, block), lambda g: (0, g))] * cores
        + [pl.BlockSpec((rows, width + units), lambda g: (0, 0))] * (cores - 1)
        + [pl.BlockSpec((8, width), lambda g: (0, 0)), TOKEN_SPEC],
        out_shape=[
            jax.ShapeDtypeStruct((rows, width), jnp.bfloat16),
            pltpu.HBM((rows, units), jnp.bfloat16),
        ]
        + [jax.ShapeDtypeStruct((1, units), jnp.float32)] * cores
        + [jax.ShapeDtypeStruct((rows, width + units), jnp.bfloat16)] * (cores - 1)
        + [jax.ShapeDtypeStruct((8, width), jnp.float32), TOKEN],
        compiler_params=pltpu.CompilerParams(vmem_limit_bytes=VMEM_BYTES),
        cost_estimate=cost(6),
        name="ffn_back_hidden",
    )(
        upstream,
        in_hbm(normed),
        in_hbm(scale),
        gain[None],
        *[in_hbm(each) for each in outs],
        *[in_hbm(each) for each in slopes],
        *after,
    )
    return (
        found[0],
        found[1],
        found[2 : 2 + cores],
        found[2 + cores : -2],
        found[-2],
        (found[-1],),
    )


def ffn_back_stream(
    upstream, hidden, packets, ins, normed, slope, gain, places, reach, after=(), reads=(), relay=False
):
    rows, width = upstream.shape
    cores = len(ins)
    units = ins[0].shape[0]
    block = min(units, 256)
    steps = units // block
    lanes = width // cores
    relays = cores - 1 if relay else 0
    rims_out = 1 if reach else 0

    def kernel(core_ref, upstream_ref, normed_ref, slope_ref, gain_ref, *refs):
        hidden_refs, in_refs = refs[:cores], refs[cores : 2 * cores]
        found_refs = refs[-4 - cores - relays - rims_out :]
        mid_ref, conv_grad_ref = found_refs[:2]
        cut_refs = found_refs[2 : 1 + cores]
        sums_ref, token_ref, total_ref = found_refs[-3:]
        token_ref[...] = jnp.zeros(TOKEN.shape, TOKEN.dtype)
        for i in range(relays):
            relay_ref = found_refs[1 + cores + i]
            lane = pl.multiple_of(width + pl.program_id(0) * block, block)
            relay_ref[:, pl.ds(lane, block)] = hidden_refs[1 + i][...]

            @pl.when(pl.program_id(0) == 0)
            def _(i=i, relay_ref=relay_ref):
                relay_ref[:, :width] = refs[2 * cores + i][...]

        @pl.when(pl.program_id(0) == 0)
        def _():
            total_ref[...] = upstream_ref[...]

        for at, size in row_chunks(rows, 512):
            some = pl.ds(at, size)
            total_ref[some, :] += sum(
                jnp.dot(
                    hidden_refs[c][some, :], in_refs[c][...], preferred_element_type=jnp.float32
                )
                for c in range(cores)
            )

        @pl.when(pl.program_id(0) == steps - 1)
        def _():
            totals = [jnp.zeros((1, width), jnp.float32)] * 3
            for at, size in row_chunks(rows, 128):
                some = pl.ds(at, size)
                grad, value = total_ref[some, :], wide(normed_ref[some, :])
                conv_grad = low(norm_back(grad * gain_ref[...], value, wide(slope_ref[some, :])))
                mid_ref[some, :] = grad
                conv_grad_ref[some, :] = conv_grad
                for i, each in enumerate((grad * value, grad, wide(conv_grad))):
                    totals[i] = totals[i] + jnp.sum(each, 0, keepdims=True)
            sums_ref[...] = jnp.zeros(sums_ref.shape, jnp.float32)
            for i in range(3):
                sums_ref[i : i + 1, :] = totals[i]
            for c in range(1, cores):
                first = lax.rem(core_ref[0] - c + cores, cores) * lanes
                cut_refs[c - 1][...] = conv_grad_ref[:, pl.ds(pl.multiple_of(first, lanes), lanes)]
            if reach:
                first = pl.multiple_of((1 - core_ref[1]) * (rows - reach), ROW_TILE)
                found_refs[-4][...] = conv_grad_ref[pl.ds(first, reach), :]

    whole = pl.BlockSpec((rows, width), lambda g, core: (0, 0))
    found = pl.pallas_call(
        kernel,
        grid_spec=pltpu.PrefetchScalarGridSpec(
            num_scalar_prefetch=1,
            grid=(steps,),
            in_specs=[whole, whole, whole, pl.BlockSpec((1, width), lambda g, core: (0, 0))]
            + [pl.BlockSpec((rows, block), lambda g, core: (0, g))]
            + [pl.BlockSpec((rows, block), lambda g, core: (0, width // block + g))] * (cores - 1)
            + [pl.BlockSpec((block, width), lambda g, core: (g, 0))] * cores
            + [whole] * relays
            + tokens(after)
            + [ANYWHERE] * len(reads),
            out_specs=[whole, whole]
            + [pl.BlockSpec((rows, lanes), lambda g, core: (0, 0))] * (cores - 1)
            + [pl.BlockSpec((rows, width + units), lambda g, core: (0, 0))] * relays
            + [pl.BlockSpec((reach, width), lambda g, core: (0, 0))] * rims_out
            + [pl.BlockSpec((8, width), lambda g, core: (0, 0)), TOKEN_SPEC],
            scratch_shapes=[pltpu.VMEM((rows, width), jnp.float32)],
        ),
        out_shape=[
            jax.ShapeDtypeStruct((rows, width), jnp.float32),
            jax.ShapeDtypeStruct((rows, width), jnp.bfloat16),
        ]
        + [jax.ShapeDtypeStruct((rows, lanes), jnp.bfloat16)] * (cores - 1)
        + [jax.ShapeDtypeStruct((rows, width + units), jnp.bfloat16)] * relays
        + [jax.ShapeDtypeStruct((reach, width), jnp.bfloat16)] * rims_out
        + [jax.ShapeDtypeStruct((8, width), jnp.float32), TOKEN],
        compiler_params=pltpu.CompilerParams(vmem_limit_bytes=VMEM_BYTES),
        cost_estimate=cost(5),
        name="ffn_back_stream",
    )(
        jnp.stack(places[:2]).astype(jnp.int32),
        upstream,
        in_hbm(normed),
        in_hbm(slope),
        gain[None],
        in_hbm(hidden),
        *packets,
        *[in_hbm(each) for each in ins],
        *packets[:relays],
        *after,
        *reads,
    )
    return (
        found[0],
        found[1],
        found[2 : 1 + cores],
        found[1 + cores : 1 + cores + relays],
        found[1 + cores + relays] if reach else None,
        found[-2],
        (found[-1],),
    )


def conv_data_grad(extended, weight, upstream, step, kind, after=()):
    taps, inner, width = weight.shape
    rows = upstream.shape[0]
    group = tap_groups(taps)
    steps = taps // group

    def kernel(extended_ref, weight_ref, upstream_ref, *refs):
        out_ref, token_ref, total_ref = refs[-3:]
        token_ref[...] = jnp.zeros(TOKEN.shape, TOKEN.dtype)
        first = pl.program_id(0) * group
        total = None
        for j in range(group):
            start = pl.multiple_of((taps - 1 - first - j) * step, ROW_TILE)
            term = lax.dot_general(
                extended_ref[pl.ds(start, rows), :],
                weight_ref[j],
                (((1,), (1,)), ((), ())),
                preferred_element_type=jnp.float32,
            )
            total = term if total is None else total + term

        @pl.when(pl.program_id(0) == 0)
        def _():
            total_ref[...] = total

        @pl.when(pl.program_id(0) > 0)
        def _():
            total_ref[...] += total

        @pl.when(pl.program_id(0) == steps - 1)
        def _():
            out_ref[...] = (upstream_ref[...] + wide(low(total_ref[...]))).astype(kind)

    whole = pl.BlockSpec((rows, inner), lambda g: (0, 0))
    found = pl.pallas_call(
        kernel,
        grid=(steps,),
        in_specs=[
            pl.BlockSpec(extended.shape, lambda g: (0, 0)),
            pl.BlockSpec((group, inner, width), lambda g: (g, 0, 0)),
            whole,
        ]
        + tokens(after),
        out_specs=(whole, TOKEN_SPEC),
        out_shape=(jax.ShapeDtypeStruct((rows, inner), kind), TOKEN),
        scratch_shapes=[pltpu.VMEM((rows, inner), jnp.float32)],
        compiler_params=pltpu.CompilerParams(vmem_limit_bytes=VMEM_BYTES),
        cost_estimate=cost(6),
        name="conv_data_grad",
    )(extended, in_hbm(weight), upstream, *after)
    return found[0], (found[1],)


def hold(arrays, after, reads=()):
    count = len(arrays)
    if count == 0:
        return [], after

    def kernel(*refs):
        refs[-1][...] = jnp.zeros(TOKEN.shape, TOKEN.dtype)

    found = pl.pallas_call(
        kernel,
        in_specs=[ANYWHERE] * (count + len(reads)) + [WHOLE] * len(after),
        out_specs=[ANYWHERE] * count + [WHOLE],
        out_shape=[jax.ShapeDtypeStruct(each.shape, each.dtype) for each in arrays] + [TOKEN],
        input_output_aliases={i: i for i in range(count)},
        compiler_params=pltpu.CompilerParams(vmem_limit_bytes=1 * MIB),
        cost_estimate=cost(0.5),
        name="hold",
    )(*arrays, *reads, *after)
    return list(found[:-1]), (found[-1],)


def join_rows(parts, after=(), reads=()):
    def kernel(*refs):
        out_ref, token_ref = refs[-2:]
        token_ref[...] = jnp.zeros(TOKEN.shape, TOKEN.dtype)
        first = 0
        for i, part in enumerate(parts):
            out_ref[first : first + part.shape[0]] = refs[i][...]
            first += part.shape[0]

    shape = (sum(part.shape[0] for part in parts), parts[0].shape[1])
    found = pl.pallas_call(
        kernel,
        in_specs=[WHOLE] * len(parts) + [ANYWHERE] * len(reads) + [WHOLE] * len(after),
        out_specs=[WHOLE] * 2,
        out_shape=[jax.ShapeDtypeStruct(shape, parts[0].dtype), TOKEN],
        compiler_params=pltpu.CompilerParams(vmem_limit_bytes=10 * MIB),
        cost_estimate=cost(1.5),
        name="join_rows",
    )(*parts, *reads, *after)
    return found[0], (found[1],)


def restack(groups, reads=(), after=(), fixed=False):
    cuts = [cut for _, each in groups for cut in each]
    if any(last is not None and (first % ROW_TILE or last % ROW_TILE) for first, last, _ in cuts):
        return [
            jnp.stack([array[first:last].reshape(shape) for array in arrays])
            for arrays, each in groups
            for first, last, shape in each
        ], after
    flat = [array for arrays, _ in groups for array in arrays]
    plan = []
    shapes = []
    at = 0
    for arrays, each in groups:
        for first, last, shape in each:
            for slot in range(len(arrays)):
                plan.append((at + slot, first, last, len(shapes), slot))
            held = shape if last is None else (last - first,) + arrays[0].shape[1:]
            shapes.append(jax.ShapeDtypeStruct((len(arrays),) + held, arrays[0].dtype))
        at += len(arrays)

    def kernel(*refs):
        out_refs = refs[-2 - len(shapes) : -2]
        token_ref, sem_ref = refs[-2:]
        token_ref[...] = jnp.zeros(TOKEN.shape, TOKEN.dtype)
        copies = []
        for source, first, last, target, slot in plan:
            ref = refs[source]
            copies.append(
                pltpu.make_async_copy(
                    ref if last is None else ref.at[pl.ds(first, last - first)],
                    out_refs[target].at[slot],
                    sem_ref.at[len(copies)],
                )
            )
        copy_all(copies)

    found = pl.pallas_call(
        kernel,
        in_specs=[ANYWHERE] * (len(flat) + len(reads)) + [WHOLE] * len(after),
        out_specs=[WHOLE] * (len(shapes) + 1),
        out_shape=shapes + [TOKEN],
        scratch_shapes=[pltpu.SemaphoreType.DMA((len(plan),))],
        compiler_params=pltpu.CompilerParams(vmem_limit_bytes=10 * MIB),
        cost_estimate=cost(1.5),
        name="restack",
    )(*([in_hbm(each) for each in flat] if fixed else flat), *reads, *after)
    return [
        each.reshape((each.shape[0],) + shape) for each, (_, _, shape) in zip(found, cuts)
    ], (found[-1],)


def conv_weight_grad(
    extendeds, upstream, arrived, places, sizes, taps, step, after=(), reads=()
):
    cores, seqs, acrosses, tap_peers = sizes
    rows = upstream.shape[0]
    inner = extendeds[0].shape[1]
    lanes = upstream.shape[1] // cores
    slab = inner // (seqs * acrosses * tap_peers)
    direct = slab % ROW_TILE == 0
    half = (tap_peers + 1) // 2
    rest = tap_peers - half
    seconds = acrosses if rest else 0
    outs = seqs + seconds if direct else 1

    def kernel(place_ref, *refs):
        out_refs = refs[-2 - outs : -2]
        token_ref, found_ref = refs[-2:]
        token_ref[...] = jnp.zeros(TOKEN.shape, TOKEN.dtype)
        start = pl.multiple_of(pl.program_id(0) * step, ROW_TILE)
        found = low(
            sum(
                lax.dot_general(
                    refs[c][pl.ds(start, rows), :],
                    refs[cores + c][...],
                    (((0,), (0,)), ((), ())),
                    preferred_element_type=jnp.float32,
                )
                for c in range(cores)
            )
        )
        if not direct:
            out_refs[0][0] = found
            return
        found_ref[...] = found

        def chunk(slot_t, slot_s, slot_a):
            t = lax.rem(place_ref[3] - slot_t + tap_peers, tap_peers)
            at = lax.rem(place_ref[1] - slot_s + seqs, seqs)
            a = lax.rem(place_ref[2] - slot_a + acrosses, acrosses)
            first = pl.multiple_of(((t * seqs + at) * acrosses + a) * slab, slab)
            return found_ref[pl.ds(first, slab), :]

        for s in range(seqs):
            for a in range(acrosses):
                for t in range(half):
                    out_refs[s][a, t, 0] = chunk(t, s, a)
                for t in range(half, tap_peers):
                    out_refs[seqs + a][s, t - half, 0] = chunk(t, s, a)

    if direct:
        shapes = [(acrosses, half, taps, slab, lanes)] * seqs
        shapes += [(seqs, rest, taps, slab, lanes)] * seconds
        specs = [
            pl.BlockSpec(shape[:2] + (1, slab, lanes), lambda k, place: (0, 0, k, 0, 0))
            for shape in shapes
        ]
    else:
        shapes = [(taps, inner, lanes)]
        specs = [pl.BlockSpec((1, inner, lanes), lambda k, place: (k, 0, 0))]
    found = pl.pallas_call(
        kernel,
        grid_spec=pltpu.PrefetchScalarGridSpec(
            num_scalar_prefetch=1,
            grid=(taps,),
            in_specs=[pl.BlockSpec(extendeds[0].shape, lambda k, place: (0, 0))] * cores
            + [pl.BlockSpec((rows, lanes), lambda k, place: (0, place[0]))]
            + [pl.BlockSpec((rows, lanes), lambda k, place: (0, 0))] * (cores - 1)
            + tokens(after)
            + [ANYWHERE] * len(reads),
            out_specs=specs + [TOKEN_SPEC],
            scratch_shapes=[pltpu.VMEM((inner, lanes), jnp.bfloat16)],
        ),
        out_shape=[jax.ShapeDtypeStruct(shape, jnp.bfloat16) for shape in shapes] + [TOKEN],
        compiler_params=pltpu.CompilerParams(vmem_limit_bytes=VMEM_BYTES),
        cost_estimate=cost(9),
        name="conv_weight_grad",
    )(jnp.stack(places).astype(jnp.int32), *extendeds, upstream, *arrived, *after, *reads)
    token = found[-1]
    if not direct:
        found = found[0].reshape(taps, tap_peers, seqs, acrosses, slab, lanes)
        for axis, which in ((1, 3), (2, 1), (3, 2)):
            found = relative(found, axis, places[which], sizes[which])
        found = found.transpose(2, 3, 1, 0, 4, 5)
        found = [found[s, :, :half] for s in range(seqs)] + [
            found[:, a, half:] for a in range(seconds)
        ]
    flat = [each.reshape(-1, lanes) for each in found[: seqs + seconds]]
    return flat[:seqs], flat[seqs:], token


def ffn_weight_grad(pairs, sizes, ffn_rows, after=()):
    cores, seqs, acrosses, tap_peers = sizes
    rows, width = pairs[0][1].shape
    block = tap_peers * ffn_rows
    half = (tap_peers + 1) // 2
    rest = tap_peers - half
    seconds = seqs if rest else 0
    transposed = (((0,), (0,)), ((), ()))
    if ffn_rows % ROW_TILE:
        found = jnp.stack(
            [
                low(
                    sum(
                        lax.dot_general(a, b, transposed, preferred_element_type=jnp.float32)
                        for a, b in [(left, right)]
                        + [(ends[:, width:], starts[:, :width]) for ends, starts in packets]
                    )
                ).reshape(acrosses, seqs, tap_peers, ffn_rows, width)
                for left, right, packets in pairs
            ],
            3,
        )
        token = jnp.zeros(TOKEN.shape, TOKEN.dtype)
        return (
            [found[a, :, :half].reshape(-1, width) for a in range(acrosses)],
            [found[:, s, half:].reshape(-1, width) for s in range(seconds)],
            token,
        )
    outs = acrosses + seconds

    def kernel(*refs):
        out_refs, token_ref = refs[-1 - outs : -1], refs[-1]
        token_ref[...] = jnp.zeros(TOKEN.shape, TOKEN.dtype)
        step = pl.program_id(0)
        for which in range(2):
            base = 2 * cores * which
            found = low(
                sum(
                    lax.dot_general(
                        refs[base + 2 * c][...],
                        refs[base + 2 * c + 1][...],
                        transposed,
                        preferred_element_type=jnp.float32,
                    )
                    for c in range(cores)
                )
            ).reshape(tap_peers, ffn_rows, width)
            for a in range(acrosses):

                @pl.when(step // seqs == a)
                def _(a=a):
                    out_refs[a][0, :, which] = found[:half]

            for s in range(seconds):

                @pl.when(lax.rem(step, seqs) == s)
                def _(s=s):
                    out_refs[acrosses + s][0, :, which] = found[half:]

    right_spec = pl.BlockSpec((rows, width), lambda g: (0, 0))
    left_spec = pl.BlockSpec((rows, block), lambda g: (0, g))
    late_spec = pl.BlockSpec((rows, block), lambda g: (0, width // block + g))

    def first_spec(a):
        return pl.BlockSpec(
            (1, half, 2, ffn_rows, width),
            lambda g: (jnp.clip(g - a * seqs, 0, seqs - 1), 0, 0, 0, 0),
        )

    second_spec = pl.BlockSpec(
        (1, rest, 2, ffn_rows, width), lambda g: (g // seqs, 0, 0, 0, 0)
    )
    operands = []
    for left, right, packets in pairs:
        operands += [in_hbm(left), right]
        for ends, starts in packets:
            operands += [ends, starts]
    found = pl.pallas_call(
        kernel,
        grid=(acrosses * seqs,),
        in_specs=([left_spec, right_spec] + [late_spec, right_spec] * (cores - 1)) * 2
        + tokens(after),
        out_specs=[first_spec(a) for a in range(acrosses)]
        + [second_spec] * seconds
        + [TOKEN_SPEC],
        out_shape=[jax.ShapeDtypeStruct((seqs, half, 2, ffn_rows, width), jnp.bfloat16)] * acrosses
        + [jax.ShapeDtypeStruct((acrosses, rest, 2, ffn_rows, width), jnp.bfloat16)] * seconds
        + [TOKEN],
        compiler_params=pltpu.CompilerParams(vmem_limit_bytes=VMEM_BYTES),
        cost_estimate=cost(8),
        name="ffn_weight_grad",
    )(*operands, *after)
    flat = [each.reshape(-1, width) for each in found[:-1]]
    return flat[:acrosses], flat[acrosses:], found[-1]


def group_slots(groups, lanes):
    flat, where = [], []
    rows = groups[0][0][0].size // (groups[0][1] * lanes)
    for parts, slots in groups:
        where += [(len(flat), len(parts), slot) for slot in range(slots)]
        flat += [part.reshape(slots, rows, lanes) for part in parts]
    return flat, where, rows


def slot_sum(refs, place, first=0):
    start, count, at = place
    return low(sum(wide(refs[first + start + i][at]) for i in range(count)))


def merge_slots(conv_groups, ffn_groups, after=()):
    lanes, width = conv_groups[0][0][0].shape[-1], ffn_groups[0][0][0].shape[-1]
    cuts = width // lanes
    conv_parts, conv_where, conv_rows = group_slots(conv_groups, lanes)
    ffn_parts, ffn_where, ffn_rows = group_slots(ffn_groups, width)
    slots = len(conv_where)
    if conv_rows % ROW_TILE or ffn_rows % ROW_TILE:
        merged = []
        for slot in range(slots):
            ffn = slot_sum(ffn_parts, ffn_where[slot])
            merged.append(
                jnp.concatenate(
                    [slot_sum(conv_parts, conv_where[slot])]
                    + [ffn[:, i * lanes : (i + 1) * lanes] for i in range(cuts)]
                )
            )
        return merged, after

    def kernel(*refs):
        out_refs, token_ref = refs[-1 - slots : -1], refs[-1]
        token_ref[...] = jnp.zeros(TOKEN.shape, TOKEN.dtype)
        for slot in range(slots):
            out_refs[slot][:conv_rows] = slot_sum(refs, conv_where[slot])
            ffn = slot_sum(refs, ffn_where[slot], len(conv_parts))
            for i in range(cuts):
                first = conv_rows + i * ffn_rows
                out_refs[slot][first : first + ffn_rows] = ffn[:, i * lanes : (i + 1) * lanes]

    found = pl.pallas_call(
        kernel,
        in_specs=[WHOLE] * (len(conv_parts) + len(ffn_parts) + len(after)),
        out_specs=[WHOLE] * (slots + 1),
        out_shape=[jax.ShapeDtypeStruct((conv_rows + cuts * ffn_rows, lanes), jnp.bfloat16)] * slots
        + [TOKEN],
        compiler_params=pltpu.CompilerParams(vmem_limit_bytes=10 * MIB),
        cost_estimate=cost(1.5),
        name="merge_slots",
    )(*conv_parts, *ffn_parts, *after)
    return found[:slots], (found[slots],)


def append_slots(groups, packed, after=(), reads=()):
    lanes = groups[0][0][0].shape[-1]
    parts, where, rows = group_slots(groups, lanes)
    slots = len(where)
    if rows % ROW_TILE:
        return [
            jnp.concatenate([slot_sum(parts, where[slot])] + packed) for slot in range(slots)
        ], after

    def kernel(*refs):
        out_refs, token_ref = refs[-1 - slots : -1], refs[-1]
        token_ref[...] = jnp.zeros(TOKEN.shape, TOKEN.dtype)
        for slot in range(slots):
            out_refs[slot][:rows] = slot_sum(refs, where[slot])
            if packed:
                out_refs[slot][rows:] = refs[len(parts)][...]

    shape = jax.ShapeDtypeStruct((rows + sum(each.shape[0] for each in packed), lanes), jnp.bfloat16)
    found = pl.pallas_call(
        kernel,
        in_specs=[WHOLE] * (len(packed) + len(parts) + len(after)) + [ANYWHERE] * len(reads),
        out_specs=[WHOLE] * (slots + 1),
        out_shape=[shape] * slots + [TOKEN],
        compiler_params=pltpu.CompilerParams(vmem_limit_bytes=8 * MIB),
        cost_estimate=cost(1),
        name="append_slots",
    )(*parts, *packed, *after, *reads)
    return found[:slots], (found[slots],)


def pack_small(row_groups, biases, losses, places, sizes, ffn_rows, after=()):
    cores, seqs, acrosses, tap_peers = sizes
    width = row_groups[0][0].shape[1]
    head_rows = sum(count for _, count in row_groups)
    hidden = cores * biases[0][0].shape[1]
    bias_rows = hidden // width
    used = head_rows + len(biases) * bias_rows + 2
    rows = -(-used // ROW_TILE) * ROW_TILE
    lanes = width // 2
    per_row = width // ffn_rows
    if ffn_rows % 64:
        terms = jnp.stack([losses[0, 0], losses[1, 0]])
        terms = jnp.stack([terms, terms - wide(low(terms))])
        pieces = [array[:count] for array, count in row_groups]
        for each in biases:
            bias = jnp.stack(each).reshape(cores, acrosses, seqs, tap_peers, ffn_rows)
            for axis, which in enumerate((0, 2, 1, 3)):
                bias = relative(bias, axis, places[which], sizes[which])
            pieces.append(bias.transpose(1, 0, 2, 3, 4).reshape(-1, width))
        pieces.append(jnp.pad(terms, ((0, rows - used), (0, width - 2))))
        packed = low(jnp.concatenate(pieces))
        return jnp.concatenate([packed[:, :lanes], packed[:, lanes:]]), after

    def kernel(place_ref, *refs):
        packed_ref, token_ref, rows_ref = refs[-3:]
        token_ref[...] = jnp.zeros(TOKEN.shape, TOKEN.dtype)
        rows_ref[...] = jnp.zeros(rows_ref.shape, jnp.float32)
        at = 0
        for i, (_, count) in enumerate(row_groups):
            rows_ref[at : at + count, :] = refs[i][:count, :]
            at += count
        shape = (cores, acrosses, seqs, tap_peers)
        owners = (0, 2, 1, 3)
        for b in range(len(biases)):
            blocks = {}
            for slot in np.ndindex(*shape):
                first = ((slot[1] * seqs + slot[2]) * tap_peers + slot[3]) * ffn_rows
                ref = refs[len(row_groups) + b * cores + slot[0]]
                blocks[slot] = ref[:, first : first + ffn_rows]
            for axis, size in enumerate(shape):
                turned = {}
                for slot in blocks:
                    place = lax.rem(place_ref[owners[axis]] - slot[axis] + size, size)
                    value = blocks[slot[:axis] + (0,) + slot[axis + 1 :]]
                    for other in range(1, size):
                        candidate = blocks[slot[:axis] + (other,) + slot[axis + 1 :]]
                        value = jnp.where(place == other, candidate, value)
                    turned[slot] = value
                blocks = turned
            ordered = [
                blocks[(c, a, s, t)]
                for a in range(acrosses)
                for c in range(cores)
                for s in range(seqs)
                for t in range(tap_peers)
            ]
            for row in range(bias_rows):
                line = ordered[row * per_row : (row + 1) * per_row]
                rows_ref[at : at + 1, :] = jnp.concatenate(line, 1)
                at += 1
        losses_ref = refs[len(row_groups) + len(biases) * cores]
        lane = lax.broadcasted_iota(jnp.int32, (1, width), 1)
        objective = jnp.broadcast_to(losses_ref[0:1, 0:1], (1, width))
        scored = jnp.broadcast_to(losses_ref[1:2, 0:1], (1, width))
        line = jnp.where(lane == 0, objective, jnp.where(lane == 1, scored, 0.0))
        rows_ref[at : at + 1, :] = line
        rows_ref[at + 1 : at + 2, :] = line - wide(low(line))
        packed_ref[:rows, :] = low(rows_ref[:, :lanes])
        packed_ref[rows:, :] = low(rows_ref[:, lanes:])

    flat = [array for array, _ in row_groups] + [each for some in biases for each in some]
    found = pl.pallas_call(
        kernel,
        in_specs=[SCALARS] + [WHOLE] * (len(flat) + 1 + len(after)),
        out_specs=[WHOLE] * 2,
        out_shape=[jax.ShapeDtypeStruct((2 * rows, lanes), jnp.bfloat16), TOKEN],
        scratch_shapes=[pltpu.VMEM((rows, width), jnp.float32)],
        compiler_params=pltpu.CompilerParams(vmem_limit_bytes=8 * MIB),
        cost_estimate=cost(2),
        name="pack_small",
    )(jnp.stack(places).astype(jnp.int32), *flat, losses, *after)
    return found[0], (found[1],)


def paired(values):
    while len(values) > 1:
        half = len(values) // 2
        if len(values) % 2:
            return sum(values[1:], values[0])
        values = [values[i] + values[i + half] for i in range(half)]
    return values[0]


def finish_small(stacks, first, width, classes, hidden, places, sizes):
    cores, seqs, acrosses = sizes[:3]
    peers, rows, lanes = stacks[0].shape
    count = rows - first
    bias_rows = hidden // width
    at_bias = 12 + classes
    at_loss = at_bias + 2 * bias_rows

    def pick(row):
        return (
            [row(2), row(5)],
            [[row(0), row(6)], [row(3), row(9)]],
            [[row(1), row(7)], [row(4), row(10)]],
            [[row(at_bias + b * bias_rows + i) for i in range(bias_rows)] for b in range(2)],
            [row(8), row(11)],
        )

    if max(cores, seqs, acrosses) > 2 or first % count or count % ROW_TILE:
        full = jnp.stack(
            [wide(each[:, first:]).reshape(seqs, acrosses, count, lanes) for each in stacks]
        )
        for axis, (place, size) in enumerate(zip(places[:3], sizes[:3])):
            full = relative(full, axis, place, size)
        total = jnp.sum(full, (0, 1, 2))
        total = jnp.concatenate([total[: count // 2], total[count // 2 :]], 1)
        conv_bias, gains, shifts, in_bias, out_bias = pick(lambda i: total[i])
        terms = total[at_loss] + total[at_loss + 1]
        return (
            jnp.stack(conv_bias),
            jnp.stack([jnp.stack(each) for each in gains]),
            jnp.stack([jnp.stack(each) for each in shifts]),
            jnp.stack([jnp.concatenate(each) for each in in_bias]),
            jnp.stack(out_bias),
            total[12:at_bias].T,
            (terms[0] / terms[1]).reshape(1, 1),
        )

    def kernel(*refs):
        conv_ref, gain_ref, shift_ref, in_ref, out_ref, head_ref, loss_ref, rows_ref = refs[cores:]
        total = paired(
            [
                paired(
                    [
                        paired([wide(refs[c][s * acrosses + a]) for a in range(acrosses)])
                        for s in range(seqs)
                    ]
                )
                for c in range(cores)
            ]
        )
        rows_ref[:, :lanes] = total[: count // 2]
        rows_ref[:, lanes:] = total[count // 2 :]
        conv_bias, gains, shifts, in_bias, out_bias = pick(lambda i: rows_ref[i : i + 1, :])
        for b in range(2):
            conv_ref[b : b + 1, :] = conv_bias[b]
            out_ref[b : b + 1, :] = out_bias[b]
            for i in range(2):
                gain_ref[b, i : i + 1, :] = gains[b][i]
                shift_ref[b, i : i + 1, :] = shifts[b][i]
            for i in range(bias_rows):
                in_ref[b : b + 1, i * width : (i + 1) * width] = in_bias[b][i]
        head_ref[...] = rows_ref[12 : 12 + 8 * (-(-classes // 8)), :].T[:, :classes]
        terms = rows_ref[at_loss : at_loss + 1, :128] + rows_ref[at_loss + 1 : at_loss + 2, :128]
        loss_ref[...] = terms[:, 0:1] / terms[:, 1:2]

    return pl.pallas_call(
        kernel,
        grid=(1,),
        in_specs=[pl.BlockSpec((peers, count, lanes), lambda g: (0, first // count, 0))] * cores,
        out_shape=(
            jax.ShapeDtypeStruct((2, width), jnp.float32),
            jax.ShapeDtypeStruct((2, 2, width), jnp.float32),
            jax.ShapeDtypeStruct((2, 2, width), jnp.float32),
            jax.ShapeDtypeStruct((2, hidden), jnp.float32),
            jax.ShapeDtypeStruct((2, width), jnp.float32),
            jax.ShapeDtypeStruct((width, classes), jnp.float32),
            jax.ShapeDtypeStruct((1, 1), jnp.float32),
        ),
        out_specs=[
            pl.BlockSpec((2, width), lambda g: (0, 0)),
            pl.BlockSpec((2, 2, width), lambda g: (0, 0, 0)),
            pl.BlockSpec((2, 2, width), lambda g: (0, 0, 0)),
            pl.BlockSpec((2, hidden), lambda g: (0, 0)),
            pl.BlockSpec((2, width), lambda g: (0, 0)),
            pl.BlockSpec((width, classes), lambda g: (0, 0)),
            pl.BlockSpec((1, 1), lambda g: (0, 0)),
        ],
        scratch_shapes=[pltpu.VMEM((count // 2, 2 * lanes), jnp.float32)],
        compiler_params=pltpu.CompilerParams(vmem_limit_bytes=4 * MIB),
        cost_estimate=cost(1.5),
        name="finish_small",
    )(*stacks)


def finish_conv(parts, conv_rows, small_rows, after=()):
    blocks, count = len(parts), len(parts[0])
    lanes = parts[0][0].shape[-1]
    flat = [part for block in parts for part in block]
    if conv_rows % ROW_TILE:
        sums = [sum(wide(part[:conv_rows]) for part in block) for block in parts]
        sums.append(paired([wide(part[conv_rows:]) for part in parts[0]]))
        return jnp.concatenate([low(total) for total in sums]), after

    def kernel(*refs):
        shard_ref, token_ref = refs[-2:]
        token_ref[...] = jnp.zeros(TOKEN.shape, TOKEN.dtype)
        shard_ref[blocks * conv_rows :] = low(
            paired([wide(refs[i][conv_rows:]) for i in range(count)])
        )
        for b in range(blocks):
            total = sum(wide(refs[b * count + i][:conv_rows]) for i in range(count))
            shard_ref[b * conv_rows : (b + 1) * conv_rows] = low(total)

    found = pl.pallas_call(
        kernel,
        in_specs=[WHOLE] * (len(flat) + len(after)),
        out_specs=[WHOLE] * 2,
        out_shape=[
            jax.ShapeDtypeStruct((blocks * conv_rows + small_rows, lanes), jnp.bfloat16),
            TOKEN,
        ],
        compiler_params=pltpu.CompilerParams(vmem_limit_bytes=8 * MIB),
        cost_estimate=cost(1.2),
        name="finish_conv",
    )(*flat, *after)
    return found[0], (found[1],)


def finish_ffn(merged, plain, conv_rows, ffn_rows, after=()):
    lanes, width = merged[0].shape[-1], plain[0].shape[-1]

    def cut_back(total):
        size = 2 * ffn_rows
        return jnp.concatenate(
            [total[i * size : (i + 1) * size] for i in range(width // lanes)], 1
        )

    if conv_rows % ROW_TILE or ffn_rows % ROW_TILE:
        sums = [sum(wide(part) for part in plain)]
        sums.append(cut_back(sum(wide(part[conv_rows:]) for part in merged)))
        return jnp.stack([each[:ffn_rows].T for each in sums]), jnp.stack(
            [each[ffn_rows:] for each in sums]
        ), after

    def kernel(*refs):
        in_ref, out_ref, token_ref = refs[-3:]
        token_ref[...] = jnp.zeros(TOKEN.shape, TOKEN.dtype)
        late = sum(wide(refs[i][conv_rows:]) for i in range(len(merged)))
        sums = [sum(wide(refs[len(merged) + i][...]) for i in range(len(plain))), cut_back(late)]
        for b in range(2):
            in_ref[b] = sums[b][:ffn_rows].T
            out_ref[b] = sums[b][ffn_rows:]

    found = pl.pallas_call(
        kernel,
        in_specs=[WHOLE] * (len(merged) + len(plain) + len(after)),
        out_specs=[WHOLE] * 3,
        out_shape=(
            jax.ShapeDtypeStruct((2, width, ffn_rows), jnp.float32),
            jax.ShapeDtypeStruct((2, ffn_rows, width), jnp.float32),
            TOKEN,
        ),
        compiler_params=pltpu.CompilerParams(vmem_limit_bytes=8 * MIB),
        cost_estimate=cost(1),
        name="finish_ffn",
    )(*merged, *plain, *after)
    return found[0], found[1], (found[2],)


def add_slots(parts, slots, after=(), reads=()):
    lanes = parts[0].shape[-1]
    rows = parts[0].size // (slots * lanes)
    parts = [part.reshape(slots, rows, lanes) for part in parts]
    block = rows // 4 if rows % (4 * ROW_TILE) == 0 else rows

    def kernel(*refs):
        out_refs, token_ref = refs[-1 - slots : -1], refs[-1]
        token_ref[...] = jnp.zeros(TOKEN.shape, TOKEN.dtype)
        for slot in range(slots):
            out_refs[slot][...] = low(sum(wide(refs[i][slot]) for i in range(len(parts))))

    found = pl.pallas_call(
        kernel,
        grid=(rows // block,),
        in_specs=[pl.BlockSpec((slots, block, lanes), lambda g: (0, g, 0))] * len(parts)
        + tokens(after)
        + [ANYWHERE] * len(reads),
        out_specs=[pl.BlockSpec((block, lanes), lambda g: (g, 0))] * slots + [TOKEN_SPEC],
        out_shape=[jax.ShapeDtypeStruct((rows, lanes), jnp.bfloat16)] * slots + [TOKEN],
        compiler_params=pltpu.CompilerParams(vmem_limit_bytes=8 * MIB),
        cost_estimate=cost(2),
        name="add_slots",
    )(*parts, *after, *reads)
    return found[:slots], found[slots]


def place_conv_grads(stacks, blocks, taps, slab, places, sizes):
    cores, seqs, acrosses = sizes[:3]
    peers, rows, lanes = stacks[0].shape
    channels = slab * seqs * acrosses
    if slab % ROW_TILE or rows % slab:
        full = jnp.stack([each[:, : blocks * taps * slab] for each in stacks])
        full = full.reshape(cores, seqs, acrosses, blocks, taps, slab, lanes)
        for axis, (place, size) in enumerate(zip(places[:3], sizes[:3])):
            full = relative(full, axis, place, size)
        return wide(
            full.transpose(3, 4, 1, 2, 5, 0, 6).reshape(blocks, taps, channels, cores * lanes)
        )
    stacks = [each.reshape(peers, rows // slab, slab, lanes) for each in stacks]

    def kernel(place_ref, *refs):
        out_ref = refs[-1]
        for c in range(cores):
            lane = pl.multiple_of(lax.rem(place_ref[0] - c + cores, cores) * lanes, lanes)
            for s in range(seqs):
                at_s = lax.rem(place_ref[1] - s + seqs, seqs)
                for a in range(acrosses):
                    at_a = lax.rem(place_ref[2] - a + acrosses, acrosses)
                    row = pl.multiple_of((at_s * acrosses + at_a) * slab, slab)
                    for b in range(blocks):
                        piece = wide(refs[c * blocks + b][s * acrosses + a, 0])
                        out_ref[b, 0, pl.ds(row, slab), pl.ds(lane, lanes)] = piece

    specs = [
        pl.BlockSpec((peers, 1, slab, lanes), lambda k, place, b=b: (0, b * taps + k, 0, 0))
        for b in range(blocks)
    ]
    return pl.pallas_call(
        kernel,
        grid_spec=pltpu.PrefetchScalarGridSpec(
            num_scalar_prefetch=1,
            grid=(taps,),
            in_specs=specs * cores,
            out_specs=pl.BlockSpec(
                (blocks, 1, channels, cores * lanes), lambda k, place: (0, k, 0, 0)
            ),
        ),
        out_shape=jax.ShapeDtypeStruct((blocks, taps, channels, cores * lanes), jnp.float32),
        compiler_params=pltpu.CompilerParams(vmem_limit_bytes=10 * MIB),
        cost_estimate=cost(5),
        name="place_conv_grads",
    )(
        jnp.stack(places[:3]).astype(jnp.int32),
        *[each for stack in stacks for each in [stack] * blocks],
    )


def copy_all(copies):
    for copy in copies:
        copy.start()
    for copy in copies:
        copy.wait()


def place_conv(pieces, places, sizes, after=(), reads=()):
    cores, seqs, acrosses, tap_peers = sizes
    taps, slab, lanes = pieces[0][0].shape[2:]
    inner = slab * seqs * acrosses * tap_peers
    if slab % ROW_TILE:
        full = jnp.stack([jnp.stack(row) for row in pieces])
        for axis, (place, size) in enumerate(zip(places, sizes)):
            full = relative(full, axis, place, size)
        return full.transpose(4, 3, 1, 2, 5, 0, 6).reshape(taps, inner, cores * lanes), after
    flat = [piece for row in pieces for piece in row]

    def kernel(place_ref, *refs):
        out_ref, token_ref, sem_ref = refs[-3:]
        token_ref[...] = jnp.zeros(TOKEN.shape, TOKEN.dtype)
        copies = []
        for c in range(cores):
            lane = lax.rem(place_ref[0] - c + cores, cores) * lanes
            for s in range(seqs):
                at_s = lax.rem(place_ref[1] - s + seqs, seqs)
                for a in range(acrosses):
                    at_a = lax.rem(place_ref[2] - a + acrosses, acrosses)
                    for t in range(tap_peers):
                        at_t = lax.rem(place_ref[3] - t + tap_peers, tap_peers)
                        row = ((at_t * seqs + at_s) * acrosses + at_a) * slab
                        copies.append(
                            pltpu.make_async_copy(
                                refs[c * seqs + s].at[a, t],
                                out_ref.at[
                                    :,
                                    pl.ds(pl.multiple_of(row, slab), slab),
                                    pl.ds(pl.multiple_of(lane, lanes), lanes),
                                ],
                                sem_ref.at[len(copies)],
                            )
                        )
        copy_all(copies)

    found = pl.pallas_call(
        kernel,
        in_specs=[SCALARS] + [ANYWHERE] * (len(flat) + len(reads)) + [WHOLE] * len(after),
        out_specs=[WHOLE] * 2,
        out_shape=[pltpu.HBM((taps, inner, cores * lanes), jnp.bfloat16), TOKEN],
        scratch_shapes=[pltpu.SemaphoreType.DMA((cores * seqs * acrosses * tap_peers,))],
        compiler_params=pltpu.CompilerParams(vmem_limit_bytes=12 * MIB),
        cost_estimate=cost(3),
        name="place_conv",
    )(jnp.stack(places).astype(jnp.int32), *flat, *reads, *after)
    return found[0], (found[1],)


def place_ffn(pieces, sizes, after=(), reads=()):
    cores, seqs, acrosses, tap_peers = sizes
    cuts, ffn_rows, lanes = pieces[0][0].shape[2:]
    cuts //= 2
    width = cuts * lanes
    units = seqs * acrosses * tap_peers * ffn_rows
    if ffn_rows % ROW_TILE:
        full = jnp.stack([jnp.stack(row) for row in pieces])
        full = full.reshape(cores, acrosses, seqs, tap_peers, 2, cuts, ffn_rows, lanes)
        full = full.transpose(4, 0, 1, 2, 3, 6, 5, 7).reshape(2, cores, units, width)
        return [full[0, c] for c in range(cores)], [full[1, c] for c in range(cores)], after
    flat = [piece for row in pieces for piece in row]

    def kernel(*refs):
        out_refs = refs[-2 - 2 * cores : -2]
        token_ref, sem_ref = refs[-2:]
        token_ref[...] = jnp.zeros(TOKEN.shape, TOKEN.dtype)
        copies = []
        for c in range(cores):
            for a in range(acrosses):
                for which in range(2):
                    for cut in range(cuts):
                        copies.append(
                            pltpu.make_async_copy(
                                refs[c * acrosses + a].at[:, :, which * cuts + cut],
                                out_refs[which * cores + c].at[
                                    a, :, :, :, pl.ds(cut * lanes, lanes)
                                ],
                                sem_ref.at[len(copies)],
                            )
                        )
        copy_all(copies)

    shape = pltpu.HBM((acrosses, seqs, tap_peers, ffn_rows, width), jnp.bfloat16)
    found = pl.pallas_call(
        kernel,
        in_specs=[ANYWHERE] * (len(flat) + len(reads)) + [WHOLE] * len(after),
        out_specs=[WHOLE] * (2 * cores + 1),
        out_shape=[shape] * (2 * cores) + [TOKEN],
        scratch_shapes=[pltpu.SemaphoreType.DMA((2 * cores * acrosses * cuts,))],
        compiler_params=pltpu.CompilerParams(vmem_limit_bytes=12 * MIB),
        cost_estimate=cost(2),
        name="place_ffn",
    )(*flat, *reads, *after)
    token = found[-1]
    found = [each.reshape(units, width) for each in found[:-1]]
    return found[:cores], found[cores:], (token,)


class Ring:
    def __init__(self, axis, size, index, pairs):
        self.axis, self.size, self.index, self.pairs = axis, size, index, pairs

    def shifted(self, value, by):
        return lax.ppermute(value, self.axis, self.pairs(lambda i: (i + by) % self.size))

    def swapped(self, value, bit):
        return lax.ppermute(value, self.axis, self.pairs(lambda i: i ^ bit))

    def gather(self, value):
        return [value] + [self.shifted(value, by) for by in range(1, self.size)]

    def swap(self, values):
        return [values[0]] + [self.shifted(values[by], -by) for by in range(1, self.size)]


def relative(value, axis, place, size):
    if size == 1:
        return value
    return jnp.stack(
        [
            lax.dynamic_index_in_dim(value, (place - slot) % size, axis, False)
            for slot in range(size)
        ],
        axis,
    )


def rings():
    peers = lax.axis_size("dp")
    cores = CORES if peers % CORES == 0 else 1
    columns = peers // cores
    place = lax.axis_index("dp")

    def plain(axis):
        size = lax.axis_size(axis)
        return Ring(
            axis, size, lax.axis_index(axis), lambda move: [(i, move(i)) for i in range(size)]
        )

    across = Ring(
        "dp",
        columns,
        place // cores,
        lambda move: [(i, move(i // cores) * cores + i % cores) for i in range(peers)],
    )
    core = Ring(
        "dp",
        cores,
        place % cores,
        lambda move: [(i, i // cores * cores + move(i % cores)) for i in range(peers)],
    )
    return core, across, plain("seq"), plain("tap")


class Reduce:
    def __init__(self, terms, order):
        self.order = order
        self.parts = [terms[0]] + [order[0].shifted(terms[s], -s) for s in range(1, order[0].size)]

    def step(self, level, after, reads=()):
        ring = self.order[level]
        found, token = add_slots(self.parts, ring.size, after, reads)
        self.parts = [found[0]] + [ring.shifted(found[s], -s) for s in range(1, ring.size)]
        return (token,)


def shared_copies(value, across, seq):
    peers, spans = lax.axis_size("dp"), lax.axis_size("seq")
    cores = peers // across.size

    def target(place, by_a, by_s):
        dp, at = place // spans, place % spans
        moved = (dp // cores + by_a) % across.size * cores + dp % cores
        return moved * spans + (at + by_s) % spans

    return [
        [
            value
            if by_a == by_s == 0
            else lax.ppermute(
                value,
                ("dp", "seq"),
                [(place, target(place, by_a, by_s)) for place in range(peers * spans)],
            )
            for by_a in range(across.size)
        ]
        for by_s in range(seq.size)
    ]


def passed_along(value, axis, by):
    peers = lax.axis_size(axis)
    pairs = [(i, i + by) for i in range(peers) if 0 <= i + by < peers]
    return lax.ppermute(value, axis, pairs)


def rims(source, reach_rows, seq, rim=None):
    span_rows = source.shape[0]
    if seq.size == 2 and reach_rows <= span_rows:
        if rim is None:
            first = (1 - seq.index) * (span_rows - reach_rows)
            rim = lax.dynamic_slice_in_dim(source, first, reach_rows, 0)
        return seq.shifted(rim, 1)
    left_parts = []
    right_parts = []
    distances = -(-reach_rows // span_rows)
    for distance in range(1, distances + 1):
        rim_count = min(span_rows, reach_rows - (distance - 1) * span_rows)
        left_parts.insert(0, passed_along(source[span_rows - rim_count :], "seq", distance))
        right_parts.append(passed_along(source[:rim_count], "seq", -distance))
    return left_parts, right_parts


def extend(source, found, seq, after=()):
    if isinstance(found, tuple):
        return join_rows(found[0] + [source] + found[1], after)
    reach, span = found.shape[0], source.shape[0]

    def kernel(place_ref, found_ref, source_ref, *refs):
        out_ref, token_ref = refs[-2:]
        token_ref[...] = jnp.zeros(TOKEN.shape, TOKEN.dtype)
        out_ref[reach : reach + span] = source_ref[...]
        zeros = jnp.zeros(found.shape, found.dtype)

        @pl.when(place_ref[0] == 0)
        def _():
            out_ref[:reach] = zeros
            out_ref[reach + span :] = found_ref[...]

        @pl.when(place_ref[0] != 0)
        def _():
            out_ref[:reach] = found_ref[...]
            out_ref[reach + span :] = zeros

    shape = jax.ShapeDtypeStruct((span + 2 * reach, source.shape[1]), source.dtype)
    extended, token = pl.pallas_call(
        kernel,
        in_specs=[SCALARS] + [WHOLE] * (2 + len(after)),
        out_specs=[WHOLE] * 2,
        out_shape=[shape, TOKEN],
        compiler_params=pltpu.CompilerParams(vmem_limit_bytes=10 * MIB),
        cost_estimate=cost(1.5),
        name="extend",
    )(seq.index.astype(jnp.int32)[None], found, source, *after)
    return extended, (token,)


def to_rows(values):
    windows, positions = values.shape[:2]
    cut = values.reshape((windows, positions // FIRST_DILATION, FIRST_DILATION) + values.shape[2:])
    return jnp.swapaxes(cut, 0, 1).reshape((windows * positions,) + values.shape[2:])


def from_rows(values, windows):
    cut = values.reshape((-1, windows, FIRST_DILATION) + values.shape[1:])
    return jnp.swapaxes(cut, 0, 1).reshape((windows, -1) + values.shape[1:])


def on_device(
    inputs,
    targets,
    masked,
    conv_weight,
    conv_bias,
    gains,
    shifts,
    in_weight,
    in_bias,
    out_weight,
    out_bias,
    head_weight,
):
    core, across, seq, tap = rings()
    taps = conv_weight.shape[1]
    channels = conv_weight.shape[2]
    width = conv_weight.shape[3]
    slab = channels // (seq.size * across.size)
    lanes = width // core.size
    hidden_width = in_bias.shape[1]
    ffn_rows = in_weight.shape[2]
    windows = inputs.shape[0]
    rows = windows * inputs.shape[1]
    steps = (FIRST_DILATION * windows, SECOND_DILATION * windows)
    units = hidden_width // core.size
    places = (core.index, seq.index, across.index, tap.index)
    sizes = (core.size, seq.size, across.size, tap.size)

    in_bias_placed = []
    for b in range(2):
        bias = in_bias[b].reshape(across.size, core.size, seq.size, tap.size, ffn_rows)
        for axis, ring in enumerate((across, core, seq, tap)):
            bias = relative(bias, axis, ring.index, ring.size)
        in_bias_placed.append(bias.transpose(1, 0, 2, 3, 4).reshape(core.size, units))

    def cut_ffn(piece):
        return piece.reshape(ffn_rows, core.size, lanes).swapaxes(0, 1).reshape(-1, lanes)

    def bundle(b):
        conv_piece = lax.dynamic_slice(
            conv_weight[b],
            (0, (seq.index * across.size + across.index) * slab, core.index * lanes),
            (taps, slab, lanes),
        )
        pieces = [
            conv_piece.reshape(taps * slab, lanes),
            cut_ffn(in_weight[b].T),
            cut_ffn(out_weight[b]),
        ]
        return jnp.concatenate(pieces)

    cuts = (
        (0, taps * slab, (taps, slab, lanes)),
        (taps * slab, taps * slab + 2 * core.size * ffn_rows, (2 * core.size, ffn_rows, lanes)),
    )

    def straight(arrays):
        return (arrays, ((0, None, arrays[0].shape),))

    conv_input = to_rows(inputs)
    stream = conv_input
    codes = to_rows(targets + masked * head_weight.shape[1])
    codes = jnp.broadcast_to(codes[:, None], (rows, 128))

    reaches = [taps // 2 * step for step in steps]
    rim_reaches = [reach if seq.size == 2 and reach <= rows else 0 for reach in reaches]

    tap_parts = tap.gather(bundle(0))
    behind = bundle(1)
    found = rims(conv_input, reaches[0], seq)
    (conv_part, ffn_part), last = restack(
        [(tap_parts, cuts)], reads=[behind] + [found if rim_reaches[0] else conv_input]
    )
    (behind,), last = hold([behind], last)
    split = (tap.size + 1) // 2
    late_parts = tap.gather(behind)
    extended, last = extend(conv_input, found, seq, last)
    extended_parts = [extended] + [core.shifted(extended, -c) for c in range(1, core.size)]
    conv_parts, ffn_parts = across.gather(conv_part), seq.gather(ffn_part)
    (conv_part, ffn_part), last = restack(
        [straight(conv_parts), straight(ffn_parts)],
        reads=[late_parts[by] for by in range(1, tap.size) if by != split],
        after=last,
    )
    conv_parts, ffn_parts = seq.gather(conv_part), across.gather(ffn_part)
    conv_slots = [core.gather(conv_part)]
    ffn_slots = [core.gather(ffn_part)]
    held, last = hold(
        conv_parts[1:] + ffn_parts[1:],
        last,
        conv_slots[0][1:] + ffn_slots[0][1:] + late_parts[1:],
    )
    conv_slots += [core.gather(each) for each in held[: seq.size - 1]]
    ffn_slots += [core.gather(each) for each in held[seq.size - 1 :]]
    (late_conv, late_ffn), last = restack([(late_parts, cuts)], after=last, fixed=True)
    late_conv_parts, late_ffn_parts = across.gather(late_conv), seq.gather(late_ffn)

    def turned(slots):
        return [[each[c] for each in slots] for c in range(core.size)]

    conv_full, in_full, out_full = [None, None], [None, None], [None, None]
    conv_full[0], last = place_conv(
        turned(conv_slots), places, sizes, last, [part for each in ffn_slots for part in each[1:]]
    )
    saved = []
    reads = []
    rim = None
    for b in range(2):
        if b == 1:
            found = rims(conv_input, reaches[1], seq, rim)
            held, last = hold(late_conv_parts[1:] + late_ffn_parts[1:], last)
            late_conv_slots += [core.gather(each) for each in held[: seq.size - 1]]
            late_ffn_slots += [core.gather(each) for each in held[seq.size - 1 :]]
            conv_full[1], last = place_conv(turned(late_conv_slots), places, sizes, last)
            in_full[1], out_full[1], last = place_ffn(turned(late_ffn_slots), sizes, last)
            extended, last = extend(conv_input, found, seq, last)
            extended_parts = [extended] + [core.shifted(extended, -c) for c in range(1, core.size)]
        (normed_conv, conv_slope, stream, lowered), last = conv_forward(
            extended,
            conv_full[b],
            stream,
            conv_bias[b],
            gains[b, 0],
            shifts[b, 0],
            steps[b],
            last,
            reads,
        )
        reads = extended_parts[1:]
        if b == 0:
            (late_conv, late_ffn), last = restack(
                [straight(late_conv_parts), straight(late_ffn_parts)], after=last
            )
            late_conv_parts, late_ffn_parts = seq.gather(late_conv), across.gather(late_ffn)
            late_conv_slots = [core.gather(late_conv)]
            late_ffn_slots = [core.gather(late_ffn)]
            in_full[0], out_full[0], last = place_ffn(turned(ffn_slots), sizes, last)
            reads = reads + late_conv_slots[0][1:] + late_ffn_slots[0][1:]
        active, hidden_slopes, (normed_ffn, scale_ffn, stream, conv_input), packets, rim, last = (
            ffn_forward(
                lowered,
                stream,
                in_full[b],
                out_full[b],
                [in_bias_placed[b][c] for c in range(core.size)],
                out_bias[b],
                gains[b, 1],
                shifts[b, 1],
                seq.index,
                rim_reaches[1] if b == 0 else 0,
                b == 1,
                last,
                reads,
            )
        )
        packets = [core.shifted(packet, -1 - c) for c, packet in enumerate(packets)]
        reads = packets
        saved.append(
            (
                extended_parts,
                conv_slope,
                normed_conv,
                (active, lowered, packets),
                hidden_slopes,
                normed_ffn,
                scale_ffn,
            )
        )

    (stream_grad, head_grad, loss_rows), last = head_and_loss(stream, head_weight, codes, last)

    ffn_rows_of_sums = [None, None]
    conv_rows_of_sums = [None, None]
    in_bias_grads = [None, None]
    ffn_sums = [None, None]
    conv_sums = [None, None]
    merged = [None, None]

    def groups(halves):
        half = (tap.size + 1) // 2
        return [(each.parts, slots) for each, slots in zip(halves, (half, tap.size - half))]

    for b in (1, 0):
        (
            extended_parts,
            conv_slope,
            normed_conv,
            active_pair,
            hidden_slopes,
            normed_ffn,
            scale_ffn,
        ) = saved[b]
        output_grad, hidden_grad, biases, packets, ffn_rows_of_sums[b], last = ffn_back_hidden(
            stream_grad, normed_ffn, scale_ffn, gains[b, 1], out_full[b], hidden_slopes, last
        )
        if b == 1:
            arrived_packets = [core.shifted(packet, -1 - c) for c, packet in enumerate(packets)]
        if b == 0:
            for each in ffn_sums[1]:
                last = each.step(1, last)
            for each in conv_sums[1]:
                last = each.step(1, last)
        stream_grad, conv_grad, conv_cuts, relayed, rim, conv_rows_of_sums[b], last = ffn_back_stream(
            stream_grad,
            hidden_grad,
            packets,
            in_full[b],
            normed_conv,
            conv_slope,
            gains[b, 0],
            places,
            rim_reaches[b],
            last,
            reads,
            relay=b == 0,
        )
        reads = []
        if b == 0:
            merged[1], last = merge_slots(
                groups(conv_sums[1]), groups(ffn_sums[1]), last
            )
            sent = [rim] if rim is not None else []
            held, last = hold(list(conv_cuts) + list(relayed) + sent, last)
            conv_cuts, relayed = held[: core.size - 1], held[core.size - 1 : 2 * core.size - 2]
            rim = held[-1] if sent else None
            merged[1] = tap.swap(merged[1])
            arrived_packets = [core.shifted(packet, -1 - c) for c, packet in enumerate(relayed)]
        arrived = [core.shifted(conv_cuts[c - 1], -c) for c in range(1, core.size)]
        in_bias_grads[b] = list(biases)
        found_rims = rims(conv_grad, reaches[b], seq, rim)

        def ffn_grads(last):
            active, lowered, packets = active_pair
            if core.size == 1:
                packets = []
            first, second, token = ffn_weight_grad(
                (
                    (hidden_grad, lowered, [(g, p) for g, p in zip(arrived_packets, packets)]),
                    (active, output_grad, [(p, g) for g, p in zip(arrived_packets, packets)]),
                ),
                sizes,
                ffn_rows,
                last,
            )
            found = [Reduce(first, (across, seq))]
            if second:
                found.append(Reduce(second, (seq, across)))
            return found, (token,)

        def conv_grads(last, reads=()):
            first, second, token = conv_weight_grad(
                extended_parts, conv_grad, arrived, places, sizes, taps, steps[b], last, reads
            )
            found = [Reduce(first, (seq, across))]
            if second:
                found.append(Reduce(second, (across, seq)))
            return found, (token,)

        if b == 1:
            ffn_sums[1], last = ffn_grads(last)
            extended_grad, last = extend(conv_grad, found_rims, seq, last)
            conv_sums[1], last = conv_grads(last)
        else:
            conv_sums[0], last = conv_grads(last, arrived_packets)
            extended_grad, last = extend(conv_grad, found_rims, seq, last)
            ffn_sums[0], last = ffn_grads(last)
            for each in conv_sums[0]:
                last = each.step(1, last, merged[1][1:])
        stream_grad, last = conv_data_grad(
            extended_grad,
            conv_full[b],
            stream_grad,
            steps[b],
            jnp.float32 if b == 1 else jnp.bfloat16,
            last,
        )

    grad_inputs = from_rows(stream_grad, windows)

    row_groups = [(each, 3) for each in conv_rows_of_sums + ffn_rows_of_sums]
    row_groups.append((head_grad, head_weight.shape[1]))
    (conv_input,), last = hold([conv_input], last)
    final_state = from_rows(conv_input, windows)
    packed, last = pack_small(row_groups, in_bias_grads, loss_rows, places, sizes, ffn_rows, last)

    conv_rows = taps * slab
    merged[0], last = append_slots(groups(conv_sums[0]), [packed], last, [final_state])
    merged[0] = tap.swap(merged[0])
    for each in ffn_sums[0]:
        last = each.step(1, last)
    shards, last = finish_conv([merged[0], merged[1]], conv_rows, packed.shape[0], last)
    ffn_late, last = append_slots(groups(ffn_sums[0]), [], last, [grad_inputs])
    ffn_late = tap.swap(ffn_late)
    copies = [each for row in shared_copies(shards, across, seq) for each in row]
    grad_in, grad_out, last = finish_ffn(merged[1], ffn_late, conv_rows, ffn_rows, last)
    (stack,), last = restack([straight(copies)], after=last)
    stacks = core.gather(stack)
    (
        grad_conv_bias,
        grad_gains,
        grad_shifts,
        grad_in_bias,
        grad_out_bias,
        grad_head_weight,
        loss,
    ) = finish_small(
        stacks, 2 * conv_rows, width, head_weight.shape[1], hidden_width, places, sizes
    )
    grad_conv = place_conv_grads(stacks, 2, taps, slab, places, sizes)
    return (
        final_state,
        grad_inputs,
        grad_conv,
        grad_conv_bias,
        grad_gains,
        grad_shifts,
        grad_in,
        grad_in_bias,
        grad_out,
        grad_out_bias,
        grad_head_weight,
        loss.reshape(()),
    )


def solution(mesh):
    placed = (
        P(("dp", "tap"), "seq", None),
        P(("dp", "tap"), "seq"),
        P(("dp", "tap"), "seq"),
        P(None, None, "tap", None),
        P(),
        P(),
        P(),
        P(None, None, ("dp", "seq", "tap")),
        P(),
        P(None, ("dp", "seq", "tap"), None),
        P(),
        P(),
    )
    return jax.shard_map(
        on_device,
        mesh=mesh,
        in_specs=placed,
        out_specs=(
            P(("dp", "tap"), "seq", None),
            P(("dp", "tap"), "seq", None),
            P(None, None, "tap", None),
            P(),
            P(),
            P(),
            P(None, None, ("dp", "seq", "tap")),
            P(),
            P(None, ("dp", "seq", "tap"), None),
            P(),
            P(),
            P(),
        ),
        check_vma=False,
    )
```

```python
import functools

import jax
import jax.numpy as jnp
import numpy as np
from jax import lax
from jax.experimental import pallas as pl
from jax.experimental.pallas import tpu as pltpu
from jax.sharding import PartitionSpec as P

FIRST_DILATION = 4
SECOND_DILATION = 32
EPSILON = 1e-05
HIGHEST_PRECISION = lax.Precision.HIGHEST
CORES = 2
ROW_TILE = 16
MIB = 1024 * 1024
VMEM_BYTES = 20 * MIB
ANYWHERE = pl.BlockSpec(memory_space=pl.ANY)
SCALARS = pl.BlockSpec(memory_space=pltpu.SMEM)


TOKEN = jax.ShapeDtypeStruct((8, 128), jnp.float32)


def cost(microseconds):
    size = int(microseconds * 3.5e6)
    return pl.CostEstimate(flops=int(microseconds * 1.1e9), bytes_accessed=size, transcendentals=0)


WHOLE = pl.BlockSpec(memory_space=pltpu.VMEM)
TOKEN_SPEC = pl.BlockSpec(TOKEN.shape, lambda *_: (0, 0))


def tokens(after):
    return [TOKEN_SPEC] * len(after)


def in_hbm(array):
    return pltpu.with_memory_space_constraint(array, pltpu.HBM)


def low(values):
    return values.astype(jnp.bfloat16)


def wide(values):
    return values.astype(jnp.float32)


def gelu_parts(values):
    phi = 0.5 * (1.0 + lax.erf(values * 0.7071067811865476))
    return (
        values * phi,
        phi + values * jnp.exp(-0.5 * values * values) * 0.3989422804014327,
    )


def normalize(values):
    center = values - jnp.mean(values, -1, keepdims=True)
    scale = lax.rsqrt(jnp.mean(center * center, -1, keepdims=True) + EPSILON)
    return (center * scale, scale)


def norm_back(upstream, normed, scale):
    return scale * (
        upstream
        - jnp.mean(upstream, -1, keepdims=True)
        - normed * jnp.mean(upstream * normed, -1, keepdims=True)
    )


def tap_groups(taps):
    return 3 if taps % 3 == 0 else 1


def row_chunks(rows, most):
    size = min(rows, most)
    return [(first, size) for first in range(0, rows, size)]


def conv_forward(extended, weight, stream, bias, gain, shift, step, after=(), reads=()):
    taps, inner, width = weight.shape
    rows = stream.shape[0]
    group = tap_groups(taps)
    steps = taps // group

    def kernel(extended_ref, weight_ref, stream_ref, bias_ref, gain_ref, shift_ref, *refs):
        normed_ref, slope_ref, next_ref, lowered_ref, token_ref, total_ref = refs[-6:]
        token_ref[...] = jnp.zeros(TOKEN.shape, TOKEN.dtype)
        first = pl.program_id(0) * group
        total = None
        for j in range(group):
            start = pl.multiple_of((first + j) * step, ROW_TILE)
            term = jnp.dot(
                extended_ref[pl.ds(start, rows), :],
                weight_ref[j],
                preferred_element_type=jnp.float32,
            )
            total = term if total is None else total + term

        @pl.when(pl.program_id(0) == 0)
        def _():
            total_ref[...] = total

        @pl.when(pl.program_id(0) > 0)
        def _():
            total_ref[...] += total

        @pl.when(pl.program_id(0) == steps - 1)
        def _():
            for at, size in row_chunks(rows, 128):
                some = pl.ds(at, size)
                value, slope = gelu_parts(total_ref[some, :] + bias_ref[...])
                normed, scale = normalize(value)
                mid = wide(stream_ref[some, :]) + normed * gain_ref[...] + shift_ref[...]
                normed_ref[some, :] = low(normed)
                slope_ref[some, :] = low(scale * slope)
                next_ref[some, :] = mid
                lowered_ref[some, :] = low(mid)

    whole = pl.BlockSpec((rows, width), lambda g: (0, 0))
    row = pl.BlockSpec((1, width), lambda g: (0, 0))
    found = pl.pallas_call(
        kernel,
        grid=(steps,),
        in_specs=[
            pl.BlockSpec(extended.shape, lambda g: (0, 0)),
            pl.BlockSpec((group, inner, width), lambda g: (g, 0, 0)),
            whole,
            row,
            row,
            row,
        ]
        + tokens(after)
        + [ANYWHERE] * len(reads),
        out_specs=[whole] * 4 + [TOKEN_SPEC],
        out_shape=[
            pltpu.HBM((rows, width), jnp.bfloat16),
            pltpu.HBM((rows, width), jnp.bfloat16),
            pltpu.HBM((rows, width), jnp.float32),
            jax.ShapeDtypeStruct((rows, width), jnp.bfloat16),
            TOKEN,
        ],
        scratch_shapes=[pltpu.VMEM((rows, width), jnp.float32)],
        compiler_params=pltpu.CompilerParams(vmem_limit_bytes=VMEM_BYTES),
        cost_estimate=cost(9),
        name="conv_forward",
    )(extended, in_hbm(weight), in_hbm(stream) if stream.dtype == jnp.float32 else stream, bias[None], gain[None], shift[None], *after, *reads)
    return found[:4], (found[4],)


def ffn_forward(
    lowered,
    stream,
    ins,
    outs,
    in_biases,
    out_bias,
    gain,
    shift,
    seq_index,
    reach,
    last_block,
    after=(),
    reads=(),
):
    rows, width = lowered.shape
    cores = len(ins)
    units = ins[0].shape[0]
    block = min(units, 256)
    steps = units // block

    rims_out = 1 if reach else 0

    def kernel(place_ref, lowered_ref, stream_ref, out_bias_ref, gain_ref, shift_ref, *refs):
        in_refs, out_refs, bias_refs = (refs[i * cores : (i + 1) * cores] for i in range(3))
        found_refs = refs[-6 - 2 * cores - rims_out :]
        active_ref, slope_refs = found_refs[0], found_refs[1 : 1 + cores]
        normed_ref, scale_ref, next_ref, rounded_ref = found_refs[1 + cores : 5 + cores]
        packet_refs = found_refs[5 + cores : 4 + 2 * cores]
        token_ref, total_ref = found_refs[-2:]
        token_ref[...] = jnp.zeros(TOKEN.shape, TOKEN.dtype)
        lane = pl.multiple_of(width + pl.program_id(0) * block, block)

        @pl.when(pl.program_id(0) == 0)
        def _():
            total_ref[...] = jnp.zeros(total_ref.shape, jnp.float32)
            for packet_ref in packet_refs:
                packet_ref[:, :width] = lowered_ref[...]

        for at, size in row_chunks(rows, 512):
            some = pl.ds(at, size)
            term = None
            for c in range(cores):
                hidden = lax.dot_general(
                    lowered_ref[some, :],
                    in_refs[c][...],
                    (((1,), (1,)), ((), ())),
                    preferred_element_type=jnp.float32,
                )
                active, slope = gelu_parts(hidden + bias_refs[c][...])
                active = low(active)
                if c == 0:
                    active_ref[some, :] = active
                else:
                    packet_refs[c - 1][some, pl.ds(lane, block)] = active
                slope_refs[c][some, :] = low(slope)
                found = jnp.dot(active, out_refs[c][...], preferred_element_type=jnp.float32)
                term = found if term is None else term + found
            total_ref[some, :] += term

        @pl.when(pl.program_id(0) == steps - 1)
        def _():
            for at, size in row_chunks(rows, 128):
                some = pl.ds(at, size)
                normed, scale = normalize(total_ref[some, :] + out_bias_ref[...])
                after_ffn = stream_ref[some, :] + normed * gain_ref[...] + shift_ref[...]
                normed_ref[some, :] = low(normed)
                scale_ref[some, :] = jnp.broadcast_to(scale, (size, 128))
                next_ref[some, :] = after_ffn
                rounded_ref[some, :] = low(after_ffn)
            if reach:
                first = pl.multiple_of((1 - place_ref[0]) * (rows - reach), ROW_TILE)
                found_refs[-3][...] = rounded_ref[pl.ds(first, reach), :]

    whole = pl.BlockSpec((rows, width), lambda g: (0, 0))
    row = pl.BlockSpec((1, width), lambda g: (0, 0))
    piece = pl.BlockSpec((block, width), lambda g: (g, 0))
    columns = pl.BlockSpec((rows, block), lambda g: (0, g))
    hidden_shape = pltpu.HBM((rows, units), jnp.bfloat16)
    found = pl.pallas_call(
        kernel,
        grid=(steps,),
        in_specs=[SCALARS, whole, whole, row, row, row]
        + [piece] * (2 * cores)
        + [pl.BlockSpec((1, block), lambda g: (0, g))] * cores
        + tokens(after)
        + [ANYWHERE] * len(reads),
        out_specs=[columns] * (1 + cores)
        + [whole, pl.BlockSpec((rows, 128), lambda g: (0, 0)), whole, whole]
        + [pl.BlockSpec((rows, width + units), lambda g: (0, 0))] * (cores - 1)
        + [pl.BlockSpec((reach, width), lambda g: (0, 0))] * rims_out
        + [TOKEN_SPEC],
        out_shape=[hidden_shape] * (1 + cores)
        + [
            pltpu.HBM((rows, width), jnp.bfloat16),
            pltpu.HBM((rows, 128), jnp.float32),
            (jax.ShapeDtypeStruct if last_block else pltpu.HBM)((rows, width), jnp.float32),
            jax.ShapeDtypeStruct((rows, width), jnp.bfloat16),
        ]
        + [jax.ShapeDtypeStruct((rows, width + units), jnp.bfloat16)] * (cores - 1)
        + [jax.ShapeDtypeStruct((reach, width), jnp.bfloat16)] * rims_out
        + [TOKEN],
        scratch_shapes=[pltpu.VMEM((rows, width), jnp.float32)],
        compiler_params=pltpu.CompilerParams(vmem_limit_bytes=VMEM_BYTES),
        cost_estimate=cost(11),
        name="ffn_forward",
    )(
        seq_index.astype(jnp.int32)[None],
        lowered,
        in_hbm(stream),
        out_bias[None],
        gain[None],
        shift[None],
        *[in_hbm(each) for each in ins],
        *[in_hbm(each) for each in outs],
        *[each[None] for each in in_biases],
        *after,
        *reads,
    )
    return (
        found[0],
        found[1 : 1 + cores],
        found[1 + cores : 5 + cores],
        found[5 + cores : 4 + 2 * cores],
        found[4 + 2 * cores] if reach else None,
        (found[-1],),
    )


def head_and_loss(stream, head_weight, codes, after=()):
    rows, width = stream.shape
    classes = head_weight.shape[1]
    padded = jnp.pad(head_weight, ((0, 0), (0, 128 - classes)))
    cuts = row_chunks(rows, 256)

    def kernel(stream_ref, head_ref, code_ref, *refs):
        grad_ref, head_grad_ref, sums_ref, token_ref = refs[-4:]
        token_ref[...] = jnp.zeros(TOKEN.shape, TOKEN.dtype)
        head_grad = jnp.zeros((128, width), jnp.float32)
        objective = jnp.zeros((1, 1), jnp.float32)
        scored = jnp.zeros((1, 1), jnp.float32)
        for at, size in cuts:
            some = pl.ds(at, size)
            value = stream_ref[some, :]
            code = code_ref[some, :]
            mask = jnp.where(code[:, :1] >= classes, 1.0, 0.0)
            logits = jnp.dot(
                value, head_ref[...], precision=HIGHEST_PRECISION, preferred_element_type=jnp.float32
            )
            lane = lax.broadcasted_iota(jnp.int32, logits.shape, 1)
            valid = lane < classes
            peak = jnp.max(jnp.where(valid, logits, -jnp.inf), -1, keepdims=True)
            exponent = jnp.where(valid, jnp.exp(jnp.where(valid, logits - peak, 0.0)), 0.0)
            denominator = jnp.sum(exponent, -1, keepdims=True)
            chosen = lane == jnp.where(code >= classes, code - classes, code)
            picked = jnp.sum(jnp.where(chosen, logits, 0.0), -1, keepdims=True)
            terms = mask * (peak + jnp.log(denominator) - picked)
            objective = objective + jnp.sum(terms, 0, keepdims=True)
            scored = scored + jnp.sum(mask, 0, keepdims=True)
            logit_grad = mask * (exponent / denominator - jnp.where(chosen, 1.0, 0.0))
            grad_ref[some, :] = lax.dot_general(
                logit_grad,
                head_ref[...],
                (((1,), (1,)), ((), ())),
                precision=HIGHEST_PRECISION,
                preferred_element_type=jnp.float32,
            )
            head_grad = head_grad + lax.dot_general(
                logit_grad,
                value,
                (((0,), (0,)), ((), ())),
                precision=HIGHEST_PRECISION,
                preferred_element_type=jnp.float32,
            )
        head_grad_ref[...] = head_grad[: head_grad_ref.shape[0]]
        at_row = lax.broadcasted_iota(jnp.int32, sums_ref.shape, 0)
        sums_ref[...] = jnp.where(at_row == 0, objective, scored)

    found = pl.pallas_call(
        kernel,
        out_shape=[
            jax.ShapeDtypeStruct((rows, width), jnp.float32),
            jax.ShapeDtypeStruct((-(-classes // 8) * 8, width), jnp.float32),
            jax.ShapeDtypeStruct((8, 128), jnp.float32),
            TOKEN,
        ],
        compiler_params=pltpu.CompilerParams(vmem_limit_bytes=VMEM_BYTES),
        cost_estimate=cost(6),
        name="head_and_loss",
    )(stream, padded, codes, *after)
    return found[:3], (found[3],)


def ffn_back_hidden(upstream, normed, scale, gain, outs, slopes, after=()):
    rows, width = upstream.shape
    cores = len(outs)
    units = outs[0].shape[0]
    block = min(units, 256)

    def kernel(upstream_ref, normed_ref, scale_ref, gain_ref, *refs):
        out_refs, slope_refs = refs[:cores], refs[cores : 2 * cores]
        found_refs = refs[-3 - 2 * cores :]
        output_grad_ref, hidden_ref = found_refs[:2]
        bias_refs, packet_refs = found_refs[2 : 2 + cores], found_refs[2 + cores : -2]
        sums_ref, token_ref = found_refs[-2:]
        token_ref[...] = jnp.zeros(TOKEN.shape, TOKEN.dtype)
        lane = pl.multiple_of(width + pl.program_id(0) * block, block)

        @pl.when(pl.program_id(0) == 0)
        def _():
            totals = [jnp.zeros((1, width), jnp.float32)] * 3
            for at, size in row_chunks(rows, 128):
                some = pl.ds(at, size)
                grad, value = upstream_ref[some, :], wide(normed_ref[some, :])
                output_grad = low(norm_back(grad * gain_ref[...], value, scale_ref[some, :1]))
                output_grad_ref[some, :] = output_grad
                for packet_ref in packet_refs:
                    packet_ref[some, :width] = output_grad
                for i, each in enumerate((grad * value, grad, wide(output_grad))):
                    totals[i] = totals[i] + jnp.sum(each, 0, keepdims=True)
            sums_ref[...] = jnp.zeros(sums_ref.shape, jnp.float32)
            for i in range(3):
                sums_ref[i : i + 1, :] = totals[i]

        for c in range(cores):
            total = jnp.zeros((1, block), jnp.float32)
            for at, size in row_chunks(rows, 512):
                some = pl.ds(at, size)
                active_grad = lax.dot_general(
                    output_grad_ref[some, :],
                    out_refs[c][...],
                    (((1,), (1,)), ((), ())),
                    preferred_element_type=jnp.float32,
                )
                hidden_grad = low(active_grad * wide(slope_refs[c][some, :]))
                if c == 0:
                    hidden_ref[some, :] = hidden_grad
                else:
                    packet_refs[c - 1][some, pl.ds(lane, block)] = hidden_grad
                total = total + jnp.sum(wide(hidden_grad), 0, keepdims=True)
            bias_refs[c][...] = total

    whole = pl.BlockSpec((rows, width), lambda g: (0, 0))
    columns = pl.BlockSpec((rows, block), lambda g: (0, g))
    found = pl.pallas_call(
        kernel,
        grid=(units // block,),
        in_specs=[
            whole,
            whole,
            pl.BlockSpec((rows, 128), lambda g: (0, 0)),
            pl.BlockSpec((1, width), lambda g: (0, 0)),
        ]
        + [pl.BlockSpec((block, width), lambda g: (g, 0))] * cores
        + [columns] * cores
        + tokens(after),
        out_specs=[whole, columns]
        + [pl.BlockSpec((1, block), lambda g: (0, g))] * cores
        + [pl.BlockSpec((rows, width + units), lambda g: (0, 0))] * (cores - 1)
        + [pl.BlockSpec((8, width), lambda g: (0, 0)), TOKEN_SPEC],
        out_shape=[
            jax.ShapeDtypeStruct((rows, width), jnp.bfloat16),
            pltpu.HBM((rows, units), jnp.bfloat16),
        ]
        + [jax.ShapeDtypeStruct((1, units), jnp.float32)] * cores
        + [jax.ShapeDtypeStruct((rows, width + units), jnp.bfloat16)] * (cores - 1)
        + [jax.ShapeDtypeStruct((8, width), jnp.float32), TOKEN],
        compiler_params=pltpu.CompilerParams(vmem_limit_bytes=VMEM_BYTES),
        cost_estimate=cost(6),
        name="ffn_back_hidden",
    )(
        upstream,
        in_hbm(normed),
        in_hbm(scale),
        gain[None],
        *[in_hbm(each) for each in outs],
        *[in_hbm(each) for each in slopes],
        *after,
    )
    return (
        found[0],
        found[1],
        found[2 : 2 + cores],
        found[2 + cores : -2],
        found[-2],
        (found[-1],),
    )


def ffn_back_stream(
    upstream, hidden, packets, ins, normed, slope, gain, places, reach, after=(), reads=(), relay=False
):
    rows, width = upstream.shape
    cores = len(ins)
    units = ins[0].shape[0]
    block = min(units, 256)
    steps = units // block
    lanes = width // cores
    relays = cores - 1 if relay else 0
    rims_out = 1 if reach else 0

    def kernel(core_ref, upstream_ref, normed_ref, slope_ref, gain_ref, *refs):
        hidden_refs, in_refs = refs[:cores], refs[cores : 2 * cores]
        found_refs = refs[-4 - cores - relays - rims_out :]
        mid_ref, conv_grad_ref = found_refs[:2]
        cut_refs = found_refs[2 : 1 + cores]
        sums_ref, token_ref, total_ref = found_refs[-3:]
        token_ref[...] = jnp.zeros(TOKEN.shape, TOKEN.dtype)
        for i in range(relays):
            relay_ref = found_refs[1 + cores + i]
            lane = pl.multiple_of(width + pl.program_id(0) * block, block)
            relay_ref[:, pl.ds(lane, block)] = hidden_refs[1 + i][...]

            @pl.when(pl.program_id(0) == 0)
            def _(i=i, relay_ref=relay_ref):
                relay_ref[:, :width] = refs[2 * cores + i][...]

        @pl.when(pl.program_id(0) == 0)
        def _():
            total_ref[...] = upstream_ref[...]

        for at, size in row_chunks(rows, 512):
            some = pl.ds(at, size)
            total_ref[some, :] += sum(
                jnp.dot(
                    hidden_refs[c][some, :], in_refs[c][...], preferred_element_type=jnp.float32
                )
                for c in range(cores)
            )

        @pl.when(pl.program_id(0) == steps - 1)
        def _():
            totals = [jnp.zeros((1, width), jnp.float32)] * 3
            for at, size in row_chunks(rows, 128):
                some = pl.ds(at, size)
                grad, value = total_ref[some, :], wide(normed_ref[some, :])
                conv_grad = low(norm_back(grad * gain_ref[...], value, wide(slope_ref[some, :])))
                mid_ref[some, :] = grad
                conv_grad_ref[some, :] = conv_grad
                for i, each in enumerate((grad * value, grad, wide(conv_grad))):
                    totals[i] = totals[i] + jnp.sum(each, 0, keepdims=True)
            sums_ref[...] = jnp.zeros(sums_ref.shape, jnp.float32)
            for i in range(3):
                sums_ref[i : i + 1, :] = totals[i]
            for c in range(1, cores):
                first = lax.rem(core_ref[0] - c + cores, cores) * lanes
                cut_refs[c - 1][...] = conv_grad_ref[:, pl.ds(pl.multiple_of(first, lanes), lanes)]
            if reach:
                first = pl.multiple_of((1 - core_ref[1]) * (rows - reach), ROW_TILE)
                found_refs[-4][...] = conv_grad_ref[pl.ds(first, reach), :]

    whole = pl.BlockSpec((rows, width), lambda g, core: (0, 0))
    found = pl.pallas_call(
        kernel,
        grid_spec=pltpu.PrefetchScalarGridSpec(
            num_scalar_prefetch=1,
            grid=(steps,),
            in_specs=[whole, whole, whole, pl.BlockSpec((1, width), lambda g, core: (0, 0))]
            + [pl.BlockSpec((rows, block), lambda g, core: (0, g))]
            + [pl.BlockSpec((rows, block), lambda g, core: (0, width // block + g))] * (cores - 1)
            + [pl.BlockSpec((block, width), lambda g, core: (g, 0))] * cores
            + [whole] * relays
            + tokens(after)
            + [ANYWHERE] * len(reads),
            out_specs=[whole, whole]
            + [pl.BlockSpec((rows, lanes), lambda g, core: (0, 0))] * (cores - 1)
            + [pl.BlockSpec((rows, width + units), lambda g, core: (0, 0))] * relays
            + [pl.BlockSpec((reach, width), lambda g, core: (0, 0))] * rims_out
            + [pl.BlockSpec((8, width), lambda g, core: (0, 0)), TOKEN_SPEC],
            scratch_shapes=[pltpu.VMEM((rows, width), jnp.float32)],
        ),
        out_shape=[
            jax.ShapeDtypeStruct((rows, width), jnp.float32),
            jax.ShapeDtypeStruct((rows, width), jnp.bfloat16),
        ]
        + [jax.ShapeDtypeStruct((rows, lanes), jnp.bfloat16)] * (cores - 1)
        + [jax.ShapeDtypeStruct((rows, width + units), jnp.bfloat16)] * relays
        + [jax.ShapeDtypeStruct((reach, width), jnp.bfloat16)] * rims_out
        + [jax.ShapeDtypeStruct((8, width), jnp.float32), TOKEN],
        compiler_params=pltpu.CompilerParams(vmem_limit_bytes=VMEM_BYTES),
        cost_estimate=cost(5),
        name="ffn_back_stream",
    )(
        jnp.stack(places[:2]).astype(jnp.int32),
        upstream,
        in_hbm(normed),
        in_hbm(slope),
        gain[None],
        in_hbm(hidden),
        *packets,
        *[in_hbm(each) for each in ins],
        *packets[:relays],
        *after,
        *reads,
    )
    return (
        found[0],
        found[1],
        found[2 : 1 + cores],
        found[1 + cores : 1 + cores + relays],
        found[1 + cores + relays] if reach else None,
        found[-2],
        (found[-1],),
    )


def conv_data_grad(extended, weight, upstream, step, kind, after=()):
    taps, inner, width = weight.shape
    rows = upstream.shape[0]
    group = tap_groups(taps)
    steps = taps // group

    def kernel(extended_ref, weight_ref, upstream_ref, *refs):
        out_ref, token_ref, total_ref = refs[-3:]
        token_ref[...] = jnp.zeros(TOKEN.shape, TOKEN.dtype)
        first = pl.program_id(0) * group
        total = None
        for j in range(group):
            start = pl.multiple_of((taps - 1 - first - j) * step, ROW_TILE)
            term = lax.dot_general(
                extended_ref[pl.ds(start, rows), :],
                weight_ref[j],
                (((1,), (1,)), ((), ())),
                preferred_element_type=jnp.float32,
            )
            total = term if total is None else total + term

        @pl.when(pl.program_id(0) == 0)
        def _():
            total_ref[...] = total

        @pl.when(pl.program_id(0) > 0)
        def _():
            total_ref[...] += total

        @pl.when(pl.program_id(0) == steps - 1)
        def _():
            out_ref[...] = (upstream_ref[...] + wide(low(total_ref[...]))).astype(kind)

    whole = pl.BlockSpec((rows, inner), lambda g: (0, 0))
    found = pl.pallas_call(
        kernel,
        grid=(steps,),
        in_specs=[
            pl.BlockSpec(extended.shape, lambda g: (0, 0)),
            pl.BlockSpec((group, inner, width), lambda g: (g, 0, 0)),
            whole,
        ]
        + tokens(after),
        out_specs=(whole, TOKEN_SPEC),
        out_shape=(jax.ShapeDtypeStruct((rows, inner), kind), TOKEN),
        scratch_shapes=[pltpu.VMEM((rows, inner), jnp.float32)],
        compiler_params=pltpu.CompilerParams(vmem_limit_bytes=VMEM_BYTES),
        cost_estimate=cost(6),
        name="conv_data_grad",
    )(extended, in_hbm(weight), upstream, *after)
    return found[0], (found[1],)


def hold(arrays, after, reads=()):
    count = len(arrays)
    if count == 0:
        return [], after

    def kernel(*refs):
        refs[-1][...] = jnp.zeros(TOKEN.shape, TOKEN.dtype)

    found = pl.pallas_call(
        kernel,
        in_specs=[ANYWHERE] * (count + len(reads)) + [WHOLE] * len(after),
        out_specs=[ANYWHERE] * count + [WHOLE],
        out_shape=[jax.ShapeDtypeStruct(each.shape, each.dtype) for each in arrays] + [TOKEN],
        input_output_aliases={i: i for i in range(count)},
        compiler_params=pltpu.CompilerParams(vmem_limit_bytes=1 * MIB),
        cost_estimate=cost(0.5),
        name="hold",
    )(*arrays, *reads, *after)
    return list(found[:-1]), (found[-1],)


def join_rows(parts, after=(), reads=()):
    def kernel(*refs):
        out_ref, token_ref = refs[-2:]
        token_ref[...] = jnp.zeros(TOKEN.shape, TOKEN.dtype)
        first = 0
        for i, part in enumerate(parts):
            out_ref[first : first + part.shape[0]] = refs[i][...]
            first += part.shape[0]

    shape = (sum(part.shape[0] for part in parts), parts[0].shape[1])
    found = pl.pallas_call(
        kernel,
        in_specs=[WHOLE] * len(parts) + [ANYWHERE] * len(reads) + [WHOLE] * len(after),
        out_specs=[WHOLE] * 2,
        out_shape=[jax.ShapeDtypeStruct(shape, parts[0].dtype), TOKEN],
        compiler_params=pltpu.CompilerParams(vmem_limit_bytes=10 * MIB),
        cost_estimate=cost(1.5),
        name="join_rows",
    )(*parts, *reads, *after)
    return found[0], (found[1],)


def restack(groups, reads=(), after=(), fixed=False):
    cuts = [cut for _, each in groups for cut in each]
    if any(last is not None and (first % ROW_TILE or last % ROW_TILE) for first, last, _ in cuts):
        return [
            jnp.stack([array[first:last].reshape(shape) for array in arrays])
            for arrays, each in groups
            for first, last, shape in each
        ], after
    flat = [array for arrays, _ in groups for array in arrays]
    plan = []
    shapes = []
    at = 0
    for arrays, each in groups:
        for first, last, shape in each:
            for slot in range(len(arrays)):
                plan.append((at + slot, first, last, len(shapes), slot))
            held = shape if last is None else (last - first,) + arrays[0].shape[1:]
            shapes.append(jax.ShapeDtypeStruct((len(arrays),) + held, arrays[0].dtype))
        at += len(arrays)

    def kernel(*refs):
        out_refs = refs[-2 - len(shapes) : -2]
        token_ref, sem_ref = refs[-2:]
        token_ref[...] = jnp.zeros(TOKEN.shape, TOKEN.dtype)
        copies = []
        for source, first, last, target, slot in plan:
            ref = refs[source]
            copies.append(
                pltpu.make_async_copy(
                    ref if last is None else ref.at[pl.ds(first, last - first)],
                    out_refs[target].at[slot],
                    sem_ref.at[len(copies)],
                )
            )
        copy_all(copies)

    found = pl.pallas_call(
        kernel,
        in_specs=[ANYWHERE] * (len(flat) + len(reads)) + [WHOLE] * len(after),
        out_specs=[WHOLE] * (len(shapes) + 1),
        out_shape=shapes + [TOKEN],
        scratch_shapes=[pltpu.SemaphoreType.DMA((len(plan),))],
        compiler_params=pltpu.CompilerParams(vmem_limit_bytes=10 * MIB),
        cost_estimate=cost(1.5),
        name="restack",
    )(*([in_hbm(each) for each in flat] if fixed else flat), *reads, *after)
    return [
        each.reshape((each.shape[0],) + shape) for each, (_, _, shape) in zip(found, cuts)
    ], (found[-1],)


def conv_weight_grad(
    extendeds, upstream, arrived, places, sizes, taps, step, after=(), reads=()
):
    cores, seqs, acrosses, tap_peers = sizes
    rows = upstream.shape[0]
    inner = extendeds[0].shape[1]
    lanes = upstream.shape[1] // cores
    slab = inner // (seqs * acrosses * tap_peers)
    direct = slab % ROW_TILE == 0
    half = (tap_peers + 1) // 2
    rest = tap_peers - half
    seconds = acrosses if rest else 0
    outs = seqs + seconds if direct else 1

    def kernel(place_ref, *refs):
        out_refs = refs[-2 - outs : -2]
        token_ref, found_ref = refs[-2:]
        token_ref[...] = jnp.zeros(TOKEN.shape, TOKEN.dtype)
        start = pl.multiple_of(pl.program_id(0) * step, ROW_TILE)
        found = low(
            sum(
                lax.dot_general(
                    refs[c][pl.ds(start, rows), :],
                    refs[cores + c][...],
                    (((0,), (0,)), ((), ())),
                    preferred_element_type=jnp.float32,
                )
                for c in range(cores)
            )
        )
        if not direct:
            out_refs[0][0] = found
            return
        found_ref[...] = found

        def chunk(slot_t, slot_s, slot_a):
            t = lax.rem(place_ref[3] - slot_t + tap_peers, tap_peers)
            at = lax.rem(place_ref[1] - slot_s + seqs, seqs)
            a = lax.rem(place_ref[2] - slot_a + acrosses, acrosses)
            first = pl.multiple_of(((t * seqs + at) * acrosses + a) * slab, slab)
            return found_ref[pl.ds(first, slab), :]

        for s in range(seqs):
            for a in range(acrosses):
                for t in range(half):
                    out_refs[s][a, t, 0] = chunk(t, s, a)
                for t in range(half, tap_peers):
                    out_refs[seqs + a][s, t - half, 0] = chunk(t, s, a)

    if direct:
        shapes = [(acrosses, half, taps, slab, lanes)] * seqs
        shapes += [(seqs, rest, taps, slab, lanes)] * seconds
        specs = [
            pl.BlockSpec(shape[:2] + (1, slab, lanes), lambda k, place: (0, 0, k, 0, 0))
            for shape in shapes
        ]
    else:
        shapes = [(taps, inner, lanes)]
        specs = [pl.BlockSpec((1, inner, lanes), lambda k, place: (k, 0, 0))]
    found = pl.pallas_call(
        kernel,
        grid_spec=pltpu.PrefetchScalarGridSpec(
            num_scalar_prefetch=1,
            grid=(taps,),
            in_specs=[pl.BlockSpec(extendeds[0].shape, lambda k, place: (0, 0))] * cores
            + [pl.BlockSpec((rows, lanes), lambda k, place: (0, place[0]))]
            + [pl.BlockSpec((rows, lanes), lambda k, place: (0, 0))] * (cores - 1)
            + tokens(after)
            + [ANYWHERE] * len(reads),
            out_specs=specs + [TOKEN_SPEC],
            scratch_shapes=[pltpu.VMEM((inner, lanes), jnp.bfloat16)],
        ),
        out_shape=[jax.ShapeDtypeStruct(shape, jnp.bfloat16) for shape in shapes] + [TOKEN],
        compiler_params=pltpu.CompilerParams(vmem_limit_bytes=VMEM_BYTES),
        cost_estimate=cost(9),
        name="conv_weight_grad",
    )(jnp.stack(places).astype(jnp.int32), *extendeds, upstream, *arrived, *after, *reads)
    token = found[-1]
    if not direct:
        found = found[0].reshape(taps, tap_peers, seqs, acrosses, slab, lanes)
        for axis, which in ((1, 3), (2, 1), (3, 2)):
            found = relative(found, axis, places[which], sizes[which])
        found = found.transpose(2, 3, 1, 0, 4, 5)
        found = [found[s, :, :half] for s in range(seqs)] + [
            found[:, a, half:] for a in range(seconds)
        ]
    flat = [each.reshape(-1, lanes) for each in found[: seqs + seconds]]
    return flat[:seqs], flat[seqs:], token


def ffn_weight_grad(pairs, sizes, ffn_rows, after=()):
    cores, seqs, acrosses, tap_peers = sizes
    rows, width = pairs[0][1].shape
    block = tap_peers * ffn_rows
    half = (tap_peers + 1) // 2
    rest = tap_peers - half
    seconds = seqs if rest else 0
    transposed = (((0,), (0,)), ((), ()))
    if ffn_rows % ROW_TILE:
        found = jnp.stack(
            [
                low(
                    sum(
                        lax.dot_general(a, b, transposed, preferred_element_type=jnp.float32)
                        for a, b in [(left, right)]
                        + [(ends[:, width:], starts[:, :width]) for ends, starts in packets]
                    )
                ).reshape(acrosses, seqs, tap_peers, ffn_rows, width)
                for left, right, packets in pairs
            ],
            3,
        )
        token = jnp.zeros(TOKEN.shape, TOKEN.dtype)
        return (
            [found[a, :, :half].reshape(-1, width) for a in range(acrosses)],
            [found[:, s, half:].reshape(-1, width) for s in range(seconds)],
            token,
        )
    outs = acrosses + seconds

    def kernel(*refs):
        out_refs, token_ref = refs[-1 - outs : -1], refs[-1]
        token_ref[...] = jnp.zeros(TOKEN.shape, TOKEN.dtype)
        step = pl.program_id(0)
        for which in range(2):
            base = 2 * cores * which
            found = low(
                sum(
                    lax.dot_general(
                        refs[base + 2 * c][...],
                        refs[base + 2 * c + 1][...],
                        transposed,
                        preferred_element_type=jnp.float32,
                    )
                    for c in range(cores)
                )
            ).reshape(tap_peers, ffn_rows, width)
            for a in range(acrosses):

                @pl.when(step // seqs == a)
                def _(a=a):
                    out_refs[a][0, :, which] = found[:half]

            for s in range(seconds):

                @pl.when(lax.rem(step, seqs) == s)
                def _(s=s):
                    out_refs[acrosses + s][0, :, which] = found[half:]

    right_spec = pl.BlockSpec((rows, width), lambda g: (0, 0))
    left_spec = pl.BlockSpec((rows, block), lambda g: (0, g))
    late_spec = pl.BlockSpec((rows, block), lambda g: (0, width // block + g))

    def first_spec(a):
        return pl.BlockSpec(
            (1, half, 2, ffn_rows, width),
            lambda g: (jnp.clip(g - a * seqs, 0, seqs - 1), 0, 0, 0, 0),
        )

    second_spec = pl.BlockSpec(
        (1, rest, 2, ffn_rows, width), lambda g: (g // seqs, 0, 0, 0, 0)
    )
    operands = []
    for left, right, packets in pairs:
        operands += [in_hbm(left), right]
        for ends, starts in packets:
            operands += [ends, starts]
    found = pl.pallas_call(
        kernel,
        grid=(acrosses * seqs,),
        in_specs=([left_spec, right_spec] + [late_spec, right_spec] * (cores - 1)) * 2
        + tokens(after),
        out_specs=[first_spec(a) for a in range(acrosses)]
        + [second_spec] * seconds
        + [TOKEN_SPEC],
        out_shape=[jax.ShapeDtypeStruct((seqs, half, 2, ffn_rows, width), jnp.bfloat16)] * acrosses
        + [jax.ShapeDtypeStruct((acrosses, rest, 2, ffn_rows, width), jnp.bfloat16)] * seconds
        + [TOKEN],
        compiler_params=pltpu.CompilerParams(vmem_limit_bytes=VMEM_BYTES),
        cost_estimate=cost(8),
        name="ffn_weight_grad",
    )(*operands, *after)
    flat = [each.reshape(-1, width) for each in found[:-1]]
    return flat[:acrosses], flat[acrosses:], found[-1]


def group_slots(groups, lanes):
    flat, where = [], []
    rows = groups[0][0][0].size // (groups[0][1] * lanes)
    for parts, slots in groups:
        where += [(len(flat), len(parts), slot) for slot in range(slots)]
        flat += [part.reshape(slots, rows, lanes) for part in parts]
    return flat, where, rows


def slot_sum(refs, place, first=0):
    start, count, at = place
    return low(sum(wide(refs[first + start + i][at]) for i in range(count)))


def merge_slots(conv_groups, ffn_groups, after=()):
    lanes, width = conv_groups[0][0][0].shape[-1], ffn_groups[0][0][0].shape[-1]
    cuts = width // lanes
    conv_parts, conv_where, conv_rows = group_slots(conv_groups, lanes)
    ffn_parts, ffn_where, ffn_rows = group_slots(ffn_groups, width)
    slots = len(conv_where)
    if conv_rows % ROW_TILE or ffn_rows % ROW_TILE:
        merged = []
        for slot in range(slots):
            ffn = slot_sum(ffn_parts, ffn_where[slot])
            merged.append(
                jnp.concatenate(
                    [slot_sum(conv_parts, conv_where[slot])]
                    + [ffn[:, i * lanes : (i + 1) * lanes] for i in range(cuts)]
                )
            )
        return merged, after

    def kernel(*refs):
        out_refs, token_ref = refs[-1 - slots : -1], refs[-1]
        token_ref[...] = jnp.zeros(TOKEN.shape, TOKEN.dtype)
        for slot in range(slots):
            out_refs[slot][:conv_rows] = slot_sum(refs, conv_where[slot])
            ffn = slot_sum(refs, ffn_where[slot], len(conv_parts))
            for i in range(cuts):
                first = conv_rows + i * ffn_rows
                out_refs[slot][first : first + ffn_rows] = ffn[:, i * lanes : (i + 1) * lanes]

    found = pl.pallas_call(
        kernel,
        in_specs=[WHOLE] * (len(conv_parts) + len(ffn_parts) + len(after)),
        out_specs=[WHOLE] * (slots + 1),
        out_shape=[jax.ShapeDtypeStruct((conv_rows + cuts * ffn_rows, lanes), jnp.bfloat16)] * slots
        + [TOKEN],
        compiler_params=pltpu.CompilerParams(vmem_limit_bytes=10 * MIB),
        cost_estimate=cost(1.5),
        name="merge_slots",
    )(*conv_parts, *ffn_parts, *after)
    return found[:slots], (found[slots],)


def append_slots(groups, packed, after=(), reads=()):
    lanes = groups[0][0][0].shape[-1]
    parts, where, rows = group_slots(groups, lanes)
    slots = len(where)
    if rows % ROW_TILE:
        return [
            jnp.concatenate([slot_sum(parts, where[slot])] + packed) for slot in range(slots)
        ], after

    def kernel(*refs):
        out_refs, token_ref = refs[-1 - slots : -1], refs[-1]
        token_ref[...] = jnp.zeros(TOKEN.shape, TOKEN.dtype)
        for slot in range(slots):
            out_refs[slot][:rows] = slot_sum(refs, where[slot])
            if packed:
                out_refs[slot][rows:] = refs[len(parts)][...]

    shape = jax.ShapeDtypeStruct((rows + sum(each.shape[0] for each in packed), lanes), jnp.bfloat16)
    found = pl.pallas_call(
        kernel,
        in_specs=[WHOLE] * (len(packed) + len(parts) + len(after)) + [ANYWHERE] * len(reads),
        out_specs=[WHOLE] * (slots + 1),
        out_shape=[shape] * slots + [TOKEN],
        compiler_params=pltpu.CompilerParams(vmem_limit_bytes=8 * MIB),
        cost_estimate=cost(1),
        name="append_slots",
    )(*parts, *packed, *after, *reads)
    return found[:slots], (found[slots],)


def pack_small(row_groups, biases, losses, places, sizes, ffn_rows, after=(), reads=()):
    cores, seqs, acrosses, tap_peers = sizes
    width = row_groups[0][0].shape[1]
    head_rows = sum(count for _, count in row_groups)
    hidden = cores * biases[0][0].shape[1]
    bias_rows = hidden // width
    used = head_rows + len(biases) * bias_rows + 2
    rows = -(-used // ROW_TILE) * ROW_TILE
    lanes = width // 2
    per_row = width // ffn_rows
    if ffn_rows % 64:
        terms = jnp.stack([losses[0, 0], losses[1, 0]])
        terms = jnp.stack([terms, terms - wide(low(terms))])
        pieces = [array[:count] for array, count in row_groups]
        for each in biases:
            bias = jnp.stack(each).reshape(cores, acrosses, seqs, tap_peers, ffn_rows)
            for axis, which in enumerate((0, 2, 1, 3)):
                bias = relative(bias, axis, places[which], sizes[which])
            pieces.append(bias.transpose(1, 0, 2, 3, 4).reshape(-1, width))
        pieces.append(jnp.pad(terms, ((0, rows - used), (0, width - 2))))
        packed = low(jnp.concatenate(pieces))
        return jnp.concatenate([packed[:, :lanes], packed[:, lanes:]]), after

    def kernel(place_ref, *refs):
        packed_ref, token_ref, rows_ref = refs[-3:]
        token_ref[...] = jnp.zeros(TOKEN.shape, TOKEN.dtype)
        rows_ref[...] = jnp.zeros(rows_ref.shape, jnp.float32)
        at = 0
        for i, (_, count) in enumerate(row_groups):
            rows_ref[at : at + count, :] = refs[i][:count, :]
            at += count
        shape = (cores, acrosses, seqs, tap_peers)
        owners = (0, 2, 1, 3)
        for b in range(len(biases)):
            blocks = {}
            for slot in np.ndindex(*shape):
                first = ((slot[1] * seqs + slot[2]) * tap_peers + slot[3]) * ffn_rows
                ref = refs[len(row_groups) + b * cores + slot[0]]
                blocks[slot] = ref[:, first : first + ffn_rows]
            for axis, size in enumerate(shape):
                turned = {}
                for slot in blocks:
                    place = lax.rem(place_ref[owners[axis]] - slot[axis] + size, size)
                    value = blocks[slot[:axis] + (0,) + slot[axis + 1 :]]
                    for other in range(1, size):
                        candidate = blocks[slot[:axis] + (other,) + slot[axis + 1 :]]
                        value = jnp.where(place == other, candidate, value)
                    turned[slot] = value
                blocks = turned
            ordered = [
                blocks[(c, a, s, t)]
                for a in range(acrosses)
                for c in range(cores)
                for s in range(seqs)
                for t in range(tap_peers)
            ]
            for row in range(bias_rows):
                line = ordered[row * per_row : (row + 1) * per_row]
                rows_ref[at : at + 1, :] = jnp.concatenate(line, 1)
                at += 1
        losses_ref = refs[len(row_groups) + len(biases) * cores]
        lane = lax.broadcasted_iota(jnp.int32, (1, width), 1)
        objective = jnp.broadcast_to(losses_ref[0:1, 0:1], (1, width))
        scored = jnp.broadcast_to(losses_ref[1:2, 0:1], (1, width))
        line = jnp.where(lane == 0, objective, jnp.where(lane == 1, scored, 0.0))
        rows_ref[at : at + 1, :] = line
        rows_ref[at + 1 : at + 2, :] = line - wide(low(line))
        packed_ref[:rows, :] = low(rows_ref[:, :lanes])
        packed_ref[rows:, :] = low(rows_ref[:, lanes:])

    flat = [array for array, _ in row_groups] + [each for some in biases for each in some]
    found = pl.pallas_call(
        kernel,
        in_specs=[SCALARS] + [WHOLE] * (len(flat) + 1 + len(after)) + [ANYWHERE] * len(reads),
        out_specs=[WHOLE] * 2,
        out_shape=[jax.ShapeDtypeStruct((2 * rows, lanes), jnp.bfloat16), TOKEN],
        scratch_shapes=[pltpu.VMEM((rows, width), jnp.float32)],
        compiler_params=pltpu.CompilerParams(vmem_limit_bytes=8 * MIB),
        cost_estimate=cost(2),
        name="pack_small",
    )(jnp.stack(places).astype(jnp.int32), *flat, losses, *after, *reads)
    return found[0], (found[1],)


def paired(values):
    while len(values) > 1:
        half = len(values) // 2
        if len(values) % 2:
            return sum(values[1:], values[0])
        values = [values[i] + values[i + half] for i in range(half)]
    return values[0]


def finish_small(stacks, first, width, classes, hidden, places, sizes):
    cores, seqs, acrosses = sizes[:3]
    peers, rows, lanes = stacks[0].shape
    count = rows - first
    bias_rows = hidden // width
    at_bias = 12 + classes
    at_loss = at_bias + 2 * bias_rows

    def pick(row):
        return (
            [row(2), row(5)],
            [[row(0), row(6)], [row(3), row(9)]],
            [[row(1), row(7)], [row(4), row(10)]],
            [[row(at_bias + b * bias_rows + i) for i in range(bias_rows)] for b in range(2)],
            [row(8), row(11)],
        )

    if max(cores, seqs, acrosses) > 2 or first % count or count % ROW_TILE:
        full = jnp.stack(
            [wide(each[:, first:]).reshape(seqs, acrosses, count, lanes) for each in stacks]
        )
        for axis, (place, size) in enumerate(zip(places[:3], sizes[:3])):
            full = relative(full, axis, place, size)
        total = jnp.sum(full, (0, 1, 2))
        total = jnp.concatenate([total[: count // 2], total[count // 2 :]], 1)
        conv_bias, gains, shifts, in_bias, out_bias = pick(lambda i: total[i])
        terms = total[at_loss] + total[at_loss + 1]
        return (
            jnp.stack(conv_bias),
            jnp.stack([jnp.stack(each) for each in gains]),
            jnp.stack([jnp.stack(each) for each in shifts]),
            jnp.stack([jnp.concatenate(each) for each in in_bias]),
            jnp.stack(out_bias),
            total[12:at_bias].T,
            (terms[0] / terms[1]).reshape(1, 1),
        )

    def kernel(*refs):
        conv_ref, gain_ref, shift_ref, in_ref, out_ref, head_ref, loss_ref, rows_ref = refs[cores:]
        total = paired(
            [
                paired(
                    [
                        paired([wide(refs[c][s * acrosses + a]) for a in range(acrosses)])
                        for s in range(seqs)
                    ]
                )
                for c in range(cores)
            ]
        )
        rows_ref[:, :lanes] = total[: count // 2]
        rows_ref[:, lanes:] = total[count // 2 :]
        conv_bias, gains, shifts, in_bias, out_bias = pick(lambda i: rows_ref[i : i + 1, :])
        for b in range(2):
            conv_ref[b : b + 1, :] = conv_bias[b]
            out_ref[b : b + 1, :] = out_bias[b]
            for i in range(2):
                gain_ref[b, i : i + 1, :] = gains[b][i]
                shift_ref[b, i : i + 1, :] = shifts[b][i]
            for i in range(bias_rows):
                in_ref[b : b + 1, i * width : (i + 1) * width] = in_bias[b][i]
        head_ref[...] = rows_ref[12 : 12 + 8 * (-(-classes // 8)), :].T[:, :classes]
        terms = rows_ref[at_loss : at_loss + 1, :128] + rows_ref[at_loss + 1 : at_loss + 2, :128]
        loss_ref[...] = terms[:, 0:1] / terms[:, 1:2]

    return pl.pallas_call(
        kernel,
        grid=(1,),
        in_specs=[pl.BlockSpec((peers, count, lanes), lambda g: (0, first // count, 0))] * cores,
        out_shape=(
            jax.ShapeDtypeStruct((2, width), jnp.float32),
            jax.ShapeDtypeStruct((2, 2, width), jnp.float32),
            jax.ShapeDtypeStruct((2, 2, width), jnp.float32),
            jax.ShapeDtypeStruct((2, hidden), jnp.float32),
            jax.ShapeDtypeStruct((2, width), jnp.float32),
            jax.ShapeDtypeStruct((width, classes), jnp.float32),
            jax.ShapeDtypeStruct((1, 1), jnp.float32),
        ),
        out_specs=[
            pl.BlockSpec((2, width), lambda g: (0, 0)),
            pl.BlockSpec((2, 2, width), lambda g: (0, 0, 0)),
            pl.BlockSpec((2, 2, width), lambda g: (0, 0, 0)),
            pl.BlockSpec((2, hidden), lambda g: (0, 0)),
            pl.BlockSpec((2, width), lambda g: (0, 0)),
            pl.BlockSpec((width, classes), lambda g: (0, 0)),
            pl.BlockSpec((1, 1), lambda g: (0, 0)),
        ],
        scratch_shapes=[pltpu.VMEM((count // 2, 2 * lanes), jnp.float32)],
        compiler_params=pltpu.CompilerParams(vmem_limit_bytes=4 * MIB),
        cost_estimate=cost(1.5),
        name="finish_small",
    )(*stacks)


def finish_conv(parts, conv_rows, small_rows, after=()):
    blocks, count = len(parts), len(parts[0])
    lanes = parts[0][0].shape[-1]
    flat = [part for block in parts for part in block]
    if conv_rows % ROW_TILE:
        sums = [sum(wide(part[:conv_rows]) for part in block) for block in parts]
        sums.append(paired([wide(part[conv_rows:]) for part in parts[0]]))
        return jnp.concatenate([low(total) for total in sums]), after

    def kernel(*refs):
        shard_ref, token_ref = refs[-2:]
        token_ref[...] = jnp.zeros(TOKEN.shape, TOKEN.dtype)
        shard_ref[blocks * conv_rows :] = low(
            paired([wide(refs[i][conv_rows:]) for i in range(count)])
        )
        for b in range(blocks):
            total = sum(wide(refs[b * count + i][:conv_rows]) for i in range(count))
            shard_ref[b * conv_rows : (b + 1) * conv_rows] = low(total)

    found = pl.pallas_call(
        kernel,
        in_specs=[WHOLE] * (len(flat) + len(after)),
        out_specs=[WHOLE] * 2,
        out_shape=[
            jax.ShapeDtypeStruct((blocks * conv_rows + small_rows, lanes), jnp.bfloat16),
            TOKEN,
        ],
        compiler_params=pltpu.CompilerParams(vmem_limit_bytes=8 * MIB),
        cost_estimate=cost(1.2),
        name="finish_conv",
    )(*flat, *after)
    return found[0], (found[1],)


def finish_ffn(merged, plain, conv_rows, ffn_rows, after=()):
    lanes, width = merged[0].shape[-1], plain[0].shape[-1]

    def cut_back(total):
        size = 2 * ffn_rows
        return jnp.concatenate(
            [total[i * size : (i + 1) * size] for i in range(width // lanes)], 1
        )

    if conv_rows % ROW_TILE or ffn_rows % ROW_TILE:
        sums = [sum(wide(part) for part in plain)]
        sums.append(cut_back(sum(wide(part[conv_rows:]) for part in merged)))
        return jnp.stack([each[:ffn_rows].T for each in sums]), jnp.stack(
            [each[ffn_rows:] for each in sums]
        ), after

    def kernel(*refs):
        in_ref, out_ref, token_ref = refs[-3:]
        token_ref[...] = jnp.zeros(TOKEN.shape, TOKEN.dtype)
        late = sum(wide(refs[i][conv_rows:]) for i in range(len(merged)))
        sums = [sum(wide(refs[len(merged) + i][...]) for i in range(len(plain))), cut_back(late)]
        for b in range(2):
            in_ref[b] = sums[b][:ffn_rows].T
            out_ref[b] = sums[b][ffn_rows:]

    found = pl.pallas_call(
        kernel,
        in_specs=[WHOLE] * (len(merged) + len(plain) + len(after)),
        out_specs=[WHOLE] * 3,
        out_shape=(
            jax.ShapeDtypeStruct((2, width, ffn_rows), jnp.float32),
            jax.ShapeDtypeStruct((2, ffn_rows, width), jnp.float32),
            TOKEN,
        ),
        compiler_params=pltpu.CompilerParams(vmem_limit_bytes=8 * MIB),
        cost_estimate=cost(1),
        name="finish_ffn",
    )(*merged, *plain, *after)
    return found[0], found[1], (found[2],)


def add_slots(parts, slots, after=(), reads=()):
    lanes = parts[0].shape[-1]
    rows = parts[0].size // (slots * lanes)
    parts = [part.reshape(slots, rows, lanes) for part in parts]
    block = rows // 4 if rows % (4 * ROW_TILE) == 0 else rows

    def kernel(*refs):
        out_refs, token_ref = refs[-1 - slots : -1], refs[-1]
        token_ref[...] = jnp.zeros(TOKEN.shape, TOKEN.dtype)
        for slot in range(slots):
            out_refs[slot][...] = low(sum(wide(refs[i][slot]) for i in range(len(parts))))

    found = pl.pallas_call(
        kernel,
        grid=(rows // block,),
        in_specs=[pl.BlockSpec((slots, block, lanes), lambda g: (0, g, 0))] * len(parts)
        + tokens(after)
        + [ANYWHERE] * len(reads),
        out_specs=[pl.BlockSpec((block, lanes), lambda g: (g, 0))] * slots + [TOKEN_SPEC],
        out_shape=[jax.ShapeDtypeStruct((rows, lanes), jnp.bfloat16)] * slots + [TOKEN],
        compiler_params=pltpu.CompilerParams(vmem_limit_bytes=8 * MIB),
        cost_estimate=cost(2),
        name="add_slots",
    )(*parts, *after, *reads)
    return found[:slots], found[slots]


def place_conv_grads(stacks, blocks, taps, slab, places, sizes):
    cores, seqs, acrosses = sizes[:3]
    peers, rows, lanes = stacks[0].shape
    channels = slab * seqs * acrosses
    if slab % ROW_TILE or rows % slab:
        full = jnp.stack([each[:, : blocks * taps * slab] for each in stacks])
        full = full.reshape(cores, seqs, acrosses, blocks, taps, slab, lanes)
        for axis, (place, size) in enumerate(zip(places[:3], sizes[:3])):
            full = relative(full, axis, place, size)
        return wide(
            full.transpose(3, 4, 1, 2, 5, 0, 6).reshape(blocks, taps, channels, cores * lanes)
        )
    stacks = [each.reshape(peers, rows // slab, slab, lanes) for each in stacks]

    def kernel(place_ref, *refs):
        out_ref = refs[-1]
        for c in range(cores):
            lane = pl.multiple_of(lax.rem(place_ref[0] - c + cores, cores) * lanes, lanes)
            for s in range(seqs):
                at_s = lax.rem(place_ref[1] - s + seqs, seqs)
                for a in range(acrosses):
                    at_a = lax.rem(place_ref[2] - a + acrosses, acrosses)
                    row = pl.multiple_of((at_s * acrosses + at_a) * slab, slab)
                    for b in range(blocks):
                        piece = wide(refs[c * blocks + b][s * acrosses + a, 0])
                        out_ref[b, 0, pl.ds(row, slab), pl.ds(lane, lanes)] = piece

    specs = [
        pl.BlockSpec((peers, 1, slab, lanes), lambda k, place, b=b: (0, b * taps + k, 0, 0))
        for b in range(blocks)
    ]
    return pl.pallas_call(
        kernel,
        grid_spec=pltpu.PrefetchScalarGridSpec(
            num_scalar_prefetch=1,
            grid=(taps,),
            in_specs=specs * cores,
            out_specs=pl.BlockSpec(
                (blocks, 1, channels, cores * lanes), lambda k, place: (0, k, 0, 0)
            ),
        ),
        out_shape=jax.ShapeDtypeStruct((blocks, taps, channels, cores * lanes), jnp.float32),
        compiler_params=pltpu.CompilerParams(vmem_limit_bytes=10 * MIB),
        cost_estimate=cost(5),
        name="place_conv_grads",
    )(
        jnp.stack(places[:3]).astype(jnp.int32),
        *[each for stack in stacks for each in [stack] * blocks],
    )


def copy_all(copies):
    for copy in copies:
        copy.start()
    for copy in copies:
        copy.wait()


def place_conv(pieces, places, sizes, after=(), reads=()):
    cores, seqs, acrosses, tap_peers = sizes
    taps, slab, lanes = pieces[0][0].shape[2:]
    inner = slab * seqs * acrosses * tap_peers
    if slab % ROW_TILE:
        full = jnp.stack([jnp.stack(row) for row in pieces])
        for axis, (place, size) in enumerate(zip(places, sizes)):
            full = relative(full, axis, place, size)
        return full.transpose(4, 3, 1, 2, 5, 0, 6).reshape(taps, inner, cores * lanes), after
    flat = [piece for row in pieces for piece in row]

    def kernel(place_ref, *refs):
        out_ref, token_ref, sem_ref = refs[-3:]
        token_ref[...] = jnp.zeros(TOKEN.shape, TOKEN.dtype)
        copies = []
        for c in range(cores):
            lane = lax.rem(place_ref[0] - c + cores, cores) * lanes
            for s in range(seqs):
                at_s = lax.rem(place_ref[1] - s + seqs, seqs)
                for a in range(acrosses):
                    at_a = lax.rem(place_ref[2] - a + acrosses, acrosses)
                    for t in range(tap_peers):
                        at_t = lax.rem(place_ref[3] - t + tap_peers, tap_peers)
                        row = ((at_t * seqs + at_s) * acrosses + at_a) * slab
                        copies.append(
                            pltpu.make_async_copy(
                                refs[c * seqs + s].at[a, t],
                                out_ref.at[
                                    :,
                                    pl.ds(pl.multiple_of(row, slab), slab),
                                    pl.ds(pl.multiple_of(lane, lanes), lanes),
                                ],
                                sem_ref.at[len(copies)],
                            )
                        )
        copy_all(copies)

    found = pl.pallas_call(
        kernel,
        in_specs=[SCALARS] + [ANYWHERE] * (len(flat) + len(reads)) + [WHOLE] * len(after),
        out_specs=[WHOLE] * 2,
        out_shape=[pltpu.HBM((taps, inner, cores * lanes), jnp.bfloat16), TOKEN],
        scratch_shapes=[pltpu.SemaphoreType.DMA((cores * seqs * acrosses * tap_peers,))],
        compiler_params=pltpu.CompilerParams(vmem_limit_bytes=12 * MIB),
        cost_estimate=cost(3),
        name="place_conv",
    )(jnp.stack(places).astype(jnp.int32), *flat, *reads, *after)
    return found[0], (found[1],)


def place_ffn(pieces, sizes, after=(), reads=()):
    cores, seqs, acrosses, tap_peers = sizes
    cuts, ffn_rows, lanes = pieces[0][0].shape[2:]
    cuts //= 2
    width = cuts * lanes
    units = seqs * acrosses * tap_peers * ffn_rows
    if ffn_rows % ROW_TILE:
        full = jnp.stack([jnp.stack(row) for row in pieces])
        full = full.reshape(cores, acrosses, seqs, tap_peers, 2, cuts, ffn_rows, lanes)
        full = full.transpose(4, 0, 1, 2, 3, 6, 5, 7).reshape(2, cores, units, width)
        return [full[0, c] for c in range(cores)], [full[1, c] for c in range(cores)], after
    flat = [piece for row in pieces for piece in row]

    def kernel(*refs):
        out_refs = refs[-2 - 2 * cores : -2]
        token_ref, sem_ref = refs[-2:]
        token_ref[...] = jnp.zeros(TOKEN.shape, TOKEN.dtype)
        copies = []
        for c in range(cores):
            for a in range(acrosses):
                for which in range(2):
                    for cut in range(cuts):
                        copies.append(
                            pltpu.make_async_copy(
                                refs[c * acrosses + a].at[:, :, which * cuts + cut],
                                out_refs[which * cores + c].at[
                                    a, :, :, :, pl.ds(cut * lanes, lanes)
                                ],
                                sem_ref.at[len(copies)],
                            )
                        )
        copy_all(copies)

    shape = pltpu.HBM((acrosses, seqs, tap_peers, ffn_rows, width), jnp.bfloat16)
    found = pl.pallas_call(
        kernel,
        in_specs=[ANYWHERE] * (len(flat) + len(reads)) + [WHOLE] * len(after),
        out_specs=[WHOLE] * (2 * cores + 1),
        out_shape=[shape] * (2 * cores) + [TOKEN],
        scratch_shapes=[pltpu.SemaphoreType.DMA((2 * cores * acrosses * cuts,))],
        compiler_params=pltpu.CompilerParams(vmem_limit_bytes=12 * MIB),
        cost_estimate=cost(2),
        name="place_ffn",
    )(*flat, *reads, *after)
    token = found[-1]
    found = [each.reshape(units, width) for each in found[:-1]]
    return found[:cores], found[cores:], (token,)


class Ring:
    def __init__(self, axis, size, index, pairs):
        self.axis, self.size, self.index, self.pairs = axis, size, index, pairs

    def shifted(self, value, by):
        return lax.ppermute(value, self.axis, self.pairs(lambda i: (i + by) % self.size))

    def swapped(self, value, bit):
        return lax.ppermute(value, self.axis, self.pairs(lambda i: i ^ bit))

    def gather(self, value):
        return [value] + [self.shifted(value, by) for by in range(1, self.size)]

    def swap(self, values):
        return [values[0]] + [self.shifted(values[by], -by) for by in range(1, self.size)]


def relative(value, axis, place, size):
    if size == 1:
        return value
    return jnp.stack(
        [
            lax.dynamic_index_in_dim(value, (place - slot) % size, axis, False)
            for slot in range(size)
        ],
        axis,
    )


def rings():
    peers = lax.axis_size("dp")
    cores = CORES if peers % CORES == 0 else 1
    columns = peers // cores
    place = lax.axis_index("dp")

    def plain(axis):
        size = lax.axis_size(axis)
        return Ring(
            axis, size, lax.axis_index(axis), lambda move: [(i, move(i)) for i in range(size)]
        )

    across = Ring(
        "dp",
        columns,
        place // cores,
        lambda move: [(i, move(i // cores) * cores + i % cores) for i in range(peers)],
    )
    core = Ring(
        "dp",
        cores,
        place % cores,
        lambda move: [(i, i // cores * cores + move(i % cores)) for i in range(peers)],
    )
    return core, across, plain("seq"), plain("tap")


class Reduce:
    def __init__(self, terms, order):
        self.order = order
        self.parts = [terms[0]] + [order[0].shifted(terms[s], -s) for s in range(1, order[0].size)]

    def step(self, level, after, reads=()):
        ring = self.order[level]
        found, token = add_slots(self.parts, ring.size, after, reads)
        self.parts = [found[0]] + [ring.shifted(found[s], -s) for s in range(1, ring.size)]
        return (token,)


def shared_copies(value, across, seq):
    peers, spans = lax.axis_size("dp"), lax.axis_size("seq")
    cores = peers // across.size

    def target(place, by_a, by_s):
        dp, at = place // spans, place % spans
        moved = (dp // cores + by_a) % across.size * cores + dp % cores
        return moved * spans + (at + by_s) % spans

    return [
        [
            value
            if by_a == by_s == 0
            else lax.ppermute(
                value,
                ("dp", "seq"),
                [(place, target(place, by_a, by_s)) for place in range(peers * spans)],
            )
            for by_a in range(across.size)
        ]
        for by_s in range(seq.size)
    ]


def passed_along(value, axis, by):
    peers = lax.axis_size(axis)
    pairs = [(i, i + by) for i in range(peers) if 0 <= i + by < peers]
    return lax.ppermute(value, axis, pairs)


def rims(source, reach_rows, seq, rim=None):
    span_rows = source.shape[0]
    if seq.size == 2 and reach_rows <= span_rows:
        if rim is None:
            first = (1 - seq.index) * (span_rows - reach_rows)
            rim = lax.dynamic_slice_in_dim(source, first, reach_rows, 0)
        return seq.shifted(rim, 1)
    left_parts = []
    right_parts = []
    distances = -(-reach_rows // span_rows)
    for distance in range(1, distances + 1):
        rim_count = min(span_rows, reach_rows - (distance - 1) * span_rows)
        left_parts.insert(0, passed_along(source[span_rows - rim_count :], "seq", distance))
        right_parts.append(passed_along(source[:rim_count], "seq", -distance))
    return left_parts, right_parts


def extend(source, found, seq, after=()):
    if isinstance(found, tuple):
        return join_rows(found[0] + [source] + found[1], after)
    reach, span = found.shape[0], source.shape[0]

    def kernel(place_ref, found_ref, source_ref, *refs):
        out_ref, token_ref = refs[-2:]
        token_ref[...] = jnp.zeros(TOKEN.shape, TOKEN.dtype)
        out_ref[reach : reach + span] = source_ref[...]
        zeros = jnp.zeros(found.shape, found.dtype)

        @pl.when(place_ref[0] == 0)
        def _():
            out_ref[:reach] = zeros
            out_ref[reach + span :] = found_ref[...]

        @pl.when(place_ref[0] != 0)
        def _():
            out_ref[:reach] = found_ref[...]
            out_ref[reach + span :] = zeros

    shape = jax.ShapeDtypeStruct((span + 2 * reach, source.shape[1]), source.dtype)
    extended, token = pl.pallas_call(
        kernel,
        in_specs=[SCALARS] + [WHOLE] * (2 + len(after)),
        out_specs=[WHOLE] * 2,
        out_shape=[shape, TOKEN],
        compiler_params=pltpu.CompilerParams(vmem_limit_bytes=10 * MIB),
        cost_estimate=cost(1.5),
        name="extend",
    )(seq.index.astype(jnp.int32)[None], found, source, *after)
    return extended, (token,)


def to_rows(values):
    windows, positions = values.shape[:2]
    cut = values.reshape((windows, positions // FIRST_DILATION, FIRST_DILATION) + values.shape[2:])
    return jnp.swapaxes(cut, 0, 1).reshape((windows * positions,) + values.shape[2:])


def from_rows(values, windows):
    cut = values.reshape((-1, windows, FIRST_DILATION) + values.shape[1:])
    return jnp.swapaxes(cut, 0, 1).reshape((windows, -1) + values.shape[1:])


def on_device(
    inputs,
    targets,
    masked,
    conv_weight,
    conv_bias,
    gains,
    shifts,
    in_weight,
    in_bias,
    out_weight,
    out_bias,
    head_weight,
):
    core, across, seq, tap = rings()
    taps = conv_weight.shape[1]
    channels = conv_weight.shape[2]
    width = conv_weight.shape[3]
    slab = channels // (seq.size * across.size)
    lanes = width // core.size
    hidden_width = in_bias.shape[1]
    ffn_rows = in_weight.shape[2]
    windows = inputs.shape[0]
    rows = windows * inputs.shape[1]
    steps = (FIRST_DILATION * windows, SECOND_DILATION * windows)
    units = hidden_width // core.size
    places = (core.index, seq.index, across.index, tap.index)
    sizes = (core.size, seq.size, across.size, tap.size)

    in_bias_placed = []
    for b in range(2):
        bias = in_bias[b].reshape(across.size, core.size, seq.size, tap.size, ffn_rows)
        for axis, ring in enumerate((across, core, seq, tap)):
            bias = relative(bias, axis, ring.index, ring.size)
        in_bias_placed.append(bias.transpose(1, 0, 2, 3, 4).reshape(core.size, units))

    def cut_ffn(piece):
        return piece.reshape(ffn_rows, core.size, lanes).swapaxes(0, 1).reshape(-1, lanes)

    def bundle(b, ready=None):
        conv_piece = lax.dynamic_slice(
            conv_weight[b],
            (0, (seq.index * across.size + across.index) * slab, core.index * lanes),
            (taps, slab, lanes),
        )
        pieces = [
            conv_piece.reshape(taps * slab, lanes),
            cut_ffn(in_weight[b].T),
            cut_ffn(out_weight[b]),
        ]
        if ready is not None:
            pieces = [piece + ready for piece in pieces]
        return jnp.concatenate(pieces)

    cuts = (
        (0, taps * slab, (taps, slab, lanes)),
        (taps * slab, taps * slab + 2 * core.size * ffn_rows, (2 * core.size, ffn_rows, lanes)),
    )

    def straight(arrays):
        return (arrays, ((0, None, arrays[0].shape),))

    conv_input = to_rows(inputs)
    stream = conv_input
    codes = to_rows(targets + masked * head_weight.shape[1])
    codes = jnp.broadcast_to(codes[:, None], (rows, 128))

    reaches = [taps // 2 * step for step in steps]
    rim_reaches = [reach if seq.size == 2 and reach <= rows else 0 for reach in reaches]

    tap_parts = tap.gather(bundle(0))
    found = rims(conv_input, reaches[0], seq)
    behind = bundle(1, tap_parts[-1][0, 0] * 0)
    (conv_part, ffn_part), last = restack(
        [(tap_parts, cuts)], reads=[behind] + [found if rim_reaches[0] else conv_input]
    )
    (behind,), last = hold([behind], last)
    split = (tap.size + 1) // 2
    late_parts = tap.gather(behind)
    extended, last = extend(conv_input, found, seq, last)
    extended_parts = [extended] + [core.shifted(extended, -c) for c in range(1, core.size)]
    conv_parts, ffn_parts = across.gather(conv_part), seq.gather(ffn_part)
    (conv_part, ffn_part), last = restack(
        [straight(conv_parts), straight(ffn_parts)],
        reads=late_parts[1:split],
        after=last,
    )
    conv_parts, ffn_parts = seq.gather(conv_part), across.gather(ffn_part)
    conv_slots = [core.gather(conv_part)]
    ffn_slots = [core.gather(ffn_part)]
    held, last = hold(
        conv_parts[1:] + ffn_parts[1:],
        last,
        conv_slots[0][1:] + ffn_slots[0][1:] + late_parts[1:],
    )
    conv_slots += [core.gather(each) for each in held[: seq.size - 1]]
    ffn_slots += [core.gather(each) for each in held[seq.size - 1 :]]
    (late_conv, late_ffn), last = restack([(late_parts, cuts)], after=last, fixed=True)
    late_conv_parts, late_ffn_parts = across.gather(late_conv), seq.gather(late_ffn)

    def turned(slots):
        return [[each[c] for each in slots] for c in range(core.size)]

    conv_full, in_full, out_full = [None, None], [None, None], [None, None]
    conv_full[0], last = place_conv(
        turned(conv_slots), places, sizes, last, [part for each in ffn_slots for part in each[1:]]
    )
    saved = []
    reads = []
    rim = None
    for b in range(2):
        if b == 1:
            found = rims(conv_input, reaches[1], seq, rim)
            held, last = hold(late_conv_parts[1:] + late_ffn_parts[1:], last)
            late_conv_slots += [core.gather(each) for each in held[: seq.size - 1]]
            late_ffn_slots += [core.gather(each) for each in held[seq.size - 1 :]]
            conv_full[1], last = place_conv(turned(late_conv_slots), places, sizes, last)
            in_full[1], out_full[1], last = place_ffn(turned(late_ffn_slots), sizes, last)
            extended, last = extend(conv_input, found, seq, last)
            extended_parts = [extended] + [core.shifted(extended, -c) for c in range(1, core.size)]
        (normed_conv, conv_slope, stream, lowered), last = conv_forward(
            extended,
            conv_full[b],
            stream,
            conv_bias[b],
            gains[b, 0],
            shifts[b, 0],
            steps[b],
            last,
            reads,
        )
        reads = extended_parts[1:]
        if b == 0:
            (late_conv, late_ffn), last = restack(
                [straight(late_conv_parts), straight(late_ffn_parts)], after=last
            )
            late_conv_parts, late_ffn_parts = seq.gather(late_conv), across.gather(late_ffn)
            late_conv_slots = [core.gather(late_conv)]
            late_ffn_slots = [core.gather(late_ffn)]
            in_full[0], out_full[0], last = place_ffn(turned(ffn_slots), sizes, last)
            reads = reads + late_conv_slots[0][1:] + late_ffn_slots[0][1:]
        active, hidden_slopes, (normed_ffn, scale_ffn, stream, conv_input), packets, rim, last = (
            ffn_forward(
                lowered,
                stream,
                in_full[b],
                out_full[b],
                [in_bias_placed[b][c] for c in range(core.size)],
                out_bias[b],
                gains[b, 1],
                shifts[b, 1],
                seq.index,
                rim_reaches[1] if b == 0 else 0,
                b == 1,
                last,
                reads,
            )
        )
        packets = [core.shifted(packet, -1 - c) for c, packet in enumerate(packets)]
        reads = packets
        saved.append(
            (
                extended_parts,
                conv_slope,
                normed_conv,
                (active, lowered, packets),
                hidden_slopes,
                normed_ffn,
                scale_ffn,
            )
        )

    (stream_grad, head_grad, loss_rows), last = head_and_loss(stream, head_weight, codes, last)

    ffn_rows_of_sums = [None, None]
    conv_rows_of_sums = [None, None]
    in_bias_grads = [None, None]
    ffn_sums = [None, None]
    conv_sums = [None, None]
    merged = [None, None]

    def groups(halves):
        half = (tap.size + 1) // 2
        return [(each.parts, slots) for each, slots in zip(halves, (half, tap.size - half))]

    for b in (1, 0):
        (
            extended_parts,
            conv_slope,
            normed_conv,
            active_pair,
            hidden_slopes,
            normed_ffn,
            scale_ffn,
        ) = saved[b]
        output_grad, hidden_grad, biases, packets, ffn_rows_of_sums[b], last = ffn_back_hidden(
            stream_grad, normed_ffn, scale_ffn, gains[b, 1], out_full[b], hidden_slopes, last
        )
        if b == 1:
            arrived_packets = [core.shifted(packet, -1 - c) for c, packet in enumerate(packets)]
        if b == 0:
            for each in ffn_sums[1]:
                last = each.step(1, last)
            for each in conv_sums[1]:
                last = each.step(1, last)
        stream_grad, conv_grad, conv_cuts, relayed, rim, conv_rows_of_sums[b], last = ffn_back_stream(
            stream_grad,
            hidden_grad,
            packets,
            in_full[b],
            normed_conv,
            conv_slope,
            gains[b, 0],
            places,
            rim_reaches[b],
            last,
            reads,
            relay=b == 0,
        )
        reads = []
        if b == 0:
            merged[1], last = merge_slots(
                groups(conv_sums[1]), groups(ffn_sums[1]), last
            )
            sent = [rim] if rim is not None else []
            held, last = hold(list(conv_cuts) + list(relayed) + sent, last)
            conv_cuts, relayed = held[: core.size - 1], held[core.size - 1 : 2 * core.size - 2]
            rim = held[-1] if sent else None
            merged[1] = tap.swap(merged[1])
            arrived_packets = [core.shifted(packet, -1 - c) for c, packet in enumerate(relayed)]
        arrived = [core.shifted(conv_cuts[c - 1], -c) for c in range(1, core.size)]
        in_bias_grads[b] = list(biases)
        found_rims = rims(conv_grad, reaches[b], seq, rim)

        def ffn_grads(last):
            active, lowered, packets = active_pair
            if core.size == 1:
                packets = []
            first, second, token = ffn_weight_grad(
                (
                    (hidden_grad, lowered, [(g, p) for g, p in zip(arrived_packets, packets)]),
                    (active, output_grad, [(p, g) for g, p in zip(arrived_packets, packets)]),
                ),
                sizes,
                ffn_rows,
                last,
            )
            found = [Reduce(first, (across, seq))]
            if second:
                found.append(Reduce(second, (seq, across)))
            return found, (token,)

        def conv_grads(last, reads=()):
            first, second, token = conv_weight_grad(
                extended_parts, conv_grad, arrived, places, sizes, taps, steps[b], last, reads
            )
            found = [Reduce(first, (seq, across))]
            if second:
                found.append(Reduce(second, (across, seq)))
            return found, (token,)

        if b == 1:
            ffn_sums[1], last = ffn_grads(last)
            extended_grad, last = extend(conv_grad, found_rims, seq, last)
            conv_sums[1], last = conv_grads(last)
        else:
            conv_sums[0], last = conv_grads(last, arrived_packets)
            extended_grad, last = extend(conv_grad, found_rims, seq, last)
            ffn_sums[0], last = ffn_grads(last)
            for each in conv_sums[0]:
                last = each.step(1, last, merged[1][1:])
        if b == 1:
            stream_grad, last = conv_data_grad(
                extended_grad, conv_full[1], stream_grad, steps[1], jnp.float32, last
            )

    row_groups = [(each, 3) for each in conv_rows_of_sums + ffn_rows_of_sums]
    row_groups.append((head_grad, head_weight.shape[1]))
    (conv_input,), last = hold([conv_input], last)
    final_state = from_rows(conv_input, windows)
    packed, last = pack_small(row_groups, in_bias_grads, loss_rows, places, sizes, ffn_rows, last, [final_state])

    conv_rows = taps * slab
    merged[0], last = append_slots(groups(conv_sums[0]), [packed], last)
    merged[0] = tap.swap(merged[0])
    stream_grad, last = conv_data_grad(
        extended_grad, conv_full[0], stream_grad, steps[0], jnp.bfloat16, last
    )
    for each in ffn_sums[0]:
        last = each.step(1, last)
    shards, last = finish_conv([merged[0], merged[1]], conv_rows, packed.shape[0], last)
    ffn_late, last = append_slots(groups(ffn_sums[0]), [], last)
    ffn_late = tap.swap(ffn_late)
    grad_inputs = from_rows(stream_grad, windows)
    copies = [each for row in shared_copies(shards, across, seq) for each in row]
    grad_in, grad_out, last = finish_ffn(merged[1], ffn_late, conv_rows, ffn_rows, last)
    (stack,), last = restack([straight(copies)], after=last)
    stacks = core.gather(stack)
    (
        grad_conv_bias,
        grad_gains,
        grad_shifts,
        grad_in_bias,
        grad_out_bias,
        grad_head_weight,
        loss,
    ) = finish_small(
        stacks, 2 * conv_rows, width, head_weight.shape[1], hidden_width, places, sizes
    )
    grad_conv = place_conv_grads(stacks, 2, taps, slab, places, sizes)
    return (
        final_state,
        grad_inputs,
        grad_conv,
        grad_conv_bias,
        grad_gains,
        grad_shifts,
        grad_in,
        grad_in_bias,
        grad_out,
        grad_out_bias,
        grad_head_weight,
        loss.reshape(()),
    )


def solution(mesh):
    placed = (
        P(("dp", "tap"), "seq", None),
        P(("dp", "tap"), "seq"),
        P(("dp", "tap"), "seq"),
        P(None, None, "tap", None),
        P(),
        P(),
        P(),
        P(None, None, ("dp", "seq", "tap")),
        P(),
        P(None, ("dp", "seq", "tap"), None),
        P(),
        P(),
    )
    return jax.shard_map(
        on_device,
        mesh=mesh,
        in_specs=placed,
        out_specs=(
            P(("dp", "tap"), "seq", None),
            P(("dp", "tap"), "seq", None),
            P(None, None, "tap", None),
            P(),
            P(),
            P(),
            P(None, None, ("dp", "seq", "tap")),
            P(),
            P(None, ("dp", "seq", "tap"), None),
            P(),
            P(),
            P(),
        ),
        check_vma=False,
    )
```

```python
import functools

import jax
import jax.numpy as jnp
import numpy as np
from jax import lax
from jax.experimental import pallas as pl
from jax.experimental.pallas import tpu as pltpu
from jax.sharding import PartitionSpec as P

FIRST_DILATION = 4
SECOND_DILATION = 32
EPSILON = 1e-05
HIGHEST_PRECISION = lax.Precision.HIGHEST
CORES = 2
ROW_TILE = 16
MIB = 1024 * 1024
VMEM_BYTES = 20 * MIB
ANYWHERE = pl.BlockSpec(memory_space=pl.ANY)
SCALARS = pl.BlockSpec(memory_space=pltpu.SMEM)


TOKEN = jax.ShapeDtypeStruct((8, 128), jnp.float32)


def cost(microseconds):
    size = int(microseconds * 3.5e6)
    return pl.CostEstimate(flops=int(microseconds * 1.1e9), bytes_accessed=size, transcendentals=0)


WHOLE = pl.BlockSpec(memory_space=pltpu.VMEM)
TOKEN_SPEC = pl.BlockSpec(TOKEN.shape, lambda *_: (0, 0))


def tokens(after):
    return [TOKEN_SPEC] * len(after)


def in_hbm(array):
    return pltpu.with_memory_space_constraint(array, pltpu.HBM)


def low(values):
    return values.astype(jnp.bfloat16)


def wide(values):
    return values.astype(jnp.float32)


def gelu_parts(values):
    phi = 0.5 * (1.0 + lax.erf(values * 0.7071067811865476))
    return (
        values * phi,
        phi + values * jnp.exp(-0.5 * values * values) * 0.3989422804014327,
    )


def normalize(values):
    center = values - jnp.mean(values, -1, keepdims=True)
    scale = lax.rsqrt(jnp.mean(center * center, -1, keepdims=True) + EPSILON)
    return (center * scale, scale)


def norm_back(upstream, normed, scale):
    return scale * (
        upstream
        - jnp.mean(upstream, -1, keepdims=True)
        - normed * jnp.mean(upstream * normed, -1, keepdims=True)
    )


def tap_groups(taps):
    return 3 if taps % 3 == 0 else 1


def row_chunks(rows, most):
    size = min(rows, most)
    return [(first, size) for first in range(0, rows, size)]


def conv_forward(extended, weight, stream, bias, gain, shift, step, after=(), reads=()):
    taps, inner, width = weight.shape
    rows = stream.shape[0]
    group = tap_groups(taps)
    steps = taps // group

    def kernel(extended_ref, weight_ref, stream_ref, bias_ref, gain_ref, shift_ref, *refs):
        normed_ref, slope_ref, next_ref, lowered_ref, token_ref, total_ref = refs[-6:]
        token_ref[...] = jnp.zeros(TOKEN.shape, TOKEN.dtype)
        first = pl.program_id(0) * group
        total = None
        for j in range(group):
            start = pl.multiple_of((first + j) * step, ROW_TILE)
            term = jnp.dot(
                extended_ref[pl.ds(start, rows), :],
                weight_ref[j],
                preferred_element_type=jnp.float32,
            )
            total = term if total is None else total + term

        @pl.when(pl.program_id(0) == 0)
        def _():
            total_ref[...] = total

        @pl.when(pl.program_id(0) > 0)
        def _():
            total_ref[...] += total

        @pl.when(pl.program_id(0) == steps - 1)
        def _():
            for at, size in row_chunks(rows, 128):
                some = pl.ds(at, size)
                value, slope = gelu_parts(total_ref[some, :] + bias_ref[...])
                normed, scale = normalize(value)
                mid = wide(stream_ref[some, :]) + normed * gain_ref[...] + shift_ref[...]
                normed_ref[some, :] = low(normed)
                slope_ref[some, :] = low(scale * slope)
                next_ref[some, :] = mid
                lowered_ref[some, :] = low(mid)

    whole = pl.BlockSpec((rows, width), lambda g: (0, 0))
    row = pl.BlockSpec((1, width), lambda g: (0, 0))
    found = pl.pallas_call(
        kernel,
        grid=(steps,),
        in_specs=[
            pl.BlockSpec(extended.shape, lambda g: (0, 0)),
            pl.BlockSpec((group, inner, width), lambda g: (g, 0, 0)),
            whole,
            row,
            row,
            row,
        ]
        + tokens(after)
        + [ANYWHERE] * len(reads),
        out_specs=[whole] * 4 + [TOKEN_SPEC],
        out_shape=[
            pltpu.HBM((rows, width), jnp.bfloat16),
            pltpu.HBM((rows, width), jnp.bfloat16),
            pltpu.HBM((rows, width), jnp.float32),
            jax.ShapeDtypeStruct((rows, width), jnp.bfloat16),
            TOKEN,
        ],
        scratch_shapes=[pltpu.VMEM((rows, width), jnp.float32)],
        compiler_params=pltpu.CompilerParams(vmem_limit_bytes=VMEM_BYTES),
        cost_estimate=cost(9),
        name="conv_forward",
    )(extended, in_hbm(weight), in_hbm(stream) if stream.dtype == jnp.float32 else stream, bias[None], gain[None], shift[None], *after, *reads)
    return found[:4], (found[4],)


def ffn_forward(
    lowered,
    stream,
    ins,
    outs,
    in_biases,
    out_bias,
    gain,
    shift,
    seq_index,
    reach,
    last_block,
    after=(),
    reads=(),
):
    rows, width = lowered.shape
    cores = len(ins)
    units = ins[0].shape[0]
    block = min(units, 256)
    steps = units // block

    rims_out = 1 if reach else 0

    def kernel(place_ref, lowered_ref, stream_ref, out_bias_ref, gain_ref, shift_ref, *refs):
        in_refs, out_refs, bias_refs = (refs[i * cores : (i + 1) * cores] for i in range(3))
        found_refs = refs[-6 - 2 * cores - rims_out :]
        active_ref, slope_refs = found_refs[0], found_refs[1 : 1 + cores]
        normed_ref, scale_ref, next_ref, rounded_ref = found_refs[1 + cores : 5 + cores]
        packet_refs = found_refs[5 + cores : 4 + 2 * cores]
        token_ref, total_ref = found_refs[-2:]
        token_ref[...] = jnp.zeros(TOKEN.shape, TOKEN.dtype)
        lane = pl.multiple_of(width + pl.program_id(0) * block, block)

        @pl.when(pl.program_id(0) == 0)
        def _():
            total_ref[...] = jnp.zeros(total_ref.shape, jnp.float32)
            for packet_ref in packet_refs:
                packet_ref[:, :width] = lowered_ref[...]

        for at, size in row_chunks(rows, 512):
            some = pl.ds(at, size)
            term = None
            for c in range(cores):
                hidden = lax.dot_general(
                    lowered_ref[some, :],
                    in_refs[c][...],
                    (((1,), (1,)), ((), ())),
                    preferred_element_type=jnp.float32,
                )
                active, slope = gelu_parts(hidden + bias_refs[c][...])
                active = low(active)
                if c == 0:
                    active_ref[some, :] = active
                else:
                    packet_refs[c - 1][some, pl.ds(lane, block)] = active
                slope_refs[c][some, :] = low(slope)
                found = jnp.dot(active, out_refs[c][...], preferred_element_type=jnp.float32)
                term = found if term is None else term + found
            total_ref[some, :] += term

        @pl.when(pl.program_id(0) == steps - 1)
        def _():
            for at, size in row_chunks(rows, 128):
                some = pl.ds(at, size)
                normed, scale = normalize(total_ref[some, :] + out_bias_ref[...])
                after_ffn = stream_ref[some, :] + normed * gain_ref[...] + shift_ref[...]
                normed_ref[some, :] = low(normed)
                scale_ref[some, :] = jnp.broadcast_to(scale, (size, 128))
                next_ref[some, :] = after_ffn
                rounded_ref[some, :] = low(after_ffn)
            if reach:
                first = pl.multiple_of((1 - place_ref[0]) * (rows - reach), ROW_TILE)
                found_refs[-3][...] = rounded_ref[pl.ds(first, reach), :]

    whole = pl.BlockSpec((rows, width), lambda g: (0, 0))
    row = pl.BlockSpec((1, width), lambda g: (0, 0))
    piece = pl.BlockSpec((block, width), lambda g: (g, 0))
    columns = pl.BlockSpec((rows, block), lambda g: (0, g))
    hidden_shape = pltpu.HBM((rows, units), jnp.bfloat16)
    found = pl.pallas_call(
        kernel,
        grid=(steps,),
        in_specs=[SCALARS, whole, whole, row, row, row]
        + [piece] * (2 * cores)
        + [pl.BlockSpec((1, block), lambda g: (0, g))] * cores
        + tokens(after)
        + [ANYWHERE] * len(reads),
        out_specs=[columns] * (1 + cores)
        + [whole, pl.BlockSpec((rows, 128), lambda g: (0, 0)), whole, whole]
        + [pl.BlockSpec((rows, width + units), lambda g: (0, 0))] * (cores - 1)
        + [pl.BlockSpec((reach, width), lambda g: (0, 0))] * rims_out
        + [TOKEN_SPEC],
        out_shape=[hidden_shape] * (1 + cores)
        + [
            pltpu.HBM((rows, width), jnp.bfloat16),
            pltpu.HBM((rows, 128), jnp.float32),
            (jax.ShapeDtypeStruct if last_block else pltpu.HBM)((rows, width), jnp.float32),
            jax.ShapeDtypeStruct((rows, width), jnp.bfloat16),
        ]
        + [jax.ShapeDtypeStruct((rows, width + units), jnp.bfloat16)] * (cores - 1)
        + [jax.ShapeDtypeStruct((reach, width), jnp.bfloat16)] * rims_out
        + [TOKEN],
        scratch_shapes=[pltpu.VMEM((rows, width), jnp.float32)],
        compiler_params=pltpu.CompilerParams(vmem_limit_bytes=VMEM_BYTES),
        cost_estimate=cost(11),
        name="ffn_forward",
    )(
        seq_index.astype(jnp.int32)[None],
        lowered,
        in_hbm(stream),
        out_bias[None],
        gain[None],
        shift[None],
        *[in_hbm(each) for each in ins],
        *[in_hbm(each) for each in outs],
        *[each[None] for each in in_biases],
        *after,
        *reads,
    )
    return (
        found[0],
        found[1 : 1 + cores],
        found[1 + cores : 5 + cores],
        found[5 + cores : 4 + 2 * cores],
        found[4 + 2 * cores] if reach else None,
        (found[-1],),
    )


def head_and_loss(stream, head_weight, codes, after=()):
    rows, width = stream.shape
    classes = head_weight.shape[1]
    padded = jnp.pad(head_weight, ((0, 0), (0, 128 - classes)))
    cuts = row_chunks(rows, 256)

    def kernel(stream_ref, head_ref, code_ref, *refs):
        grad_ref, head_grad_ref, sums_ref, token_ref = refs[-4:]
        token_ref[...] = jnp.zeros(TOKEN.shape, TOKEN.dtype)
        head_grad = jnp.zeros((128, width), jnp.float32)
        objective = jnp.zeros((1, 1), jnp.float32)
        scored = jnp.zeros((1, 1), jnp.float32)
        for at, size in cuts:
            some = pl.ds(at, size)
            value = stream_ref[some, :]
            code = code_ref[some, :]
            mask = jnp.where(code[:, :1] >= classes, 1.0, 0.0)
            logits = jnp.dot(
                value, head_ref[...], precision=HIGHEST_PRECISION, preferred_element_type=jnp.float32
            )
            lane = lax.broadcasted_iota(jnp.int32, logits.shape, 1)
            valid = lane < classes
            peak = jnp.max(jnp.where(valid, logits, -jnp.inf), -1, keepdims=True)
            exponent = jnp.where(valid, jnp.exp(jnp.where(valid, logits - peak, 0.0)), 0.0)
            denominator = jnp.sum(exponent, -1, keepdims=True)
            chosen = lane == jnp.where(code >= classes, code - classes, code)
            picked = jnp.sum(jnp.where(chosen, logits, 0.0), -1, keepdims=True)
            terms = mask * (peak + jnp.log(denominator) - picked)
            objective = objective + jnp.sum(terms, 0, keepdims=True)
            scored = scored + jnp.sum(mask, 0, keepdims=True)
            logit_grad = mask * (exponent / denominator - jnp.where(chosen, 1.0, 0.0))
            grad_ref[some, :] = lax.dot_general(
                logit_grad,
                head_ref[...],
                (((1,), (1,)), ((), ())),
                precision=HIGHEST_PRECISION,
                preferred_element_type=jnp.float32,
            )
            head_grad = head_grad + lax.dot_general(
                logit_grad,
                value,
                (((0,), (0,)), ((), ())),
                precision=HIGHEST_PRECISION,
                preferred_element_type=jnp.float32,
            )
        head_grad_ref[...] = head_grad[: head_grad_ref.shape[0]]
        at_row = lax.broadcasted_iota(jnp.int32, sums_ref.shape, 0)
        sums_ref[...] = jnp.where(at_row == 0, objective, scored)

    found = pl.pallas_call(
        kernel,
        out_shape=[
            jax.ShapeDtypeStruct((rows, width), jnp.float32),
            jax.ShapeDtypeStruct((-(-classes // 8) * 8, width), jnp.float32),
            jax.ShapeDtypeStruct((8, 128), jnp.float32),
            TOKEN,
        ],
        compiler_params=pltpu.CompilerParams(vmem_limit_bytes=VMEM_BYTES),
        cost_estimate=cost(6),
        name="head_and_loss",
    )(stream, padded, codes, *after)
    return found[:3], (found[3],)


def ffn_back_hidden(upstream, normed, scale, gain, outs, slopes, after=()):
    rows, width = upstream.shape
    cores = len(outs)
    units = outs[0].shape[0]
    block = min(units, 256)

    def kernel(upstream_ref, normed_ref, scale_ref, gain_ref, *refs):
        out_refs, slope_refs = refs[:cores], refs[cores : 2 * cores]
        found_refs = refs[-3 - 2 * cores :]
        output_grad_ref, hidden_ref = found_refs[:2]
        bias_refs, packet_refs = found_refs[2 : 2 + cores], found_refs[2 + cores : -2]
        sums_ref, token_ref = found_refs[-2:]
        token_ref[...] = jnp.zeros(TOKEN.shape, TOKEN.dtype)
        lane = pl.multiple_of(width + pl.program_id(0) * block, block)

        @pl.when(pl.program_id(0) == 0)
        def _():
            totals = [jnp.zeros((1, width), jnp.float32)] * 3
            for at, size in row_chunks(rows, 128):
                some = pl.ds(at, size)
                grad, value = upstream_ref[some, :], wide(normed_ref[some, :])
                output_grad = low(norm_back(grad * gain_ref[...], value, scale_ref[some, :1]))
                output_grad_ref[some, :] = output_grad
                for packet_ref in packet_refs:
                    packet_ref[some, :width] = output_grad
                for i, each in enumerate((grad * value, grad, wide(output_grad))):
                    totals[i] = totals[i] + jnp.sum(each, 0, keepdims=True)
            sums_ref[...] = jnp.zeros(sums_ref.shape, jnp.float32)
            for i in range(3):
                sums_ref[i : i + 1, :] = totals[i]

        for c in range(cores):
            total = jnp.zeros((1, block), jnp.float32)
            for at, size in row_chunks(rows, 512):
                some = pl.ds(at, size)
                active_grad = lax.dot_general(
                    output_grad_ref[some, :],
                    out_refs[c][...],
                    (((1,), (1,)), ((), ())),
                    preferred_element_type=jnp.float32,
                )
                hidden_grad = low(active_grad * wide(slope_refs[c][some, :]))
                if c == 0:
                    hidden_ref[some, :] = hidden_grad
                else:
                    packet_refs[c - 1][some, pl.ds(lane, block)] = hidden_grad
                total = total + jnp.sum(wide(hidden_grad), 0, keepdims=True)
            bias_refs[c][...] = total

    whole = pl.BlockSpec((rows, width), lambda g: (0, 0))
    columns = pl.BlockSpec((rows, block), lambda g: (0, g))
    found = pl.pallas_call(
        kernel,
        grid=(units // block,),
        in_specs=[
            whole,
            whole,
            pl.BlockSpec((rows, 128), lambda g: (0, 0)),
            pl.BlockSpec((1, width), lambda g: (0, 0)),
        ]
        + [pl.BlockSpec((block, width), lambda g: (g, 0))] * cores
        + [columns] * cores
        + tokens(after),
        out_specs=[whole, columns]
        + [pl.BlockSpec((1, block), lambda g: (0, g))] * cores
        + [pl.BlockSpec((rows, width + units), lambda g: (0, 0))] * (cores - 1)
        + [pl.BlockSpec((8, width), lambda g: (0, 0)), TOKEN_SPEC],
        out_shape=[
            jax.ShapeDtypeStruct((rows, width), jnp.bfloat16),
            pltpu.HBM((rows, units), jnp.bfloat16),
        ]
        + [jax.ShapeDtypeStruct((1, units), jnp.float32)] * cores
        + [jax.ShapeDtypeStruct((rows, width + units), jnp.bfloat16)] * (cores - 1)
        + [jax.ShapeDtypeStruct((8, width), jnp.float32), TOKEN],
        compiler_params=pltpu.CompilerParams(vmem_limit_bytes=VMEM_BYTES),
        cost_estimate=cost(6),
        name="ffn_back_hidden",
    )(
        upstream,
        in_hbm(normed),
        in_hbm(scale),
        gain[None],
        *[in_hbm(each) for each in outs],
        *[in_hbm(each) for each in slopes],
        *after,
    )
    return (
        found[0],
        found[1],
        found[2 : 2 + cores],
        found[2 + cores : -2],
        found[-2],
        (found[-1],),
    )


def ffn_back_stream(
    upstream, hidden, packets, ins, normed, slope, gain, places, reach, after=(), reads=(), relay=False
):
    rows, width = upstream.shape
    cores = len(ins)
    units = ins[0].shape[0]
    block = min(units, 256)
    steps = units // block
    lanes = width // cores
    relays = cores - 1 if relay else 0
    rims_out = 1 if reach else 0

    def kernel(core_ref, upstream_ref, normed_ref, slope_ref, gain_ref, *refs):
        hidden_refs, in_refs = refs[:cores], refs[cores : 2 * cores]
        found_refs = refs[-4 - cores - relays - rims_out :]
        mid_ref, conv_grad_ref = found_refs[:2]
        cut_refs = found_refs[2 : 1 + cores]
        sums_ref, token_ref, total_ref = found_refs[-3:]
        token_ref[...] = jnp.zeros(TOKEN.shape, TOKEN.dtype)
        for i in range(relays):
            relay_ref = found_refs[1 + cores + i]
            lane = pl.multiple_of(width + pl.program_id(0) * block, block)
            relay_ref[:, pl.ds(lane, block)] = hidden_refs[1 + i][...]

            @pl.when(pl.program_id(0) == 0)
            def _(i=i, relay_ref=relay_ref):
                relay_ref[:, :width] = refs[2 * cores + i][...]

        @pl.when(pl.program_id(0) == 0)
        def _():
            total_ref[...] = upstream_ref[...]

        for at, size in row_chunks(rows, 512):
            some = pl.ds(at, size)
            total_ref[some, :] += sum(
                jnp.dot(
                    hidden_refs[c][some, :], in_refs[c][...], preferred_element_type=jnp.float32
                )
                for c in range(cores)
            )

        @pl.when(pl.program_id(0) == steps - 1)
        def _():
            totals = [jnp.zeros((1, width), jnp.float32)] * 3
            for at, size in row_chunks(rows, 128):
                some = pl.ds(at, size)
                grad, value = total_ref[some, :], wide(normed_ref[some, :])
                conv_grad = low(norm_back(grad * gain_ref[...], value, wide(slope_ref[some, :])))
                mid_ref[some, :] = grad
                conv_grad_ref[some, :] = conv_grad
                for i, each in enumerate((grad * value, grad, wide(conv_grad))):
                    totals[i] = totals[i] + jnp.sum(each, 0, keepdims=True)
            sums_ref[...] = jnp.zeros(sums_ref.shape, jnp.float32)
            for i in range(3):
                sums_ref[i : i + 1, :] = totals[i]
            for c in range(1, cores):
                first = lax.rem(core_ref[0] - c + cores, cores) * lanes
                cut_refs[c - 1][...] = conv_grad_ref[:, pl.ds(pl.multiple_of(first, lanes), lanes)]
            if reach:
                first = pl.multiple_of((1 - core_ref[1]) * (rows - reach), ROW_TILE)
                found_refs[-4][...] = conv_grad_ref[pl.ds(first, reach), :]

    whole = pl.BlockSpec((rows, width), lambda g, core: (0, 0))
    found = pl.pallas_call(
        kernel,
        grid_spec=pltpu.PrefetchScalarGridSpec(
            num_scalar_prefetch=1,
            grid=(steps,),
            in_specs=[whole, whole, whole, pl.BlockSpec((1, width), lambda g, core: (0, 0))]
            + [pl.BlockSpec((rows, block), lambda g, core: (0, g))]
            + [pl.BlockSpec((rows, block), lambda g, core: (0, width // block + g))] * (cores - 1)
            + [pl.BlockSpec((block, width), lambda g, core: (g, 0))] * cores
            + [whole] * relays
            + tokens(after)
            + [ANYWHERE] * len(reads),
            out_specs=[whole, whole]
            + [pl.BlockSpec((rows, lanes), lambda g, core: (0, 0))] * (cores - 1)
            + [pl.BlockSpec((rows, width + units), lambda g, core: (0, 0))] * relays
            + [pl.BlockSpec((reach, width), lambda g, core: (0, 0))] * rims_out
            + [pl.BlockSpec((8, width), lambda g, core: (0, 0)), TOKEN_SPEC],
            scratch_shapes=[pltpu.VMEM((rows, width), jnp.float32)],
        ),
        out_shape=[
            jax.ShapeDtypeStruct((rows, width), jnp.float32),
            jax.ShapeDtypeStruct((rows, width), jnp.bfloat16),
        ]
        + [jax.ShapeDtypeStruct((rows, lanes), jnp.bfloat16)] * (cores - 1)
        + [jax.ShapeDtypeStruct((rows, width + units), jnp.bfloat16)] * relays
        + [jax.ShapeDtypeStruct((reach, width), jnp.bfloat16)] * rims_out
        + [jax.ShapeDtypeStruct((8, width), jnp.float32), TOKEN],
        compiler_params=pltpu.CompilerParams(vmem_limit_bytes=VMEM_BYTES),
        cost_estimate=cost(5),
        name="ffn_back_stream",
    )(
        jnp.stack(places[:2]).astype(jnp.int32),
        upstream,
        in_hbm(normed),
        in_hbm(slope),
        gain[None],
        in_hbm(hidden),
        *packets,
        *[in_hbm(each) for each in ins],
        *packets[:relays],
        *after,
        *reads,
    )
    return (
        found[0],
        found[1],
        found[2 : 1 + cores],
        found[1 + cores : 1 + cores + relays],
        found[1 + cores + relays] if reach else None,
        found[-2],
        (found[-1],),
    )


def conv_data_grad(extended, weight, upstream, step, kind, after=()):
    taps, inner, width = weight.shape
    rows = upstream.shape[0]
    group = tap_groups(taps)
    steps = taps // group

    def kernel(extended_ref, weight_ref, upstream_ref, *refs):
        out_ref, token_ref, total_ref = refs[-3:]
        token_ref[...] = jnp.zeros(TOKEN.shape, TOKEN.dtype)
        first = pl.program_id(0) * group
        total = None
        for j in range(group):
            start = pl.multiple_of((taps - 1 - first - j) * step, ROW_TILE)
            term = lax.dot_general(
                extended_ref[pl.ds(start, rows), :],
                weight_ref[j],
                (((1,), (1,)), ((), ())),
                preferred_element_type=jnp.float32,
            )
            total = term if total is None else total + term

        @pl.when(pl.program_id(0) == 0)
        def _():
            total_ref[...] = total

        @pl.when(pl.program_id(0) > 0)
        def _():
            total_ref[...] += total

        @pl.when(pl.program_id(0) == steps - 1)
        def _():
            out_ref[...] = (upstream_ref[...] + wide(low(total_ref[...]))).astype(kind)

    whole = pl.BlockSpec((rows, inner), lambda g: (0, 0))
    found = pl.pallas_call(
        kernel,
        grid=(steps,),
        in_specs=[
            pl.BlockSpec(extended.shape, lambda g: (0, 0)),
            pl.BlockSpec((group, inner, width), lambda g: (g, 0, 0)),
            whole,
        ]
        + tokens(after),
        out_specs=(whole, TOKEN_SPEC),
        out_shape=(jax.ShapeDtypeStruct((rows, inner), kind), TOKEN),
        scratch_shapes=[pltpu.VMEM((rows, inner), jnp.float32)],
        compiler_params=pltpu.CompilerParams(vmem_limit_bytes=VMEM_BYTES),
        cost_estimate=cost(6),
        name="conv_data_grad",
    )(extended, in_hbm(weight), upstream, *after)
    return found[0], (found[1],)


def hold(arrays, after, reads=()):
    count = len(arrays)
    if count == 0:
        return [], after

    def kernel(*refs):
        refs[-1][...] = jnp.zeros(TOKEN.shape, TOKEN.dtype)

    found = pl.pallas_call(
        kernel,
        in_specs=[ANYWHERE] * (count + len(reads)) + [WHOLE] * len(after),
        out_specs=[ANYWHERE] * count + [WHOLE],
        out_shape=[jax.ShapeDtypeStruct(each.shape, each.dtype) for each in arrays] + [TOKEN],
        input_output_aliases={i: i for i in range(count)},
        compiler_params=pltpu.CompilerParams(vmem_limit_bytes=1 * MIB),
        cost_estimate=cost(0.5),
        name="hold",
    )(*arrays, *reads, *after)
    return list(found[:-1]), (found[-1],)


def join_rows(parts, after=(), reads=()):
    def kernel(*refs):
        out_ref, token_ref = refs[-2:]
        token_ref[...] = jnp.zeros(TOKEN.shape, TOKEN.dtype)
        first = 0
        for i, part in enumerate(parts):
            out_ref[first : first + part.shape[0]] = refs[i][...]
            first += part.shape[0]

    shape = (sum(part.shape[0] for part in parts), parts[0].shape[1])
    found = pl.pallas_call(
        kernel,
        in_specs=[WHOLE] * len(parts) + [ANYWHERE] * len(reads) + [WHOLE] * len(after),
        out_specs=[WHOLE] * 2,
        out_shape=[jax.ShapeDtypeStruct(shape, parts[0].dtype), TOKEN],
        compiler_params=pltpu.CompilerParams(vmem_limit_bytes=10 * MIB),
        cost_estimate=cost(1.5),
        name="join_rows",
    )(*parts, *reads, *after)
    return found[0], (found[1],)


def restack(groups, reads=(), after=(), fixed=False):
    cuts = [cut for _, each in groups for cut in each]
    if any(last is not None and (first % ROW_TILE or last % ROW_TILE) for first, last, _ in cuts):
        return [
            jnp.stack([array[first:last].reshape(shape) for array in arrays])
            for arrays, each in groups
            for first, last, shape in each
        ], after
    flat = [array for arrays, _ in groups for array in arrays]
    plan = []
    shapes = []
    at = 0
    for arrays, each in groups:
        for first, last, shape in each:
            for slot in range(len(arrays)):
                plan.append((at + slot, first, last, len(shapes), slot))
            held = shape if last is None else (last - first,) + arrays[0].shape[1:]
            shapes.append(jax.ShapeDtypeStruct((len(arrays),) + held, arrays[0].dtype))
        at += len(arrays)

    def kernel(*refs):
        out_refs = refs[-2 - len(shapes) : -2]
        token_ref, sem_ref = refs[-2:]
        token_ref[...] = jnp.zeros(TOKEN.shape, TOKEN.dtype)
        copies = []
        for source, first, last, target, slot in plan:
            ref = refs[source]
            copies.append(
                pltpu.make_async_copy(
                    ref if last is None else ref.at[pl.ds(first, last - first)],
                    out_refs[target].at[slot],
                    sem_ref.at[len(copies)],
                )
            )
        copy_all(copies)

    found = pl.pallas_call(
        kernel,
        in_specs=[ANYWHERE] * (len(flat) + len(reads)) + [WHOLE] * len(after),
        out_specs=[WHOLE] * (len(shapes) + 1),
        out_shape=shapes + [TOKEN],
        scratch_shapes=[pltpu.SemaphoreType.DMA((len(plan),))],
        compiler_params=pltpu.CompilerParams(vmem_limit_bytes=10 * MIB),
        cost_estimate=cost(1.5),
        name="restack",
    )(*([in_hbm(each) for each in flat] if fixed else flat), *reads, *after)
    return [
        each.reshape((each.shape[0],) + shape) for each, (_, _, shape) in zip(found, cuts)
    ], (found[-1],)


def conv_weight_grad(
    extendeds, upstream, arrived, places, sizes, taps, step, after=(), reads=()
):
    cores, seqs, acrosses, tap_peers = sizes
    rows = upstream.shape[0]
    inner = extendeds[0].shape[1]
    lanes = upstream.shape[1] // cores
    slab = inner // (seqs * acrosses * tap_peers)
    direct = slab % ROW_TILE == 0
    half = (tap_peers + 1) // 2
    rest = tap_peers - half
    seconds = acrosses if rest else 0
    outs = seqs + seconds if direct else 1

    def kernel(place_ref, *refs):
        out_refs = refs[-2 - outs : -2]
        token_ref, found_ref = refs[-2:]
        token_ref[...] = jnp.zeros(TOKEN.shape, TOKEN.dtype)
        start = pl.multiple_of(pl.program_id(0) * step, ROW_TILE)
        found = low(
            sum(
                lax.dot_general(
                    refs[c][pl.ds(start, rows), :],
                    refs[cores + c][...],
                    (((0,), (0,)), ((), ())),
                    preferred_element_type=jnp.float32,
                )
                for c in range(cores)
            )
        )
        if not direct:
            out_refs[0][0] = found
            return
        found_ref[...] = found

        def chunk(slot_t, slot_s, slot_a):
            t = lax.rem(place_ref[3] - slot_t + tap_peers, tap_peers)
            at = lax.rem(place_ref[1] - slot_s + seqs, seqs)
            a = lax.rem(place_ref[2] - slot_a + acrosses, acrosses)
            first = pl.multiple_of(((t * seqs + at) * acrosses + a) * slab, slab)
            return found_ref[pl.ds(first, slab), :]

        for s in range(seqs):
            for a in range(acrosses):
                for t in range(half):
                    out_refs[s][a, t, 0] = chunk(t, s, a)
                for t in range(half, tap_peers):
                    out_refs[seqs + a][s, t - half, 0] = chunk(t, s, a)

    if direct:
        shapes = [(acrosses, half, taps, slab, lanes)] * seqs
        shapes += [(seqs, rest, taps, slab, lanes)] * seconds
        specs = [
            pl.BlockSpec(shape[:2] + (1, slab, lanes), lambda k, place: (0, 0, k, 0, 0))
            for shape in shapes
        ]
    else:
        shapes = [(taps, inner, lanes)]
        specs = [pl.BlockSpec((1, inner, lanes), lambda k, place: (k, 0, 0))]
    found = pl.pallas_call(
        kernel,
        grid_spec=pltpu.PrefetchScalarGridSpec(
            num_scalar_prefetch=1,
            grid=(taps,),
            in_specs=[pl.BlockSpec(extendeds[0].shape, lambda k, place: (0, 0))] * cores
            + [pl.BlockSpec((rows, lanes), lambda k, place: (0, place[0]))]
            + [pl.BlockSpec((rows, lanes), lambda k, place: (0, 0))] * (cores - 1)
            + tokens(after)
            + [ANYWHERE] * len(reads),
            out_specs=specs + [TOKEN_SPEC],
            scratch_shapes=[pltpu.VMEM((inner, lanes), jnp.bfloat16)],
        ),
        out_shape=[jax.ShapeDtypeStruct(shape, jnp.bfloat16) for shape in shapes] + [TOKEN],
        compiler_params=pltpu.CompilerParams(vmem_limit_bytes=VMEM_BYTES),
        cost_estimate=cost(9),
        name="conv_weight_grad",
    )(jnp.stack(places).astype(jnp.int32), *extendeds, upstream, *arrived, *after, *reads)
    token = found[-1]
    if not direct:
        found = found[0].reshape(taps, tap_peers, seqs, acrosses, slab, lanes)
        for axis, which in ((1, 3), (2, 1), (3, 2)):
            found = relative(found, axis, places[which], sizes[which])
        found = found.transpose(2, 3, 1, 0, 4, 5)
        found = [found[s, :, :half] for s in range(seqs)] + [
            found[:, a, half:] for a in range(seconds)
        ]
    flat = [each.reshape(-1, lanes) for each in found[: seqs + seconds]]
    return flat[:seqs], flat[seqs:], token


def ffn_weight_grad(pairs, sizes, ffn_rows, after=()):
    cores, seqs, acrosses, tap_peers = sizes
    rows, width = pairs[0][1].shape
    block = tap_peers * ffn_rows
    half = (tap_peers + 1) // 2
    rest = tap_peers - half
    seconds = seqs if rest else 0
    transposed = (((0,), (0,)), ((), ()))
    if ffn_rows % ROW_TILE:
        found = jnp.stack(
            [
                low(
                    sum(
                        lax.dot_general(a, b, transposed, preferred_element_type=jnp.float32)
                        for a, b in [(left, right)]
                        + [(ends[:, width:], starts[:, :width]) for ends, starts in packets]
                    )
                ).reshape(acrosses, seqs, tap_peers, ffn_rows, width)
                for left, right, packets in pairs
            ],
            3,
        )
        token = jnp.zeros(TOKEN.shape, TOKEN.dtype)
        return (
            [found[a, :, :half].reshape(-1, width) for a in range(acrosses)],
            [found[:, s, half:].reshape(-1, width) for s in range(seconds)],
            token,
        )
    outs = acrosses + seconds

    def kernel(*refs):
        out_refs, token_ref = refs[-1 - outs : -1], refs[-1]
        token_ref[...] = jnp.zeros(TOKEN.shape, TOKEN.dtype)
        step = pl.program_id(0)
        for which in range(2):
            base = 2 * cores * which
            found = low(
                sum(
                    lax.dot_general(
                        refs[base + 2 * c][...],
                        refs[base + 2 * c + 1][...],
                        transposed,
                        preferred_element_type=jnp.float32,
                    )
                    for c in range(cores)
                )
            ).reshape(tap_peers, ffn_rows, width)
            for a in range(acrosses):

                @pl.when(step // seqs == a)
                def _(a=a):
                    out_refs[a][0, :, which] = found[:half]

            for s in range(seconds):

                @pl.when(lax.rem(step, seqs) == s)
                def _(s=s):
                    out_refs[acrosses + s][0, :, which] = found[half:]

    right_spec = pl.BlockSpec((rows, width), lambda g: (0, 0))
    left_spec = pl.BlockSpec((rows, block), lambda g: (0, g))
    late_spec = pl.BlockSpec((rows, block), lambda g: (0, width // block + g))

    def first_spec(a):
        return pl.BlockSpec(
            (1, half, 2, ffn_rows, width),
            lambda g: (jnp.clip(g - a * seqs, 0, seqs - 1), 0, 0, 0, 0),
        )

    second_spec = pl.BlockSpec(
        (1, rest, 2, ffn_rows, width), lambda g: (g // seqs, 0, 0, 0, 0)
    )
    operands = []
    for left, right, packets in pairs:
        operands += [in_hbm(left), right]
        for ends, starts in packets:
            operands += [ends, starts]
    found = pl.pallas_call(
        kernel,
        grid=(acrosses * seqs,),
        in_specs=([left_spec, right_spec] + [late_spec, right_spec] * (cores - 1)) * 2
        + tokens(after),
        out_specs=[first_spec(a) for a in range(acrosses)]
        + [second_spec] * seconds
        + [TOKEN_SPEC],
        out_shape=[jax.ShapeDtypeStruct((seqs, half, 2, ffn_rows, width), jnp.bfloat16)] * acrosses
        + [jax.ShapeDtypeStruct((acrosses, rest, 2, ffn_rows, width), jnp.bfloat16)] * seconds
        + [TOKEN],
        compiler_params=pltpu.CompilerParams(vmem_limit_bytes=VMEM_BYTES),
        cost_estimate=cost(8),
        name="ffn_weight_grad",
    )(*operands, *after)
    flat = [each.reshape(-1, width) for each in found[:-1]]
    return flat[:acrosses], flat[acrosses:], found[-1]


def group_slots(groups, lanes):
    flat, where = [], []
    rows = groups[0][0][0].size // (groups[0][1] * lanes)
    for parts, slots in groups:
        where += [(len(flat), len(parts), slot) for slot in range(slots)]
        flat += [part.reshape(slots, rows, lanes) for part in parts]
    return flat, where, rows


def slot_sum(refs, place, first=0):
    start, count, at = place
    return low(sum(wide(refs[first + start + i][at]) for i in range(count)))


def merge_slots(conv_groups, ffn_groups, after=()):
    lanes, width = conv_groups[0][0][0].shape[-1], ffn_groups[0][0][0].shape[-1]
    cuts = width // lanes
    conv_parts, conv_where, conv_rows = group_slots(conv_groups, lanes)
    ffn_parts, ffn_where, ffn_rows = group_slots(ffn_groups, width)
    slots = len(conv_where)
    if conv_rows % ROW_TILE or ffn_rows % ROW_TILE:
        merged = []
        for slot in range(slots):
            ffn = slot_sum(ffn_parts, ffn_where[slot])
            merged.append(
                jnp.concatenate(
                    [slot_sum(conv_parts, conv_where[slot])]
                    + [ffn[:, i * lanes : (i + 1) * lanes] for i in range(cuts)]
                )
            )
        return merged, after

    def kernel(*refs):
        out_refs, token_ref = refs[-1 - slots : -1], refs[-1]
        token_ref[...] = jnp.zeros(TOKEN.shape, TOKEN.dtype)
        for slot in range(slots):
            out_refs[slot][:conv_rows] = slot_sum(refs, conv_where[slot])
            ffn = slot_sum(refs, ffn_where[slot], len(conv_parts))
            for i in range(cuts):
                first = conv_rows + i * ffn_rows
                out_refs[slot][first : first + ffn_rows] = ffn[:, i * lanes : (i + 1) * lanes]

    found = pl.pallas_call(
        kernel,
        in_specs=[WHOLE] * (len(conv_parts) + len(ffn_parts) + len(after)),
        out_specs=[WHOLE] * (slots + 1),
        out_shape=[jax.ShapeDtypeStruct((conv_rows + cuts * ffn_rows, lanes), jnp.bfloat16)] * slots
        + [TOKEN],
        compiler_params=pltpu.CompilerParams(vmem_limit_bytes=10 * MIB),
        cost_estimate=cost(1.5),
        name="merge_slots",
    )(*conv_parts, *ffn_parts, *after)
    return found[:slots], (found[slots],)


def append_slots(groups, packed, after=(), reads=()):
    lanes = groups[0][0][0].shape[-1]
    parts, where, rows = group_slots(groups, lanes)
    slots = len(where)
    if rows % ROW_TILE:
        return [
            jnp.concatenate([slot_sum(parts, where[slot])] + packed) for slot in range(slots)
        ], after

    def kernel(*refs):
        out_refs, token_ref = refs[-1 - slots : -1], refs[-1]
        token_ref[...] = jnp.zeros(TOKEN.shape, TOKEN.dtype)
        for slot in range(slots):
            out_refs[slot][:rows] = slot_sum(refs, where[slot])
            if packed:
                out_refs[slot][rows:] = refs[len(parts)][...]

    shape = jax.ShapeDtypeStruct((rows + sum(each.shape[0] for each in packed), lanes), jnp.bfloat16)
    found = pl.pallas_call(
        kernel,
        in_specs=[WHOLE] * (len(packed) + len(parts) + len(after)) + [ANYWHERE] * len(reads),
        out_specs=[WHOLE] * (slots + 1),
        out_shape=[shape] * slots + [TOKEN],
        compiler_params=pltpu.CompilerParams(vmem_limit_bytes=8 * MIB),
        cost_estimate=cost(1),
        name="append_slots",
    )(*parts, *packed, *after, *reads)
    return found[:slots], (found[slots],)


def pack_small(row_groups, biases, losses, places, sizes, ffn_rows, after=(), reads=()):
    cores, seqs, acrosses, tap_peers = sizes
    width = row_groups[0][0].shape[1]
    head_rows = sum(count for _, count in row_groups)
    hidden = cores * biases[0][0].shape[1]
    bias_rows = hidden // width
    used = head_rows + len(biases) * bias_rows + 2
    rows = -(-used // ROW_TILE) * ROW_TILE
    lanes = width // 2
    per_row = width // ffn_rows
    if ffn_rows % 64:
        terms = jnp.stack([losses[0, 0], losses[1, 0]])
        terms = jnp.stack([terms, terms - wide(low(terms))])
        pieces = [array[:count] for array, count in row_groups]
        for each in biases:
            bias = jnp.stack(each).reshape(cores, acrosses, seqs, tap_peers, ffn_rows)
            for axis, which in enumerate((0, 2, 1, 3)):
                bias = relative(bias, axis, places[which], sizes[which])
            pieces.append(bias.transpose(1, 0, 2, 3, 4).reshape(-1, width))
        pieces.append(jnp.pad(terms, ((0, rows - used), (0, width - 2))))
        packed = low(jnp.concatenate(pieces))
        return jnp.concatenate([packed[:, :lanes], packed[:, lanes:]]), after

    def kernel(place_ref, *refs):
        packed_ref, token_ref, rows_ref = refs[-3:]
        token_ref[...] = jnp.zeros(TOKEN.shape, TOKEN.dtype)
        rows_ref[...] = jnp.zeros(rows_ref.shape, jnp.float32)
        at = 0
        for i, (_, count) in enumerate(row_groups):
            rows_ref[at : at + count, :] = refs[i][:count, :]
            at += count
        shape = (cores, acrosses, seqs, tap_peers)
        owners = (0, 2, 1, 3)
        for b in range(len(biases)):
            blocks = {}
            for slot in np.ndindex(*shape):
                first = ((slot[1] * seqs + slot[2]) * tap_peers + slot[3]) * ffn_rows
                ref = refs[len(row_groups) + b * cores + slot[0]]
                blocks[slot] = ref[:, first : first + ffn_rows]
            for axis, size in enumerate(shape):
                turned = {}
                for slot in blocks:
                    place = lax.rem(place_ref[owners[axis]] - slot[axis] + size, size)
                    value = blocks[slot[:axis] + (0,) + slot[axis + 1 :]]
                    for other in range(1, size):
                        candidate = blocks[slot[:axis] + (other,) + slot[axis + 1 :]]
                        value = jnp.where(place == other, candidate, value)
                    turned[slot] = value
                blocks = turned
            ordered = [
                blocks[(c, a, s, t)]
                for a in range(acrosses)
                for c in range(cores)
                for s in range(seqs)
                for t in range(tap_peers)
            ]
            for row in range(bias_rows):
                line = ordered[row * per_row : (row + 1) * per_row]
                rows_ref[at : at + 1, :] = jnp.concatenate(line, 1)
                at += 1
        losses_ref = refs[len(row_groups) + len(biases) * cores]
        lane = lax.broadcasted_iota(jnp.int32, (1, width), 1)
        objective = jnp.broadcast_to(losses_ref[0:1, 0:1], (1, width))
        scored = jnp.broadcast_to(losses_ref[1:2, 0:1], (1, width))
        line = jnp.where(lane == 0, objective, jnp.where(lane == 1, scored, 0.0))
        rows_ref[at : at + 1, :] = line
        rows_ref[at + 1 : at + 2, :] = line - wide(low(line))
        packed_ref[:rows, :] = low(rows_ref[:, :lanes])
        packed_ref[rows:, :] = low(rows_ref[:, lanes:])

    flat = [array for array, _ in row_groups] + [each for some in biases for each in some]
    found = pl.pallas_call(
        kernel,
        in_specs=[SCALARS] + [WHOLE] * (len(flat) + 1 + len(after)) + [ANYWHERE] * len(reads),
        out_specs=[WHOLE] * 2,
        out_shape=[jax.ShapeDtypeStruct((2 * rows, lanes), jnp.bfloat16), TOKEN],
        scratch_shapes=[pltpu.VMEM((rows, width), jnp.float32)],
        compiler_params=pltpu.CompilerParams(vmem_limit_bytes=8 * MIB),
        cost_estimate=cost(2),
        name="pack_small",
    )(jnp.stack(places).astype(jnp.int32), *flat, losses, *after, *reads)
    return found[0], (found[1],)


def paired(values):
    while len(values) > 1:
        half = len(values) // 2
        if len(values) % 2:
            return sum(values[1:], values[0])
        values = [values[i] + values[i + half] for i in range(half)]
    return values[0]


def finish_small(stacks, first, width, classes, hidden, places, sizes):
    cores, seqs, acrosses = sizes[:3]
    peers, rows, lanes = stacks[0].shape
    count = rows - first
    bias_rows = hidden // width
    at_bias = 12 + classes
    at_loss = at_bias + 2 * bias_rows

    def pick(row):
        return (
            [row(2), row(5)],
            [[row(0), row(6)], [row(3), row(9)]],
            [[row(1), row(7)], [row(4), row(10)]],
            [[row(at_bias + b * bias_rows + i) for i in range(bias_rows)] for b in range(2)],
            [row(8), row(11)],
        )

    if max(cores, seqs, acrosses) > 2 or first % count or count % ROW_TILE:
        full = jnp.stack(
            [wide(each[:, first:]).reshape(seqs, acrosses, count, lanes) for each in stacks]
        )
        for axis, (place, size) in enumerate(zip(places[:3], sizes[:3])):
            full = relative(full, axis, place, size)
        total = jnp.sum(full, (0, 1, 2))
        total = jnp.concatenate([total[: count // 2], total[count // 2 :]], 1)
        conv_bias, gains, shifts, in_bias, out_bias = pick(lambda i: total[i])
        terms = total[at_loss] + total[at_loss + 1]
        return (
            jnp.stack(conv_bias),
            jnp.stack([jnp.stack(each) for each in gains]),
            jnp.stack([jnp.stack(each) for each in shifts]),
            jnp.stack([jnp.concatenate(each) for each in in_bias]),
            jnp.stack(out_bias),
            total[12:at_bias].T,
            (terms[0] / terms[1]).reshape(1, 1),
        )

    def kernel(*refs):
        conv_ref, gain_ref, shift_ref, in_ref, out_ref, head_ref, loss_ref, rows_ref = refs[cores:]
        total = paired(
            [
                paired(
                    [
                        paired([wide(refs[c][s * acrosses + a]) for a in range(acrosses)])
                        for s in range(seqs)
                    ]
                )
                for c in range(cores)
            ]
        )
        rows_ref[:, :lanes] = total[: count // 2]
        rows_ref[:, lanes:] = total[count // 2 :]
        conv_bias, gains, shifts, in_bias, out_bias = pick(lambda i: rows_ref[i : i + 1, :])
        for b in range(2):
            conv_ref[b : b + 1, :] = conv_bias[b]
            out_ref[b : b + 1, :] = out_bias[b]
            for i in range(2):
                gain_ref[b, i : i + 1, :] = gains[b][i]
                shift_ref[b, i : i + 1, :] = shifts[b][i]
            for i in range(bias_rows):
                in_ref[b : b + 1, i * width : (i + 1) * width] = in_bias[b][i]
        head_ref[...] = rows_ref[12 : 12 + 8 * (-(-classes // 8)), :].T[:, :classes]
        terms = rows_ref[at_loss : at_loss + 1, :128] + rows_ref[at_loss + 1 : at_loss + 2, :128]
        loss_ref[...] = terms[:, 0:1] / terms[:, 1:2]

    return pl.pallas_call(
        kernel,
        grid=(1,),
        in_specs=[pl.BlockSpec((peers, count, lanes), lambda g: (0, first // count, 0))] * cores,
        out_shape=(
            jax.ShapeDtypeStruct((2, width), jnp.float32),
            jax.ShapeDtypeStruct((2, 2, width), jnp.float32),
            jax.ShapeDtypeStruct((2, 2, width), jnp.float32),
            jax.ShapeDtypeStruct((2, hidden), jnp.float32),
            jax.ShapeDtypeStruct((2, width), jnp.float32),
            jax.ShapeDtypeStruct((width, classes), jnp.float32),
            jax.ShapeDtypeStruct((1, 1), jnp.float32),
        ),
        out_specs=[
            pl.BlockSpec((2, width), lambda g: (0, 0)),
            pl.BlockSpec((2, 2, width), lambda g: (0, 0, 0)),
            pl.BlockSpec((2, 2, width), lambda g: (0, 0, 0)),
            pl.BlockSpec((2, hidden), lambda g: (0, 0)),
            pl.BlockSpec((2, width), lambda g: (0, 0)),
            pl.BlockSpec((width, classes), lambda g: (0, 0)),
            pl.BlockSpec((1, 1), lambda g: (0, 0)),
        ],
        scratch_shapes=[pltpu.VMEM((count // 2, 2 * lanes), jnp.float32)],
        compiler_params=pltpu.CompilerParams(vmem_limit_bytes=4 * MIB),
        cost_estimate=cost(1.5),
        name="finish_small",
    )(*stacks)


def finish_conv(parts, conv_rows, small_rows, after=()):
    blocks, count = len(parts), len(parts[0])
    lanes = parts[0][0].shape[-1]
    flat = [part for block in parts for part in block]
    if conv_rows % ROW_TILE:
        sums = [sum(wide(part[:conv_rows]) for part in block) for block in parts]
        sums.append(paired([wide(part[conv_rows:]) for part in parts[0]]))
        return jnp.concatenate([low(total) for total in sums]), after

    def kernel(*refs):
        shard_ref, token_ref = refs[-2:]
        token_ref[...] = jnp.zeros(TOKEN.shape, TOKEN.dtype)
        shard_ref[blocks * conv_rows :] = low(
            paired([wide(refs[i][conv_rows:]) for i in range(count)])
        )
        for b in range(blocks):
            total = sum(wide(refs[b * count + i][:conv_rows]) for i in range(count))
            shard_ref[b * conv_rows : (b + 1) * conv_rows] = low(total)

    found = pl.pallas_call(
        kernel,
        in_specs=[WHOLE] * (len(flat) + len(after)),
        out_specs=[WHOLE] * 2,
        out_shape=[
            jax.ShapeDtypeStruct((blocks * conv_rows + small_rows, lanes), jnp.bfloat16),
            TOKEN,
        ],
        compiler_params=pltpu.CompilerParams(vmem_limit_bytes=8 * MIB),
        cost_estimate=cost(1.2),
        name="finish_conv",
    )(*flat, *after)
    return found[0], (found[1],)


def finish_ffn(merged, plain, conv_rows, ffn_rows, after=()):
    lanes, width = merged[0].shape[-1], plain[0].shape[-1]

    def cut_back(total):
        size = 2 * ffn_rows
        return jnp.concatenate(
            [total[i * size : (i + 1) * size] for i in range(width // lanes)], 1
        )

    if conv_rows % ROW_TILE or ffn_rows % ROW_TILE:
        sums = [sum(wide(part) for part in plain)]
        sums.append(cut_back(sum(wide(part[conv_rows:]) for part in merged)))
        return jnp.stack([each[:ffn_rows].T for each in sums]), jnp.stack(
            [each[ffn_rows:] for each in sums]
        ), after

    def kernel(*refs):
        in_ref, out_ref, token_ref = refs[-3:]
        token_ref[...] = jnp.zeros(TOKEN.shape, TOKEN.dtype)
        late = sum(wide(refs[i][conv_rows:]) for i in range(len(merged)))
        sums = [sum(wide(refs[len(merged) + i][...]) for i in range(len(plain))), cut_back(late)]
        for b in range(2):
            in_ref[b] = sums[b][:ffn_rows].T
            out_ref[b] = sums[b][ffn_rows:]

    found = pl.pallas_call(
        kernel,
        in_specs=[WHOLE] * (len(merged) + len(plain) + len(after)),
        out_specs=[WHOLE] * 3,
        out_shape=(
            jax.ShapeDtypeStruct((2, width, ffn_rows), jnp.float32),
            jax.ShapeDtypeStruct((2, ffn_rows, width), jnp.float32),
            TOKEN,
        ),
        compiler_params=pltpu.CompilerParams(vmem_limit_bytes=8 * MIB),
        cost_estimate=cost(1),
        name="finish_ffn",
    )(*merged, *plain, *after)
    return found[0], found[1], (found[2],)


def add_slots(parts, slots, after=(), reads=()):
    lanes = parts[0].shape[-1]
    rows = parts[0].size // (slots * lanes)
    parts = [part.reshape(slots, rows, lanes) for part in parts]
    block = rows // 4 if rows % (4 * ROW_TILE) == 0 else rows

    def kernel(*refs):
        out_refs, token_ref = refs[-1 - slots : -1], refs[-1]
        token_ref[...] = jnp.zeros(TOKEN.shape, TOKEN.dtype)
        for slot in range(slots):
            out_refs[slot][...] = low(sum(wide(refs[i][slot]) for i in range(len(parts))))

    found = pl.pallas_call(
        kernel,
        grid=(rows // block,),
        in_specs=[pl.BlockSpec((slots, block, lanes), lambda g: (0, g, 0))] * len(parts)
        + tokens(after)
        + [ANYWHERE] * len(reads),
        out_specs=[pl.BlockSpec((block, lanes), lambda g: (g, 0))] * slots + [TOKEN_SPEC],
        out_shape=[jax.ShapeDtypeStruct((rows, lanes), jnp.bfloat16)] * slots + [TOKEN],
        compiler_params=pltpu.CompilerParams(vmem_limit_bytes=8 * MIB),
        cost_estimate=cost(2),
        name="add_slots",
    )(*parts, *after, *reads)
    return found[:slots], found[slots]


def place_conv_grads(stacks, blocks, taps, slab, places, sizes):
    cores, seqs, acrosses = sizes[:3]
    peers, rows, lanes = stacks[0].shape
    channels = slab * seqs * acrosses
    if slab % ROW_TILE or rows % slab:
        full = jnp.stack([each[:, : blocks * taps * slab] for each in stacks])
        full = full.reshape(cores, seqs, acrosses, blocks, taps, slab, lanes)
        for axis, (place, size) in enumerate(zip(places[:3], sizes[:3])):
            full = relative(full, axis, place, size)
        return wide(
            full.transpose(3, 4, 1, 2, 5, 0, 6).reshape(blocks, taps, channels, cores * lanes)
        )
    stacks = [each.reshape(peers, rows // slab, slab, lanes) for each in stacks]

    def kernel(place_ref, *refs):
        out_ref = refs[-1]
        for c in range(cores):
            lane = pl.multiple_of(lax.rem(place_ref[0] - c + cores, cores) * lanes, lanes)
            for s in range(seqs):
                at_s = lax.rem(place_ref[1] - s + seqs, seqs)
                for a in range(acrosses):
                    at_a = lax.rem(place_ref[2] - a + acrosses, acrosses)
                    row = pl.multiple_of((at_s * acrosses + at_a) * slab, slab)
                    for b in range(blocks):
                        piece = wide(refs[c * blocks + b][s * acrosses + a, 0])
                        out_ref[b, 0, pl.ds(row, slab), pl.ds(lane, lanes)] = piece

    specs = [
        pl.BlockSpec((peers, 1, slab, lanes), lambda k, place, b=b: (0, b * taps + k, 0, 0))
        for b in range(blocks)
    ]
    return pl.pallas_call(
        kernel,
        grid_spec=pltpu.PrefetchScalarGridSpec(
            num_scalar_prefetch=1,
            grid=(taps,),
            in_specs=specs * cores,
            out_specs=pl.BlockSpec(
                (blocks, 1, channels, cores * lanes), lambda k, place: (0, k, 0, 0)
            ),
        ),
        out_shape=jax.ShapeDtypeStruct((blocks, taps, channels, cores * lanes), jnp.float32),
        compiler_params=pltpu.CompilerParams(vmem_limit_bytes=10 * MIB),
        cost_estimate=cost(5),
        name="place_conv_grads",
    )(
        jnp.stack(places[:3]).astype(jnp.int32),
        *[each for stack in stacks for each in [stack] * blocks],
    )


def copy_all(copies):
    for copy in copies:
        copy.start()
    for copy in copies:
        copy.wait()


def place_conv(pieces, places, sizes, after=(), reads=()):
    cores, seqs, acrosses, tap_peers = sizes
    taps, slab, lanes = pieces[0][0].shape[2:]
    inner = slab * seqs * acrosses * tap_peers
    if slab % ROW_TILE:
        full = jnp.stack([jnp.stack(row) for row in pieces])
        for axis, (place, size) in enumerate(zip(places, sizes)):
            full = relative(full, axis, place, size)
        return full.transpose(4, 3, 1, 2, 5, 0, 6).reshape(taps, inner, cores * lanes), after
    flat = [piece for row in pieces for piece in row]

    def kernel(place_ref, *refs):
        out_ref, token_ref, sem_ref = refs[-3:]
        token_ref[...] = jnp.zeros(TOKEN.shape, TOKEN.dtype)
        copies = []
        for c in range(cores):
            lane = lax.rem(place_ref[0] - c + cores, cores) * lanes
            for s in range(seqs):
                at_s = lax.rem(place_ref[1] - s + seqs, seqs)
                for a in range(acrosses):
                    at_a = lax.rem(place_ref[2] - a + acrosses, acrosses)
                    for t in range(tap_peers):
                        at_t = lax.rem(place_ref[3] - t + tap_peers, tap_peers)
                        row = ((at_t * seqs + at_s) * acrosses + at_a) * slab
                        copies.append(
                            pltpu.make_async_copy(
                                refs[c * seqs + s].at[a, t],
                                out_ref.at[
                                    :,
                                    pl.ds(pl.multiple_of(row, slab), slab),
                                    pl.ds(pl.multiple_of(lane, lanes), lanes),
                                ],
                                sem_ref.at[len(copies)],
                            )
                        )
        copy_all(copies)

    found = pl.pallas_call(
        kernel,
        in_specs=[SCALARS] + [ANYWHERE] * (len(flat) + len(reads)) + [WHOLE] * len(after),
        out_specs=[WHOLE] * 2,
        out_shape=[pltpu.HBM((taps, inner, cores * lanes), jnp.bfloat16), TOKEN],
        scratch_shapes=[pltpu.SemaphoreType.DMA((cores * seqs * acrosses * tap_peers,))],
        compiler_params=pltpu.CompilerParams(vmem_limit_bytes=12 * MIB),
        cost_estimate=cost(3),
        name="place_conv",
    )(jnp.stack(places).astype(jnp.int32), *flat, *reads, *after)
    return found[0], (found[1],)


def place_ffn(pieces, sizes, after=(), reads=()):
    cores, seqs, acrosses, tap_peers = sizes
    cuts, ffn_rows, lanes = pieces[0][0].shape[2:]
    cuts //= 2
    width = cuts * lanes
    units = seqs * acrosses * tap_peers * ffn_rows
    if ffn_rows % ROW_TILE:
        full = jnp.stack([jnp.stack(row) for row in pieces])
        full = full.reshape(cores, acrosses, seqs, tap_peers, 2, cuts, ffn_rows, lanes)
        full = full.transpose(4, 0, 1, 2, 3, 6, 5, 7).reshape(2, cores, units, width)
        return [full[0, c] for c in range(cores)], [full[1, c] for c in range(cores)], after
    flat = [piece for row in pieces for piece in row]

    def kernel(*refs):
        out_refs = refs[-2 - 2 * cores : -2]
        token_ref, sem_ref = refs[-2:]
        token_ref[...] = jnp.zeros(TOKEN.shape, TOKEN.dtype)
        copies = []
        for c in range(cores):
            for a in range(acrosses):
                for which in range(2):
                    for cut in range(cuts):
                        copies.append(
                            pltpu.make_async_copy(
                                refs[c * acrosses + a].at[:, :, which * cuts + cut],
                                out_refs[which * cores + c].at[
                                    a, :, :, :, pl.ds(cut * lanes, lanes)
                                ],
                                sem_ref.at[len(copies)],
                            )
                        )
        copy_all(copies)

    shape = pltpu.HBM((acrosses, seqs, tap_peers, ffn_rows, width), jnp.bfloat16)
    found = pl.pallas_call(
        kernel,
        in_specs=[ANYWHERE] * (len(flat) + len(reads)) + [WHOLE] * len(after),
        out_specs=[WHOLE] * (2 * cores + 1),
        out_shape=[shape] * (2 * cores) + [TOKEN],
        scratch_shapes=[pltpu.SemaphoreType.DMA((2 * cores * acrosses * cuts,))],
        compiler_params=pltpu.CompilerParams(vmem_limit_bytes=12 * MIB),
        cost_estimate=cost(2),
        name="place_ffn",
    )(*flat, *reads, *after)
    token = found[-1]
    found = [each.reshape(units, width) for each in found[:-1]]
    return found[:cores], found[cores:], (token,)


class Ring:
    def __init__(self, axis, size, index, pairs):
        self.axis, self.size, self.index, self.pairs = axis, size, index, pairs

    def shifted(self, value, by):
        return lax.ppermute(value, self.axis, self.pairs(lambda i: (i + by) % self.size))

    def swapped(self, value, bit):
        return lax.ppermute(value, self.axis, self.pairs(lambda i: i ^ bit))

    def gather(self, value):
        return [value] + [self.shifted(value, by) for by in range(1, self.size)]

    def swap(self, values):
        return [values[0]] + [self.shifted(values[by], -by) for by in range(1, self.size)]


def relative(value, axis, place, size):
    if size == 1:
        return value
    return jnp.stack(
        [
            lax.dynamic_index_in_dim(value, (place - slot) % size, axis, False)
            for slot in range(size)
        ],
        axis,
    )


def rings():
    peers = lax.axis_size("dp")
    cores = CORES if peers % CORES == 0 else 1
    columns = peers // cores
    place = lax.axis_index("dp")

    def plain(axis):
        size = lax.axis_size(axis)
        return Ring(
            axis, size, lax.axis_index(axis), lambda move: [(i, move(i)) for i in range(size)]
        )

    across = Ring(
        "dp",
        columns,
        place // cores,
        lambda move: [(i, move(i // cores) * cores + i % cores) for i in range(peers)],
    )
    core = Ring(
        "dp",
        cores,
        place % cores,
        lambda move: [(i, i // cores * cores + move(i % cores)) for i in range(peers)],
    )
    return core, across, plain("seq"), plain("tap")


class Reduce:
    def __init__(self, terms, order):
        self.order = order
        self.parts = [terms[0]] + [order[0].shifted(terms[s], -s) for s in range(1, order[0].size)]

    def step(self, level, after, reads=()):
        ring = self.order[level]
        found, token = add_slots(self.parts, ring.size, after, reads)
        self.parts = [found[0]] + [ring.shifted(found[s], -s) for s in range(1, ring.size)]
        return (token,)


def shared_copies(value, across, seq):
    peers, spans = lax.axis_size("dp"), lax.axis_size("seq")
    cores = peers // across.size

    def target(place, by_a, by_s):
        dp, at = place // spans, place % spans
        moved = (dp // cores + by_a) % across.size * cores + dp % cores
        return moved * spans + (at + by_s) % spans

    return [
        [
            value
            if by_a == by_s == 0
            else lax.ppermute(
                value,
                ("dp", "seq"),
                [(place, target(place, by_a, by_s)) for place in range(peers * spans)],
            )
            for by_a in range(across.size)
        ]
        for by_s in range(seq.size)
    ]


def passed_along(value, axis, by):
    peers = lax.axis_size(axis)
    pairs = [(i, i + by) for i in range(peers) if 0 <= i + by < peers]
    return lax.ppermute(value, axis, pairs)


def rims(source, reach_rows, seq, rim=None):
    span_rows = source.shape[0]
    if seq.size == 2 and reach_rows <= span_rows:
        if rim is None:
            first = (1 - seq.index) * (span_rows - reach_rows)
            rim = lax.dynamic_slice_in_dim(source, first, reach_rows, 0)
        return seq.shifted(rim, 1)
    left_parts = []
    right_parts = []
    distances = -(-reach_rows // span_rows)
    for distance in range(1, distances + 1):
        rim_count = min(span_rows, reach_rows - (distance - 1) * span_rows)
        left_parts.insert(0, passed_along(source[span_rows - rim_count :], "seq", distance))
        right_parts.append(passed_along(source[:rim_count], "seq", -distance))
    return left_parts, right_parts


def extend(source, found, seq, after=()):
    if isinstance(found, tuple):
        return join_rows(found[0] + [source] + found[1], after)
    reach, span = found.shape[0], source.shape[0]

    def kernel(place_ref, found_ref, source_ref, *refs):
        out_ref, token_ref = refs[-2:]
        token_ref[...] = jnp.zeros(TOKEN.shape, TOKEN.dtype)
        out_ref[reach : reach + span] = source_ref[...]
        zeros = jnp.zeros(found.shape, found.dtype)

        @pl.when(place_ref[0] == 0)
        def _():
            out_ref[:reach] = zeros
            out_ref[reach + span :] = found_ref[...]

        @pl.when(place_ref[0] != 0)
        def _():
            out_ref[:reach] = found_ref[...]
            out_ref[reach + span :] = zeros

    shape = jax.ShapeDtypeStruct((span + 2 * reach, source.shape[1]), source.dtype)
    extended, token = pl.pallas_call(
        kernel,
        in_specs=[SCALARS] + [WHOLE] * (2 + len(after)),
        out_specs=[WHOLE] * 2,
        out_shape=[shape, TOKEN],
        compiler_params=pltpu.CompilerParams(vmem_limit_bytes=10 * MIB),
        cost_estimate=cost(1.5),
        name="extend",
    )(seq.index.astype(jnp.int32)[None], found, source, *after)
    return extended, (token,)


def to_rows(values):
    windows, positions = values.shape[:2]
    cut = values.reshape((windows, positions // FIRST_DILATION, FIRST_DILATION) + values.shape[2:])
    return jnp.swapaxes(cut, 0, 1).reshape((windows * positions,) + values.shape[2:])


def from_rows(values, windows):
    cut = values.reshape((-1, windows, FIRST_DILATION) + values.shape[1:])
    return jnp.swapaxes(cut, 0, 1).reshape((windows, -1) + values.shape[1:])


def on_device(
    inputs,
    targets,
    masked,
    conv_weight,
    conv_bias,
    gains,
    shifts,
    in_weight,
    in_bias,
    out_weight,
    out_bias,
    head_weight,
):
    core, across, seq, tap = rings()
    taps = conv_weight.shape[1]
    channels = conv_weight.shape[2]
    width = conv_weight.shape[3]
    slab = channels // (seq.size * across.size)
    lanes = width // core.size
    hidden_width = in_bias.shape[1]
    ffn_rows = in_weight.shape[2]
    windows = inputs.shape[0]
    rows = windows * inputs.shape[1]
    steps = (FIRST_DILATION * windows, SECOND_DILATION * windows)
    units = hidden_width // core.size
    places = (core.index, seq.index, across.index, tap.index)
    sizes = (core.size, seq.size, across.size, tap.size)

    in_bias_placed = []
    for b in range(2):
        bias = in_bias[b].reshape(across.size, core.size, seq.size, tap.size, ffn_rows)
        for axis, ring in enumerate((across, core, seq, tap)):
            bias = relative(bias, axis, ring.index, ring.size)
        in_bias_placed.append(bias.transpose(1, 0, 2, 3, 4).reshape(core.size, units))

    def cut_ffn(piece):
        return piece.reshape(ffn_rows, core.size, lanes).swapaxes(0, 1).reshape(-1, lanes)

    def bundle(b, ready=None):
        conv_piece = lax.dynamic_slice(
            conv_weight[b],
            (0, (seq.index * across.size + across.index) * slab, core.index * lanes),
            (taps, slab, lanes),
        )
        pieces = [
            conv_piece.reshape(taps * slab, lanes),
            cut_ffn(in_weight[b].T),
            cut_ffn(out_weight[b]),
        ]
        if ready is not None:
            pieces = [piece + ready for piece in pieces]
        return jnp.concatenate(pieces)

    cuts = (
        (0, taps * slab, (taps, slab, lanes)),
        (taps * slab, taps * slab + 2 * core.size * ffn_rows, (2 * core.size, ffn_rows, lanes)),
    )

    def straight(arrays):
        return (arrays, ((0, None, arrays[0].shape),))

    conv_input = to_rows(inputs)
    stream = conv_input
    codes = to_rows(targets + masked * head_weight.shape[1])
    codes = jnp.broadcast_to(codes[:, None], (rows, 128))

    reaches = [taps // 2 * step for step in steps]
    rim_reaches = [reach if seq.size == 2 and reach <= rows else 0 for reach in reaches]

    tap_parts = tap.gather(bundle(0))
    found = rims(conv_input, reaches[0], seq)
    behind = bundle(1, tap_parts[-1][0, 0] * 0)
    (conv_part, ffn_part), last = restack(
        [(tap_parts, cuts)], reads=[behind] + [found if rim_reaches[0] else conv_input]
    )
    (behind,), last = hold([behind], last)
    split = (tap.size + 1) // 2
    late_parts = tap.gather(behind)
    extended, last = extend(conv_input, found, seq, last)
    extended_parts = [extended] + [core.shifted(extended, -c) for c in range(1, core.size)]
    conv_parts, ffn_parts = across.gather(conv_part), seq.gather(ffn_part)
    (conv_part, ffn_part), last = restack(
        [straight(conv_parts), straight(ffn_parts)],
        reads=late_parts[1:split],
        after=last,
    )
    conv_parts, ffn_parts = seq.gather(conv_part), across.gather(ffn_part)
    conv_slots = [core.gather(conv_part)]
    ffn_slots = [core.gather(ffn_part)]
    held, last = hold(
        conv_parts[1:] + ffn_parts[1:],
        last,
        conv_slots[0][1:] + ffn_slots[0][1:] + late_parts[1:],
    )
    conv_slots += [core.gather(each) for each in held[: seq.size - 1]]
    ffn_slots += [core.gather(each) for each in held[seq.size - 1 :]]
    (late_conv, late_ffn), last = restack([(late_parts, cuts)], after=last, fixed=True)
    late_conv_parts, late_ffn_parts = across.gather(late_conv), seq.gather(late_ffn)

    def turned(slots):
        return [[each[c] for each in slots] for c in range(core.size)]

    conv_full, in_full, out_full = [None, None], [None, None], [None, None]
    conv_full[0], last = place_conv(
        turned(conv_slots), places, sizes, last, [part for each in ffn_slots for part in each[1:]]
    )
    saved = []
    reads = []
    rim = None
    for b in range(2):
        if b == 1:
            found = rims(conv_input, reaches[1], seq, rim)
            held, last = hold(late_conv_parts[1:] + late_ffn_parts[1:], last)
            late_conv_slots += [core.gather(each) for each in held[: seq.size - 1]]
            late_ffn_slots += [core.gather(each) for each in held[seq.size - 1 :]]
            conv_full[1], last = place_conv(turned(late_conv_slots), places, sizes, last)
            in_full[1], out_full[1], last = place_ffn(turned(late_ffn_slots), sizes, last)
            extended, last = extend(conv_input, found, seq, last)
            extended_parts = [extended] + [core.shifted(extended, -c) for c in range(1, core.size)]
        (normed_conv, conv_slope, stream, lowered), last = conv_forward(
            extended,
            conv_full[b],
            stream,
            conv_bias[b],
            gains[b, 0],
            shifts[b, 0],
            steps[b],
            last,
            reads,
        )
        reads = extended_parts[1:]
        if b == 0:
            (late_conv, late_ffn), last = restack(
                [straight(late_conv_parts), straight(late_ffn_parts)], after=last
            )
            late_conv_parts, late_ffn_parts = seq.gather(late_conv), across.gather(late_ffn)
            late_conv_slots = [core.gather(late_conv)]
            late_ffn_slots = [core.gather(late_ffn)]
            in_full[0], out_full[0], last = place_ffn(turned(ffn_slots), sizes, last)
            reads = reads + late_conv_slots[0][1:] + late_ffn_slots[0][1:]
        active, hidden_slopes, (normed_ffn, scale_ffn, stream, conv_input), packets, rim, last = (
            ffn_forward(
                lowered,
                stream,
                in_full[b],
                out_full[b],
                [in_bias_placed[b][c] for c in range(core.size)],
                out_bias[b],
                gains[b, 1],
                shifts[b, 1],
                seq.index,
                rim_reaches[1] if b == 0 else 0,
                b == 1,
                last,
                reads,
            )
        )
        packets = [core.shifted(packet, -1 - c) for c, packet in enumerate(packets)]
        reads = packets
        saved.append(
            (
                extended_parts,
                conv_slope,
                normed_conv,
                (active, lowered, packets),
                hidden_slopes,
                normed_ffn,
                scale_ffn,
            )
        )

    (stream_grad, head_grad, loss_rows), last = head_and_loss(stream, head_weight, codes, last)

    ffn_rows_of_sums = [None, None]
    conv_rows_of_sums = [None, None]
    in_bias_grads = [None, None]
    ffn_sums = [None, None]
    conv_sums = [None, None]
    merged = [None, None]

    def groups(halves):
        half = (tap.size + 1) // 2
        return [(each.parts, slots) for each, slots in zip(halves, (half, tap.size - half))]

    for b in (1, 0):
        (
            extended_parts,
            conv_slope,
            normed_conv,
            active_pair,
            hidden_slopes,
            normed_ffn,
            scale_ffn,
        ) = saved[b]
        output_grad, hidden_grad, biases, packets, ffn_rows_of_sums[b], last = ffn_back_hidden(
            stream_grad, normed_ffn, scale_ffn, gains[b, 1], out_full[b], hidden_slopes, last
        )
        if b == 1:
            arrived_packets = [core.shifted(packet, -1 - c) for c, packet in enumerate(packets)]
        if b == 0:
            for each in ffn_sums[1]:
                last = each.step(1, last)
            for each in conv_sums[1]:
                last = each.step(1, last)
        stream_grad, conv_grad, conv_cuts, relayed, rim, conv_rows_of_sums[b], last = ffn_back_stream(
            stream_grad,
            hidden_grad,
            packets,
            in_full[b],
            normed_conv,
            conv_slope,
            gains[b, 0],
            places,
            rim_reaches[b],
            last,
            reads,
            relay=b == 0,
        )
        reads = []
        if b == 0:
            merged[1], last = merge_slots(
                groups(conv_sums[1]), groups(ffn_sums[1]), last
            )
            sent = [rim] if rim is not None else []
            held, last = hold(list(conv_cuts) + list(relayed) + sent, last)
            conv_cuts, relayed = held[: core.size - 1], held[core.size - 1 : 2 * core.size - 2]
            rim = held[-1] if sent else None
            merged[1] = tap.swap(merged[1])
            arrived_packets = [core.shifted(packet, -1 - c) for c, packet in enumerate(relayed)]
        arrived = [core.shifted(conv_cuts[c - 1], -c) for c in range(1, core.size)]
        in_bias_grads[b] = list(biases)
        found_rims = rims(conv_grad, reaches[b], seq, rim)

        def ffn_grads(last):
            active, lowered, packets = active_pair
            if core.size == 1:
                packets = []
            first, second, token = ffn_weight_grad(
                (
                    (hidden_grad, lowered, [(g, p) for g, p in zip(arrived_packets, packets)]),
                    (active, output_grad, [(p, g) for g, p in zip(arrived_packets, packets)]),
                ),
                sizes,
                ffn_rows,
                last,
            )
            found = [Reduce(first, (across, seq))]
            if second:
                found.append(Reduce(second, (seq, across)))
            return found, (token,)

        def conv_grads(last, reads=()):
            first, second, token = conv_weight_grad(
                extended_parts, conv_grad, arrived, places, sizes, taps, steps[b], last, reads
            )
            found = [Reduce(first, (seq, across))]
            if second:
                found.append(Reduce(second, (across, seq)))
            return found, (token,)

        if b == 1:
            ffn_sums[1], last = ffn_grads(last)
            extended_grad, last = extend(conv_grad, found_rims, seq, last)
            conv_sums[1], last = conv_grads(last)
        else:
            conv_sums[0], last = conv_grads(last, arrived_packets)
            extended_grad, last = extend(conv_grad, found_rims, seq, last)
            ffn_sums[0], last = ffn_grads(last)
            for each in conv_sums[0]:
                last = each.step(1, last, merged[1][1:])
        if b == 1:
            stream_grad, last = conv_data_grad(
                extended_grad, conv_full[1], stream_grad, steps[1], jnp.float32, last
            )

    row_groups = [(each, 3) for each in conv_rows_of_sums + ffn_rows_of_sums]
    row_groups.append((head_grad, head_weight.shape[1]))
    (conv_input,), last = hold([conv_input], last)
    final_state = from_rows(conv_input, windows)
    packed, last = pack_small(row_groups, in_bias_grads, loss_rows, places, sizes, ffn_rows, last, [final_state])

    conv_rows = taps * slab
    merged[0], last = append_slots(groups(conv_sums[0]), [packed], last)
    merged[0] = tap.swap(merged[0])
    stream_grad, last = conv_data_grad(
        extended_grad, conv_full[0], stream_grad, steps[0], jnp.bfloat16, last
    )
    for each in ffn_sums[0]:
        last = each.step(1, last)
    shards, last = finish_conv([merged[0], merged[1]], conv_rows, packed.shape[0], last)
    ffn_late, last = append_slots(groups(ffn_sums[0]), [], last)
    ffn_late = tap.swap(ffn_late)
    grad_inputs = from_rows(stream_grad, windows)
    copies = [each for row in shared_copies(shards, across, seq) for each in row]
    (stack,), last = restack([straight(copies)], reads=[grad_inputs] + ffn_late[1:], after=last)
    stacks = core.gather(stack)
    grad_in, grad_out, last = finish_ffn(merged[1], ffn_late, conv_rows, ffn_rows, last)
    (
        grad_conv_bias,
        grad_gains,
        grad_shifts,
        grad_in_bias,
        grad_out_bias,
        grad_head_weight,
        loss,
    ) = finish_small(
        stacks, 2 * conv_rows, width, head_weight.shape[1], hidden_width, places, sizes
    )
    grad_conv = place_conv_grads(stacks, 2, taps, slab, places, sizes)
    return (
        final_state,
        grad_inputs,
        grad_conv,
        grad_conv_bias,
        grad_gains,
        grad_shifts,
        grad_in,
        grad_in_bias,
        grad_out,
        grad_out_bias,
        grad_head_weight,
        loss.reshape(()),
    )


def solution(mesh):
    placed = (
        P(("dp", "tap"), "seq", None),
        P(("dp", "tap"), "seq"),
        P(("dp", "tap"), "seq"),
        P(None, None, "tap", None),
        P(),
        P(),
        P(),
        P(None, None, ("dp", "seq", "tap")),
        P(),
        P(None, ("dp", "seq", "tap"), None),
        P(),
        P(),
    )
    return jax.shard_map(
        on_device,
        mesh=mesh,
        in_specs=placed,
        out_specs=(
            P(("dp", "tap"), "seq", None),
            P(("dp", "tap"), "seq", None),
            P(None, None, "tap", None),
            P(),
            P(),
            P(),
            P(None, None, ("dp", "seq", "tap")),
            P(),
            P(None, ("dp", "seq", "tap"), None),
            P(),
            P(),
            P(),
        ),
        check_vma=False,
    )
```

```python
import functools

import jax
import jax.numpy as jnp
import numpy as np
from jax import lax
from jax.experimental import pallas as pl
from jax.experimental.pallas import tpu as pltpu
from jax.sharding import PartitionSpec as P

FIRST_DILATION = 4
SECOND_DILATION = 32
EPSILON = 1e-05
HIGHEST_PRECISION = lax.Precision.HIGHEST
CORES = 2
ROW_TILE = 16
MIB = 1024 * 1024
VMEM_BYTES = 20 * MIB
ANYWHERE = pl.BlockSpec(memory_space=pl.ANY)
SCALARS = pl.BlockSpec(memory_space=pltpu.SMEM)


TOKEN = jax.ShapeDtypeStruct((8, 128), jnp.float32)


def cost(microseconds):
    size = int(microseconds * 3.5e6)
    return pl.CostEstimate(flops=int(microseconds * 1.1e9), bytes_accessed=size, transcendentals=0)


WHOLE = pl.BlockSpec(memory_space=pltpu.VMEM)
TOKEN_SPEC = pl.BlockSpec(TOKEN.shape, lambda *_: (0, 0))


def tokens(after):
    return [TOKEN_SPEC] * len(after)


def in_hbm(array):
    return pltpu.with_memory_space_constraint(array, pltpu.HBM)


def low(values):
    return values.astype(jnp.bfloat16)


def wide(values):
    return values.astype(jnp.float32)


def gelu_parts(values):
    phi = 0.5 * (1.0 + lax.erf(values * 0.7071067811865476))
    return (
        values * phi,
        phi + values * jnp.exp(-0.5 * values * values) * 0.3989422804014327,
    )


def normalize(values):
    center = values - jnp.mean(values, -1, keepdims=True)
    scale = lax.rsqrt(jnp.mean(center * center, -1, keepdims=True) + EPSILON)
    return (center * scale, scale)


def norm_back(upstream, normed, scale):
    return scale * (
        upstream
        - jnp.mean(upstream, -1, keepdims=True)
        - normed * jnp.mean(upstream * normed, -1, keepdims=True)
    )


def tap_groups(taps):
    return 3 if taps % 3 == 0 else 1


def row_chunks(rows, most):
    size = min(rows, most)
    return [(first, size) for first in range(0, rows, size)]


def conv_forward(extended, weight, stream, bias, gain, shift, step, after=(), reads=()):
    taps, inner, width = weight.shape
    rows = stream.shape[0]
    group = tap_groups(taps)
    steps = taps // group

    def kernel(extended_ref, weight_ref, stream_ref, bias_ref, gain_ref, shift_ref, *refs):
        normed_ref, slope_ref, next_ref, lowered_ref, token_ref, total_ref = refs[-6:]
        token_ref[...] = jnp.zeros(TOKEN.shape, TOKEN.dtype)
        first = pl.program_id(0) * group
        total = None
        for j in range(group):
            start = pl.multiple_of((first + j) * step, ROW_TILE)
            term = jnp.dot(
                extended_ref[pl.ds(start, rows), :],
                weight_ref[j],
                preferred_element_type=jnp.float32,
            )
            total = term if total is None else total + term

        @pl.when(pl.program_id(0) == 0)
        def _():
            total_ref[...] = total

        @pl.when(pl.program_id(0) > 0)
        def _():
            total_ref[...] += total

        @pl.when(pl.program_id(0) == steps - 1)
        def _():
            for at, size in row_chunks(rows, 128):
                some = pl.ds(at, size)
                value, slope = gelu_parts(total_ref[some, :] + bias_ref[...])
                normed, scale = normalize(value)
                mid = wide(stream_ref[some, :]) + normed * gain_ref[...] + shift_ref[...]
                normed_ref[some, :] = low(normed)
                slope_ref[some, :] = low(scale * slope)
                next_ref[some, :] = mid
                lowered_ref[some, :] = low(mid)

    whole = pl.BlockSpec((rows, width), lambda g: (0, 0))
    row = pl.BlockSpec((1, width), lambda g: (0, 0))
    found = pl.pallas_call(
        kernel,
        grid=(steps,),
        in_specs=[
            pl.BlockSpec(extended.shape, lambda g: (0, 0)),
            pl.BlockSpec((group, inner, width), lambda g: (g, 0, 0)),
            whole,
            row,
            row,
            row,
        ]
        + tokens(after)
        + [ANYWHERE] * len(reads),
        out_specs=[whole] * 4 + [TOKEN_SPEC],
        out_shape=[
            pltpu.HBM((rows, width), jnp.bfloat16),
            pltpu.HBM((rows, width), jnp.bfloat16),
            pltpu.HBM((rows, width), jnp.float32),
            jax.ShapeDtypeStruct((rows, width), jnp.bfloat16),
            TOKEN,
        ],
        scratch_shapes=[pltpu.VMEM((rows, width), jnp.float32)],
        compiler_params=pltpu.CompilerParams(vmem_limit_bytes=VMEM_BYTES),
        cost_estimate=cost(9),
        name="conv_forward",
    )(extended, in_hbm(weight), in_hbm(stream) if stream.dtype == jnp.float32 else stream, bias[None], gain[None], shift[None], *after, *reads)
    return found[:4], (found[4],)


def ffn_forward(
    lowered,
    stream,
    ins,
    outs,
    in_biases,
    out_bias,
    gain,
    shift,
    seq_index,
    reach,
    last_block,
    after=(),
    reads=(),
):
    rows, width = lowered.shape
    cores = len(ins)
    units = ins[0].shape[0]
    block = min(units, 256)
    steps = units // block

    rims_out = 1 if reach else 0

    def kernel(place_ref, lowered_ref, stream_ref, out_bias_ref, gain_ref, shift_ref, *refs):
        in_refs, out_refs, bias_refs = (refs[i * cores : (i + 1) * cores] for i in range(3))
        found_refs = refs[-6 - 2 * cores - rims_out :]
        active_ref, slope_refs = found_refs[0], found_refs[1 : 1 + cores]
        normed_ref, scale_ref, next_ref, rounded_ref = found_refs[1 + cores : 5 + cores]
        packet_refs = found_refs[5 + cores : 4 + 2 * cores]
        token_ref, total_ref = found_refs[-2:]
        token_ref[...] = jnp.zeros(TOKEN.shape, TOKEN.dtype)
        lane = pl.multiple_of(width + pl.program_id(0) * block, block)

        @pl.when(pl.program_id(0) == 0)
        def _():
            total_ref[...] = jnp.zeros(total_ref.shape, jnp.float32)
            for packet_ref in packet_refs:
                packet_ref[:, :width] = lowered_ref[...]

        for at, size in row_chunks(rows, 512):
            some = pl.ds(at, size)
            term = None
            for c in range(cores):
                hidden = lax.dot_general(
                    lowered_ref[some, :],
                    in_refs[c][...],
                    (((1,), (1,)), ((), ())),
                    preferred_element_type=jnp.float32,
                )
                active, slope = gelu_parts(hidden + bias_refs[c][...])
                active = low(active)
                if c == 0:
                    active_ref[some, :] = active
                else:
                    packet_refs[c - 1][some, pl.ds(lane, block)] = active
                slope_refs[c][some, :] = low(slope)
                found = jnp.dot(active, out_refs[c][...], preferred_element_type=jnp.float32)
                term = found if term is None else term + found
            total_ref[some, :] += term

        @pl.when(pl.program_id(0) == steps - 1)
        def _():
            for at, size in row_chunks(rows, 128):
                some = pl.ds(at, size)
                normed, scale = normalize(total_ref[some, :] + out_bias_ref[...])
                after_ffn = stream_ref[some, :] + normed * gain_ref[...] + shift_ref[...]
                normed_ref[some, :] = low(normed)
                scale_ref[some, :] = jnp.broadcast_to(scale, (size, 128))
                next_ref[some, :] = after_ffn
                rounded_ref[some, :] = low(after_ffn)
            if reach:
                first = pl.multiple_of((1 - place_ref[0]) * (rows - reach), ROW_TILE)
                found_refs[-3][...] = rounded_ref[pl.ds(first, reach), :]

    whole = pl.BlockSpec((rows, width), lambda g: (0, 0))
    row = pl.BlockSpec((1, width), lambda g: (0, 0))
    piece = pl.BlockSpec((block, width), lambda g: (g, 0))
    columns = pl.BlockSpec((rows, block), lambda g: (0, g))
    hidden_shape = pltpu.HBM((rows, units), jnp.bfloat16)
    found = pl.pallas_call(
        kernel,
        grid=(steps,),
        in_specs=[SCALARS, whole, whole, row, row, row]
        + [piece] * (2 * cores)
        + [pl.BlockSpec((1, block), lambda g: (0, g))] * cores
        + tokens(after)
        + [ANYWHERE] * len(reads),
        out_specs=[columns] * (1 + cores)
        + [whole, pl.BlockSpec((rows, 128), lambda g: (0, 0)), whole, whole]
        + [pl.BlockSpec((rows, width + units), lambda g: (0, 0))] * (cores - 1)
        + [pl.BlockSpec((reach, width), lambda g: (0, 0))] * rims_out
        + [TOKEN_SPEC],
        out_shape=[hidden_shape] * (1 + cores)
        + [
            pltpu.HBM((rows, width), jnp.bfloat16),
            pltpu.HBM((rows, 128), jnp.float32),
            (jax.ShapeDtypeStruct if last_block else pltpu.HBM)((rows, width), jnp.float32),
            jax.ShapeDtypeStruct((rows, width), jnp.bfloat16),
        ]
        + [jax.ShapeDtypeStruct((rows, width + units), jnp.bfloat16)] * (cores - 1)
        + [jax.ShapeDtypeStruct((reach, width), jnp.bfloat16)] * rims_out
        + [TOKEN],
        scratch_shapes=[pltpu.VMEM((rows, width), jnp.float32)],
        compiler_params=pltpu.CompilerParams(vmem_limit_bytes=VMEM_BYTES),
        cost_estimate=cost(11),
        name="ffn_forward",
    )(
        seq_index.astype(jnp.int32)[None],
        lowered,
        in_hbm(stream),
        out_bias[None],
        gain[None],
        shift[None],
        *[in_hbm(each) for each in ins],
        *[in_hbm(each) for each in outs],
        *[each[None] for each in in_biases],
        *after,
        *reads,
    )
    return (
        found[0],
        found[1 : 1 + cores],
        found[1 + cores : 5 + cores],
        found[5 + cores : 4 + 2 * cores],
        found[4 + 2 * cores] if reach else None,
        (found[-1],),
    )


def head_and_loss(stream, head_weight, codes, after=()):
    rows, width = stream.shape
    classes = head_weight.shape[1]
    padded = jnp.pad(head_weight, ((0, 0), (0, 128 - classes)))
    cuts = row_chunks(rows, 256)

    def kernel(stream_ref, head_ref, code_ref, *refs):
        grad_ref, head_grad_ref, sums_ref, token_ref = refs[-4:]
        token_ref[...] = jnp.zeros(TOKEN.shape, TOKEN.dtype)
        head_grad = jnp.zeros((128, width), jnp.float32)
        objective = jnp.zeros((1, 1), jnp.float32)
        scored = jnp.zeros((1, 1), jnp.float32)
        for at, size in cuts:
            some = pl.ds(at, size)
            value = stream_ref[some, :]
            code = code_ref[some, :]
            mask = jnp.where(code[:, :1] >= classes, 1.0, 0.0)
            logits = jnp.dot(
                value, head_ref[...], precision=HIGHEST_PRECISION, preferred_element_type=jnp.float32
            )
            lane = lax.broadcasted_iota(jnp.int32, logits.shape, 1)
            valid = lane < classes
            peak = jnp.max(jnp.where(valid, logits, -jnp.inf), -1, keepdims=True)
            exponent = jnp.where(valid, jnp.exp(jnp.where(valid, logits - peak, 0.0)), 0.0)
            denominator = jnp.sum(exponent, -1, keepdims=True)
            chosen = lane == jnp.where(code >= classes, code - classes, code)
            picked = jnp.sum(jnp.where(chosen, logits, 0.0), -1, keepdims=True)
            terms = mask * (peak + jnp.log(denominator) - picked)
            objective = objective + jnp.sum(terms, 0, keepdims=True)
            scored = scored + jnp.sum(mask, 0, keepdims=True)
            logit_grad = mask * (exponent / denominator - jnp.where(chosen, 1.0, 0.0))
            grad_ref[some, :] = lax.dot_general(
                logit_grad,
                head_ref[...],
                (((1,), (1,)), ((), ())),
                precision=HIGHEST_PRECISION,
                preferred_element_type=jnp.float32,
            )
            head_grad = head_grad + lax.dot_general(
                logit_grad,
                value,
                (((0,), (0,)), ((), ())),
                precision=HIGHEST_PRECISION,
                preferred_element_type=jnp.float32,
            )
        head_grad_ref[...] = head_grad[: head_grad_ref.shape[0]]
        at_row = lax.broadcasted_iota(jnp.int32, sums_ref.shape, 0)
        sums_ref[...] = jnp.where(at_row == 0, objective, scored)

    found = pl.pallas_call(
        kernel,
        out_shape=[
            jax.ShapeDtypeStruct((rows, width), jnp.float32),
            jax.ShapeDtypeStruct((-(-classes // 8) * 8, width), jnp.float32),
            jax.ShapeDtypeStruct((8, 128), jnp.float32),
            TOKEN,
        ],
        compiler_params=pltpu.CompilerParams(vmem_limit_bytes=VMEM_BYTES),
        cost_estimate=cost(6),
        name="head_and_loss",
    )(stream, padded, codes, *after)
    return found[:3], (found[3],)


def ffn_back_hidden(upstream, normed, scale, gain, outs, slopes, after=()):
    rows, width = upstream.shape
    cores = len(outs)
    units = outs[0].shape[0]
    block = min(units, 256)

    def kernel(upstream_ref, normed_ref, scale_ref, gain_ref, *refs):
        out_refs, slope_refs = refs[:cores], refs[cores : 2 * cores]
        found_refs = refs[-3 - 2 * cores :]
        output_grad_ref, hidden_ref = found_refs[:2]
        bias_refs, packet_refs = found_refs[2 : 2 + cores], found_refs[2 + cores : -2]
        sums_ref, token_ref = found_refs[-2:]
        token_ref[...] = jnp.zeros(TOKEN.shape, TOKEN.dtype)
        lane = pl.multiple_of(width + pl.program_id(0) * block, block)

        @pl.when(pl.program_id(0) == 0)
        def _():
            totals = [jnp.zeros((1, width), jnp.float32)] * 3
            for at, size in row_chunks(rows, 128):
                some = pl.ds(at, size)
                grad, value = upstream_ref[some, :], wide(normed_ref[some, :])
                output_grad = low(norm_back(grad * gain_ref[...], value, scale_ref[some, :1]))
                output_grad_ref[some, :] = output_grad
                for packet_ref in packet_refs:
                    packet_ref[some, :width] = output_grad
                for i, each in enumerate((grad * value, grad, wide(output_grad))):
                    totals[i] = totals[i] + jnp.sum(each, 0, keepdims=True)
            sums_ref[...] = jnp.zeros(sums_ref.shape, jnp.float32)
            for i in range(3):
                sums_ref[i : i + 1, :] = totals[i]

        for c in range(cores):
            total = jnp.zeros((1, block), jnp.float32)
            for at, size in row_chunks(rows, 512):
                some = pl.ds(at, size)
                active_grad = lax.dot_general(
                    output_grad_ref[some, :],
                    out_refs[c][...],
                    (((1,), (1,)), ((), ())),
                    preferred_element_type=jnp.float32,
                )
                hidden_grad = low(active_grad * wide(slope_refs[c][some, :]))
                if c == 0:
                    hidden_ref[some, :] = hidden_grad
                else:
                    packet_refs[c - 1][some, pl.ds(lane, block)] = hidden_grad
                total = total + jnp.sum(wide(hidden_grad), 0, keepdims=True)
            bias_refs[c][...] = total

    whole = pl.BlockSpec((rows, width), lambda g: (0, 0))
    columns = pl.BlockSpec((rows, block), lambda g: (0, g))
    found = pl.pallas_call(
        kernel,
        grid=(units // block,),
        in_specs=[
            whole,
            whole,
            pl.BlockSpec((rows, 128), lambda g: (0, 0)),
            pl.BlockSpec((1, width), lambda g: (0, 0)),
        ]
        + [pl.BlockSpec((block, width), lambda g: (g, 0))] * cores
        + [columns] * cores
        + tokens(after),
        out_specs=[whole, columns]
        + [pl.BlockSpec((1, block), lambda g: (0, g))] * cores
        + [pl.BlockSpec((rows, width + units), lambda g: (0, 0))] * (cores - 1)
        + [pl.BlockSpec((8, width), lambda g: (0, 0)), TOKEN_SPEC],
        out_shape=[
            jax.ShapeDtypeStruct((rows, width), jnp.bfloat16),
            pltpu.HBM((rows, units), jnp.bfloat16),
        ]
        + [jax.ShapeDtypeStruct((1, units), jnp.float32)] * cores
        + [jax.ShapeDtypeStruct((rows, width + units), jnp.bfloat16)] * (cores - 1)
        + [jax.ShapeDtypeStruct((8, width), jnp.float32), TOKEN],
        compiler_params=pltpu.CompilerParams(vmem_limit_bytes=VMEM_BYTES),
        cost_estimate=cost(6),
        name="ffn_back_hidden",
    )(
        upstream,
        in_hbm(normed),
        in_hbm(scale),
        gain[None],
        *[in_hbm(each) for each in outs],
        *[in_hbm(each) for each in slopes],
        *after,
    )
    return (
        found[0],
        found[1],
        found[2 : 2 + cores],
        found[2 + cores : -2],
        found[-2],
        (found[-1],),
    )


def ffn_back_stream(
    upstream, hidden, packets, ins, normed, slope, gain, places, reach, after=(), reads=(), relay=False
):
    rows, width = upstream.shape
    cores = len(ins)
    units = ins[0].shape[0]
    block = min(units, 256)
    steps = units // block
    lanes = width // cores
    relays = cores - 1 if relay else 0
    rims_out = 1 if reach else 0

    def kernel(core_ref, upstream_ref, normed_ref, slope_ref, gain_ref, *refs):
        hidden_refs, in_refs = refs[:cores], refs[cores : 2 * cores]
        found_refs = refs[-4 - cores - relays - rims_out :]
        mid_ref, conv_grad_ref = found_refs[:2]
        cut_refs = found_refs[2 : 1 + cores]
        sums_ref, token_ref, total_ref = found_refs[-3:]
        token_ref[...] = jnp.zeros(TOKEN.shape, TOKEN.dtype)
        for i in range(relays):
            relay_ref = found_refs[1 + cores + i]
            lane = pl.multiple_of(width + pl.program_id(0) * block, block)
            relay_ref[:, pl.ds(lane, block)] = hidden_refs[1 + i][...]

            @pl.when(pl.program_id(0) == 0)
            def _(i=i, relay_ref=relay_ref):
                relay_ref[:, :width] = refs[2 * cores + i][...]

        @pl.when(pl.program_id(0) == 0)
        def _():
            total_ref[...] = upstream_ref[...]

        for at, size in row_chunks(rows, 512):
            some = pl.ds(at, size)
            total_ref[some, :] += sum(
                jnp.dot(
                    hidden_refs[c][some, :], in_refs[c][...], preferred_element_type=jnp.float32
                )
                for c in range(cores)
            )

        @pl.when(pl.program_id(0) == steps - 1)
        def _():
            totals = [jnp.zeros((1, width), jnp.float32)] * 3
            for at, size in row_chunks(rows, 128):
                some = pl.ds(at, size)
                grad, value = total_ref[some, :], wide(normed_ref[some, :])
                conv_grad = low(norm_back(grad * gain_ref[...], value, wide(slope_ref[some, :])))
                mid_ref[some, :] = grad
                conv_grad_ref[some, :] = conv_grad
                for i, each in enumerate((grad * value, grad, wide(conv_grad))):
                    totals[i] = totals[i] + jnp.sum(each, 0, keepdims=True)
            sums_ref[...] = jnp.zeros(sums_ref.shape, jnp.float32)
            for i in range(3):
                sums_ref[i : i + 1, :] = totals[i]
            for c in range(1, cores):
                first = lax.rem(core_ref[0] - c + cores, cores) * lanes
                cut_refs[c - 1][...] = conv_grad_ref[:, pl.ds(pl.multiple_of(first, lanes), lanes)]
            if reach:
                first = pl.multiple_of((1 - core_ref[1]) * (rows - reach), ROW_TILE)
                found_refs[-4][...] = conv_grad_ref[pl.ds(first, reach), :]

    whole = pl.BlockSpec((rows, width), lambda g, core: (0, 0))
    found = pl.pallas_call(
        kernel,
        grid_spec=pltpu.PrefetchScalarGridSpec(
            num_scalar_prefetch=1,
            grid=(steps,),
            in_specs=[whole, whole, whole, pl.BlockSpec((1, width), lambda g, core: (0, 0))]
            + [pl.BlockSpec((rows, block), lambda g, core: (0, g))]
            + [pl.BlockSpec((rows, block), lambda g, core: (0, width // block + g))] * (cores - 1)
            + [pl.BlockSpec((block, width), lambda g, core: (g, 0))] * cores
            + [whole] * relays
            + tokens(after)
            + [ANYWHERE] * len(reads),
            out_specs=[whole, whole]
            + [pl.BlockSpec((rows, lanes), lambda g, core: (0, 0))] * (cores - 1)
            + [pl.BlockSpec((rows, width + units), lambda g, core: (0, 0))] * relays
            + [pl.BlockSpec((reach, width), lambda g, core: (0, 0))] * rims_out
            + [pl.BlockSpec((8, width), lambda g, core: (0, 0)), TOKEN_SPEC],
            scratch_shapes=[pltpu.VMEM((rows, width), jnp.float32)],
        ),
        out_shape=[
            jax.ShapeDtypeStruct((rows, width), jnp.float32),
            jax.ShapeDtypeStruct((rows, width), jnp.bfloat16),
        ]
        + [jax.ShapeDtypeStruct((rows, lanes), jnp.bfloat16)] * (cores - 1)
        + [jax.ShapeDtypeStruct((rows, width + units), jnp.bfloat16)] * relays
        + [jax.ShapeDtypeStruct((reach, width), jnp.bfloat16)] * rims_out
        + [jax.ShapeDtypeStruct((8, width), jnp.float32), TOKEN],
        compiler_params=pltpu.CompilerParams(vmem_limit_bytes=VMEM_BYTES),
        cost_estimate=cost(5),
        name="ffn_back_stream",
    )(
        jnp.stack(places[:2]).astype(jnp.int32),
        upstream,
        in_hbm(normed),
        in_hbm(slope),
        gain[None],
        in_hbm(hidden),
        *packets,
        *[in_hbm(each) for each in ins],
        *packets[:relays],
        *after,
        *reads,
    )
    return (
        found[0],
        found[1],
        found[2 : 1 + cores],
        found[1 + cores : 1 + cores + relays],
        found[1 + cores + relays] if reach else None,
        found[-2],
        (found[-1],),
    )


def conv_data_grad(extended, weight, upstream, step, kind, after=()):
    taps, inner, width = weight.shape
    rows = upstream.shape[0]
    group = tap_groups(taps)
    steps = taps // group

    def kernel(extended_ref, weight_ref, upstream_ref, *refs):
        out_ref, token_ref, total_ref = refs[-3:]
        token_ref[...] = jnp.zeros(TOKEN.shape, TOKEN.dtype)
        first = pl.program_id(0) * group
        total = None
        for j in range(group):
            start = pl.multiple_of((taps - 1 - first - j) * step, ROW_TILE)
            term = lax.dot_general(
                extended_ref[pl.ds(start, rows), :],
                weight_ref[j],
                (((1,), (1,)), ((), ())),
                preferred_element_type=jnp.float32,
            )
            total = term if total is None else total + term

        @pl.when(pl.program_id(0) == 0)
        def _():
            total_ref[...] = total

        @pl.when(pl.program_id(0) > 0)
        def _():
            total_ref[...] += total

        @pl.when(pl.program_id(0) == steps - 1)
        def _():
            out_ref[...] = (upstream_ref[...] + wide(low(total_ref[...]))).astype(kind)

    whole = pl.BlockSpec((rows, inner), lambda g: (0, 0))
    found = pl.pallas_call(
        kernel,
        grid=(steps,),
        in_specs=[
            pl.BlockSpec(extended.shape, lambda g: (0, 0)),
            pl.BlockSpec((group, inner, width), lambda g: (g, 0, 0)),
            whole,
        ]
        + tokens(after),
        out_specs=(whole, TOKEN_SPEC),
        out_shape=(jax.ShapeDtypeStruct((rows, inner), kind), TOKEN),
        scratch_shapes=[pltpu.VMEM((rows, inner), jnp.float32)],
        compiler_params=pltpu.CompilerParams(vmem_limit_bytes=VMEM_BYTES),
        cost_estimate=cost(6),
        name="conv_data_grad",
    )(extended, in_hbm(weight), upstream, *after)
    return found[0], (found[1],)


def hold(arrays, after, reads=()):
    count = len(arrays)
    if count == 0:
        return [], after

    def kernel(*refs):
        refs[-1][...] = jnp.zeros(TOKEN.shape, TOKEN.dtype)

    found = pl.pallas_call(
        kernel,
        in_specs=[ANYWHERE] * (count + len(reads)) + [WHOLE] * len(after),
        out_specs=[ANYWHERE] * count + [WHOLE],
        out_shape=[jax.ShapeDtypeStruct(each.shape, each.dtype) for each in arrays] + [TOKEN],
        input_output_aliases={i: i for i in range(count)},
        compiler_params=pltpu.CompilerParams(vmem_limit_bytes=1 * MIB),
        cost_estimate=cost(0.5),
        name="hold",
    )(*arrays, *reads, *after)
    return list(found[:-1]), (found[-1],)


def join_rows(parts, after=(), reads=()):
    def kernel(*refs):
        out_ref, token_ref = refs[-2:]
        token_ref[...] = jnp.zeros(TOKEN.shape, TOKEN.dtype)
        first = 0
        for i, part in enumerate(parts):
            out_ref[first : first + part.shape[0]] = refs[i][...]
            first += part.shape[0]

    shape = (sum(part.shape[0] for part in parts), parts[0].shape[1])
    found = pl.pallas_call(
        kernel,
        in_specs=[WHOLE] * len(parts) + [ANYWHERE] * len(reads) + [WHOLE] * len(after),
        out_specs=[WHOLE] * 2,
        out_shape=[jax.ShapeDtypeStruct(shape, parts[0].dtype), TOKEN],
        compiler_params=pltpu.CompilerParams(vmem_limit_bytes=10 * MIB),
        cost_estimate=cost(1.5),
        name="join_rows",
    )(*parts, *reads, *after)
    return found[0], (found[1],)


def restack(groups, reads=(), after=(), fixed=False):
    cuts = [cut for _, each in groups for cut in each]
    if any(last is not None and (first % ROW_TILE or last % ROW_TILE) for first, last, _ in cuts):
        return [
            jnp.stack([array[first:last].reshape(shape) for array in arrays])
            for arrays, each in groups
            for first, last, shape in each
        ], after
    flat = [array for arrays, _ in groups for array in arrays]
    plan = []
    shapes = []
    at = 0
    for arrays, each in groups:
        for first, last, shape in each:
            for slot in range(len(arrays)):
                plan.append((at + slot, first, last, len(shapes), slot))
            held = shape if last is None else (last - first,) + arrays[0].shape[1:]
            shapes.append(jax.ShapeDtypeStruct((len(arrays),) + held, arrays[0].dtype))
        at += len(arrays)

    def kernel(*refs):
        out_refs = refs[-2 - len(shapes) : -2]
        token_ref, sem_ref = refs[-2:]
        token_ref[...] = jnp.zeros(TOKEN.shape, TOKEN.dtype)
        copies = []
        for source, first, last, target, slot in plan:
            ref = refs[source]
            copies.append(
                pltpu.make_async_copy(
                    ref if last is None else ref.at[pl.ds(first, last - first)],
                    out_refs[target].at[slot],
                    sem_ref.at[len(copies)],
                )
            )
        copy_all(copies)

    found = pl.pallas_call(
        kernel,
        in_specs=[ANYWHERE] * (len(flat) + len(reads)) + [WHOLE] * len(after),
        out_specs=[WHOLE] * (len(shapes) + 1),
        out_shape=shapes + [TOKEN],
        scratch_shapes=[pltpu.SemaphoreType.DMA((len(plan),))],
        compiler_params=pltpu.CompilerParams(vmem_limit_bytes=10 * MIB),
        cost_estimate=cost(1.5),
        name="restack",
    )(*([in_hbm(each) for each in flat] if fixed else flat), *reads, *after)
    return [
        each.reshape((each.shape[0],) + shape) for each, (_, _, shape) in zip(found, cuts)
    ], (found[-1],)


def conv_weight_grad(
    extendeds, upstream, arrived, places, sizes, taps, step, after=(), reads=()
):
    cores, seqs, acrosses, tap_peers = sizes
    rows = upstream.shape[0]
    inner = extendeds[0].shape[1]
    lanes = upstream.shape[1] // cores
    slab = inner // (seqs * acrosses * tap_peers)
    direct = slab % ROW_TILE == 0
    half = (tap_peers + 1) // 2
    rest = tap_peers - half
    seconds = acrosses if rest else 0
    outs = seqs + seconds if direct else 1

    def kernel(place_ref, *refs):
        out_refs = refs[-2 - outs : -2]
        token_ref, found_ref = refs[-2:]
        token_ref[...] = jnp.zeros(TOKEN.shape, TOKEN.dtype)
        start = pl.multiple_of(pl.program_id(0) * step, ROW_TILE)
        found = low(
            sum(
                lax.dot_general(
                    refs[c][pl.ds(start, rows), :],
                    refs[cores + c][...],
                    (((0,), (0,)), ((), ())),
                    preferred_element_type=jnp.float32,
                )
                for c in range(cores)
            )
        )
        if not direct:
            out_refs[0][0] = found
            return
        found_ref[...] = found

        def chunk(slot_t, slot_s, slot_a):
            t = lax.rem(place_ref[3] - slot_t + tap_peers, tap_peers)
            at = lax.rem(place_ref[1] - slot_s + seqs, seqs)
            a = lax.rem(place_ref[2] - slot_a + acrosses, acrosses)
            first = pl.multiple_of(((t * seqs + at) * acrosses + a) * slab, slab)
            return found_ref[pl.ds(first, slab), :]

        for s in range(seqs):
            for a in range(acrosses):
                for t in range(half):
                    out_refs[s][a, t, 0] = chunk(t, s, a)
                for t in range(half, tap_peers):
                    out_refs[seqs + a][s, t - half, 0] = chunk(t, s, a)

    if direct:
        shapes = [(acrosses, half, taps, slab, lanes)] * seqs
        shapes += [(seqs, rest, taps, slab, lanes)] * seconds
        specs = [
            pl.BlockSpec(shape[:2] + (1, slab, lanes), lambda k, place: (0, 0, k, 0, 0))
            for shape in shapes
        ]
    else:
        shapes = [(taps, inner, lanes)]
        specs = [pl.BlockSpec((1, inner, lanes), lambda k, place: (k, 0, 0))]
    found = pl.pallas_call(
        kernel,
        grid_spec=pltpu.PrefetchScalarGridSpec(
            num_scalar_prefetch=1,
            grid=(taps,),
            in_specs=[pl.BlockSpec(extendeds[0].shape, lambda k, place: (0, 0))] * cores
            + [pl.BlockSpec((rows, lanes), lambda k, place: (0, place[0]))]
            + [pl.BlockSpec((rows, lanes), lambda k, place: (0, 0))] * (cores - 1)
            + tokens(after)
            + [ANYWHERE] * len(reads),
            out_specs=specs + [TOKEN_SPEC],
            scratch_shapes=[pltpu.VMEM((inner, lanes), jnp.bfloat16)],
        ),
        out_shape=[jax.ShapeDtypeStruct(shape, jnp.bfloat16) for shape in shapes] + [TOKEN],
        compiler_params=pltpu.CompilerParams(vmem_limit_bytes=VMEM_BYTES),
        cost_estimate=cost(9),
        name="conv_weight_grad",
    )(jnp.stack(places).astype(jnp.int32), *extendeds, upstream, *arrived, *after, *reads)
    token = found[-1]
    if not direct:
        found = found[0].reshape(taps, tap_peers, seqs, acrosses, slab, lanes)
        for axis, which in ((1, 3), (2, 1), (3, 2)):
            found = relative(found, axis, places[which], sizes[which])
        found = found.transpose(2, 3, 1, 0, 4, 5)
        found = [found[s, :, :half] for s in range(seqs)] + [
            found[:, a, half:] for a in range(seconds)
        ]
    flat = [each.reshape(-1, lanes) for each in found[: seqs + seconds]]
    return flat[:seqs], flat[seqs:], token


def ffn_weight_grad(pairs, sizes, ffn_rows, after=()):
    cores, seqs, acrosses, tap_peers = sizes
    rows, width = pairs[0][1].shape
    block = tap_peers * ffn_rows
    half = (tap_peers + 1) // 2
    rest = tap_peers - half
    seconds = seqs if rest else 0
    transposed = (((0,), (0,)), ((), ()))
    if ffn_rows % ROW_TILE:
        found = jnp.stack(
            [
                low(
                    sum(
                        lax.dot_general(a, b, transposed, preferred_element_type=jnp.float32)
                        for a, b in [(left, right)]
                        + [(ends[:, width:], starts[:, :width]) for ends, starts in packets]
                    )
                ).reshape(acrosses, seqs, tap_peers, ffn_rows, width)
                for left, right, packets in pairs
            ],
            3,
        )
        token = jnp.zeros(TOKEN.shape, TOKEN.dtype)
        return (
            [found[a, :, :half].reshape(-1, width) for a in range(acrosses)],
            [found[:, s, half:].reshape(-1, width) for s in range(seconds)],
            token,
        )
    outs = acrosses + seconds

    def kernel(*refs):
        out_refs, token_ref = refs[-1 - outs : -1], refs[-1]
        token_ref[...] = jnp.zeros(TOKEN.shape, TOKEN.dtype)
        step = pl.program_id(0)
        for which in range(2):
            base = 2 * cores * which
            found = low(
                sum(
                    lax.dot_general(
                        refs[base + 2 * c][...],
                        refs[base + 2 * c + 1][...],
                        transposed,
                        preferred_element_type=jnp.float32,
                    )
                    for c in range(cores)
                )
            ).reshape(tap_peers, ffn_rows, width)
            for a in range(acrosses):

                @pl.when(step // seqs == a)
                def _(a=a):
                    out_refs[a][0, :, which] = found[:half]

            for s in range(seconds):

                @pl.when(lax.rem(step, seqs) == s)
                def _(s=s):
                    out_refs[acrosses + s][0, :, which] = found[half:]

    right_spec = pl.BlockSpec((rows, width), lambda g: (0, 0))
    left_spec = pl.BlockSpec((rows, block), lambda g: (0, g))
    late_spec = pl.BlockSpec((rows, block), lambda g: (0, width // block + g))

    def first_spec(a):
        return pl.BlockSpec(
            (1, half, 2, ffn_rows, width),
            lambda g: (jnp.clip(g - a * seqs, 0, seqs - 1), 0, 0, 0, 0),
        )

    second_spec = pl.BlockSpec(
        (1, rest, 2, ffn_rows, width), lambda g: (g // seqs, 0, 0, 0, 0)
    )
    operands = []
    for left, right, packets in pairs:
        operands += [in_hbm(left), right]
        for ends, starts in packets:
            operands += [ends, starts]
    found = pl.pallas_call(
        kernel,
        grid=(acrosses * seqs,),
        in_specs=([left_spec, right_spec] + [late_spec, right_spec] * (cores - 1)) * 2
        + tokens(after),
        out_specs=[first_spec(a) for a in range(acrosses)]
        + [second_spec] * seconds
        + [TOKEN_SPEC],
        out_shape=[jax.ShapeDtypeStruct((seqs, half, 2, ffn_rows, width), jnp.bfloat16)] * acrosses
        + [jax.ShapeDtypeStruct((acrosses, rest, 2, ffn_rows, width), jnp.bfloat16)] * seconds
        + [TOKEN],
        compiler_params=pltpu.CompilerParams(vmem_limit_bytes=VMEM_BYTES),
        cost_estimate=cost(8),
        name="ffn_weight_grad",
    )(*operands, *after)
    flat = [each.reshape(-1, width) for each in found[:-1]]
    return flat[:acrosses], flat[acrosses:], found[-1]


def group_slots(groups, lanes):
    flat, where = [], []
    rows = groups[0][0][0].size // (groups[0][1] * lanes)
    for parts, slots in groups:
        where += [(len(flat), len(parts), slot) for slot in range(slots)]
        flat += [part.reshape(slots, rows, lanes) for part in parts]
    return flat, where, rows


def slot_sum(refs, place, first=0):
    start, count, at = place
    return low(sum(wide(refs[first + start + i][at]) for i in range(count)))


def merge_slots(conv_groups, ffn_groups, after=()):
    lanes, width = conv_groups[0][0][0].shape[-1], ffn_groups[0][0][0].shape[-1]
    cuts = width // lanes
    conv_parts, conv_where, conv_rows = group_slots(conv_groups, lanes)
    ffn_parts, ffn_where, ffn_rows = group_slots(ffn_groups, width)
    slots = len(conv_where)
    if conv_rows % ROW_TILE or ffn_rows % ROW_TILE:
        merged = []
        for slot in range(slots):
            ffn = slot_sum(ffn_parts, ffn_where[slot])
            merged.append(
                jnp.concatenate(
                    [slot_sum(conv_parts, conv_where[slot])]
                    + [ffn[:, i * lanes : (i + 1) * lanes] for i in range(cuts)]
                )
            )
        return merged, after

    def kernel(*refs):
        out_refs, token_ref = refs[-1 - slots : -1], refs[-1]
        token_ref[...] = jnp.zeros(TOKEN.shape, TOKEN.dtype)
        for slot in range(slots):
            out_refs[slot][:conv_rows] = slot_sum(refs, conv_where[slot])
            ffn = slot_sum(refs, ffn_where[slot], len(conv_parts))
            for i in range(cuts):
                first = conv_rows + i * ffn_rows
                out_refs[slot][first : first + ffn_rows] = ffn[:, i * lanes : (i + 1) * lanes]

    found = pl.pallas_call(
        kernel,
        in_specs=[WHOLE] * (len(conv_parts) + len(ffn_parts) + len(after)),
        out_specs=[WHOLE] * (slots + 1),
        out_shape=[jax.ShapeDtypeStruct((conv_rows + cuts * ffn_rows, lanes), jnp.bfloat16)] * slots
        + [TOKEN],
        compiler_params=pltpu.CompilerParams(vmem_limit_bytes=10 * MIB),
        cost_estimate=cost(1.5),
        name="merge_slots",
    )(*conv_parts, *ffn_parts, *after)
    return found[:slots], (found[slots],)


def append_slots(groups, packed, after=(), reads=()):
    lanes = groups[0][0][0].shape[-1]
    parts, where, rows = group_slots(groups, lanes)
    slots = len(where)
    if rows % ROW_TILE:
        return [
            jnp.concatenate([slot_sum(parts, where[slot])] + packed) for slot in range(slots)
        ], after

    def kernel(*refs):
        out_refs, token_ref = refs[-1 - slots : -1], refs[-1]
        token_ref[...] = jnp.zeros(TOKEN.shape, TOKEN.dtype)
        for slot in range(slots):
            out_refs[slot][:rows] = slot_sum(refs, where[slot])
            if packed:
                out_refs[slot][rows:] = refs[len(parts)][...]

    shape = jax.ShapeDtypeStruct((rows + sum(each.shape[0] for each in packed), lanes), jnp.bfloat16)
    found = pl.pallas_call(
        kernel,
        in_specs=[WHOLE] * (len(packed) + len(parts) + len(after)) + [ANYWHERE] * len(reads),
        out_specs=[WHOLE] * (slots + 1),
        out_shape=[shape] * slots + [TOKEN],
        compiler_params=pltpu.CompilerParams(vmem_limit_bytes=8 * MIB),
        cost_estimate=cost(1),
        name="append_slots",
    )(*parts, *packed, *after, *reads)
    return found[:slots], (found[slots],)


def pack_small(row_groups, biases, losses, places, sizes, ffn_rows, after=(), reads=()):
    cores, seqs, acrosses, tap_peers = sizes
    width = row_groups[0][0].shape[1]
    head_rows = sum(count for _, count in row_groups)
    hidden = cores * biases[0][0].shape[1]
    bias_rows = hidden // width
    used = head_rows + len(biases) * bias_rows + 2
    rows = -(-used // ROW_TILE) * ROW_TILE
    lanes = width // 2
    per_row = width // ffn_rows
    if ffn_rows % 64:
        terms = jnp.stack([losses[0, 0], losses[1, 0]])
        terms = jnp.stack([terms, terms - wide(low(terms))])
        pieces = [array[:count] for array, count in row_groups]
        for each in biases:
            bias = jnp.stack(each).reshape(cores, acrosses, seqs, tap_peers, ffn_rows)
            for axis, which in enumerate((0, 2, 1, 3)):
                bias = relative(bias, axis, places[which], sizes[which])
            pieces.append(bias.transpose(1, 0, 2, 3, 4).reshape(-1, width))
        pieces.append(jnp.pad(terms, ((0, rows - used), (0, width - 2))))
        packed = low(jnp.concatenate(pieces))
        return jnp.concatenate([packed[:, :lanes], packed[:, lanes:]]), after

    def kernel(place_ref, *refs):
        packed_ref, token_ref, rows_ref = refs[-3:]
        token_ref[...] = jnp.zeros(TOKEN.shape, TOKEN.dtype)
        rows_ref[...] = jnp.zeros(rows_ref.shape, jnp.float32)
        at = 0
        for i, (_, count) in enumerate(row_groups):
            rows_ref[at : at + count, :] = refs[i][:count, :]
            at += count
        shape = (cores, acrosses, seqs, tap_peers)
        owners = (0, 2, 1, 3)
        for b in range(len(biases)):
            blocks = {}
            for slot in np.ndindex(*shape):
                first = ((slot[1] * seqs + slot[2]) * tap_peers + slot[3]) * ffn_rows
                ref = refs[len(row_groups) + b * cores + slot[0]]
                blocks[slot] = ref[:, first : first + ffn_rows]
            for axis, size in enumerate(shape):
                turned = {}
                for slot in blocks:
                    place = lax.rem(place_ref[owners[axis]] - slot[axis] + size, size)
                    value = blocks[slot[:axis] + (0,) + slot[axis + 1 :]]
                    for other in range(1, size):
                        candidate = blocks[slot[:axis] + (other,) + slot[axis + 1 :]]
                        value = jnp.where(place == other, candidate, value)
                    turned[slot] = value
                blocks = turned
            ordered = [
                blocks[(c, a, s, t)]
                for a in range(acrosses)
                for c in range(cores)
                for s in range(seqs)
                for t in range(tap_peers)
            ]
            for row in range(bias_rows):
                line = ordered[row * per_row : (row + 1) * per_row]
                rows_ref[at : at + 1, :] = jnp.concatenate(line, 1)
                at += 1
        losses_ref = refs[len(row_groups) + len(biases) * cores]
        lane = lax.broadcasted_iota(jnp.int32, (1, width), 1)
        objective = jnp.broadcast_to(losses_ref[0:1, 0:1], (1, width))
        scored = jnp.broadcast_to(losses_ref[1:2, 0:1], (1, width))
        line = jnp.where(lane == 0, objective, jnp.where(lane == 1, scored, 0.0))
        rows_ref[at : at + 1, :] = line
        rows_ref[at + 1 : at + 2, :] = line - wide(low(line))
        packed_ref[:rows, :] = low(rows_ref[:, :lanes])
        packed_ref[rows:, :] = low(rows_ref[:, lanes:])

    flat = [array for array, _ in row_groups] + [each for some in biases for each in some]
    found = pl.pallas_call(
        kernel,
        in_specs=[SCALARS] + [WHOLE] * (len(flat) + 1 + len(after)) + [ANYWHERE] * len(reads),
        out_specs=[WHOLE] * 2,
        out_shape=[jax.ShapeDtypeStruct((2 * rows, lanes), jnp.bfloat16), TOKEN],
        scratch_shapes=[pltpu.VMEM((rows, width), jnp.float32)],
        compiler_params=pltpu.CompilerParams(vmem_limit_bytes=8 * MIB),
        cost_estimate=cost(2),
        name="pack_small",
    )(jnp.stack(places).astype(jnp.int32), *flat, losses, *after, *reads)
    return found[0], (found[1],)


def paired(values):
    while len(values) > 1:
        half = len(values) // 2
        if len(values) % 2:
            return sum(values[1:], values[0])
        values = [values[i] + values[i + half] for i in range(half)]
    return values[0]


def finish_small(stacks, first, width, classes, hidden, places, sizes):
    cores, seqs, acrosses = sizes[:3]
    peers, rows, lanes = stacks[0].shape
    count = rows - first
    bias_rows = hidden // width
    at_bias = 12 + classes
    at_loss = at_bias + 2 * bias_rows

    def pick(row):
        return (
            [row(2), row(5)],
            [[row(0), row(6)], [row(3), row(9)]],
            [[row(1), row(7)], [row(4), row(10)]],
            [[row(at_bias + b * bias_rows + i) for i in range(bias_rows)] for b in range(2)],
            [row(8), row(11)],
        )

    if max(cores, seqs, acrosses) > 2 or first % count or count % ROW_TILE:
        full = jnp.stack(
            [wide(each[:, first:]).reshape(seqs, acrosses, count, lanes) for each in stacks]
        )
        for axis, (place, size) in enumerate(zip(places[:3], sizes[:3])):
            full = relative(full, axis, place, size)
        total = jnp.sum(full, (0, 1, 2))
        total = jnp.concatenate([total[: count // 2], total[count // 2 :]], 1)
        conv_bias, gains, shifts, in_bias, out_bias = pick(lambda i: total[i])
        terms = total[at_loss] + total[at_loss + 1]
        return (
            jnp.stack(conv_bias),
            jnp.stack([jnp.stack(each) for each in gains]),
            jnp.stack([jnp.stack(each) for each in shifts]),
            jnp.stack([jnp.concatenate(each) for each in in_bias]),
            jnp.stack(out_bias),
            total[12:at_bias].T,
            (terms[0] / terms[1]).reshape(1, 1),
        )

    def kernel(*refs):
        conv_ref, gain_ref, shift_ref, in_ref, out_ref, head_ref, loss_ref, rows_ref = refs[cores:]
        total = paired(
            [
                paired(
                    [
                        paired([wide(refs[c][s * acrosses + a]) for a in range(acrosses)])
                        for s in range(seqs)
                    ]
                )
                for c in range(cores)
            ]
        )
        rows_ref[:, :lanes] = total[: count // 2]
        rows_ref[:, lanes:] = total[count // 2 :]
        conv_bias, gains, shifts, in_bias, out_bias = pick(lambda i: rows_ref[i : i + 1, :])
        for b in range(2):
            conv_ref[b : b + 1, :] = conv_bias[b]
            out_ref[b : b + 1, :] = out_bias[b]
            for i in range(2):
                gain_ref[b, i : i + 1, :] = gains[b][i]
                shift_ref[b, i : i + 1, :] = shifts[b][i]
            for i in range(bias_rows):
                in_ref[b : b + 1, i * width : (i + 1) * width] = in_bias[b][i]
        head_ref[...] = rows_ref[12 : 12 + 8 * (-(-classes // 8)), :].T[:, :classes]
        terms = rows_ref[at_loss : at_loss + 1, :128] + rows_ref[at_loss + 1 : at_loss + 2, :128]
        loss_ref[...] = terms[:, 0:1] / terms[:, 1:2]

    return pl.pallas_call(
        kernel,
        grid=(1,),
        in_specs=[pl.BlockSpec((peers, count, lanes), lambda g: (0, first // count, 0))] * cores,
        out_shape=(
            jax.ShapeDtypeStruct((2, width), jnp.float32),
            jax.ShapeDtypeStruct((2, 2, width), jnp.float32),
            jax.ShapeDtypeStruct((2, 2, width), jnp.float32),
            jax.ShapeDtypeStruct((2, hidden), jnp.float32),
            jax.ShapeDtypeStruct((2, width), jnp.float32),
            jax.ShapeDtypeStruct((width, classes), jnp.float32),
            jax.ShapeDtypeStruct((1, 1), jnp.float32),
        ),
        out_specs=[
            pl.BlockSpec((2, width), lambda g: (0, 0)),
            pl.BlockSpec((2, 2, width), lambda g: (0, 0, 0)),
            pl.BlockSpec((2, 2, width), lambda g: (0, 0, 0)),
            pl.BlockSpec((2, hidden), lambda g: (0, 0)),
            pl.BlockSpec((2, width), lambda g: (0, 0)),
            pl.BlockSpec((width, classes), lambda g: (0, 0)),
            pl.BlockSpec((1, 1), lambda g: (0, 0)),
        ],
        scratch_shapes=[pltpu.VMEM((count // 2, 2 * lanes), jnp.float32)],
        compiler_params=pltpu.CompilerParams(vmem_limit_bytes=4 * MIB),
        cost_estimate=cost(1.5),
        name="finish_small",
    )(*stacks)


def finish_conv(parts, conv_rows, small_rows, after=()):
    blocks, count = len(parts), len(parts[0])
    lanes = parts[0][0].shape[-1]
    flat = [part for block in parts for part in block]
    if conv_rows % ROW_TILE:
        sums = [sum(wide(part[:conv_rows]) for part in block) for block in parts]
        sums.append(paired([wide(part[conv_rows:]) for part in parts[0]]))
        return jnp.concatenate([low(total) for total in sums]), after

    def kernel(*refs):
        shard_ref, token_ref = refs[-2:]
        token_ref[...] = jnp.zeros(TOKEN.shape, TOKEN.dtype)
        shard_ref[blocks * conv_rows :] = low(
            paired([wide(refs[i][conv_rows:]) for i in range(count)])
        )
        for b in range(blocks):
            total = sum(wide(refs[b * count + i][:conv_rows]) for i in range(count))
            shard_ref[b * conv_rows : (b + 1) * conv_rows] = low(total)

    found = pl.pallas_call(
        kernel,
        in_specs=[WHOLE] * (len(flat) + len(after)),
        out_specs=[WHOLE] * 2,
        out_shape=[
            jax.ShapeDtypeStruct((blocks * conv_rows + small_rows, lanes), jnp.bfloat16),
            TOKEN,
        ],
        compiler_params=pltpu.CompilerParams(vmem_limit_bytes=8 * MIB),
        cost_estimate=cost(1.2),
        name="finish_conv",
    )(*flat, *after)
    return found[0], (found[1],)


def finish_ffn(merged, plain, conv_rows, ffn_rows, after=()):
    lanes, width = merged[0].shape[-1], plain[0].shape[-1]

    def cut_back(total):
        size = 2 * ffn_rows
        return jnp.concatenate(
            [total[i * size : (i + 1) * size] for i in range(width // lanes)], 1
        )

    if conv_rows % ROW_TILE or ffn_rows % ROW_TILE:
        sums = [sum(wide(part) for part in plain)]
        sums.append(cut_back(sum(wide(part[conv_rows:]) for part in merged)))
        return jnp.stack([each[:ffn_rows].T for each in sums]), jnp.stack(
            [each[ffn_rows:] for each in sums]
        ), after

    def kernel(*refs):
        in_ref, out_ref, token_ref = refs[-3:]
        token_ref[...] = jnp.zeros(TOKEN.shape, TOKEN.dtype)
        late = sum(wide(refs[i][conv_rows:]) for i in range(len(merged)))
        sums = [sum(wide(refs[len(merged) + i][...]) for i in range(len(plain))), cut_back(late)]
        for b in range(2):
            in_ref[b] = sums[b][:ffn_rows].T
            out_ref[b] = sums[b][ffn_rows:]

    found = pl.pallas_call(
        kernel,
        in_specs=[WHOLE] * (len(merged) + len(plain) + len(after)),
        out_specs=[WHOLE] * 3,
        out_shape=(
            jax.ShapeDtypeStruct((2, width, ffn_rows), jnp.float32),
            jax.ShapeDtypeStruct((2, ffn_rows, width), jnp.float32),
            TOKEN,
        ),
        compiler_params=pltpu.CompilerParams(vmem_limit_bytes=8 * MIB),
        cost_estimate=cost(1),
        name="finish_ffn",
    )(*merged, *plain, *after)
    return found[0], found[1], (found[2],)


def add_slots(parts, slots, after=(), reads=()):
    lanes = parts[0].shape[-1]
    rows = parts[0].size // (slots * lanes)
    parts = [part.reshape(slots, rows, lanes) for part in parts]
    block = rows // 4 if rows % (4 * ROW_TILE) == 0 else rows

    def kernel(*refs):
        out_refs, token_ref = refs[-1 - slots : -1], refs[-1]
        token_ref[...] = jnp.zeros(TOKEN.shape, TOKEN.dtype)
        for slot in range(slots):
            out_refs[slot][...] = low(sum(wide(refs[i][slot]) for i in range(len(parts))))

    found = pl.pallas_call(
        kernel,
        grid=(rows // block,),
        in_specs=[pl.BlockSpec((slots, block, lanes), lambda g: (0, g, 0))] * len(parts)
        + tokens(after)
        + [ANYWHERE] * len(reads),
        out_specs=[pl.BlockSpec((block, lanes), lambda g: (g, 0))] * slots + [TOKEN_SPEC],
        out_shape=[jax.ShapeDtypeStruct((rows, lanes), jnp.bfloat16)] * slots + [TOKEN],
        compiler_params=pltpu.CompilerParams(vmem_limit_bytes=8 * MIB),
        cost_estimate=cost(2),
        name="add_slots",
    )(*parts, *after, *reads)
    return found[:slots], found[slots]


def place_conv_grads(stacks, blocks, taps, slab, places, sizes):
    cores, seqs, acrosses = sizes[:3]
    peers, rows, lanes = stacks[0].shape
    channels = slab * seqs * acrosses
    if slab % ROW_TILE or rows % slab:
        full = jnp.stack([each[:, : blocks * taps * slab] for each in stacks])
        full = full.reshape(cores, seqs, acrosses, blocks, taps, slab, lanes)
        for axis, (place, size) in enumerate(zip(places[:3], sizes[:3])):
            full = relative(full, axis, place, size)
        return wide(
            full.transpose(3, 4, 1, 2, 5, 0, 6).reshape(blocks, taps, channels, cores * lanes)
        )
    stacks = [each.reshape(peers, rows // slab, slab, lanes) for each in stacks]

    def kernel(place_ref, *refs):
        out_ref = refs[-1]
        for c in range(cores):
            lane = pl.multiple_of(lax.rem(place_ref[0] - c + cores, cores) * lanes, lanes)
            for s in range(seqs):
                at_s = lax.rem(place_ref[1] - s + seqs, seqs)
                for a in range(acrosses):
                    at_a = lax.rem(place_ref[2] - a + acrosses, acrosses)
                    row = pl.multiple_of((at_s * acrosses + at_a) * slab, slab)
                    for b in range(blocks):
                        piece = wide(refs[c * blocks + b][s * acrosses + a, 0])
                        out_ref[b, 0, pl.ds(row, slab), pl.ds(lane, lanes)] = piece

    specs = [
        pl.BlockSpec((peers, 1, slab, lanes), lambda k, place, b=b: (0, b * taps + k, 0, 0))
        for b in range(blocks)
    ]
    return pl.pallas_call(
        kernel,
        grid_spec=pltpu.PrefetchScalarGridSpec(
            num_scalar_prefetch=1,
            grid=(taps,),
            in_specs=specs * cores,
            out_specs=pl.BlockSpec(
                (blocks, 1, channels, cores * lanes), lambda k, place: (0, k, 0, 0)
            ),
        ),
        out_shape=jax.ShapeDtypeStruct((blocks, taps, channels, cores * lanes), jnp.float32),
        compiler_params=pltpu.CompilerParams(vmem_limit_bytes=10 * MIB),
        cost_estimate=cost(5),
        name="place_conv_grads",
    )(
        jnp.stack(places[:3]).astype(jnp.int32),
        *[each for stack in stacks for each in [stack] * blocks],
    )


def copy_all(copies):
    for copy in copies:
        copy.start()
    for copy in copies:
        copy.wait()


def place_conv(pieces, places, sizes, after=(), reads=()):
    cores, seqs, acrosses, tap_peers = sizes
    taps, slab, lanes = pieces[0][0].shape[2:]
    inner = slab * seqs * acrosses * tap_peers
    if slab % ROW_TILE:
        full = jnp.stack([jnp.stack(row) for row in pieces])
        for axis, (place, size) in enumerate(zip(places, sizes)):
            full = relative(full, axis, place, size)
        return full.transpose(4, 3, 1, 2, 5, 0, 6).reshape(taps, inner, cores * lanes), after
    flat = [piece for row in pieces for piece in row]

    def kernel(place_ref, *refs):
        out_ref, token_ref, sem_ref = refs[-3:]
        token_ref[...] = jnp.zeros(TOKEN.shape, TOKEN.dtype)
        copies = []
        for c in range(cores):
            lane = lax.rem(place_ref[0] - c + cores, cores) * lanes
            for s in range(seqs):
                at_s = lax.rem(place_ref[1] - s + seqs, seqs)
                for a in range(acrosses):
                    at_a = lax.rem(place_ref[2] - a + acrosses, acrosses)
                    for t in range(tap_peers):
                        at_t = lax.rem(place_ref[3] - t + tap_peers, tap_peers)
                        row = ((at_t * seqs + at_s) * acrosses + at_a) * slab
                        copies.append(
                            pltpu.make_async_copy(
                                refs[c * seqs + s].at[a, t],
                                out_ref.at[
                                    :,
                                    pl.ds(pl.multiple_of(row, slab), slab),
                                    pl.ds(pl.multiple_of(lane, lanes), lanes),
                                ],
                                sem_ref.at[len(copies)],
                            )
                        )
        copy_all(copies)

    found = pl.pallas_call(
        kernel,
        in_specs=[SCALARS] + [ANYWHERE] * (len(flat) + len(reads)) + [WHOLE] * len(after),
        out_specs=[WHOLE] * 2,
        out_shape=[pltpu.HBM((taps, inner, cores * lanes), jnp.bfloat16), TOKEN],
        scratch_shapes=[pltpu.SemaphoreType.DMA((cores * seqs * acrosses * tap_peers,))],
        compiler_params=pltpu.CompilerParams(vmem_limit_bytes=12 * MIB),
        cost_estimate=cost(3),
        name="place_conv",
    )(jnp.stack(places).astype(jnp.int32), *flat, *reads, *after)
    return found[0], (found[1],)


def place_ffn(pieces, sizes, after=(), reads=()):
    cores, seqs, acrosses, tap_peers = sizes
    cuts, ffn_rows, lanes = pieces[0][0].shape[2:]
    cuts //= 2
    width = cuts * lanes
    units = seqs * acrosses * tap_peers * ffn_rows
    if ffn_rows % ROW_TILE:
        full = jnp.stack([jnp.stack(row) for row in pieces])
        full = full.reshape(cores, acrosses, seqs, tap_peers, 2, cuts, ffn_rows, lanes)
        full = full.transpose(4, 0, 1, 2, 3, 6, 5, 7).reshape(2, cores, units, width)
        return [full[0, c] for c in range(cores)], [full[1, c] for c in range(cores)], after
    flat = [piece for row in pieces for piece in row]

    def kernel(*refs):
        out_refs = refs[-2 - 2 * cores : -2]
        token_ref, sem_ref = refs[-2:]
        token_ref[...] = jnp.zeros(TOKEN.shape, TOKEN.dtype)
        copies = []
        for c in range(cores):
            for a in range(acrosses):
                for which in range(2):
                    for cut in range(cuts):
                        copies.append(
                            pltpu.make_async_copy(
                                refs[c * acrosses + a].at[:, :, which * cuts + cut],
                                out_refs[which * cores + c].at[
                                    a, :, :, :, pl.ds(cut * lanes, lanes)
                                ],
                                sem_ref.at[len(copies)],
                            )
                        )
        copy_all(copies)

    shape = pltpu.HBM((acrosses, seqs, tap_peers, ffn_rows, width), jnp.bfloat16)
    found = pl.pallas_call(
        kernel,
        in_specs=[ANYWHERE] * (len(flat) + len(reads)) + [WHOLE] * len(after),
        out_specs=[WHOLE] * (2 * cores + 1),
        out_shape=[shape] * (2 * cores) + [TOKEN],
        scratch_shapes=[pltpu.SemaphoreType.DMA((2 * cores * acrosses * cuts,))],
        compiler_params=pltpu.CompilerParams(vmem_limit_bytes=12 * MIB),
        cost_estimate=cost(2),
        name="place_ffn",
    )(*flat, *reads, *after)
    token = found[-1]
    found = [each.reshape(units, width) for each in found[:-1]]
    return found[:cores], found[cores:], (token,)


class Ring:
    def __init__(self, axis, size, index, pairs):
        self.axis, self.size, self.index, self.pairs = axis, size, index, pairs

    def shifted(self, value, by):
        return lax.ppermute(value, self.axis, self.pairs(lambda i: (i + by) % self.size))

    def swapped(self, value, bit):
        return lax.ppermute(value, self.axis, self.pairs(lambda i: i ^ bit))

    def gather(self, value):
        return [value] + [self.shifted(value, by) for by in range(1, self.size)]

    def swap(self, values):
        return [values[0]] + [self.shifted(values[by], -by) for by in range(1, self.size)]


def relative(value, axis, place, size):
    if size == 1:
        return value
    return jnp.stack(
        [
            lax.dynamic_index_in_dim(value, (place - slot) % size, axis, False)
            for slot in range(size)
        ],
        axis,
    )


def rings():
    peers = lax.axis_size("dp")
    cores = CORES if peers % CORES == 0 else 1
    columns = peers // cores
    place = lax.axis_index("dp")

    def plain(axis):
        size = lax.axis_size(axis)
        return Ring(
            axis, size, lax.axis_index(axis), lambda move: [(i, move(i)) for i in range(size)]
        )

    across = Ring(
        "dp",
        columns,
        place // cores,
        lambda move: [(i, move(i // cores) * cores + i % cores) for i in range(peers)],
    )
    core = Ring(
        "dp",
        cores,
        place % cores,
        lambda move: [(i, i // cores * cores + move(i % cores)) for i in range(peers)],
    )
    return core, across, plain("seq"), plain("tap")


class Reduce:
    def __init__(self, terms, order):
        self.order = order
        self.parts = [terms[0]] + [order[0].shifted(terms[s], -s) for s in range(1, order[0].size)]

    def step(self, level, after, reads=()):
        ring = self.order[level]
        found, token = add_slots(self.parts, ring.size, after, reads)
        self.parts = [found[0]] + [ring.shifted(found[s], -s) for s in range(1, ring.size)]
        return (token,)


def shared_copies(value, across, seq):
    peers, spans = lax.axis_size("dp"), lax.axis_size("seq")
    cores = peers // across.size

    def target(place, by_a, by_s):
        dp, at = place // spans, place % spans
        moved = (dp // cores + by_a) % across.size * cores + dp % cores
        return moved * spans + (at + by_s) % spans

    return [
        [
            value
            if by_a == by_s == 0
            else lax.ppermute(
                value,
                ("dp", "seq"),
                [(place, target(place, by_a, by_s)) for place in range(peers * spans)],
            )
            for by_a in range(across.size)
        ]
        for by_s in range(seq.size)
    ]


def passed_along(value, axis, by):
    peers = lax.axis_size(axis)
    pairs = [(i, i + by) for i in range(peers) if 0 <= i + by < peers]
    return lax.ppermute(value, axis, pairs)


def rims(source, reach_rows, seq, rim=None):
    span_rows = source.shape[0]
    if seq.size == 2 and reach_rows <= span_rows:
        if rim is None:
            first = (1 - seq.index) * (span_rows - reach_rows)
            rim = lax.dynamic_slice_in_dim(source, first, reach_rows, 0)
        return seq.shifted(rim, 1)
    left_parts = []
    right_parts = []
    distances = -(-reach_rows // span_rows)
    for distance in range(1, distances + 1):
        rim_count = min(span_rows, reach_rows - (distance - 1) * span_rows)
        left_parts.insert(0, passed_along(source[span_rows - rim_count :], "seq", distance))
        right_parts.append(passed_along(source[:rim_count], "seq", -distance))
    return left_parts, right_parts


def extend(source, found, seq, after=()):
    if isinstance(found, tuple):
        return join_rows(found[0] + [source] + found[1], after)
    reach, span = found.shape[0], source.shape[0]

    def kernel(place_ref, found_ref, source_ref, *refs):
        out_ref, token_ref = refs[-2:]
        token_ref[...] = jnp.zeros(TOKEN.shape, TOKEN.dtype)
        out_ref[reach : reach + span] = source_ref[...]
        zeros = jnp.zeros(found.shape, found.dtype)

        @pl.when(place_ref[0] == 0)
        def _():
            out_ref[:reach] = zeros
            out_ref[reach + span :] = found_ref[...]

        @pl.when(place_ref[0] != 0)
        def _():
            out_ref[:reach] = found_ref[...]
            out_ref[reach + span :] = zeros

    shape = jax.ShapeDtypeStruct((span + 2 * reach, source.shape[1]), source.dtype)
    extended, token = pl.pallas_call(
        kernel,
        in_specs=[SCALARS] + [WHOLE] * (2 + len(after)),
        out_specs=[WHOLE] * 2,
        out_shape=[shape, TOKEN],
        compiler_params=pltpu.CompilerParams(vmem_limit_bytes=10 * MIB),
        cost_estimate=cost(1.5),
        name="extend",
    )(seq.index.astype(jnp.int32)[None], found, source, *after)
    return extended, (token,)


def to_rows(values):
    windows, positions = values.shape[:2]
    cut = values.reshape((windows, positions // FIRST_DILATION, FIRST_DILATION) + values.shape[2:])
    return jnp.swapaxes(cut, 0, 1).reshape((windows * positions,) + values.shape[2:])


def from_rows(values, windows):
    cut = values.reshape((-1, windows, FIRST_DILATION) + values.shape[1:])
    return jnp.swapaxes(cut, 0, 1).reshape((windows, -1) + values.shape[1:])


def on_device(
    inputs,
    targets,
    masked,
    conv_weight,
    conv_bias,
    gains,
    shifts,
    in_weight,
    in_bias,
    out_weight,
    out_bias,
    head_weight,
):
    core, across, seq, tap = rings()
    taps = conv_weight.shape[1]
    channels = conv_weight.shape[2]
    width = conv_weight.shape[3]
    slab = channels // (seq.size * across.size)
    lanes = width // core.size
    hidden_width = in_bias.shape[1]
    ffn_rows = in_weight.shape[2]
    windows = inputs.shape[0]
    rows = windows * inputs.shape[1]
    steps = (FIRST_DILATION * windows, SECOND_DILATION * windows)
    units = hidden_width // core.size
    places = (core.index, seq.index, across.index, tap.index)
    sizes = (core.size, seq.size, across.size, tap.size)

    in_bias_placed = []
    for b in range(2):
        bias = in_bias[b].reshape(across.size, core.size, seq.size, tap.size, ffn_rows)
        for axis, ring in enumerate((across, core, seq, tap)):
            bias = relative(bias, axis, ring.index, ring.size)
        in_bias_placed.append(bias.transpose(1, 0, 2, 3, 4).reshape(core.size, units))

    def cut_ffn(piece):
        return piece.reshape(ffn_rows, core.size, lanes).swapaxes(0, 1).reshape(-1, lanes)

    def bundle(b, ready=None):
        conv_piece = lax.dynamic_slice(
            conv_weight[b],
            (0, (seq.index * across.size + across.index) * slab, core.index * lanes),
            (taps, slab, lanes),
        )
        pieces = [
            conv_piece.reshape(taps * slab, lanes),
            cut_ffn(in_weight[b].T),
            cut_ffn(out_weight[b]),
        ]
        if ready is not None:
            pieces = [piece + ready for piece in pieces]
        return jnp.concatenate(pieces)

    cuts = (
        (0, taps * slab, (taps, slab, lanes)),
        (taps * slab, taps * slab + 2 * core.size * ffn_rows, (2 * core.size, ffn_rows, lanes)),
    )

    def straight(arrays):
        return (arrays, ((0, None, arrays[0].shape),))

    conv_input = to_rows(inputs)
    stream = conv_input
    codes = to_rows(targets + masked * head_weight.shape[1])
    codes = jnp.broadcast_to(codes[:, None], (rows, 128))

    reaches = [taps // 2 * step for step in steps]
    rim_reaches = [reach if seq.size == 2 and reach <= rows else 0 for reach in reaches]

    tap_parts = tap.gather(bundle(0))
    found = rims(conv_input, reaches[0], seq)
    behind = bundle(1, tap_parts[-1][0, 0] * 0)
    (conv_part, ffn_part), last = restack(
        [(tap_parts, cuts)], reads=[behind] + [found if rim_reaches[0] else conv_input]
    )
    (behind,), last = hold([behind], last)
    split = (tap.size + 1) // 2
    late_parts = tap.gather(behind)
    extended, last = extend(conv_input, found, seq, last)
    extended_parts = [extended] + [core.shifted(extended, -c) for c in range(1, core.size)]
    conv_parts, ffn_parts = across.gather(conv_part), seq.gather(ffn_part)
    (conv_part, ffn_part), last = restack(
        [straight(conv_parts), straight(ffn_parts)],
        reads=late_parts[1:split],
        after=last,
    )
    conv_parts, ffn_parts = seq.gather(conv_part), across.gather(ffn_part)
    conv_slots = [core.gather(conv_part)]
    ffn_slots = [core.gather(ffn_part)]
    held, last = hold(
        conv_parts[1:] + ffn_parts[1:],
        last,
        conv_slots[0][1:] + ffn_slots[0][1:] + late_parts[1:],
    )
    conv_slots += [core.gather(each) for each in held[: seq.size - 1]]
    ffn_slots += [core.gather(each) for each in held[seq.size - 1 :]]
    (late_conv, late_ffn), last = restack([(late_parts, cuts)], after=last, fixed=True)
    late_conv_parts, late_ffn_parts = across.gather(late_conv), seq.gather(late_ffn)

    def turned(slots):
        return [[each[c] for each in slots] for c in range(core.size)]

    conv_full, in_full, out_full = [None, None], [None, None], [None, None]
    conv_full[0], last = place_conv(
        turned(conv_slots), places, sizes, last, [part for each in ffn_slots for part in each[1:]]
    )
    saved = []
    reads = []
    rim = None
    for b in range(2):
        if b == 1:
            found = rims(conv_input, reaches[1], seq, rim)
            held, last = hold(late_conv_parts[1:] + late_ffn_parts[1:], last)
            late_conv_slots += [core.gather(each) for each in held[: seq.size - 1]]
            late_ffn_slots += [core.gather(each) for each in held[seq.size - 1 :]]
            conv_full[1], last = place_conv(turned(late_conv_slots), places, sizes, last)
            in_full[1], out_full[1], last = place_ffn(turned(late_ffn_slots), sizes, last)
            extended, last = extend(conv_input, found, seq, last)
            extended_parts = [extended] + [core.shifted(extended, -c) for c in range(1, core.size)]
        (normed_conv, conv_slope, stream, lowered), last = conv_forward(
            extended,
            conv_full[b],
            stream,
            conv_bias[b],
            gains[b, 0],
            shifts[b, 0],
            steps[b],
            last,
            reads,
        )
        reads = extended_parts[1:]
        if b == 0:
            (late_conv, late_ffn), last = restack(
                [straight(late_conv_parts), straight(late_ffn_parts)], after=last
            )
            late_conv_parts, late_ffn_parts = seq.gather(late_conv), across.gather(late_ffn)
            late_conv_slots = [core.gather(late_conv)]
            late_ffn_slots = [core.gather(late_ffn)]
            in_full[0], out_full[0], last = place_ffn(turned(ffn_slots), sizes, last)
            reads = reads + late_conv_slots[0][1:] + late_ffn_slots[0][1:]
        active, hidden_slopes, (normed_ffn, scale_ffn, stream, conv_input), packets, rim, last = (
            ffn_forward(
                lowered,
                stream,
                in_full[b],
                out_full[b],
                [in_bias_placed[b][c] for c in range(core.size)],
                out_bias[b],
                gains[b, 1],
                shifts[b, 1],
                seq.index,
                rim_reaches[1] if b == 0 else 0,
                b == 1,
                last,
                reads,
            )
        )
        packets = [core.shifted(packet, -1 - c) for c, packet in enumerate(packets)]
        reads = packets
        saved.append(
            (
                extended_parts,
                conv_slope,
                normed_conv,
                (active, lowered, packets),
                hidden_slopes,
                normed_ffn,
                scale_ffn,
            )
        )

    (stream_grad, head_grad, loss_rows), last = head_and_loss(stream, head_weight, codes, last)

    ffn_rows_of_sums = [None, None]
    conv_rows_of_sums = [None, None]
    in_bias_grads = [None, None]
    ffn_sums = [None, None]
    conv_sums = [None, None]
    merged = [None, None]

    def groups(halves):
        half = (tap.size + 1) // 2
        return [(each.parts, slots) for each, slots in zip(halves, (half, tap.size - half))]

    for b in (1, 0):
        (
            extended_parts,
            conv_slope,
            normed_conv,
            active_pair,
            hidden_slopes,
            normed_ffn,
            scale_ffn,
        ) = saved[b]
        output_grad, hidden_grad, biases, packets, ffn_rows_of_sums[b], last = ffn_back_hidden(
            stream_grad, normed_ffn, scale_ffn, gains[b, 1], out_full[b], hidden_slopes, last
        )
        if b == 1:
            arrived_packets = [core.shifted(packet, -1 - c) for c, packet in enumerate(packets)]
        if b == 0:
            for each in ffn_sums[1]:
                last = each.step(1, last)
            for each in conv_sums[1]:
                last = each.step(1, last)
        stream_grad, conv_grad, conv_cuts, relayed, rim, conv_rows_of_sums[b], last = ffn_back_stream(
            stream_grad,
            hidden_grad,
            packets,
            in_full[b],
            normed_conv,
            conv_slope,
            gains[b, 0],
            places,
            rim_reaches[b],
            last,
            reads,
            relay=b == 0,
        )
        reads = []
        if b == 0:
            merged[1], last = merge_slots(
                groups(conv_sums[1]), groups(ffn_sums[1]), last
            )
            sent = [rim] if rim is not None else []
            held, last = hold(list(conv_cuts) + list(relayed) + sent, last)
            conv_cuts, relayed = held[: core.size - 1], held[core.size - 1 : 2 * core.size - 2]
            rim = held[-1] if sent else None
            merged[1] = tap.swap(merged[1])
            arrived_packets = [core.shifted(packet, -1 - c) for c, packet in enumerate(relayed)]
        arrived = [core.shifted(conv_cuts[c - 1], -c) for c in range(1, core.size)]
        in_bias_grads[b] = list(biases)
        found_rims = rims(conv_grad, reaches[b], seq, rim)

        def ffn_grads(last):
            active, lowered, packets = active_pair
            if core.size == 1:
                packets = []
            first, second, token = ffn_weight_grad(
                (
                    (hidden_grad, lowered, [(g, p) for g, p in zip(arrived_packets, packets)]),
                    (active, output_grad, [(p, g) for g, p in zip(arrived_packets, packets)]),
                ),
                sizes,
                ffn_rows,
                last,
            )
            found = [Reduce(first, (across, seq))]
            if second:
                found.append(Reduce(second, (seq, across)))
            return found, (token,)

        def conv_grads(last, reads=()):
            first, second, token = conv_weight_grad(
                extended_parts, conv_grad, arrived, places, sizes, taps, steps[b], last, reads
            )
            found = [Reduce(first, (seq, across))]
            if second:
                found.append(Reduce(second, (across, seq)))
            return found, (token,)

        if b == 1:
            ffn_sums[1], last = ffn_grads(last)
            extended_grad, last = extend(conv_grad, found_rims, seq, last)
            conv_sums[1], last = conv_grads(last)
        else:
            conv_sums[0], last = conv_grads(last, arrived_packets)
            extended_grad, last = extend(conv_grad, found_rims, seq, last)
            ffn_sums[0], last = ffn_grads(last)
            for each in conv_sums[0]:
                last = each.step(1, last, merged[1][1:])
        if b == 1:
            stream_grad, last = conv_data_grad(
                extended_grad, conv_full[1], stream_grad, steps[1], jnp.float32, last
            )

    row_groups = [(each, 3) for each in conv_rows_of_sums + ffn_rows_of_sums]
    row_groups.append((head_grad, head_weight.shape[1]))
    (conv_input,), last = hold([conv_input], last)
    final_state = from_rows(conv_input, windows)
    packed, last = pack_small(row_groups, in_bias_grads, loss_rows, places, sizes, ffn_rows, last, [final_state])

    conv_rows = taps * slab
    merged[0], last = append_slots(groups(conv_sums[0]), [packed], last)
    merged[0] = tap.swap(merged[0])
    stream_grad, last = conv_data_grad(
        extended_grad, conv_full[0], stream_grad, steps[0], jnp.bfloat16, last
    )
    for each in ffn_sums[0]:
        last = each.step(1, last)
    shards, last = finish_conv([merged[0], merged[1]], conv_rows, packed.shape[0], last)
    ffn_late, last = append_slots(groups(ffn_sums[0]), [], last)
    ffn_late = tap.swap(ffn_late)
    grad_inputs = from_rows(stream_grad, windows)
    copies = [each for row in shared_copies(shards, across, seq) for each in row]
    (stack,), last = restack([straight(copies)], reads=[grad_inputs], after=last)
    stacks = core.gather(stack)
    grad_in, grad_out, last = finish_ffn(merged[1], ffn_late, conv_rows, ffn_rows, last)
    (
        grad_conv_bias,
        grad_gains,
        grad_shifts,
        grad_in_bias,
        grad_out_bias,
        grad_head_weight,
        loss,
    ) = finish_small(
        stacks, 2 * conv_rows, width, head_weight.shape[1], hidden_width, places, sizes
    )
    grad_conv = place_conv_grads(stacks, 2, taps, slab, places, sizes)
    return (
        final_state,
        grad_inputs,
        grad_conv,
        grad_conv_bias,
        grad_gains,
        grad_shifts,
        grad_in,
        grad_in_bias,
        grad_out,
        grad_out_bias,
        grad_head_weight,
        loss.reshape(()),
    )


def solution(mesh):
    placed = (
        P(("dp", "tap"), "seq", None),
        P(("dp", "tap"), "seq"),
        P(("dp", "tap"), "seq"),
        P(None, None, "tap", None),
        P(),
        P(),
        P(),
        P(None, None, ("dp", "seq", "tap")),
        P(),
        P(None, ("dp", "seq", "tap"), None),
        P(),
        P(),
    )
    return jax.shard_map(
        on_device,
        mesh=mesh,
        in_specs=placed,
        out_specs=(
            P(("dp", "tap"), "seq", None),
            P(("dp", "tap"), "seq", None),
            P(None, None, "tap", None),
            P(),
            P(),
            P(),
            P(None, None, ("dp", "seq", "tap")),
            P(),
            P(None, ("dp", "seq", "tap"), None),
            P(),
            P(),
            P(),
        ),
        check_vma=False,
    )
```
